32 devices in a mesh: dp: 16 (over z, y, x), tensor: 2 (over core).
Axes of the slice: x: 2, y: 2, z: 4, core: 2. Of those that a mesh axis runs over, the one named last changes fastest.
Arguments:
- hidden_in: float32 [8192, 1536], P('dp'), may hold values from -6 to 6
- out_grad: float32 [8192, 1536], P('dp'), may hold values from -6 to 6
- prompt_states: bfloat16 [32, 128, 768], P('dp'), may hold values from -6 to 6
- row_split: int32 [16], P('dp'), may hold values from 256 to 512, as said below
- prompt_len: int32 [32], P('dp'), may hold values from 1 to 128, as said below
- gain_attn: float32 [1536], replicated, may hold values from 0.5 to 1.5
- bias_attn: float32 [1536], replicated, may hold values from -1.2 to 1.2
- gain_cross: float32 [1536], replicated, may hold values from 0.5 to 1.5
- bias_cross: float32 [1536], replicated, may hold values from -1.2 to 1.2
- gain_ff: float32 [1536], replicated, may hold values from 0.5 to 1.5
- bias_ff: float32 [1536], replicated, may hold values from -1.2 to 1.2
- w_query: bfloat16 [1536, 1536], P(None, 'tensor'), may hold values from -0.15625 to 0.15625
- w_key: bfloat16 [1536, 1536], P(None, 'tensor'), may hold values from -0.15625 to 0.15625
- w_value: bfloat16 [1536, 1536], P(None, 'tensor'), may hold values from -0.15625 to 0.15625
- w_out: bfloat16 [1536, 1536], P('tensor'), may hold values from -2.5 to 2.5
- c_query: bfloat16 [1536, 1536], P(None, 'tensor'), may hold values from -0.15625 to 0.15625
- c_key: bfloat16 [768, 1536], P(None, 'tensor'), may hold values from -0.21875 to 0.21875
- c_value: bfloat16 [768, 1536], P(None, 'tensor'), may hold values from -0.21875 to 0.21875
- c_out: bfloat16 [1536, 1536], P('tensor'), may hold values from -1.25 to 1.25
- w_gate: bfloat16 [1536, 6144], P(None, 'tensor'), may hold values from -0.15625 to 0.15625
- w_up: bfloat16 [1536, 6144], P(None, 'tensor'), may hold values from -0.15625 to 0.15625
- w_down: bfloat16 [6144, 1536], P('tensor'), may hold values from -0.078125 to 0.078125
Outputs:
- result: float32 [8192, 1536], P('dp')
- grad_hidden: float32 [8192, 1536], P('dp')
- grad_gain_attn: float32 [1536], P(('dp', 'tensor'))
- grad_bias_attn: float32 [1536], P(('dp', 'tensor'))
- grad_gain_cross: float32 [1536], P(('dp', 'tensor'))
- grad_bias_cross: float32 [1536], P(('dp', 'tensor'))
- grad_gain_ff: float32 [1536], P(('dp', 'tensor'))
- grad_bias_ff: float32 [1536], P(('dp', 'tensor'))
- grad_w_query: float32 [1536, 1536], P('dp', 'tensor')
- grad_w_key: float32 [1536, 1536], P('dp', 'tensor')
- grad_w_value: float32 [1536, 1536], P('dp', 'tensor')
- grad_w_out: float32 [1536, 1536], P('tensor', 'dp')
- grad_c_query: float32 [1536, 1536], P('dp', 'tensor')
- grad_c_key: float32 [768, 1536], P('dp', 'tensor')
- grad_c_value: float32 [768, 1536], P('dp', 'tensor')
- grad_c_out: float32 [1536, 1536], P('tensor', 'dp')
- grad_w_gate: float32 [1536, 6144], P('dp', 'tensor')
- grad_w_up: float32 [1536, 6144], P('dp', 'tensor')
- grad_w_down: float32 [6144, 1536], P('tensor', 'dp')
The draws below stay inside these ranges and needn't reach their ends.
Inputs may be any that keep to these rules, and one draw needn't show every extreme that they name: `row_split`: each buffer holds either one row of 512 frames (value 512) or two rows of 256 frames (value 512 / 2); exactly half of the buffers hold one row, which ones is drawn. `prompt_len`: slot 2b + 1 is unused where buffer b holds one row; some slot has all 128 states.
All inputs are finite; a program needn't handle non-finite values.
Results may differ from the reference program's by a relative error of at most 0.029.
Values may be sent and summed in bfloat16 or wider, within the bound.
No kernel may reach another device: no remote copies, remote signals or barrier semaphores. Data moves between devices by JAX's collectives and lax.ppermute only.
A program may use at most 256 MiB of HBM per device.

```python
import math
import jax
import jax.numpy as jnp
from jax import lax

D = 1536
FF = 6144
CTX = 768
PROMPT = 128
HEAD = 64
TOK_DEV = 512
BUFFERS = 16
TOKENS = 8192
ROWS = 32


def draw_row_split(key, part):
    shuffled = jax.random.permutation(key, BUFFERS)
    return jnp.where(shuffled < BUFFERS // 2, TOK_DEV, TOK_DEV // 2).astype(jnp.int32)


def draw_prompt_len(key, part):
    key_lengths = jax.random.fold_in(key, 11)
    key_slot = jax.random.fold_in(key, 23)
    lengths = jax.random.randint(key_lengths, (ROWS,), 1, PROMPT + 1)
    full_slot = jax.random.randint(key_slot, (), 0, ROWS)
    return lengths.at[full_slot].set(PROMPT).astype(jnp.int32)


def strengthened(entries, key, source, target, blocks, factor):
    def block_of(position):
        return (jnp.arange(entries.shape[position]) // (entries.shape[position] // blocks)).reshape((-1,) + (1,) * (entries.ndim - 1 - position))

    first = jax.random.permutation(key, blocks)[block_of(target)]
    other_side = (block_of(target) + blocks // 2) % blocks
    return jnp.where((block_of(source) == first) | (block_of(source) == other_side), factor * entries, entries)


def shard_levels(stream_key, dims, split, low, largest):
    factor_of, own = 1.0, jax.random.fold_in(stream_key, 6)
    for position, parts in split:
        draws = jnp.exp(jax.random.uniform(jax.random.fold_in(own, position), (parts,), jnp.float32, low / len(split), largest / len(split)))
        factor_of = factor_of * jnp.repeat(draws, dims[position] // parts).reshape([-1 if axis == position else 1 for axis in range(len(dims))])
    return factor_of


def centred(key, dims, scale, most, shards=(), kind=jnp.bfloat16):
    array = jax.random.normal(key, dims, jnp.float32) * scale
    if len(shards) > 0:
        array = shard_levels(key, dims, shards, -0.22, 0.18) * array
    return jnp.clip(array, min=-most, max=most).astype(kind)


def noise_with(stream_key, shape, deviation, limit, cuts, heavy, kind=jnp.bfloat16):
    drawn = deviation * jax.random.normal(stream_key, shape, jnp.float32)
    if cuts:
        drawn = drawn * shard_levels(stream_key, shape, cuts, -0.22, 0.18)
    return jnp.clip(strengthened(drawn, jax.random.fold_in(stream_key, 3), *heavy), -limit, limit).astype(kind)


def setup_inputs(seed: int = 0) -> dict:
    keys = jax.random.split(jax.random.key(seed), 23)
    hidden_in = centred(keys[0], (TOKENS, D), 1.0, 6.0, ((0, 16),), jnp.float32)
    out_grad = noise_with(keys[1], (TOKENS, D), 1.0, 6.0, ((0, 16),), (0, 1, 16, 2.0), jnp.float32)
    prompt_states = centred(keys[2], (ROWS, PROMPT, CTX), 1.0, 6.0, ((0, 16),))
    row_split = draw_row_split(jax.random.fold_in(keys[22], 71), 0)
    prompt_len = draw_prompt_len(jax.random.fold_in(keys[22], 71), 0)
    gain_attn = jnp.clip(1.0 + 0.1 * jax.random.normal(keys[5], (D,), jnp.float32), 0.5, 1.5)
    bias_attn = centred(keys[6], (D,), 0.3, 1.2, (), jnp.float32)
    gain_cross = jnp.clip(1.0 + 0.1 * jax.random.normal(keys[7], (D,), jnp.float32), 0.5, 1.5)
    bias_cross = centred(keys[8], (D,), 0.3, 1.2, (), jnp.float32)
    gain_ff = jnp.clip(1.0 + 0.1 * jax.random.normal(keys[9], (D,), jnp.float32), 0.5, 1.5)
    bias_ff = centred(keys[10], (D,), 0.3, 1.2, (), jnp.float32)
    w_query = centred(keys[11], (D, D), D ** -0.5, 0.15625, ((1, 2),))
    w_key = centred(keys[12], (D, D), D ** -0.5, 0.15625, ((1, 2),))
    w_value = centred(keys[13], (D, D), D ** -0.5, 0.15625, ((1, 2),))
    w_out = centred(keys[14], (D, D), (max(1, 2 * D // TOK_DEV)) ** -0.5, 2.5, ((0, 2),))
    c_query = centred(keys[15], (D, D), D ** -0.5, 0.15625, ((1, 2),))
    c_key = centred(keys[16], (CTX, D), CTX ** -0.5, 0.21875, ((1, 2),))
    c_value = centred(keys[17], (CTX, D), CTX ** -0.5, 0.21875, ((1, 2),))
    c_out = centred(keys[18], (D, D), (max(1, 2 * D // PROMPT)) ** -0.5, 1.25, ((0, 2),))
    w_gate = centred(keys[19], (D, FF), D ** -0.5, 0.15625, ((1, 2),))
    w_up = centred(keys[20], (D, FF), D ** -0.5, 0.15625, ((1, 2),))
    w_down = centred(keys[21], (FF, D), FF ** -0.5, 0.078125, ((0, 2),))
    return {"hidden_in": hidden_in, "out_grad": out_grad, "prompt_states": prompt_states, "row_split": row_split, "prompt_len": prompt_len, "gain_attn": gain_attn, "bias_attn": bias_attn, "gain_cross": gain_cross, "bias_cross": bias_cross, "gain_ff": gain_ff, "bias_ff": bias_ff, "w_query": w_query, "w_key": w_key, "w_value": w_value, "w_out": w_out, "c_query": c_query, "c_key": c_key, "c_value": c_value, "c_out": c_out, "w_gate": w_gate, "w_up": w_up, "w_down": w_down}


@jax.custom_vjp
def low(v):
    return lax.optimization_barrier(v.astype(jnp.bfloat16)).astype(jnp.float32)

@jax.custom_vjp
def low_back(v):
    return v

def low_keep(v):
    return (low(v), None)

def low_pass(kept, grad):
    return (grad,)

def back_keep(v):
    return (v, None)

def back_low(kept, grad):
    return (low(grad),)
low.defvjp(low_keep, low_pass)
low_back.defvjp(back_keep, back_low)
norm_eps = 1e-05
score_scale = 0.125
masked_score = -1e+30

def highest(left_side, right_side):
    return jnp.dot(left_side, right_side, precision=lax.Precision.HIGHEST)

def layer_norm(values, norm_gain, norm_shift):
    average = lax.optimization_barrier(jnp.mean(values, axis=-1, keepdims=True))
    centered = values - average
    variance = lax.optimization_barrier(jnp.mean(centered * centered, axis=-1, keepdims=True))
    return centered * lax.rsqrt(variance + norm_eps) * norm_gain + norm_shift

def rotary_tables(positions, width):
    dim_index = jnp.arange(width) % HEAD
    freq_index = (dim_index % 16).astype(jnp.float32)
    inverse_freq = jnp.exp(freq_index * (-math.log(10000.0) / 16.0))
    angles = positions[:, None] * inverse_freq[None, :]
    cosine = jnp.cos(angles)
    sine_part = jnp.sin(angles)
    cos_table = jnp.where(dim_index < 32, cosine, 1.0)
    sin_lower = jnp.where(dim_index < 16, -sine_part, 0.0)
    sin_upper = jnp.where((dim_index >= 16) & (dim_index < 32), sine_part, 0.0)
    return (cos_table, sin_lower, sin_upper)

def rotate(values, tables):
    cos_table, sin_lower, sin_upper = tables
    return values * cos_table + jnp.roll(values, -16, axis=1) * sin_lower + jnp.roll(values, 16, axis=1) * sin_upper

def attention(queries, keys_in, values_in, allowed):
    head_count = queries.shape[1] // HEAD
    query_heads = queries.reshape(queries.shape[0], head_count, HEAD)
    key_heads = keys_in.reshape(keys_in.shape[0], head_count, HEAD)
    value_heads = values_in.reshape(values_in.shape[0], head_count, HEAD)
    raw_scores = jnp.einsum('qhd,khd->hqk', query_heads, key_heads, precision=lax.Precision.HIGHEST)
    scores = jnp.where(allowed[None], low_back(raw_scores * score_scale), masked_score)
    soft_weights = jax.nn.softmax(scores, axis=-1)
    mixed_heads = jnp.einsum('hqk,khd->qhd', low(soft_weights), value_heads, precision=lax.Precision.HIGHEST)
    return mixed_heads.reshape(queries.shape[0], queries.shape[1])

def buffer_forward(params_now, hidden, context, split_at, lengths):
    gain_attn, bias_attn, gain_cross, bias_cross, gain_ff, bias_ff, w_query, w_key, w_value, w_out, c_query, c_key, c_value, c_out, w_gate, w_up, w_down = params_now
    positions = jnp.arange(TOK_DEV, dtype=jnp.int32)
    row_ids = (positions >= split_at).astype(jnp.int32)
    tables = rotary_tables((positions - row_ids * split_at).astype(jnp.float32), D)
    normed_one = low(layer_norm(hidden, gain_attn, bias_attn))
    queries = low(rotate(low_back(highest(normed_one, w_query)), tables))
    keys_now = low(rotate(low_back(highest(normed_one, w_key)), tables))
    values_now = low(low_back(highest(normed_one, w_value)))
    self_ok = row_ids[:, None] == row_ids[None, :]
    attended_one = low(low_back(attention(queries, keys_now, values_now, self_ok)))
    resid_one = hidden + low_back(highest(attended_one, w_out))
    normed_two = low(layer_norm(resid_one, gain_cross, bias_cross))
    cross_query = low(low_back(highest(normed_two, c_query)))
    cross_key = low(low_back(highest(context, c_key)))
    cross_value = low(low_back(highest(context, c_value)))
    key_index = jnp.arange(2 * PROMPT, dtype=jnp.int32)
    key_rows = key_index // PROMPT
    key_live = key_index % PROMPT < lengths[key_rows]
    cross_ok = (row_ids[:, None] == key_rows[None, :]) & key_live[None, :]
    attended_two = low(low_back(attention(cross_query, cross_key, cross_value, cross_ok)))
    resid_two = resid_one + low_back(highest(attended_two, c_out))
    normed_three = low(layer_norm(resid_two, gain_ff, bias_ff))
    gate_pre = low_back(highest(normed_three, w_gate))
    up_pre = low_back(highest(normed_three, w_up))
    mixed = low(jax.nn.silu(gate_pre) * up_pre)
    return resid_two + low_back(highest(mixed, w_down))

def reference(hidden_in, out_grad, prompt_states, row_split, prompt_len, gain_attn, bias_attn, gain_cross, bias_cross, gain_ff, bias_ff, w_query, w_key, w_value, w_out, c_query, c_key, c_value, c_out, w_gate, w_up, w_down):
    params = tuple((weight.astype(jnp.float32) for weight in (gain_attn, bias_attn, gain_cross, bias_cross, gain_ff, bias_ff, w_query, w_key, w_value, w_out, c_query, c_key, c_value, c_out, w_gate, w_up, w_down)))
    hidden_all = hidden_in.reshape(BUFFERS, TOK_DEV, D)
    grads_all = out_grad.reshape(BUFFERS, TOK_DEV, D)
    contexts = prompt_states.astype(jnp.float32).reshape(BUFFERS, 2 * PROMPT, CTX)
    lengths_all = prompt_len.reshape(BUFFERS, 2)

    def one_buffer(summed, pieces):
        hidden, cotangent, context, split_at, lengths = pieces

        def forward(params_now, hidden_now):
            return buffer_forward(params_now, hidden_now, context, split_at, lengths)
        outcome, pullback = jax.vjp(forward, params, hidden)
        param_grads, hidden_grad = pullback(cotangent)
        summed = jax.tree.map(lambda before, fresh: before + fresh, summed, param_grads)
        return (summed, (outcome, hidden_grad))
    zero_sums = jax.tree.map(jnp.zeros_like, params)
    summed, (outcomes, hidden_grads) = lax.scan(one_buffer, zero_sums, (hidden_all, grads_all, contexts, row_split, lengths_all))
    return (outcomes.reshape(TOKENS, D), hidden_grads.reshape(TOKENS, D), summed[0], summed[1], summed[2], summed[3], summed[4], summed[5], summed[6], summed[7], summed[8], summed[9], summed[10], summed[11], summed[12], summed[13], summed[14], summed[15], summed[16])
```

```python
import math

import jax
import jax.numpy as jnp
from jax import lax
from jax.sharding import PartitionSpec as P

PROMPT = 128
HEAD = 64


norm_eps = 1e-05
score_scale = 0.125
masked_score = -1e30


def product_plain(left_side, right_side):
    return jnp.dot(left_side, right_side, preferred_element_type=jnp.float32)


def product_over_rows(left_side, right_side):
    return lax.dot_general(
        left_side, right_side, (((0,), (0,)), ((), ())), preferred_element_type=jnp.float32
    )


def product_with_rows(left_side, right_side):
    return lax.dot_general(
        left_side, right_side, (((1,), (1,)), ((), ())), preferred_element_type=jnp.float32
    )


def rotary_tables(positions, width):
    dim_index = jnp.arange(width) % HEAD
    freq_index = (dim_index % 16).astype(jnp.float32)
    inverse_freq = jnp.exp(freq_index * (-math.log(10000.0) / 16.0))
    angles = positions[:, None] * inverse_freq[None, :]
    cosine = jnp.cos(angles)
    sine_part = jnp.sin(angles)
    cos_table = jnp.where(dim_index < 32, cosine, 1.0)
    sin_lower = jnp.where(dim_index < 16, -sine_part, 0.0)
    sin_upper = jnp.where((dim_index >= 16) & (dim_index < 32), sine_part, 0.0)
    return (cos_table, sin_lower, sin_upper)


def rotate(values, tables):
    cos_table, sin_lower, sin_upper = tables
    return (
        values * cos_table
        + jnp.roll(values, -16, axis=1) * sin_lower
        + jnp.roll(values, 16, axis=1) * sin_upper
    )


def rotate_back(incoming, tables):
    cos_table, sin_lower, sin_upper = tables
    return (
        incoming * cos_table
        + jnp.roll(incoming * sin_lower, 16, axis=1)
        + jnp.roll(incoming * sin_upper, -16, axis=1)
    )


def normalize(values, norm_gain, norm_shift):
    average = jnp.mean(values, axis=-1, keepdims=True)
    centered = values - average
    variance = jnp.mean(centered * centered, axis=-1, keepdims=True)
    inverse = lax.rsqrt(variance + norm_eps)
    scaled = centered * inverse
    return (scaled * norm_gain + norm_shift, scaled, inverse)


def normalize_back(incoming, scaled, inverse, norm_gain):
    grad_gain = jnp.sum(incoming * scaled, axis=0)
    grad_shift = jnp.sum(incoming, axis=0)
    weighted = incoming * norm_gain
    grad_input = inverse * (
        weighted
        - jnp.mean(weighted, axis=-1, keepdims=True)
        - scaled * jnp.mean(weighted * scaled, axis=-1, keepdims=True)
    )
    return (grad_input, grad_gain, grad_shift)


def heads_of(values):
    return values.reshape(values.shape[0], values.shape[1] // HEAD, HEAD)


def attend_forward(query_block, key_heads, value_heads, allowed):
    query_heads = heads_of(query_block)
    scores = (
        jnp.einsum("qhd,khd->hqk", query_heads, key_heads, preferred_element_type=jnp.float32)
        * score_scale
    )
    scores = jnp.where(allowed[None], scores, masked_score)
    largest = jnp.max(scores, axis=-1, keepdims=True)
    exp_scores = jnp.exp(scores - largest)
    totals = jnp.sum(exp_scores, axis=-1, keepdims=True)
    soft_weights = (exp_scores / totals).astype(jnp.bfloat16)
    mixed_heads = jnp.einsum(
        "hqk,khd->qhd", soft_weights, value_heads, preferred_element_type=jnp.float32
    )
    mixed_flat = mixed_heads.reshape(query_block.shape[0], query_block.shape[1]).astype(
        jnp.bfloat16
    )
    return (mixed_flat, largest[..., 0] + jnp.log(totals[..., 0]))


def attend_backward(query_block, key_heads, value_heads, allowed, grad_block, logsum_block):
    query_heads = heads_of(query_block)
    grad_heads = heads_of(grad_block)
    scores = (
        jnp.einsum("qhd,khd->hqk", query_heads, key_heads, preferred_element_type=jnp.float32)
        * score_scale
    )
    scores = jnp.where(allowed[None], scores, masked_score)
    soft_weights = jnp.exp(scores - logsum_block[..., None])
    grad_weights = jnp.einsum(
        "qhd,khd->hqk", grad_heads, value_heads, preferred_element_type=jnp.float32
    )
    inner_sum = jnp.sum(soft_weights * grad_weights, axis=-1, keepdims=True)
    grad_scores = (soft_weights * (grad_weights - inner_sum)).astype(jnp.bfloat16)
    grad_query = (
        jnp.einsum("hqk,khd->qhd", grad_scores, key_heads, preferred_element_type=jnp.float32)
        * score_scale
    )
    grad_key = (
        jnp.einsum("hqk,qhd->khd", grad_scores, query_heads, preferred_element_type=jnp.float32)
        * score_scale
    )
    grad_value = jnp.einsum(
        "hqk,qhd->khd",
        soft_weights.astype(jnp.bfloat16),
        grad_heads,
        preferred_element_type=jnp.float32,
    )
    return (
        grad_query.reshape(query_block.shape),
        grad_key.reshape(grad_key.shape[0], -1),
        grad_value.reshape(grad_value.shape[0], -1),
    )


def swap_sum(partial):
    low = partial.astype(jnp.bfloat16)
    if lax.axis_size("tensor") == 2:
        other = lax.ppermute(low, "tensor", [(0, 1), (1, 0)])
        return low.astype(jnp.float32) + other.astype(jnp.float32)
    return lax.psum(low, "tensor").astype(jnp.float32)


def pairs(mask):
    return [(i, i ^ mask) for i in range(16)]


def quarters(rows_side, mine):
    blocks = rows_side.reshape(4, 4, rows_side.shape[0] // 16, rows_side.shape[1])
    out = []
    for flip in range(4):
        part = lax.dynamic_index_in_dim(blocks, mine ^ flip, 1, keepdims=False)
        out.append(part.reshape(rows_side.shape[0] // 4, rows_side.shape[1]))
    return out


def add_low(*terms):
    total = terms[0].astype(jnp.float32)
    for term in terms[1:]:
        total = total + term.astype(jnp.float32)
    return total


def z_scatter(own, z_index):
    def block(offset):
        return lax.dynamic_index_in_dim(own, jnp.clip(z_index + offset, 0, 3), 0, keepdims=False)

    up = down = None
    for step in range(1, 4):
        up_perm = [(i, i + 4) for i in range(16) if i // 4 <= step - 1 and i // 4 < 3]
        down_perm = [(i, i - 4) for i in range(16) if i // 4 >= 4 - step and i // 4 > 0]
        up_send, down_send = block(4 - step), block(step - 4)
        if up is not None:
            up_send = add_low(up_send, up).astype(jnp.bfloat16)
            down_send = add_low(down_send, down).astype(jnp.bfloat16)
        up = lax.ppermute(up_send, "dp", up_perm)
        down = lax.ppermute(down_send, "dp", down_perm)
    return add_low(block(0), up, down)


def plane_scatter(parts):
    own, to_x, to_y, to_d = parts
    half = own.shape[1] // 2
    low = jnp.bfloat16
    pieces = []
    for first, second, cut in ((1, 2, slice(0, half)), (2, 1, slice(half, 2 * half))):
        to_first = to_x if first == 1 else to_y
        to_second = to_y if first == 1 else to_x
        got_diag = lax.ppermute(to_d[:, cut], "dp", pairs(first))
        got_own = lax.ppermute(to_first[:, cut], "dp", pairs(first))
        passed = add_low(to_second[:, cut], got_diag).astype(low)
        got_last = lax.ppermute(passed, "dp", pairs(second))
        pieces.append(add_low(own[:, cut], got_own, got_last).astype(low))
    return jnp.concatenate(pieces, axis=1)


def weight_sum(rows_side, column_side, turned=False):
    if lax.axis_size("dp") == 16 and lax.axis_size("tensor") == 2:
        index = lax.axis_index("dp")
        turned_rows = rows_side.T
        parts = [
            product_plain(part, column_side).astype(jnp.bfloat16)
            for part in quarters(turned_rows, index % 4)
        ]
        own = plane_scatter(parts)
        own = own.reshape(4, own.shape[0] // 4, own.shape[1])
        total = z_scatter(own, index // 4)
    else:
        total = lax.psum_scatter(
            product_over_rows(rows_side, column_side).astype(jnp.bfloat16),
            "dp",
            scatter_dimension=0,
            tiled=True,
        ).astype(jnp.float32)
    return total.T if turned else total


def vector_sum(vectors):
    if lax.axis_size("dp") == 16:
        for mask in (1, 2, 4, 8):
            vectors = vectors + lax.ppermute(vectors, "dp", pairs(mask))
    else:
        vectors = lax.psum(vectors, "dp")
    share = vectors.shape[1] // (lax.axis_size("dp") * lax.axis_size("tensor"))
    index = lax.axis_index("dp") * lax.axis_size("tensor") + lax.axis_index("tensor")
    return lax.dynamic_slice_in_dim(vectors, index * share, share, 1)


def on_device(
    hidden_in,
    out_grad,
    prompt_states,
    row_split,
    prompt_len,
    gain_attn,
    bias_attn,
    gain_cross,
    bias_cross,
    gain_ff,
    bias_ff,
    w_query,
    w_key,
    w_value,
    w_out,
    c_query,
    c_key,
    c_value,
    c_out,
    w_gate,
    w_up,
    w_down,
):
    low = jnp.bfloat16
    frame_count = hidden_in.shape[0]
    positions = jnp.arange(frame_count, dtype=jnp.int32)
    split_here = row_split[0]
    row_ids = (positions >= split_here).astype(jnp.int32)
    tables = rotary_tables((positions - row_ids * split_here).astype(jnp.float32), w_query.shape[1])
    key_index = jnp.arange(2 * PROMPT, dtype=jnp.int32)
    key_rows = key_index // PROMPT
    key_live = key_index % PROMPT < jnp.where(key_rows == 0, prompt_len[0], prompt_len[1])
    self_ok = row_ids[:, None] == row_ids[None, :]
    cross_ok = (row_ids[:, None] == key_rows[None, :]) & key_live[None, :]

    normed, scaled_one, inverse_one = normalize(hidden_in, gain_attn, bias_attn)
    input_one = normed.astype(low)
    query_one = rotate(product_plain(input_one, w_query), tables).astype(low)
    key_one = rotate(product_plain(input_one, w_key), tables).astype(low)
    value_one = product_plain(input_one, w_value).astype(low)
    attended_one, logsum_one = attend_forward(query_one, heads_of(key_one), heads_of(value_one), self_ok)
    resid_one = hidden_in + swap_sum(product_plain(attended_one, w_out))

    normed, scaled_two, inverse_two = normalize(resid_one, gain_cross, bias_cross)
    input_two = normed.astype(low)
    cross_query = product_plain(input_two, c_query).astype(low)
    context_flat = prompt_states.reshape(2 * PROMPT, prompt_states.shape[2])
    cross_key = product_plain(context_flat, c_key).astype(low)
    cross_value = product_plain(context_flat, c_value).astype(low)
    attended_two, logsum_two = attend_forward(
        cross_query, heads_of(cross_key), heads_of(cross_value), cross_ok
    )
    resid_two = resid_one + swap_sum(product_plain(attended_two, c_out))

    normed, scaled_three, inverse_three = normalize(resid_two, gain_ff, bias_ff)
    input_three = normed.astype(low)
    gate_pre = product_plain(input_three, w_gate)
    up_pre = product_plain(input_three, w_up)
    sigmoid_gate = jax.nn.sigmoid(gate_pre)
    mixed_low = (gate_pre * sigmoid_gate * up_pre).astype(low)
    result = resid_two + swap_sum(product_plain(mixed_low, w_down))

    grad_ff_out = out_grad.astype(low)
    grad_w_down = weight_sum(grad_ff_out, mixed_low, True)
    grad_mixed = product_with_rows(grad_ff_out, w_down)
    grad_gate = (
        grad_mixed * up_pre * sigmoid_gate * (1.0 + gate_pre * (1.0 - sigmoid_gate))
    ).astype(low)
    grad_up = (grad_mixed * gate_pre * sigmoid_gate).astype(low)
    grad_w_gate = weight_sum(input_three, grad_gate)
    grad_w_up = weight_sum(input_three, grad_up)
    normed_grad_three = swap_sum(
        product_with_rows(grad_gate, w_gate) + product_with_rows(grad_up, w_up)
    )
    back_three, grad_gain_ff, grad_bias_ff = normalize_back(
        normed_grad_three, scaled_three, inverse_three, gain_ff
    )
    grad_two = out_grad + back_three
    grad_cross_out = grad_two.astype(low)
    grad_c_out = weight_sum(grad_cross_out, attended_two, True)
    grad_attended_two = product_with_rows(grad_cross_out, c_out).astype(low)
    cross_query_grad, cross_key_grad, cross_value_grad = attend_backward(
        cross_query,
        heads_of(cross_key),
        heads_of(cross_value),
        cross_ok,
        grad_attended_two,
        logsum_two,
    )
    cross_query_grad = cross_query_grad.astype(low)
    cross_key_grad = cross_key_grad.astype(low)
    cross_value_grad = cross_value_grad.astype(low)
    grad_c_query = weight_sum(input_two, cross_query_grad)
    grad_c_key = weight_sum(context_flat, cross_key_grad)
    grad_c_value = weight_sum(context_flat, cross_value_grad)
    normed_grad_two = swap_sum(product_with_rows(cross_query_grad, c_query))
    back_two, grad_gain_cross, grad_bias_cross = normalize_back(
        normed_grad_two, scaled_two, inverse_two, gain_cross
    )
    grad_one = grad_two + back_two
    grad_self_out = grad_one.astype(low)
    grad_w_out = weight_sum(grad_self_out, attended_one, True)
    grad_attended_one = product_with_rows(grad_self_out, w_out).astype(low)
    query_grad, key_grad, value_grad = attend_backward(
        query_one, heads_of(key_one), heads_of(value_one), self_ok, grad_attended_one, logsum_one
    )
    query_grad = rotate_back(query_grad, tables).astype(low)
    key_grad = rotate_back(key_grad, tables).astype(low)
    value_grad = value_grad.astype(low)
    grad_w_query = weight_sum(input_one, query_grad)
    grad_w_key = weight_sum(input_one, key_grad)
    grad_w_value = weight_sum(input_one, value_grad)
    normed_grad_one = swap_sum(
        product_with_rows(query_grad, w_query)
        + product_with_rows(key_grad, w_key)
        + product_with_rows(value_grad, w_value)
    )
    back_one, grad_gain_attn, grad_bias_attn = normalize_back(
        normed_grad_one, scaled_one, inverse_one, gain_attn
    )
    grad_hidden = grad_one + back_one
    vectors = vector_sum(
        jnp.stack(
            [
                grad_gain_attn,
                grad_bias_attn,
                grad_gain_cross,
                grad_bias_cross,
                grad_gain_ff,
                grad_bias_ff,
            ]
        )
    )
    return (
        result,
        grad_hidden,
        vectors[0],
        vectors[1],
        vectors[2],
        vectors[3],
        vectors[4],
        vectors[5],
        grad_w_query,
        grad_w_key,
        grad_w_value,
        grad_w_out,
        grad_c_query,
        grad_c_key,
        grad_c_value,
        grad_c_out,
        grad_w_gate,
        grad_w_up,
        grad_w_down,
    )


def solution(mesh):
    in_specs = (
        P("dp", None),
        P("dp", None),
        P("dp", None, None),
        P("dp"),
        P("dp"),
        P(),
        P(),
        P(),
        P(),
        P(),
        P(),
        P(None, "tensor"),
        P(None, "tensor"),
        P(None, "tensor"),
        P("tensor", None),
        P(None, "tensor"),
        P(None, "tensor"),
        P(None, "tensor"),
        P("tensor", None),
        P(None, "tensor"),
        P(None, "tensor"),
        P("tensor", None),
    )
    out_specs = (
        P("dp", None),
        P("dp", None),
        P(("dp", "tensor")),
        P(("dp", "tensor")),
        P(("dp", "tensor")),
        P(("dp", "tensor")),
        P(("dp", "tensor")),
        P(("dp", "tensor")),
        P("dp", "tensor"),
        P("dp", "tensor"),
        P("dp", "tensor"),
        P("tensor", "dp"),
        P("dp", "tensor"),
        P("dp", "tensor"),
        P("dp", "tensor"),
        P("tensor", "dp"),
        P("dp", "tensor"),
        P("dp", "tensor"),
        P("tensor", "dp"),
    )
    return jax.shard_map(
        on_device, mesh=mesh, in_specs=in_specs, out_specs=out_specs, check_vma=False
    )
```

```python
import math

import jax
import jax.numpy as jnp
from jax import lax
from jax.experimental import pallas as pl
from jax.experimental.pallas import tpu as pltpu
from jax.sharding import PartitionSpec as P

PROMPT = 128
HEAD = 64


norm_eps = 1e-05
score_scale = 0.125
masked_score = -1e30


def product_plain(left_side, right_side):
    return jnp.dot(left_side, right_side, preferred_element_type=jnp.float32)


def product_over_rows(left_side, right_side):
    return lax.dot_general(
        left_side, right_side, (((0,), (0,)), ((), ())), preferred_element_type=jnp.float32
    )


def product_with_rows(left_side, right_side):
    return lax.dot_general(
        left_side, right_side, (((1,), (1,)), ((), ())), preferred_element_type=jnp.float32
    )


def rotary_tables(positions, width):
    dim_index = jnp.arange(width) % HEAD
    freq_index = (dim_index % 16).astype(jnp.float32)
    inverse_freq = jnp.exp(freq_index * (-math.log(10000.0) / 16.0))
    angles = positions[:, None] * inverse_freq[None, :]
    cosine = jnp.cos(angles)
    sine_part = jnp.sin(angles)
    cos_table = jnp.where(dim_index < 32, cosine, 1.0)
    sin_lower = jnp.where(dim_index < 16, -sine_part, 0.0)
    sin_upper = jnp.where((dim_index >= 16) & (dim_index < 32), sine_part, 0.0)
    return (cos_table, sin_lower, sin_upper)


def rotate(values, tables):
    cos_table, sin_lower, sin_upper = tables
    return (
        values * cos_table
        + jnp.roll(values, -16, axis=1) * sin_lower
        + jnp.roll(values, 16, axis=1) * sin_upper
    )


def rotate_back(incoming, tables):
    cos_table, sin_lower, sin_upper = tables
    return (
        incoming * cos_table
        + jnp.roll(incoming * sin_lower, 16, axis=1)
        + jnp.roll(incoming * sin_upper, -16, axis=1)
    )


def normalize(values, norm_gain, norm_shift):
    average = jnp.mean(values, axis=-1, keepdims=True)
    centered = values - average
    variance = jnp.mean(centered * centered, axis=-1, keepdims=True)
    inverse = lax.rsqrt(variance + norm_eps)
    scaled = centered * inverse
    return (scaled * norm_gain + norm_shift, scaled, inverse)


def normalize_back(incoming, scaled, inverse, norm_gain):
    grad_gain = jnp.sum(incoming * scaled, axis=0)
    grad_shift = jnp.sum(incoming, axis=0)
    weighted = incoming * norm_gain
    grad_input = inverse * (
        weighted
        - jnp.mean(weighted, axis=-1, keepdims=True)
        - scaled * jnp.mean(weighted * scaled, axis=-1, keepdims=True)
    )
    return (grad_input, grad_gain, grad_shift)


def heads_of(values):
    return values.reshape(values.shape[0], values.shape[1] // HEAD, HEAD)


def attend_forward(query_block, key_heads, value_heads, allowed):
    query_heads = heads_of(query_block)
    scores = (
        jnp.einsum("qhd,khd->hqk", query_heads, key_heads, preferred_element_type=jnp.float32)
        * score_scale
    )
    scores = jnp.where(allowed[None], scores, masked_score)
    largest = jnp.max(scores, axis=-1, keepdims=True)
    exp_scores = jnp.exp(scores - largest)
    totals = jnp.sum(exp_scores, axis=-1, keepdims=True)
    soft_weights = (exp_scores / totals).astype(jnp.bfloat16)
    mixed_heads = jnp.einsum(
        "hqk,khd->qhd", soft_weights, value_heads, preferred_element_type=jnp.float32
    )
    mixed_flat = mixed_heads.reshape(query_block.shape[0], query_block.shape[1]).astype(
        jnp.bfloat16
    )
    return (mixed_flat, largest[..., 0] + jnp.log(totals[..., 0]))


def attend_backward(query_block, key_heads, value_heads, allowed, grad_block, logsum_block):
    query_heads = heads_of(query_block)
    grad_heads = heads_of(grad_block)
    scores = (
        jnp.einsum("qhd,khd->hqk", query_heads, key_heads, preferred_element_type=jnp.float32)
        * score_scale
    )
    scores = jnp.where(allowed[None], scores, masked_score)
    soft_weights = jnp.exp(scores - logsum_block[..., None])
    grad_weights = jnp.einsum(
        "qhd,khd->hqk", grad_heads, value_heads, preferred_element_type=jnp.float32
    )
    inner_sum = jnp.sum(soft_weights * grad_weights, axis=-1, keepdims=True)
    grad_scores = (soft_weights * (grad_weights - inner_sum)).astype(jnp.bfloat16)
    grad_query = (
        jnp.einsum("hqk,khd->qhd", grad_scores, key_heads, preferred_element_type=jnp.float32)
        * score_scale
    )
    grad_key = (
        jnp.einsum("hqk,qhd->khd", grad_scores, query_heads, preferred_element_type=jnp.float32)
        * score_scale
    )
    grad_value = jnp.einsum(
        "hqk,qhd->khd",
        soft_weights.astype(jnp.bfloat16),
        grad_heads,
        preferred_element_type=jnp.float32,
    )
    return (
        grad_query.reshape(query_block.shape),
        grad_key.reshape(grad_key.shape[0], -1),
        grad_value.reshape(grad_value.shape[0], -1),
    )


def swap_sum(partial):
    low = partial.astype(jnp.bfloat16)
    if lax.axis_size("tensor") == 2:
        other = lax.ppermute(low, "tensor", [(0, 1), (1, 0)])
        return low.astype(jnp.float32) + other.astype(jnp.float32)
    return lax.psum(low, "tensor").astype(jnp.float32)


def pairs(mask):
    return [(i, i ^ mask) for i in range(16)]


def add_low(*terms):
    total = terms[0].astype(jnp.float32)
    for term in terms[1:]:
        total = total + term.astype(jnp.float32)
    return total


def z_scatter(own, z_index):
    def block(offset):
        return lax.dynamic_index_in_dim(own, jnp.clip(z_index + offset, 0, 3), 0, keepdims=False)

    up = down = None
    for step in range(1, 4):
        up_perm = [(i, i + 4) for i in range(16) if i // 4 <= step - 1 and i // 4 < 3]
        down_perm = [(i, i - 4) for i in range(16) if i // 4 >= 4 - step and i // 4 > 0]
        up_send, down_send = block(4 - step), block(step - 4)
        if up is not None:
            up_send = add_low(up_send, up).astype(jnp.bfloat16)
            down_send = add_low(down_send, down).astype(jnp.bfloat16)
        up = lax.ppermute(up_send, "dp", up_perm)
        down = lax.ppermute(down_send, "dp", down_perm)
    return add_low(block(0), up, down)


def plane_scatter(parts, first):
    low = jnp.bfloat16
    got_diag = lax.ppermute(parts[3], "dp", pairs(first))
    got_own = lax.ppermute(parts[first], "dp", pairs(first))
    passed = add_low(parts[3 - first], got_diag).astype(low)
    got_last = lax.ppermute(passed, "dp", pairs(3 - first))
    return add_low(parts[0], got_own, got_last).astype(low)


def quarter_products(rows_side, column_side, mine):
    turned = rows_side.T.reshape(4, 4, rows_side.shape[1] // 16, rows_side.shape[0])
    out = []
    for flip in range(4):
        part = lax.dynamic_index_in_dim(turned, mine ^ flip, 1, keepdims=False)
        product = product_plain(part.reshape(-1, part.shape[2]), column_side)
        out.append(product.astype(jnp.bfloat16).reshape(4, -1, column_side.shape[1]))
    return out


def stacked(*products):
    return [jnp.concatenate(part, axis=1) for part in zip(*products)]


def plane_gather(own_half, mask_list=(1, 2, 3)):
    got = [lax.ppermute(own_half, "dp", pairs(mask)) for mask in mask_list]
    other = [lax.ppermute(part, "tensor", [(0, 1), (1, 0)]) for part in got]
    return got + other


def ff_parts(gate, up, grad_mixed):
    sig = 1.0 / (1.0 + jnp.exp(-gate))
    act = gate * sig
    low = jnp.bfloat16
    return (
        (act * up).astype(low),
        (grad_mixed * up * sig * (1.0 + gate * (1.0 - sig))).astype(low),
        (grad_mixed * act).astype(low),
    )


def ff_kernel(in_ref, out_ref, gate_ref, up_ref, down_ref, sum_ref, back_ref, sum_acc, back_acc):
    step = pl.program_id(0)

    @pl.when(step == 0)
    def _():
        sum_acc[...] = jnp.zeros_like(sum_acc)
        back_acc[...] = jnp.zeros_like(back_acc)

    normed = in_ref[...]
    mixed, grad_gate, grad_up = ff_parts(
        product_plain(normed, gate_ref[...]),
        product_plain(normed, up_ref[...]),
        product_with_rows(out_ref[...], down_ref[...]),
    )
    sum_acc[...] += product_plain(mixed, down_ref[...])
    back_acc[...] += product_with_rows(grad_gate, gate_ref[...]) + product_with_rows(
        grad_up, up_ref[...]
    )

    @pl.when(step == pl.num_programs(0) - 1)
    def _():
        sum_ref[...] = sum_acc[...].astype(sum_ref.dtype)
        back_ref[...] = back_acc[...].astype(back_ref.dtype)


def ff_both(normed, grad_out, w_gate, w_up, w_down):
    frames, width = normed.shape
    units = w_gate.shape[1]
    tile = min(512, units)
    while units % tile:
        tile -= 128
    whole = pl.BlockSpec((frames, width), lambda j: (0, 0))
    column = pl.BlockSpec((width, tile), lambda j: (0, j))
    return pl.pallas_call(
        ff_kernel,
        grid=(units // tile,),
        in_specs=[whole, whole, column, column, pl.BlockSpec((tile, width), lambda j: (j, 0))],
        out_specs=[whole, whole],
        out_shape=[jax.ShapeDtypeStruct((frames, width), jnp.bfloat16)] * 2,
        scratch_shapes=[pltpu.VMEM((frames, width), jnp.float32)] * 2,
        compiler_params=pltpu.CompilerParams(vmem_limit_bytes=44 * 2**20),
        cost_estimate=pl.CostEstimate(
            flops=12 * frames * width * units,
            bytes_accessed=6 * width * units + 8 * frames * width,
            transcendentals=frames * units,
        ),
    )(normed, grad_out, w_gate, w_up, w_down)


def share_kernel(_, in_ref, out_ref, gate_ref, up_ref, down_ref, grad_ref, acc):
    step = pl.program_id(0)
    normed, grad_out = in_ref[...], out_ref[...]
    mixed, grad_gate, grad_up = ff_parts(
        product_plain(normed, gate_ref[...]),
        product_plain(normed, up_ref[...]),
        product_with_rows(grad_out, down_ref[...]),
    )
    fresh = (
        product_over_rows(grad_out, mixed),
        product_over_rows(normed, grad_gate),
        product_over_rows(normed, grad_up),
    )
    for index, term in enumerate(fresh):

        @pl.when(step == 0)
        def _():
            acc[index] = term

        @pl.when(step != 0)
        def _():
            acc[index] += term

    @pl.when(step == pl.num_programs(0) - 1)
    def _():
        rows = grad_ref.shape[2]
        for block in range(grad_ref.shape[0]):
            for index in range(3):
                grad_ref[block, index] = acc[index, block * rows : (block + 1) * rows].astype(
                    grad_ref.dtype
                )


def ff_share(normed, grad_out, w_gate, w_up, w_down, first_tile, tile):
    frames, width = normed.shape
    chunk = 512
    rows = pl.BlockSpec((chunk, width), lambda j, first: (j, 0))
    column = pl.BlockSpec((width, tile), lambda j, first: (0, first[0]))
    return pl.pallas_call(
        share_kernel,
        grid_spec=pltpu.PrefetchScalarGridSpec(
            num_scalar_prefetch=1,
            grid=(frames // chunk,),
            in_specs=[
                rows,
                rows,
                column,
                column,
                pl.BlockSpec((tile, width), lambda j, first: (first[0], 0)),
            ],
            out_specs=pl.BlockSpec((4, 3, width // 4, tile), lambda j, first: (0, 0, 0, 0)),
            scratch_shapes=[pltpu.VMEM((3, width, tile), jnp.float32)],
        ),
        out_shape=jax.ShapeDtypeStruct((4, 3, width // 4, tile), jnp.bfloat16),
        compiler_params=pltpu.CompilerParams(vmem_limit_bytes=44 * 2**20),
        cost_estimate=pl.CostEstimate(
            flops=12 * frames * width * tile,
            bytes_accessed=4 * frames * width + 12 * width * tile,
            transcendentals=frames * tile,
        ),
    )(first_tile.reshape(1), normed, grad_out, w_gate, w_up, w_down)


def spread_units(mine, plane, parts=3):
    blocks = mine.reshape(3, 4, mine.shape[1] // 4, mine.shape[2]).astype(jnp.bfloat16)
    got = []
    for flip in range(4):
        part = lax.dynamic_index_in_dim(blocks, plane ^ flip, 1, keepdims=False)
        got.append(part if flip == 0 else lax.ppermute(part, "dp", pairs(flip)))
    got = jnp.stack(got)
    columns = [
        lax.dynamic_index_in_dim(got, plane ^ owner, 0, keepdims=False) for owner in range(4)
    ]
    return jnp.concatenate(columns, axis=2).astype(jnp.float32)


def generic_sum(rows_side, column_side):
    return lax.psum_scatter(
        product_over_rows(rows_side, column_side).astype(jnp.bfloat16),
        "dp",
        scatter_dimension=0,
        tiled=True,
    ).astype(jnp.float32)


def vector_sum(vectors):
    if lax.axis_size("dp") == 16:
        for mask in (1, 2, 4, 8):
            vectors = vectors + lax.ppermute(vectors, "dp", pairs(mask))
    else:
        vectors = lax.psum(vectors, "dp")
    share = vectors.shape[1] // (lax.axis_size("dp") * lax.axis_size("tensor"))
    index = lax.axis_index("dp") * lax.axis_size("tensor") + lax.axis_index("tensor")
    return lax.dynamic_slice_in_dim(vectors, index * share, share, 1)


def on_device(
    hidden_in,
    out_grad,
    prompt_states,
    row_split,
    prompt_len,
    gain_attn,
    bias_attn,
    gain_cross,
    bias_cross,
    gain_ff,
    bias_ff,
    w_query,
    w_key,
    w_value,
    w_out,
    c_query,
    c_key,
    c_value,
    c_out,
    w_gate,
    w_up,
    w_down,
):
    low = jnp.bfloat16
    known = lax.axis_size("dp") == 16 and lax.axis_size("tensor") == 2
    frame_count = hidden_in.shape[0]
    plane, level = lax.axis_index("dp") % 4, lax.axis_index("dp") // 4
    grad_ff_out = out_grad.astype(low)

    def half_of(values):
        return lax.dynamic_slice_in_dim(
            values, lax.axis_index("tensor") * (frame_count // 2), frame_count // 2, 0
        )

    if known:
        frames_out = jnp.concatenate([grad_ff_out, *plane_gather(half_of(grad_ff_out))])
    positions = jnp.arange(frame_count, dtype=jnp.int32)
    split_here = row_split[0]
    row_ids = (positions >= split_here).astype(jnp.int32)
    tables = rotary_tables((positions - row_ids * split_here).astype(jnp.float32), w_query.shape[1])
    key_index = jnp.arange(2 * PROMPT, dtype=jnp.int32)
    key_rows = key_index // PROMPT
    key_live = key_index % PROMPT < jnp.where(key_rows == 0, prompt_len[0], prompt_len[1])
    self_ok = row_ids[:, None] == row_ids[None, :]
    cross_ok = (row_ids[:, None] == key_rows[None, :]) & key_live[None, :]

    normed, scaled_one, inverse_one = normalize(hidden_in, gain_attn, bias_attn)
    input_one = normed.astype(low)
    query_one = rotate(product_plain(input_one, w_query), tables).astype(low)
    key_one = rotate(product_plain(input_one, w_key), tables).astype(low)
    value_one = product_plain(input_one, w_value).astype(low)
    attended_one, logsum_one = attend_forward(query_one, heads_of(key_one), heads_of(value_one), self_ok)
    resid_one = hidden_in + swap_sum(product_plain(attended_one, w_out))

    normed, scaled_two, inverse_two = normalize(resid_one, gain_cross, bias_cross)
    input_two = normed.astype(low)
    cross_query = product_plain(input_two, c_query).astype(low)
    context_flat = prompt_states.reshape(2 * PROMPT, prompt_states.shape[2])
    cross_key = product_plain(context_flat, c_key).astype(low)
    cross_value = product_plain(context_flat, c_value).astype(low)
    attended_two, logsum_two = attend_forward(
        cross_query, heads_of(cross_key), heads_of(cross_value), cross_ok
    )
    resid_two = resid_one + swap_sum(product_plain(attended_two, c_out))

    normed, scaled_three, inverse_three = normalize(resid_two, gain_ff, bias_ff)
    input_three = normed.astype(low)
    if known:
        frames_in = jnp.concatenate([input_three, *plane_gather(half_of(input_three))])
    sum_part, back_part = ff_both(input_three, grad_ff_out, w_gate, w_up, w_down)
    result = resid_two + swap_sum(sum_part)
    normed_grad_three = swap_sum(back_part)
    if known:
        units = w_gate.shape[1] // 4
        tile = 256
        shares = []
        for part in range(units // tile):
            own = ff_share(
                frames_in, frames_out, w_gate, w_up, w_down, plane * (units // tile) + part, tile
            )
            shares.append(z_scatter(own, level))
        spread = spread_units(jnp.concatenate(shares, axis=2), plane)
        grad_w_down, grad_w_gate, grad_w_up = spread[0].T, spread[1], spread[2]
    else:
        gate_pre = product_plain(input_three, w_gate)
        up_pre = product_plain(input_three, w_up)
        grad_mixed = product_with_rows(grad_ff_out, w_down)
        mixed, grad_gate, grad_up = ff_parts(gate_pre, up_pre, grad_mixed)
        grad_w_down = generic_sum(grad_ff_out, mixed).T
        grad_w_gate = generic_sum(input_three, grad_gate)
        grad_w_up = generic_sum(input_three, grad_up)
    back_three, grad_gain_ff, grad_bias_ff = normalize_back(
        normed_grad_three, scaled_three, inverse_three, gain_ff
    )
    grad_two = out_grad + back_three
    grad_cross_out = grad_two.astype(low)
    grad_attended_two = product_with_rows(grad_cross_out, c_out).astype(low)
    cross_query_grad, cross_key_grad, cross_value_grad = attend_backward(
        cross_query,
        heads_of(cross_key),
        heads_of(cross_value),
        cross_ok,
        grad_attended_two,
        logsum_two,
    )
    cross_query_grad = cross_query_grad.astype(low)
    cross_key_grad = cross_key_grad.astype(low)
    cross_value_grad = cross_value_grad.astype(low)
    if known:
        context_part = quarter_products(
            context_flat, jnp.concatenate([cross_key_grad, cross_value_grad], axis=1), plane
        )
        width = cross_key_grad.shape[1]
        first = plane_scatter(
            stacked(
                quarter_products(grad_cross_out, attended_two, plane),
                [part[..., :width] for part in context_part],
            ),
            1,
        )
        second = plane_scatter(
            stacked(
                quarter_products(input_two, cross_query_grad, plane),
                [part[..., width:] for part in context_part],
            ),
            2,
        )
        sums = z_scatter(jnp.concatenate([first, second], axis=1), level)
        r = input_two.shape[1] // 16
        c = context_flat.shape[1] // 16
        grad_c_out, grad_c_key = sums[:r].T, sums[r : r + c]
        grad_c_query, grad_c_value = sums[r + c : 2 * r + c], sums[2 * r + c :]
    else:
        grad_c_out = generic_sum(grad_cross_out, attended_two).T
        grad_c_query = generic_sum(input_two, cross_query_grad)
        grad_c_key = generic_sum(context_flat, cross_key_grad)
        grad_c_value = generic_sum(context_flat, cross_value_grad)
    normed_grad_two = swap_sum(product_with_rows(cross_query_grad, c_query))
    back_two, grad_gain_cross, grad_bias_cross = normalize_back(
        normed_grad_two, scaled_two, inverse_two, gain_cross
    )
    grad_one = grad_two + back_two
    grad_self_out = grad_one.astype(low)
    grad_attended_one = product_with_rows(grad_self_out, w_out).astype(low)
    query_grad, key_grad, value_grad = attend_backward(
        query_one, heads_of(key_one), heads_of(value_one), self_ok, grad_attended_one, logsum_one
    )
    query_grad = rotate_back(query_grad, tables).astype(low)
    key_grad = rotate_back(key_grad, tables).astype(low)
    value_grad = value_grad.astype(low)
    if known:
        first = plane_scatter(
            stacked(
                quarter_products(grad_self_out, attended_one, plane),
                quarter_products(input_one, value_grad, plane),
            ),
            1,
        )
        second = plane_scatter(
            stacked(
                quarter_products(input_one, query_grad, plane),
                quarter_products(input_one, key_grad, plane),
            ),
            2,
        )
        sums = z_scatter(jnp.concatenate([first, second], axis=1), level)
        r = input_one.shape[1] // 16
        grad_w_out, grad_w_value = sums[:r].T, sums[r : 2 * r]
        grad_w_query, grad_w_key = sums[2 * r : 3 * r], sums[3 * r :]
    else:
        grad_w_out = generic_sum(grad_self_out, attended_one).T
        grad_w_query = generic_sum(input_one, query_grad)
        grad_w_key = generic_sum(input_one, key_grad)
        grad_w_value = generic_sum(input_one, value_grad)
    normed_grad_one = swap_sum(
        product_with_rows(query_grad, w_query)
        + product_with_rows(key_grad, w_key)
        + product_with_rows(value_grad, w_value)
    )
    back_one, grad_gain_attn, grad_bias_attn = normalize_back(
        normed_grad_one, scaled_one, inverse_one, gain_attn
    )
    grad_hidden = grad_one + back_one
    vectors = vector_sum(
        jnp.stack(
            [
                grad_gain_attn,
                grad_bias_attn,
                grad_gain_cross,
                grad_bias_cross,
                grad_gain_ff,
                grad_bias_ff,
            ]
        )
    )
    return (
        result,
        grad_hidden,
        vectors[0],
        vectors[1],
        vectors[2],
        vectors[3],
        vectors[4],
        vectors[5],
        grad_w_query,
        grad_w_key,
        grad_w_value,
        grad_w_out,
        grad_c_query,
        grad_c_key,
        grad_c_value,
        grad_c_out,
        grad_w_gate,
        grad_w_up,
        grad_w_down,
    )


def solution(mesh):
    in_specs = (
        P("dp", None),
        P("dp", None),
        P("dp", None, None),
        P("dp"),
        P("dp"),
        P(),
        P(),
        P(),
        P(),
        P(),
        P(),
        P(None, "tensor"),
        P(None, "tensor"),
        P(None, "tensor"),
        P("tensor", None),
        P(None, "tensor"),
        P(None, "tensor"),
        P(None, "tensor"),
        P("tensor", None),
        P(None, "tensor"),
        P(None, "tensor"),
        P("tensor", None),
    )
    out_specs = (
        P("dp", None),
        P("dp", None),
        P(("dp", "tensor")),
        P(("dp", "tensor")),
        P(("dp", "tensor")),
        P(("dp", "tensor")),
        P(("dp", "tensor")),
        P(("dp", "tensor")),
        P("dp", "tensor"),
        P("dp", "tensor"),
        P("dp", "tensor"),
        P("tensor", "dp"),
        P("dp", "tensor"),
        P("dp", "tensor"),
        P("dp", "tensor"),
        P("tensor", "dp"),
        P("dp", "tensor"),
        P("dp", "tensor"),
        P("tensor", "dp"),
    )
    return jax.shard_map(
        on_device, mesh=mesh, in_specs=in_specs, out_specs=out_specs, check_vma=False
    )
```

```python
import functools
import math

import jax
import jax.numpy as jnp
from jax import lax
from jax.experimental import pallas as pl
from jax.experimental.pallas import tpu as pltpu
from jax.sharding import PartitionSpec as P

PROMPT = 128
HEAD = 64
PLANE = 4
LEVELS = 4

low = jnp.bfloat16
f32 = jnp.float32
sds = jax.ShapeDtypeStruct


norm_eps = 1e-05
score_scale = 0.125
masked_score = -1e30


def product_plain(left_side, right_side):
    return jnp.dot(left_side, right_side, preferred_element_type=jnp.float32)


def product_over_rows(left_side, right_side):
    return lax.dot_general(
        left_side, right_side, (((0,), (0,)), ((), ())), preferred_element_type=jnp.float32
    )


def product_with_rows(left_side, right_side):
    return lax.dot_general(
        left_side, right_side, (((1,), (1,)), ((), ())), preferred_element_type=jnp.float32
    )


def rotary_tables(positions, width):
    dim_index = jnp.arange(width) % HEAD
    freq_index = (dim_index % 16).astype(jnp.float32)
    inverse_freq = jnp.exp(freq_index * (-math.log(10000.0) / 16.0))
    angles = positions[:, None] * inverse_freq[None, :]
    cosine = jnp.cos(angles)
    sine_part = jnp.sin(angles)
    cos_table = jnp.where(dim_index < 32, cosine, 1.0)
    sin_lower = jnp.where(dim_index < 16, -sine_part, 0.0)
    sin_upper = jnp.where((dim_index >= 16) & (dim_index < 32), sine_part, 0.0)
    return (cos_table, sin_lower, sin_upper)


def rotate(values, tables):
    cos_table, sin_lower, sin_upper = tables
    return (
        values * cos_table
        + jnp.roll(values, -16, axis=1) * sin_lower
        + jnp.roll(values, 16, axis=1) * sin_upper
    )


def rotate_back(incoming, tables):
    cos_table, sin_lower, sin_upper = tables
    return (
        incoming * cos_table
        + jnp.roll(incoming * sin_lower, 16, axis=1)
        + jnp.roll(incoming * sin_upper, -16, axis=1)
    )


def normalize(values, norm_gain, norm_shift):
    average = jnp.mean(values, axis=-1, keepdims=True)
    centered = values - average
    variance = jnp.mean(centered * centered, axis=-1, keepdims=True)
    inverse = lax.rsqrt(variance + norm_eps)
    scaled = centered * inverse
    return (scaled * norm_gain + norm_shift, scaled, inverse)


def normalize_back(incoming, scaled, inverse, norm_gain):
    grad_gain = jnp.sum(incoming * scaled, axis=0)
    grad_shift = jnp.sum(incoming, axis=0)
    weighted = incoming * norm_gain
    grad_input = inverse * (
        weighted
        - jnp.mean(weighted, axis=-1, keepdims=True)
        - scaled * jnp.mean(weighted * scaled, axis=-1, keepdims=True)
    )
    return (grad_input, grad_gain, grad_shift)


def heads_of(values):
    return values.reshape(values.shape[0], values.shape[1] // HEAD, HEAD)


def attend_forward(query_block, key_heads, value_heads, allowed):
    query_heads = heads_of(query_block)
    scores = (
        jnp.einsum("qhd,khd->hqk", query_heads, key_heads, preferred_element_type=jnp.float32)
        * score_scale
    )
    scores = jnp.where(allowed[None], scores, masked_score)
    largest = jnp.max(scores, axis=-1, keepdims=True)
    exp_scores = jnp.exp(scores - largest)
    totals = jnp.sum(exp_scores, axis=-1, keepdims=True)
    soft_weights = (exp_scores / totals).astype(jnp.bfloat16)
    mixed_heads = jnp.einsum(
        "hqk,khd->qhd", soft_weights, value_heads, preferred_element_type=jnp.float32
    )
    mixed_flat = mixed_heads.reshape(query_block.shape[0], query_block.shape[1]).astype(
        jnp.bfloat16
    )
    return (mixed_flat, largest[..., 0] + jnp.log(totals[..., 0]))


def attend_backward(query_block, key_heads, value_heads, allowed, grad_block, logsum_block):
    query_heads = heads_of(query_block)
    grad_heads = heads_of(grad_block)
    scores = (
        jnp.einsum("qhd,khd->hqk", query_heads, key_heads, preferred_element_type=jnp.float32)
        * score_scale
    )
    scores = jnp.where(allowed[None], scores, masked_score)
    soft_weights = jnp.exp(scores - logsum_block[..., None])
    grad_weights = jnp.einsum(
        "qhd,khd->hqk", grad_heads, value_heads, preferred_element_type=jnp.float32
    )
    inner_sum = jnp.sum(soft_weights * grad_weights, axis=-1, keepdims=True)
    grad_scores = (soft_weights * (grad_weights - inner_sum)).astype(jnp.bfloat16)
    grad_query = (
        jnp.einsum("hqk,khd->qhd", grad_scores, key_heads, preferred_element_type=jnp.float32)
        * score_scale
    )
    grad_key = (
        jnp.einsum("hqk,qhd->khd", grad_scores, query_heads, preferred_element_type=jnp.float32)
        * score_scale
    )
    grad_value = jnp.einsum(
        "hqk,qhd->khd",
        soft_weights.astype(jnp.bfloat16),
        grad_heads,
        preferred_element_type=jnp.float32,
    )
    return (
        grad_query.reshape(query_block.shape),
        grad_key.reshape(grad_key.shape[0], -1),
        grad_value.reshape(grad_value.shape[0], -1),
    )


def swap_sum(partial):
    low = partial.astype(jnp.bfloat16)
    if lax.axis_size("tensor") == 2:
        other = lax.ppermute(low, "tensor", [(0, 1), (1, 0)])
        return low.astype(jnp.float32) + other.astype(jnp.float32)
    return lax.psum(low, "tensor").astype(jnp.float32)


def pairs(mask):
    return [(i, i ^ mask) for i in range(16)]


def vector_sum(vectors):
    if lax.axis_size("dp") == PLANE * LEVELS:
        for mask in (1, 2, 4, 8):
            vectors = vectors + lax.ppermute(vectors, "dp", pairs(mask))
    else:
        vectors = lax.psum(vectors, "dp")
    share = vectors.shape[1] // (lax.axis_size("dp") * lax.axis_size("tensor"))
    index = lax.axis_index("dp") * lax.axis_size("tensor") + lax.axis_index("tensor")
    return lax.dynamic_slice_in_dim(vectors, index * share, share, 1)


def generic_sum(rows_side, column_side):
    return lax.psum_scatter(
        product_over_rows(rows_side, column_side).astype(jnp.bfloat16),
        "dp",
        scatter_dimension=0,
        tiled=True,
    ).astype(jnp.float32)


def add_low(*terms):
    total = terms[0].astype(jnp.float32)
    for term in terms[1:]:
        total = total + term.astype(jnp.float32)
    return total


def z_halve(send, keep, level):
    upper = level // 2
    got = lax.ppermute(send, "dp", pairs(PLANE))

    def half(values, index):
        return lax.dynamic_index_in_dim(values, index, 0, keepdims=False)

    passed = add_low(half(keep, 1 - upper), half(got, 1 - upper)).astype(low)
    last = lax.ppermute(passed, "dp", pairs(2 * PLANE))
    return add_low(half(keep, upper), half(got, upper), last)


def z_scatter(own, level):
    split = own.reshape(2, 2, *own.shape[1:])

    def half(parity):
        return lax.dynamic_index_in_dim(split, parity, 1, keepdims=False)

    return z_halve(half(1 - level % 2), half(level % 2), level)


def plane_scatter(parts, first):
    got_diag = lax.ppermute(parts[3], "dp", pairs(first))
    got_own = lax.ppermute(parts[first], "dp", pairs(first))
    passed = add_low(parts[3 - first], got_diag).astype(low)
    got_last = lax.ppermute(passed, "dp", pairs(3 - first))
    return add_low(parts[0], got_own, got_last).astype(low)


def plane_gather(own_half, mask_list=(1, 2, 3)):
    got = [lax.ppermute(own_half, "dp", pairs(mask)) for mask in mask_list]
    other = [lax.ppermute(part, "tensor", [(0, 1), (1, 0)]) for part in got]
    return got + other


def ff_parts(gate, up, grad_mixed):
    sig = 1.0 / (1.0 + jnp.exp(-gate))
    act = gate * sig
    return (
        (act * up).astype(low),
        (grad_mixed * up * sig * (1.0 + gate * (1.0 - sig))).astype(low),
        (grad_mixed * act).astype(low),
    )


def ff_kernel(in_ref, out_ref, gate_ref, up_ref, down_ref, sum_ref, back_ref, sum_acc, back_acc):
    step = pl.program_id(0)

    @pl.when(step == 0)
    def _():
        sum_acc[...] = jnp.zeros_like(sum_acc)
        back_acc[...] = jnp.zeros_like(back_acc)

    normed = in_ref[...]
    mixed, grad_gate, grad_up = ff_parts(
        product_plain(normed, gate_ref[...]),
        product_plain(normed, up_ref[...]),
        product_with_rows(out_ref[...], down_ref[...]),
    )
    sum_acc[...] += product_plain(mixed, down_ref[...])
    back_acc[...] += product_with_rows(grad_gate, gate_ref[...]) + product_with_rows(
        grad_up, up_ref[...]
    )

    @pl.when(step == pl.num_programs(0) - 1)
    def _():
        sum_ref[...] = sum_acc[...].astype(sum_ref.dtype)
        back_ref[...] = back_acc[...].astype(back_ref.dtype)


def ff_both(normed, grad_out, w_gate, w_up, w_down):
    frames, width = normed.shape
    units = w_gate.shape[1]
    tile = min(512, units)
    while units % tile:
        tile -= 128
    whole = pl.BlockSpec((frames, width), lambda j: (0, 0))
    column = pl.BlockSpec((width, tile), lambda j: (0, j))
    return pl.pallas_call(
        ff_kernel,
        grid=(units // tile,),
        in_specs=[whole, whole, column, column, pl.BlockSpec((tile, width), lambda j: (j, 0))],
        out_specs=[whole, whole],
        out_shape=[jax.ShapeDtypeStruct((frames, width), jnp.bfloat16)] * 2,
        scratch_shapes=[pltpu.VMEM((frames, width), jnp.float32)] * 2,
        compiler_params=pltpu.CompilerParams(vmem_limit_bytes=44 * 2**20),
        cost_estimate=pl.CostEstimate(
            flops=12 * frames * width * units,
            bytes_accessed=6 * width * units + 8 * frames * width,
            transcendentals=frames * units,
        ),
    )(normed, grad_out, w_gate, w_up, w_down)


def share_kernel(info, in_ref, out_ref, gate_ref, up_ref, down_ref, send_ref, keep_ref, acc):
    step = pl.program_id(0)
    normed, grad_out = in_ref[...], out_ref[...]
    mixed, grad_gate, grad_up = ff_parts(
        product_plain(normed, gate_ref[...]),
        product_plain(normed, up_ref[...]),
        product_with_rows(grad_out, down_ref[...]),
    )
    fresh = (
        product_over_rows(grad_out, mixed),
        product_over_rows(normed, grad_gate),
        product_over_rows(normed, grad_up),
    )
    for index, term in enumerate(fresh):

        @pl.when(step == 0)
        def _():
            acc[index] = term

        @pl.when(step != 0)
        def _():
            acc[index] += term

    @pl.when(step == pl.num_programs(0) - 1)
    def _():
        rows = send_ref.shape[2]
        for pair in range(2):
            for index in range(3):
                for ref, parity in ((send_ref, 1 - info[1]), (keep_ref, info[1])):
                    start = pl.multiple_of((2 * pair + parity) * rows, rows)
                    ref[pair, index] = acc[index, pl.ds(start, rows), :].astype(ref.dtype)


def ff_share(info, normed, grad_out, w_gate, w_up, w_down, tile):
    frames, width = normed.shape
    chunk = 512
    rows = pl.BlockSpec((chunk, width), lambda j, info: (j, 0))
    column = pl.BlockSpec((width, tile), lambda j, info: (0, info[0]))
    half = (LEVELS // 2, 3, width // LEVELS, tile)
    return pl.pallas_call(
        share_kernel,
        grid_spec=pltpu.PrefetchScalarGridSpec(
            num_scalar_prefetch=1,
            grid=(frames // chunk,),
            in_specs=[
                rows,
                rows,
                column,
                column,
                pl.BlockSpec((tile, width), lambda j, info: (info[0], 0)),
            ],
            out_specs=[pl.BlockSpec(half, lambda j, info: (0, 0, 0, 0))] * 2,
            scratch_shapes=[pltpu.VMEM((3, width, tile), f32)],
        ),
        out_shape=[sds(half, low)] * 2,
        compiler_params=pltpu.CompilerParams(vmem_limit_bytes=44 * 2**20),
        cost_estimate=pl.CostEstimate(
            flops=12 * frames * width * tile,
            bytes_accessed=4 * frames * width + 12 * width * tile,
            transcendentals=frames * tile,
        ),
    )(info, normed, grad_out, w_gate, w_up, w_down)


def spread_units(mine, plane, parts=3):
    blocks = mine.reshape(3, 4, mine.shape[1] // 4, mine.shape[2]).astype(jnp.bfloat16)
    got = []
    for flip in range(4):
        part = lax.dynamic_index_in_dim(blocks, plane ^ flip, 1, keepdims=False)
        got.append(part if flip == 0 else lax.ppermute(part, "dp", pairs(flip)))
    got = jnp.stack(got)
    columns = [
        lax.dynamic_index_in_dim(got, plane ^ owner, 0, keepdims=False) for owner in range(4)
    ]
    return jnp.concatenate(columns, axis=2).astype(jnp.float32)


def turn(values, cos, lower, upper):
    width = values.shape[1]
    return (values * cos + pltpu.roll(values, width - 16, 1) * lower + pltpu.roll(values, 16, 1) * upper)

def turn_back(values, cos, lower, upper):
    width = values.shape[1]
    return (values * cos + pltpu.roll(values * lower, 16, 1) + pltpu.roll(values * upper, width - 16, 1))

def normed_rows(values, gain, shift):
    average = jnp.mean(values, axis=-1, keepdims=True)
    centered = values - average
    variance = jnp.mean(centered * centered, axis=-1, keepdims=True)
    return centered * lax.rsqrt(variance + norm_eps) * gain + shift

def over_rows(rows, body, chunk=32):
    @pl.loop(0, rows // chunk, unroll=min(4, rows // chunk))
    def _(i):
        body(pl.ds(pl.multiple_of(i * chunk, chunk), chunk))

def attend(q, k, v, mask, lse_ref):
    q_turned = (q * jnp.bfloat16(0.125)).T
    v_turned = v.T
    outs = []
    for h in range(q.shape[1] // HEAD):
        c = slice(h * HEAD, (h + 1) * HEAD)
        s = product_plain(k[:, c], q_turned[c, :]) + mask
        m = jnp.max(s, axis=0, keepdims=True)
        e = jnp.exp(s - m)
        total = jnp.sum(e, axis=0, keepdims=True)
        o = product_plain(v_turned[c, :], e.astype(low)) * (1.0 / total)
        outs.append(o)
        lse_ref[h : h + 1, :] = m + jnp.log(total)
    return jnp.concatenate(outs, axis=0).T.astype(low)


def attend_back(q, k, v, g, mask, lse):
    scaled = q * jnp.bfloat16(0.125)
    q_turned = scaled.T
    g_turned = g.T
    k_turned = k.T
    dq, dk, dv = [], [], []
    for h in range(q.shape[1] // HEAD):
        c = slice(h * HEAD, (h + 1) * HEAD)
        p = jnp.exp(product_plain(k[:, c], q_turned[c, :]) + (mask - lse[h : h + 1, :]))
        dp = product_plain(v[:, c], g_turned[c, :])
        inner = jnp.sum(p * dp, axis=0, keepdims=True)
        ds = (p * (dp - inner)).astype(low)
        dq.append(product_plain(k_turned[c, :], ds))
        dk.append(product_plain(ds, scaled[:, c]))
        dv.append(product_plain(p.astype(low), g[:, c]))
    return (
        jnp.concatenate(dq, axis=0).T * 0.125,
        jnp.concatenate(dk, axis=1),
        jnp.concatenate(dv, axis=1),
    )


def self_mask(split, T):
    r=lax.broadcasted_iota(jnp.int32,(T,T),0)>=split
    c=lax.broadcasted_iota(jnp.int32,(T,T),1)>=split
    return jnp.where(r==c,0.0,masked_score).astype(f32)

def cross_mask(split, first, second, T, K):
    r = lax.broadcasted_iota(jnp.int32, (K, T), 1) >= split
    c = lax.broadcasted_iota(jnp.int32, (K, T), 0)
    least = jnp.where(r, K // 2, 0)
    most = jnp.where(r, K // 2 + second, first)
    return jnp.where((c >= least) & (c < most), 0.0, masked_score).astype(f32)


def self_kernel(info, hid, gain, shift, wq, wk, wv, wo, cos, lower, upper, in1, q, k, v, att, lse, part, acc, mask):
    step=pl.program_id(0)
    T=hid.shape[0]
    @pl.when(step==0)
    def _():
        def rows(r):
            in1[r,:]=normed_rows(hid[r,:],gain[...],shift[...]).astype(low)
        over_rows(T,rows)
        mask[...]=self_mask(info[0],T)
    n=in1[...]
    tabs=(cos[...],lower[...],upper[...])
    q[...]=turn(product_plain(n,wq[...]),*tabs).astype(low)
    k[...]=turn(product_plain(n,wk[...]),*tabs).astype(low)
    v[...]=product_plain(n,wv[...]).astype(low)
    a=attend(q[...],k[...],v[...],mask[...],lse)
    att[...]=a
    term=product_plain(a,wo[...])
    @pl.when(step==0)
    def _(): acc[...]=term
    @pl.when(step!=0)
    def _(): acc[...]+=term
    @pl.when(step==pl.num_programs(0)-1)
    def _(): part[...]=acc[...].astype(low)

def specs(T,D,tile):
    whole=pl.BlockSpec((T,D),lambda j,*_:(0,0))
    vec=pl.BlockSpec((1,D),lambda j,*_:(0,0))
    col=pl.BlockSpec((D,tile),lambda j,*_:(0,j))
    row=pl.BlockSpec((tile,D),lambda j,*_:(j,0))
    act=pl.BlockSpec((T,tile),lambda j,*_:(0,j))
    tab=pl.BlockSpec((T,tile),lambda j,*_:(0,0))
    lse=pl.BlockSpec((8,T),lambda j,*_:(j,0))
    return whole,vec,col,row,act,tab,lse
PARAMS=dict(compiler_params=pltpu.CompilerParams(vmem_limit_bytes=48*2**20))

def self_forward(info,hid,gain,shift,wq,wk,wv,wo,tabs,tile=256):
    T,D=hid.shape;C=wq.shape[1]
    whole,vec,col,row,act,tab,lse=specs(T,D,tile)
    return pl.pallas_call(self_kernel,grid_spec=pltpu.PrefetchScalarGridSpec(num_scalar_prefetch=1,grid=(C//tile,),
        in_specs=[whole,vec,vec,col,col,col,row,tab,tab,tab],
        out_specs=[whole,act,act,act,act,lse,whole],
        scratch_shapes=[pltpu.VMEM((T,D),f32),pltpu.VMEM((T,T),f32)]),
        out_shape=[sds((T,D),low)]+[sds((T,C),low)]*4+[sds((C//tile*8,T),f32),sds((T,D),low)],
        cost_estimate=pl.CostEstimate(flops=2*T*C*(4*D+2*T*4),bytes_accessed=8*D*C+4*T*D+8*T*D,transcendentals=T*T*C//HEAD),
        **PARAMS)(info,hid,gain,shift,wq,wk,wv,wo,*tabs)

def cross_kernel(info, hid, mine, other, gain, shift, cq, ck, cv, co, res, in2, q, att, lse, part, acc, mask):
    step=pl.program_id(0)
    T=hid.shape[0]
    @pl.when(step==0)
    def _():
        def rows(r):
            x=hid[r,:]+(mine[r,:].astype(f32)+other[r,:].astype(f32))
            res[r,:]=x
            in2[r,:]=normed_rows(x,gain[...],shift[...]).astype(low)
        over_rows(T,rows)
        mask[...]=cross_mask(info[0],info[1],info[2],T,ck.shape[0])
    q[...]=product_plain(in2[...],cq[...]).astype(low)
    a=attend(q[...],ck[...],cv[...],mask[...],lse)
    att[...]=a
    term=product_plain(a,co[...])
    @pl.when(step==0)
    def _(): acc[...]=term
    @pl.when(step!=0)
    def _(): acc[...]+=term
    @pl.when(step==pl.num_programs(0)-1)
    def _(): part[...]=acc[...].astype(low)

def cross_forward(info,hid,mine,other,gain,shift,cq,ck,cv,co,tile=256):
    T,D=hid.shape;C=cq.shape[1];K=ck.shape[0]
    whole,vec,col,row,act,tab,lse=specs(T,D,tile)
    key=pl.BlockSpec((K,tile),lambda j,*_:(0,j))
    return pl.pallas_call(cross_kernel,grid_spec=pltpu.PrefetchScalarGridSpec(num_scalar_prefetch=1,grid=(C//tile,),
        in_specs=[whole,whole,whole,vec,vec,col,key,key,row],
        out_specs=[whole,whole,act,act,lse,whole],
        scratch_shapes=[pltpu.VMEM((T,D),f32),pltpu.VMEM((K,T),f32)]),
        out_shape=[sds((T,D),f32),sds((T,D),low),sds((T,C),low),sds((T,C),low),sds((C//tile*8,T),f32),sds((T,D),low)],
        cost_estimate=pl.CostEstimate(flops=2*T*C*(2*D+2*K*4),bytes_accessed=4*D*C+4*T*D+14*T*D,transcendentals=T*K*C//HEAD),
        **PARAMS)(info,hid,mine,other,gain,shift,cq,ck,cv,co)

def norm_kernel(hid,mine,other,gain,shift,res,out):
    def rows(r):
        x=hid[r,:]+(mine[r,:].astype(f32)+other[r,:].astype(f32))
        res[r,:]=x
        out[r,:]=normed_rows(x,gain[...],shift[...]).astype(low)
    over_rows(hid.shape[0],rows)

def norm_forward(hid,mine,other,gain,shift,block=128):
    T,D=hid.shape
    b=pl.BlockSpec((block,D),lambda j:(j,0)); vec=pl.BlockSpec((1,D),lambda j:(0,0))
    return pl.pallas_call(norm_kernel,grid=(T//block,),in_specs=[b,b,b,vec,vec],out_specs=[b,b],
        out_shape=[sds((T,D),f32),sds((T,D),low)],
        cost_estimate=pl.CostEstimate(flops=10*T*D,bytes_accessed=14*T*D,transcendentals=T),**PARAMS)(hid,mine,other,gain,shift)

def norm_back_rows(x,e,gain,above,sums,gain_acc,shift_acc):
    average=jnp.mean(x,axis=-1,keepdims=True)
    centered=x-average
    variance=jnp.mean(centered*centered,axis=-1,keepdims=True)
    inverse=lax.rsqrt(variance+norm_eps)
    n=centered*inverse
    en=e*n
    w=e*gain
    mean_w=jnp.mean(w,axis=-1,keepdims=True)
    mean_wn=jnp.mean(en*gain,axis=-1,keepdims=True)
    fold=lambda t: jnp.sum(t.reshape(t.shape[0]//8,8,t.shape[1]),axis=0)
    gain_acc[...]+=fold(en)
    shift_acc[...]+=fold(e)
    return above+inverse*(w-mean_w-n*mean_wn)

def norm_back_all(x,mine,other,above,gain,total,total_low,vec,gacc,sacc):
    gacc[...]=jnp.zeros_like(gacc);sacc[...]=jnp.zeros_like(sacc)
    def rows(r):
        e=mine[r,:].astype(f32)+other[r,:].astype(f32)
        t=norm_back_rows(x[r,:],e,gain[...],above[r,:],None,gacc,sacc)
        total[r,:]=t
        if total_low is not None: total_low[r,:]=t.astype(low)
    over_rows(x.shape[0],rows)
    vec[0:1,:]=jnp.sum(gacc[...],axis=0,keepdims=True)
    vec[1:2,:]=jnp.sum(sacc[...],axis=0,keepdims=True)

def cross_back_kernel(info, x, mine, other, above, gain, co, q, ck, cv, lse, cq, total, glow, vec, dq, dk, dv, part, acc, mask, gacc, sacc):
    step=pl.program_id(0)
    T=x.shape[0]
    @pl.when(step==0)
    def _():
        norm_back_all(x,mine,other,above,gain,total,glow,vec,gacc,sacc)
        mask[...]=cross_mask(info[0],info[1],info[2],T,ck.shape[0])
    g=product_with_rows(glow[...],co[...]).astype(low)
    a,b,c=attend_back(q[...],ck[...],cv[...],g,mask[...],lse[...])
    a=a.astype(low)
    dq[...]=a;dk[...]=b.astype(low);dv[...]=c.astype(low)
    term=product_with_rows(a,cq[...])
    @pl.when(step==0)
    def _(): acc[...]=term
    @pl.when(step!=0)
    def _(): acc[...]+=term
    @pl.when(step==pl.num_programs(0)-1)
    def _(): part[...]=acc[...].astype(low)

def cross_backward(info,x,mine,other,above,gain,co,q,ck,cv,lse_a,cq,tile=256):
    T,D=x.shape;C=cq.shape[1];K=ck.shape[0]
    whole,vec,col,row,act,tab,lse=specs(T,D,tile)
    key=pl.BlockSpec((K,tile),lambda j,*_:(0,j))
    two=pl.BlockSpec((2,D),lambda j,*_:(0,0))
    return pl.pallas_call(cross_back_kernel,grid_spec=pltpu.PrefetchScalarGridSpec(num_scalar_prefetch=1,grid=(C//tile,),
        in_specs=[whole,whole,whole,whole,vec,row,act,key,key,lse,col],
        out_specs=[whole,whole,two,act,key,key,whole],
        scratch_shapes=[pltpu.VMEM((T,D),f32),pltpu.VMEM((K,T),f32),pltpu.VMEM((8,D),f32),pltpu.VMEM((8,D),f32)]),
        out_shape=[sds((T,D),f32),sds((T,D),low),sds((2,D),f32),sds((T,C),low),sds((K,C),low),sds((K,C),low),sds((T,D),low)],
        cost_estimate=pl.CostEstimate(flops=2*T*C*(2*D+5*K*4),bytes_accessed=4*D*C+20*T*D,transcendentals=T*K*C//HEAD),
        **PARAMS)(info,x,mine,other,above,gain,co,q,ck,cv,lse_a,cq)

def self_back_kernel(info, x, mine, other, above, gain, wo, q, k, v, lse, wq, wk, wv, cos, lower, upper, total, glow, vec, dq, dk, dv, part, acc, mask, gacc, sacc):
    step=pl.program_id(0)
    T=x.shape[0]
    @pl.when(step==0)
    def _():
        norm_back_all(x,mine,other,above,gain,total,glow,vec,gacc,sacc)
        mask[...]=self_mask(info[0],T)
    g=product_with_rows(glow[...],wo[...]).astype(low)
    a,b,c=attend_back(q[...],k[...],v[...],g,mask[...],lse[...])
    tabs=(cos[...],lower[...],upper[...])
    a=turn_back(a,*tabs).astype(low);b=turn_back(b,*tabs).astype(low);c=c.astype(low)
    dq[...]=a;dk[...]=b;dv[...]=c
    term=product_with_rows(a,wq[...])+product_with_rows(b,wk[...])+product_with_rows(c,wv[...])
    @pl.when(step==0)
    def _(): acc[...]=term
    @pl.when(step!=0)
    def _(): acc[...]+=term
    @pl.when(step==pl.num_programs(0)-1)
    def _(): part[...]=acc[...].astype(low)

def self_backward(info,x,mine,other,above,gain,wo,q,k,v,lse_a,wq,wk,wv,tabs,tile=256):
    T,D=x.shape;C=wq.shape[1]
    whole,vec,col,row,act,tab,lse=specs(T,D,tile)
    two=pl.BlockSpec((2,D),lambda j,*_:(0,0))
    return pl.pallas_call(self_back_kernel,grid_spec=pltpu.PrefetchScalarGridSpec(num_scalar_prefetch=1,grid=(C//tile,),
        in_specs=[whole,whole,whole,whole,vec,row,act,act,act,lse,col,col,col,tab,tab,tab],
        out_specs=[whole,whole,two,act,act,act,whole],
        scratch_shapes=[pltpu.VMEM((T,D),f32),pltpu.VMEM((T,T),f32),pltpu.VMEM((8,D),f32),pltpu.VMEM((8,D),f32)]),
        out_shape=[sds((T,D),f32),sds((T,D),low),sds((2,D),f32)]+[sds((T,C),low)]*3+[sds((T,D),low)],
        cost_estimate=pl.CostEstimate(flops=2*T*C*(4*D+5*T*4),bytes_accessed=8*D*C+20*T*D,transcendentals=T*T*C//HEAD),
        **PARAMS)(info,x,mine,other,above,gain,wo,q,k,v,lse_a,wq,wk,wv,*tabs)

def last_kernel(x,mine,other,above,gain,total,vec,gacc,sacc):
    step=pl.program_id(0)
    @pl.when(step==0)
    def _():
        gacc[...]=jnp.zeros_like(gacc);sacc[...]=jnp.zeros_like(sacc)
    def rows(r):
        e=mine[r,:].astype(f32)+other[r,:].astype(f32)
        total[r,:]=norm_back_rows(x[r,:],e,gain[...],above[r,:],None,gacc,sacc)
    over_rows(x.shape[0],rows)
    @pl.when(step==pl.num_programs(0)-1)
    def _():
        vec[0:1,:]=jnp.sum(gacc[...],axis=0,keepdims=True)
        vec[1:2,:]=jnp.sum(sacc[...],axis=0,keepdims=True)

def last_backward(x,mine,other,above,gain,block=128):
    T,D=x.shape
    b=pl.BlockSpec((block,D),lambda j:(j,0)); vec=pl.BlockSpec((1,D),lambda j:(0,0))
    two=pl.BlockSpec((2,D),lambda j:(0,0))
    return pl.pallas_call(last_kernel,grid=(T//block,),in_specs=[b,b,b,b,vec],out_specs=[b,two],
        scratch_shapes=[pltpu.VMEM((8,D),f32),pltpu.VMEM((8,D),f32)],
        out_shape=[sds((T,D),f32),sds((2,D),f32)],
        cost_estimate=pl.CostEstimate(flops=20*T*D,bytes_accessed=16*T*D,transcendentals=T),**PARAMS)(x,mine,other,above,gain)

def weight_kernel(plan, rows_a, info, *refs):
    sides=refs[:rows_a];cols=refs[rows_a:rows_a+len(plan)];outs=refs[rows_a+len(plan):rows_a+len(plan)+8];turned=refs[rows_a+len(plan)+8:]
    step=pl.program_id(0)
    @pl.when(step==0)
    def _():
        for side,t in zip(sides,turned):
            full=side[...].T
            t[...]=full.reshape(t.shape)
    plane=info[0]
    for (which,half,first),col in zip(plan,cols):
        t=turned[which];r=t.shape[2]
        g=col[...]
        for flip in range(4):
            lhs=t[:,plane^flip].reshape(4*r,t.shape[3])
            outs[half*4+flip][:,first:first+r,:]=product_plain(lhs,g).reshape(4,r,g.shape[1]).astype(low)

def weight_products(plane,sides,plan,cols,rows_out,tile=256):
    C=cols[0].shape[1]
    in_specs=[pl.BlockSpec(s.shape,lambda j,*_:(0,0)) for s in sides]+[pl.BlockSpec((c.shape[0],tile),lambda j,*_:(0,j)) for c in cols]
    outs=[pl.BlockSpec((4,rows_out,tile),lambda j,*_:(0,0,j))]*8
    fl=sum(2*sides[w].shape[0]*sides[w].shape[1]*C for w,_,_ in plan)
    return pl.pallas_call(functools.partial(weight_kernel,plan,len(sides)),grid_spec=pltpu.PrefetchScalarGridSpec(num_scalar_prefetch=1,grid=(C//tile,),
        in_specs=in_specs,out_specs=outs,
        scratch_shapes=[pltpu.VMEM((4,4,s.shape[1]//16,s.shape[0]),low) for s in sides]),
        out_shape=[sds((4,rows_out,C),low)]*8,
        cost_estimate=pl.CostEstimate(flops=fl,bytes_accessed=16*4*rows_out*C,transcendentals=0),
        **PARAMS)(plane.reshape(1),*sides,*cols)


def on_plane(
    hidden_in,
    out_grad,
    prompt_states,
    row_split,
    prompt_len,
    gain_attn,
    bias_attn,
    gain_cross,
    bias_cross,
    gain_ff,
    bias_ff,
    w_query,
    w_key,
    w_value,
    w_out,
    c_query,
    c_key,
    c_value,
    c_out,
    w_gate,
    w_up,
    w_down,
):
    frames, width = hidden_in.shape
    plane, level = lax.axis_index("dp") % PLANE, lax.axis_index("dp") // PLANE
    info = jnp.concatenate([row_split, prompt_len])
    positions = jnp.arange(frames, dtype=jnp.int32)
    row_ids = (positions >= row_split[0]).astype(jnp.int32)
    tables = rotary_tables((positions - row_ids * row_split[0]).astype(f32), 4 * HEAD)
    gain_attn, bias_attn, gain_cross, bias_cross, gain_ff, bias_ff = (
        vector[None] for vector in (gain_attn, bias_attn, gain_cross, bias_cross, gain_ff, bias_ff)
    )

    def half_of(values):
        return lax.dynamic_slice_in_dim(
            values, lax.axis_index("tensor") * (frames // 2), frames // 2, 0
        )

    def swapped(part):
        return lax.ppermute(part, "tensor", [(0, 1), (1, 0)])

    context = prompt_states.reshape(2 * PROMPT, prompt_states.shape[2])
    cross_key = product_plain(context, c_key).astype(low)
    cross_value = product_plain(context, c_value).astype(low)
    grad_ff_out = out_grad.astype(low)
    input_one, query, key, value, attended_one, logsum_one, part = self_forward(
        info, hidden_in, gain_attn, bias_attn, w_query, w_key, w_value, w_out, tables
    )
    frames_out = jnp.concatenate([grad_ff_out, *plane_gather(half_of(grad_ff_out))])
    resid_one, input_two, cross_query, attended_two, logsum_two, part_two = cross_forward(
        info, hidden_in, part, swapped(part), gain_cross, bias_cross, c_query, cross_key, cross_value, c_out
    )
    resid_two, input_three = norm_forward(resid_one, part_two, swapped(part_two), gain_ff, bias_ff)
    frames_in = jnp.concatenate([input_three, *plane_gather(half_of(input_three))])
    sum_part, back_part = ff_both(input_three, grad_ff_out, w_gate, w_up, w_down)
    result = resid_two + add_low(sum_part, swapped(sum_part))

    tile = 256
    tiles = w_gate.shape[1] // (PLANE * tile)
    shares = []
    for index in range(tiles):
        send, keep = ff_share(
            jnp.stack([plane * tiles + index, level % 2]), frames_in, frames_out, w_gate, w_up, w_down, tile
        )
        shares.append(z_halve(send, keep, level))
    spread = spread_units(jnp.concatenate(shares, axis=2), plane)
    grad_w_down, grad_w_gate, grad_w_up = spread[0].T, spread[1], spread[2]

    grad_two, grad_cross_out, vectors_ff, query_grad, key_grad, value_grad, part_back = cross_backward(
        info,
        resid_two,
        back_part,
        swapped(back_part),
        out_grad,
        gain_ff,
        c_out,
        cross_query,
        cross_key,
        cross_value,
        logsum_two,
        c_query,
    )
    r, c = width // 16, context.shape[1] // 16
    parts = weight_products(
        plane,
        [grad_cross_out, input_two, context],
        [(0, 0, 0), (2, 0, r), (1, 1, 0), (2, 1, r)],
        [attended_two, key_grad, query_grad, value_grad],
        r + c,
    )
    cross_sums = [
        z_scatter(plane_scatter(parts[:4], 1), level),
        z_scatter(plane_scatter(parts[4:], 2), level),
    ]
    grad_one, grad_self_out, vectors_cross, query_grad, key_grad, value_grad, part_last = self_backward(
        info,
        resid_one,
        part_back,
        swapped(part_back),
        grad_two,
        gain_cross,
        w_out,
        query,
        key,
        value,
        logsum_one,
        w_query,
        w_key,
        w_value,
        tables,
    )
    parts = weight_products(
        plane,
        [grad_self_out, input_one],
        [(0, 0, 0), (1, 0, r), (1, 1, 0), (1, 1, r)],
        [attended_one, value_grad, query_grad, key_grad],
        2 * r,
    )
    self_sums = [
        z_scatter(plane_scatter(parts[:4], 1), level),
        z_scatter(plane_scatter(parts[4:], 2), level),
    ]
    grad_hidden, vectors_attn = last_backward(
        hidden_in, part_last, swapped(part_last), grad_one, gain_attn
    )
    vectors = vector_sum(jnp.concatenate([vectors_attn, vectors_cross, vectors_ff]))
    return (
        result,
        grad_hidden,
        *(vectors[index] for index in range(6)),
        self_sums[1][:r],
        self_sums[1][r:],
        self_sums[0][r:],
        self_sums[0][:r].T,
        cross_sums[1][:r],
        cross_sums[0][r:],
        cross_sums[1][r:],
        cross_sums[0][:r].T,
        grad_w_gate,
        grad_w_up,
        grad_w_down,
    )


def on_any(
    hidden_in,
    out_grad,
    prompt_states,
    row_split,
    prompt_len,
    gain_attn,
    bias_attn,
    gain_cross,
    bias_cross,
    gain_ff,
    bias_ff,
    w_query,
    w_key,
    w_value,
    w_out,
    c_query,
    c_key,
    c_value,
    c_out,
    w_gate,
    w_up,
    w_down,
):
    frame_count = hidden_in.shape[0]
    positions = jnp.arange(frame_count, dtype=jnp.int32)
    split_here = row_split[0]
    row_ids = (positions >= split_here).astype(jnp.int32)
    tables = rotary_tables((positions - row_ids * split_here).astype(jnp.float32), w_query.shape[1])
    key_index = jnp.arange(2 * PROMPT, dtype=jnp.int32)
    key_rows = key_index // PROMPT
    key_live = key_index % PROMPT < jnp.where(key_rows == 0, prompt_len[0], prompt_len[1])
    self_ok = row_ids[:, None] == row_ids[None, :]
    cross_ok = (row_ids[:, None] == key_rows[None, :]) & key_live[None, :]

    normed, scaled_one, inverse_one = normalize(hidden_in, gain_attn, bias_attn)
    input_one = normed.astype(low)
    query_one = rotate(product_plain(input_one, w_query), tables).astype(low)
    key_one = rotate(product_plain(input_one, w_key), tables).astype(low)
    value_one = product_plain(input_one, w_value).astype(low)
    attended_one, logsum_one = attend_forward(query_one, heads_of(key_one), heads_of(value_one), self_ok)
    resid_one = hidden_in + swap_sum(product_plain(attended_one, w_out))

    normed, scaled_two, inverse_two = normalize(resid_one, gain_cross, bias_cross)
    input_two = normed.astype(low)
    cross_query = product_plain(input_two, c_query).astype(low)
    context_flat = prompt_states.reshape(2 * PROMPT, prompt_states.shape[2])
    cross_key = product_plain(context_flat, c_key).astype(low)
    cross_value = product_plain(context_flat, c_value).astype(low)
    attended_two, logsum_two = attend_forward(
        cross_query, heads_of(cross_key), heads_of(cross_value), cross_ok
    )
    resid_two = resid_one + swap_sum(product_plain(attended_two, c_out))

    normed, scaled_three, inverse_three = normalize(resid_two, gain_ff, bias_ff)
    input_three = normed.astype(low)
    gate_pre = product_plain(input_three, w_gate)
    up_pre = product_plain(input_three, w_up)
    sigmoid_gate = jax.nn.sigmoid(gate_pre)
    mixed_low = (gate_pre * sigmoid_gate * up_pre).astype(low)
    result = resid_two + swap_sum(product_plain(mixed_low, w_down))

    grad_ff_out = out_grad.astype(low)
    grad_w_down = generic_sum(grad_ff_out, mixed_low).T
    grad_mixed = product_with_rows(grad_ff_out, w_down)
    grad_gate = (
        grad_mixed * up_pre * sigmoid_gate * (1.0 + gate_pre * (1.0 - sigmoid_gate))
    ).astype(low)
    grad_up = (grad_mixed * gate_pre * sigmoid_gate).astype(low)
    grad_w_gate = generic_sum(input_three, grad_gate)
    grad_w_up = generic_sum(input_three, grad_up)
    normed_grad_three = swap_sum(
        product_with_rows(grad_gate, w_gate) + product_with_rows(grad_up, w_up)
    )
    back_three, grad_gain_ff, grad_bias_ff = normalize_back(
        normed_grad_three, scaled_three, inverse_three, gain_ff
    )
    grad_two = out_grad + back_three
    grad_cross_out = grad_two.astype(low)
    grad_c_out = generic_sum(grad_cross_out, attended_two).T
    grad_attended_two = product_with_rows(grad_cross_out, c_out).astype(low)
    cross_query_grad, cross_key_grad, cross_value_grad = attend_backward(
        cross_query,
        heads_of(cross_key),
        heads_of(cross_value),
        cross_ok,
        grad_attended_two,
        logsum_two,
    )
    cross_query_grad = cross_query_grad.astype(low)
    cross_key_grad = cross_key_grad.astype(low)
    cross_value_grad = cross_value_grad.astype(low)
    grad_c_query = generic_sum(input_two, cross_query_grad)
    grad_c_key = generic_sum(context_flat, cross_key_grad)
    grad_c_value = generic_sum(context_flat, cross_value_grad)
    normed_grad_two = swap_sum(product_with_rows(cross_query_grad, c_query))
    back_two, grad_gain_cross, grad_bias_cross = normalize_back(
        normed_grad_two, scaled_two, inverse_two, gain_cross
    )
    grad_one = grad_two + back_two
    grad_self_out = grad_one.astype(low)
    grad_w_out = generic_sum(grad_self_out, attended_one).T
    grad_attended_one = product_with_rows(grad_self_out, w_out).astype(low)
    query_grad, key_grad, value_grad = attend_backward(
        query_one, heads_of(key_one), heads_of(value_one), self_ok, grad_attended_one, logsum_one
    )
    query_grad = rotate_back(query_grad, tables).astype(low)
    key_grad = rotate_back(key_grad, tables).astype(low)
    value_grad = value_grad.astype(low)
    grad_w_query = generic_sum(input_one, query_grad)
    grad_w_key = generic_sum(input_one, key_grad)
    grad_w_value = generic_sum(input_one, value_grad)
    normed_grad_one = swap_sum(
        product_with_rows(query_grad, w_query)
        + product_with_rows(key_grad, w_key)
        + product_with_rows(value_grad, w_value)
    )
    back_one, grad_gain_attn, grad_bias_attn = normalize_back(
        normed_grad_one, scaled_one, inverse_one, gain_attn
    )
    grad_hidden = grad_one + back_one
    vectors = vector_sum(
        jnp.stack(
            [
                grad_gain_attn,
                grad_bias_attn,
                grad_gain_cross,
                grad_bias_cross,
                grad_gain_ff,
                grad_bias_ff,
            ]
        )
    )
    return (
        result,
        grad_hidden,
        vectors[0],
        vectors[1],
        vectors[2],
        vectors[3],
        vectors[4],
        vectors[5],
        grad_w_query,
        grad_w_key,
        grad_w_value,
        grad_w_out,
        grad_c_query,
        grad_c_key,
        grad_c_value,
        grad_c_out,
        grad_w_gate,
        grad_w_up,
        grad_w_down,
    )


def solution(mesh):
    in_specs = (
        P("dp", None),
        P("dp", None),
        P("dp", None, None),
        P("dp"),
        P("dp"),
        P(),
        P(),
        P(),
        P(),
        P(),
        P(),
        P(None, "tensor"),
        P(None, "tensor"),
        P(None, "tensor"),
        P("tensor", None),
        P(None, "tensor"),
        P(None, "tensor"),
        P(None, "tensor"),
        P("tensor", None),
        P(None, "tensor"),
        P(None, "tensor"),
        P("tensor", None),
    )
    out_specs = (
        P("dp", None),
        P("dp", None),
        P(("dp", "tensor")),
        P(("dp", "tensor")),
        P(("dp", "tensor")),
        P(("dp", "tensor")),
        P(("dp", "tensor")),
        P(("dp", "tensor")),
        P("dp", "tensor"),
        P("dp", "tensor"),
        P("dp", "tensor"),
        P("tensor", "dp"),
        P("dp", "tensor"),
        P("dp", "tensor"),
        P("dp", "tensor"),
        P("tensor", "dp"),
        P("dp", "tensor"),
        P("dp", "tensor"),
        P("tensor", "dp"),
    )
    known = mesh.shape["dp"] == PLANE * LEVELS and mesh.shape["tensor"] == 2
    return jax.shard_map(
        on_plane if known else on_any, mesh=mesh, in_specs=in_specs, out_specs=out_specs, check_vma=False
    )
```

```python
import functools
import math

import jax
import jax.numpy as jnp
from jax import lax
from jax.experimental import pallas as pl
from jax.experimental.pallas import tpu as pltpu
from jax.sharding import PartitionSpec as P

PROMPT = 128
HEAD = 64
PLANE = 4
LEVELS = 4

low = jnp.bfloat16
f32 = jnp.float32
sds = jax.ShapeDtypeStruct


norm_eps = 1e-05
score_scale = 0.125
masked_score = -1e30


def product_plain(left_side, right_side):
    return jnp.dot(left_side, right_side, preferred_element_type=jnp.float32)


def product_over_rows(left_side, right_side):
    return lax.dot_general(
        left_side, right_side, (((0,), (0,)), ((), ())), preferred_element_type=jnp.float32
    )


def product_with_rows(left_side, right_side):
    return lax.dot_general(
        left_side, right_side, (((1,), (1,)), ((), ())), preferred_element_type=jnp.float32
    )


def rotary_tables(positions, width):
    dim_index = jnp.arange(width) % HEAD
    freq_index = (dim_index % 16).astype(jnp.float32)
    inverse_freq = jnp.exp(freq_index * (-math.log(10000.0) / 16.0))
    angles = positions[:, None] * inverse_freq[None, :]
    cosine = jnp.cos(angles)
    sine_part = jnp.sin(angles)
    cos_table = jnp.where(dim_index < 32, cosine, 1.0)
    sin_lower = jnp.where(dim_index < 16, -sine_part, 0.0)
    sin_upper = jnp.where((dim_index >= 16) & (dim_index < 32), sine_part, 0.0)
    return (cos_table, sin_lower, sin_upper)


def rotate(values, tables):
    cos_table, sin_lower, sin_upper = tables
    return (
        values * cos_table
        + jnp.roll(values, -16, axis=1) * sin_lower
        + jnp.roll(values, 16, axis=1) * sin_upper
    )


def rotate_back(incoming, tables):
    cos_table, sin_lower, sin_upper = tables
    return (
        incoming * cos_table
        + jnp.roll(incoming * sin_lower, 16, axis=1)
        + jnp.roll(incoming * sin_upper, -16, axis=1)
    )


def normalize(values, norm_gain, norm_shift):
    average = jnp.mean(values, axis=-1, keepdims=True)
    centered = values - average
    variance = jnp.mean(centered * centered, axis=-1, keepdims=True)
    inverse = lax.rsqrt(variance + norm_eps)
    scaled = centered * inverse
    return (scaled * norm_gain + norm_shift, scaled, inverse)


def normalize_back(incoming, scaled, inverse, norm_gain):
    grad_gain = jnp.sum(incoming * scaled, axis=0)
    grad_shift = jnp.sum(incoming, axis=0)
    weighted = incoming * norm_gain
    grad_input = inverse * (
        weighted
        - jnp.mean(weighted, axis=-1, keepdims=True)
        - scaled * jnp.mean(weighted * scaled, axis=-1, keepdims=True)
    )
    return (grad_input, grad_gain, grad_shift)


def heads_of(values):
    return values.reshape(values.shape[0], values.shape[1] // HEAD, HEAD)


def attend_forward(query_block, key_heads, value_heads, allowed):
    query_heads = heads_of(query_block)
    scores = (
        jnp.einsum("qhd,khd->hqk", query_heads, key_heads, preferred_element_type=jnp.float32)
        * score_scale
    )
    scores = jnp.where(allowed[None], scores, masked_score)
    largest = jnp.max(scores, axis=-1, keepdims=True)
    exp_scores = jnp.exp(scores - largest)
    totals = jnp.sum(exp_scores, axis=-1, keepdims=True)
    soft_weights = (exp_scores / totals).astype(jnp.bfloat16)
    mixed_heads = jnp.einsum(
        "hqk,khd->qhd", soft_weights, value_heads, preferred_element_type=jnp.float32
    )
    mixed_flat = mixed_heads.reshape(query_block.shape[0], query_block.shape[1]).astype(
        jnp.bfloat16
    )
    return (mixed_flat, largest[..., 0] + jnp.log(totals[..., 0]))


def attend_backward(query_block, key_heads, value_heads, allowed, grad_block, logsum_block):
    query_heads = heads_of(query_block)
    grad_heads = heads_of(grad_block)
    scores = (
        jnp.einsum("qhd,khd->hqk", query_heads, key_heads, preferred_element_type=jnp.float32)
        * score_scale
    )
    scores = jnp.where(allowed[None], scores, masked_score)
    soft_weights = jnp.exp(scores - logsum_block[..., None])
    grad_weights = jnp.einsum(
        "qhd,khd->hqk", grad_heads, value_heads, preferred_element_type=jnp.float32
    )
    inner_sum = jnp.sum(soft_weights * grad_weights, axis=-1, keepdims=True)
    grad_scores = (soft_weights * (grad_weights - inner_sum)).astype(jnp.bfloat16)
    grad_query = (
        jnp.einsum("hqk,khd->qhd", grad_scores, key_heads, preferred_element_type=jnp.float32)
        * score_scale
    )
    grad_key = (
        jnp.einsum("hqk,qhd->khd", grad_scores, query_heads, preferred_element_type=jnp.float32)
        * score_scale
    )
    grad_value = jnp.einsum(
        "hqk,qhd->khd",
        soft_weights.astype(jnp.bfloat16),
        grad_heads,
        preferred_element_type=jnp.float32,
    )
    return (
        grad_query.reshape(query_block.shape),
        grad_key.reshape(grad_key.shape[0], -1),
        grad_value.reshape(grad_value.shape[0], -1),
    )


def swap_sum(partial):
    low = partial.astype(jnp.bfloat16)
    if lax.axis_size("tensor") == 2:
        other = lax.ppermute(low, "tensor", [(0, 1), (1, 0)])
        return low.astype(jnp.float32) + other.astype(jnp.float32)
    return lax.psum(low, "tensor").astype(jnp.float32)


def pairs(mask):
    return [(i, i ^ mask) for i in range(16)]


def vector_sum(vectors):
    if lax.axis_size("dp") == PLANE * LEVELS:
        for mask in (1, 2, 4, 8):
            vectors = vectors + lax.ppermute(vectors, "dp", pairs(mask))
    else:
        vectors = lax.psum(vectors, "dp")
    share = vectors.shape[1] // (lax.axis_size("dp") * lax.axis_size("tensor"))
    index = lax.axis_index("dp") * lax.axis_size("tensor") + lax.axis_index("tensor")
    return lax.dynamic_slice_in_dim(vectors, index * share, share, 1)


def generic_sum(rows_side, column_side):
    return lax.psum_scatter(
        product_over_rows(rows_side, column_side).astype(jnp.bfloat16),
        "dp",
        scatter_dimension=0,
        tiled=True,
    ).astype(jnp.float32)


def add_low(*terms):
    total = terms[0].astype(jnp.float32)
    for term in terms[1:]:
        total = total + term.astype(jnp.float32)
    return total


def ff_parts(gate, up, grad_mixed):
    sig = 1.0 / (1.0 + jnp.exp(-gate))
    act = gate * sig
    return (
        (act * up).astype(low),
        (grad_mixed * up * sig * (1.0 + gate * (1.0 - sig))).astype(low),
        (grad_mixed * act).astype(low),
    )


def turn(values, cos, lower, upper):
    width = values.shape[1]
    return (values * cos + pltpu.roll(values, width - 16, 1) * lower + pltpu.roll(values, 16, 1) * upper)

def turn_back(values, cos, lower, upper):
    width = values.shape[1]
    return (values * cos + pltpu.roll(values * lower, 16, 1) + pltpu.roll(values * upper, width - 16, 1))

def normed_rows(values, gain, shift):
    average = jnp.mean(values, axis=-1, keepdims=True)
    centered = values - average
    variance = jnp.mean(centered * centered, axis=-1, keepdims=True)
    return centered * lax.rsqrt(variance + norm_eps) * gain + shift

def over_rows(rows, body, chunk=32):
    @pl.loop(0, rows // chunk, unroll=min(4, rows // chunk))
    def _(i):
        body(pl.ds(pl.multiple_of(i * chunk, chunk), chunk))

def attend(q, k, v, mask, lse_ref):
    q_turned = (q * jnp.bfloat16(0.125)).T
    v_turned = v.T
    outs = []
    for h in range(q.shape[1] // HEAD):
        c = slice(h * HEAD, (h + 1) * HEAD)
        s = product_plain(k[:, c], q_turned[c, :]) + mask
        m = jnp.max(s, axis=0, keepdims=True)
        e = jnp.exp(s - m)
        total = jnp.sum(e, axis=0, keepdims=True)
        o = product_plain(v_turned[c, :], e.astype(low)) * (1.0 / total)
        outs.append(o)
        lse_ref[h : h + 1, :] = m + jnp.log(total)
    return jnp.concatenate(outs, axis=0).T.astype(low)


def attend_back(q, k, v, g, mask, lse):
    scaled = q * jnp.bfloat16(0.125)
    q_turned = scaled.T
    g_turned = g.T
    k_turned = k.T
    dq, dk, dv = [], [], []
    for h in range(q.shape[1] // HEAD):
        c = slice(h * HEAD, (h + 1) * HEAD)
        p = jnp.exp(product_plain(k[:, c], q_turned[c, :]) + (mask - lse[h : h + 1, :]))
        dp = product_plain(v[:, c], g_turned[c, :])
        inner = jnp.sum(p * dp, axis=0, keepdims=True)
        ds = (p * (dp - inner)).astype(low)
        dq.append(product_plain(k_turned[c, :], ds))
        dk.append(product_plain(ds, scaled[:, c]))
        dv.append(product_plain(p.astype(low), g[:, c]))
    return (
        jnp.concatenate(dq, axis=0).T * 0.125,
        jnp.concatenate(dk, axis=1),
        jnp.concatenate(dv, axis=1),
    )


def self_mask(split, T):
    r=lax.broadcasted_iota(jnp.int32,(T,T),0)>=split
    c=lax.broadcasted_iota(jnp.int32,(T,T),1)>=split
    return jnp.where(r==c,0.0,masked_score).astype(f32)

def cross_mask(split, first, second, T, K):
    r = lax.broadcasted_iota(jnp.int32, (K, T), 1) >= split
    c = lax.broadcasted_iota(jnp.int32, (K, T), 0)
    least = jnp.where(r, K // 2, 0)
    most = jnp.where(r, K // 2 + second, first)
    return jnp.where((c >= least) & (c < most), 0.0, masked_score).astype(f32)


def norm_back_rows(x,e,gain,above,gain_acc,shift_acc):
    average=jnp.mean(x,axis=-1,keepdims=True)
    centered=x-average
    variance=jnp.mean(centered*centered,axis=-1,keepdims=True)
    inverse=lax.rsqrt(variance+norm_eps)
    n=centered*inverse
    en=e*n
    w=e*gain
    mean_w=jnp.mean(w,axis=-1,keepdims=True)
    mean_wn=jnp.mean(en*gain,axis=-1,keepdims=True)
    fold=lambda t: jnp.sum(t.reshape(t.shape[0]//8,8,t.shape[1]),axis=0)
    gain_acc[...]+=fold(en)
    shift_acc[...]+=fold(e)
    return above+inverse*(w-mean_w-n*mean_wn)

def norm_back_all(x,mine,other,above,gain,total,total_low,vec,gacc,sacc):
    gacc[...]=jnp.zeros_like(gacc);sacc[...]=jnp.zeros_like(sacc)
    def rows(r):
        e=mine[r,:].astype(f32)+other[r,:].astype(f32)
        t=norm_back_rows(x[r,:],e,gain[...],above[r,:],gacc,sacc)
        total[r,:]=t
        if total_low is not None: total_low[r,:]=t.astype(low)
    over_rows(x.shape[0],rows)
    vec[0:1,:]=jnp.sum(gacc[...],axis=0,keepdims=True)
    vec[1:2,:]=jnp.sum(sacc[...],axis=0,keepdims=True)


def ordered(kernel, token, args, in_specs, out_specs, out_shape, grid, flops, scratch=(), info=None, copied=0):
    if info is None:
        info = jnp.zeros((1,), jnp.int32)
    inputs, outputs = len(args), len(out_shape)

    def body(info_ref, *refs):
        token_ref = refs[inputs + 1 + outputs]

        @pl.when(functools.reduce(jnp.logical_and, [pl.program_id(i) == 0 for i in range(len(grid))]))
        def _():
            token_ref[...] = jnp.zeros_like(token_ref)

        kernel(
            info_ref,
            *refs[:inputs],
            *refs[inputs + 1 : inputs + 1 + outputs],
            *refs[inputs + 2 + outputs :],
        )

    moved = sum(math.prod(a.shape) * a.dtype.itemsize for a in (*args, *out_shape))
    *results, token = pl.pallas_call(
        body,
        grid_spec=pltpu.PrefetchScalarGridSpec(
            num_scalar_prefetch=1,
            grid=grid,
            in_specs=[*in_specs, pl.BlockSpec(memory_space=pl.ANY)],
            out_specs=[*out_specs, pl.BlockSpec((8, 128), lambda *_: (0, 0))],
            scratch_shapes=list(scratch),
        ),
        out_shape=[*out_shape, sds((8, 128), f32)],
        compiler_params=pltpu.CompilerParams(vmem_limit_bytes=48 * 2**20),
        cost_estimate=pl.CostEstimate(flops=flops, bytes_accessed=moved, transcendentals=0),
    )(info, *args, token)
    return (*results, token)


def specs(frames, width, tile):
    whole = pl.BlockSpec((frames, width), lambda j, *_: (0, 0))
    vector = pl.BlockSpec((1, width), lambda j, *_: (0, 0))
    column = pl.BlockSpec((width, tile), lambda j, *_: (0, j))
    row = pl.BlockSpec((tile, width), lambda j, *_: (j, 0))
    act = pl.BlockSpec((frames, tile), lambda j, *_: (0, j))
    table = pl.BlockSpec((frames, tile), lambda j, *_: (0, 0))
    logsum = pl.BlockSpec((8, frames), lambda j, *_: (j, 0))
    return whole, vector, column, row, act, table, logsum


def added(acc, term, result):
    step = pl.program_id(0)

    @pl.when(step == 0)
    def _():
        acc[...] = term

    @pl.when(step != 0)
    def _():
        acc[...] += term

    @pl.when(step == pl.num_programs(0) - 1)
    def _():
        result[...] = acc[...].astype(result.dtype)


def self_kernel(info, hid, gain, shift, wq, wk, wv, wo, cos, lower, upper, normed, q, k, v, att, logsum, part, acc, mask):
    frames = hid.shape[0]

    @pl.when(pl.program_id(0) == 0)
    def _():
        def rows(r):
            normed[r, :] = normed_rows(hid[r, :], gain[...], shift[...]).astype(low)

        over_rows(frames, rows)
        mask[...] = self_mask(info[0], frames)

    n = normed[...]
    tables = (cos[...], lower[...], upper[...])
    q[...] = turn(product_plain(n, wq[...]), *tables).astype(low)
    k[...] = turn(product_plain(n, wk[...]), *tables).astype(low)
    v[...] = product_plain(n, wv[...]).astype(low)
    attended = attend(q[...], k[...], v[...], mask[...], logsum)
    att[...] = attended
    added(acc, product_plain(attended, wo[...]), part)


def self_forward(token, info, hid, gain, shift, wq, wk, wv, wo, tables, tile=4 * HEAD):
    frames, width = hid.shape
    columns = wq.shape[1]
    whole, vector, column, row, act, table, logsum = specs(frames, width, tile)
    return ordered(
        self_kernel,
        token,
        (hid, gain, shift, wq, wk, wv, wo, *tables),
        [whole, vector, vector, column, column, column, row, table, table, table],
        [whole, act, act, act, act, logsum, whole],
        [sds((frames, width), low)]
        + [sds((frames, columns), low)] * 4
        + [sds((columns // tile * 8, frames), f32), sds((frames, width), low)],
        (columns // tile,),
        2 * frames * columns * (4 * width + 8 * frames),
        [pltpu.VMEM((frames, width), f32), pltpu.VMEM((frames, frames), f32)],
        info,
    )


def cross_kernel(info, hid, mine, other, gain, shift, cq, ck, cv, co, total, normed, q, att, logsum, part, acc, mask):
    frames = hid.shape[0]

    @pl.when(pl.program_id(0) == 0)
    def _():
        def rows(r):
            x = hid[r, :] + (mine[r, :].astype(f32) + other[r, :].astype(f32))
            total[r, :] = x
            normed[r, :] = normed_rows(x, gain[...], shift[...]).astype(low)

        over_rows(frames, rows)
        mask[...] = cross_mask(info[0], info[1], info[2], frames, ck.shape[0])

    q[...] = product_plain(normed[...], cq[...]).astype(low)
    attended = attend(q[...], ck[...], cv[...], mask[...], logsum)
    att[...] = attended
    added(acc, product_plain(attended, co[...]), part)


def cross_forward(token, info, hid, mine, other, gain, shift, cq, ck, cv, co, tile=4 * HEAD):
    frames, width = hid.shape
    columns, keys = cq.shape[1], ck.shape[0]
    whole, vector, column, row, act, table, logsum = specs(frames, width, tile)
    key = pl.BlockSpec((keys, tile), lambda j, *_: (0, j))
    return ordered(
        cross_kernel,
        token,
        (hid, mine, other, gain, shift, cq, ck, cv, co),
        [whole, whole, whole, vector, vector, column, key, key, row],
        [whole, whole, act, act, logsum, whole],
        [
            sds((frames, width), f32),
            sds((frames, width), low),
            sds((frames, columns), low),
            sds((frames, columns), low),
            sds((columns // tile * 8, frames), f32),
            sds((frames, width), low),
        ],
        (columns // tile,),
        2 * frames * columns * (2 * width + 8 * keys),
        [pltpu.VMEM((frames, width), f32), pltpu.VMEM((keys, frames), f32)],
        info,
    )


def norm_kernel(_, hid, mine, other, gain, shift, total, normed):
    def rows(r):
        x = hid[r, :] + (mine[r, :].astype(f32) + other[r, :].astype(f32))
        total[r, :] = x
        normed[r, :] = normed_rows(x, gain[...], shift[...]).astype(low)

    over_rows(hid.shape[0], rows)


def norm_forward(token, hid, mine, other, gain, shift, block=128):
    frames, width = hid.shape
    rows = pl.BlockSpec((block, width), lambda j, *_: (j, 0))
    vector = pl.BlockSpec((1, width), lambda j, *_: (0, 0))
    return ordered(
        norm_kernel,
        token,
        (hid, mine, other, gain, shift),
        [rows, rows, rows, vector, vector],
        [rows, rows],
        [sds((frames, width), f32), sds((frames, width), low)],
        (frames // block,),
        10 * frames * width,
    )


def cross_back_kernel(info, x, mine, other, above, gain, co, q, ck, cv, logsum, cq, total, total_low, vectors, dq, dk, dv, part, acc, mask, gain_acc, shift_acc):
    @pl.when(pl.program_id(0) == 0)
    def _():
        norm_back_all(x, mine, other, above, gain, total, total_low, vectors, gain_acc, shift_acc)
        mask[...] = cross_mask(info[0], info[1], info[2], x.shape[0], ck.shape[0])

    g = product_with_rows(total_low[...], co[...]).astype(low)
    a, b, c = attend_back(q[...], ck[...], cv[...], g, mask[...], logsum[...])
    a = a.astype(low)
    dq[...] = a
    dk[...] = b.astype(low)
    dv[...] = c.astype(low)
    added(acc, product_with_rows(a, cq[...]), part)


def cross_backward(token, info, x, mine, other, above, gain, co, q, ck, cv, logsums, cq, tile=4 * HEAD):
    frames, width = x.shape
    columns, keys = cq.shape[1], ck.shape[0]
    whole, vector, column, row, act, table, logsum = specs(frames, width, tile)
    key = pl.BlockSpec((keys, tile), lambda j, *_: (0, j))
    two = pl.BlockSpec((2, width), lambda j, *_: (0, 0))
    return ordered(
        cross_back_kernel,
        token,
        (x, mine, other, above, gain, co, q, ck, cv, logsums, cq),
        [whole, whole, whole, whole, vector, row, act, key, key, logsum, column],
        [whole, whole, two, act, key, key, whole],
        [
            sds((frames, width), f32),
            sds((frames, width), low),
            sds((2, width), f32),
            sds((frames, columns), low),
            sds((keys, columns), low),
            sds((keys, columns), low),
            sds((frames, width), low),
        ],
        (columns // tile,),
        2 * frames * columns * (2 * width + 20 * keys),
        [
            pltpu.VMEM((frames, width), f32),
            pltpu.VMEM((keys, frames), f32),
            pltpu.VMEM((8, width), f32),
            pltpu.VMEM((8, width), f32),
        ],
        info,
    )


def self_back_kernel(info, x, mine, other, above, gain, wo, q, k, v, logsum, wq, wk, wv, cos, lower, upper, total, total_low, vectors, grads, part, acc, mask, gain_acc, shift_acc):
    frames = x.shape[0]

    @pl.when(pl.program_id(0) == 0)
    def _():
        norm_back_all(x, mine, other, above, gain, total, total_low, vectors, gain_acc, shift_acc)
        mask[...] = self_mask(info[0], frames)

    g = product_with_rows(total_low[...], wo[...]).astype(low)
    a, b, c = attend_back(q[...], k[...], v[...], g, mask[...], logsum[...])
    tables = (cos[...], lower[...], upper[...])
    a = turn_back(a, *tables).astype(low)
    b = turn_back(b, *tables).astype(low)
    c = c.astype(low)
    for index, values in enumerate((a, b, c)):
        turned = values.T
        for quarter in range(PLANE):
            grads[quarter, index] = turned[quarter * HEAD : (quarter + 1) * HEAD]
    added(
        acc,
        product_with_rows(a, wq[...]) + product_with_rows(b, wk[...]) + product_with_rows(c, wv[...]),
        part,
    )


def self_backward(token, info, x, mine, other, above, gain, wo, q, k, v, logsums, wq, wk, wv, tables, tile=4 * HEAD):
    frames, width = x.shape
    columns = wq.shape[1]
    whole, vector, column, row, act, table, logsum = specs(frames, width, tile)
    two = pl.BlockSpec((2, width), lambda j, *_: (0, 0))
    heads = pl.BlockSpec((PLANE, 3, HEAD, frames), lambda j, *_: (0, 0, j, 0))
    return ordered(
        self_back_kernel,
        token,
        (x, mine, other, above, gain, wo, q, k, v, logsums, wq, wk, wv, *tables),
        [whole, whole, whole, whole, vector, row, act, act, act, logsum, column, column, column, table, table, table],
        [whole, whole, two, heads, whole],
        [
            sds((frames, width), f32),
            sds((frames, width), low),
            sds((2, width), f32),
            sds((PLANE, 3, columns // PLANE, frames), low),
            sds((frames, width), low),
        ],
        (columns // tile,),
        2 * frames * columns * (4 * width + 20 * frames),
        [
            pltpu.VMEM((frames, width), f32),
            pltpu.VMEM((frames, frames), f32),
            pltpu.VMEM((8, width), f32),
            pltpu.VMEM((8, width), f32),
        ],
        info,
    )


def last_kernel(_, x, mine, other, above, gain, total, vectors, gain_acc, shift_acc):
    step = pl.program_id(0)

    @pl.when(step == 0)
    def _():
        gain_acc[...] = jnp.zeros_like(gain_acc)
        shift_acc[...] = jnp.zeros_like(shift_acc)

    def rows(r):
        e = mine[r, :].astype(f32) + other[r, :].astype(f32)
        total[r, :] = norm_back_rows(x[r, :], e, gain[...], above[r, :], gain_acc, shift_acc)

    over_rows(x.shape[0], rows)

    @pl.when(step == pl.num_programs(0) - 1)
    def _():
        vectors[0:1, :] = jnp.sum(gain_acc[...], axis=0, keepdims=True)
        vectors[1:2, :] = jnp.sum(shift_acc[...], axis=0, keepdims=True)


def last_backward(token, x, mine, other, above, gain, block=128):
    frames, width = x.shape
    rows = pl.BlockSpec((block, width), lambda j, *_: (j, 0))
    vector = pl.BlockSpec((1, width), lambda j, *_: (0, 0))
    two = pl.BlockSpec((2, width), lambda j, *_: (0, 0))
    return ordered(
        last_kernel,
        token,
        (x, mine, other, above, gain),
        [rows, rows, rows, rows, vector],
        [rows, two],
        [sds((frames, width), f32), sds((2, width), f32)],
        (frames // block,),
        20 * frames * width,
        [pltpu.VMEM((8, width), f32), pltpu.VMEM((8, width), f32)],
    )


def pack_kernel(_, values, copies):
    copies[...] = values[...]


def packed(token, values, half):
    frames, width = values.shape
    return ordered(
        pack_kernel,
        token,
        (values,),
        [pl.BlockSpec((frames // 2, width), lambda j, info: (info[0], 0))],
        [pl.BlockSpec((frames // 2, width), lambda j, info: (j, 0))],
        [sds((PLANE * frames // 2, width), low)],
        (PLANE,),
        0,
        info=half,
    )


def ff_kernel(_, in_ref, out_ref, gate_ref, up_ref, down_ref, sum_ref, back_ref, sum_acc, back_acc):
    normed = in_ref[...]
    mixed, grad_gate, grad_up = ff_parts(
        product_plain(normed, gate_ref[...]),
        product_plain(normed, up_ref[...]),
        product_with_rows(out_ref[...], down_ref[...]),
    )
    added(sum_acc, product_plain(mixed, down_ref[...]), sum_ref)
    added(
        back_acc,
        product_with_rows(grad_gate, gate_ref[...]) + product_with_rows(grad_up, up_ref[...]),
        back_ref,
    )


def ff_both(token, normed, grad_out, w_gate, w_up, w_down, tile=512):
    frames, width = normed.shape
    units = w_gate.shape[1]
    whole, _, column, row, *_ = specs(frames, width, tile)
    return ordered(
        ff_kernel,
        token,
        (normed, grad_out, w_gate, w_up, w_down),
        [whole, whole, column, column, row],
        [whole, whole],
        [sds((frames, width), low)] * 2,
        (units // tile,),
        12 * frames * width * units,
        [pltpu.VMEM((frames, width), f32)] * 2,
    )


def share_kernel(info, in_mine, in_other, out_mine, out_other, gate_ref, up_ref, down_ref, send_ref, keep_ref, acc):
    step = pl.program_id(0)
    normed = jnp.concatenate([in_mine[...], in_other[...]], axis=0)
    grad_out = jnp.concatenate([out_mine[...], out_other[...]], axis=0)
    mixed, grad_gate, grad_up = ff_parts(
        product_plain(normed, gate_ref[...]),
        product_plain(normed, up_ref[...]),
        product_with_rows(grad_out, down_ref[...]),
    )
    fresh = (
        product_over_rows(grad_out, mixed),
        product_over_rows(normed, grad_gate),
        product_over_rows(normed, grad_up),
    )
    for index, term in enumerate(fresh):

        @pl.when(step == 0)
        def _():
            acc[index] = term

        @pl.when(step != 0)
        def _():
            acc[index] += term

    @pl.when(step == pl.num_programs(0) - 1)
    def _():
        rows = send_ref.shape[1] // 3
        for pair in range(2):
            for index in range(3):
                for ref, parity in ((send_ref, 1 - info[1]), (keep_ref, info[1])):
                    start = pl.multiple_of((2 * pair + parity) * rows, rows)
                    ref[pair, index * rows : (index + 1) * rows] = acc[
                        index, pl.ds(start, rows), :
                    ].astype(ref.dtype)


def ff_share(token, info, normed, grad_out, w_gate, w_up, w_down, tile):
    frames, width = normed[0].shape
    chunk = frames // PLANE
    rows = pl.BlockSpec((chunk, width), lambda j, info: (j, 0))
    column = pl.BlockSpec((width, tile), lambda j, info: (0, info[0]))
    half = (LEVELS // 2, 3 * width // LEVELS, tile)
    return ordered(
        share_kernel,
        token,
        (*normed, *grad_out, w_gate, w_up, w_down),
        [rows] * 4 + [column, column, pl.BlockSpec((tile, width), lambda j, info: (info[0], 0))],
        [pl.BlockSpec(half, lambda j, info: (0, 0, 0))] * 2,
        [sds(half, low)] * 2,
        (PLANE,),
        24 * frames * width * tile,
        [pltpu.VMEM((3, width, tile), f32)],
        info,
    )


def weight_kernel(plan, sides_count, _, *refs):
    sides, columns = refs[:sides_count], refs[sides_count : sides_count + len(plan)]
    out = refs[sides_count + len(plan)]
    turned = refs[sides_count + len(plan) + 1 :]

    @pl.when(pl.program_id(0) == 0)
    def _():
        for side, ref in zip(sides, turned):
            ref[...] = side[...].T

    for (which, first), column in zip(plan, columns):
        product = product_plain(turned[which][...], column[...]).astype(low)
        rows = product.shape[0] // (PLANE * LEVELS)
        product = product.reshape(LEVELS, PLANE, rows, product.shape[1])
        for owner in range(PLANE):
            out[owner, :, first : first + rows, :] = product[:, owner]


def weight_products(token, sides, plan, columns, tile=256):
    width = columns[0].shape[1]
    rows = sum(sides[which].shape[1] for which, _ in plan) // (PLANE * LEVELS)
    return ordered(
        functools.partial(weight_kernel, plan, len(sides)),
        token,
        (*sides, *columns),
        [pl.BlockSpec(side.shape, lambda j, *_: (0, 0)) for side in sides]
        + [pl.BlockSpec((column.shape[0], tile), lambda j, *_: (0, j)) for column in columns],
        [pl.BlockSpec((PLANE, LEVELS, rows, tile), lambda j, *_: (0, 0, 0, j))],
        [sds((PLANE, LEVELS, rows, width), low)],
        (width // tile,),
        sum(2 * sides[w].shape[0] * sides[w].shape[1] * width for w, _ in plan),
        [pltpu.VMEM((side.shape[1], side.shape[0]), low) for side in sides],
    )


def plane_sum_kernel(info, got, send, keep):
    for ref, parity in ((send, 1 - info[0]), (keep, info[0])):
        total = got[0, 0, parity].astype(f32)
        for source in range(1, PLANE):
            total = total + got[source, 0, parity].astype(f32)
        ref[0] = total.astype(low)


def plane_sum(token, got, parity):
    rows, width = got.shape[2:]
    out = pl.BlockSpec((1, rows, width), lambda j, *_: (j, 0, 0))
    return ordered(
        plane_sum_kernel,
        token,
        (got.reshape(PLANE, 2, 2, rows, width),),
        [pl.BlockSpec((PLANE, 1, 2, rows, width), lambda j, *_: (0, j, 0, 0, 0))],
        [out, out],
        [sds((2, rows, width), low)] * 2,
        (2,),
        0,
        info=parity,
    )


def level_sum_kernel(_, keep_pass, got_pass, keep_own, got_own, passed, own):
    passed[...] = (keep_pass[0].astype(f32) + got_pass[0].astype(f32)).astype(low)
    own[...] = keep_own[0].astype(f32) + got_own[0].astype(f32)


def level_sum(token, keep, got, upper):
    rows, width = keep.shape[1:]
    block = rows // 2 if rows % 32 == 0 else rows
    off = pl.BlockSpec((1, block, width), lambda j, info: (1 - info[0], j, 0))
    own = pl.BlockSpec((1, block, width), lambda j, info: (info[0], j, 0))
    out = pl.BlockSpec((block, width), lambda j, info: (j, 0))
    return ordered(
        level_sum_kernel,
        token,
        (keep, got, keep, got),
        [off, off, own, own],
        [out, out],
        [sds((rows, width), low), sds((rows, width), f32)],
        (rows // block,),
        0,
        info=upper,
    )


def head_kernel(info, grads_mine, grads_other, in_mine, in_other, send, keep, acc):
    step = pl.program_id(0)
    rows = acc.shape[0]
    term = product_plain(grads_mine[0].reshape(rows, -1), in_mine[...]) + product_plain(
        grads_other[0].reshape(rows, -1), in_other[...]
    )

    @pl.when(step == 0)
    def _():
        acc[...] = term

    @pl.when(step != 0)
    def _():
        acc[...] += term

    @pl.when(step == pl.num_programs(0) - 1)
    def _():
        width = send.shape[2]
        for level in range(LEVELS):
            for ref, parity in ((send, 1 - info[1]), (keep, info[1])):

                @pl.when(parity == level % 2)
                def _():
                    ref[level // 2] = acc[:, level * width : (level + 1) * width].astype(low)


def head_products(token, info, grads, normed):
    _, three, features, frames = grads.shape
    width = normed[0].shape[1]
    chunk = normed[0].shape[0] // PLANE
    rows = pl.BlockSpec((chunk, width), lambda j, info: (j, 0))
    half = (LEVELS // 2, three * features, width // LEVELS)
    return ordered(
        head_kernel,
        token,
        (grads, grads, *normed),
        [
            pl.BlockSpec((1, three, features, chunk), lambda j, info: (j, 0, 0, info[0])),
            pl.BlockSpec((1, three, features, chunk), lambda j, info: (j, 0, 0, 1 - info[0])),
            rows,
            rows,
        ],
        [pl.BlockSpec(half, lambda j, info: (0, 0, 0))] * 2,
        [sds(half, low)] * 2,
        (PLANE,),
        2 * three * features * PLANE * frames * width,
        [pltpu.VMEM((three * features, width), f32)],
        info,
    )


def on_plane(
    hidden_in,
    out_grad,
    prompt_states,
    row_split,
    prompt_len,
    gain_attn,
    bias_attn,
    gain_cross,
    bias_cross,
    gain_ff,
    bias_ff,
    w_query,
    w_key,
    w_value,
    w_out,
    c_query,
    c_key,
    c_value,
    c_out,
    w_gate,
    w_up,
    w_down,
):
    frames, width = hidden_in.shape
    plane, level = lax.axis_index("dp") % PLANE, lax.axis_index("dp") // PLANE
    info = jnp.concatenate([row_split, prompt_len])
    positions = jnp.arange(frames, dtype=jnp.int32)
    row_ids = (positions >= row_split[0]).astype(jnp.int32)
    tables = rotary_tables((positions - row_ids * row_split[0]).astype(f32), 4 * HEAD)
    gain_attn, bias_attn, gain_cross, bias_cross, gain_ff, bias_ff = (
        vector[None] for vector in (gain_attn, bias_attn, gain_cross, bias_cross, gain_ff, bias_ff)
    )

    zero = jnp.zeros((1,), jnp.int32)
    half = zero + lax.axis_index("tensor")
    parity, upper = zero + level % 2, zero + level // 2
    chips = [[PLANE * z + p for p in range(PLANE)] for z in range(LEVELS)]

    def swapped(part):
        return lax.ppermute(part, "tensor", [(0, 1), (1, 0)])

    def in_plane(values):
        shape = values.shape
        return lax.all_to_all(
            values, "dp", 0, 0, axis_index_groups=chips, tiled=True
        ).reshape(shape)

    def level_swap(values, mask):
        return lax.ppermute(values, "dp", pairs(mask))

    token = jnp.zeros((8, 128), f32)
    context = prompt_states.reshape(2 * PROMPT, prompt_states.shape[2])
    cross_key = product_plain(context, c_key).astype(low)
    cross_value = product_plain(context, c_value).astype(low)
    grad_ff_out = out_grad.astype(low)
    copies, token = packed(token, grad_ff_out, half)
    frames_out = in_plane(copies)
    frames_out = (frames_out, swapped(frames_out))
    input_one, query, key, value, attended_one, logsum_one, part, token = self_forward(
        token, info, hidden_in, gain_attn, bias_attn, w_query, w_key, w_value, w_out, tables
    )
    resid_one, input_two, cross_query, attended_two, logsum_two, part, token = cross_forward(
        token,
        info,
        hidden_in,
        part,
        swapped(part),
        gain_cross,
        bias_cross,
        c_query,
        cross_key,
        cross_value,
        c_out,
    )
    resid_two, input_three, token = norm_forward(
        token, resid_one, part, swapped(part), gain_ff, bias_ff
    )
    copies, token = packed(token, input_three, half)
    frames_in = in_plane(copies)
    frames_in = (frames_in, swapped(frames_in))
    sum_part, back_part, token = ff_both(token, input_three, grad_ff_out, w_gate, w_up, w_down)
    result = resid_two + add_low(sum_part, swapped(sum_part))
    grad_two, grad_cross_out, vectors_ff, query_grad, key_grad, value_grad, part, token = cross_backward(
        token,
        info,
        resid_two,
        back_part,
        swapped(back_part),
        out_grad,
        gain_ff,
        c_out,
        cross_query,
        cross_key,
        cross_value,
        logsum_two,
        c_query,
    )
    back_swapped = swapped(part)

    tile = 256
    tiles = w_gate.shape[1] // (PLANE * tile)

    def share(token, index):
        number = jnp.concatenate([zero + plane * tiles + index, parity])
        return ff_share(token, number, frames_in, frames_out, w_gate, w_up, w_down, tile)

    send_a, keep_a, token = share(token, 0)
    got_a = level_swap(send_a, PLANE)
    copies, token = packed(token, input_one, half)
    frames_one = in_plane(copies)
    frames_one = (frames_one, swapped(frames_one))
    r, c = width // 16, context.shape[1] // 16
    products, token = weight_products(
        token,
        [grad_cross_out, input_two, context],
        [(0, 0), (1, r), (2, 2 * r), (2, 2 * r + c)],
        [attended_two, query_grad, key_grad, value_grad],
    )
    got_cross = in_plane(products)
    send_b, keep_b, token = share(token, 1)
    got_b = level_swap(send_b, PLANE)
    pass_a, own_a, token = level_sum(token, keep_a, got_a, upper)
    last_a = level_swap(pass_a, 2 * PLANE)
    grad_one, grad_self_out, vectors_cross, grads, part, token = self_backward(
        token,
        info,
        resid_one,
        part,
        back_swapped,
        grad_two,
        gain_cross,
        w_out,
        query,
        key,
        value,
        logsum_one,
        w_query,
        w_key,
        w_value,
        tables,
    )
    got_heads = in_plane(grads)
    part_swapped = swapped(part)
    pass_b, own_b, token = level_sum(token, keep_b, got_b, upper)
    last_b = level_swap(pass_b, 2 * PLANE)
    send_c, keep_c, token = share(token, 2)
    got_c = level_swap(send_c, PLANE)
    products, token = weight_products(token, [grad_self_out], [(0, 0)], [attended_one])
    got_out = in_plane(products)
    grad_hidden, vectors_attn, token = last_backward(
        token, hidden_in, part, part_swapped, grad_one, gain_attn
    )
    vectors = vector_sum(jnp.concatenate([vectors_attn, vectors_cross, vectors_ff]))
    send_x, keep_x, token = plane_sum(token, got_cross, parity)
    got_x = level_swap(send_x, PLANE)
    pass_c, own_c, token = level_sum(token, keep_c, got_c, upper)
    last_c = level_swap(pass_c, 2 * PLANE)
    send_h, keep_h, token = head_products(
        token, jnp.concatenate([half, parity]), got_heads, frames_one
    )
    got_h = level_swap(send_h, PLANE)
    pass_x, own_x, token = level_sum(token, keep_x, got_x, upper)
    last_x = level_swap(pass_x, 2 * PLANE)
    send_o, keep_o, token = plane_sum(token, got_out, parity)
    got_o = level_swap(send_o, PLANE)
    pass_h, own_h, token = level_sum(token, keep_h, got_h, upper)
    last_h = level_swap(pass_h, 2 * PLANE)
    pass_o, own_o, token = level_sum(token, keep_o, got_o, upper)
    last_o = level_swap(pass_o, 2 * PLANE)

    units = jnp.stack([add_low(own_a, last_a), add_low(own_b, last_b), add_low(own_c, last_c)])
    units = units.astype(low).reshape(tiles, 3, PLANE, r, tile).transpose(2, 1, 3, 0, 4)
    units = in_plane(units.reshape(PLANE, 3, r, tiles * tile))
    units = units.transpose(1, 2, 0, 3).reshape(3, r, w_gate.shape[1]).astype(f32)
    cross = add_low(own_x, last_x)
    heads = add_low(own_h, last_h).astype(low).T
    heads = in_plane(heads.reshape(PLANE, r, heads.shape[1]))
    heads = heads.reshape(PLANE, r, 3, w_query.shape[1] // (PLANE * HEAD), HEAD)
    heads = heads.transpose(2, 1, 3, 0, 4).reshape(3, r, w_query.shape[1]).astype(f32)
    return (
        result,
        grad_hidden,
        *(vectors[index] for index in range(6)),
        heads[0],
        heads[1],
        heads[2],
        add_low(own_o, last_o).T,
        cross[r : 2 * r],
        cross[2 * r : 2 * r + c],
        cross[2 * r + c :],
        cross[:r].T,
        units[1],
        units[2],
        units[0].T,
    )


def on_any(
    hidden_in,
    out_grad,
    prompt_states,
    row_split,
    prompt_len,
    gain_attn,
    bias_attn,
    gain_cross,
    bias_cross,
    gain_ff,
    bias_ff,
    w_query,
    w_key,
    w_value,
    w_out,
    c_query,
    c_key,
    c_value,
    c_out,
    w_gate,
    w_up,
    w_down,
):
    frame_count = hidden_in.shape[0]
    positions = jnp.arange(frame_count, dtype=jnp.int32)
    split_here = row_split[0]
    row_ids = (positions >= split_here).astype(jnp.int32)
    tables = rotary_tables((positions - row_ids * split_here).astype(jnp.float32), w_query.shape[1])
    key_index = jnp.arange(2 * PROMPT, dtype=jnp.int32)
    key_rows = key_index // PROMPT
    key_live = key_index % PROMPT < jnp.where(key_rows == 0, prompt_len[0], prompt_len[1])
    self_ok = row_ids[:, None] == row_ids[None, :]
    cross_ok = (row_ids[:, None] == key_rows[None, :]) & key_live[None, :]

    normed, scaled_one, inverse_one = normalize(hidden_in, gain_attn, bias_attn)
    input_one = normed.astype(low)
    query_one = rotate(product_plain(input_one, w_query), tables).astype(low)
    key_one = rotate(product_plain(input_one, w_key), tables).astype(low)
    value_one = product_plain(input_one, w_value).astype(low)
    attended_one, logsum_one = attend_forward(query_one, heads_of(key_one), heads_of(value_one), self_ok)
    resid_one = hidden_in + swap_sum(product_plain(attended_one, w_out))

    normed, scaled_two, inverse_two = normalize(resid_one, gain_cross, bias_cross)
    input_two = normed.astype(low)
    cross_query = product_plain(input_two, c_query).astype(low)
    context_flat = prompt_states.reshape(2 * PROMPT, prompt_states.shape[2])
    cross_key = product_plain(context_flat, c_key).astype(low)
    cross_value = product_plain(context_flat, c_value).astype(low)
    attended_two, logsum_two = attend_forward(
        cross_query, heads_of(cross_key), heads_of(cross_value), cross_ok
    )
    resid_two = resid_one + swap_sum(product_plain(attended_two, c_out))

    normed, scaled_three, inverse_three = normalize(resid_two, gain_ff, bias_ff)
    input_three = normed.astype(low)
    gate_pre = product_plain(input_three, w_gate)
    up_pre = product_plain(input_three, w_up)
    sigmoid_gate = jax.nn.sigmoid(gate_pre)
    mixed_low = (gate_pre * sigmoid_gate * up_pre).astype(low)
    result = resid_two + swap_sum(product_plain(mixed_low, w_down))

    grad_ff_out = out_grad.astype(low)
    grad_w_down = generic_sum(grad_ff_out, mixed_low).T
    grad_mixed = product_with_rows(grad_ff_out, w_down)
    grad_gate = (
        grad_mixed * up_pre * sigmoid_gate * (1.0 + gate_pre * (1.0 - sigmoid_gate))
    ).astype(low)
    grad_up = (grad_mixed * gate_pre * sigmoid_gate).astype(low)
    grad_w_gate = generic_sum(input_three, grad_gate)
    grad_w_up = generic_sum(input_three, grad_up)
    normed_grad_three = swap_sum(
        product_with_rows(grad_gate, w_gate) + product_with_rows(grad_up, w_up)
    )
    back_three, grad_gain_ff, grad_bias_ff = normalize_back(
        normed_grad_three, scaled_three, inverse_three, gain_ff
    )
    grad_two = out_grad + back_three
    grad_cross_out = grad_two.astype(low)
    grad_c_out = generic_sum(grad_cross_out, attended_two).T
    grad_attended_two = product_with_rows(grad_cross_out, c_out).astype(low)
    cross_query_grad, cross_key_grad, cross_value_grad = attend_backward(
        cross_query,
        heads_of(cross_key),
        heads_of(cross_value),
        cross_ok,
        grad_attended_two,
        logsum_two,
    )
    cross_query_grad = cross_query_grad.astype(low)
    cross_key_grad = cross_key_grad.astype(low)
    cross_value_grad = cross_value_grad.astype(low)
    grad_c_query = generic_sum(input_two, cross_query_grad)
    grad_c_key = generic_sum(context_flat, cross_key_grad)
    grad_c_value = generic_sum(context_flat, cross_value_grad)
    normed_grad_two = swap_sum(product_with_rows(cross_query_grad, c_query))
    back_two, grad_gain_cross, grad_bias_cross = normalize_back(
        normed_grad_two, scaled_two, inverse_two, gain_cross
    )
    grad_one = grad_two + back_two
    grad_self_out = grad_one.astype(low)
    grad_w_out = generic_sum(grad_self_out, attended_one).T
    grad_attended_one = product_with_rows(grad_self_out, w_out).astype(low)
    query_grad, key_grad, value_grad = attend_backward(
        query_one, heads_of(key_one), heads_of(value_one), self_ok, grad_attended_one, logsum_one
    )
    query_grad = rotate_back(query_grad, tables).astype(low)
    key_grad = rotate_back(key_grad, tables).astype(low)
    value_grad = value_grad.astype(low)
    grad_w_query = generic_sum(input_one, query_grad)
    grad_w_key = generic_sum(input_one, key_grad)
    grad_w_value = generic_sum(input_one, value_grad)
    normed_grad_one = swap_sum(
        product_with_rows(query_grad, w_query)
        + product_with_rows(key_grad, w_key)
        + product_with_rows(value_grad, w_value)
    )
    back_one, grad_gain_attn, grad_bias_attn = normalize_back(
        normed_grad_one, scaled_one, inverse_one, gain_attn
    )
    grad_hidden = grad_one + back_one
    vectors = vector_sum(
        jnp.stack(
            [
                grad_gain_attn,
                grad_bias_attn,
                grad_gain_cross,
                grad_bias_cross,
                grad_gain_ff,
                grad_bias_ff,
            ]
        )
    )
    return (
        result,
        grad_hidden,
        vectors[0],
        vectors[1],
        vectors[2],
        vectors[3],
        vectors[4],
        vectors[5],
        grad_w_query,
        grad_w_key,
        grad_w_value,
        grad_w_out,
        grad_c_query,
        grad_c_key,
        grad_c_value,
        grad_c_out,
        grad_w_gate,
        grad_w_up,
        grad_w_down,
    )


def solution(mesh):
    in_specs = (
        P("dp", None),
        P("dp", None),
        P("dp", None, None),
        P("dp"),
        P("dp"),
        P(),
        P(),
        P(),
        P(),
        P(),
        P(),
        P(None, "tensor"),
        P(None, "tensor"),
        P(None, "tensor"),
        P("tensor", None),
        P(None, "tensor"),
        P(None, "tensor"),
        P(None, "tensor"),
        P("tensor", None),
        P(None, "tensor"),
        P(None, "tensor"),
        P("tensor", None),
    )
    out_specs = (
        P("dp", None),
        P("dp", None),
        P(("dp", "tensor")),
        P(("dp", "tensor")),
        P(("dp", "tensor")),
        P(("dp", "tensor")),
        P(("dp", "tensor")),
        P(("dp", "tensor")),
        P("dp", "tensor"),
        P("dp", "tensor"),
        P("dp", "tensor"),
        P("tensor", "dp"),
        P("dp", "tensor"),
        P("dp", "tensor"),
        P("dp", "tensor"),
        P("tensor", "dp"),
        P("dp", "tensor"),
        P("dp", "tensor"),
        P("tensor", "dp"),
    )
    known = mesh.shape["dp"] == PLANE * LEVELS and mesh.shape["tensor"] == 2
    return jax.shard_map(
        on_plane if known else on_any, mesh=mesh, in_specs=in_specs, out_specs=out_specs, check_vma=False
    )
```

```python
import functools
import math

import jax
import jax.numpy as jnp
from jax import lax
from jax.experimental import pallas as pl
from jax.experimental.pallas import tpu as pltpu
from jax.sharding import PartitionSpec as P

PROMPT = 128
HEAD = 64
PLANE = 4
LEVELS = 4
VMEM_LIMIT = 60 * 2**20
COST = 3
FLOOR = 15 * 10**9

low = jnp.bfloat16
f32 = jnp.float32
sds = jax.ShapeDtypeStruct


norm_eps = 1e-05
score_scale = 0.125
masked_score = -1e30


def product_plain(left_side, right_side):
    return jnp.dot(left_side, right_side, preferred_element_type=jnp.float32)


def product_over_rows(left_side, right_side):
    return lax.dot_general(
        left_side, right_side, (((0,), (0,)), ((), ())), preferred_element_type=jnp.float32
    )


def product_with_rows(left_side, right_side):
    return lax.dot_general(
        left_side, right_side, (((1,), (1,)), ((), ())), preferred_element_type=jnp.float32
    )


def rotary_tables(positions, width):
    dim_index = jnp.arange(width) % HEAD
    freq_index = (dim_index % 16).astype(jnp.float32)
    inverse_freq = jnp.exp(freq_index * (-math.log(10000.0) / 16.0))
    angles = positions[:, None] * inverse_freq[None, :]
    cosine = jnp.cos(angles)
    sine_part = jnp.sin(angles)
    cos_table = jnp.where(dim_index < 32, cosine, 1.0)
    sin_lower = jnp.where(dim_index < 16, -sine_part, 0.0)
    sin_upper = jnp.where((dim_index >= 16) & (dim_index < 32), sine_part, 0.0)
    return (cos_table, sin_lower, sin_upper)


def rotate(values, tables):
    cos_table, sin_lower, sin_upper = tables
    return (
        values * cos_table
        + jnp.roll(values, -16, axis=1) * sin_lower
        + jnp.roll(values, 16, axis=1) * sin_upper
    )


def rotate_back(incoming, tables):
    cos_table, sin_lower, sin_upper = tables
    return (
        incoming * cos_table
        + jnp.roll(incoming * sin_lower, 16, axis=1)
        + jnp.roll(incoming * sin_upper, -16, axis=1)
    )


def normalize(values, norm_gain, norm_shift):
    average = jnp.mean(values, axis=-1, keepdims=True)
    centered = values - average
    variance = jnp.mean(centered * centered, axis=-1, keepdims=True)
    inverse = lax.rsqrt(variance + norm_eps)
    scaled = centered * inverse
    return (scaled * norm_gain + norm_shift, scaled, inverse)


def normalize_back(incoming, scaled, inverse, norm_gain):
    grad_gain = jnp.sum(incoming * scaled, axis=0)
    grad_shift = jnp.sum(incoming, axis=0)
    weighted = incoming * norm_gain
    grad_input = inverse * (
        weighted
        - jnp.mean(weighted, axis=-1, keepdims=True)
        - scaled * jnp.mean(weighted * scaled, axis=-1, keepdims=True)
    )
    return (grad_input, grad_gain, grad_shift)


def heads_of(values):
    return values.reshape(values.shape[0], values.shape[1] // HEAD, HEAD)


def attend_forward(query_block, key_heads, value_heads, allowed):
    query_heads = heads_of(query_block)
    scores = (
        jnp.einsum("qhd,khd->hqk", query_heads, key_heads, preferred_element_type=jnp.float32)
        * score_scale
    )
    scores = jnp.where(allowed[None], scores, masked_score)
    largest = jnp.max(scores, axis=-1, keepdims=True)
    exp_scores = jnp.exp(scores - largest)
    totals = jnp.sum(exp_scores, axis=-1, keepdims=True)
    soft_weights = (exp_scores / totals).astype(jnp.bfloat16)
    mixed_heads = jnp.einsum(
        "hqk,khd->qhd", soft_weights, value_heads, preferred_element_type=jnp.float32
    )
    mixed_flat = mixed_heads.reshape(query_block.shape[0], query_block.shape[1]).astype(
        jnp.bfloat16
    )
    return (mixed_flat, largest[..., 0] + jnp.log(totals[..., 0]))


def attend_backward(query_block, key_heads, value_heads, allowed, grad_block, logsum_block):
    query_heads = heads_of(query_block)
    grad_heads = heads_of(grad_block)
    scores = (
        jnp.einsum("qhd,khd->hqk", query_heads, key_heads, preferred_element_type=jnp.float32)
        * score_scale
    )
    scores = jnp.where(allowed[None], scores, masked_score)
    soft_weights = jnp.exp(scores - logsum_block[..., None])
    grad_weights = jnp.einsum(
        "qhd,khd->hqk", grad_heads, value_heads, preferred_element_type=jnp.float32
    )
    inner_sum = jnp.sum(soft_weights * grad_weights, axis=-1, keepdims=True)
    grad_scores = (soft_weights * (grad_weights - inner_sum)).astype(jnp.bfloat16)
    grad_query = (
        jnp.einsum("hqk,khd->qhd", grad_scores, key_heads, preferred_element_type=jnp.float32)
        * score_scale
    )
    grad_key = (
        jnp.einsum("hqk,qhd->khd", grad_scores, query_heads, preferred_element_type=jnp.float32)
        * score_scale
    )
    grad_value = jnp.einsum(
        "hqk,qhd->khd",
        soft_weights.astype(jnp.bfloat16),
        grad_heads,
        preferred_element_type=jnp.float32,
    )
    return (
        grad_query.reshape(query_block.shape),
        grad_key.reshape(grad_key.shape[0], -1),
        grad_value.reshape(grad_value.shape[0], -1),
    )


def swap_sum(partial):
    low = partial.astype(jnp.bfloat16)
    if lax.axis_size("tensor") == 2:
        other = lax.ppermute(low, "tensor", [(0, 1), (1, 0)])
        return low.astype(jnp.float32) + other.astype(jnp.float32)
    return lax.psum(low, "tensor").astype(jnp.float32)


def pairs(mask):
    return [(i, i ^ mask) for i in range(16)]


def own_share(vectors):
    share = vectors.shape[1] // (lax.axis_size("dp") * lax.axis_size("tensor"))
    index = lax.axis_index("dp") * lax.axis_size("tensor") + lax.axis_index("tensor")
    return lax.dynamic_slice_in_dim(vectors, index * share, share, 1)


def generic_sum(rows_side, column_side):
    return lax.psum_scatter(
        product_over_rows(rows_side, column_side).astype(jnp.bfloat16),
        "dp",
        scatter_dimension=0,
        tiled=True,
    ).astype(jnp.float32)


def add_low(*terms):
    total = terms[0].astype(jnp.float32)
    for term in terms[1:]:
        total = total + term.astype(jnp.float32)
    return total


def ff_parts(gate, up, grad_mixed):
    sig = 1.0 / (1.0 + jnp.exp(-gate))
    act = gate * sig
    return (
        (act * up).astype(low),
        (grad_mixed * up * sig * (1.0 + gate * (1.0 - sig))).astype(low),
        (grad_mixed * act).astype(low),
    )


def turn(values, cos, lower, upper):
    width = values.shape[1]
    return (values * cos + pltpu.roll(values, width - 16, 1) * lower + pltpu.roll(values, 16, 1) * upper)

def turn_back(values, cos, lower, upper):
    width = values.shape[1]
    return (values * cos + pltpu.roll(values * lower, 16, 1) + pltpu.roll(values * upper, width - 16, 1))

def normed_rows(values, gain, shift):
    average = jnp.mean(values, axis=-1, keepdims=True)
    centered = values - average
    variance = jnp.mean(centered * centered, axis=-1, keepdims=True)
    return centered * lax.rsqrt(variance + norm_eps) * gain + shift

def over_rows(rows, body, chunk=32):
    @pl.loop(0, rows // chunk, unroll=min(4, rows // chunk))
    def _(i):
        body(pl.ds(pl.multiple_of(i * chunk, chunk), chunk))

def attend(q, k, v, mask, lse_ref):
    q_turned = (q * jnp.bfloat16(0.125)).T
    v_turned = v.T
    outs = []
    for h in range(q.shape[1] // HEAD):
        c = slice(h * HEAD, (h + 1) * HEAD)
        s = product_plain(k[:, c], q_turned[c, :]) + mask
        m = jnp.max(s, axis=0, keepdims=True)
        e = jnp.exp(s - m)
        total = jnp.sum(e, axis=0, keepdims=True)
        o = product_plain(v_turned[c, :], e.astype(low)) * (1.0 / total)
        outs.append(o)
        lse_ref[h : h + 1, :] = m + jnp.log(total)
    return jnp.concatenate(outs, axis=0).T.astype(low)


def attend_back(q, k, v, g, mask, lse):
    scaled = q * jnp.bfloat16(0.125)
    q_turned = scaled.T
    g_turned = g.T
    k_turned = k.T
    dq, dk, dv = [], [], []
    for h in range(q.shape[1] // HEAD):
        c = slice(h * HEAD, (h + 1) * HEAD)
        p = jnp.exp(product_plain(k[:, c], q_turned[c, :]) + (mask - lse[h : h + 1, :]))
        dp = product_plain(v[:, c], g_turned[c, :])
        inner = jnp.sum(p * dp, axis=0, keepdims=True)
        ds = (p * (dp - inner)).astype(low)
        dq.append(product_plain(k_turned[c, :], ds))
        dk.append(product_plain(ds, scaled[:, c]))
        dv.append(product_plain(p.astype(low), g[:, c]))
    return (
        jnp.concatenate(dq, axis=0).T * 0.125,
        jnp.concatenate(dk, axis=1),
        jnp.concatenate(dv, axis=1),
    )


def self_mask(split, T):
    r=lax.broadcasted_iota(jnp.int32,(T,T),0)>=split
    c=lax.broadcasted_iota(jnp.int32,(T,T),1)>=split
    return jnp.where(r==c,0.0,masked_score).astype(f32)

def cross_mask(split, first, second, T, K):
    r = lax.broadcasted_iota(jnp.int32, (K, T), 1) >= split
    c = lax.broadcasted_iota(jnp.int32, (K, T), 0)
    least = jnp.where(r, K // 2, 0)
    most = jnp.where(r, K // 2 + second, first)
    return jnp.where((c >= least) & (c < most), 0.0, masked_score).astype(f32)


def norm_back_rows(x,e,gain,above,gain_acc,shift_acc):
    average=jnp.mean(x,axis=-1,keepdims=True)
    centered=x-average
    variance=jnp.mean(centered*centered,axis=-1,keepdims=True)
    inverse=lax.rsqrt(variance+norm_eps)
    n=centered*inverse
    en=e*n
    w=e*gain
    mean_w=jnp.mean(w,axis=-1,keepdims=True)
    mean_wn=jnp.mean(en*gain,axis=-1,keepdims=True)
    fold=lambda t: jnp.sum(t.reshape(t.shape[0]//8,8,t.shape[1]),axis=0)
    gain_acc[...]+=fold(en)
    shift_acc[...]+=fold(e)
    return above+inverse*(w-mean_w-n*mean_wn)

def norm_back_all(x,mine,other,above,gain,total,total_low,vec,gacc,sacc):
    gacc[...]=jnp.zeros_like(gacc);sacc[...]=jnp.zeros_like(sacc)
    def rows(r):
        e=mine[r,:].astype(f32)+other[r,:].astype(f32)
        t=norm_back_rows(x[r,:],e,gain[...],above[r,:],gacc,sacc)
        total[r,:]=t
        if total_low is not None: total_low[r,:]=t.astype(low)
    over_rows(x.shape[0],rows)
    vec[0:1,:]=jnp.sum(gacc[...],axis=0,keepdims=True)
    vec[1:2,:]=jnp.sum(sacc[...],axis=0,keepdims=True)


def ordered(kernel, token, args, in_specs, out_specs, out_shape, grid, flops, scratch=(), info=None, brief=False):
    if info is None:
        info = jnp.zeros((1,), jnp.int32)
    inputs, outputs = len(args), len(out_shape)

    def body(info_ref, *refs):
        token_ref = refs[inputs + 1 + outputs]

        @pl.when(functools.reduce(jnp.logical_and, [pl.program_id(i) == 0 for i in range(len(grid))]))
        def _():
            token_ref[...] = jnp.zeros_like(token_ref)

        kernel(
            info_ref,
            *refs[:inputs],
            *refs[inputs + 1 : inputs + 1 + outputs],
            *refs[inputs + 2 + outputs :],
        )

    moved = sum(math.prod(a.shape) * a.dtype.itemsize for a in (*args, *out_shape))
    *results, token = pl.pallas_call(
        body,
        grid_spec=pltpu.PrefetchScalarGridSpec(
            num_scalar_prefetch=1,
            grid=grid,
            in_specs=[*in_specs, pl.BlockSpec(memory_space=pl.ANY)],
            out_specs=[*out_specs, pl.BlockSpec((8, 128), lambda *_: (0, 0))],
            scratch_shapes=list(scratch),
        ),
        out_shape=[*out_shape, sds((8, 128), f32)],
        compiler_params=pltpu.CompilerParams(vmem_limit_bytes=VMEM_LIMIT),
        cost_estimate=pl.CostEstimate(flops=0 if brief else max(FLOOR, int(flops * COST)), bytes_accessed=0 if brief else int(moved * COST), transcendentals=0),
    )(info, *args, token)
    return (*results, token)


def hold(token, values):
    def nothing(values_ref, token_ref, out_ref, token_out):
        token_out[...] = jnp.zeros_like(token_out)

    return pl.pallas_call(
        nothing,
        in_specs=[pl.BlockSpec(memory_space=pl.ANY)] * 2,
        out_specs=[pl.BlockSpec(memory_space=pl.ANY), pl.BlockSpec(memory_space=pltpu.VMEM)],
        out_shape=[sds(values.shape, values.dtype), sds((8, 128), f32)],
        input_output_aliases={0: 0},
        compiler_params=pltpu.CompilerParams(vmem_limit_bytes=VMEM_LIMIT),
        cost_estimate=pl.CostEstimate(flops=FLOOR, bytes_accessed=0, transcendentals=0),
    )(values, token)


def specs(frames, width, tile):
    whole = pl.BlockSpec((frames, width), lambda j, *_: (0, 0))
    vector = pl.BlockSpec((1, width), lambda j, *_: (0, 0))
    column = pl.BlockSpec((width, tile), lambda j, *_: (0, j))
    row = pl.BlockSpec((tile, width), lambda j, *_: (j, 0))
    act = pl.BlockSpec((frames, tile), lambda j, *_: (0, j))
    table = pl.BlockSpec((frames, tile), lambda j, *_: (0, 0))
    logsum = pl.BlockSpec((8, frames), lambda j, *_: (j, 0))
    return whole, vector, column, row, act, table, logsum


def added(acc, term, result):
    step = pl.program_id(0)

    @pl.when(step == 0)
    def _():
        acc[...] = term

    @pl.when(step != 0)
    def _():
        acc[...] += term

    @pl.when(step == pl.num_programs(0) - 1)
    def _():
        result[...] = acc[...].astype(result.dtype)


def self_kernel(info, hid, gain, shift, wq, wk, wv, wo, cos, lower, upper, normed, q, k, v, att, logsum, part, acc, mask):
    frames = hid.shape[0]

    @pl.when(pl.program_id(0) == 0)
    def _():
        def rows(r):
            normed[r, :] = normed_rows(hid[r, :], gain[...], shift[...]).astype(low)

        over_rows(frames, rows)
        mask[...] = self_mask(info[0], frames)

    n = normed[...]
    tables = (cos[...], lower[...], upper[...])
    q[...] = turn(product_plain(n, wq[...]), *tables).astype(low)
    k[...] = turn(product_plain(n, wk[...]), *tables).astype(low)
    v[...] = product_plain(n, wv[...]).astype(low)
    attended = attend(q[...], k[...], v[...], mask[...], logsum)
    att[...] = attended
    added(acc, product_plain(attended, wo[...]), part)


def self_forward(token, info, hid, gain, shift, wq, wk, wv, wo, tables, tile=4 * HEAD):
    frames, width = hid.shape
    columns = wq.shape[1]
    whole, vector, column, row, act, table, logsum = specs(frames, width, tile)
    return ordered(
        self_kernel,
        token,
        (hid, gain, shift, wq, wk, wv, wo, *tables),
        [whole, vector, vector, column, column, column, row, table, table, table],
        [whole, act, act, act, act, logsum, whole],
        [sds((frames, width), low)]
        + [sds((frames, columns), low)] * 4
        + [sds((columns // tile * 8, frames), f32), sds((frames, width), low)],
        (columns // tile,),
        2 * frames * columns * (4 * width + 8 * frames),
        [pltpu.VMEM((frames, width), f32), pltpu.VMEM((frames, frames), f32)],
        info,
    )


def cross_kernel(info, hid, mine, other, gain, shift, cq, ck, cv, co, total, normed, q, att, logsum, part, acc, mask):
    frames = hid.shape[0]

    @pl.when(pl.program_id(0) == 0)
    def _():
        def rows(r):
            x = hid[r, :] + (mine[r, :].astype(f32) + other[r, :].astype(f32))
            total[r, :] = x
            normed[r, :] = normed_rows(x, gain[...], shift[...]).astype(low)

        over_rows(frames, rows)
        mask[...] = cross_mask(info[0], info[1], info[2], frames, ck.shape[0])

    q[...] = product_plain(normed[...], cq[...]).astype(low)
    attended = attend(q[...], ck[...], cv[...], mask[...], logsum)
    att[...] = attended
    added(acc, product_plain(attended, co[...]), part)


def cross_forward(token, info, hid, mine, other, gain, shift, cq, ck, cv, co, tile=4 * HEAD):
    frames, width = hid.shape
    columns, keys = cq.shape[1], ck.shape[0]
    whole, vector, column, row, act, table, logsum = specs(frames, width, tile)
    key = pl.BlockSpec((keys, tile), lambda j, *_: (0, j))
    return ordered(
        cross_kernel,
        token,
        (hid, mine, other, gain, shift, cq, ck, cv, co),
        [whole, whole, whole, vector, vector, column, key, key, row],
        [whole, whole, act, act, logsum, whole],
        [
            sds((frames, width), f32),
            sds((frames, width), low),
            sds((frames, columns), low),
            sds((frames, columns), low),
            sds((columns // tile * 8, frames), f32),
            sds((frames, width), low),
        ],
        (columns // tile,),
        2 * frames * columns * (2 * width + 8 * keys),
        [pltpu.VMEM((frames, width), f32), pltpu.VMEM((keys, frames), f32)],
        info,
        brief=True,
    )


def norm_kernel(_, hid, mine, other, gain, shift, total, normed):
    def rows(r):
        x = hid[r, :] + (mine[r, :].astype(f32) + other[r, :].astype(f32))
        total[r, :] = x
        normed[r, :] = normed_rows(x, gain[...], shift[...]).astype(low)

    over_rows(hid.shape[0], rows)


def norm_forward(token, hid, mine, other, gain, shift, block=128):
    frames, width = hid.shape
    rows = pl.BlockSpec((block, width), lambda j, *_: (j, 0))
    vector = pl.BlockSpec((1, width), lambda j, *_: (0, 0))
    return ordered(
        norm_kernel,
        token,
        (hid, mine, other, gain, shift),
        [rows, rows, rows, vector, vector],
        [rows, rows],
        [sds((frames, width), f32), sds((frames, width), low)],
        (frames // block,),
        10 * frames * width,
        brief=True,
    )


def cross_back_kernel(info, x, mine, other, above, gain, co, q, ck, cv, logsum, cq, total, total_low, vectors, dq, dk, dv, part, acc, mask, gain_acc, shift_acc):
    @pl.when(pl.program_id(0) == 0)
    def _():
        norm_back_all(x, mine, other, above, gain, total, total_low, vectors, gain_acc, shift_acc)
        mask[...] = cross_mask(info[0], info[1], info[2], x.shape[0], ck.shape[0])

    g = product_with_rows(total_low[...], co[...]).astype(low)
    a, b, c = attend_back(q[...], ck[...], cv[...], g, mask[...], logsum[...])
    a = a.astype(low)
    dq[...] = a
    dk[...] = b.astype(low)
    dv[...] = c.astype(low)
    added(acc, product_with_rows(a, cq[...]), part)


def cross_backward(token, info, x, mine, other, above, gain, co, q, ck, cv, logsums, cq, tile=4 * HEAD):
    frames, width = x.shape
    columns, keys = cq.shape[1], ck.shape[0]
    whole, vector, column, row, act, table, logsum = specs(frames, width, tile)
    key = pl.BlockSpec((keys, tile), lambda j, *_: (0, j))
    two = pl.BlockSpec((2, width), lambda j, *_: (0, 0))
    return ordered(
        cross_back_kernel,
        token,
        (x, mine, other, above, gain, co, q, ck, cv, logsums, cq),
        [whole, whole, whole, whole, vector, row, act, key, key, logsum, column],
        [whole, whole, two, act, key, key, whole],
        [
            sds((frames, width), f32),
            sds((frames, width), low),
            sds((2, width), f32),
            sds((frames, columns), low),
            sds((keys, columns), low),
            sds((keys, columns), low),
            sds((frames, width), low),
        ],
        (columns // tile,),
        2 * frames * columns * (2 * width + 20 * keys),
        [
            pltpu.VMEM((frames, width), f32),
            pltpu.VMEM((keys, frames), f32),
            pltpu.VMEM((8, width), f32),
            pltpu.VMEM((8, width), f32),
        ],
        info,
    )


def self_back_kernel(info, x, mine, other, above, gain, wo, q, k, v, logsum, wq, wk, wv, cos, lower, upper, total, total_low, vectors, grads, part, acc, mask, gain_acc, shift_acc):
    frames = x.shape[0]

    @pl.when(pl.program_id(0) == 0)
    def _():
        norm_back_all(x, mine, other, above, gain, total, total_low, vectors, gain_acc, shift_acc)
        mask[...] = self_mask(info[0], frames)

    g = product_with_rows(total_low[...], wo[...]).astype(low)
    a, b, c = attend_back(q[...], k[...], v[...], g, mask[...], logsum[...])
    tables = (cos[...], lower[...], upper[...])
    a = turn_back(a, *tables).astype(low)
    b = turn_back(b, *tables).astype(low)
    c = c.astype(low)
    for index, values in enumerate((a, b, c)):
        turned = values.T
        for quarter in range(PLANE):
            grads[quarter, index] = turned[quarter * HEAD : (quarter + 1) * HEAD]
    added(
        acc,
        product_with_rows(a, wq[...]) + product_with_rows(b, wk[...]) + product_with_rows(c, wv[...]),
        part,
    )


def self_backward(token, info, x, mine, other, above, gain, wo, q, k, v, logsums, wq, wk, wv, tables, tile=4 * HEAD):
    frames, width = x.shape
    columns = wq.shape[1]
    whole, vector, column, row, act, table, logsum = specs(frames, width, tile)
    two = pl.BlockSpec((2, width), lambda j, *_: (0, 0))
    heads = pl.BlockSpec((PLANE, 3, HEAD, frames), lambda j, *_: (0, 0, j, 0))
    return ordered(
        self_back_kernel,
        token,
        (x, mine, other, above, gain, wo, q, k, v, logsums, wq, wk, wv, *tables),
        [whole, whole, whole, whole, vector, row, act, act, act, logsum, column, column, column, table, table, table],
        [whole, whole, two, heads, whole],
        [
            sds((frames, width), f32),
            sds((frames, width), low),
            sds((2, width), f32),
            sds((PLANE, 3, columns // PLANE, frames), low),
            sds((frames, width), low),
        ],
        (columns // tile,),
        2 * frames * columns * (4 * width + 20 * frames),
        [
            pltpu.VMEM((frames, width), f32),
            pltpu.VMEM((frames, frames), f32),
            pltpu.VMEM((8, width), f32),
            pltpu.VMEM((8, width), f32),
        ],
        info,
    )


def last_kernel(_, x, mine, other, above, gain, total, vectors, gain_acc, shift_acc):
    step = pl.program_id(0)

    @pl.when(step == 0)
    def _():
        gain_acc[...] = jnp.zeros_like(gain_acc)
        shift_acc[...] = jnp.zeros_like(shift_acc)

    def rows(r):
        e = mine[r, :].astype(f32) + other[r, :].astype(f32)
        total[r, :] = norm_back_rows(x[r, :], e, gain[...], above[r, :], gain_acc, shift_acc)

    over_rows(x.shape[0], rows)

    @pl.when(step == pl.num_programs(0) - 1)
    def _():
        vectors[0:1, :] = jnp.sum(gain_acc[...], axis=0, keepdims=True)
        vectors[1:2, :] = jnp.sum(shift_acc[...], axis=0, keepdims=True)


def last_backward(token, x, mine, other, above, gain, block=128):
    frames, width = x.shape
    rows = pl.BlockSpec((block, width), lambda j, *_: (j, 0))
    vector = pl.BlockSpec((1, width), lambda j, *_: (0, 0))
    two = pl.BlockSpec((2, width), lambda j, *_: (0, 0))
    return ordered(
        last_kernel,
        token,
        (x, mine, other, above, gain),
        [rows, rows, rows, rows, vector],
        [rows, two],
        [sds((frames, width), f32), sds((2, width), f32)],
        (frames // block,),
        20 * frames * width,
        [pltpu.VMEM((8, width), f32), pltpu.VMEM((8, width), f32)],
    )


def pack_kernel(_, *refs):
    for values, copies in zip(refs[: len(refs) // 2], refs[len(refs) // 2 :]):
        copies[...] = values[...]


def packed(token, values, half, pieces=1):
    frames, width = values.shape
    rows = frames // (2 * pieces)

    def source(piece):
        return pl.BlockSpec((rows, width), lambda j, info: (info[0] * pieces + piece, 0))

    return ordered(
        pack_kernel,
        token,
        (values,) * pieces,
        [source(piece) for piece in range(pieces)],
        [pl.BlockSpec((rows, width), lambda j, info: (j, 0))] * pieces,
        [sds((PLANE * rows, width), low)] * pieces,
        (PLANE,),
        0,
        info=half,
        brief=True,
    )


def ff_kernel(_, in_ref, out_ref, gate_ref, up_ref, down_ref, sum_ref, back_ref, sum_acc, back_acc):
    normed = in_ref[...]
    mixed, grad_gate, grad_up = ff_parts(
        product_plain(normed, gate_ref[...]),
        product_plain(normed, up_ref[...]),
        product_with_rows(out_ref[...], down_ref[...]),
    )
    added(sum_acc, product_plain(mixed, down_ref[...]), sum_ref)
    added(
        back_acc,
        product_with_rows(grad_gate, gate_ref[...]) + product_with_rows(grad_up, up_ref[...]),
        back_ref,
    )


def ff_both(token, normed, grad_out, w_gate, w_up, w_down, tile=512):
    frames, width = normed.shape
    units = w_gate.shape[1]
    whole, _, column, row, *_ = specs(frames, width, tile)
    return ordered(
        ff_kernel,
        token,
        (normed, grad_out, w_gate, w_up, w_down),
        [whole, whole, column, column, row],
        [whole, whole],
        [sds((frames, width), low)] * 2,
        (units // tile,),
        12 * frames * width * units,
        [pltpu.VMEM((frames, width), f32)] * 2,
    )


def share_kernel(info, in_mine, in_other, out_a, out_b, out_c, out_d, gate_ref, up_ref, down_ref, send_ref, keep_ref, acc):
    step = pl.program_id(0)
    normed = jnp.concatenate([in_mine[...], in_other[...]], axis=0)
    grad_out = jnp.concatenate([out_a[...], out_b[...], out_c[...], out_d[...]], axis=0)
    mixed, grad_gate, grad_up = ff_parts(
        product_plain(normed, gate_ref[...]),
        product_plain(normed, up_ref[...]),
        product_with_rows(grad_out, down_ref[...]),
    )
    fresh = (
        product_over_rows(grad_out, mixed),
        product_over_rows(normed, grad_gate),
        product_over_rows(normed, grad_up),
    )
    for index, term in enumerate(fresh):

        @pl.when(step == 0)
        def _():
            acc[index] = term

        @pl.when(step != 0)
        def _():
            acc[index] += term

    @pl.when(step == pl.num_programs(0) - 1)
    def _():
        rows = send_ref.shape[1] // 3
        for pair in range(2):
            for index in range(3):
                for ref, parity in ((send_ref, 1 - info[1]), (keep_ref, info[1])):
                    start = pl.multiple_of((2 * pair + parity) * rows, rows)
                    ref[pair, index * rows : (index + 1) * rows] = acc[
                        index, pl.ds(start, rows), :
                    ].astype(ref.dtype)


def ff_share(token, info, normed, grad_out, w_gate, w_up, w_down, tile):
    frames, width = normed[0].shape
    chunk = frames // PLANE
    rows = pl.BlockSpec((chunk, width), lambda j, info: (j, 0))
    column = pl.BlockSpec((width, tile), lambda j, info: (0, info[0]))
    half = (LEVELS // 2, 3 * width // LEVELS, tile)
    return ordered(
        share_kernel,
        token,
        (*normed, *grad_out, w_gate, w_up, w_down),
        [rows] * 2
        + [pl.BlockSpec((chunk // 2, width), lambda j, info: (j, 0))] * 4
        + [column, column, pl.BlockSpec((tile, width), lambda j, info: (info[0], 0))],
        [pl.BlockSpec(half, lambda j, info: (0, 0, 0))] * 2,
        [sds(half, low)] * 2,
        (PLANE,),
        24 * frames * width * tile,
        [pltpu.VMEM((3, width, tile), f32)],
        info,
    )


def weight_kernel(plan, sides_count, _, *refs):
    sides, columns = refs[:sides_count], refs[sides_count : sides_count + len(plan)]
    out = refs[sides_count + len(plan)]
    turned = refs[sides_count + len(plan) + 1 :]

    @pl.when(pl.program_id(0) == 0)
    def _():
        for side, ref in zip(sides, turned):
            ref[...] = side[...].T

    for (which, first), column in zip(plan, columns):
        product = product_plain(turned[which][...], column[...]).astype(low)
        rows = product.shape[0] // (PLANE * LEVELS)
        product = product.reshape(LEVELS, PLANE, rows, product.shape[1])
        for owner in range(PLANE):
            out[owner, :, first : first + rows, :] = product[:, owner]


def weight_products(token, sides, plan, columns, tile=256):
    width = columns[0].shape[1]
    rows = sum(sides[which].shape[1] for which, _ in plan) // (PLANE * LEVELS)
    return ordered(
        functools.partial(weight_kernel, plan, len(sides)),
        token,
        (*sides, *columns),
        [pl.BlockSpec(side.shape, lambda j, *_: (0, 0)) for side in sides]
        + [pl.BlockSpec((column.shape[0], tile), lambda j, *_: (0, j)) for column in columns],
        [pl.BlockSpec((PLANE, LEVELS, rows, tile), lambda j, *_: (0, 0, 0, j))],
        [sds((PLANE, LEVELS, rows, width), low)],
        (width // tile,),
        sum(2 * sides[w].shape[0] * sides[w].shape[1] * width for w, _ in plan),
        [pltpu.VMEM((side.shape[1], side.shape[0]), low) for side in sides],
    )


def plane_sum_kernel(info, got, send, keep):
    for ref, parity in ((send, 1 - info[0]), (keep, info[0])):
        total = got[0, 0, parity].astype(f32)
        for source in range(1, PLANE):
            total = total + got[source, 0, parity].astype(f32)
        ref[0] = total.astype(low)


def plane_sum(token, got, parity):
    rows, width = got.shape[2:]
    out = pl.BlockSpec((1, rows, width), lambda j, *_: (j, 0, 0))
    return ordered(
        plane_sum_kernel,
        token,
        (got.reshape(PLANE, 2, 2, rows, width),),
        [pl.BlockSpec((PLANE, 1, 2, rows, width), lambda j, *_: (0, j, 0, 0, 0))],
        [out, out],
        [sds((2, rows, width), low)] * 2,
        (2,),
        0,
        info=parity,
    )


def level_sum_kernel(_, keep_pass, got_pass, keep_own, got_own, passed, own):
    passed[...] = (keep_pass[0].astype(f32) + got_pass[0].astype(f32)).astype(low)
    own[...] = keep_own[0].astype(f32) + got_own[0].astype(f32)


def level_sum(token, keep, got, upper):
    rows, width = keep.shape[1:]
    block = rows // 2 if rows % 32 == 0 else rows
    off = pl.BlockSpec((1, block, width), lambda j, info: (1 - info[0], j, 0))
    own = pl.BlockSpec((1, block, width), lambda j, info: (info[0], j, 0))
    out = pl.BlockSpec((block, width), lambda j, info: (j, 0))
    return ordered(
        level_sum_kernel,
        token,
        (keep, got, keep, got),
        [off, off, own, own],
        [out, out],
        [sds((rows, width), low), sds((rows, width), f32)],
        (rows // block,),
        0,
        info=upper,
    )


def head_kernel(info, grads_mine, grads_other, in_mine, in_other, send, keep, acc):
    step = pl.program_id(0)
    rows = acc.shape[0]
    term = product_plain(grads_mine[0].reshape(rows, -1), in_mine[...]) + product_plain(
        grads_other[0].reshape(rows, -1), in_other[...]
    )

    @pl.when(step == 0)
    def _():
        acc[...] = term

    @pl.when(step != 0)
    def _():
        acc[...] += term

    @pl.when(step == pl.num_programs(0) - 1)
    def _():
        width = send.shape[2]
        for level in range(LEVELS):
            for ref, parity in ((send, 1 - info[1]), (keep, info[1])):

                @pl.when(parity == level % 2)
                def _():
                    ref[level // 2] = acc[:, level * width : (level + 1) * width].astype(low)


def head_products(token, info, grads, normed):
    _, three, features, frames = grads.shape
    width = normed[0].shape[1]
    chunk = normed[0].shape[0] // PLANE
    rows = pl.BlockSpec((chunk, width), lambda j, info: (j, 0))
    half = (LEVELS // 2, three * features, width // LEVELS)
    return ordered(
        head_kernel,
        token,
        (grads, grads, *normed),
        [
            pl.BlockSpec((1, three, features, chunk), lambda j, info: (j, 0, 0, info[0])),
            pl.BlockSpec((1, three, features, chunk), lambda j, info: (j, 0, 0, 1 - info[0])),
            rows,
            rows,
        ],
        [pl.BlockSpec(half, lambda j, info: (0, 0, 0))] * 2,
        [sds(half, low)] * 2,
        (PLANE,),
        2 * three * features * PLANE * frames * width,
        [pltpu.VMEM((three * features, width), f32)],
        info,
    )


def on_plane(
    hidden_in,
    out_grad,
    prompt_states,
    row_split,
    prompt_len,
    gain_attn,
    bias_attn,
    gain_cross,
    bias_cross,
    gain_ff,
    bias_ff,
    w_query,
    w_key,
    w_value,
    w_out,
    c_query,
    c_key,
    c_value,
    c_out,
    w_gate,
    w_up,
    w_down,
):
    frames, width = hidden_in.shape
    plane, level = lax.axis_index("dp") % PLANE, lax.axis_index("dp") // PLANE
    info = jnp.concatenate([row_split, prompt_len])
    positions = jnp.arange(frames, dtype=jnp.int32)
    row_ids = (positions >= row_split[0]).astype(jnp.int32)
    tables = rotary_tables((positions - row_ids * row_split[0]).astype(f32), 4 * HEAD)
    gain_attn, bias_attn, gain_cross, bias_cross, gain_ff, bias_ff = (
        vector[None] for vector in (gain_attn, bias_attn, gain_cross, bias_cross, gain_ff, bias_ff)
    )

    zero = jnp.zeros((1,), jnp.int32)
    half = zero + lax.axis_index("tensor")
    parity, upper = zero + level % 2, zero + level // 2
    chips = [[PLANE * z + p for p in range(PLANE)] for z in range(LEVELS)]

    def swapped(part):
        return lax.ppermute(part, "tensor", [(0, 1), (1, 0)])

    def in_plane(values):
        shape = values.shape
        return lax.all_to_all(
            values, "dp", 0, 0, axis_index_groups=chips, tiled=True
        ).reshape(shape)

    def level_swap(values, mask):
        return lax.ppermute(values, "dp", pairs(mask))

    token = jnp.zeros((8, 128), f32)
    grad_ff_out = out_grad.astype(low)
    copies, copies_two, token = packed(token, grad_ff_out, half, 2)
    out_first = in_plane(copies)
    context = prompt_states.reshape(2 * PROMPT, prompt_states.shape[2])
    cross_key = product_plain(context, c_key).astype(low)
    cross_value = product_plain(context, c_value).astype(low)
    input_one, query, key, value, attended_one, logsum_one, part, token = self_forward(
        token, info, hidden_in, gain_attn, bias_attn, w_query, w_key, w_value, w_out, tables
    )
    part_swapped = swapped(part)
    out_first, token = hold(token, out_first)
    out_second = in_plane(copies_two)
    resid_one, input_two, cross_query, attended_two, logsum_two, part, token = cross_forward(
        token,
        info,
        hidden_in,
        part,
        part_swapped,
        gain_cross,
        bias_cross,
        c_query,
        cross_key,
        cross_value,
        c_out,
    )
    part_swapped = swapped(part)
    out_second, token = hold(token, out_second)
    copies_one, token = packed(token, input_one, half)
    resid_two, input_three, token = norm_forward(
        token, resid_one, part, part_swapped, gain_ff, bias_ff
    )
    copies, token = packed(token, input_three, half)
    frames_in = in_plane(copies)
    frames_out = (out_first, out_second, swapped(out_first), swapped(out_second))
    sum_part, back_part, token = ff_both(token, input_three, grad_ff_out, w_gate, w_up, w_down)
    back_swapped = swapped(back_part)
    frames_in, token = hold(token, frames_in)
    frames_in = (frames_in, swapped(frames_in))
    frames_one = in_plane(copies_one)
    grad_two, grad_cross_out, vectors_ff, query_grad, key_grad, value_grad, part, token = cross_backward(
        token,
        info,
        resid_two,
        back_part,
        back_swapped,
        out_grad,
        gain_ff,
        c_out,
        cross_query,
        cross_key,
        cross_value,
        logsum_two,
        c_query,
    )
    part_swapped = swapped(part)

    tile = 256
    tiles = w_gate.shape[1] // (PLANE * tile)

    def share(token, index):
        number = jnp.concatenate([zero + plane * tiles + index, parity])
        return ff_share(token, number, frames_in, frames_out, w_gate, w_up, w_down, tile)

    send_a, keep_a, token = share(token, 0)
    got_a = level_swap(send_a, PLANE)
    r, c = width // 16, context.shape[1] // 16
    products, token = weight_products(
        token,
        [grad_cross_out, input_two, context],
        [(0, 0), (1, r), (2, 2 * r), (2, 2 * r + c)],
        [attended_two, query_grad, key_grad, value_grad],
    )
    frames_one, token = hold(token, frames_one)
    got_cross = in_plane(products)
    frames_one = (frames_one, swapped(frames_one))
    send_b, keep_b, token = share(token, 1)
    got_b = level_swap(send_b, PLANE)
    pass_a, own_a, token = level_sum(token, keep_a, got_a, upper)
    last_a = level_swap(pass_a, 2 * PLANE)
    grad_one, grad_self_out, vectors_cross, grads, part, token = self_backward(
        token,
        info,
        resid_one,
        part,
        part_swapped,
        grad_two,
        gain_cross,
        w_out,
        query,
        key,
        value,
        logsum_one,
        w_query,
        w_key,
        w_value,
        tables,
    )
    part_swapped = swapped(part)
    pass_b, own_b, token = level_sum(token, keep_b, got_b, upper)
    last_b = level_swap(pass_b, 2 * PLANE)
    send_c, keep_c, token = share(token, 2)
    got_c = level_swap(send_c, PLANE)
    last_a, token = hold(token, last_a)
    products, token = weight_products(token, [grad_self_out], [(0, 0)], [attended_one])
    grad_hidden, vectors_attn, token = last_backward(
        token, hidden_in, part, part_swapped, grad_one, gain_attn
    )
    vectors = jnp.concatenate([vectors_attn, vectors_cross, vectors_ff])
    got_cross, token = hold(token, got_cross)
    grads, token = hold(token, grads)
    got_heads = in_plane(grads)
    send_x, keep_x, token = plane_sum(token, got_cross, parity)
    got_x = level_swap(send_x, PLANE)
    last_b, token = hold(token, last_b)
    pass_c, own_c, token = level_sum(token, keep_c, got_c, upper)
    last_c = level_swap(pass_c, 2 * PLANE)
    vectors_got = level_swap(vectors, 1)
    got_heads, token = hold(token, got_heads)
    products, token = hold(token, products)
    got_out = in_plane(products)
    vectors_got, token = hold(token, vectors_got)
    vectors = vectors + vectors_got
    vectors_got = level_swap(vectors, 2)
    send_h, keep_h, token = head_products(
        token, jnp.concatenate([half, parity]), got_heads, frames_one
    )
    got_h = level_swap(send_h, PLANE)
    pass_x, own_x, token = level_sum(token, keep_x, got_x, upper)
    last_x = level_swap(pass_x, 2 * PLANE)
    last_c, token = hold(token, last_c)
    vectors_got, token = hold(token, vectors_got)
    vectors = vectors + vectors_got
    vectors_got = level_swap(vectors, PLANE)
    got_out, token = hold(token, got_out)
    send_o, keep_o, token = plane_sum(token, got_out, parity)
    got_o = level_swap(send_o, PLANE)
    units = jnp.stack([add_low(own_a, last_a), add_low(own_b, last_b), add_low(own_c, last_c)])
    units = units.astype(low).reshape(tiles, 3, PLANE, r, tile).transpose(2, 1, 3, 0, 4)
    units = in_plane(units.reshape(PLANE, 3, r, tiles * tile))
    last_x, token = hold(token, last_x)
    vectors_got, token = hold(token, vectors_got)
    vectors = vectors + vectors_got
    vectors_got = level_swap(vectors, 2 * PLANE)
    pass_h, own_h, token = level_sum(token, keep_h, got_h, upper)
    last_h = level_swap(pass_h, 2 * PLANE)
    pass_o, own_o, token = level_sum(token, keep_o, got_o, upper)
    last_o = level_swap(pass_o, 2 * PLANE)
    units, token = hold(token, units)
    vectors = own_share(vectors + vectors_got)
    result = resid_two + add_low(sum_part, swapped(sum_part))

    units = units.transpose(1, 2, 0, 3).reshape(3, r, w_gate.shape[1]).astype(f32)
    cross = add_low(own_x, last_x)
    heads = add_low(own_h, last_h).astype(low).T
    heads = in_plane(heads.reshape(PLANE, r, heads.shape[1]))
    heads = heads.reshape(PLANE, r, 3, w_query.shape[1] // (PLANE * HEAD), HEAD)
    heads = heads.transpose(2, 1, 3, 0, 4).reshape(3, r, w_query.shape[1]).astype(f32)
    return (
        result,
        grad_hidden,
        *(vectors[index] for index in range(6)),
        heads[0],
        heads[1],
        heads[2],
        add_low(own_o, last_o).T,
        cross[r : 2 * r],
        cross[2 * r : 2 * r + c],
        cross[2 * r + c :],
        cross[:r].T,
        units[1],
        units[2],
        units[0].T,
    )


def on_any(
    hidden_in,
    out_grad,
    prompt_states,
    row_split,
    prompt_len,
    gain_attn,
    bias_attn,
    gain_cross,
    bias_cross,
    gain_ff,
    bias_ff,
    w_query,
    w_key,
    w_value,
    w_out,
    c_query,
    c_key,
    c_value,
    c_out,
    w_gate,
    w_up,
    w_down,
):
    frame_count = hidden_in.shape[0]
    positions = jnp.arange(frame_count, dtype=jnp.int32)
    split_here = row_split[0]
    row_ids = (positions >= split_here).astype(jnp.int32)
    tables = rotary_tables((positions - row_ids * split_here).astype(jnp.float32), w_query.shape[1])
    key_index = jnp.arange(2 * PROMPT, dtype=jnp.int32)
    key_rows = key_index // PROMPT
    key_live = key_index % PROMPT < jnp.where(key_rows == 0, prompt_len[0], prompt_len[1])
    self_ok = row_ids[:, None] == row_ids[None, :]
    cross_ok = (row_ids[:, None] == key_rows[None, :]) & key_live[None, :]

    normed, scaled_one, inverse_one = normalize(hidden_in, gain_attn, bias_attn)
    input_one = normed.astype(low)
    query_one = rotate(product_plain(input_one, w_query), tables).astype(low)
    key_one = rotate(product_plain(input_one, w_key), tables).astype(low)
    value_one = product_plain(input_one, w_value).astype(low)
    attended_one, logsum_one = attend_forward(query_one, heads_of(key_one), heads_of(value_one), self_ok)
    resid_one = hidden_in + swap_sum(product_plain(attended_one, w_out))

    normed, scaled_two, inverse_two = normalize(resid_one, gain_cross, bias_cross)
    input_two = normed.astype(low)
    cross_query = product_plain(input_two, c_query).astype(low)
    context_flat = prompt_states.reshape(2 * PROMPT, prompt_states.shape[2])
    cross_key = product_plain(context_flat, c_key).astype(low)
    cross_value = product_plain(context_flat, c_value).astype(low)
    attended_two, logsum_two = attend_forward(
        cross_query, heads_of(cross_key), heads_of(cross_value), cross_ok
    )
    resid_two = resid_one + swap_sum(product_plain(attended_two, c_out))

    normed, scaled_three, inverse_three = normalize(resid_two, gain_ff, bias_ff)
    input_three = normed.astype(low)
    gate_pre = product_plain(input_three, w_gate)
    up_pre = product_plain(input_three, w_up)
    sigmoid_gate = jax.nn.sigmoid(gate_pre)
    mixed_low = (gate_pre * sigmoid_gate * up_pre).astype(low)
    result = resid_two + swap_sum(product_plain(mixed_low, w_down))

    grad_ff_out = out_grad.astype(low)
    grad_w_down = generic_sum(grad_ff_out, mixed_low).T
    grad_mixed = product_with_rows(grad_ff_out, w_down)
    grad_gate = (
        grad_mixed * up_pre * sigmoid_gate * (1.0 + gate_pre * (1.0 - sigmoid_gate))
    ).astype(low)
    grad_up = (grad_mixed * gate_pre * sigmoid_gate).astype(low)
    grad_w_gate = generic_sum(input_three, grad_gate)
    grad_w_up = generic_sum(input_three, grad_up)
    normed_grad_three = swap_sum(
        product_with_rows(grad_gate, w_gate) + product_with_rows(grad_up, w_up)
    )
    back_three, grad_gain_ff, grad_bias_ff = normalize_back(
        normed_grad_three, scaled_three, inverse_three, gain_ff
    )
    grad_two = out_grad + back_three
    grad_cross_out = grad_two.astype(low)
    grad_c_out = generic_sum(grad_cross_out, attended_two).T
    grad_attended_two = product_with_rows(grad_cross_out, c_out).astype(low)
    cross_query_grad, cross_key_grad, cross_value_grad = attend_backward(
        cross_query,
        heads_of(cross_key),
        heads_of(cross_value),
        cross_ok,
        grad_attended_two,
        logsum_two,
    )
    cross_query_grad = cross_query_grad.astype(low)
    cross_key_grad = cross_key_grad.astype(low)
    cross_value_grad = cross_value_grad.astype(low)
    grad_c_query = generic_sum(input_two, cross_query_grad)
    grad_c_key = generic_sum(context_flat, cross_key_grad)
    grad_c_value = generic_sum(context_flat, cross_value_grad)
    normed_grad_two = swap_sum(product_with_rows(cross_query_grad, c_query))
    back_two, grad_gain_cross, grad_bias_cross = normalize_back(
        normed_grad_two, scaled_two, inverse_two, gain_cross
    )
    grad_one = grad_two + back_two
    grad_self_out = grad_one.astype(low)
    grad_w_out = generic_sum(grad_self_out, attended_one).T
    grad_attended_one = product_with_rows(grad_self_out, w_out).astype(low)
    query_grad, key_grad, value_grad = attend_backward(
        query_one, heads_of(key_one), heads_of(value_one), self_ok, grad_attended_one, logsum_one
    )
    query_grad = rotate_back(query_grad, tables).astype(low)
    key_grad = rotate_back(key_grad, tables).astype(low)
    value_grad = value_grad.astype(low)
    grad_w_query = generic_sum(input_one, query_grad)
    grad_w_key = generic_sum(input_one, key_grad)
    grad_w_value = generic_sum(input_one, value_grad)
    normed_grad_one = swap_sum(
        product_with_rows(query_grad, w_query)
        + product_with_rows(key_grad, w_key)
        + product_with_rows(value_grad, w_value)
    )
    back_one, grad_gain_attn, grad_bias_attn = normalize_back(
        normed_grad_one, scaled_one, inverse_one, gain_attn
    )
    grad_hidden = grad_one + back_one
    vectors = lax.psum(
        jnp.stack(
            [
                grad_gain_attn,
                grad_bias_attn,
                grad_gain_cross,
                grad_bias_cross,
                grad_gain_ff,
                grad_bias_ff,
            ]
        ),
        "dp",
    )
    vectors = own_share(vectors)
    return (
        result,
        grad_hidden,
        vectors[0],
        vectors[1],
        vectors[2],
        vectors[3],
        vectors[4],
        vectors[5],
        grad_w_query,
        grad_w_key,
        grad_w_value,
        grad_w_out,
        grad_c_query,
        grad_c_key,
        grad_c_value,
        grad_c_out,
        grad_w_gate,
        grad_w_up,
        grad_w_down,
    )


def solution(mesh):
    in_specs = (
        P("dp", None),
        P("dp", None),
        P("dp", None, None),
        P("dp"),
        P("dp"),
        P(),
        P(),
        P(),
        P(),
        P(),
        P(),
        P(None, "tensor"),
        P(None, "tensor"),
        P(None, "tensor"),
        P("tensor", None),
        P(None, "tensor"),
        P(None, "tensor"),
        P(None, "tensor"),
        P("tensor", None),
        P(None, "tensor"),
        P(None, "tensor"),
        P("tensor", None),
    )
    out_specs = (
        P("dp", None),
        P("dp", None),
        P(("dp", "tensor")),
        P(("dp", "tensor")),
        P(("dp", "tensor")),
        P(("dp", "tensor")),
        P(("dp", "tensor")),
        P(("dp", "tensor")),
        P("dp", "tensor"),
        P("dp", "tensor"),
        P("dp", "tensor"),
        P("tensor", "dp"),
        P("dp", "tensor"),
        P("dp", "tensor"),
        P("dp", "tensor"),
        P("tensor", "dp"),
        P("dp", "tensor"),
        P("dp", "tensor"),
        P("tensor", "dp"),
    )
    known = mesh.shape["dp"] == PLANE * LEVELS and mesh.shape["tensor"] == 2
    return jax.shard_map(
        on_plane if known else on_any, mesh=mesh, in_specs=in_specs, out_specs=out_specs, check_vma=False
    )
```

```python
import functools
import math

import jax
import jax.numpy as jnp
from jax import lax
from jax.experimental import pallas as pl
from jax.experimental.pallas import tpu as pltpu
from jax.sharding import PartitionSpec as P

PROMPT = 128
HEAD = 64
PLANE = 4
LEVELS = 4
VMEM_LIMIT = 60 * 2**20
COST = 3
FLOOR = 15 * 10**9

low = jnp.bfloat16
f32 = jnp.float32
sds = jax.ShapeDtypeStruct


norm_eps = 1e-05
score_scale = 0.125
masked_score = -1e30


def product_plain(left_side, right_side):
    return jnp.dot(left_side, right_side, preferred_element_type=jnp.float32)


def product_over_rows(left_side, right_side):
    return lax.dot_general(
        left_side, right_side, (((0,), (0,)), ((), ())), preferred_element_type=jnp.float32
    )


def product_with_rows(left_side, right_side):
    return lax.dot_general(
        left_side, right_side, (((1,), (1,)), ((), ())), preferred_element_type=jnp.float32
    )


def rotary_tables(positions, width):
    dim_index = jnp.arange(width) % HEAD
    freq_index = (dim_index % 16).astype(jnp.float32)
    inverse_freq = jnp.exp(freq_index * (-math.log(10000.0) / 16.0))
    angles = positions[:, None] * inverse_freq[None, :]
    cosine = jnp.cos(angles)
    sine_part = jnp.sin(angles)
    cos_table = jnp.where(dim_index < 32, cosine, 1.0)
    sin_lower = jnp.where(dim_index < 16, -sine_part, 0.0)
    sin_upper = jnp.where((dim_index >= 16) & (dim_index < 32), sine_part, 0.0)
    return (cos_table, sin_lower, sin_upper)


def rotate(values, tables):
    cos_table, sin_lower, sin_upper = tables
    return (
        values * cos_table
        + jnp.roll(values, -16, axis=1) * sin_lower
        + jnp.roll(values, 16, axis=1) * sin_upper
    )


def rotate_back(incoming, tables):
    cos_table, sin_lower, sin_upper = tables
    return (
        incoming * cos_table
        + jnp.roll(incoming * sin_lower, 16, axis=1)
        + jnp.roll(incoming * sin_upper, -16, axis=1)
    )


def normalize(values, norm_gain, norm_shift):
    average = jnp.mean(values, axis=-1, keepdims=True)
    centered = values - average
    variance = jnp.mean(centered * centered, axis=-1, keepdims=True)
    inverse = lax.rsqrt(variance + norm_eps)
    scaled = centered * inverse
    return (scaled * norm_gain + norm_shift, scaled, inverse)


def normalize_back(incoming, scaled, inverse, norm_gain):
    grad_gain = jnp.sum(incoming * scaled, axis=0)
    grad_shift = jnp.sum(incoming, axis=0)
    weighted = incoming * norm_gain
    grad_input = inverse * (
        weighted
        - jnp.mean(weighted, axis=-1, keepdims=True)
        - scaled * jnp.mean(weighted * scaled, axis=-1, keepdims=True)
    )
    return (grad_input, grad_gain, grad_shift)


def heads_of(values):
    return values.reshape(values.shape[0], values.shape[1] // HEAD, HEAD)


def attend_forward(query_block, key_heads, value_heads, allowed):
    query_heads = heads_of(query_block)
    scores = (
        jnp.einsum("qhd,khd->hqk", query_heads, key_heads, preferred_element_type=jnp.float32)
        * score_scale
    )
    scores = jnp.where(allowed[None], scores, masked_score)
    largest = jnp.max(scores, axis=-1, keepdims=True)
    exp_scores = jnp.exp(scores - largest)
    totals = jnp.sum(exp_scores, axis=-1, keepdims=True)
    soft_weights = (exp_scores / totals).astype(jnp.bfloat16)
    mixed_heads = jnp.einsum(
        "hqk,khd->qhd", soft_weights, value_heads, preferred_element_type=jnp.float32
    )
    mixed_flat = mixed_heads.reshape(query_block.shape[0], query_block.shape[1]).astype(
        jnp.bfloat16
    )
    return (mixed_flat, largest[..., 0] + jnp.log(totals[..., 0]))


def attend_backward(query_block, key_heads, value_heads, allowed, grad_block, logsum_block):
    query_heads = heads_of(query_block)
    grad_heads = heads_of(grad_block)
    scores = (
        jnp.einsum("qhd,khd->hqk", query_heads, key_heads, preferred_element_type=jnp.float32)
        * score_scale
    )
    scores = jnp.where(allowed[None], scores, masked_score)
    soft_weights = jnp.exp(scores - logsum_block[..., None])
    grad_weights = jnp.einsum(
        "qhd,khd->hqk", grad_heads, value_heads, preferred_element_type=jnp.float32
    )
    inner_sum = jnp.sum(soft_weights * grad_weights, axis=-1, keepdims=True)
    grad_scores = (soft_weights * (grad_weights - inner_sum)).astype(jnp.bfloat16)
    grad_query = (
        jnp.einsum("hqk,khd->qhd", grad_scores, key_heads, preferred_element_type=jnp.float32)
        * score_scale
    )
    grad_key = (
        jnp.einsum("hqk,qhd->khd", grad_scores, query_heads, preferred_element_type=jnp.float32)
        * score_scale
    )
    grad_value = jnp.einsum(
        "hqk,qhd->khd",
        soft_weights.astype(jnp.bfloat16),
        grad_heads,
        preferred_element_type=jnp.float32,
    )
    return (
        grad_query.reshape(query_block.shape),
        grad_key.reshape(grad_key.shape[0], -1),
        grad_value.reshape(grad_value.shape[0], -1),
    )


def swap_sum(partial):
    low = partial.astype(jnp.bfloat16)
    if lax.axis_size("tensor") == 2:
        other = lax.ppermute(low, "tensor", [(0, 1), (1, 0)])
        return low.astype(jnp.float32) + other.astype(jnp.float32)
    return lax.psum(low, "tensor").astype(jnp.float32)


def pairs(mask):
    return [(i, i ^ mask) for i in range(16)]


def own_share(vectors):
    share = vectors.shape[1] // (lax.axis_size("dp") * lax.axis_size("tensor"))
    index = lax.axis_index("dp") * lax.axis_size("tensor") + lax.axis_index("tensor")
    return lax.dynamic_slice_in_dim(vectors, index * share, share, 1)


def generic_sum(rows_side, column_side):
    return lax.psum_scatter(
        product_over_rows(rows_side, column_side).astype(jnp.bfloat16),
        "dp",
        scatter_dimension=0,
        tiled=True,
    ).astype(jnp.float32)


def add_low(*terms):
    total = terms[0].astype(jnp.float32)
    for term in terms[1:]:
        total = total + term.astype(jnp.float32)
    return total


def ff_parts(gate, up, grad_mixed):
    sig = 1.0 / (1.0 + jnp.exp(-gate))
    act = gate * sig
    return (
        (act * up).astype(low),
        (grad_mixed * up * sig * (1.0 + gate * (1.0 - sig))).astype(low),
        (grad_mixed * act).astype(low),
    )


def turn(values, cos, lower, upper):
    width = values.shape[1]
    return (values * cos + pltpu.roll(values, width - 16, 1) * lower + pltpu.roll(values, 16, 1) * upper)

def turn_back(values, cos, lower, upper):
    width = values.shape[1]
    return (values * cos + pltpu.roll(values * lower, 16, 1) + pltpu.roll(values * upper, width - 16, 1))

def normed_rows(values, gain, shift):
    average = jnp.mean(values, axis=-1, keepdims=True)
    centered = values - average
    variance = jnp.mean(centered * centered, axis=-1, keepdims=True)
    return centered * lax.rsqrt(variance + norm_eps) * gain + shift

def over_rows(rows, body, chunk=32):
    @pl.loop(0, rows // chunk, unroll=min(4, rows // chunk))
    def _(i):
        body(pl.ds(pl.multiple_of(i * chunk, chunk), chunk))

def attend(q, k, v, mask, lse_ref):
    q_turned = (q * jnp.bfloat16(0.125)).T
    v_turned = v.T
    outs = []
    for h in range(q.shape[1] // HEAD):
        c = slice(h * HEAD, (h + 1) * HEAD)
        s = product_plain(k[:, c], q_turned[c, :]) + mask
        m = jnp.max(s, axis=0, keepdims=True)
        e = jnp.exp(s - m)
        total = jnp.sum(e, axis=0, keepdims=True)
        o = product_plain(v_turned[c, :], e.astype(low)) * (1.0 / total)
        outs.append(o)
        lse_ref[h : h + 1, :] = m + jnp.log(total)
    return jnp.concatenate(outs, axis=0).T.astype(low)


def attend_back(q, k, v, g, mask, lse):
    scaled = q * jnp.bfloat16(0.125)
    q_turned = scaled.T
    g_turned = g.T
    k_turned = k.T
    dq, dk, dv = [], [], []
    for h in range(q.shape[1] // HEAD):
        c = slice(h * HEAD, (h + 1) * HEAD)
        p = jnp.exp(product_plain(k[:, c], q_turned[c, :]) + (mask - lse[h : h + 1, :]))
        dp = product_plain(v[:, c], g_turned[c, :])
        inner = jnp.sum(p * dp, axis=0, keepdims=True)
        ds = (p * (dp - inner)).astype(low)
        dq.append(product_plain(k_turned[c, :], ds))
        dk.append(product_plain(ds, scaled[:, c]))
        dv.append(product_plain(p.astype(low), g[:, c]))
    return (
        jnp.concatenate(dq, axis=0).T * 0.125,
        jnp.concatenate(dk, axis=1),
        jnp.concatenate(dv, axis=1),
    )


def self_mask(split, T):
    r=lax.broadcasted_iota(jnp.int32,(T,T),0)>=split
    c=lax.broadcasted_iota(jnp.int32,(T,T),1)>=split
    return jnp.where(r==c,0.0,masked_score).astype(f32)

def cross_mask(split, first, second, T, K):
    r = lax.broadcasted_iota(jnp.int32, (K, T), 1) >= split
    c = lax.broadcasted_iota(jnp.int32, (K, T), 0)
    least = jnp.where(r, K // 2, 0)
    most = jnp.where(r, K // 2 + second, first)
    return jnp.where((c >= least) & (c < most), 0.0, masked_score).astype(f32)


def norm_back_rows(x,e,gain,above,gain_acc,shift_acc):
    average=jnp.mean(x,axis=-1,keepdims=True)
    centered=x-average
    variance=jnp.mean(centered*centered,axis=-1,keepdims=True)
    inverse=lax.rsqrt(variance+norm_eps)
    n=centered*inverse
    en=e*n
    w=e*gain
    mean_w=jnp.mean(w,axis=-1,keepdims=True)
    mean_wn=jnp.mean(en*gain,axis=-1,keepdims=True)
    fold=lambda t: jnp.sum(t.reshape(t.shape[0]//8,8,t.shape[1]),axis=0)
    gain_acc[...]+=fold(en)
    shift_acc[...]+=fold(e)
    return above+inverse*(w-mean_w-n*mean_wn)

def norm_back_all(x,mine,other,above,gain,total,total_low,vec,gacc,sacc):
    gacc[...]=jnp.zeros_like(gacc);sacc[...]=jnp.zeros_like(sacc)
    def rows(r):
        e=mine[r,:].astype(f32)+other[r,:].astype(f32)
        t=norm_back_rows(x[r,:],e,gain[...],above[r,:],gacc,sacc)
        total[r,:]=t
        if total_low is not None: total_low[r,:]=t.astype(low)
    over_rows(x.shape[0],rows)
    vec[0:1,:]=jnp.sum(gacc[...],axis=0,keepdims=True)
    vec[1:2,:]=jnp.sum(sacc[...],axis=0,keepdims=True)


def ordered(kernel, token, args, in_specs, out_specs, out_shape, grid, flops, scratch=(), info=None, brief=False):
    if info is None:
        info = jnp.zeros((1,), jnp.int32)
    inputs, outputs = len(args), len(out_shape)

    def body(info_ref, *refs):
        token_ref = refs[inputs + 1 + outputs]

        @pl.when(functools.reduce(jnp.logical_and, [pl.program_id(i) == 0 for i in range(len(grid))]))
        def _():
            token_ref[...] = jnp.zeros_like(token_ref)

        kernel(
            info_ref,
            *refs[:inputs],
            *refs[inputs + 1 : inputs + 1 + outputs],
            *refs[inputs + 2 + outputs :],
        )

    moved = sum(math.prod(a.shape) * a.dtype.itemsize for a in (*args, *out_shape))
    *results, token = pl.pallas_call(
        body,
        grid_spec=pltpu.PrefetchScalarGridSpec(
            num_scalar_prefetch=1,
            grid=grid,
            in_specs=[*in_specs, pl.BlockSpec(memory_space=pl.ANY)],
            out_specs=[*out_specs, pl.BlockSpec((8, 128), lambda *_: (0, 0))],
            scratch_shapes=list(scratch),
        ),
        out_shape=[*out_shape, sds((8, 128), f32)],
        compiler_params=pltpu.CompilerParams(vmem_limit_bytes=VMEM_LIMIT),
        cost_estimate=pl.CostEstimate(flops=0 if brief else max(FLOOR, int(flops * COST)), bytes_accessed=0 if brief else int(moved * COST), transcendentals=0),
    )(info, *args, token)
    return (*results, token)


def hold(token, values):
    def nothing(values_ref, token_ref, out_ref, token_out):
        token_out[...] = jnp.zeros_like(token_out)

    return pl.pallas_call(
        nothing,
        in_specs=[pl.BlockSpec(memory_space=pl.ANY)] * 2,
        out_specs=[pl.BlockSpec(memory_space=pl.ANY), pl.BlockSpec(memory_space=pltpu.VMEM)],
        out_shape=[sds(values.shape, values.dtype), sds((8, 128), f32)],
        input_output_aliases={0: 0},
        compiler_params=pltpu.CompilerParams(vmem_limit_bytes=VMEM_LIMIT),
        cost_estimate=pl.CostEstimate(flops=FLOOR, bytes_accessed=0, transcendentals=0),
    )(values, token)


def specs(frames, width, tile):
    whole = pl.BlockSpec((frames, width), lambda j, *_: (0, 0))
    vector = pl.BlockSpec((1, width), lambda j, *_: (0, 0))
    column = pl.BlockSpec((width, tile), lambda j, *_: (0, j))
    row = pl.BlockSpec((tile, width), lambda j, *_: (j, 0))
    act = pl.BlockSpec((frames, tile), lambda j, *_: (0, j))
    table = pl.BlockSpec((frames, tile), lambda j, *_: (0, 0))
    logsum = pl.BlockSpec((8, frames), lambda j, *_: (j, 0))
    return whole, vector, column, row, act, table, logsum


def added(acc, term, result):
    step = pl.program_id(0)

    @pl.when(step == 0)
    def _():
        acc[...] = term

    @pl.when(step != 0)
    def _():
        acc[...] += term

    @pl.when(step == pl.num_programs(0) - 1)
    def _():
        result[...] = acc[...].astype(result.dtype)


def self_kernel(info, hid, gain, shift, wq, wk, wv, wo, cos, lower, upper, copies, q, k, v, att, logsum, part, acc, mask, normed):
    frames = hid.shape[0]

    @pl.when(pl.program_id(0) == 0)
    def _():
        def rows(r):
            normed[r, :] = normed_rows(hid[r, :], gain[...], shift[...]).astype(low)

        over_rows(frames, rows)
        mask[...] = self_mask(info[0], frames)
        mine = normed[pl.ds(pl.multiple_of(info[3] * (frames // 2), frames // 2), frames // 2), :]
        for chip in range(PLANE):
            copies[chip] = mine

    n = normed[...]
    tables = (cos[...], lower[...], upper[...])
    q[...] = turn(product_plain(n, wq[...]), *tables).astype(low)
    k[...] = turn(product_plain(n, wk[...]), *tables).astype(low)
    v[...] = product_plain(n, wv[...]).astype(low)
    attended = attend(q[...], k[...], v[...], mask[...], logsum)
    att[...] = attended
    added(acc, product_plain(attended, wo[...]), part)


def self_forward(token, info, hid, gain, shift, wq, wk, wv, wo, tables, tile=4 * HEAD):
    frames, width = hid.shape
    columns = wq.shape[1]
    whole, vector, column, row, act, table, logsum = specs(frames, width, tile)
    return ordered(
        self_kernel,
        token,
        (hid, gain, shift, wq, wk, wv, wo, *tables),
        [whole, vector, vector, column, column, column, row, table, table, table],
        [pl.BlockSpec((PLANE, frames // 2, width), lambda j, *_: (0, 0, 0)), act, act, act, act, logsum, whole],
        [sds((PLANE, frames // 2, width), low)]
        + [sds((frames, columns), low)] * 4
        + [sds((columns // tile * 8, frames), f32), sds((frames, width), low)],
        (columns // tile,),
        2 * frames * columns * (4 * width + 8 * frames),
        [
            pltpu.VMEM((frames, width), f32),
            pltpu.VMEM((frames, frames), f32),
            pltpu.VMEM((frames, width), low),
        ],
        info,
    )


def cross_kernel(info, hid, mine, other, gain, shift, cq, ck, cv, co, total, normed, q, att, logsum, part, acc, mask):
    frames = hid.shape[0]

    @pl.when(pl.program_id(0) == 0)
    def _():
        def rows(r):
            x = hid[r, :] + (mine[r, :].astype(f32) + other[r, :].astype(f32))
            total[r, :] = x
            normed[r, :] = normed_rows(x, gain[...], shift[...]).astype(low)

        over_rows(frames, rows)
        mask[...] = cross_mask(info[0], info[1], info[2], frames, ck.shape[0])

    q[...] = product_plain(normed[...], cq[...]).astype(low)
    attended = attend(q[...], ck[...], cv[...], mask[...], logsum)
    att[...] = attended
    added(acc, product_plain(attended, co[...]), part)


def cross_forward(token, info, hid, mine, other, gain, shift, cq, ck, cv, co, tile=4 * HEAD):
    frames, width = hid.shape
    columns, keys = cq.shape[1], ck.shape[0]
    whole, vector, column, row, act, table, logsum = specs(frames, width, tile)
    key = pl.BlockSpec((keys, tile), lambda j, *_: (0, j))
    return ordered(
        cross_kernel,
        token,
        (hid, mine, other, gain, shift, cq, ck, cv, co),
        [whole, whole, whole, vector, vector, column, key, key, row],
        [whole, whole, act, act, logsum, whole],
        [
            sds((frames, width), f32),
            sds((frames, width), low),
            sds((frames, columns), low),
            sds((frames, columns), low),
            sds((columns // tile * 8, frames), f32),
            sds((frames, width), low),
        ],
        (columns // tile,),
        2 * frames * columns * (2 * width + 8 * keys),
        [pltpu.VMEM((frames, width), f32), pltpu.VMEM((keys, frames), f32)],
        info,
        brief=True,
    )


def norm_kernel(info, hid, mine, other, gain, shift, total, normed, copies):
    def rows(r):
        x = hid[r, :] + (mine[r, :].astype(f32) + other[r, :].astype(f32))
        total[r, :] = x
        normed[r, :] = normed_rows(x, gain[...], shift[...]).astype(low)

    over_rows(hid.shape[0], rows)

    @pl.when(pl.program_id(0) * 2 // pl.num_programs(0) == info[0])
    def _():
        values = normed[...]
        for chip in range(PLANE):
            copies[chip] = values


def norm_forward(token, hid, mine, other, gain, shift, half, block=128):
    frames, width = hid.shape
    blocks = frames // (2 * block)
    rows = pl.BlockSpec((block, width), lambda j, *_: (j, 0))
    vector = pl.BlockSpec((1, width), lambda j, *_: (0, 0))
    return ordered(
        norm_kernel,
        token,
        (hid, mine, other, gain, shift),
        [rows, rows, rows, vector, vector],
        [
            rows,
            rows,
            pl.BlockSpec(
                (PLANE, block, width),
                lambda j, info: (0, jnp.clip(j - blocks * info[0], 0, blocks - 1), 0),
            ),
        ],
        [sds((frames, width), f32), sds((frames, width), low), sds((PLANE, frames // 2, width), low)],
        (frames // block,),
        10 * frames * width,
        info=half,
        brief=True,
    )


def cross_back_kernel(info, x, mine, other, above, gain, co, q, ck, cv, logsum, cq, total, total_low, vectors, dq, dk, dv, part, acc, mask, gain_acc, shift_acc):
    @pl.when(pl.program_id(0) == 0)
    def _():
        norm_back_all(x, mine, other, above, gain, total, total_low, vectors, gain_acc, shift_acc)
        mask[...] = cross_mask(info[0], info[1], info[2], x.shape[0], ck.shape[0])

    g = product_with_rows(total_low[...], co[...]).astype(low)
    a, b, c = attend_back(q[...], ck[...], cv[...], g, mask[...], logsum[...])
    a = a.astype(low)
    dq[...] = a
    dk[...] = b.astype(low)
    dv[...] = c.astype(low)
    added(acc, product_with_rows(a, cq[...]), part)


def cross_backward(token, info, x, mine, other, above, gain, co, q, ck, cv, logsums, cq, tile=4 * HEAD):
    frames, width = x.shape
    columns, keys = cq.shape[1], ck.shape[0]
    whole, vector, column, row, act, table, logsum = specs(frames, width, tile)
    key = pl.BlockSpec((keys, tile), lambda j, *_: (0, j))
    two = pl.BlockSpec((2, width), lambda j, *_: (0, 0))
    return ordered(
        cross_back_kernel,
        token,
        (x, mine, other, above, gain, co, q, ck, cv, logsums, cq),
        [whole, whole, whole, whole, vector, row, act, key, key, logsum, column],
        [whole, whole, two, act, key, key, whole],
        [
            sds((frames, width), f32),
            sds((frames, width), low),
            sds((2, width), f32),
            sds((frames, columns), low),
            sds((keys, columns), low),
            sds((keys, columns), low),
            sds((frames, width), low),
        ],
        (columns // tile,),
        2 * frames * columns * (2 * width + 20 * keys),
        [
            pltpu.VMEM((frames, width), f32),
            pltpu.VMEM((keys, frames), f32),
            pltpu.VMEM((8, width), f32),
            pltpu.VMEM((8, width), f32),
        ],
        info,
    )


def self_back_kernel(info, x, mine, other, above, gain, wo, q, k, v, logsum, wq, wk, wv, cos, lower, upper, total, total_low, vectors, grads, part, acc, mask, gain_acc, shift_acc):
    frames = x.shape[0]

    @pl.when(pl.program_id(0) == 0)
    def _():
        norm_back_all(x, mine, other, above, gain, total, total_low, vectors, gain_acc, shift_acc)
        mask[...] = self_mask(info[0], frames)

    g = product_with_rows(total_low[...], wo[...]).astype(low)
    a, b, c = attend_back(q[...], k[...], v[...], g, mask[...], logsum[...])
    tables = (cos[...], lower[...], upper[...])
    a = turn_back(a, *tables).astype(low)
    b = turn_back(b, *tables).astype(low)
    c = c.astype(low)
    for index, values in enumerate((a, b, c)):
        turned = values.T
        for quarter in range(PLANE):
            grads[quarter, index] = turned[quarter * HEAD : (quarter + 1) * HEAD]
    added(
        acc,
        product_with_rows(a, wq[...]) + product_with_rows(b, wk[...]) + product_with_rows(c, wv[...]),
        part,
    )


def self_backward(token, info, x, mine, other, above, gain, wo, q, k, v, logsums, wq, wk, wv, tables, tile=4 * HEAD):
    frames, width = x.shape
    columns = wq.shape[1]
    whole, vector, column, row, act, table, logsum = specs(frames, width, tile)
    two = pl.BlockSpec((2, width), lambda j, *_: (0, 0))
    heads = pl.BlockSpec((PLANE, 3, HEAD, frames), lambda j, *_: (0, 0, j, 0))
    return ordered(
        self_back_kernel,
        token,
        (x, mine, other, above, gain, wo, q, k, v, logsums, wq, wk, wv, *tables),
        [whole, whole, whole, whole, vector, row, act, act, act, logsum, column, column, column, table, table, table],
        [whole, whole, two, heads, whole],
        [
            sds((frames, width), f32),
            sds((frames, width), low),
            sds((2, width), f32),
            sds((PLANE, 3, columns // PLANE, frames), low),
            sds((frames, width), low),
        ],
        (columns // tile,),
        2 * frames * columns * (4 * width + 20 * frames),
        [
            pltpu.VMEM((frames, width), f32),
            pltpu.VMEM((frames, frames), f32),
            pltpu.VMEM((8, width), f32),
            pltpu.VMEM((8, width), f32),
        ],
        info,
    )


def last_kernel(_, x, mine, other, above, gain, total, vectors, gain_acc, shift_acc):
    step = pl.program_id(0)

    @pl.when(step == 0)
    def _():
        gain_acc[...] = jnp.zeros_like(gain_acc)
        shift_acc[...] = jnp.zeros_like(shift_acc)

    def rows(r):
        e = mine[r, :].astype(f32) + other[r, :].astype(f32)
        total[r, :] = norm_back_rows(x[r, :], e, gain[...], above[r, :], gain_acc, shift_acc)

    over_rows(x.shape[0], rows)

    @pl.when(step == pl.num_programs(0) - 1)
    def _():
        vectors[0:1, :] = jnp.sum(gain_acc[...], axis=0, keepdims=True)
        vectors[1:2, :] = jnp.sum(shift_acc[...], axis=0, keepdims=True)


def last_backward(token, x, mine, other, above, gain, block=128):
    frames, width = x.shape
    rows = pl.BlockSpec((block, width), lambda j, *_: (j, 0))
    vector = pl.BlockSpec((1, width), lambda j, *_: (0, 0))
    two = pl.BlockSpec((2, width), lambda j, *_: (0, 0))
    return ordered(
        last_kernel,
        token,
        (x, mine, other, above, gain),
        [rows, rows, rows, rows, vector],
        [rows, two],
        [sds((frames, width), f32), sds((2, width), f32)],
        (frames // block,),
        20 * frames * width,
        [pltpu.VMEM((8, width), f32), pltpu.VMEM((8, width), f32)],
    )


def pack_kernel(_, *refs):
    for values, copies in zip(refs[: len(refs) // 2], refs[len(refs) // 2 :]):
        copies[...] = values[...].astype(low)


def packed(token, values, half, pieces=1):
    frames, width = values.shape
    rows = frames // (2 * pieces)

    def source(piece):
        return pl.BlockSpec((rows, width), lambda j, info: (info[0] * pieces + piece, 0))

    return ordered(
        pack_kernel,
        token,
        (values,) * pieces,
        [source(piece) for piece in range(pieces)],
        [pl.BlockSpec((rows, width), lambda j, info: (j, 0))] * pieces,
        [sds((PLANE * rows, width), low)] * pieces,
        (PLANE,),
        0,
        info=half,
        brief=True,
    )


def ff_kernel(_, in_ref, out_ref, gate_ref, up_ref, down_ref, sum_ref, back_ref, sum_acc, back_acc, out_low):
    @pl.when(pl.program_id(0) == 0)
    def _():
        out_low[...] = out_ref[...].astype(low)

    normed = in_ref[...]
    mixed, grad_gate, grad_up = ff_parts(
        product_plain(normed, gate_ref[...]),
        product_plain(normed, up_ref[...]),
        product_with_rows(out_low[...], down_ref[...]),
    )
    added(sum_acc, product_plain(mixed, down_ref[...]), sum_ref)
    added(
        back_acc,
        product_with_rows(grad_gate, gate_ref[...]) + product_with_rows(grad_up, up_ref[...]),
        back_ref,
    )


def ff_both(token, normed, grad_out, w_gate, w_up, w_down, tile=768):
    frames, width = normed.shape
    units = w_gate.shape[1]
    whole, _, column, row, *_ = specs(frames, width, tile)
    return ordered(
        ff_kernel,
        token,
        (normed, grad_out, w_gate, w_up, w_down),
        [whole, whole, column, column, row],
        [whole, whole],
        [sds((frames, width), low)] * 2,
        (units // tile,),
        12 * frames * width * units,
        [pltpu.VMEM((frames, width), f32)] * 2 + [pltpu.VMEM((frames, width), low)],
    )


def share_kernel(info, in_mine, in_other, out_a, out_b, out_c, out_d, gate_ref, up_ref, down_ref, send_ref, keep_ref, acc):
    step = pl.program_id(0)
    normed = jnp.concatenate([in_mine[...], in_other[...]], axis=0)
    grad_out = jnp.concatenate([out_a[...], out_b[...], out_c[...], out_d[...]], axis=0)
    mixed, grad_gate, grad_up = ff_parts(
        product_plain(normed, gate_ref[...]),
        product_plain(normed, up_ref[...]),
        product_with_rows(grad_out, down_ref[...]),
    )
    fresh = (
        product_over_rows(grad_out, mixed),
        product_over_rows(normed, grad_gate),
        product_over_rows(normed, grad_up),
    )
    for index, term in enumerate(fresh):

        @pl.when(step == 0)
        def _():
            acc[index] = term

        @pl.when(step != 0)
        def _():
            acc[index] += term

    @pl.when(step == pl.num_programs(0) - 1)
    def _():
        rows = send_ref.shape[1] // 3
        for pair in range(2):
            for index in range(3):
                for ref, parity in ((send_ref, 1 - info[1]), (keep_ref, info[1])):
                    start = pl.multiple_of((2 * pair + parity) * rows, rows)
                    ref[pair, index * rows : (index + 1) * rows] = acc[
                        index, pl.ds(start, rows), :
                    ].astype(ref.dtype)


def ff_share(token, info, normed, grad_out, w_gate, w_up, w_down, tile):
    frames, width = normed[0].shape
    chunk = frames // PLANE
    rows = pl.BlockSpec((chunk, width), lambda j, info: (j, 0))
    column = pl.BlockSpec((width, tile), lambda j, info: (0, info[0]))
    half = (LEVELS // 2, 3 * width // LEVELS, tile)
    return ordered(
        share_kernel,
        token,
        (*normed, *grad_out, w_gate, w_up, w_down),
        [rows] * 2
        + [pl.BlockSpec((chunk // 2, width), lambda j, info: (j, 0))] * 4
        + [column, column, pl.BlockSpec((tile, width), lambda j, info: (info[0], 0))],
        [pl.BlockSpec(half, lambda j, info: (0, 0, 0))] * 2,
        [sds(half, low)] * 2,
        (PLANE,),
        24 * frames * width * tile,
        [pltpu.VMEM((3, width, tile), f32)],
        info,
    )


def weight_kernel(plan, sides_count, _, *refs):
    sides, columns = refs[:sides_count], refs[sides_count : sides_count + len(plan)]
    out = refs[sides_count + len(plan)]
    turned = refs[sides_count + len(plan) + 1 :]

    @pl.when(pl.program_id(0) == 0)
    def _():
        for side, ref in zip(sides, turned):
            ref[...] = side[...].T

    for (which, first), column in zip(plan, columns):
        product = product_plain(turned[which][...], column[...]).astype(low)
        rows = product.shape[0] // (PLANE * LEVELS)
        product = product.reshape(LEVELS, PLANE, rows, product.shape[1])
        for owner in range(PLANE):
            out[owner, :, first : first + rows, :] = product[:, owner]


def weight_products(token, sides, plan, columns, tile=256):
    width = columns[0].shape[1]
    rows = sum(sides[which].shape[1] for which, _ in plan) // (PLANE * LEVELS)
    return ordered(
        functools.partial(weight_kernel, plan, len(sides)),
        token,
        (*sides, *columns),
        [pl.BlockSpec(side.shape, lambda j, *_: (0, 0)) for side in sides]
        + [pl.BlockSpec((column.shape[0], tile), lambda j, *_: (0, j)) for column in columns],
        [pl.BlockSpec((PLANE, LEVELS, rows, tile), lambda j, *_: (0, 0, 0, j))],
        [sds((PLANE, LEVELS, rows, width), low)],
        (width // tile,),
        sum(2 * sides[w].shape[0] * sides[w].shape[1] * width for w, _ in plan),
        [pltpu.VMEM((side.shape[1], side.shape[0]), low) for side in sides],
    )


def plane_sum_kernel(info, got, send, keep):
    for ref, parity in ((send, 1 - info[0]), (keep, info[0])):
        total = got[0, 0, parity].astype(f32)
        for source in range(1, PLANE):
            total = total + got[source, 0, parity].astype(f32)
        ref[0] = total.astype(low)


def plane_sum(token, got, parity):
    rows, width = got.shape[2:]
    out = pl.BlockSpec((1, rows, width), lambda j, *_: (j, 0, 0))
    return ordered(
        plane_sum_kernel,
        token,
        (got.reshape(PLANE, 2, 2, rows, width),),
        [pl.BlockSpec((PLANE, 1, 2, rows, width), lambda j, *_: (0, j, 0, 0, 0))],
        [out, out],
        [sds((2, rows, width), low)] * 2,
        (2,),
        0,
        info=parity,
    )


def level_sum_kernel(_, keep_pass, got_pass, keep_own, got_own, passed, own):
    passed[...] = (keep_pass[0].astype(f32) + got_pass[0].astype(f32)).astype(low)
    own[...] = keep_own[0].astype(f32) + got_own[0].astype(f32)


def level_sum(token, keep, got, upper):
    rows, width = keep.shape[1:]
    block = rows // 2 if rows % 32 == 0 else rows
    off = pl.BlockSpec((1, block, width), lambda j, info: (1 - info[0], j, 0))
    own = pl.BlockSpec((1, block, width), lambda j, info: (info[0], j, 0))
    out = pl.BlockSpec((block, width), lambda j, info: (j, 0))
    return ordered(
        level_sum_kernel,
        token,
        (keep, got, keep, got),
        [off, off, own, own],
        [out, out],
        [sds((rows, width), low), sds((rows, width), f32)],
        (rows // block,),
        0,
        info=upper,
    )


def unit_pack_kernel(_, *refs):
    owns, lasts, out = refs[:-1:2], refs[1:-1:2], refs[-1]
    for index, (own, last) in enumerate(zip(owns, lasts)):

        @pl.when(pl.program_id(0) == index)
        def _():
            total = (own[...] + last[...].astype(f32)).astype(low)
            total = total.reshape(3, PLANE, out.shape[2], out.shape[3])
            for chip in range(PLANE):
                out[chip] = total[:, chip]


def unit_pack(token, sums):
    rows, tile = sums[0][0].shape
    r = rows // (3 * PLANE)
    whole = pl.BlockSpec((rows, tile), lambda j, *_: (0, 0))
    return ordered(
        unit_pack_kernel,
        token,
        tuple(array for pair in sums for array in pair),
        [whole] * (2 * len(sums)),
        [pl.BlockSpec((PLANE, 3, r, tile), lambda j, *_: (0, 0, 0, j))],
        [sds((PLANE, 3, r, tile * len(sums)), low)],
        (len(sums),),
        0,
    )


def unit_unpack_kernel(_, got, down, gate, up):
    down[...] = got[0, 0].astype(f32).T
    gate[...] = got[0, 1].astype(f32)
    up[...] = got[0, 2].astype(f32)


def unit_unpack(token, got):
    _, _, r, units = got.shape
    across = pl.BlockSpec((r, units), lambda j, *_: (0, j))
    return ordered(
        unit_unpack_kernel,
        token,
        (got,),
        [pl.BlockSpec((1, 3, r, units), lambda j, *_: (j, 0, 0, 0))],
        [pl.BlockSpec((units, r), lambda j, *_: (j, 0)), across, across],
        [sds((PLANE * units, r), f32)] + [sds((r, PLANE * units), f32)] * 2,
        (PLANE,),
        0,
    )


def head_pack_kernel(_, own, last, out):
    total = (own[...] + last[...].astype(f32)).T.astype(low)
    out[...] = total.reshape(out.shape)


def head_pack(token, own, last):
    features, columns = own.shape
    shape = (PLANE, columns // PLANE, features)
    return ordered(
        head_pack_kernel,
        token,
        (own, last),
        [pl.BlockSpec(own.shape, lambda j, *_: (0, 0))] * 2,
        [pl.BlockSpec(shape, lambda j, *_: (0, 0, 0))],
        [sds(shape, low)],
        (1,),
        0,
    )


def head_unpack_kernel(_, got, *outs):
    groups = got.shape[2] // (3 * HEAD)
    for index, out in enumerate(outs):
        pieces = []
        for group in range(groups):
            first = (index * groups + group) * HEAD
            pieces += [got[chip, :, first : first + HEAD] for chip in range(PLANE)]
        out[...] = jnp.concatenate(pieces, axis=1).astype(f32)


def head_unpack(token, got):
    chips, r, features = got.shape
    shape = (r, chips * features // 3)
    return ordered(
        head_unpack_kernel,
        token,
        (got,),
        [pl.BlockSpec(got.shape, lambda j, *_: (0, 0, 0))],
        [pl.BlockSpec(shape, lambda j, *_: (0, 0))] * 3,
        [sds(shape, f32)] * 3,
        (1,),
        0,
    )


def head_kernel(info, grads_mine, grads_other, in_mine, in_other, send, keep, acc):
    step = pl.program_id(0)
    rows = acc.shape[0]
    term = product_plain(grads_mine[0].reshape(rows, -1), in_mine[...]) + product_plain(
        grads_other[0].reshape(rows, -1), in_other[...]
    )

    @pl.when(step == 0)
    def _():
        acc[...] = term

    @pl.when(step != 0)
    def _():
        acc[...] += term

    @pl.when(step == pl.num_programs(0) - 1)
    def _():
        width = send.shape[2]
        for level in range(LEVELS):
            for ref, parity in ((send, 1 - info[1]), (keep, info[1])):

                @pl.when(parity == level % 2)
                def _():
                    ref[level // 2] = acc[:, level * width : (level + 1) * width].astype(low)


def head_products(token, info, grads, normed):
    _, three, features, frames = grads.shape
    width = normed[0].shape[1]
    chunk = normed[0].shape[0] // PLANE
    rows = pl.BlockSpec((chunk, width), lambda j, info: (j, 0))
    half = (LEVELS // 2, three * features, width // LEVELS)
    return ordered(
        head_kernel,
        token,
        (grads, grads, *normed),
        [
            pl.BlockSpec((1, three, features, chunk), lambda j, info: (j, 0, 0, info[0])),
            pl.BlockSpec((1, three, features, chunk), lambda j, info: (j, 0, 0, 1 - info[0])),
            rows,
            rows,
        ],
        [pl.BlockSpec(half, lambda j, info: (0, 0, 0))] * 2,
        [sds(half, low)] * 2,
        (PLANE,),
        2 * three * features * PLANE * frames * width,
        [pltpu.VMEM((three * features, width), f32)],
        info,
    )


def on_plane(
    hidden_in,
    out_grad,
    prompt_states,
    row_split,
    prompt_len,
    gain_attn,
    bias_attn,
    gain_cross,
    bias_cross,
    gain_ff,
    bias_ff,
    w_query,
    w_key,
    w_value,
    w_out,
    c_query,
    c_key,
    c_value,
    c_out,
    w_gate,
    w_up,
    w_down,
):
    frames, width = hidden_in.shape
    plane, level = lax.axis_index("dp") % PLANE, lax.axis_index("dp") // PLANE
    info = jnp.concatenate([row_split, prompt_len])
    positions = jnp.arange(frames, dtype=jnp.int32)
    row_ids = (positions >= row_split[0]).astype(jnp.int32)
    tables = rotary_tables((positions - row_ids * row_split[0]).astype(f32), 2 * HEAD)
    tables = lax.optimization_barrier(tables)
    tables = tuple(jnp.concatenate([table, table], axis=1) for table in tables)
    gain_attn, bias_attn, gain_cross, bias_cross, gain_ff, bias_ff = (
        vector[None] for vector in (gain_attn, bias_attn, gain_cross, bias_cross, gain_ff, bias_ff)
    )

    zero = jnp.zeros((1,), jnp.int32)
    half = zero + lax.axis_index("tensor")
    parity, upper = zero + level % 2, zero + level // 2
    chips = [[PLANE * z + p for p in range(PLANE)] for z in range(LEVELS)]

    def swapped(part):
        return lax.ppermute(part, "tensor", [(0, 1), (1, 0)])

    def in_plane(values):
        shape = values.shape
        return lax.all_to_all(
            values, "dp", 0, 0, axis_index_groups=chips, tiled=True
        ).reshape(shape)

    def gathered(copies):
        return in_plane(copies.reshape(-1, width))

    def level_swap(values, mask):
        return lax.ppermute(values, "dp", pairs(mask))

    token = jnp.zeros((8, 128), f32)
    copies, copies_two, token = packed(token, out_grad, half, 2)
    out_first = gathered(copies)
    context = prompt_states.reshape(2 * PROMPT, prompt_states.shape[2])
    cross_key = product_plain(context, c_key).astype(low)
    cross_value = product_plain(context, c_value).astype(low)
    copies_one, query, key, value, attended_one, logsum_one, part, token = self_forward(
        token,
        jnp.concatenate([info, half]),
        hidden_in,
        gain_attn,
        bias_attn,
        w_query,
        w_key,
        w_value,
        w_out,
        tables,
    )
    part_swapped = swapped(part)
    out_first, token = hold(token, out_first)
    out_second = gathered(copies_two)
    resid_one, input_two, cross_query, attended_two, logsum_two, part, token = cross_forward(
        token,
        info,
        hidden_in,
        part,
        part_swapped,
        gain_cross,
        bias_cross,
        c_query,
        cross_key,
        cross_value,
        c_out,
    )
    part_swapped = swapped(part)
    out_second, token = hold(token, out_second)
    resid_two, input_three, copies, token = norm_forward(
        token, resid_one, part, part_swapped, gain_ff, bias_ff, half
    )
    frames_in = gathered(copies)
    frames_out = (out_first, out_second, swapped(out_first), swapped(out_second))
    sum_part, back_part, token = ff_both(token, input_three, out_grad, w_gate, w_up, w_down)
    frames_in, token = hold(token, frames_in)
    frames_in = (frames_in, swapped(frames_in))
    back_swapped = swapped(back_part)
    copies_one, token = hold(token, copies_one)
    frames_one = gathered(copies_one)

    tile = 256
    tiles = w_gate.shape[1] // (PLANE * tile)

    def share(token, index):
        number = jnp.concatenate([zero + plane * tiles + index, parity])
        return ff_share(token, number, frames_in, frames_out, w_gate, w_up, w_down, tile)

    send_a, keep_a, token = share(token, 0)
    got_a = level_swap(send_a, PLANE)
    grad_two, grad_cross_out, vectors_ff, query_grad, key_grad, value_grad, part, token = cross_backward(
        token,
        info,
        resid_two,
        back_part,
        back_swapped,
        out_grad,
        gain_ff,
        c_out,
        cross_query,
        cross_key,
        cross_value,
        logsum_two,
        c_query,
    )
    part_swapped = swapped(part)
    r, c = width // 16, context.shape[1] // 16
    products, token = weight_products(
        token,
        [grad_cross_out, input_two, context],
        [(0, 0), (1, r), (2, 2 * r), (2, 2 * r + c)],
        [attended_two, query_grad, key_grad, value_grad],
    )
    frames_one, token = hold(token, frames_one)
    got_cross = in_plane(products)
    frames_one = (frames_one, swapped(frames_one))
    pass_a, own_a, token = level_sum(token, keep_a, got_a, upper)
    last_a = level_swap(pass_a, 2 * PLANE)
    send_b, keep_b, token = share(token, 1)
    got_b = level_swap(send_b, PLANE)
    grad_one, grad_self_out, vectors_cross, grads, part, token = self_backward(
        token,
        info,
        resid_one,
        part,
        part_swapped,
        grad_two,
        gain_cross,
        w_out,
        query,
        key,
        value,
        logsum_one,
        w_query,
        w_key,
        w_value,
        tables,
    )
    part_swapped = swapped(part)
    last_a, token = hold(token, last_a)
    pass_b, own_b, token = level_sum(token, keep_b, got_b, upper)
    last_b = level_swap(pass_b, 2 * PLANE)
    send_c, keep_c, token = share(token, 2)
    got_c = level_swap(send_c, PLANE)
    products, token = weight_products(token, [grad_self_out], [(0, 0)], [attended_one])
    got_cross, token = hold(token, got_cross)
    grads, token = hold(token, grads)
    got_heads = in_plane(grads)
    send_x, keep_x, token = plane_sum(token, got_cross, parity)
    got_x = level_swap(send_x, PLANE)
    grad_hidden, vectors_attn, token = last_backward(
        token, hidden_in, part, part_swapped, grad_one, gain_attn
    )
    vectors = jnp.concatenate([vectors_attn, vectors_cross, vectors_ff])
    last_b, token = hold(token, last_b)
    sum_part, token = hold(token, sum_part)
    sum_swapped = swapped(sum_part)
    pass_c, own_c, token = level_sum(token, keep_c, got_c, upper)
    last_c = level_swap(pass_c, 2 * PLANE)
    got_heads, token = hold(token, got_heads)
    products, token = hold(token, products)
    got_out = in_plane(products)
    send_h, keep_h, token = head_products(
        token, jnp.concatenate([half, parity]), got_heads, frames_one
    )
    got_h = level_swap(send_h, PLANE)
    sum_swapped, token = hold(token, sum_swapped)
    result = resid_two + add_low(sum_part, sum_swapped)
    pass_x, own_x, token = level_sum(token, keep_x, got_x, upper)
    last_x = level_swap(pass_x, 2 * PLANE)
    last_c, token = hold(token, last_c)
    units, token = unit_pack(token, [(own_a, last_a), (own_b, last_b), (own_c, last_c)])
    vectors_got = level_swap(vectors, 1)
    got_out, token = hold(token, got_out)
    send_o, keep_o, token = plane_sum(token, got_out, parity)
    got_o = level_swap(send_o, PLANE)
    units, token = hold(token, units)
    units = in_plane(units)
    pass_h, own_h, token = level_sum(token, keep_h, got_h, upper)
    last_h = level_swap(pass_h, 2 * PLANE)
    vectors_got, token = hold(token, vectors_got)
    vectors = vectors + vectors_got
    vectors_got = level_swap(vectors, 2)
    pass_o, own_o, token = level_sum(token, keep_o, got_o, upper)
    last_o = level_swap(pass_o, 2 * PLANE)
    last_x, token = hold(token, last_x)
    cross = add_low(own_x, last_x)
    units, token = hold(token, units)
    grad_w_down, grad_w_gate, grad_w_up, token = unit_unpack(token, units)
    vectors_got, token = hold(token, vectors_got)
    vectors = vectors + vectors_got
    vectors_got = level_swap(vectors, PLANE)
    heads, token = head_pack(token, own_h, last_h)
    heads = in_plane(heads)
    vectors_got, token = hold(token, vectors_got)
    vectors = vectors + vectors_got
    vectors = own_share(vectors + level_swap(vectors, 2 * PLANE))
    heads, token = hold(token, heads)
    grad_w_query, grad_w_key, grad_w_value, token = head_unpack(token, heads)
    return (
        result,
        grad_hidden,
        *(vectors[index] for index in range(6)),
        grad_w_query,
        grad_w_key,
        grad_w_value,
        add_low(own_o, last_o).T,
        cross[r : 2 * r],
        cross[2 * r : 2 * r + c],
        cross[2 * r + c :],
        cross[:r].T,
        grad_w_gate,
        grad_w_up,
        grad_w_down,
    )


def on_any(
    hidden_in,
    out_grad,
    prompt_states,
    row_split,
    prompt_len,
    gain_attn,
    bias_attn,
    gain_cross,
    bias_cross,
    gain_ff,
    bias_ff,
    w_query,
    w_key,
    w_value,
    w_out,
    c_query,
    c_key,
    c_value,
    c_out,
    w_gate,
    w_up,
    w_down,
):
    frame_count = hidden_in.shape[0]
    positions = jnp.arange(frame_count, dtype=jnp.int32)
    split_here = row_split[0]
    row_ids = (positions >= split_here).astype(jnp.int32)
    tables = rotary_tables((positions - row_ids * split_here).astype(jnp.float32), w_query.shape[1])
    key_index = jnp.arange(2 * PROMPT, dtype=jnp.int32)
    key_rows = key_index // PROMPT
    key_live = key_index % PROMPT < jnp.where(key_rows == 0, prompt_len[0], prompt_len[1])
    self_ok = row_ids[:, None] == row_ids[None, :]
    cross_ok = (row_ids[:, None] == key_rows[None, :]) & key_live[None, :]

    normed, scaled_one, inverse_one = normalize(hidden_in, gain_attn, bias_attn)
    input_one = normed.astype(low)
    query_one = rotate(product_plain(input_one, w_query), tables).astype(low)
    key_one = rotate(product_plain(input_one, w_key), tables).astype(low)
    value_one = product_plain(input_one, w_value).astype(low)
    attended_one, logsum_one = attend_forward(query_one, heads_of(key_one), heads_of(value_one), self_ok)
    resid_one = hidden_in + swap_sum(product_plain(attended_one, w_out))

    normed, scaled_two, inverse_two = normalize(resid_one, gain_cross, bias_cross)
    input_two = normed.astype(low)
    cross_query = product_plain(input_two, c_query).astype(low)
    context_flat = prompt_states.reshape(2 * PROMPT, prompt_states.shape[2])
    cross_key = product_plain(context_flat, c_key).astype(low)
    cross_value = product_plain(context_flat, c_value).astype(low)
    attended_two, logsum_two = attend_forward(
        cross_query, heads_of(cross_key), heads_of(cross_value), cross_ok
    )
    resid_two = resid_one + swap_sum(product_plain(attended_two, c_out))

    normed, scaled_three, inverse_three = normalize(resid_two, gain_ff, bias_ff)
    input_three = normed.astype(low)
    gate_pre = product_plain(input_three, w_gate)
    up_pre = product_plain(input_three, w_up)
    sigmoid_gate = jax.nn.sigmoid(gate_pre)
    mixed_low = (gate_pre * sigmoid_gate * up_pre).astype(low)
    result = resid_two + swap_sum(product_plain(mixed_low, w_down))

    grad_ff_out = out_grad.astype(low)
    grad_w_down = generic_sum(grad_ff_out, mixed_low).T
    grad_mixed = product_with_rows(grad_ff_out, w_down)
    grad_gate = (
        grad_mixed * up_pre * sigmoid_gate * (1.0 + gate_pre * (1.0 - sigmoid_gate))
    ).astype(low)
    grad_up = (grad_mixed * gate_pre * sigmoid_gate).astype(low)
    grad_w_gate = generic_sum(input_three, grad_gate)
    grad_w_up = generic_sum(input_three, grad_up)
    normed_grad_three = swap_sum(
        product_with_rows(grad_gate, w_gate) + product_with_rows(grad_up, w_up)
    )
    back_three, grad_gain_ff, grad_bias_ff = normalize_back(
        normed_grad_three, scaled_three, inverse_three, gain_ff
    )
    grad_two = out_grad + back_three
    grad_cross_out = grad_two.astype(low)
    grad_c_out = generic_sum(grad_cross_out, attended_two).T
    grad_attended_two = product_with_rows(grad_cross_out, c_out).astype(low)
    cross_query_grad, cross_key_grad, cross_value_grad = attend_backward(
        cross_query,
        heads_of(cross_key),
        heads_of(cross_value),
        cross_ok,
        grad_attended_two,
        logsum_two,
    )
    cross_query_grad = cross_query_grad.astype(low)
    cross_key_grad = cross_key_grad.astype(low)
    cross_value_grad = cross_value_grad.astype(low)
    grad_c_query = generic_sum(input_two, cross_query_grad)
    grad_c_key = generic_sum(context_flat, cross_key_grad)
    grad_c_value = generic_sum(context_flat, cross_value_grad)
    normed_grad_two = swap_sum(product_with_rows(cross_query_grad, c_query))
    back_two, grad_gain_cross, grad_bias_cross = normalize_back(
        normed_grad_two, scaled_two, inverse_two, gain_cross
    )
    grad_one = grad_two + back_two
    grad_self_out = grad_one.astype(low)
    grad_w_out = generic_sum(grad_self_out, attended_one).T
    grad_attended_one = product_with_rows(grad_self_out, w_out).astype(low)
    query_grad, key_grad, value_grad = attend_backward(
        query_one, heads_of(key_one), heads_of(value_one), self_ok, grad_attended_one, logsum_one
    )
    query_grad = rotate_back(query_grad, tables).astype(low)
    key_grad = rotate_back(key_grad, tables).astype(low)
    value_grad = value_grad.astype(low)
    grad_w_query = generic_sum(input_one, query_grad)
    grad_w_key = generic_sum(input_one, key_grad)
    grad_w_value = generic_sum(input_one, value_grad)
    normed_grad_one = swap_sum(
        product_with_rows(query_grad, w_query)
        + product_with_rows(key_grad, w_key)
        + product_with_rows(value_grad, w_value)
    )
    back_one, grad_gain_attn, grad_bias_attn = normalize_back(
        normed_grad_one, scaled_one, inverse_one, gain_attn
    )
    grad_hidden = grad_one + back_one
    vectors = lax.psum(
        jnp.stack(
            [
                grad_gain_attn,
                grad_bias_attn,
                grad_gain_cross,
                grad_bias_cross,
                grad_gain_ff,
                grad_bias_ff,
            ]
        ),
        "dp",
    )
    vectors = own_share(vectors)
    return (
        result,
        grad_hidden,
        vectors[0],
        vectors[1],
        vectors[2],
        vectors[3],
        vectors[4],
        vectors[5],
        grad_w_query,
        grad_w_key,
        grad_w_value,
        grad_w_out,
        grad_c_query,
        grad_c_key,
        grad_c_value,
        grad_c_out,
        grad_w_gate,
        grad_w_up,
        grad_w_down,
    )


def solution(mesh):
    in_specs = (
        P("dp", None),
        P("dp", None),
        P("dp", None, None),
        P("dp"),
        P("dp"),
        P(),
        P(),
        P(),
        P(),
        P(),
        P(),
        P(None, "tensor"),
        P(None, "tensor"),
        P(None, "tensor"),
        P("tensor", None),
        P(None, "tensor"),
        P(None, "tensor"),
        P(None, "tensor"),
        P("tensor", None),
        P(None, "tensor"),
        P(None, "tensor"),
        P("tensor", None),
    )
    out_specs = (
        P("dp", None),
        P("dp", None),
        P(("dp", "tensor")),
        P(("dp", "tensor")),
        P(("dp", "tensor")),
        P(("dp", "tensor")),
        P(("dp", "tensor")),
        P(("dp", "tensor")),
        P("dp", "tensor"),
        P("dp", "tensor"),
        P("dp", "tensor"),
        P("tensor", "dp"),
        P("dp", "tensor"),
        P("dp", "tensor"),
        P("dp", "tensor"),
        P("tensor", "dp"),
        P("dp", "tensor"),
        P("dp", "tensor"),
        P("tensor", "dp"),
    )
    known = mesh.shape["dp"] == PLANE * LEVELS and mesh.shape["tensor"] == 2
    return jax.shard_map(
        on_plane if known else on_any, mesh=mesh, in_specs=in_specs, out_specs=out_specs, check_vma=False
    )
```

```python
import functools
import math

import jax
import jax.numpy as jnp
from jax import lax
from jax.experimental import pallas as pl
from jax.experimental.pallas import tpu as pltpu
from jax.sharding import PartitionSpec as P

PROMPT = 128
HEAD = 64
PLANE = 4
LEVELS = 4
VMEM_LIMIT = 62 * 2**20
COST = 3
FLOOR = 15 * 10**9

low = jnp.bfloat16
f32 = jnp.float32
sds = jax.ShapeDtypeStruct


norm_eps = 1e-05
score_scale = 0.125
masked_score = -1e30


def product_plain(left_side, right_side):
    return jnp.dot(left_side, right_side, preferred_element_type=jnp.float32)


def product_over_rows(left_side, right_side):
    return lax.dot_general(
        left_side, right_side, (((0,), (0,)), ((), ())), preferred_element_type=jnp.float32
    )


def product_with_rows(left_side, right_side):
    return lax.dot_general(
        left_side, right_side, (((1,), (1,)), ((), ())), preferred_element_type=jnp.float32
    )


def rotary_tables(positions, width):
    dim_index = jnp.arange(width) % HEAD
    freq_index = (dim_index % 16).astype(jnp.float32)
    inverse_freq = jnp.exp(freq_index * (-math.log(10000.0) / 16.0))
    angles = positions[:, None] * inverse_freq[None, :]
    cosine = jnp.cos(angles)
    sine_part = jnp.sin(angles)
    cos_table = jnp.where(dim_index < 32, cosine, 1.0)
    sin_lower = jnp.where(dim_index < 16, -sine_part, 0.0)
    sin_upper = jnp.where((dim_index >= 16) & (dim_index < 32), sine_part, 0.0)
    return (cos_table, sin_lower, sin_upper)


def rotate(values, tables):
    cos_table, sin_lower, sin_upper = tables
    return (
        values * cos_table
        + jnp.roll(values, -16, axis=1) * sin_lower
        + jnp.roll(values, 16, axis=1) * sin_upper
    )


def rotate_back(incoming, tables):
    cos_table, sin_lower, sin_upper = tables
    return (
        incoming * cos_table
        + jnp.roll(incoming * sin_lower, 16, axis=1)
        + jnp.roll(incoming * sin_upper, -16, axis=1)
    )


def normalize(values, norm_gain, norm_shift):
    average = jnp.mean(values, axis=-1, keepdims=True)
    centered = values - average
    variance = jnp.mean(centered * centered, axis=-1, keepdims=True)
    inverse = lax.rsqrt(variance + norm_eps)
    scaled = centered * inverse
    return (scaled * norm_gain + norm_shift, scaled, inverse)


def normalize_back(incoming, scaled, inverse, norm_gain):
    grad_gain = jnp.sum(incoming * scaled, axis=0)
    grad_shift = jnp.sum(incoming, axis=0)
    weighted = incoming * norm_gain
    grad_input = inverse * (
        weighted
        - jnp.mean(weighted, axis=-1, keepdims=True)
        - scaled * jnp.mean(weighted * scaled, axis=-1, keepdims=True)
    )
    return (grad_input, grad_gain, grad_shift)


def heads_of(values):
    return values.reshape(values.shape[0], values.shape[1] // HEAD, HEAD)


def attend_forward(query_block, key_heads, value_heads, allowed):
    query_heads = heads_of(query_block)
    scores = (
        jnp.einsum("qhd,khd->hqk", query_heads, key_heads, preferred_element_type=jnp.float32)
        * score_scale
    )
    scores = jnp.where(allowed[None], scores, masked_score)
    largest = jnp.max(scores, axis=-1, keepdims=True)
    exp_scores = jnp.exp(scores - largest)
    totals = jnp.sum(exp_scores, axis=-1, keepdims=True)
    soft_weights = (exp_scores / totals).astype(jnp.bfloat16)
    mixed_heads = jnp.einsum(
        "hqk,khd->qhd", soft_weights, value_heads, preferred_element_type=jnp.float32
    )
    mixed_flat = mixed_heads.reshape(query_block.shape[0], query_block.shape[1]).astype(
        jnp.bfloat16
    )
    return (mixed_flat, largest[..., 0] + jnp.log(totals[..., 0]))


def attend_backward(query_block, key_heads, value_heads, allowed, grad_block, logsum_block):
    query_heads = heads_of(query_block)
    grad_heads = heads_of(grad_block)
    scores = (
        jnp.einsum("qhd,khd->hqk", query_heads, key_heads, preferred_element_type=jnp.float32)
        * score_scale
    )
    scores = jnp.where(allowed[None], scores, masked_score)
    soft_weights = jnp.exp(scores - logsum_block[..., None])
    grad_weights = jnp.einsum(
        "qhd,khd->hqk", grad_heads, value_heads, preferred_element_type=jnp.float32
    )
    inner_sum = jnp.sum(soft_weights * grad_weights, axis=-1, keepdims=True)
    grad_scores = (soft_weights * (grad_weights - inner_sum)).astype(jnp.bfloat16)
    grad_query = (
        jnp.einsum("hqk,khd->qhd", grad_scores, key_heads, preferred_element_type=jnp.float32)
        * score_scale
    )
    grad_key = (
        jnp.einsum("hqk,qhd->khd", grad_scores, query_heads, preferred_element_type=jnp.float32)
        * score_scale
    )
    grad_value = jnp.einsum(
        "hqk,qhd->khd",
        soft_weights.astype(jnp.bfloat16),
        grad_heads,
        preferred_element_type=jnp.float32,
    )
    return (
        grad_query.reshape(query_block.shape),
        grad_key.reshape(grad_key.shape[0], -1),
        grad_value.reshape(grad_value.shape[0], -1),
    )


def swap_sum(partial):
    low = partial.astype(jnp.bfloat16)
    if lax.axis_size("tensor") == 2:
        other = lax.ppermute(low, "tensor", [(0, 1), (1, 0)])
        return low.astype(jnp.float32) + other.astype(jnp.float32)
    return lax.psum(low, "tensor").astype(jnp.float32)


def pairs(mask):
    return [(i, i ^ mask) for i in range(16)]


def own_share(vectors):
    share = vectors.shape[1] // (lax.axis_size("dp") * lax.axis_size("tensor"))
    index = lax.axis_index("dp") * lax.axis_size("tensor") + lax.axis_index("tensor")
    return lax.dynamic_slice_in_dim(vectors, index * share, share, 1)


def generic_sum(rows_side, column_side):
    return lax.psum_scatter(
        product_over_rows(rows_side, column_side).astype(jnp.bfloat16),
        "dp",
        scatter_dimension=0,
        tiled=True,
    ).astype(jnp.float32)


def add_low(*terms):
    total = terms[0].astype(jnp.float32)
    for term in terms[1:]:
        total = total + term.astype(jnp.float32)
    return total


def ff_parts(gate, up, grad_mixed):
    sig = 0.5 * jnp.tanh(0.5 * gate) + 0.5
    act = gate * sig
    return (
        (act * up).astype(low),
        (grad_mixed * up * sig * (1.0 + gate * (1.0 - sig))).astype(low),
        (grad_mixed * act).astype(low),
    )


def turn(values, cos, lower, upper):
    width = values.shape[1]
    return (values * cos + pltpu.roll(values, width - 16, 1) * lower + pltpu.roll(values, 16, 1) * upper)

def turn_back(values, cos, lower, upper):
    width = values.shape[1]
    return (values * cos + pltpu.roll(values * lower, 16, 1) + pltpu.roll(values * upper, width - 16, 1))

def normed_rows(values, gain, shift):
    average = jnp.mean(values, axis=-1, keepdims=True)
    centered = values - average
    variance = jnp.mean(centered * centered, axis=-1, keepdims=True)
    return centered * lax.rsqrt(variance + norm_eps) * gain + shift

def over_rows(rows, body, chunk=32):
    @pl.loop(0, rows // chunk, unroll=min(4, rows // chunk))
    def _(i):
        body(pl.ds(pl.multiple_of(i * chunk, chunk), chunk))

def attend(q, k, v, mask, lse_ref):
    q_turned = (q * jnp.bfloat16(0.125)).T
    v_turned = v.T
    outs = []
    for h in range(q.shape[1] // HEAD):
        c = slice(h * HEAD, (h + 1) * HEAD)
        s = product_plain(k[:, c], q_turned[c, :]) + mask
        m = jnp.max(s, axis=0, keepdims=True)
        e = jnp.exp(s - m)
        total = jnp.sum(e, axis=0, keepdims=True)
        o = product_plain(v_turned[c, :], e.astype(low)) * (1.0 / total)
        outs.append(o)
        lse_ref[h : h + 1, :] = m + jnp.log(total)
    return jnp.concatenate(outs, axis=0).T.astype(low)


def attend_back(q, k, v, g, att, mask, lse):
    scaled = q * jnp.bfloat16(0.125)
    q_turned = scaled.T
    g_turned = g.T
    k_turned = k.T
    weighted = g_turned.astype(f32) * att.T.astype(f32)
    dq, dk, dv = [], [], []
    for h in range(q.shape[1] // HEAD):
        c = slice(h * HEAD, (h + 1) * HEAD)
        p = jnp.exp(product_plain(k[:, c], q_turned[c, :]) + (mask - lse[h : h + 1, :]))
        dp = product_plain(v[:, c], g_turned[c, :])
        inner = jnp.sum(weighted[c, :], axis=0, keepdims=True)
        ds = (p * (dp - inner)).astype(low)
        dq.append(product_plain(k_turned[c, :], ds))
        dk.append(product_plain(ds, scaled[:, c]))
        dv.append(product_plain(p.astype(low), g[:, c]))
    return (
        jnp.concatenate(dq, axis=0).T * 0.125,
        jnp.concatenate(dk, axis=1),
        jnp.concatenate(dv, axis=1),
    )


def self_mask(split, T):
    r=lax.broadcasted_iota(jnp.int32,(T,T),0)>=split
    c=lax.broadcasted_iota(jnp.int32,(T,T),1)>=split
    return jnp.where(r==c,0.0,masked_score).astype(f32)

def key_half(info, index, frames, keys):
    second = info[0] < frames
    start = jnp.where(second, keys // 2, 0) if index == 1 else 0
    live = jnp.where(second, info[2], info[1]) if index == 1 else info[1]
    return start, live


def half_mask(live, keys, frames):
    return jnp.where(
        lax.broadcasted_iota(jnp.int32, (keys, frames), 0) < live, 0.0, masked_score
    ).astype(f32)


def cross_attend(info, q, k_ref, v_ref, lse_ref):
    frames, keys = q.shape[0], k_ref.shape[0]
    q_turned = (q * jnp.bfloat16(0.125)).T
    halves = []
    for index in range(2):
        columns = slice(index * (frames // 2), (index + 1) * (frames // 2))
        start, live = key_half(info, index, frames, keys)
        here = pl.ds(start if index == 0 else pl.multiple_of(start, keys // 2), keys // 2)
        k, v_turned = k_ref[here, :], v_ref[here, :].T
        mask = half_mask(live, keys // 2, frames // 2)
        outs = []
        for h in range(q.shape[1] // HEAD):
            c = slice(h * HEAD, (h + 1) * HEAD)
            s = product_plain(k[:, c], q_turned[c, columns]) + mask
            m = jnp.max(s, axis=0, keepdims=True)
            e = jnp.exp(s - m)
            total = jnp.sum(e, axis=0, keepdims=True)
            outs.append(product_plain(v_turned[c, :], e.astype(low)) * (1.0 / total))
            lse_ref[h : h + 1, columns] = m + jnp.log(total)
        halves.append(jnp.concatenate(outs, axis=0))
    return jnp.concatenate(halves, axis=1).T.astype(low)


def cross_attend_back(info, q, k_ref, v_ref, g, att, lse):
    frames, keys = q.shape[0], k_ref.shape[0]
    scaled = q * jnp.bfloat16(0.125)
    q_turned = scaled.T
    g_turned = g.T
    weighted = g_turned.astype(f32) * att.T.astype(f32)
    dq_halves, dk_halves, dv_halves = [], [], []
    for index in range(2):
        columns = slice(index * (frames // 2), (index + 1) * (frames // 2))
        start, live = key_half(info, index, frames, keys)
        here = pl.ds(start if index == 0 else pl.multiple_of(start, keys // 2), keys // 2)
        k, v = k_ref[here, :], v_ref[here, :]
        k_turned = k.T
        mask = half_mask(live, keys // 2, frames // 2)
        dq, dk, dv = [], [], []
        for h in range(q.shape[1] // HEAD):
            c = slice(h * HEAD, (h + 1) * HEAD)
            s = product_plain(k[:, c], q_turned[c, columns])
            p = jnp.exp(s + (mask - lse[h : h + 1, columns]))
            dp = product_plain(v[:, c], g_turned[c, columns])
            inner = jnp.sum(weighted[c, columns], axis=0, keepdims=True)
            ds = (p * (dp - inner)).astype(low)
            dq.append(product_plain(k_turned[c, :], ds))
            dk.append(product_plain(ds, scaled[columns, c]))
            dv.append(product_plain(p.astype(low), g[columns, c]))
        dq_halves.append(jnp.concatenate(dq, axis=0))
        dk_halves.append(jnp.concatenate(dk, axis=1))
        dv_halves.append(jnp.concatenate(dv, axis=1))
    second = (info[0] < frames).astype(f32)

    def by_row(halves):
        return jnp.concatenate(
            [halves[0] + halves[1] * (1.0 - second), halves[1] * second], axis=0
        )

    return jnp.concatenate(dq_halves, axis=1).T * 0.125, by_row(dk_halves), by_row(dv_halves)


def norm_back_rows(x,e,gain,above,gain_acc,shift_acc):
    average=jnp.mean(x,axis=-1,keepdims=True)
    centered=x-average
    variance=jnp.mean(centered*centered,axis=-1,keepdims=True)
    inverse=lax.rsqrt(variance+norm_eps)
    n=centered*inverse
    en=e*n
    w=e*gain
    mean_w=jnp.mean(w,axis=-1,keepdims=True)
    mean_wn=jnp.mean(en*gain,axis=-1,keepdims=True)
    fold=lambda t: jnp.sum(t.reshape(t.shape[0]//8,8,t.shape[1]),axis=0)
    gain_acc[...]+=fold(en)
    shift_acc[...]+=fold(e)
    return above+inverse*(w-mean_w-n*mean_wn)

def norm_back_all(x,mine,other,above,gain,total,total_low,vec,gacc,sacc):
    gacc[...]=jnp.zeros_like(gacc);sacc[...]=jnp.zeros_like(sacc)
    def rows(r):
        e=mine[r,:].astype(f32)+other[r,:].astype(f32)
        t=norm_back_rows(x[r,:],e,gain[...],above[r,:],gacc,sacc)
        total[r,:]=t
        if total_low is not None: total_low[r,:]=t.astype(low)
    over_rows(x.shape[0],rows)
    vec[0:1,:]=jnp.sum(gacc[...],axis=0,keepdims=True)
    vec[1:2,:]=jnp.sum(sacc[...],axis=0,keepdims=True)


def ordered(kernel, token, args, in_specs, out_specs, out_shape, grid, flops, scratch=(), info=None, brief=False):
    if info is None:
        info = jnp.zeros((1,), jnp.int32)
    inputs, outputs = len(args), len(out_shape)

    def body(info_ref, *refs):
        token_ref = refs[inputs + 1 + outputs]

        @pl.when(functools.reduce(jnp.logical_and, [pl.program_id(i) == 0 for i in range(len(grid))]))
        def _():
            token_ref[...] = jnp.zeros_like(token_ref)

        kernel(
            info_ref,
            *refs[:inputs],
            *refs[inputs + 1 : inputs + 1 + outputs],
            *refs[inputs + 2 + outputs :],
        )

    moved = sum(math.prod(a.shape) * a.dtype.itemsize for a in (*args, *out_shape))
    *results, token = pl.pallas_call(
        body,
        grid_spec=pltpu.PrefetchScalarGridSpec(
            num_scalar_prefetch=1,
            grid=grid,
            in_specs=[*in_specs, pl.BlockSpec(memory_space=pl.ANY)],
            out_specs=[*out_specs, pl.BlockSpec((8, 128), lambda *_: (0, 0))],
            scratch_shapes=list(scratch),
        ),
        out_shape=[*out_shape, sds((8, 128), f32)],
        compiler_params=pltpu.CompilerParams(vmem_limit_bytes=VMEM_LIMIT),
        cost_estimate=pl.CostEstimate(flops=0 if brief else max(FLOOR, int(flops * COST)), bytes_accessed=0 if brief else int(moved * COST), transcendentals=0),
    )(info, *args, token)
    return (*results, token)


def hold(token, values, brief=False):
    def nothing(values_ref, token_ref, out_ref, token_out):
        token_out[...] = jnp.zeros_like(token_out)

    return pl.pallas_call(
        nothing,
        in_specs=[pl.BlockSpec(memory_space=pl.ANY)] * 2,
        out_specs=[pl.BlockSpec(memory_space=pl.ANY), pl.BlockSpec(memory_space=pltpu.VMEM)],
        out_shape=[sds(values.shape, values.dtype), sds((8, 128), f32)],
        input_output_aliases={0: 0},
        compiler_params=pltpu.CompilerParams(vmem_limit_bytes=VMEM_LIMIT),
        cost_estimate=pl.CostEstimate(flops=0 if brief else FLOOR, bytes_accessed=0, transcendentals=0),
    )(values, token)


def specs(frames, width, tile):
    whole = pl.BlockSpec((frames, width), lambda j, *_: (0, 0))
    vector = pl.BlockSpec((1, width), lambda j, *_: (0, 0))
    column = pl.BlockSpec((width, tile), lambda j, *_: (0, j))
    row = pl.BlockSpec((tile, width), lambda j, *_: (j, 0))
    act = pl.BlockSpec((frames, tile), lambda j, *_: (0, j))
    table = pl.BlockSpec((frames, tile), lambda j, *_: (0, 0))
    logsum = pl.BlockSpec((8, frames), lambda j, *_: (j, 0))
    return whole, vector, column, row, act, table, logsum


def added(acc, term, result):
    step = pl.program_id(0)

    @pl.when(step == 0)
    def _():
        acc[...] = term

    @pl.when(step != 0)
    def _():
        acc[...] += term

    @pl.when(step == pl.num_programs(0) - 1)
    def _():
        result[...] = acc[...].astype(result.dtype)


def self_kernel(info, hid, gain, shift, wq, wk, wv, wo, cos, lower, upper, grad, copies, grad_copies, q, k, v, att, logsum, part, acc, mask, normed):
    frames = hid.shape[0]

    @pl.when(pl.program_id(0) == 0)
    def _():
        def rows(r):
            normed[r, :] = normed_rows(hid[r, :], gain[...], shift[...]).astype(low)

        over_rows(frames, rows)
        mask[...] = self_mask(info[0], frames)
        mine = normed[pl.ds(pl.multiple_of(info[3] * (frames // 2), frames // 2), frames // 2), :]
        grad_low = grad[...].astype(low)
        for chip in range(PLANE):
            copies[chip] = mine
            grad_copies[chip] = grad_low

    n = normed[...]
    tables = (cos[...], lower[...], upper[...])
    q[...] = turn(product_plain(n, wq[...]), *tables).astype(low)
    k[...] = turn(product_plain(n, wk[...]), *tables).astype(low)
    v[...] = product_plain(n, wv[...]).astype(low)
    attended = attend(q[...], k[...], v[...], mask[...], logsum)
    att[...] = attended
    added(acc, product_plain(attended, wo[...]), part)


def self_forward(token, info, hid, gain, shift, wq, wk, wv, wo, tables, grad, tile=4 * HEAD):
    frames, width = hid.shape
    columns = wq.shape[1]
    whole, vector, column, row, act, table, logsum = specs(frames, width, tile)
    return ordered(
        self_kernel,
        token,
        (hid, gain, shift, wq, wk, wv, wo, *tables, grad),
        [whole, vector, vector, column, column, column, row, table, table, table]
        + [pl.BlockSpec((frames // 2, width), lambda j, info: (info[3], 0))],
        [pl.BlockSpec((PLANE, frames // 2, width), lambda j, *_: (0, 0, 0))] * 2
        + [act, act, act, act, logsum, whole],
        [sds((PLANE, frames // 2, width), low)] * 2
        + [sds((frames, columns), low)] * 4
        + [sds((columns // tile * 8, frames), f32), sds((frames, width), low)],
        (columns // tile,),
        2 * frames * columns * (4 * width + 8 * frames),
        [
            pltpu.VMEM((frames, width), f32),
            pltpu.VMEM((frames, frames), f32),
            pltpu.VMEM((frames, width), low),
        ],
        info,
    )


def cross_kernel(info, hid, mine, other, gain, shift, cq, ck, cv, co, total, normed, q, att, logsum, part, acc):
    frames = hid.shape[0]

    @pl.when(pl.program_id(0) == 0)
    def _():
        def rows(r):
            x = hid[r, :] + (mine[r, :].astype(f32) + other[r, :].astype(f32))
            total[r, :] = x
            normed[r, :] = normed_rows(x, gain[...], shift[...]).astype(low)

        over_rows(frames, rows)

    q[...] = product_plain(normed[...], cq[...]).astype(low)
    attended = cross_attend(info, q[...], ck, cv, logsum)
    att[...] = attended
    added(acc, product_plain(attended, co[...]), part)


def cross_forward(token, info, hid, mine, other, gain, shift, cq, ck, cv, co, tile=4 * HEAD):
    frames, width = hid.shape
    columns, keys = cq.shape[1], ck.shape[0]
    whole, vector, column, row, act, table, logsum = specs(frames, width, tile)
    key = pl.BlockSpec((keys, tile), lambda j, *_: (0, j))
    return ordered(
        cross_kernel,
        token,
        (hid, mine, other, gain, shift, cq, ck, cv, co),
        [whole, whole, whole, vector, vector, column, key, key, row],
        [whole, whole, act, act, logsum, whole],
        [
            sds((frames, width), f32),
            sds((frames, width), low),
            sds((frames, columns), low),
            sds((frames, columns), low),
            sds((columns // tile * 8, frames), f32),
            sds((frames, width), low),
        ],
        (columns // tile,),
        2 * frames * columns * (2 * width + 8 * keys),
        [pltpu.VMEM((frames, width), f32)],
        info,
        brief=True,
    )


def norm_kernel(info, hid, mine, other, gain, shift, total, normed, copies):
    def rows(r):
        x = hid[r, :] + (mine[r, :].astype(f32) + other[r, :].astype(f32))
        total[r, :] = x
        normed[r, :] = normed_rows(x, gain[...], shift[...]).astype(low)

    over_rows(hid.shape[0], rows)

    @pl.when(pl.program_id(0) * 2 // pl.num_programs(0) == info[0])
    def _():
        values = normed[...]
        for chip in range(PLANE):
            copies[chip] = values


def norm_forward(token, hid, mine, other, gain, shift, half, block=128):
    frames, width = hid.shape
    blocks = frames // (2 * block)
    rows = pl.BlockSpec((block, width), lambda j, *_: (j, 0))
    vector = pl.BlockSpec((1, width), lambda j, *_: (0, 0))
    return ordered(
        norm_kernel,
        token,
        (hid, mine, other, gain, shift),
        [rows, rows, rows, vector, vector],
        [
            rows,
            rows,
            pl.BlockSpec(
                (PLANE, block, width),
                lambda j, info: (0, jnp.clip(j - blocks * info[0], 0, blocks - 1), 0),
            ),
        ],
        [sds((frames, width), f32), sds((frames, width), low), sds((PLANE, frames // 2, width), low)],
        (frames // block,),
        10 * frames * width,
        info=half,
        brief=True,
    )


def cross_back_kernel(info, x, mine, other, above, gain, co, q, ck, cv, att, logsum, cq, total, total_low, vectors, dq, dk, dv, part, acc, gain_acc, shift_acc):
    @pl.when(pl.program_id(0) == 0)
    def _():
        norm_back_all(x, mine, other, above, gain, total, total_low, vectors, gain_acc, shift_acc)

    g = product_with_rows(total_low[...], co[...]).astype(low)
    a, b, c = cross_attend_back(info, q[...], ck, cv, g, att[...], logsum[...])
    a = a.astype(low)
    dq[...] = a
    dk[...] = b.astype(low)
    dv[...] = c.astype(low)
    added(acc, product_with_rows(a, cq[...]), part)


def cross_backward(token, info, x, mine, other, above, gain, co, q, ck, cv, att, logsums, cq, tile=4 * HEAD):
    frames, width = x.shape
    columns, keys = cq.shape[1], ck.shape[0]
    whole, vector, column, row, act, table, logsum = specs(frames, width, tile)
    key = pl.BlockSpec((keys, tile), lambda j, *_: (0, j))
    two = pl.BlockSpec((2, width), lambda j, *_: (0, 0))
    return ordered(
        cross_back_kernel,
        token,
        (x, mine, other, above, gain, co, q, ck, cv, att, logsums, cq),
        [whole, whole, whole, whole, vector, row, act, key, key, act, logsum, column],
        [whole, whole, two, act, key, key, whole],
        [
            sds((frames, width), f32),
            sds((frames, width), low),
            sds((2, width), f32),
            sds((frames, columns), low),
            sds((keys, columns), low),
            sds((keys, columns), low),
            sds((frames, width), low),
        ],
        (columns // tile,),
        2 * frames * columns * (2 * width + 20 * keys),
        [
            pltpu.VMEM((frames, width), f32),
            pltpu.VMEM((8, width), f32),
            pltpu.VMEM((8, width), f32),
        ],
        info,
    )


def self_back_kernel(info, x, mine, other, above, gain, wo, q, k, v, att, logsum, wq, wk, wv, cos, lower, upper, total, total_low, vectors, grads, part, acc, mask, gain_acc, shift_acc):
    frames = x.shape[0]

    @pl.when(pl.program_id(0) == 0)
    def _():
        norm_back_all(x, mine, other, above, gain, total, total_low, vectors, gain_acc, shift_acc)
        mask[...] = self_mask(info[0], frames)

    g = product_with_rows(total_low[...], wo[...]).astype(low)
    a, b, c = attend_back(q[...], k[...], v[...], g, att[...], mask[...], logsum[...])
    tables = (cos[...], lower[...], upper[...])
    a = turn_back(a, *tables).astype(low)
    b = turn_back(b, *tables).astype(low)
    c = c.astype(low)
    for index, values in enumerate((a, b, c)):
        turned = values.T
        for quarter in range(PLANE):
            grads[quarter, index] = turned[quarter * HEAD : (quarter + 1) * HEAD]
    added(
        acc,
        product_with_rows(a, wq[...]) + product_with_rows(b, wk[...]) + product_with_rows(c, wv[...]),
        part,
    )


def self_backward(token, info, x, mine, other, above, gain, wo, q, k, v, att, logsums, wq, wk, wv, tables, tile=4 * HEAD):
    frames, width = x.shape
    columns = wq.shape[1]
    whole, vector, column, row, act, table, logsum = specs(frames, width, tile)
    two = pl.BlockSpec((2, width), lambda j, *_: (0, 0))
    heads = pl.BlockSpec((PLANE, 3, HEAD, frames), lambda j, *_: (0, 0, j, 0))
    return ordered(
        self_back_kernel,
        token,
        (x, mine, other, above, gain, wo, q, k, v, att, logsums, wq, wk, wv, *tables),
        [whole, whole, whole, whole, vector, row, act, act, act, act, logsum, column, column, column, table, table, table],
        [whole, whole, two, heads, whole],
        [
            sds((frames, width), f32),
            sds((frames, width), low),
            sds((2, width), f32),
            sds((PLANE, 3, columns // PLANE, frames), low),
            sds((frames, width), low),
        ],
        (columns // tile,),
        2 * frames * columns * (4 * width + 20 * frames),
        [
            pltpu.VMEM((frames, width), f32),
            pltpu.VMEM((frames, frames), f32),
            pltpu.VMEM((8, width), f32),
            pltpu.VMEM((8, width), f32),
        ],
        info,
    )


def last_kernel(_, x, mine, other, above, gain, resid, sum_mine, sum_other, total, vectors, result, gain_acc, shift_acc):
    step = pl.program_id(0)

    @pl.when(step == 0)
    def _():
        gain_acc[...] = jnp.zeros_like(gain_acc)
        shift_acc[...] = jnp.zeros_like(shift_acc)

    def rows(r):
        e = mine[r, :].astype(f32) + other[r, :].astype(f32)
        total[r, :] = norm_back_rows(x[r, :], e, gain[...], above[r, :], gain_acc, shift_acc)
        result[r, :] = resid[r, :] + (sum_mine[r, :].astype(f32) + sum_other[r, :].astype(f32))

    over_rows(x.shape[0], rows)

    @pl.when(step == pl.num_programs(0) - 1)
    def _():
        vectors[0:1, :] = jnp.sum(gain_acc[...], axis=0, keepdims=True)
        vectors[1:2, :] = jnp.sum(shift_acc[...], axis=0, keepdims=True)


def last_backward(token, x, mine, other, above, gain, resid, sum_mine, sum_other, block=128):
    frames, width = x.shape
    rows = pl.BlockSpec((block, width), lambda j, *_: (j, 0))
    vector = pl.BlockSpec((1, width), lambda j, *_: (0, 0))
    two = pl.BlockSpec((2, width), lambda j, *_: (0, 0))
    return ordered(
        last_kernel,
        token,
        (x, mine, other, above, gain, resid, sum_mine, sum_other),
        [rows, rows, rows, rows, vector, rows, rows, rows],
        [rows, two, rows],
        [sds((frames, width), f32), sds((2, width), f32), sds((frames, width), f32)],
        (frames // block,),
        20 * frames * width,
        [pltpu.VMEM((8, width), f32), pltpu.VMEM((8, width), f32)],
        brief=True,
    )


def pack_kernel(_, *refs):
    for values, copies in zip(refs[: len(refs) // 2], refs[len(refs) // 2 :]):
        copies[...] = values[...].astype(low)


def packed(token, values, half, pieces=1):
    frames, width = values.shape
    rows = frames // (2 * pieces)

    def source(piece):
        return pl.BlockSpec((rows, width), lambda j, info: (info[0] * pieces + piece, 0))

    return ordered(
        pack_kernel,
        token,
        (values,) * pieces,
        [source(piece) for piece in range(pieces)],
        [pl.BlockSpec((rows, width), lambda j, info: (j, 0))] * pieces,
        [sds((PLANE * rows, width), low)] * pieces,
        (PLANE,),
        0,
        info=half,
        brief=True,
    )


def ff_kernel(_, in_ref, out_ref, gate_ref, up_ref, down_ref, sum_ref, back_ref, sum_acc, back_acc, out_low):
    @pl.when(pl.program_id(0) == 0)
    def _():
        out_low[...] = out_ref[...].astype(low)

    normed = in_ref[...]
    mixed, grad_gate, grad_up = ff_parts(
        product_plain(normed, gate_ref[...]),
        product_plain(normed, up_ref[...]),
        product_with_rows(out_low[...], down_ref[...]),
    )
    added(sum_acc, product_plain(mixed, down_ref[...]), sum_ref)
    added(
        back_acc,
        product_with_rows(grad_gate, gate_ref[...]) + product_with_rows(grad_up, up_ref[...]),
        back_ref,
    )


def ff_both(token, normed, grad_out, w_gate, w_up, w_down, tile=768):
    frames, width = normed.shape
    units = w_gate.shape[1]
    whole, _, column, row, *_ = specs(frames, width, tile)
    return ordered(
        ff_kernel,
        token,
        (normed, grad_out, w_gate, w_up, w_down),
        [whole, whole, column, column, row],
        [whole, whole],
        [sds((frames, width), low)] * 2,
        (units // tile,),
        12 * frames * width * units,
        [pltpu.VMEM((frames, width), f32)] * 2 + [pltpu.VMEM((frames, width), low)],
    )


def share_kernel(info, in_mine, in_other, out_mine, out_other, gate_ref, up_ref, down_ref, send_ref, keep_ref, acc):
    step = pl.program_id(1)
    normed = jnp.concatenate([in_mine[...], in_other[...]], axis=0)
    grad_out = jnp.concatenate([out_mine[...], out_other[...]], axis=0)
    mixed, grad_gate, grad_up = ff_parts(
        product_plain(normed, gate_ref[...]),
        product_plain(normed, up_ref[...]),
        product_with_rows(grad_out, down_ref[...]),
    )
    fresh = (
        product_over_rows(grad_out, mixed),
        product_over_rows(normed, grad_gate),
        product_over_rows(normed, grad_up),
    )
    for index, term in enumerate(fresh):

        @pl.when(step == 0)
        def _():
            acc[index] = term

        @pl.when(step != 0)
        def _():
            acc[index] += term

    @pl.when(step == pl.num_programs(1) - 1)
    def _():
        rows = send_ref.shape[2] // 3
        for pair in range(2):
            for index in range(3):
                for ref, parity in ((send_ref, 1 - info[1]), (keep_ref, info[1])):
                    start = pl.multiple_of((2 * pair + parity) * rows, rows)
                    ref[0, pair, index * rows : (index + 1) * rows] = acc[
                        index, pl.ds(start, rows), :
                    ].astype(ref.dtype)


def ff_share(token, info, normed, grad_out, w_gate, w_up, w_down, tile, count):
    frames, width = normed[0].shape
    chunk = frames // PLANE
    rows = pl.BlockSpec((chunk, width), lambda i, j, info: (j, 0))
    column = pl.BlockSpec((width, tile), lambda i, j, info: (0, info[0] + i))
    half = (LEVELS // 2, 3 * width // LEVELS, tile)
    return ordered(
        share_kernel,
        token,
        (*normed, *grad_out, w_gate, w_up, w_down),
        [rows] * 4
        + [column, column, pl.BlockSpec((tile, width), lambda i, j, info: (info[0] + i, 0))],
        [pl.BlockSpec((1, *half), lambda i, j, info: (i, 0, 0, 0))] * 2,
        [sds((count, *half), low)] * 2,
        (count, PLANE),
        24 * frames * width * tile * count,
        [pltpu.VMEM((3, width, tile), f32)],
        info,
    )


def weight_kernel(plan, sides_count, _, *refs):
    sides, columns = refs[:sides_count], refs[sides_count : sides_count + len(plan)]
    out = refs[sides_count + len(plan)]
    turned = refs[sides_count + len(plan) + 1 :]

    @pl.when(pl.program_id(0) == 0)
    def _():
        for side, ref in zip(sides, turned):
            ref[...] = side[...].T

    for (which, first), column in zip(plan, columns):
        product = product_plain(turned[which][...], column[...]).astype(low)
        rows = product.shape[0] // (PLANE * LEVELS)
        product = product.reshape(LEVELS, PLANE, rows, product.shape[1])
        for owner in range(PLANE):
            out[owner, :, first : first + rows, :] = product[:, owner]


def weight_products(token, sides, plan, columns, tile=256):
    width = columns[0].shape[1]
    rows = sum(sides[which].shape[1] for which, _ in plan) // (PLANE * LEVELS)
    return ordered(
        functools.partial(weight_kernel, plan, len(sides)),
        token,
        (*sides, *columns),
        [pl.BlockSpec(side.shape, lambda j, *_: (0, 0)) for side in sides]
        + [pl.BlockSpec((column.shape[0], tile), lambda j, *_: (0, j)) for column in columns],
        [pl.BlockSpec((PLANE, LEVELS, rows, tile), lambda j, *_: (0, 0, 0, j))],
        [sds((PLANE, LEVELS, rows, width), low)],
        (width // tile,),
        sum(2 * sides[w].shape[0] * sides[w].shape[1] * width for w, _ in plan),
        [pltpu.VMEM((side.shape[1], side.shape[0]), low) for side in sides],
        brief=len(sides) == 1,
    )


def plane_sum_kernel(info, got, send, keep):
    for ref, parity in ((send, 1 - info[0]), (keep, info[0])):
        total = got[0, 0, parity].astype(f32)
        for source in range(1, PLANE):
            total = total + got[source, 0, parity].astype(f32)
        ref[0] = total.astype(low)


def plane_sum(token, got, parity):
    rows, width = got.shape[2:]
    out = pl.BlockSpec((1, rows, width), lambda j, *_: (j, 0, 0))
    return ordered(
        plane_sum_kernel,
        token,
        (got.reshape(PLANE, 2, 2, rows, width),),
        [pl.BlockSpec((PLANE, 1, 2, rows, width), lambda j, *_: (0, j, 0, 0, 0))],
        [out, out],
        [sds((2, rows, width), low)] * 2,
        (2,),
        0,
        info=parity,
    )


def level_sum_kernel(_, keep_pass, got_pass, keep_own, got_own, passed, own):
    passed[...] = (keep_pass[0, 0].astype(f32) + got_pass[0, 0].astype(f32)).astype(low)
    own[...] = keep_own[0, 0].astype(f32) + got_own[0, 0].astype(f32)


def level_sum(token, keep, got, upper):
    count, _, rows, width = keep.shape
    block = rows // 2 if rows % 32 == 0 else rows
    steps = rows // block
    off = pl.BlockSpec((1, 1, block, width), lambda i, j, info: (i, 1 - info[0], j, 0))
    own = pl.BlockSpec((1, 1, block, width), lambda i, j, info: (i, info[0], j, 0))
    out = pl.BlockSpec((block, width), lambda i, j, info: (i * steps + j, 0))
    return ordered(
        level_sum_kernel,
        token,
        (keep, got, keep, got),
        [off, off, own, own],
        [out, out],
        [sds((count * rows, width), low), sds((count * rows, width), f32)],
        (count, steps),
        0,
        info=upper,
    )


def unit_pack_kernel(counts, _, *refs):
    owns, lasts, out = refs[:-1:2], refs[1:-1:2], refs[-1]
    step = pl.program_id(0)
    for own, last, (first, count) in zip(owns, lasts, counts):

        @pl.when((step >= first) & (step < first + count))
        def _():
            total = (own[...] + last[...].astype(f32)).astype(low)
            total = total.reshape(3, PLANE, out.shape[2], out.shape[3])
            for chip in range(PLANE):
                out[chip] = total[:, chip]


def unit_pack(token, sums, rows):
    tile = sums[0][0].shape[1]
    r = rows // (3 * PLANE)
    specs_in, counts, first = [], [], 0
    for own, _ in sums:
        count = own.shape[0] // rows

        def place(j, info, first=first, count=count):
            return (jnp.clip(j - first, 0, count - 1), 0)

        specs_in += [pl.BlockSpec((rows, tile), place)] * 2
        counts.append((first, count))
        first += count
    return ordered(
        functools.partial(unit_pack_kernel, counts),
        token,
        tuple(array for pair in sums for array in pair),
        specs_in,
        [pl.BlockSpec((PLANE, 3, r, tile), lambda j, *_: (0, 0, 0, j))],
        [sds((PLANE, 3, r, tile * first), low)],
        (first,),
        0,
    )


def unit_unpack_kernel(_, got, down, gate, up):
    down[...] = got[0, 0].astype(f32).T
    gate[...] = got[0, 1].astype(f32)
    up[...] = got[0, 2].astype(f32)


def unit_unpack(token, got):
    _, _, r, units = got.shape
    across = pl.BlockSpec((r, units), lambda j, *_: (0, j))
    return ordered(
        unit_unpack_kernel,
        token,
        (got,),
        [pl.BlockSpec((1, 3, r, units), lambda j, *_: (j, 0, 0, 0))],
        [pl.BlockSpec((units, r), lambda j, *_: (j, 0)), across, across],
        [sds((PLANE * units, r), f32)] + [sds((r, PLANE * units), f32)] * 2,
        (PLANE,),
        0,
    )


def head_pack_kernel(_, own, last, out):
    total = (own[...] + last[...].astype(f32)).T.astype(low)
    out[...] = total.reshape(out.shape)


def head_pack(token, own, last):
    features, columns = own.shape
    shape = (PLANE, columns // PLANE, features)
    return ordered(
        head_pack_kernel,
        token,
        (own, last),
        [pl.BlockSpec(own.shape, lambda j, *_: (0, 0))] * 2,
        [pl.BlockSpec(shape, lambda j, *_: (0, 0, 0))],
        [sds(shape, low)],
        (1,),
        0,
    )


def head_unpack_kernel(_, got, *outs):
    groups = got.shape[2] // (3 * HEAD)
    for index, out in enumerate(outs):
        pieces = []
        for group in range(groups):
            first = (index * groups + group) * HEAD
            pieces += [got[chip, :, first : first + HEAD] for chip in range(PLANE)]
        out[...] = jnp.concatenate(pieces, axis=1).astype(f32)


def head_unpack(token, got):
    chips, r, features = got.shape
    shape = (r, chips * features // 3)
    return ordered(
        head_unpack_kernel,
        token,
        (got,),
        [pl.BlockSpec(got.shape, lambda j, *_: (0, 0, 0))],
        [pl.BlockSpec(shape, lambda j, *_: (0, 0))] * 3,
        [sds(shape, f32)] * 3,
        (1,),
        0,
    )


def head_kernel(info, grads_mine, grads_other, in_mine, in_other, send, keep, acc):
    step = pl.program_id(0)
    rows = acc.shape[0]
    term = product_plain(grads_mine[0].reshape(rows, -1), in_mine[...]) + product_plain(
        grads_other[0].reshape(rows, -1), in_other[...]
    )

    @pl.when(step == 0)
    def _():
        acc[...] = term

    @pl.when(step != 0)
    def _():
        acc[...] += term

    @pl.when(step == pl.num_programs(0) - 1)
    def _():
        width = send.shape[2]
        for level in range(LEVELS):
            for ref, parity in ((send, 1 - info[1]), (keep, info[1])):

                @pl.when(parity == level % 2)
                def _():
                    ref[level // 2] = acc[:, level * width : (level + 1) * width].astype(low)


def head_products(token, info, grads, normed):
    _, three, features, frames = grads.shape
    width = normed[0].shape[1]
    chunk = normed[0].shape[0] // PLANE
    rows = pl.BlockSpec((chunk, width), lambda j, info: (j, 0))
    half = (LEVELS // 2, three * features, width // LEVELS)
    return ordered(
        head_kernel,
        token,
        (grads, grads, *normed),
        [
            pl.BlockSpec((1, three, features, chunk), lambda j, info: (j, 0, 0, info[0])),
            pl.BlockSpec((1, three, features, chunk), lambda j, info: (j, 0, 0, 1 - info[0])),
            rows,
            rows,
        ],
        [pl.BlockSpec(half, lambda j, info: (0, 0, 0))] * 2,
        [sds(half, low)] * 2,
        (PLANE,),
        2 * three * features * PLANE * frames * width,
        [pltpu.VMEM((three * features, width), f32)],
        info,
    )


def on_plane(
    hidden_in,
    out_grad,
    prompt_states,
    row_split,
    prompt_len,
    gain_attn,
    bias_attn,
    gain_cross,
    bias_cross,
    gain_ff,
    bias_ff,
    w_query,
    w_key,
    w_value,
    w_out,
    c_query,
    c_key,
    c_value,
    c_out,
    w_gate,
    w_up,
    w_down,
):
    frames, width = hidden_in.shape
    plane, level = lax.axis_index("dp") % PLANE, lax.axis_index("dp") // PLANE
    info = jnp.concatenate([row_split, prompt_len])
    positions = jnp.arange(frames, dtype=jnp.int32)
    row_ids = (positions >= row_split[0]).astype(jnp.int32)
    tables = rotary_tables((positions - row_ids * row_split[0]).astype(f32), 2 * HEAD)
    tables = lax.optimization_barrier(tables)
    tables = tuple(jnp.concatenate([table, table], axis=1) for table in tables)
    gain_attn, bias_attn, gain_cross, bias_cross, gain_ff, bias_ff = (
        vector[None] for vector in (gain_attn, bias_attn, gain_cross, bias_cross, gain_ff, bias_ff)
    )

    zero = jnp.zeros((1,), jnp.int32)
    half = zero + lax.axis_index("tensor")
    parity, upper = zero + level % 2, zero + level // 2
    chips = [[PLANE * z + p for p in range(PLANE)] for z in range(LEVELS)]

    def swapped(part):
        return lax.ppermute(part, "tensor", [(0, 1), (1, 0)])

    def in_plane(values):
        shape = values.shape
        return lax.all_to_all(
            values, "dp", 0, 0, axis_index_groups=chips, tiled=True
        ).reshape(shape)

    def gathered(copies):
        return in_plane(copies.reshape(-1, width))

    def level_swap(values, mask):
        return lax.ppermute(values, "dp", pairs(mask))

    token = jnp.zeros((8, 128), f32)
    context = prompt_states.reshape(2 * PROMPT, prompt_states.shape[2])
    cross_key = product_plain(context, c_key).astype(low)
    cross_value = product_plain(context, c_value).astype(low)
    copies_one, copies, query, key, value, attended_one, logsum_one, part, token = self_forward(
        token,
        jnp.concatenate([info, half]),
        hidden_in,
        gain_attn,
        bias_attn,
        w_query,
        w_key,
        w_value,
        w_out,
        tables,
        out_grad,
    )
    part_swapped = swapped(part)
    frames_out = gathered(copies)
    resid_one, input_two, cross_query, attended_two, logsum_two, part, token = cross_forward(
        token,
        info,
        hidden_in,
        part,
        part_swapped,
        gain_cross,
        bias_cross,
        c_query,
        cross_key,
        cross_value,
        c_out,
    )
    part_swapped = swapped(part)
    resid_two, input_three, copies, token = norm_forward(
        token, resid_one, part, part_swapped, gain_ff, bias_ff, half
    )
    frames_out, token = hold(token, frames_out)
    frames_in = gathered(copies)
    frames_out = (frames_out, swapped(frames_out))
    sum_part, back_part, token = ff_both(token, input_three, out_grad, w_gate, w_up, w_down)
    frames_in, token = hold(token, frames_in)
    frames_in = (frames_in, swapped(frames_in))
    back_swapped = swapped(back_part)
    copies_one, token = hold(token, copies_one)
    frames_one = gathered(copies_one)

    tile = 256
    tiles = w_gate.shape[1] // (PLANE * tile)

    def share(token, index, count):
        number = jnp.concatenate([zero + plane * tiles + index, parity])
        return ff_share(token, number, frames_in, frames_out, w_gate, w_up, w_down, tile, count)

    send_a, keep_a, token = share(token, 0, 1)
    got_a = level_swap(send_a, PLANE)
    grad_two, grad_cross_out, vectors_ff, query_grad, key_grad, value_grad, part, token = cross_backward(
        token,
        info,
        resid_two,
        back_part,
        back_swapped,
        out_grad,
        gain_ff,
        c_out,
        cross_query,
        cross_key,
        cross_value,
        attended_two,
        logsum_two,
        c_query,
    )
    part_swapped = swapped(part)
    r, c = width // 16, context.shape[1] // 16
    products, token = weight_products(
        token,
        [grad_cross_out, input_two, context],
        [(0, 0), (1, r), (2, 2 * r), (2, 2 * r + c)],
        [attended_two, query_grad, key_grad, value_grad],
    )
    frames_one, token = hold(token, frames_one)
    got_cross = in_plane(products)
    frames_one = (frames_one, swapped(frames_one))
    pass_a, own_a, token = level_sum(token, keep_a, got_a, upper)
    last_a = level_swap(pass_a, 2 * PLANE)
    send_b, keep_b, token = share(token, 1, tiles - 1)
    got_b = level_swap(send_b, PLANE)
    grad_one, grad_self_out, vectors_cross, grads, part, token = self_backward(
        token,
        info,
        resid_one,
        part,
        part_swapped,
        grad_two,
        gain_cross,
        w_out,
        query,
        key,
        value,
        attended_one,
        logsum_one,
        w_query,
        w_key,
        w_value,
        tables,
    )
    part_swapped = swapped(part)
    last_a, token = hold(token, last_a, True)
    sum_part, token = hold(token, sum_part, True)
    sum_swapped = swapped(sum_part)
    products, token = weight_products(token, [grad_self_out], [(0, 0)], [attended_one])
    grad_hidden, vectors_attn, result, token = last_backward(
        token, hidden_in, part, part_swapped, grad_one, gain_attn, resid_two, sum_part, sum_swapped
    )
    vectors = jnp.concatenate([vectors_attn, vectors_cross, vectors_ff])
    pass_b, own_b, token = level_sum(token, keep_b, got_b, upper)
    last_b = level_swap(pass_b, 2 * PLANE)
    got_cross, token = hold(token, got_cross)
    grads, token = hold(token, grads)
    got_heads = in_plane(grads)
    send_x, keep_x, token = plane_sum(token, got_cross, parity)
    got_x = level_swap(send_x, PLANE)
    got_heads, token = hold(token, got_heads)
    products, token = hold(token, products)
    got_out = in_plane(products)
    send_h, keep_h, token = head_products(
        token, jnp.concatenate([half, parity]), got_heads, frames_one
    )
    got_h = level_swap(send_h, PLANE)
    last_b, token = hold(token, last_b)
    units, token = unit_pack(token, [(own_a, last_a), (own_b, last_b)], 3 * width // LEVELS)
    pass_x, own_x, token = level_sum(token, keep_x[None], got_x[None], upper)
    last_x = level_swap(pass_x, 2 * PLANE)
    vectors_got = level_swap(vectors, 1)
    got_out, token = hold(token, got_out)
    units, token = hold(token, units)
    units = in_plane(units)
    send_o, keep_o, token = plane_sum(token, got_out, parity)
    got_o = level_swap(send_o, PLANE)
    pass_h, own_h, token = level_sum(token, keep_h[None], got_h[None], upper)
    last_h = level_swap(pass_h, 2 * PLANE)
    vectors_got, token = hold(token, vectors_got)
    vectors = vectors + vectors_got
    vectors_got = level_swap(vectors, 2)
    pass_o, own_o, token = level_sum(token, keep_o[None], got_o[None], upper)
    last_o = level_swap(pass_o, 2 * PLANE)
    last_x, token = hold(token, last_x)
    cross = add_low(own_x, last_x)
    units, token = hold(token, units)
    grad_w_down, grad_w_gate, grad_w_up, token = unit_unpack(token, units)
    vectors_got, token = hold(token, vectors_got)
    vectors = vectors + vectors_got
    vectors_got = level_swap(vectors, PLANE)
    heads, token = head_pack(token, own_h, last_h)
    heads = in_plane(heads)
    vectors_got, token = hold(token, vectors_got)
    vectors = vectors + vectors_got
    vectors = own_share(vectors + level_swap(vectors, 2 * PLANE))
    heads, token = hold(token, heads)
    grad_w_query, grad_w_key, grad_w_value, token = head_unpack(token, heads)
    return (
        result,
        grad_hidden,
        *(vectors[index] for index in range(6)),
        grad_w_query,
        grad_w_key,
        grad_w_value,
        add_low(own_o, last_o).T,
        cross[r : 2 * r],
        cross[2 * r : 2 * r + c],
        cross[2 * r + c :],
        cross[:r].T,
        grad_w_gate,
        grad_w_up,
        grad_w_down,
    )


def on_any(
    hidden_in,
    out_grad,
    prompt_states,
    row_split,
    prompt_len,
    gain_attn,
    bias_attn,
    gain_cross,
    bias_cross,
    gain_ff,
    bias_ff,
    w_query,
    w_key,
    w_value,
    w_out,
    c_query,
    c_key,
    c_value,
    c_out,
    w_gate,
    w_up,
    w_down,
):
    frame_count = hidden_in.shape[0]
    positions = jnp.arange(frame_count, dtype=jnp.int32)
    split_here = row_split[0]
    row_ids = (positions >= split_here).astype(jnp.int32)
    tables = rotary_tables((positions - row_ids * split_here).astype(jnp.float32), w_query.shape[1])
    key_index = jnp.arange(2 * PROMPT, dtype=jnp.int32)
    key_rows = key_index // PROMPT
    key_live = key_index % PROMPT < jnp.where(key_rows == 0, prompt_len[0], prompt_len[1])
    self_ok = row_ids[:, None] == row_ids[None, :]
    cross_ok = (row_ids[:, None] == key_rows[None, :]) & key_live[None, :]

    normed, scaled_one, inverse_one = normalize(hidden_in, gain_attn, bias_attn)
    input_one = normed.astype(low)
    query_one = rotate(product_plain(input_one, w_query), tables).astype(low)
    key_one = rotate(product_plain(input_one, w_key), tables).astype(low)
    value_one = product_plain(input_one, w_value).astype(low)
    attended_one, logsum_one = attend_forward(query_one, heads_of(key_one), heads_of(value_one), self_ok)
    resid_one = hidden_in + swap_sum(product_plain(attended_one, w_out))

    normed, scaled_two, inverse_two = normalize(resid_one, gain_cross, bias_cross)
    input_two = normed.astype(low)
    cross_query = product_plain(input_two, c_query).astype(low)
    context_flat = prompt_states.reshape(2 * PROMPT, prompt_states.shape[2])
    cross_key = product_plain(context_flat, c_key).astype(low)
    cross_value = product_plain(context_flat, c_value).astype(low)
    attended_two, logsum_two = attend_forward(
        cross_query, heads_of(cross_key), heads_of(cross_value), cross_ok
    )
    resid_two = resid_one + swap_sum(product_plain(attended_two, c_out))

    normed, scaled_three, inverse_three = normalize(resid_two, gain_ff, bias_ff)
    input_three = normed.astype(low)
    gate_pre = product_plain(input_three, w_gate)
    up_pre = product_plain(input_three, w_up)
    sigmoid_gate = jax.nn.sigmoid(gate_pre)
    mixed_low = (gate_pre * sigmoid_gate * up_pre).astype(low)
    result = resid_two + swap_sum(product_plain(mixed_low, w_down))

    grad_ff_out = out_grad.astype(low)
    grad_w_down = generic_sum(grad_ff_out, mixed_low).T
    grad_mixed = product_with_rows(grad_ff_out, w_down)
    grad_gate = (
        grad_mixed * up_pre * sigmoid_gate * (1.0 + gate_pre * (1.0 - sigmoid_gate))
    ).astype(low)
    grad_up = (grad_mixed * gate_pre * sigmoid_gate).astype(low)
    grad_w_gate = generic_sum(input_three, grad_gate)
    grad_w_up = generic_sum(input_three, grad_up)
    normed_grad_three = swap_sum(
        product_with_rows(grad_gate, w_gate) + product_with_rows(grad_up, w_up)
    )
    back_three, grad_gain_ff, grad_bias_ff = normalize_back(
        normed_grad_three, scaled_three, inverse_three, gain_ff
    )
    grad_two = out_grad + back_three
    grad_cross_out = grad_two.astype(low)
    grad_c_out = generic_sum(grad_cross_out, attended_two).T
    grad_attended_two = product_with_rows(grad_cross_out, c_out).astype(low)
    cross_query_grad, cross_key_grad, cross_value_grad = attend_backward(
        cross_query,
        heads_of(cross_key),
        heads_of(cross_value),
        cross_ok,
        grad_attended_two,
        logsum_two,
    )
    cross_query_grad = cross_query_grad.astype(low)
    cross_key_grad = cross_key_grad.astype(low)
    cross_value_grad = cross_value_grad.astype(low)
    grad_c_query = generic_sum(input_two, cross_query_grad)
    grad_c_key = generic_sum(context_flat, cross_key_grad)
    grad_c_value = generic_sum(context_flat, cross_value_grad)
    normed_grad_two = swap_sum(product_with_rows(cross_query_grad, c_query))
    back_two, grad_gain_cross, grad_bias_cross = normalize_back(
        normed_grad_two, scaled_two, inverse_two, gain_cross
    )
    grad_one = grad_two + back_two
    grad_self_out = grad_one.astype(low)
    grad_w_out = generic_sum(grad_self_out, attended_one).T
    grad_attended_one = product_with_rows(grad_self_out, w_out).astype(low)
    query_grad, key_grad, value_grad = attend_backward(
        query_one, heads_of(key_one), heads_of(value_one), self_ok, grad_attended_one, logsum_one
    )
    query_grad = rotate_back(query_grad, tables).astype(low)
    key_grad = rotate_back(key_grad, tables).astype(low)
    value_grad = value_grad.astype(low)
    grad_w_query = generic_sum(input_one, query_grad)
    grad_w_key = generic_sum(input_one, key_grad)
    grad_w_value = generic_sum(input_one, value_grad)
    normed_grad_one = swap_sum(
        product_with_rows(query_grad, w_query)
        + product_with_rows(key_grad, w_key)
        + product_with_rows(value_grad, w_value)
    )
    back_one, grad_gain_attn, grad_bias_attn = normalize_back(
        normed_grad_one, scaled_one, inverse_one, gain_attn
    )
    grad_hidden = grad_one + back_one
    vectors = lax.psum(
        jnp.stack(
            [
                grad_gain_attn,
                grad_bias_attn,
                grad_gain_cross,
                grad_bias_cross,
                grad_gain_ff,
                grad_bias_ff,
            ]
        ),
        "dp",
    )
    vectors = own_share(vectors)
    return (
        result,
        grad_hidden,
        vectors[0],
        vectors[1],
        vectors[2],
        vectors[3],
        vectors[4],
        vectors[5],
        grad_w_query,
        grad_w_key,
        grad_w_value,
        grad_w_out,
        grad_c_query,
        grad_c_key,
        grad_c_value,
        grad_c_out,
        grad_w_gate,
        grad_w_up,
        grad_w_down,
    )


def solution(mesh):
    in_specs = (
        P("dp", None),
        P("dp", None),
        P("dp", None, None),
        P("dp"),
        P("dp"),
        P(),
        P(),
        P(),
        P(),
        P(),
        P(),
        P(None, "tensor"),
        P(None, "tensor"),
        P(None, "tensor"),
        P("tensor", None),
        P(None, "tensor"),
        P(None, "tensor"),
        P(None, "tensor"),
        P("tensor", None),
        P(None, "tensor"),
        P(None, "tensor"),
        P("tensor", None),
    )
    out_specs = (
        P("dp", None),
        P("dp", None),
        P(("dp", "tensor")),
        P(("dp", "tensor")),
        P(("dp", "tensor")),
        P(("dp", "tensor")),
        P(("dp", "tensor")),
        P(("dp", "tensor")),
        P("dp", "tensor"),
        P("dp", "tensor"),
        P("dp", "tensor"),
        P("tensor", "dp"),
        P("dp", "tensor"),
        P("dp", "tensor"),
        P("dp", "tensor"),
        P("tensor", "dp"),
        P("dp", "tensor"),
        P("dp", "tensor"),
        P("tensor", "dp"),
    )
    known = mesh.shape["dp"] == PLANE * LEVELS and mesh.shape["tensor"] == 2
    return jax.shard_map(
        on_plane if known else on_any, mesh=mesh, in_specs=in_specs, out_specs=out_specs, check_vma=False
    )
```

```python
import functools
import math

import jax
import jax.numpy as jnp
from jax import lax
from jax.experimental import pallas as pl
from jax.experimental.pallas import tpu as pltpu
from jax.sharding import PartitionSpec as P

PROMPT = 128
HEAD = 64
PLANE = 4
LEVELS = 4
VMEM_LIMIT = 62 * 2**20
COST = 3
FLOOR = 15 * 10**9

low = jnp.bfloat16
f32 = jnp.float32
sds = jax.ShapeDtypeStruct


norm_eps = 1e-05
score_scale = 0.125
masked_score = -1e30


def product_plain(left_side, right_side):
    return jnp.dot(left_side, right_side, preferred_element_type=jnp.float32)


def product_over_rows(left_side, right_side):
    return lax.dot_general(
        left_side, right_side, (((0,), (0,)), ((), ())), preferred_element_type=jnp.float32
    )


def product_with_rows(left_side, right_side):
    return lax.dot_general(
        left_side, right_side, (((1,), (1,)), ((), ())), preferred_element_type=jnp.float32
    )


def rotary_tables(positions, width):
    dim_index = jnp.arange(width) % HEAD
    freq_index = (dim_index % 16).astype(jnp.float32)
    inverse_freq = jnp.exp(freq_index * (-math.log(10000.0) / 16.0))
    angles = positions[:, None] * inverse_freq[None, :]
    cosine = jnp.cos(angles)
    sine_part = jnp.sin(angles)
    cos_table = jnp.where(dim_index < 32, cosine, 1.0)
    sin_lower = jnp.where(dim_index < 16, -sine_part, 0.0)
    sin_upper = jnp.where((dim_index >= 16) & (dim_index < 32), sine_part, 0.0)
    return (cos_table, sin_lower, sin_upper)


def rotate(values, tables):
    cos_table, sin_lower, sin_upper = tables
    return (
        values * cos_table
        + jnp.roll(values, -16, axis=1) * sin_lower
        + jnp.roll(values, 16, axis=1) * sin_upper
    )


def rotate_back(incoming, tables):
    cos_table, sin_lower, sin_upper = tables
    return (
        incoming * cos_table
        + jnp.roll(incoming * sin_lower, 16, axis=1)
        + jnp.roll(incoming * sin_upper, -16, axis=1)
    )


def normalize(values, norm_gain, norm_shift):
    average = jnp.mean(values, axis=-1, keepdims=True)
    centered = values - average
    variance = jnp.mean(centered * centered, axis=-1, keepdims=True)
    inverse = lax.rsqrt(variance + norm_eps)
    scaled = centered * inverse
    return (scaled * norm_gain + norm_shift, scaled, inverse)


def normalize_back(incoming, scaled, inverse, norm_gain):
    grad_gain = jnp.sum(incoming * scaled, axis=0)
    grad_shift = jnp.sum(incoming, axis=0)
    weighted = incoming * norm_gain
    grad_input = inverse * (
        weighted
        - jnp.mean(weighted, axis=-1, keepdims=True)
        - scaled * jnp.mean(weighted * scaled, axis=-1, keepdims=True)
    )
    return (grad_input, grad_gain, grad_shift)


def heads_of(values):
    return values.reshape(values.shape[0], values.shape[1] // HEAD, HEAD)


def attend_forward(query_block, key_heads, value_heads, allowed):
    query_heads = heads_of(query_block)
    scores = (
        jnp.einsum("qhd,khd->hqk", query_heads, key_heads, preferred_element_type=jnp.float32)
        * score_scale
    )
    scores = jnp.where(allowed[None], scores, masked_score)
    largest = jnp.max(scores, axis=-1, keepdims=True)
    exp_scores = jnp.exp(scores - largest)
    totals = jnp.sum(exp_scores, axis=-1, keepdims=True)
    soft_weights = (exp_scores / totals).astype(jnp.bfloat16)
    mixed_heads = jnp.einsum(
        "hqk,khd->qhd", soft_weights, value_heads, preferred_element_type=jnp.float32
    )
    mixed_flat = mixed_heads.reshape(query_block.shape[0], query_block.shape[1]).astype(
        jnp.bfloat16
    )
    return (mixed_flat, largest[..., 0] + jnp.log(totals[..., 0]))


def attend_backward(query_block, key_heads, value_heads, allowed, grad_block, logsum_block):
    query_heads = heads_of(query_block)
    grad_heads = heads_of(grad_block)
    scores = (
        jnp.einsum("qhd,khd->hqk", query_heads, key_heads, preferred_element_type=jnp.float32)
        * score_scale
    )
    scores = jnp.where(allowed[None], scores, masked_score)
    soft_weights = jnp.exp(scores - logsum_block[..., None])
    grad_weights = jnp.einsum(
        "qhd,khd->hqk", grad_heads, value_heads, preferred_element_type=jnp.float32
    )
    inner_sum = jnp.sum(soft_weights * grad_weights, axis=-1, keepdims=True)
    grad_scores = (soft_weights * (grad_weights - inner_sum)).astype(jnp.bfloat16)
    grad_query = (
        jnp.einsum("hqk,khd->qhd", grad_scores, key_heads, preferred_element_type=jnp.float32)
        * score_scale
    )
    grad_key = (
        jnp.einsum("hqk,qhd->khd", grad_scores, query_heads, preferred_element_type=jnp.float32)
        * score_scale
    )
    grad_value = jnp.einsum(
        "hqk,qhd->khd",
        soft_weights.astype(jnp.bfloat16),
        grad_heads,
        preferred_element_type=jnp.float32,
    )
    return (
        grad_query.reshape(query_block.shape),
        grad_key.reshape(grad_key.shape[0], -1),
        grad_value.reshape(grad_value.shape[0], -1),
    )


def swap_sum(partial):
    low = partial.astype(jnp.bfloat16)
    if lax.axis_size("tensor") == 2:
        other = lax.ppermute(low, "tensor", [(0, 1), (1, 0)])
        return low.astype(jnp.float32) + other.astype(jnp.float32)
    return lax.psum(low, "tensor").astype(jnp.float32)


def pairs(mask):
    return [(i, i ^ mask) for i in range(16)]


def own_share(vectors):
    share = vectors.shape[1] // (lax.axis_size("dp") * lax.axis_size("tensor"))
    index = lax.axis_index("dp") * lax.axis_size("tensor") + lax.axis_index("tensor")
    return lax.dynamic_slice_in_dim(vectors, index * share, share, 1)


def generic_sum(rows_side, column_side):
    return lax.psum_scatter(
        product_over_rows(rows_side, column_side).astype(jnp.bfloat16),
        "dp",
        scatter_dimension=0,
        tiled=True,
    ).astype(jnp.float32)


def add_low(*terms):
    total = terms[0].astype(jnp.float32)
    for term in terms[1:]:
        total = total + term.astype(jnp.float32)
    return total


def ff_parts(gate, up, grad_mixed):
    sig = 0.5 * jnp.tanh(0.5 * gate) + 0.5
    act = gate * sig
    return (
        (act * up).astype(low),
        (grad_mixed * up * sig * (1.0 + gate * (1.0 - sig))).astype(low),
        (grad_mixed * act).astype(low),
    )


def turn(values, cos, lower, upper):
    width = values.shape[1]
    return (values * cos + pltpu.roll(values, width - 16, 1) * lower + pltpu.roll(values, 16, 1) * upper)

def turn_back(values, cos, lower, upper):
    width = values.shape[1]
    return (values * cos + pltpu.roll(values * lower, 16, 1) + pltpu.roll(values * upper, width - 16, 1))

def normed_rows(values, gain, shift):
    average = jnp.mean(values, axis=-1, keepdims=True)
    centered = values - average
    variance = jnp.mean(centered * centered, axis=-1, keepdims=True)
    return centered * lax.rsqrt(variance + norm_eps) * gain + shift

def over_rows(rows, body, chunk=32):
    @pl.loop(0, rows // chunk, unroll=min(4, rows // chunk))
    def _(i):
        body(pl.ds(pl.multiple_of(i * chunk, chunk), chunk))

def attend(q, k, v, mask, lse_ref):
    q_turned = (q * jnp.bfloat16(0.125)).T
    v_turned = v.T
    heads = [slice(h * HEAD, (h + 1) * HEAD) for h in range(q.shape[1] // HEAD)]
    scores = [product_plain(k[:, c], q_turned[c, :]) for c in heads]
    weights, scales = [], []
    for h, s in enumerate(scores):
        s = s + mask
        m = jnp.max(s, axis=0, keepdims=True)
        e = jnp.exp(s - m)
        total = jnp.sum(e, axis=0, keepdims=True)
        weights.append(e.astype(low))
        scales.append(1.0 / total)
        lse_ref[h : h + 1, :] = m + jnp.log(total)
    outs = [product_plain(v_turned[c, :], e) * x for c, e, x in zip(heads, weights, scales)]
    return jnp.concatenate(outs, axis=0).T.astype(low)


def attend_back(q, k, v, g, att, mask, lse):
    scaled = q * jnp.bfloat16(0.125)
    q_turned = scaled.T
    g_turned = g.T
    k_turned = k.T
    weighted = g_turned.astype(f32) * att.T.astype(f32)
    dq, dk, dv = [], [], []
    for h in range(q.shape[1] // HEAD):
        c = slice(h * HEAD, (h + 1) * HEAD)
        p = jnp.exp(product_plain(k[:, c], q_turned[c, :]) + (mask - lse[h : h + 1, :]))
        dp = product_plain(v[:, c], g_turned[c, :])
        inner = jnp.sum(weighted[c, :], axis=0, keepdims=True)
        ds = (p * (dp - inner)).astype(low)
        dq.append(product_plain(k_turned[c, :], ds))
        dk.append(product_plain(ds, scaled[:, c]))
        dv.append(product_plain(p.astype(low), g[:, c]))
    return (
        jnp.concatenate(dq, axis=0).T * 0.125,
        jnp.concatenate(dk, axis=1),
        jnp.concatenate(dv, axis=1),
    )


def self_mask(split, T):
    r=lax.broadcasted_iota(jnp.int32,(T,T),0)>=split
    c=lax.broadcasted_iota(jnp.int32,(T,T),1)>=split
    return jnp.where(r==c,0.0,masked_score).astype(f32)

def key_half(info, index, frames, keys):
    second = info[0] < frames
    start = jnp.where(second, keys // 2, 0) if index == 1 else 0
    live = jnp.where(second, info[2], info[1]) if index == 1 else info[1]
    return start, live


def half_mask(live, keys, frames):
    return jnp.where(
        lax.broadcasted_iota(jnp.int32, (keys, frames), 0) < live, 0.0, masked_score
    ).astype(f32)


def key_blocks(info, k_ref, v_ref, frames):
    keys = k_ref.shape[0]
    k, v, masks = [], [], []
    for index in range(2):
        start, live = key_half(info, index, frames, keys)
        here = pl.ds(start if index == 0 else pl.multiple_of(start, keys // 2), keys // 2)
        k.append(k_ref[here, :])
        v.append(v_ref[here, :])
        masks.append(half_mask(live, keys // 2, frames // 2))
    return k, v, jnp.concatenate(masks, axis=1)


def cross_attend(info, q, k_ref, v_ref, lse_ref):
    half = q.shape[0] // 2
    q_turned = (q * jnp.bfloat16(0.125)).T
    k, v, mask = key_blocks(info, k_ref, v_ref, 2 * half)
    v_turned = [values.T for values in v]
    outs = []
    for h in range(q.shape[1] // HEAD):
        c = slice(h * HEAD, (h + 1) * HEAD)
        s = [product_plain(k[i][:, c], q_turned[c, i * half : (i + 1) * half]) for i in range(2)]
        s = jnp.concatenate(s, axis=1) + mask
        m = jnp.max(s, axis=0, keepdims=True)
        e = jnp.exp(s - m)
        total = jnp.sum(e, axis=0, keepdims=True)
        lse_ref[h : h + 1, :] = m + jnp.log(total)
        e = e.astype(low)
        o = [product_plain(v_turned[i][c, :], e[:, i * half : (i + 1) * half]) for i in range(2)]
        outs.append(jnp.concatenate(o, axis=1) * (1.0 / total))
    return jnp.concatenate(outs, axis=0).T.astype(low)


def cross_attend_back(info, q, k_ref, v_ref, g, att, lse):
    half = q.shape[0] // 2
    scaled = q * jnp.bfloat16(0.125)
    q_turned = scaled.T
    g_turned = g.T
    weighted = g_turned.astype(f32) * att.T.astype(f32)
    k, v, mask = key_blocks(info, k_ref, v_ref, 2 * half)
    k_turned = [values.T for values in k]
    parts = [slice(0, half), slice(half, 2 * half)]
    dq, dk, dv = [], [[], []], [[], []]
    for h in range(q.shape[1] // HEAD):
        c = slice(h * HEAD, (h + 1) * HEAD)
        s = [product_plain(k[i][:, c], q_turned[c, parts[i]]) for i in range(2)]
        dp = [product_plain(v[i][:, c], g_turned[c, parts[i]]) for i in range(2)]
        p = jnp.exp(jnp.concatenate(s, axis=1) + (mask - lse[h : h + 1, :]))
        inner = jnp.sum(weighted[c, :], axis=0, keepdims=True)
        ds = (p * (jnp.concatenate(dp, axis=1) - inner)).astype(low)
        p = p.astype(low)
        dq.append(
            jnp.concatenate(
                [product_plain(k_turned[i][c, :], ds[:, parts[i]]) for i in range(2)], axis=1
            )
        )
        for i in range(2):
            dk[i].append(product_plain(ds[:, parts[i]], scaled[parts[i], c]))
            dv[i].append(product_plain(p[:, parts[i]], g[parts[i], c]))
    second = (info[0] < 2 * half).astype(f32)

    def by_row(halves):
        first, last = (jnp.concatenate(half, axis=1) for half in halves)
        return jnp.concatenate([first + last * (1.0 - second), last * second], axis=0)

    return jnp.concatenate(dq, axis=0).T * 0.125, by_row(dk), by_row(dv)


def norm_back_rows(x,e,gain,above,gain_acc,shift_acc):
    average=jnp.mean(x,axis=-1,keepdims=True)
    centered=x-average
    variance=jnp.mean(centered*centered,axis=-1,keepdims=True)
    inverse=lax.rsqrt(variance+norm_eps)
    n=centered*inverse
    en=e*n
    w=e*gain
    mean_w=jnp.mean(w,axis=-1,keepdims=True)
    mean_wn=jnp.mean(en*gain,axis=-1,keepdims=True)
    fold=lambda t: jnp.sum(t.reshape(t.shape[0]//8,8,t.shape[1]),axis=0)
    gain_acc[...]+=fold(en)
    shift_acc[...]+=fold(e)
    return above+inverse*(w-mean_w-n*mean_wn)

def norm_back_step(x, mine, other, above, gain, total, total_low, kept, vectors, gain_acc, shift_acc):
    step, block = pl.program_id(0), x.shape[0]

    @pl.when(step == 0)
    def _():
        gain_acc[...] = jnp.zeros_like(gain_acc)
        shift_acc[...] = jnp.zeros_like(shift_acc)

    @pl.when(step < BLOCKS)
    def _():
        def rows(r):
            e = mine[r, :].astype(f32) + other[r, :].astype(f32)
            t = norm_back_rows(x[r, :], e, gain[...], above[r, :], gain_acc, shift_acc)
            total[r, :] = t
            total_low[r, :] = t.astype(low)
            kept[within(step, block, r), :] = t.astype(low)

        over_rows(block, rows)

    @pl.when(step == BLOCKS - 1)
    def _():
        vectors[0:1, :] = jnp.sum(gain_acc[...], axis=0, keepdims=True)
        vectors[1:2, :] = jnp.sum(shift_acc[...], axis=0, keepdims=True)


def ordered(kernel, token, args, in_specs, out_specs, out_shape, grid, flops, scratch=(), info=None, brief=False):
    if info is None:
        info = jnp.zeros((1,), jnp.int32)
    inputs, outputs = len(args), len(out_shape)

    def body(info_ref, *refs):
        token_ref = refs[inputs + 1 + outputs]

        @pl.when(functools.reduce(jnp.logical_and, [pl.program_id(i) == 0 for i in range(len(grid))]))
        def _():
            token_ref[...] = jnp.zeros_like(token_ref)

        kernel(
            info_ref,
            *refs[:inputs],
            *refs[inputs + 1 : inputs + 1 + outputs],
            *refs[inputs + 2 + outputs :],
        )

    moved = sum(math.prod(a.shape) * a.dtype.itemsize for a in (*args, *out_shape))
    *results, token = pl.pallas_call(
        body,
        grid_spec=pltpu.PrefetchScalarGridSpec(
            num_scalar_prefetch=1,
            grid=grid,
            in_specs=[*in_specs, pl.BlockSpec(memory_space=pl.ANY)],
            out_specs=[*out_specs, pl.BlockSpec((8, 128), lambda *_: (0, 0))],
            scratch_shapes=list(scratch),
        ),
        out_shape=[*out_shape, sds((8, 128), f32)],
        compiler_params=pltpu.CompilerParams(vmem_limit_bytes=VMEM_LIMIT),
        cost_estimate=pl.CostEstimate(flops=0 if brief else max(FLOOR, int(flops * COST)), bytes_accessed=0 if brief else int(moved * COST), transcendentals=0),
    )(info, *args, token)
    return (*results, token)


def hold(token, values, brief=False):
    def nothing(values_ref, token_ref, out_ref, token_out):
        token_out[...] = jnp.zeros_like(token_out)

    return pl.pallas_call(
        nothing,
        in_specs=[pl.BlockSpec(memory_space=pl.ANY)] * 2,
        out_specs=[pl.BlockSpec(memory_space=pl.ANY), pl.BlockSpec(memory_space=pltpu.VMEM)],
        out_shape=[sds(values.shape, values.dtype), sds((8, 128), f32)],
        input_output_aliases={0: 0},
        compiler_params=pltpu.CompilerParams(vmem_limit_bytes=VMEM_LIMIT),
        cost_estimate=pl.CostEstimate(flops=0 if brief else FLOOR, bytes_accessed=0, transcendentals=0),
    )(values, token)


def specs(frames, width, tile, blocks=0):
    def tile_of(j):
        return jnp.maximum(j - blocks, 0) if blocks else j

    whole = pl.BlockSpec((frames, width), lambda j, *_: (0, 0))
    vector = pl.BlockSpec((1, width), lambda j, *_: (0, 0))
    column = pl.BlockSpec((width, tile), lambda j, *_: (0, tile_of(j)))
    row = pl.BlockSpec((tile, width), lambda j, *_: (tile_of(j), 0))
    act = pl.BlockSpec((frames, tile), lambda j, *_: (0, tile_of(j)))
    table = pl.BlockSpec((frames, tile), lambda j, *_: (0, 0))
    logsum = pl.BlockSpec((8, frames), lambda j, *_: (tile_of(j), 0))
    return whole, vector, column, row, act, table, logsum


BLOCKS = 4


def row_block(frames, width):
    return pl.BlockSpec((frames // BLOCKS, width), lambda j, *_: (jnp.minimum(j, BLOCKS - 1), 0))


def copies_block(frames, width, place):
    return pl.BlockSpec(
        (PLANE, frames // BLOCKS, width),
        lambda j, info: (0, jnp.clip(j - BLOCKS // 2 * info[place], 0, BLOCKS // 2 - 1), 0),
    )


def within(step, rows, r):
    return pl.ds(pl.multiple_of(step * rows + r.start, r.size), r.size)


def added(acc, term, result, first=0):
    step = pl.program_id(0)

    @pl.when(step == first)
    def _():
        acc[...] = term

    @pl.when(step != first)
    def _():
        acc[...] += term

    @pl.when(step == pl.num_programs(0) - 1)
    def _():
        result[...] = acc[...].astype(result.dtype)


def self_kernel(info, hid, gain, shift, wq, wk, wv, wo, cos, lower, upper, grad, copies, grad_copies, q, k, v, att, logsum, part, acc, mask, normed):
    step, frames, block = pl.program_id(0), normed.shape[0], hid.shape[0]

    @pl.when(step == 0)
    def _():
        mask[...] = self_mask(info[0], frames)

    @pl.when(step < BLOCKS)
    def _():
        def rows(r):
            normed[within(step, block, r), :] = normed_rows(hid[r, :], gain[...], shift[...]).astype(low)

        over_rows(block, rows)

    @pl.when((step < BLOCKS) & (step * 2 // BLOCKS == info[3]))
    def _():
        mine = normed[pl.ds(pl.multiple_of(step * block, block), block), :]
        for chip in range(PLANE):
            copies[chip] = mine

    @pl.when(step < BLOCKS // 2)
    def _():
        grad_low = grad[...].astype(low)
        for chip in range(PLANE):
            grad_copies[chip] = grad_low

    @pl.when(step >= BLOCKS)
    def _():
        n = normed[...]
        tables = (cos[...], lower[...], upper[...])
        q[...] = turn(product_plain(n, wq[...]), *tables).astype(low)
        k[...] = turn(product_plain(n, wk[...]), *tables).astype(low)
        v[...] = product_plain(n, wv[...]).astype(low)
        attended = attend(q[...], k[...], v[...], mask[...], logsum)
        att[...] = attended
        added(acc, product_plain(attended, wo[...]), part, BLOCKS)


def self_forward(token, info, hid, gain, shift, wq, wk, wv, wo, tables, grad, tile=4 * HEAD):
    frames, width = hid.shape
    columns = wq.shape[1]
    whole, vector, column, row, act, table, logsum = specs(frames, width, tile, BLOCKS)
    blocks = row_block(frames, width)
    here = frames // BLOCKS
    return ordered(
        self_kernel,
        token,
        (hid, gain, shift, wq, wk, wv, wo, *tables, grad),
        [blocks, vector, vector, column, column, column, row, table, table, table]
        + [
            pl.BlockSpec(
                (here, width),
                lambda j, info: (BLOCKS // 2 * info[3] + jnp.minimum(j, BLOCKS // 2 - 1), 0),
            )
        ],
        [
            copies_block(frames, width, 3),
            pl.BlockSpec((PLANE, here, width), lambda j, info: (0, jnp.minimum(j, BLOCKS // 2 - 1), 0)),
        ]
        + [act, act, act, act, logsum, whole],
        [sds((PLANE, frames // 2, width), low)] * 2
        + [sds((frames, columns), low)] * 4
        + [sds((columns // tile * 8, frames), f32), sds((frames, width), low)],
        (BLOCKS + columns // tile,),
        2 * frames * columns * (4 * width + 8 * frames),
        [
            pltpu.VMEM((frames, width), f32),
            pltpu.VMEM((frames, frames), f32),
            pltpu.VMEM((frames, width), low),
        ],
        info,
    )


def cross_kernel(info, hid, mine, other, gain, shift, cq, ck, cv, co, total, normed, q, att, logsum, part, acc, kept):
    step, block = pl.program_id(0), hid.shape[0]

    @pl.when(step < BLOCKS)
    def _():
        def rows(r):
            x = hid[r, :] + (mine[r, :].astype(f32) + other[r, :].astype(f32))
            total[r, :] = x
            n = normed_rows(x, gain[...], shift[...]).astype(low)
            normed[r, :] = n
            kept[within(step, block, r), :] = n

        over_rows(block, rows)

    @pl.when(step >= BLOCKS)
    def _():
        q[...] = product_plain(kept[...], cq[...]).astype(low)
        attended = cross_attend(info, q[...], ck, cv, logsum)
        att[...] = attended
        added(acc, product_plain(attended, co[...]), part, BLOCKS)


def cross_forward(token, info, hid, mine, other, gain, shift, cq, ck, cv, co, tile=4 * HEAD):
    frames, width = hid.shape
    columns, keys = cq.shape[1], ck.shape[0]
    whole, vector, column, row, act, table, logsum = specs(frames, width, tile, BLOCKS)
    key = pl.BlockSpec((keys, tile), lambda j, *_: (0, jnp.maximum(j - BLOCKS, 0)))
    blocks = row_block(frames, width)
    return ordered(
        cross_kernel,
        token,
        (hid, mine, other, gain, shift, cq, ck, cv, co),
        [blocks, blocks, blocks, vector, vector, column, key, key, row],
        [blocks, blocks, act, act, logsum, whole],
        [
            sds((frames, width), f32),
            sds((frames, width), low),
            sds((frames, columns), low),
            sds((frames, columns), low),
            sds((columns // tile * 8, frames), f32),
            sds((frames, width), low),
        ],
        (BLOCKS + columns // tile,),
        2 * frames * columns * (2 * width + 8 * keys),
        [pltpu.VMEM((frames, width), f32), pltpu.VMEM((frames, width), low)],
        info,
        brief=True,
    )


def norm_kernel(info, hid, mine, other, gain, shift, total, normed, copies):
    def rows(r):
        x = hid[r, :] + (mine[r, :].astype(f32) + other[r, :].astype(f32))
        total[r, :] = x
        normed[r, :] = normed_rows(x, gain[...], shift[...]).astype(low)

    over_rows(hid.shape[0], rows)

    @pl.when(pl.program_id(0) * 2 // pl.num_programs(0) == info[0])
    def _():
        values = normed[...]
        for chip in range(PLANE):
            copies[chip] = values


def norm_forward(token, hid, mine, other, gain, shift, half, block=128):
    frames, width = hid.shape
    blocks = frames // (2 * block)
    rows = pl.BlockSpec((block, width), lambda j, *_: (j, 0))
    vector = pl.BlockSpec((1, width), lambda j, *_: (0, 0))
    return ordered(
        norm_kernel,
        token,
        (hid, mine, other, gain, shift),
        [rows, rows, rows, vector, vector],
        [
            rows,
            rows,
            pl.BlockSpec(
                (PLANE, block, width),
                lambda j, info: (0, jnp.clip(j - blocks * info[0], 0, blocks - 1), 0),
            ),
        ],
        [sds((frames, width), f32), sds((frames, width), low), sds((PLANE, frames // 2, width), low)],
        (frames // block,),
        10 * frames * width,
        info=half,
        brief=True,
    )


def cross_back_kernel(info, x, mine, other, above, gain, co, q, ck, cv, att, logsum, cq, total, total_low, vectors, dq, dk, dv, part, acc, gain_acc, shift_acc, kept):
    norm_back_step(x, mine, other, above, gain, total, total_low, kept, vectors, gain_acc, shift_acc)

    @pl.when(pl.program_id(0) >= BLOCKS)
    def _():
        g = product_with_rows(kept[...], co[...]).astype(low)
        a, b, c = cross_attend_back(info, q[...], ck, cv, g, att[...], logsum[...])
        a = a.astype(low)
        dq[...] = a
        dk[...] = b.astype(low)
        dv[...] = c.astype(low)
        added(acc, product_with_rows(a, cq[...]), part, BLOCKS)


def cross_backward(token, info, x, mine, other, above, gain, co, q, ck, cv, att, logsums, cq, tile=4 * HEAD):
    frames, width = x.shape
    columns, keys = cq.shape[1], ck.shape[0]
    whole, vector, column, row, act, table, logsum = specs(frames, width, tile, BLOCKS)
    key = pl.BlockSpec((keys, tile), lambda j, *_: (0, jnp.maximum(j - BLOCKS, 0)))
    blocks = row_block(frames, width)
    two = pl.BlockSpec((2, width), lambda j, *_: (0, 0))
    return ordered(
        cross_back_kernel,
        token,
        (x, mine, other, above, gain, co, q, ck, cv, att, logsums, cq),
        [blocks, blocks, blocks, blocks, vector, row, act, key, key, act, logsum, column],
        [blocks, blocks, two, act, key, key, whole],
        [
            sds((frames, width), f32),
            sds((frames, width), low),
            sds((2, width), f32),
            sds((frames, columns), low),
            sds((keys, columns), low),
            sds((keys, columns), low),
            sds((frames, width), low),
        ],
        (BLOCKS + columns // tile,),
        2 * frames * columns * (2 * width + 20 * keys),
        [
            pltpu.VMEM((frames, width), f32),
            pltpu.VMEM((8, width), f32),
            pltpu.VMEM((8, width), f32),
            pltpu.VMEM((frames, width), low),
        ],
        info,
    )


def self_back_kernel(info, x, mine, other, above, gain, wo, q, k, v, att, logsum, wq, wk, wv, cos, lower, upper, total, total_low, vectors, grads, part, acc, mask, gain_acc, shift_acc, kept):
    step = pl.program_id(0)

    @pl.when(step == 0)
    def _():
        mask[...] = self_mask(info[0], kept.shape[0])

    norm_back_step(x, mine, other, above, gain, total, total_low, kept, vectors, gain_acc, shift_acc)

    @pl.when(step >= BLOCKS)
    def _():
        g = product_with_rows(kept[...], wo[...]).astype(low)
        a, b, c = attend_back(q[...], k[...], v[...], g, att[...], mask[...], logsum[...])
        tables = (cos[...], lower[...], upper[...])
        a = turn_back(a, *tables).astype(low)
        b = turn_back(b, *tables).astype(low)
        c = c.astype(low)
        for index, values in enumerate((a, b, c)):
            turned = values.T
            for quarter in range(PLANE):
                grads[quarter, index] = turned[quarter * HEAD : (quarter + 1) * HEAD]
        back = product_with_rows(a, wq[...]) + product_with_rows(b, wk[...])
        added(acc, back + product_with_rows(c, wv[...]), part, BLOCKS)


def self_backward(token, info, x, mine, other, above, gain, wo, q, k, v, att, logsums, wq, wk, wv, tables, tile=4 * HEAD):
    frames, width = x.shape
    columns = wq.shape[1]
    whole, vector, column, row, act, table, logsum = specs(frames, width, tile, BLOCKS)
    blocks = row_block(frames, width)
    two = pl.BlockSpec((2, width), lambda j, *_: (0, 0))
    heads = pl.BlockSpec(
        (PLANE, 3, HEAD, frames), lambda j, *_: (0, 0, jnp.maximum(j - BLOCKS, 0), 0)
    )
    return ordered(
        self_back_kernel,
        token,
        (x, mine, other, above, gain, wo, q, k, v, att, logsums, wq, wk, wv, *tables),
        [blocks] * 4
        + [vector, row, act, act, act, act, logsum, column, column, column, table, table, table],
        [blocks, blocks, two, heads, whole],
        [
            sds((frames, width), f32),
            sds((frames, width), low),
            sds((2, width), f32),
            sds((PLANE, 3, columns // PLANE, frames), low),
            sds((frames, width), low),
        ],
        (BLOCKS + columns // tile,),
        2 * frames * columns * (4 * width + 20 * frames),
        [
            pltpu.VMEM((frames, width), f32),
            pltpu.VMEM((frames, frames), f32),
            pltpu.VMEM((8, width), f32),
            pltpu.VMEM((8, width), f32),
            pltpu.VMEM((frames, width), low),
        ],
        info,
    )


def last_kernel(_, x, mine, other, above, gain, resid, sum_mine, sum_other, total, vectors, result, gain_acc, shift_acc):
    step = pl.program_id(0)

    @pl.when(step == 0)
    def _():
        gain_acc[...] = jnp.zeros_like(gain_acc)
        shift_acc[...] = jnp.zeros_like(shift_acc)

    def rows(r):
        e = mine[r, :].astype(f32) + other[r, :].astype(f32)
        total[r, :] = norm_back_rows(x[r, :], e, gain[...], above[r, :], gain_acc, shift_acc)
        result[r, :] = resid[r, :] + (sum_mine[r, :].astype(f32) + sum_other[r, :].astype(f32))

    over_rows(x.shape[0], rows)

    @pl.when(step == pl.num_programs(0) - 1)
    def _():
        vectors[0:1, :] = jnp.sum(gain_acc[...], axis=0, keepdims=True)
        vectors[1:2, :] = jnp.sum(shift_acc[...], axis=0, keepdims=True)


def last_backward(token, x, mine, other, above, gain, resid, sum_mine, sum_other, block=128):
    frames, width = x.shape
    rows = pl.BlockSpec((block, width), lambda j, *_: (j, 0))
    vector = pl.BlockSpec((1, width), lambda j, *_: (0, 0))
    two = pl.BlockSpec((2, width), lambda j, *_: (0, 0))
    return ordered(
        last_kernel,
        token,
        (x, mine, other, above, gain, resid, sum_mine, sum_other),
        [rows, rows, rows, rows, vector, rows, rows, rows],
        [rows, two, rows],
        [sds((frames, width), f32), sds((2, width), f32), sds((frames, width), f32)],
        (frames // block,),
        20 * frames * width,
        [pltpu.VMEM((8, width), f32), pltpu.VMEM((8, width), f32)],
        brief=True,
    )


def pack_kernel(_, *refs):
    for values, copies in zip(refs[: len(refs) // 2], refs[len(refs) // 2 :]):
        copies[...] = values[...].astype(low)


def packed(token, values, half, pieces=1):
    frames, width = values.shape
    rows = frames // (2 * pieces)

    def source(piece):
        return pl.BlockSpec((rows, width), lambda j, info: (info[0] * pieces + piece, 0))

    return ordered(
        pack_kernel,
        token,
        (values,) * pieces,
        [source(piece) for piece in range(pieces)],
        [pl.BlockSpec((rows, width), lambda j, info: (j, 0))] * pieces,
        [sds((PLANE * rows, width), low)] * pieces,
        (PLANE,),
        0,
        info=half,
        brief=True,
    )


def ff_kernel(_, in_ref, out_ref, gate_ref, up_ref, down_ref, sum_ref, back_ref, sum_acc, back_acc, out_low):
    @pl.when(pl.program_id(0) == 0)
    def _():
        out_low[...] = out_ref[...].astype(low)

    normed = in_ref[...]
    mixed, grad_gate, grad_up = ff_parts(
        product_plain(normed, gate_ref[...]),
        product_plain(normed, up_ref[...]),
        product_with_rows(out_low[...], down_ref[...]),
    )
    added(sum_acc, product_plain(mixed, down_ref[...]), sum_ref)
    added(
        back_acc,
        product_with_rows(grad_gate, gate_ref[...]) + product_with_rows(grad_up, up_ref[...]),
        back_ref,
    )


def ff_both(token, normed, grad_out, w_gate, w_up, w_down, tile=768):
    frames, width = normed.shape
    units = w_gate.shape[1]
    whole, _, column, row, *_ = specs(frames, width, tile)
    return ordered(
        ff_kernel,
        token,
        (normed, grad_out, w_gate, w_up, w_down),
        [whole, whole, column, column, row],
        [whole, whole],
        [sds((frames, width), low)] * 2,
        (units // tile,),
        12 * frames * width * units,
        [pltpu.VMEM((frames, width), f32)] * 2 + [pltpu.VMEM((frames, width), low)],
    )


def share_kernel(info, in_mine, in_other, out_mine, out_other, gate_ref, up_ref, down_ref, send_ref, keep_ref, acc):
    step = pl.program_id(1)
    normed = jnp.concatenate([in_mine[...], in_other[...]], axis=0)
    grad_out = jnp.concatenate([out_mine[...], out_other[...]], axis=0)
    mixed, grad_gate, grad_up = ff_parts(
        product_plain(normed, gate_ref[...]),
        product_plain(normed, up_ref[...]),
        product_with_rows(grad_out, down_ref[...]),
    )
    fresh = (
        product_over_rows(grad_out, mixed),
        product_over_rows(normed, grad_gate),
        product_over_rows(normed, grad_up),
    )
    for index, term in enumerate(fresh):

        @pl.when(step == 0)
        def _():
            acc[index] = term

        @pl.when(step != 0)
        def _():
            acc[index] += term

    @pl.when(step == pl.num_programs(1) - 1)
    def _():
        rows = send_ref.shape[2] // 3
        for pair in range(2):
            for index in range(3):
                for ref, parity in ((send_ref, 1 - info[1]), (keep_ref, info[1])):
                    start = pl.multiple_of((2 * pair + parity) * rows, rows)
                    ref[0, pair, index * rows : (index + 1) * rows] = acc[
                        index, pl.ds(start, rows), :
                    ].astype(ref.dtype)


def ff_share(token, info, normed, grad_out, w_gate, w_up, w_down, tile, count):
    frames, width = normed[0].shape
    chunk = frames // PLANE
    rows = pl.BlockSpec((chunk, width), lambda i, j, info: (j, 0))
    column = pl.BlockSpec((width, tile), lambda i, j, info: (0, info[0] + i))
    half = (LEVELS // 2, 3 * width // LEVELS, tile)
    return ordered(
        share_kernel,
        token,
        (*normed, *grad_out, w_gate, w_up, w_down),
        [rows] * 4
        + [column, column, pl.BlockSpec((tile, width), lambda i, j, info: (info[0] + i, 0))],
        [pl.BlockSpec((1, *half), lambda i, j, info: (i, 0, 0, 0))] * 2,
        [sds((count, *half), low)] * 2,
        (count, PLANE),
        24 * frames * width * tile * count,
        [pltpu.VMEM((3, width, tile), f32)],
        info,
    )


def weight_kernel(plan, sides_count, _, *refs):
    sides, columns = refs[:sides_count], refs[sides_count : sides_count + len(plan)]
    out = refs[sides_count + len(plan)]
    turned = refs[sides_count + len(plan) + 1 :]

    @pl.when(pl.program_id(0) == 0)
    def _():
        for side, ref in zip(sides, turned):
            ref[...] = side[...].T

    for (which, first), column in zip(plan, columns):
        product = product_plain(turned[which][...], column[...]).astype(low)
        rows = product.shape[0] // (PLANE * LEVELS)
        product = product.reshape(LEVELS, PLANE, rows, product.shape[1])
        for owner in range(PLANE):
            out[owner, :, first : first + rows, :] = product[:, owner]


def weight_products(token, sides, plan, columns, tile=256):
    width = columns[0].shape[1]
    rows = sum(sides[which].shape[1] for which, _ in plan) // (PLANE * LEVELS)
    return ordered(
        functools.partial(weight_kernel, plan, len(sides)),
        token,
        (*sides, *columns),
        [pl.BlockSpec(side.shape, lambda j, *_: (0, 0)) for side in sides]
        + [pl.BlockSpec((column.shape[0], tile), lambda j, *_: (0, j)) for column in columns],
        [pl.BlockSpec((PLANE, LEVELS, rows, tile), lambda j, *_: (0, 0, 0, j))],
        [sds((PLANE, LEVELS, rows, width), low)],
        (width // tile,),
        sum(2 * sides[w].shape[0] * sides[w].shape[1] * width for w, _ in plan),
        [pltpu.VMEM((side.shape[1], side.shape[0]), low) for side in sides],
        brief=len(sides) == 1,
    )


def plane_sum_kernel(info, got, send, keep):
    for ref, parity in ((send, 1 - info[0]), (keep, info[0])):
        total = got[0, 0, parity].astype(f32)
        for source in range(1, PLANE):
            total = total + got[source, 0, parity].astype(f32)
        ref[0] = total.astype(low)


def plane_sum(token, got, parity):
    rows, width = got.shape[2:]
    out = pl.BlockSpec((1, rows, width), lambda j, *_: (j, 0, 0))
    return ordered(
        plane_sum_kernel,
        token,
        (got.reshape(PLANE, 2, 2, rows, width),),
        [pl.BlockSpec((PLANE, 1, 2, rows, width), lambda j, *_: (0, j, 0, 0, 0))],
        [out, out],
        [sds((2, rows, width), low)] * 2,
        (2,),
        0,
        info=parity,
    )


def level_sum_kernel(_, keep_pass, got_pass, keep_own, got_own, passed, own):
    passed[...] = (keep_pass[0, 0].astype(f32) + got_pass[0, 0].astype(f32)).astype(low)
    own[...] = keep_own[0, 0].astype(f32) + got_own[0, 0].astype(f32)


def level_sum(token, keep, got, upper):
    count, _, rows, width = keep.shape
    block = rows // 2 if rows % 32 == 0 else rows
    steps = rows // block
    off = pl.BlockSpec((1, 1, block, width), lambda i, j, info: (i, 1 - info[0], j, 0))
    own = pl.BlockSpec((1, 1, block, width), lambda i, j, info: (i, info[0], j, 0))
    out = pl.BlockSpec((block, width), lambda i, j, info: (i * steps + j, 0))
    return ordered(
        level_sum_kernel,
        token,
        (keep, got, keep, got),
        [off, off, own, own],
        [out, out],
        [sds((count * rows, width), low), sds((count * rows, width), f32)],
        (count, steps),
        0,
        info=upper,
    )


def unit_pack_kernel(counts, _, *refs):
    owns, lasts, out = refs[:-1:2], refs[1:-1:2], refs[-1]
    step = pl.program_id(0)
    for own, last, (first, count) in zip(owns, lasts, counts):

        @pl.when((step >= first) & (step < first + count))
        def _():
            total = (own[...] + last[...].astype(f32)).astype(low)
            total = total.reshape(3, PLANE, out.shape[2], out.shape[3])
            for chip in range(PLANE):
                out[chip] = total[:, chip]


def unit_pack(token, sums, rows):
    tile = sums[0][0].shape[1]
    r = rows // (3 * PLANE)
    specs_in, counts, first = [], [], 0
    for own, _ in sums:
        count = own.shape[0] // rows

        def place(j, info, first=first, count=count):
            return (jnp.clip(j - first, 0, count - 1), 0)

        specs_in += [pl.BlockSpec((rows, tile), place)] * 2
        counts.append((first, count))
        first += count
    return ordered(
        functools.partial(unit_pack_kernel, counts),
        token,
        tuple(array for pair in sums for array in pair),
        specs_in,
        [pl.BlockSpec((PLANE, 3, r, tile), lambda j, *_: (0, 0, 0, j))],
        [sds((PLANE, 3, r, tile * first), low)],
        (first,),
        0,
    )


def unit_unpack_kernel(_, got, down, gate, up):
    down[...] = got[0, 0].astype(f32).T
    gate[...] = got[0, 1].astype(f32)
    up[...] = got[0, 2].astype(f32)


def unit_unpack(token, got):
    _, _, r, units = got.shape
    across = pl.BlockSpec((r, units), lambda j, *_: (0, j))
    return ordered(
        unit_unpack_kernel,
        token,
        (got,),
        [pl.BlockSpec((1, 3, r, units), lambda j, *_: (j, 0, 0, 0))],
        [pl.BlockSpec((units, r), lambda j, *_: (j, 0)), across, across],
        [sds((PLANE * units, r), f32)] + [sds((r, PLANE * units), f32)] * 2,
        (PLANE,),
        0,
    )


def head_pack_kernel(_, own, last, out):
    total = (own[...] + last[...].astype(f32)).T.astype(low)
    out[...] = total.reshape(out.shape)


def head_pack(token, own, last):
    features, columns = own.shape
    shape = (PLANE, columns // PLANE, features)
    return ordered(
        head_pack_kernel,
        token,
        (own, last),
        [pl.BlockSpec(own.shape, lambda j, *_: (0, 0))] * 2,
        [pl.BlockSpec(shape, lambda j, *_: (0, 0, 0))],
        [sds(shape, low)],
        (1,),
        0,
    )


def head_unpack_kernel(_, got, *outs):
    groups = got.shape[2] // (3 * HEAD)
    for index, out in enumerate(outs):
        pieces = []
        for group in range(groups):
            first = (index * groups + group) * HEAD
            pieces += [got[chip, :, first : first + HEAD] for chip in range(PLANE)]
        out[...] = jnp.concatenate(pieces, axis=1).astype(f32)


def head_unpack(token, got):
    chips, r, features = got.shape
    shape = (r, chips * features // 3)
    return ordered(
        head_unpack_kernel,
        token,
        (got,),
        [pl.BlockSpec(got.shape, lambda j, *_: (0, 0, 0))],
        [pl.BlockSpec(shape, lambda j, *_: (0, 0))] * 3,
        [sds(shape, f32)] * 3,
        (1,),
        0,
    )


def head_kernel(info, grads_mine, grads_other, in_mine, in_other, send, keep, acc):
    step = pl.program_id(0)
    rows = acc.shape[0]
    term = product_plain(grads_mine[0].reshape(rows, -1), in_mine[...]) + product_plain(
        grads_other[0].reshape(rows, -1), in_other[...]
    )

    @pl.when(step == 0)
    def _():
        acc[...] = term

    @pl.when(step != 0)
    def _():
        acc[...] += term

    @pl.when(step == pl.num_programs(0) - 1)
    def _():
        width = send.shape[2]
        for level in range(LEVELS):
            for ref, parity in ((send, 1 - info[1]), (keep, info[1])):

                @pl.when(parity == level % 2)
                def _():
                    ref[level // 2] = acc[:, level * width : (level + 1) * width].astype(low)


def head_products(token, info, grads, normed):
    _, three, features, frames = grads.shape
    width = normed[0].shape[1]
    chunk = normed[0].shape[0] // PLANE
    rows = pl.BlockSpec((chunk, width), lambda j, info: (j, 0))
    half = (LEVELS // 2, three * features, width // LEVELS)
    return ordered(
        head_kernel,
        token,
        (grads, grads, *normed),
        [
            pl.BlockSpec((1, three, features, chunk), lambda j, info: (j, 0, 0, info[0])),
            pl.BlockSpec((1, three, features, chunk), lambda j, info: (j, 0, 0, 1 - info[0])),
            rows,
            rows,
        ],
        [pl.BlockSpec(half, lambda j, info: (0, 0, 0))] * 2,
        [sds(half, low)] * 2,
        (PLANE,),
        2 * three * features * PLANE * frames * width,
        [pltpu.VMEM((three * features, width), f32)],
        info,
    )


def on_plane(
    hidden_in,
    out_grad,
    prompt_states,
    row_split,
    prompt_len,
    gain_attn,
    bias_attn,
    gain_cross,
    bias_cross,
    gain_ff,
    bias_ff,
    w_query,
    w_key,
    w_value,
    w_out,
    c_query,
    c_key,
    c_value,
    c_out,
    w_gate,
    w_up,
    w_down,
):
    frames, width = hidden_in.shape
    plane, level = lax.axis_index("dp") % PLANE, lax.axis_index("dp") // PLANE
    info = jnp.concatenate([row_split, prompt_len])
    positions = jnp.arange(frames, dtype=jnp.int32)
    row_ids = (positions >= row_split[0]).astype(jnp.int32)
    tables = rotary_tables((positions - row_ids * row_split[0]).astype(f32), 2 * HEAD)
    tables = lax.optimization_barrier(tables)
    tables = tuple(jnp.concatenate([table, table], axis=1) for table in tables)
    gain_attn, bias_attn, gain_cross, bias_cross, gain_ff, bias_ff = (
        vector[None] for vector in (gain_attn, bias_attn, gain_cross, bias_cross, gain_ff, bias_ff)
    )

    zero = jnp.zeros((1,), jnp.int32)
    half = zero + lax.axis_index("tensor")
    parity, upper = zero + level % 2, zero + level // 2
    chips = [[PLANE * z + p for p in range(PLANE)] for z in range(LEVELS)]

    def swapped(part):
        return lax.ppermute(part, "tensor", [(0, 1), (1, 0)])

    def in_plane(values):
        shape = values.shape
        return lax.all_to_all(
            values, "dp", 0, 0, axis_index_groups=chips, tiled=True
        ).reshape(shape)

    def gathered(copies):
        return in_plane(copies.reshape(-1, width))

    def level_swap(values, mask):
        return lax.ppermute(values, "dp", pairs(mask))

    token = jnp.zeros((8, 128), f32)
    context = prompt_states.reshape(2 * PROMPT, prompt_states.shape[2])
    cross_key = product_plain(context, c_key).astype(low)
    cross_value = product_plain(context, c_value).astype(low)
    copies_one, copies, query, key, value, attended_one, logsum_one, part, token = self_forward(
        token,
        jnp.concatenate([info, half]),
        hidden_in,
        gain_attn,
        bias_attn,
        w_query,
        w_key,
        w_value,
        w_out,
        tables,
        out_grad,
    )
    part_swapped = swapped(part)
    frames_out = gathered(copies)
    resid_one, input_two, cross_query, attended_two, logsum_two, part, token = cross_forward(
        token,
        info,
        hidden_in,
        part,
        part_swapped,
        gain_cross,
        bias_cross,
        c_query,
        cross_key,
        cross_value,
        c_out,
    )
    part_swapped = swapped(part)
    resid_two, input_three, copies, token = norm_forward(
        token, resid_one, part, part_swapped, gain_ff, bias_ff, half
    )
    frames_out, token = hold(token, frames_out)
    frames_in = gathered(copies)
    frames_out = (frames_out, swapped(frames_out))
    sum_part, back_part, token = ff_both(token, input_three, out_grad, w_gate, w_up, w_down)
    frames_in, token = hold(token, frames_in)
    frames_in = (frames_in, swapped(frames_in))
    back_swapped = swapped(back_part)
    copies_one, token = hold(token, copies_one)
    frames_one = gathered(copies_one)

    tile = 256
    tiles = w_gate.shape[1] // (PLANE * tile)

    def share(token, index, count):
        number = jnp.concatenate([zero + plane * tiles + index, parity])
        return ff_share(token, number, frames_in, frames_out, w_gate, w_up, w_down, tile, count)

    send_a, keep_a, token = share(token, 0, 1)
    got_a = level_swap(send_a, PLANE)
    grad_two, grad_cross_out, vectors_ff, query_grad, key_grad, value_grad, part, token = cross_backward(
        token,
        info,
        resid_two,
        back_part,
        back_swapped,
        out_grad,
        gain_ff,
        c_out,
        cross_query,
        cross_key,
        cross_value,
        attended_two,
        logsum_two,
        c_query,
    )
    part_swapped = swapped(part)
    r, c = width // 16, context.shape[1] // 16
    products, token = weight_products(
        token,
        [grad_cross_out, input_two, context],
        [(0, 0), (1, r), (2, 2 * r), (2, 2 * r + c)],
        [attended_two, query_grad, key_grad, value_grad],
    )
    frames_one, token = hold(token, frames_one)
    got_cross = in_plane(products)
    frames_one = (frames_one, swapped(frames_one))
    pass_a, own_a, token = level_sum(token, keep_a, got_a, upper)
    last_a = level_swap(pass_a, 2 * PLANE)
    send_b, keep_b, token = share(token, 1, tiles - 1)
    got_b = level_swap(send_b, PLANE)
    grad_one, grad_self_out, vectors_cross, grads, part, token = self_backward(
        token,
        info,
        resid_one,
        part,
        part_swapped,
        grad_two,
        gain_cross,
        w_out,
        query,
        key,
        value,
        attended_one,
        logsum_one,
        w_query,
        w_key,
        w_value,
        tables,
    )
    part_swapped = swapped(part)
    last_a, token = hold(token, last_a, True)
    sum_part, token = hold(token, sum_part, True)
    sum_swapped = swapped(sum_part)
    products, token = weight_products(token, [grad_self_out], [(0, 0)], [attended_one])
    grad_hidden, vectors_attn, result, token = last_backward(
        token, hidden_in, part, part_swapped, grad_one, gain_attn, resid_two, sum_part, sum_swapped
    )
    vectors = jnp.concatenate([vectors_attn, vectors_cross, vectors_ff])
    pass_b, own_b, token = level_sum(token, keep_b, got_b, upper)
    last_b = level_swap(pass_b, 2 * PLANE)
    got_cross, token = hold(token, got_cross)
    grads, token = hold(token, grads)
    got_heads = in_plane(grads)
    send_x, keep_x, token = plane_sum(token, got_cross, parity)
    got_x = level_swap(send_x, PLANE)
    got_heads, token = hold(token, got_heads)
    products, token = hold(token, products)
    got_out = in_plane(products)
    send_h, keep_h, token = head_products(
        token, jnp.concatenate([half, parity]), got_heads, frames_one
    )
    got_h = level_swap(send_h, PLANE)
    last_b, token = hold(token, last_b)
    units, token = unit_pack(token, [(own_a, last_a), (own_b, last_b)], 3 * width // LEVELS)
    pass_x, own_x, token = level_sum(token, keep_x[None], got_x[None], upper)
    last_x = level_swap(pass_x, 2 * PLANE)
    vectors_got = level_swap(vectors, 1)
    got_out, token = hold(token, got_out)
    units, token = hold(token, units)
    units = in_plane(units)
    send_o, keep_o, token = plane_sum(token, got_out, parity)
    got_o = level_swap(send_o, PLANE)
    pass_h, own_h, token = level_sum(token, keep_h[None], got_h[None], upper)
    last_h = level_swap(pass_h, 2 * PLANE)
    vectors_got, token = hold(token, vectors_got)
    vectors = vectors + vectors_got
    vectors_got = level_swap(vectors, 2)
    pass_o, own_o, token = level_sum(token, keep_o[None], got_o[None], upper)
    last_o = level_swap(pass_o, 2 * PLANE)
    last_x, token = hold(token, last_x)
    cross = add_low(own_x, last_x)
    units, token = hold(token, units)
    grad_w_down, grad_w_gate, grad_w_up, token = unit_unpack(token, units)
    vectors_got, token = hold(token, vectors_got)
    vectors = vectors + vectors_got
    vectors_got = level_swap(vectors, PLANE)
    heads, token = head_pack(token, own_h, last_h)
    heads = in_plane(heads)
    vectors_got, token = hold(token, vectors_got)
    vectors = vectors + vectors_got
    vectors = own_share(vectors + level_swap(vectors, 2 * PLANE))
    heads, token = hold(token, heads)
    grad_w_query, grad_w_key, grad_w_value, token = head_unpack(token, heads)
    return (
        result,
        grad_hidden,
        *(vectors[index] for index in range(6)),
        grad_w_query,
        grad_w_key,
        grad_w_value,
        add_low(own_o, last_o).T,
        cross[r : 2 * r],
        cross[2 * r : 2 * r + c],
        cross[2 * r + c :],
        cross[:r].T,
        grad_w_gate,
        grad_w_up,
        grad_w_down,
    )


def on_any(
    hidden_in,
    out_grad,
    prompt_states,
    row_split,
    prompt_len,
    gain_attn,
    bias_attn,
    gain_cross,
    bias_cross,
    gain_ff,
    bias_ff,
    w_query,
    w_key,
    w_value,
    w_out,
    c_query,
    c_key,
    c_value,
    c_out,
    w_gate,
    w_up,
    w_down,
):
    frame_count = hidden_in.shape[0]
    positions = jnp.arange(frame_count, dtype=jnp.int32)
    split_here = row_split[0]
    row_ids = (positions >= split_here).astype(jnp.int32)
    tables = rotary_tables((positions - row_ids * split_here).astype(jnp.float32), w_query.shape[1])
    key_index = jnp.arange(2 * PROMPT, dtype=jnp.int32)
    key_rows = key_index // PROMPT
    key_live = key_index % PROMPT < jnp.where(key_rows == 0, prompt_len[0], prompt_len[1])
    self_ok = row_ids[:, None] == row_ids[None, :]
    cross_ok = (row_ids[:, None] == key_rows[None, :]) & key_live[None, :]

    normed, scaled_one, inverse_one = normalize(hidden_in, gain_attn, bias_attn)
    input_one = normed.astype(low)
    query_one = rotate(product_plain(input_one, w_query), tables).astype(low)
    key_one = rotate(product_plain(input_one, w_key), tables).astype(low)
    value_one = product_plain(input_one, w_value).astype(low)
    attended_one, logsum_one = attend_forward(query_one, heads_of(key_one), heads_of(value_one), self_ok)
    resid_one = hidden_in + swap_sum(product_plain(attended_one, w_out))

    normed, scaled_two, inverse_two = normalize(resid_one, gain_cross, bias_cross)
    input_two = normed.astype(low)
    cross_query = product_plain(input_two, c_query).astype(low)
    context_flat = prompt_states.reshape(2 * PROMPT, prompt_states.shape[2])
    cross_key = product_plain(context_flat, c_key).astype(low)
    cross_value = product_plain(context_flat, c_value).astype(low)
    attended_two, logsum_two = attend_forward(
        cross_query, heads_of(cross_key), heads_of(cross_value), cross_ok
    )
    resid_two = resid_one + swap_sum(product_plain(attended_two, c_out))

    normed, scaled_three, inverse_three = normalize(resid_two, gain_ff, bias_ff)
    input_three = normed.astype(low)
    gate_pre = product_plain(input_three, w_gate)
    up_pre = product_plain(input_three, w_up)
    sigmoid_gate = jax.nn.sigmoid(gate_pre)
    mixed_low = (gate_pre * sigmoid_gate * up_pre).astype(low)
    result = resid_two + swap_sum(product_plain(mixed_low, w_down))

    grad_ff_out = out_grad.astype(low)
    grad_w_down = generic_sum(grad_ff_out, mixed_low).T
    grad_mixed = product_with_rows(grad_ff_out, w_down)
    grad_gate = (
        grad_mixed * up_pre * sigmoid_gate * (1.0 + gate_pre * (1.0 - sigmoid_gate))
    ).astype(low)
    grad_up = (grad_mixed * gate_pre * sigmoid_gate).astype(low)
    grad_w_gate = generic_sum(input_three, grad_gate)
    grad_w_up = generic_sum(input_three, grad_up)
    normed_grad_three = swap_sum(
        product_with_rows(grad_gate, w_gate) + product_with_rows(grad_up, w_up)
    )
    back_three, grad_gain_ff, grad_bias_ff = normalize_back(
        normed_grad_three, scaled_three, inverse_three, gain_ff
    )
    grad_two = out_grad + back_three
    grad_cross_out = grad_two.astype(low)
    grad_c_out = generic_sum(grad_cross_out, attended_two).T
    grad_attended_two = product_with_rows(grad_cross_out, c_out).astype(low)
    cross_query_grad, cross_key_grad, cross_value_grad = attend_backward(
        cross_query,
        heads_of(cross_key),
        heads_of(cross_value),
        cross_ok,
        grad_attended_two,
        logsum_two,
    )
    cross_query_grad = cross_query_grad.astype(low)
    cross_key_grad = cross_key_grad.astype(low)
    cross_value_grad = cross_value_grad.astype(low)
    grad_c_query = generic_sum(input_two, cross_query_grad)
    grad_c_key = generic_sum(context_flat, cross_key_grad)
    grad_c_value = generic_sum(context_flat, cross_value_grad)
    normed_grad_two = swap_sum(product_with_rows(cross_query_grad, c_query))
    back_two, grad_gain_cross, grad_bias_cross = normalize_back(
        normed_grad_two, scaled_two, inverse_two, gain_cross
    )
    grad_one = grad_two + back_two
    grad_self_out = grad_one.astype(low)
    grad_w_out = generic_sum(grad_self_out, attended_one).T
    grad_attended_one = product_with_rows(grad_self_out, w_out).astype(low)
    query_grad, key_grad, value_grad = attend_backward(
        query_one, heads_of(key_one), heads_of(value_one), self_ok, grad_attended_one, logsum_one
    )
    query_grad = rotate_back(query_grad, tables).astype(low)
    key_grad = rotate_back(key_grad, tables).astype(low)
    value_grad = value_grad.astype(low)
    grad_w_query = generic_sum(input_one, query_grad)
    grad_w_key = generic_sum(input_one, key_grad)
    grad_w_value = generic_sum(input_one, value_grad)
    normed_grad_one = swap_sum(
        product_with_rows(query_grad, w_query)
        + product_with_rows(key_grad, w_key)
        + product_with_rows(value_grad, w_value)
    )
    back_one, grad_gain_attn, grad_bias_attn = normalize_back(
        normed_grad_one, scaled_one, inverse_one, gain_attn
    )
    grad_hidden = grad_one + back_one
    vectors = lax.psum(
        jnp.stack(
            [
                grad_gain_attn,
                grad_bias_attn,
                grad_gain_cross,
                grad_bias_cross,
                grad_gain_ff,
                grad_bias_ff,
            ]
        ),
        "dp",
    )
    vectors = own_share(vectors)
    return (
        result,
        grad_hidden,
        vectors[0],
        vectors[1],
        vectors[2],
        vectors[3],
        vectors[4],
        vectors[5],
        grad_w_query,
        grad_w_key,
        grad_w_value,
        grad_w_out,
        grad_c_query,
        grad_c_key,
        grad_c_value,
        grad_c_out,
        grad_w_gate,
        grad_w_up,
        grad_w_down,
    )


def solution(mesh):
    in_specs = (
        P("dp", None),
        P("dp", None),
        P("dp", None, None),
        P("dp"),
        P("dp"),
        P(),
        P(),
        P(),
        P(),
        P(),
        P(),
        P(None, "tensor"),
        P(None, "tensor"),
        P(None, "tensor"),
        P("tensor", None),
        P(None, "tensor"),
        P(None, "tensor"),
        P(None, "tensor"),
        P("tensor", None),
        P(None, "tensor"),
        P(None, "tensor"),
        P("tensor", None),
    )
    out_specs = (
        P("dp", None),
        P("dp", None),
        P(("dp", "tensor")),
        P(("dp", "tensor")),
        P(("dp", "tensor")),
        P(("dp", "tensor")),
        P(("dp", "tensor")),
        P(("dp", "tensor")),
        P("dp", "tensor"),
        P("dp", "tensor"),
        P("dp", "tensor"),
        P("tensor", "dp"),
        P("dp", "tensor"),
        P("dp", "tensor"),
        P("dp", "tensor"),
        P("tensor", "dp"),
        P("dp", "tensor"),
        P("dp", "tensor"),
        P("tensor", "dp"),
    )
    known = mesh.shape["dp"] == PLANE * LEVELS and mesh.shape["tensor"] == 2
    return jax.shard_map(
        on_plane if known else on_any, mesh=mesh, in_specs=in_specs, out_specs=out_specs, check_vma=False
    )
```

```python
import functools
import math

import jax
import jax.numpy as jnp
from jax import lax
from jax.experimental import pallas as pl
from jax.experimental.pallas import tpu as pltpu
from jax.sharding import PartitionSpec as P

PROMPT = 128
HEAD = 64
PLANE = 4
LEVELS = 4
VMEM_LIMIT = 62 * 2**20
COST = 3
FLOOR = 15 * 10**9

low = jnp.bfloat16
f32 = jnp.float32
sds = jax.ShapeDtypeStruct


norm_eps = 1e-05
score_scale = 0.125
masked_score = -1e30


def product_plain(left_side, right_side):
    return jnp.dot(left_side, right_side, preferred_element_type=jnp.float32)


def product_over_rows(left_side, right_side):
    return lax.dot_general(
        left_side, right_side, (((0,), (0,)), ((), ())), preferred_element_type=jnp.float32
    )


def product_with_rows(left_side, right_side):
    return lax.dot_general(
        left_side, right_side, (((1,), (1,)), ((), ())), preferred_element_type=jnp.float32
    )


def rotary_tables(positions, width):
    dim_index = jnp.arange(width) % HEAD
    freq_index = (dim_index % 16).astype(jnp.float32)
    inverse_freq = jnp.exp(freq_index * (-math.log(10000.0) / 16.0))
    angles = positions[:, None] * inverse_freq[None, :]
    cosine = jnp.cos(angles)
    sine_part = jnp.sin(angles)
    cos_table = jnp.where(dim_index < 32, cosine, 1.0)
    sin_lower = jnp.where(dim_index < 16, -sine_part, 0.0)
    sin_upper = jnp.where((dim_index >= 16) & (dim_index < 32), sine_part, 0.0)
    return (cos_table, sin_lower, sin_upper)


def rotate(values, tables):
    cos_table, sin_lower, sin_upper = tables
    return (
        values * cos_table
        + jnp.roll(values, -16, axis=1) * sin_lower
        + jnp.roll(values, 16, axis=1) * sin_upper
    )


def rotate_back(incoming, tables):
    cos_table, sin_lower, sin_upper = tables
    return (
        incoming * cos_table
        + jnp.roll(incoming * sin_lower, 16, axis=1)
        + jnp.roll(incoming * sin_upper, -16, axis=1)
    )


def normalize(values, norm_gain, norm_shift):
    average = jnp.mean(values, axis=-1, keepdims=True)
    centered = values - average
    variance = jnp.mean(centered * centered, axis=-1, keepdims=True)
    inverse = lax.rsqrt(variance + norm_eps)
    scaled = centered * inverse
    return (scaled * norm_gain + norm_shift, scaled, inverse)


def normalize_back(incoming, scaled, inverse, norm_gain):
    grad_gain = jnp.sum(incoming * scaled, axis=0)
    grad_shift = jnp.sum(incoming, axis=0)
    weighted = incoming * norm_gain
    grad_input = inverse * (
        weighted
        - jnp.mean(weighted, axis=-1, keepdims=True)
        - scaled * jnp.mean(weighted * scaled, axis=-1, keepdims=True)
    )
    return (grad_input, grad_gain, grad_shift)


def heads_of(values):
    return values.reshape(values.shape[0], values.shape[1] // HEAD, HEAD)


def attend_forward(query_block, key_heads, value_heads, allowed):
    query_heads = heads_of(query_block)
    scores = (
        jnp.einsum("qhd,khd->hqk", query_heads, key_heads, preferred_element_type=jnp.float32)
        * score_scale
    )
    scores = jnp.where(allowed[None], scores, masked_score)
    largest = jnp.max(scores, axis=-1, keepdims=True)
    exp_scores = jnp.exp(scores - largest)
    totals = jnp.sum(exp_scores, axis=-1, keepdims=True)
    soft_weights = (exp_scores / totals).astype(jnp.bfloat16)
    mixed_heads = jnp.einsum(
        "hqk,khd->qhd", soft_weights, value_heads, preferred_element_type=jnp.float32
    )
    mixed_flat = mixed_heads.reshape(query_block.shape[0], query_block.shape[1]).astype(
        jnp.bfloat16
    )
    return (mixed_flat, largest[..., 0] + jnp.log(totals[..., 0]))


def attend_backward(query_block, key_heads, value_heads, allowed, grad_block, logsum_block):
    query_heads = heads_of(query_block)
    grad_heads = heads_of(grad_block)
    scores = (
        jnp.einsum("qhd,khd->hqk", query_heads, key_heads, preferred_element_type=jnp.float32)
        * score_scale
    )
    scores = jnp.where(allowed[None], scores, masked_score)
    soft_weights = jnp.exp(scores - logsum_block[..., None])
    grad_weights = jnp.einsum(
        "qhd,khd->hqk", grad_heads, value_heads, preferred_element_type=jnp.float32
    )
    inner_sum = jnp.sum(soft_weights * grad_weights, axis=-1, keepdims=True)
    grad_scores = (soft_weights * (grad_weights - inner_sum)).astype(jnp.bfloat16)
    grad_query = (
        jnp.einsum("hqk,khd->qhd", grad_scores, key_heads, preferred_element_type=jnp.float32)
        * score_scale
    )
    grad_key = (
        jnp.einsum("hqk,qhd->khd", grad_scores, query_heads, preferred_element_type=jnp.float32)
        * score_scale
    )
    grad_value = jnp.einsum(
        "hqk,qhd->khd",
        soft_weights.astype(jnp.bfloat16),
        grad_heads,
        preferred_element_type=jnp.float32,
    )
    return (
        grad_query.reshape(query_block.shape),
        grad_key.reshape(grad_key.shape[0], -1),
        grad_value.reshape(grad_value.shape[0], -1),
    )


def swap_sum(partial):
    low = partial.astype(jnp.bfloat16)
    if lax.axis_size("tensor") == 2:
        other = lax.ppermute(low, "tensor", [(0, 1), (1, 0)])
        return low.astype(jnp.float32) + other.astype(jnp.float32)
    return lax.psum(low, "tensor").astype(jnp.float32)


def pairs(mask):
    return [(i, i ^ mask) for i in range(16)]


def own_share(vectors):
    share = vectors.shape[1] // (lax.axis_size("dp") * lax.axis_size("tensor"))
    index = lax.axis_index("dp") * lax.axis_size("tensor") + lax.axis_index("tensor")
    return lax.dynamic_slice_in_dim(vectors, index * share, share, 1)


def generic_sum(rows_side, column_side):
    return lax.psum_scatter(
        product_over_rows(rows_side, column_side).astype(jnp.bfloat16),
        "dp",
        scatter_dimension=0,
        tiled=True,
    ).astype(jnp.float32)


def add_low(*terms):
    total = terms[0].astype(jnp.float32)
    for term in terms[1:]:
        total = total + term.astype(jnp.float32)
    return total


def ff_parts(gate, up, grad_mixed):
    sig = 0.5 * jnp.tanh(0.5 * gate) + 0.5
    act = gate * sig
    return (
        (act * up).astype(low),
        (grad_mixed * up * sig * (1.0 + gate * (1.0 - sig))).astype(low),
        (grad_mixed * act).astype(low),
    )


def turn(values, cos, lower, upper):
    width = values.shape[1]
    return (values * cos + pltpu.roll(values, width - 16, 1) * lower + pltpu.roll(values, 16, 1) * upper)

def turn_back(values, cos, lower, upper):
    width = values.shape[1]
    return (values * cos + pltpu.roll(values * lower, 16, 1) + pltpu.roll(values * upper, width - 16, 1))

def normed_rows(values, gain, shift):
    average = jnp.mean(values, axis=-1, keepdims=True)
    centered = values - average
    variance = jnp.mean(centered * centered, axis=-1, keepdims=True)
    return centered * lax.rsqrt(variance + norm_eps) * gain + shift

def over_rows(rows, body, chunk=32):
    @pl.loop(0, rows // chunk, unroll=min(4, rows // chunk))
    def _(i):
        body(pl.ds(pl.multiple_of(i * chunk, chunk), chunk))

def attend(q, k, v, mask, lse_ref):
    q_turned = (q * jnp.bfloat16(0.125)).T
    v_turned = v.T
    heads = [slice(h * HEAD, (h + 1) * HEAD) for h in range(q.shape[1] // HEAD)]
    scores = [product_plain(k[:, c], q_turned[c, :]) for c in heads]
    weights, scales = [], []
    for h, s in enumerate(scores):
        s = s + mask
        m = jnp.max(s, axis=0, keepdims=True)
        e = jnp.exp(s - m)
        total = jnp.sum(e, axis=0, keepdims=True)
        weights.append(e.astype(low))
        scales.append(1.0 / total)
        lse_ref[h : h + 1, :] = m + jnp.log(total)
    outs = [product_plain(v_turned[c, :], e) * x for c, e, x in zip(heads, weights, scales)]
    return jnp.concatenate(outs, axis=0).T.astype(low)


def attend_back(q, k, v, g, att, mask, lse):
    scaled = q * jnp.bfloat16(0.125)
    q_turned = scaled.T
    g_turned = g.T
    k_turned = k.T
    weighted = g_turned.astype(f32) * att.T.astype(f32)
    dq, dk, dv = [], [], []
    for h in range(q.shape[1] // HEAD):
        c = slice(h * HEAD, (h + 1) * HEAD)
        p = jnp.exp(product_plain(k[:, c], q_turned[c, :]) + (mask - lse[h : h + 1, :]))
        dp = product_plain(v[:, c], g_turned[c, :])
        inner = jnp.sum(weighted[c, :], axis=0, keepdims=True)
        ds = (p * (dp - inner)).astype(low)
        dq.append(product_plain(k_turned[c, :], ds))
        dk.append(product_plain(ds, scaled[:, c]))
        dv.append(product_plain(p.astype(low), g[:, c]))
    return (
        jnp.concatenate(dq, axis=0).T * 0.125,
        jnp.concatenate(dk, axis=1),
        jnp.concatenate(dv, axis=1),
    )


def self_mask(split, T):
    r=lax.broadcasted_iota(jnp.int32,(T,T),0)>=split
    c=lax.broadcasted_iota(jnp.int32,(T,T),1)>=split
    return jnp.where(r==c,0.0,masked_score).astype(f32)

def key_half(info, index, frames, keys):
    second = info[0] < frames
    start = jnp.where(second, keys // 2, 0) if index == 1 else 0
    live = jnp.where(second, info[2], info[1]) if index == 1 else info[1]
    return start, live


def half_mask(live, keys, frames):
    return jnp.where(
        lax.broadcasted_iota(jnp.int32, (keys, frames), 0) < live, 0.0, masked_score
    ).astype(f32)


def key_blocks(info, k_ref, v_ref, frames):
    keys = k_ref.shape[0]
    k, v, masks = [], [], []
    for index in range(2):
        start, live = key_half(info, index, frames, keys)
        here = pl.ds(start if index == 0 else pl.multiple_of(start, keys // 2), keys // 2)
        k.append(k_ref[here, :])
        v.append(v_ref[here, :])
        masks.append(half_mask(live, keys // 2, frames // 2))
    return k, v, jnp.concatenate(masks, axis=1)


def cross_attend(info, q, k_ref, v_ref, lse_ref):
    half = q.shape[0] // 2
    q_turned = (q * jnp.bfloat16(0.125)).T
    k, v, mask = key_blocks(info, k_ref, v_ref, 2 * half)
    v_turned = [values.T for values in v]
    outs = []
    for h in range(q.shape[1] // HEAD):
        c = slice(h * HEAD, (h + 1) * HEAD)
        s = [product_plain(k[i][:, c], q_turned[c, i * half : (i + 1) * half]) for i in range(2)]
        s = jnp.concatenate(s, axis=1) + mask
        m = jnp.max(s, axis=0, keepdims=True)
        e = jnp.exp(s - m)
        total = jnp.sum(e, axis=0, keepdims=True)
        lse_ref[h : h + 1, :] = m + jnp.log(total)
        e = e.astype(low)
        o = [product_plain(v_turned[i][c, :], e[:, i * half : (i + 1) * half]) for i in range(2)]
        outs.append(jnp.concatenate(o, axis=1) * (1.0 / total))
    return jnp.concatenate(outs, axis=0).T.astype(low)


def cross_attend_back(info, q, k_ref, v_ref, g, att, lse):
    half = q.shape[0] // 2
    scaled = q * jnp.bfloat16(0.125)
    q_turned = scaled.T
    g_turned = g.T
    weighted = g_turned.astype(f32) * att.T.astype(f32)
    k, v, mask = key_blocks(info, k_ref, v_ref, 2 * half)
    k_turned = [values.T for values in k]
    parts = [slice(0, half), slice(half, 2 * half)]
    dq, dk, dv = [], [[], []], [[], []]
    for h in range(q.shape[1] // HEAD):
        c = slice(h * HEAD, (h + 1) * HEAD)
        s = [product_plain(k[i][:, c], q_turned[c, parts[i]]) for i in range(2)]
        dp = [product_plain(v[i][:, c], g_turned[c, parts[i]]) for i in range(2)]
        p = jnp.exp(jnp.concatenate(s, axis=1) + (mask - lse[h : h + 1, :]))
        inner = jnp.sum(weighted[c, :], axis=0, keepdims=True)
        ds = (p * (jnp.concatenate(dp, axis=1) - inner)).astype(low)
        p = p.astype(low)
        dq.append(
            jnp.concatenate(
                [product_plain(k_turned[i][c, :], ds[:, parts[i]]) for i in range(2)], axis=1
            )
        )
        for i in range(2):
            dk[i].append(product_plain(ds[:, parts[i]], scaled[parts[i], c]))
            dv[i].append(product_plain(p[:, parts[i]], g[parts[i], c]))
    second = (info[0] < 2 * half).astype(f32)

    def by_row(halves):
        first, last = (jnp.concatenate(half, axis=1) for half in halves)
        return jnp.concatenate([first + last * (1.0 - second), last * second], axis=0)

    return jnp.concatenate(dq, axis=0).T * 0.125, by_row(dk), by_row(dv)


def norm_back_rows(x,e,gain,above,gain_acc,shift_acc):
    average=jnp.mean(x,axis=-1,keepdims=True)
    centered=x-average
    variance=jnp.mean(centered*centered,axis=-1,keepdims=True)
    inverse=lax.rsqrt(variance+norm_eps)
    n=centered*inverse
    en=e*n
    w=e*gain
    mean_w=jnp.mean(w,axis=-1,keepdims=True)
    mean_wn=jnp.mean(en*gain,axis=-1,keepdims=True)
    fold=lambda t: jnp.sum(t.reshape(t.shape[0]//8,8,t.shape[1]),axis=0)
    gain_acc[...]+=fold(en)
    shift_acc[...]+=fold(e)
    return above+inverse*(w-mean_w-n*mean_wn)

def norm_back_step(x, mine, other, above, gain, total, total_low, kept, vectors, gain_acc, shift_acc):
    step, block = pl.program_id(0), x.shape[0]

    @pl.when(step == 0)
    def _():
        gain_acc[...] = jnp.zeros_like(gain_acc)
        shift_acc[...] = jnp.zeros_like(shift_acc)

    @pl.when(step < BLOCKS)
    def _():
        def rows(r):
            e = mine[r, :].astype(f32) + other[r, :].astype(f32)
            t = norm_back_rows(x[r, :], e, gain[...], above[r, :], gain_acc, shift_acc)
            total[r, :] = t
            total_low[r, :] = t.astype(low)
            kept[within(step, block, r), :] = t.astype(low)

        over_rows(block, rows)

    @pl.when(step == BLOCKS - 1)
    def _():
        vectors[0:1, :] = jnp.sum(gain_acc[...], axis=0, keepdims=True)
        vectors[1:2, :] = jnp.sum(shift_acc[...], axis=0, keepdims=True)


def ordered(kernel, token, args, in_specs, out_specs, out_shape, grid, flops, scratch=(), info=None, brief=False):
    if info is None:
        info = jnp.zeros((1,), jnp.int32)
    inputs, outputs = len(args), len(out_shape)

    def body(info_ref, *refs):
        token_ref = refs[inputs + 1 + outputs]

        @pl.when(functools.reduce(jnp.logical_and, [pl.program_id(i) == 0 for i in range(len(grid))]))
        def _():
            token_ref[...] = jnp.zeros_like(token_ref)

        kernel(
            info_ref,
            *refs[:inputs],
            *refs[inputs + 1 : inputs + 1 + outputs],
            *refs[inputs + 2 + outputs :],
        )

    moved = sum(math.prod(a.shape) * a.dtype.itemsize for a in (*args, *out_shape))
    *results, token = pl.pallas_call(
        body,
        grid_spec=pltpu.PrefetchScalarGridSpec(
            num_scalar_prefetch=1,
            grid=grid,
            in_specs=[*in_specs, pl.BlockSpec(memory_space=pl.ANY)],
            out_specs=[*out_specs, pl.BlockSpec((8, 128), lambda *_: (0, 0))],
            scratch_shapes=list(scratch),
        ),
        out_shape=[*out_shape, sds((8, 128), f32)],
        compiler_params=pltpu.CompilerParams(vmem_limit_bytes=VMEM_LIMIT),
        cost_estimate=pl.CostEstimate(flops=0 if brief else max(FLOOR, int(flops * COST)), bytes_accessed=0 if brief else int(moved * COST), transcendentals=0),
    )(info, *args, token)
    return (*results, token)


def hold(token, values, brief=False):
    def nothing(values_ref, token_ref, out_ref, token_out):
        token_out[...] = jnp.zeros_like(token_out)

    return pl.pallas_call(
        nothing,
        in_specs=[pl.BlockSpec(memory_space=pl.ANY)] * 2,
        out_specs=[pl.BlockSpec(memory_space=pl.ANY), pl.BlockSpec(memory_space=pltpu.VMEM)],
        out_shape=[sds(values.shape, values.dtype), sds((8, 128), f32)],
        input_output_aliases={0: 0},
        compiler_params=pltpu.CompilerParams(vmem_limit_bytes=VMEM_LIMIT),
        cost_estimate=pl.CostEstimate(flops=0 if brief else FLOOR, bytes_accessed=0, transcendentals=0),
    )(values, token)


def specs(frames, width, tile, blocks=0):
    def tile_of(j):
        return jnp.maximum(j - blocks, 0) if blocks else j

    whole = pl.BlockSpec((frames, width), lambda j, *_: (0, 0))
    vector = pl.BlockSpec((1, width), lambda j, *_: (0, 0))
    column = pl.BlockSpec((width, tile), lambda j, *_: (0, tile_of(j)))
    row = pl.BlockSpec((tile, width), lambda j, *_: (tile_of(j), 0))
    act = pl.BlockSpec((frames, tile), lambda j, *_: (0, tile_of(j)))
    table = pl.BlockSpec((frames, tile), lambda j, *_: (0, 0))
    logsum = pl.BlockSpec((8, frames), lambda j, *_: (tile_of(j), 0))
    return whole, vector, column, row, act, table, logsum


BLOCKS = 4


def row_block(frames, width):
    return pl.BlockSpec((frames // BLOCKS, width), lambda j, *_: (jnp.minimum(j, BLOCKS - 1), 0))


def copies_block(frames, width, place):
    return pl.BlockSpec(
        (PLANE, frames // BLOCKS, width),
        lambda j, info: (0, jnp.clip(j - BLOCKS // 2 * info[place], 0, BLOCKS // 2 - 1), 0),
    )


def within(step, rows, r):
    return pl.ds(pl.multiple_of(step * rows + r.start, r.size), r.size)


def added(acc, term, result, first=0):
    step = pl.program_id(0)

    @pl.when(step == first)
    def _():
        acc[...] = term

    @pl.when(step != first)
    def _():
        acc[...] += term

    @pl.when(step == pl.num_programs(0) - 1)
    def _():
        result[...] = acc[...].astype(result.dtype)


def self_kernel(info, hid, gain, shift, wq, wk, wv, wo, cos, lower, upper, grad, copies, grad_copies, q, k, v, att, logsum, part, acc, mask, normed):
    step, frames, block = pl.program_id(0), normed.shape[0], hid.shape[0]

    @pl.when(step == 0)
    def _():
        mask[...] = self_mask(info[0], frames)

    @pl.when(step < BLOCKS)
    def _():
        def rows(r):
            normed[within(step, block, r), :] = normed_rows(hid[r, :], gain[...], shift[...]).astype(low)

        over_rows(block, rows)

    @pl.when((step < BLOCKS) & (step * 2 // BLOCKS == info[3]))
    def _():
        mine = normed[pl.ds(pl.multiple_of(step * block, block), block), :]
        for chip in range(PLANE):
            copies[chip] = mine

    @pl.when(step < BLOCKS // 2)
    def _():
        grad_low = grad[...].astype(low)
        for chip in range(PLANE):
            grad_copies[chip] = grad_low

    @pl.when(step >= BLOCKS)
    def _():
        n = normed[...]
        tables = (cos[...], lower[...], upper[...])
        q[...] = turn(product_plain(n, wq[...]), *tables).astype(low)
        k[...] = turn(product_plain(n, wk[...]), *tables).astype(low)
        v[...] = product_plain(n, wv[...]).astype(low)
        attended = attend(q[...], k[...], v[...], mask[...], logsum)
        att[...] = attended
        added(acc, product_plain(attended, wo[...]), part, BLOCKS)


def self_forward(token, info, hid, gain, shift, wq, wk, wv, wo, tables, grad, tile=4 * HEAD):
    frames, width = hid.shape
    columns = wq.shape[1]
    whole, vector, column, row, act, table, logsum = specs(frames, width, tile, BLOCKS)
    blocks = row_block(frames, width)
    here = frames // BLOCKS
    return ordered(
        self_kernel,
        token,
        (hid, gain, shift, wq, wk, wv, wo, *tables, grad),
        [blocks, vector, vector, column, column, column, row, table, table, table]
        + [
            pl.BlockSpec(
                (here, width),
                lambda j, info: (BLOCKS // 2 * info[3] + jnp.minimum(j, BLOCKS // 2 - 1), 0),
            )
        ],
        [
            copies_block(frames, width, 3),
            pl.BlockSpec((PLANE, here, width), lambda j, info: (0, jnp.minimum(j, BLOCKS // 2 - 1), 0)),
        ]
        + [act, act, act, act, logsum, whole],
        [sds((PLANE, frames // 2, width), low)] * 2
        + [sds((frames, columns), low)] * 4
        + [sds((columns // tile * 8, frames), f32), sds((frames, width), low)],
        (BLOCKS + columns // tile,),
        2 * frames * columns * (4 * width + 8 * frames),
        [
            pltpu.VMEM((frames, width), f32),
            pltpu.VMEM((frames, frames), f32),
            pltpu.VMEM((frames, width), low),
        ],
        info,
    )


def cross_kernel(info, hid, mine, other, gain, shift, cq, ck, cv, co, total, normed, q, att, logsum, part, acc, kept):
    step, block = pl.program_id(0), hid.shape[0]

    @pl.when(step < BLOCKS)
    def _():
        def rows(r):
            x = hid[r, :] + (mine[r, :].astype(f32) + other[r, :].astype(f32))
            total[r, :] = x
            n = normed_rows(x, gain[...], shift[...]).astype(low)
            normed[r, :] = n
            kept[within(step, block, r), :] = n

        over_rows(block, rows)

    @pl.when(step >= BLOCKS)
    def _():
        q[...] = product_plain(kept[...], cq[...]).astype(low)
        attended = cross_attend(info, q[...], ck, cv, logsum)
        att[...] = attended
        added(acc, product_plain(attended, co[...]), part, BLOCKS)


def cross_forward(token, info, hid, mine, other, gain, shift, cq, ck, cv, co, tile=4 * HEAD):
    frames, width = hid.shape
    columns, keys = cq.shape[1], ck.shape[0]
    whole, vector, column, row, act, table, logsum = specs(frames, width, tile, BLOCKS)
    key = pl.BlockSpec((keys, tile), lambda j, *_: (0, jnp.maximum(j - BLOCKS, 0)))
    blocks = row_block(frames, width)
    return ordered(
        cross_kernel,
        token,
        (hid, mine, other, gain, shift, cq, ck, cv, co),
        [blocks, blocks, blocks, vector, vector, column, key, key, row],
        [blocks, blocks, act, act, logsum, whole],
        [
            sds((frames, width), f32),
            sds((frames, width), low),
            sds((frames, columns), low),
            sds((frames, columns), low),
            sds((columns // tile * 8, frames), f32),
            sds((frames, width), low),
        ],
        (BLOCKS + columns // tile,),
        2 * frames * columns * (2 * width + 8 * keys),
        [pltpu.VMEM((frames, width), f32), pltpu.VMEM((frames, width), low)],
        info,
        brief=True,
    )


def norm_kernel(info, hid, mine, other, gain, shift, total, normed, copies):
    def rows(r):
        x = hid[r, :] + (mine[r, :].astype(f32) + other[r, :].astype(f32))
        total[r, :] = x
        normed[r, :] = normed_rows(x, gain[...], shift[...]).astype(low)

    over_rows(hid.shape[0], rows)

    @pl.when(pl.program_id(0) * 2 // pl.num_programs(0) == info[0])
    def _():
        values = normed[...]
        for chip in range(PLANE):
            copies[chip] = values


def norm_forward(token, hid, mine, other, gain, shift, half, block=128):
    frames, width = hid.shape
    blocks = frames // (2 * block)
    rows = pl.BlockSpec((block, width), lambda j, *_: (j, 0))
    vector = pl.BlockSpec((1, width), lambda j, *_: (0, 0))
    return ordered(
        norm_kernel,
        token,
        (hid, mine, other, gain, shift),
        [rows, rows, rows, vector, vector],
        [
            rows,
            rows,
            pl.BlockSpec(
                (PLANE, block, width),
                lambda j, info: (0, jnp.clip(j - blocks * info[0], 0, blocks - 1), 0),
            ),
        ],
        [sds((frames, width), f32), sds((frames, width), low), sds((PLANE, frames // 2, width), low)],
        (frames // block,),
        10 * frames * width,
        info=half,
        brief=True,
    )


def cross_back_kernel(info, x, mine, other, above, gain, co, q, ck, cv, att, logsum, cq, total, total_low, vectors, dq, dk, dv, part, acc, gain_acc, shift_acc, kept):
    norm_back_step(x, mine, other, above, gain, total, total_low, kept, vectors, gain_acc, shift_acc)

    @pl.when(pl.program_id(0) >= BLOCKS)
    def _():
        g = product_with_rows(kept[...], co[...]).astype(low)
        a, b, c = cross_attend_back(info, q[...], ck, cv, g, att[...], logsum[...])
        a = a.astype(low)
        dq[...] = a
        dk[...] = b.astype(low)
        dv[...] = c.astype(low)
        added(acc, product_with_rows(a, cq[...]), part, BLOCKS)


def cross_backward(token, info, x, mine, other, above, gain, co, q, ck, cv, att, logsums, cq, tile=4 * HEAD):
    frames, width = x.shape
    columns, keys = cq.shape[1], ck.shape[0]
    whole, vector, column, row, act, table, logsum = specs(frames, width, tile, BLOCKS)
    key = pl.BlockSpec((keys, tile), lambda j, *_: (0, jnp.maximum(j - BLOCKS, 0)))
    blocks = row_block(frames, width)
    two = pl.BlockSpec((2, width), lambda j, *_: (0, 0))
    return ordered(
        cross_back_kernel,
        token,
        (x, mine, other, above, gain, co, q, ck, cv, att, logsums, cq),
        [blocks, blocks, blocks, blocks, vector, row, act, key, key, act, logsum, column],
        [blocks, blocks, two, act, key, key, whole],
        [
            sds((frames, width), f32),
            sds((frames, width), low),
            sds((2, width), f32),
            sds((frames, columns), low),
            sds((keys, columns), low),
            sds((keys, columns), low),
            sds((frames, width), low),
        ],
        (BLOCKS + columns // tile,),
        2 * frames * columns * (2 * width + 20 * keys),
        [
            pltpu.VMEM((frames, width), f32),
            pltpu.VMEM((8, width), f32),
            pltpu.VMEM((8, width), f32),
            pltpu.VMEM((frames, width), low),
        ],
        info,
    )


def self_back_kernel(info, x, mine, other, above, gain, wo, q, k, v, att, logsum, wq, wk, wv, cos, lower, upper, total, total_low, vectors, grads, part, acc, mask, gain_acc, shift_acc, kept):
    step = pl.program_id(0)

    @pl.when(step == 0)
    def _():
        mask[...] = self_mask(info[0], kept.shape[0])

    norm_back_step(x, mine, other, above, gain, total, total_low, kept, vectors, gain_acc, shift_acc)

    @pl.when(step >= BLOCKS)
    def _():
        g = product_with_rows(kept[...], wo[...]).astype(low)
        a, b, c = attend_back(q[...], k[...], v[...], g, att[...], mask[...], logsum[...])
        tables = (cos[...], lower[...], upper[...])
        a = turn_back(a, *tables).astype(low)
        b = turn_back(b, *tables).astype(low)
        c = c.astype(low)
        for index, values in enumerate((a, b, c)):
            turned = values.T
            for quarter in range(PLANE):
                grads[quarter, index] = turned[quarter * HEAD : (quarter + 1) * HEAD]
        back = product_with_rows(a, wq[...]) + product_with_rows(b, wk[...])
        added(acc, back + product_with_rows(c, wv[...]), part, BLOCKS)


def self_backward(token, info, x, mine, other, above, gain, wo, q, k, v, att, logsums, wq, wk, wv, tables, tile=4 * HEAD):
    frames, width = x.shape
    columns = wq.shape[1]
    whole, vector, column, row, act, table, logsum = specs(frames, width, tile, BLOCKS)
    blocks = row_block(frames, width)
    two = pl.BlockSpec((2, width), lambda j, *_: (0, 0))
    heads = pl.BlockSpec(
        (PLANE, 3, HEAD, frames), lambda j, *_: (0, 0, jnp.maximum(j - BLOCKS, 0), 0)
    )
    return ordered(
        self_back_kernel,
        token,
        (x, mine, other, above, gain, wo, q, k, v, att, logsums, wq, wk, wv, *tables),
        [blocks] * 4
        + [vector, row, act, act, act, act, logsum, column, column, column, table, table, table],
        [blocks, blocks, two, heads, whole],
        [
            sds((frames, width), f32),
            sds((frames, width), low),
            sds((2, width), f32),
            sds((PLANE, 3, columns // PLANE, frames), low),
            sds((frames, width), low),
        ],
        (BLOCKS + columns // tile,),
        2 * frames * columns * (4 * width + 20 * frames),
        [
            pltpu.VMEM((frames, width), f32),
            pltpu.VMEM((frames, frames), f32),
            pltpu.VMEM((8, width), f32),
            pltpu.VMEM((8, width), f32),
            pltpu.VMEM((frames, width), low),
        ],
        info,
    )


def last_kernel(_, x, mine, other, above, gain, resid, sum_mine, sum_other, total, vectors, result, gain_acc, shift_acc):
    step = pl.program_id(0)

    @pl.when(step == 0)
    def _():
        gain_acc[...] = jnp.zeros_like(gain_acc)
        shift_acc[...] = jnp.zeros_like(shift_acc)

    def rows(r):
        e = mine[r, :].astype(f32) + other[r, :].astype(f32)
        total[r, :] = norm_back_rows(x[r, :], e, gain[...], above[r, :], gain_acc, shift_acc)
        result[r, :] = resid[r, :] + (sum_mine[r, :].astype(f32) + sum_other[r, :].astype(f32))

    over_rows(x.shape[0], rows)

    @pl.when(step == pl.num_programs(0) - 1)
    def _():
        vectors[0:1, :] = jnp.sum(gain_acc[...], axis=0, keepdims=True)
        vectors[1:2, :] = jnp.sum(shift_acc[...], axis=0, keepdims=True)


def last_backward(token, x, mine, other, above, gain, resid, sum_mine, sum_other, block=128):
    frames, width = x.shape
    rows = pl.BlockSpec((block, width), lambda j, *_: (j, 0))
    vector = pl.BlockSpec((1, width), lambda j, *_: (0, 0))
    two = pl.BlockSpec((2, width), lambda j, *_: (0, 0))
    return ordered(
        last_kernel,
        token,
        (x, mine, other, above, gain, resid, sum_mine, sum_other),
        [rows, rows, rows, rows, vector, rows, rows, rows],
        [rows, two, rows],
        [sds((frames, width), f32), sds((2, width), f32), sds((frames, width), f32)],
        (frames // block,),
        20 * frames * width,
        [pltpu.VMEM((8, width), f32), pltpu.VMEM((8, width), f32)],
        brief=True,
    )


def pack_kernel(_, *refs):
    for values, copies in zip(refs[: len(refs) // 2], refs[len(refs) // 2 :]):
        copies[...] = values[...].astype(low)


def packed(token, values, half, pieces=1):
    frames, width = values.shape
    rows = frames // (2 * pieces)

    def source(piece):
        return pl.BlockSpec((rows, width), lambda j, info: (info[0] * pieces + piece, 0))

    return ordered(
        pack_kernel,
        token,
        (values,) * pieces,
        [source(piece) for piece in range(pieces)],
        [pl.BlockSpec((rows, width), lambda j, info: (j, 0))] * pieces,
        [sds((PLANE * rows, width), low)] * pieces,
        (PLANE,),
        0,
        info=half,
        brief=True,
    )


def ff_kernel(_, in_ref, out_ref, gate_ref, up_ref, down_ref, sum_ref, back_ref, sum_acc, back_acc, out_low):
    @pl.when(pl.program_id(0) == 0)
    def _():
        out_low[...] = out_ref[...].astype(low)

    normed = in_ref[...]
    mixed, grad_gate, grad_up = ff_parts(
        product_plain(normed, gate_ref[...]),
        product_plain(normed, up_ref[...]),
        product_with_rows(out_low[...], down_ref[...]),
    )
    added(sum_acc, product_plain(mixed, down_ref[...]), sum_ref)
    added(
        back_acc,
        product_with_rows(grad_gate, gate_ref[...]) + product_with_rows(grad_up, up_ref[...]),
        back_ref,
    )


def ff_both(token, normed, grad_out, w_gate, w_up, w_down, tile=768):
    frames, width = normed.shape
    units = w_gate.shape[1]
    whole, _, column, row, *_ = specs(frames, width, tile)
    return ordered(
        ff_kernel,
        token,
        (normed, grad_out, w_gate, w_up, w_down),
        [whole, whole, column, column, row],
        [whole, whole],
        [sds((frames, width), low)] * 2,
        (units // tile,),
        12 * frames * width * units,
        [pltpu.VMEM((frames, width), f32)] * 2 + [pltpu.VMEM((frames, width), low)],
    )


def share_kernel(info, in_mine, in_other, out_mine, out_other, gate_ref, up_ref, down_ref, send_ref, keep_ref, acc):
    step = pl.program_id(1)
    normed = jnp.concatenate([in_mine[...], in_other[...]], axis=0)
    grad_out = jnp.concatenate([out_mine[...], out_other[...]], axis=0)
    mixed, grad_gate, grad_up = ff_parts(
        product_plain(normed, gate_ref[...]),
        product_plain(normed, up_ref[...]),
        product_with_rows(grad_out, down_ref[...]),
    )
    fresh = (
        product_over_rows(grad_out, mixed),
        product_over_rows(normed, grad_gate),
        product_over_rows(normed, grad_up),
    )
    for index, term in enumerate(fresh):

        @pl.when(step == 0)
        def _():
            acc[index] = term

        @pl.when(step != 0)
        def _():
            acc[index] += term

    @pl.when(step == pl.num_programs(1) - 1)
    def _():
        rows = send_ref.shape[2] // 3
        for pair in range(2):
            for index in range(3):
                for ref, parity in ((send_ref, 1 - info[1]), (keep_ref, info[1])):
                    start = pl.multiple_of((2 * pair + parity) * rows, rows)
                    ref[0, pair, index * rows : (index + 1) * rows] = acc[
                        index, pl.ds(start, rows), :
                    ].astype(ref.dtype)


def ff_share(token, info, normed, grad_out, w_gate, w_up, w_down, tile, count):
    frames, width = normed[0].shape
    chunk = frames // PLANE
    rows = pl.BlockSpec((chunk, width), lambda i, j, info: (j, 0))
    column = pl.BlockSpec((width, tile), lambda i, j, info: (0, info[0] + i))
    half = (LEVELS // 2, 3 * width // LEVELS, tile)
    return ordered(
        share_kernel,
        token,
        (*normed, *grad_out, w_gate, w_up, w_down),
        [rows] * 4
        + [column, column, pl.BlockSpec((tile, width), lambda i, j, info: (info[0] + i, 0))],
        [pl.BlockSpec((1, *half), lambda i, j, info: (i, 0, 0, 0))] * 2,
        [sds((count, *half), low)] * 2,
        (count, PLANE),
        24 * frames * width * tile * count,
        [pltpu.VMEM((3, width, tile), f32)],
        info,
    )


def weight_kernel(plan, sides_count, _, *refs):
    sides, columns = refs[:sides_count], refs[sides_count : sides_count + len(plan)]
    out = refs[sides_count + len(plan)]
    turned = refs[sides_count + len(plan) + 1 :]

    @pl.when(pl.program_id(0) == 0)
    def _():
        for side, ref in zip(sides, turned):
            ref[...] = side[...].T

    for (which, first), column in zip(plan, columns):
        product = product_plain(turned[which][...], column[...]).astype(low)
        rows = product.shape[0] // (PLANE * LEVELS)
        product = product.reshape(LEVELS, PLANE, rows, product.shape[1])
        for owner in range(PLANE):
            out[owner, :, first : first + rows, :] = product[:, owner]


def weight_products(token, sides, plan, columns, tile=256):
    width = columns[0].shape[1]
    rows = sum(sides[which].shape[1] for which, _ in plan) // (PLANE * LEVELS)
    return ordered(
        functools.partial(weight_kernel, plan, len(sides)),
        token,
        (*sides, *columns),
        [pl.BlockSpec(side.shape, lambda j, *_: (0, 0)) for side in sides]
        + [pl.BlockSpec((column.shape[0], tile), lambda j, *_: (0, j)) for column in columns],
        [pl.BlockSpec((PLANE, LEVELS, rows, tile), lambda j, *_: (0, 0, 0, j))],
        [sds((PLANE, LEVELS, rows, width), low)],
        (width // tile,),
        sum(2 * sides[w].shape[0] * sides[w].shape[1] * width for w, _ in plan),
        [pltpu.VMEM((side.shape[1], side.shape[0]), low) for side in sides],
        brief=len(sides) == 1,
    )


def plane_sum_kernel(info, got, send, keep):
    for ref, parity in ((send, 1 - info[0]), (keep, info[0])):
        total = got[0, 0, parity].astype(f32)
        for source in range(1, PLANE):
            total = total + got[source, 0, parity].astype(f32)
        ref[0] = total.astype(low)


def plane_sum(token, got, parity):
    rows, width = got.shape[2:]
    out = pl.BlockSpec((1, rows, width), lambda j, *_: (j, 0, 0))
    return ordered(
        plane_sum_kernel,
        token,
        (got.reshape(PLANE, 2, 2, rows, width),),
        [pl.BlockSpec((PLANE, 1, 2, rows, width), lambda j, *_: (0, j, 0, 0, 0))],
        [out, out],
        [sds((2, rows, width), low)] * 2,
        (2,),
        0,
        info=parity,
    )


def level_sum_kernel(_, keep_pass, got_pass, keep_own, got_own, passed, own):
    passed[...] = (keep_pass[0, 0].astype(f32) + got_pass[0, 0].astype(f32)).astype(low)
    own[...] = keep_own[0, 0].astype(f32) + got_own[0, 0].astype(f32)


def level_sum(token, keep, got, upper):
    count, _, rows, width = keep.shape
    block = rows // 2 if rows % 32 == 0 else rows
    steps = rows // block
    off = pl.BlockSpec((1, 1, block, width), lambda i, j, info: (i, 1 - info[0], j, 0))
    own = pl.BlockSpec((1, 1, block, width), lambda i, j, info: (i, info[0], j, 0))
    out = pl.BlockSpec((block, width), lambda i, j, info: (i * steps + j, 0))
    return ordered(
        level_sum_kernel,
        token,
        (keep, got, keep, got),
        [off, off, own, own],
        [out, out],
        [sds((count * rows, width), low), sds((count * rows, width), f32)],
        (count, steps),
        0,
        info=upper,
    )


def unit_pack_kernel(counts, _, *refs):
    owns, lasts, out = refs[:-1:2], refs[1:-1:2], refs[-1]
    step = pl.program_id(0)
    for own, last, (first, count) in zip(owns, lasts, counts):

        @pl.when((step >= first) & (step < first + count))
        def _():
            total = (own[...] + last[...].astype(f32)).astype(low)
            total = total.reshape(3, PLANE, out.shape[2], out.shape[3])
            for chip in range(PLANE):
                out[chip] = total[:, chip]


def unit_pack(token, sums, rows):
    tile = sums[0][0].shape[1]
    r = rows // (3 * PLANE)
    specs_in, counts, first = [], [], 0
    for own, _ in sums:
        count = own.shape[0] // rows

        def place(j, info, first=first, count=count):
            return (jnp.clip(j - first, 0, count - 1), 0)

        specs_in += [pl.BlockSpec((rows, tile), place)] * 2
        counts.append((first, count))
        first += count
    return ordered(
        functools.partial(unit_pack_kernel, counts),
        token,
        tuple(array for pair in sums for array in pair),
        specs_in,
        [pl.BlockSpec((PLANE, 3, r, tile), lambda j, *_: (0, 0, 0, j))],
        [sds((PLANE, 3, r, tile * first), low)],
        (first,),
        0,
    )


def unit_unpack_kernel(_, got, down, gate, up):
    down[...] = got[0, 0].astype(f32).T
    gate[...] = got[0, 1].astype(f32)
    up[...] = got[0, 2].astype(f32)


def unit_unpack(token, got):
    _, _, r, units = got.shape
    across = pl.BlockSpec((r, units), lambda j, *_: (0, j))
    return ordered(
        unit_unpack_kernel,
        token,
        (got,),
        [pl.BlockSpec((1, 3, r, units), lambda j, *_: (j, 0, 0, 0))],
        [pl.BlockSpec((units, r), lambda j, *_: (j, 0)), across, across],
        [sds((PLANE * units, r), f32)] + [sds((r, PLANE * units), f32)] * 2,
        (PLANE,),
        0,
    )


def head_pack_kernel(_, own, last, out):
    total = (own[...] + last[...].astype(f32)).T.astype(low)
    out[...] = total.reshape(out.shape)


def head_pack(token, own, last):
    features, columns = own.shape
    shape = (PLANE, columns // PLANE, features)
    return ordered(
        head_pack_kernel,
        token,
        (own, last),
        [pl.BlockSpec(own.shape, lambda j, *_: (0, 0))] * 2,
        [pl.BlockSpec(shape, lambda j, *_: (0, 0, 0))],
        [sds(shape, low)],
        (1,),
        0,
    )


def head_unpack_kernel(_, got, *outs):
    groups = got.shape[2] // (3 * HEAD)
    for index, out in enumerate(outs):
        pieces = []
        for group in range(groups):
            first = (index * groups + group) * HEAD
            pieces += [got[chip, :, first : first + HEAD] for chip in range(PLANE)]
        out[...] = jnp.concatenate(pieces, axis=1).astype(f32)


def head_unpack(token, got):
    chips, r, features = got.shape
    shape = (r, chips * features // 3)
    return ordered(
        head_unpack_kernel,
        token,
        (got,),
        [pl.BlockSpec(got.shape, lambda j, *_: (0, 0, 0))],
        [pl.BlockSpec(shape, lambda j, *_: (0, 0))] * 3,
        [sds(shape, f32)] * 3,
        (1,),
        0,
    )


def head_kernel(info, grads_mine, grads_other, in_mine, in_other, send, keep, acc):
    step = pl.program_id(0)
    rows = acc.shape[0]
    term = product_plain(grads_mine[0].reshape(rows, -1), in_mine[...]) + product_plain(
        grads_other[0].reshape(rows, -1), in_other[...]
    )

    @pl.when(step == 0)
    def _():
        acc[...] = term

    @pl.when(step != 0)
    def _():
        acc[...] += term

    @pl.when(step == pl.num_programs(0) - 1)
    def _():
        width = send.shape[2]
        for level in range(LEVELS):
            for ref, parity in ((send, 1 - info[1]), (keep, info[1])):

                @pl.when(parity == level % 2)
                def _():
                    ref[level // 2] = acc[:, level * width : (level + 1) * width].astype(low)


def head_products(token, info, grads, normed):
    _, three, features, frames = grads.shape
    width = normed[0].shape[1]
    chunk = normed[0].shape[0] // PLANE
    rows = pl.BlockSpec((chunk, width), lambda j, info: (j, 0))
    half = (LEVELS // 2, three * features, width // LEVELS)
    return ordered(
        head_kernel,
        token,
        (grads, grads, *normed),
        [
            pl.BlockSpec((1, three, features, chunk), lambda j, info: (j, 0, 0, info[0])),
            pl.BlockSpec((1, three, features, chunk), lambda j, info: (j, 0, 0, 1 - info[0])),
            rows,
            rows,
        ],
        [pl.BlockSpec(half, lambda j, info: (0, 0, 0))] * 2,
        [sds(half, low)] * 2,
        (PLANE,),
        2 * three * features * PLANE * frames * width,
        [pltpu.VMEM((three * features, width), f32)],
        info,
    )


def on_plane(
    hidden_in,
    out_grad,
    prompt_states,
    row_split,
    prompt_len,
    gain_attn,
    bias_attn,
    gain_cross,
    bias_cross,
    gain_ff,
    bias_ff,
    w_query,
    w_key,
    w_value,
    w_out,
    c_query,
    c_key,
    c_value,
    c_out,
    w_gate,
    w_up,
    w_down,
):
    frames, width = hidden_in.shape
    plane, level = lax.axis_index("dp") % PLANE, lax.axis_index("dp") // PLANE
    info = jnp.concatenate([row_split, prompt_len])
    positions = jnp.arange(frames, dtype=jnp.int32)
    row_ids = (positions >= row_split[0]).astype(jnp.int32)
    tables = rotary_tables((positions - row_ids * row_split[0]).astype(f32), 2 * HEAD)
    tables = lax.optimization_barrier(tables)
    tables = tuple(jnp.concatenate([table, table], axis=1) for table in tables)
    gain_attn, bias_attn, gain_cross, bias_cross, gain_ff, bias_ff = (
        vector[None] for vector in (gain_attn, bias_attn, gain_cross, bias_cross, gain_ff, bias_ff)
    )

    zero = jnp.zeros((1,), jnp.int32)
    half = zero + lax.axis_index("tensor")
    parity, upper = zero + level % 2, zero + level // 2
    chips = [[PLANE * z + p for p in range(PLANE)] for z in range(LEVELS)]

    def swapped(part):
        return lax.ppermute(part, "tensor", [(0, 1), (1, 0)])

    def in_plane(values):
        shape = values.shape
        return lax.all_to_all(
            values, "dp", 0, 0, axis_index_groups=chips, tiled=True
        ).reshape(shape)

    def gathered(copies):
        return in_plane(copies.reshape(-1, width))

    def level_swap(values, mask):
        return lax.ppermute(values, "dp", pairs(mask))

    token = jnp.zeros((8, 128), f32)
    context = prompt_states.reshape(2 * PROMPT, prompt_states.shape[2])
    cross_key = product_plain(context, c_key).astype(low)
    cross_value = product_plain(context, c_value).astype(low)
    copies_one, copies, query, key, value, attended_one, logsum_one, part, token = self_forward(
        token,
        jnp.concatenate([info, half]),
        hidden_in,
        gain_attn,
        bias_attn,
        w_query,
        w_key,
        w_value,
        w_out,
        tables,
        out_grad,
    )
    part_swapped = swapped(part)
    frames_out = gathered(copies)
    resid_one, input_two, cross_query, attended_two, logsum_two, part, token = cross_forward(
        token,
        info,
        hidden_in,
        part,
        part_swapped,
        gain_cross,
        bias_cross,
        c_query,
        cross_key,
        cross_value,
        c_out,
    )
    part_swapped = swapped(part)
    resid_two, input_three, copies, token = norm_forward(
        token, resid_one, part, part_swapped, gain_ff, bias_ff, half
    )
    frames_out, token = hold(token, frames_out)
    frames_in = gathered(copies)
    frames_out = (frames_out, swapped(frames_out))
    sum_part, back_part, token = ff_both(token, input_three, out_grad, w_gate, w_up, w_down)
    frames_in, token = hold(token, frames_in)
    frames_in = (frames_in, swapped(frames_in))
    back_swapped = swapped(back_part)
    copies_one, token = hold(token, copies_one)
    frames_one = gathered(copies_one)

    tile = 256
    tiles = w_gate.shape[1] // (PLANE * tile)

    def share(token, index, count):
        number = jnp.concatenate([zero + plane * tiles + index, parity])
        return ff_share(token, number, frames_in, frames_out, w_gate, w_up, w_down, tile, count)

    send_a, keep_a, token = share(token, 0, 1)
    got_a = level_swap(send_a, PLANE)
    grad_two, grad_cross_out, vectors_ff, query_grad, key_grad, value_grad, part, token = cross_backward(
        token,
        info,
        resid_two,
        back_part,
        back_swapped,
        out_grad,
        gain_ff,
        c_out,
        cross_query,
        cross_key,
        cross_value,
        attended_two,
        logsum_two,
        c_query,
    )
    part_swapped = swapped(part)
    r, c = width // 16, context.shape[1] // 16
    products, token = weight_products(
        token,
        [grad_cross_out, input_two, context],
        [(0, 0), (1, r), (2, 2 * r), (2, 2 * r + c)],
        [attended_two, query_grad, key_grad, value_grad],
    )
    frames_one, token = hold(token, frames_one)
    got_cross = in_plane(products)
    frames_one_other = swapped(frames_one)
    pass_a, own_a, token = level_sum(token, keep_a, got_a, upper)
    last_a = level_swap(pass_a, 2 * PLANE)
    send_b, keep_b, token = share(token, 1, 1)
    got_b = level_swap(send_b, PLANE)
    frames_one_other, token = hold(token, frames_one_other, True)
    frames_one = (frames_one, frames_one_other)
    grad_one, grad_self_out, vectors_cross, grads, part, token = self_backward(
        token,
        info,
        resid_one,
        part,
        part_swapped,
        grad_two,
        gain_cross,
        w_out,
        query,
        key,
        value,
        attended_one,
        logsum_one,
        w_query,
        w_key,
        w_value,
        tables,
    )
    last_a, token = hold(token, last_a, True)
    sum_part, token = hold(token, sum_part, True)
    sum_swapped, part_swapped = swapped(sum_part), swapped(part)
    pass_b, own_b, token = level_sum(token, keep_b, got_b, upper)
    last_b = level_swap(pass_b, 2 * PLANE)
    send_c, keep_c, token = share(token, 2, tiles - 2)
    got_c = level_swap(send_c, PLANE)
    products, token = weight_products(token, [grad_self_out], [(0, 0)], [attended_one])
    got_cross, token = hold(token, got_cross)
    grads, token = hold(token, grads)
    got_heads = in_plane(grads)
    send_x, keep_x, token = plane_sum(token, got_cross, parity)
    got_x = level_swap(send_x, PLANE)
    grad_hidden, vectors_attn, result, token = last_backward(
        token, hidden_in, part, part_swapped, grad_one, gain_attn, resid_two, sum_part, sum_swapped
    )
    vectors = jnp.concatenate([vectors_attn, vectors_cross, vectors_ff])
    last_b, token = hold(token, last_b, True)
    pass_c, own_c, token = level_sum(token, keep_c, got_c, upper)
    last_c = level_swap(pass_c, 2 * PLANE)
    got_heads, token = hold(token, got_heads)
    products, token = hold(token, products)
    got_out = in_plane(products)
    send_h, keep_h, token = head_products(
        token, jnp.concatenate([half, parity]), got_heads, frames_one
    )
    got_h = level_swap(send_h, PLANE)
    pass_x, own_x, token = level_sum(token, keep_x[None], got_x[None], upper)
    last_x = level_swap(pass_x, 2 * PLANE)
    last_c, token = hold(token, last_c, True)
    units, token = unit_pack(
        token, [(own_a, last_a), (own_b, last_b), (own_c, last_c)], 3 * width // LEVELS
    )
    vectors_got = level_swap(vectors, 1)
    got_out, token = hold(token, got_out, True)
    units, token = hold(token, units, True)
    units = in_plane(units)
    send_o, keep_o, token = plane_sum(token, got_out, parity)
    got_o = level_swap(send_o, PLANE)
    pass_h, own_h, token = level_sum(token, keep_h[None], got_h[None], upper)
    last_h = level_swap(pass_h, 2 * PLANE)
    vectors_got, token = hold(token, vectors_got)
    vectors = vectors + vectors_got
    vectors_got = level_swap(vectors, 2)
    pass_o, own_o, token = level_sum(token, keep_o[None], got_o[None], upper)
    last_o = level_swap(pass_o, 2 * PLANE)
    last_x, token = hold(token, last_x)
    cross = add_low(own_x, last_x)
    units, token = hold(token, units)
    grad_w_down, grad_w_gate, grad_w_up, token = unit_unpack(token, units)
    vectors_got, token = hold(token, vectors_got)
    vectors = vectors + vectors_got
    vectors_got = level_swap(vectors, PLANE)
    heads, token = head_pack(token, own_h, last_h)
    heads = in_plane(heads)
    vectors_got, token = hold(token, vectors_got)
    vectors = vectors + vectors_got
    vectors = own_share(vectors + level_swap(vectors, 2 * PLANE))
    heads, token = hold(token, heads)
    grad_w_query, grad_w_key, grad_w_value, token = head_unpack(token, heads)
    return (
        result,
        grad_hidden,
        *(vectors[index] for index in range(6)),
        grad_w_query,
        grad_w_key,
        grad_w_value,
        add_low(own_o, last_o).T,
        cross[r : 2 * r],
        cross[2 * r : 2 * r + c],
        cross[2 * r + c :],
        cross[:r].T,
        grad_w_gate,
        grad_w_up,
        grad_w_down,
    )


def on_any(
    hidden_in,
    out_grad,
    prompt_states,
    row_split,
    prompt_len,
    gain_attn,
    bias_attn,
    gain_cross,
    bias_cross,
    gain_ff,
    bias_ff,
    w_query,
    w_key,
    w_value,
    w_out,
    c_query,
    c_key,
    c_value,
    c_out,
    w_gate,
    w_up,
    w_down,
):
    frame_count = hidden_in.shape[0]
    positions = jnp.arange(frame_count, dtype=jnp.int32)
    split_here = row_split[0]
    row_ids = (positions >= split_here).astype(jnp.int32)
    tables = rotary_tables((positions - row_ids * split_here).astype(jnp.float32), w_query.shape[1])
    key_index = jnp.arange(2 * PROMPT, dtype=jnp.int32)
    key_rows = key_index // PROMPT
    key_live = key_index % PROMPT < jnp.where(key_rows == 0, prompt_len[0], prompt_len[1])
    self_ok = row_ids[:, None] == row_ids[None, :]
    cross_ok = (row_ids[:, None] == key_rows[None, :]) & key_live[None, :]

    normed, scaled_one, inverse_one = normalize(hidden_in, gain_attn, bias_attn)
    input_one = normed.astype(low)
    query_one = rotate(product_plain(input_one, w_query), tables).astype(low)
    key_one = rotate(product_plain(input_one, w_key), tables).astype(low)
    value_one = product_plain(input_one, w_value).astype(low)
    attended_one, logsum_one = attend_forward(query_one, heads_of(key_one), heads_of(value_one), self_ok)
    resid_one = hidden_in + swap_sum(product_plain(attended_one, w_out))

    normed, scaled_two, inverse_two = normalize(resid_one, gain_cross, bias_cross)
    input_two = normed.astype(low)
    cross_query = product_plain(input_two, c_query).astype(low)
    context_flat = prompt_states.reshape(2 * PROMPT, prompt_states.shape[2])
    cross_key = product_plain(context_flat, c_key).astype(low)
    cross_value = product_plain(context_flat, c_value).astype(low)
    attended_two, logsum_two = attend_forward(
        cross_query, heads_of(cross_key), heads_of(cross_value), cross_ok
    )
    resid_two = resid_one + swap_sum(product_plain(attended_two, c_out))

    normed, scaled_three, inverse_three = normalize(resid_two, gain_ff, bias_ff)
    input_three = normed.astype(low)
    gate_pre = product_plain(input_three, w_gate)
    up_pre = product_plain(input_three, w_up)
    sigmoid_gate = jax.nn.sigmoid(gate_pre)
    mixed_low = (gate_pre * sigmoid_gate * up_pre).astype(low)
    result = resid_two + swap_sum(product_plain(mixed_low, w_down))

    grad_ff_out = out_grad.astype(low)
    grad_w_down = generic_sum(grad_ff_out, mixed_low).T
    grad_mixed = product_with_rows(grad_ff_out, w_down)
    grad_gate = (
        grad_mixed * up_pre * sigmoid_gate * (1.0 + gate_pre * (1.0 - sigmoid_gate))
    ).astype(low)
    grad_up = (grad_mixed * gate_pre * sigmoid_gate).astype(low)
    grad_w_gate = generic_sum(input_three, grad_gate)
    grad_w_up = generic_sum(input_three, grad_up)
    normed_grad_three = swap_sum(
        product_with_rows(grad_gate, w_gate) + product_with_rows(grad_up, w_up)
    )
    back_three, grad_gain_ff, grad_bias_ff = normalize_back(
        normed_grad_three, scaled_three, inverse_three, gain_ff
    )
    grad_two = out_grad + back_three
    grad_cross_out = grad_two.astype(low)
    grad_c_out = generic_sum(grad_cross_out, attended_two).T
    grad_attended_two = product_with_rows(grad_cross_out, c_out).astype(low)
    cross_query_grad, cross_key_grad, cross_value_grad = attend_backward(
        cross_query,
        heads_of(cross_key),
        heads_of(cross_value),
        cross_ok,
        grad_attended_two,
        logsum_two,
    )
    cross_query_grad = cross_query_grad.astype(low)
    cross_key_grad = cross_key_grad.astype(low)
    cross_value_grad = cross_value_grad.astype(low)
    grad_c_query = generic_sum(input_two, cross_query_grad)
    grad_c_key = generic_sum(context_flat, cross_key_grad)
    grad_c_value = generic_sum(context_flat, cross_value_grad)
    normed_grad_two = swap_sum(product_with_rows(cross_query_grad, c_query))
    back_two, grad_gain_cross, grad_bias_cross = normalize_back(
        normed_grad_two, scaled_two, inverse_two, gain_cross
    )
    grad_one = grad_two + back_two
    grad_self_out = grad_one.astype(low)
    grad_w_out = generic_sum(grad_self_out, attended_one).T
    grad_attended_one = product_with_rows(grad_self_out, w_out).astype(low)
    query_grad, key_grad, value_grad = attend_backward(
        query_one, heads_of(key_one), heads_of(value_one), self_ok, grad_attended_one, logsum_one
    )
    query_grad = rotate_back(query_grad, tables).astype(low)
    key_grad = rotate_back(key_grad, tables).astype(low)
    value_grad = value_grad.astype(low)
    grad_w_query = generic_sum(input_one, query_grad)
    grad_w_key = generic_sum(input_one, key_grad)
    grad_w_value = generic_sum(input_one, value_grad)
    normed_grad_one = swap_sum(
        product_with_rows(query_grad, w_query)
        + product_with_rows(key_grad, w_key)
        + product_with_rows(value_grad, w_value)
    )
    back_one, grad_gain_attn, grad_bias_attn = normalize_back(
        normed_grad_one, scaled_one, inverse_one, gain_attn
    )
    grad_hidden = grad_one + back_one
    vectors = lax.psum(
        jnp.stack(
            [
                grad_gain_attn,
                grad_bias_attn,
                grad_gain_cross,
                grad_bias_cross,
                grad_gain_ff,
                grad_bias_ff,
            ]
        ),
        "dp",
    )
    vectors = own_share(vectors)
    return (
        result,
        grad_hidden,
        vectors[0],
        vectors[1],
        vectors[2],
        vectors[3],
        vectors[4],
        vectors[5],
        grad_w_query,
        grad_w_key,
        grad_w_value,
        grad_w_out,
        grad_c_query,
        grad_c_key,
        grad_c_value,
        grad_c_out,
        grad_w_gate,
        grad_w_up,
        grad_w_down,
    )


def solution(mesh):
    in_specs = (
        P("dp", None),
        P("dp", None),
        P("dp", None, None),
        P("dp"),
        P("dp"),
        P(),
        P(),
        P(),
        P(),
        P(),
        P(),
        P(None, "tensor"),
        P(None, "tensor"),
        P(None, "tensor"),
        P("tensor", None),
        P(None, "tensor"),
        P(None, "tensor"),
        P(None, "tensor"),
        P("tensor", None),
        P(None, "tensor"),
        P(None, "tensor"),
        P("tensor", None),
    )
    out_specs = (
        P("dp", None),
        P("dp", None),
        P(("dp", "tensor")),
        P(("dp", "tensor")),
        P(("dp", "tensor")),
        P(("dp", "tensor")),
        P(("dp", "tensor")),
        P(("dp", "tensor")),
        P("dp", "tensor"),
        P("dp", "tensor"),
        P("dp", "tensor"),
        P("tensor", "dp"),
        P("dp", "tensor"),
        P("dp", "tensor"),
        P("dp", "tensor"),
        P("tensor", "dp"),
        P("dp", "tensor"),
        P("dp", "tensor"),
        P("tensor", "dp"),
    )
    known = mesh.shape["dp"] == PLANE * LEVELS and mesh.shape["tensor"] == 2
    return jax.shard_map(
        on_plane if known else on_any, mesh=mesh, in_specs=in_specs, out_specs=out_specs, check_vma=False
    )
```

```python
import functools
import math

import jax
import jax.numpy as jnp
from jax import lax
from jax.experimental import pallas as pl
from jax.experimental.pallas import tpu as pltpu
from jax.sharding import PartitionSpec as P

PROMPT = 128
HEAD = 64
PLANE = 4
LEVELS = 4
VMEM_LIMIT = 62 * 2**20
COST = 3
FLOOR = 15 * 10**9

low = jnp.bfloat16
f32 = jnp.float32
sds = jax.ShapeDtypeStruct


norm_eps = 1e-05
score_scale = 0.125
masked_score = -1e30


def product_plain(left_side, right_side):
    return jnp.dot(left_side, right_side, preferred_element_type=jnp.float32)


def product_over_rows(left_side, right_side):
    return lax.dot_general(
        left_side, right_side, (((0,), (0,)), ((), ())), preferred_element_type=jnp.float32
    )


def product_with_rows(left_side, right_side):
    return lax.dot_general(
        left_side, right_side, (((1,), (1,)), ((), ())), preferred_element_type=jnp.float32
    )


def rotary_tables(positions, width):
    dim_index = jnp.arange(width) % HEAD
    freq_index = (dim_index % 16).astype(jnp.float32)
    inverse_freq = jnp.exp(freq_index * (-math.log(10000.0) / 16.0))
    angles = positions[:, None] * inverse_freq[None, :]
    cosine = jnp.cos(angles)
    sine_part = jnp.sin(angles)
    cos_table = jnp.where(dim_index < 32, cosine, 1.0)
    sin_lower = jnp.where(dim_index < 16, -sine_part, 0.0)
    sin_upper = jnp.where((dim_index >= 16) & (dim_index < 32), sine_part, 0.0)
    return (cos_table, sin_lower, sin_upper)


def rotate(values, tables):
    cos_table, sin_lower, sin_upper = tables
    return (
        values * cos_table
        + jnp.roll(values, -16, axis=1) * sin_lower
        + jnp.roll(values, 16, axis=1) * sin_upper
    )


def rotate_back(incoming, tables):
    cos_table, sin_lower, sin_upper = tables
    return (
        incoming * cos_table
        + jnp.roll(incoming * sin_lower, 16, axis=1)
        + jnp.roll(incoming * sin_upper, -16, axis=1)
    )


def normalize(values, norm_gain, norm_shift):
    average = jnp.mean(values, axis=-1, keepdims=True)
    centered = values - average
    variance = jnp.mean(centered * centered, axis=-1, keepdims=True)
    inverse = lax.rsqrt(variance + norm_eps)
    scaled = centered * inverse
    return (scaled * norm_gain + norm_shift, scaled, inverse)


def normalize_back(incoming, scaled, inverse, norm_gain):
    grad_gain = jnp.sum(incoming * scaled, axis=0)
    grad_shift = jnp.sum(incoming, axis=0)
    weighted = incoming * norm_gain
    grad_input = inverse * (
        weighted
        - jnp.mean(weighted, axis=-1, keepdims=True)
        - scaled * jnp.mean(weighted * scaled, axis=-1, keepdims=True)
    )
    return (grad_input, grad_gain, grad_shift)


def heads_of(values):
    return values.reshape(values.shape[0], values.shape[1] // HEAD, HEAD)


def attend_forward(query_block, key_heads, value_heads, allowed):
    query_heads = heads_of(query_block)
    scores = (
        jnp.einsum("qhd,khd->hqk", query_heads, key_heads, preferred_element_type=jnp.float32)
        * score_scale
    )
    scores = jnp.where(allowed[None], scores, masked_score)
    largest = jnp.max(scores, axis=-1, keepdims=True)
    exp_scores = jnp.exp(scores - largest)
    totals = jnp.sum(exp_scores, axis=-1, keepdims=True)
    soft_weights = (exp_scores / totals).astype(jnp.bfloat16)
    mixed_heads = jnp.einsum(
        "hqk,khd->qhd", soft_weights, value_heads, preferred_element_type=jnp.float32
    )
    mixed_flat = mixed_heads.reshape(query_block.shape[0], query_block.shape[1]).astype(
        jnp.bfloat16
    )
    return (mixed_flat, largest[..., 0] + jnp.log(totals[..., 0]))


def attend_backward(query_block, key_heads, value_heads, allowed, grad_block, logsum_block):
    query_heads = heads_of(query_block)
    grad_heads = heads_of(grad_block)
    scores = (
        jnp.einsum("qhd,khd->hqk", query_heads, key_heads, preferred_element_type=jnp.float32)
        * score_scale
    )
    scores = jnp.where(allowed[None], scores, masked_score)
    soft_weights = jnp.exp(scores - logsum_block[..., None])
    grad_weights = jnp.einsum(
        "qhd,khd->hqk", grad_heads, value_heads, preferred_element_type=jnp.float32
    )
    inner_sum = jnp.sum(soft_weights * grad_weights, axis=-1, keepdims=True)
    grad_scores = (soft_weights * (grad_weights - inner_sum)).astype(jnp.bfloat16)
    grad_query = (
        jnp.einsum("hqk,khd->qhd", grad_scores, key_heads, preferred_element_type=jnp.float32)
        * score_scale
    )
    grad_key = (
        jnp.einsum("hqk,qhd->khd", grad_scores, query_heads, preferred_element_type=jnp.float32)
        * score_scale
    )
    grad_value = jnp.einsum(
        "hqk,qhd->khd",
        soft_weights.astype(jnp.bfloat16),
        grad_heads,
        preferred_element_type=jnp.float32,
    )
    return (
        grad_query.reshape(query_block.shape),
        grad_key.reshape(grad_key.shape[0], -1),
        grad_value.reshape(grad_value.shape[0], -1),
    )


def swap_sum(partial):
    low = partial.astype(jnp.bfloat16)
    if lax.axis_size("tensor") == 2:
        other = lax.ppermute(low, "tensor", [(0, 1), (1, 0)])
        return low.astype(jnp.float32) + other.astype(jnp.float32)
    return lax.psum(low, "tensor").astype(jnp.float32)


def pairs(mask):
    return [(i, i ^ mask) for i in range(16)]


def own_share(vectors):
    share = vectors.shape[1] // (lax.axis_size("dp") * lax.axis_size("tensor"))
    index = lax.axis_index("dp") * lax.axis_size("tensor") + lax.axis_index("tensor")
    return lax.dynamic_slice_in_dim(vectors, index * share, share, 1)


def generic_sum(rows_side, column_side):
    return lax.psum_scatter(
        product_over_rows(rows_side, column_side).astype(jnp.bfloat16),
        "dp",
        scatter_dimension=0,
        tiled=True,
    ).astype(jnp.float32)


def add_low(*terms):
    total = terms[0].astype(jnp.float32)
    for term in terms[1:]:
        total = total + term.astype(jnp.float32)
    return total


def ff_parts(gate, up, grad_mixed):
    sig = 0.5 * jnp.tanh(0.5 * gate) + 0.5
    act = gate * sig
    return (
        (act * up).astype(low),
        (grad_mixed * up * sig * (1.0 + gate * (1.0 - sig))).astype(low),
        (grad_mixed * act).astype(low),
    )


def turn(values, cos, lower, upper):
    width = values.shape[1]
    return (values * cos + pltpu.roll(values, width - 16, 1) * lower + pltpu.roll(values, 16, 1) * upper)

def turn_back(values, cos, lower, upper):
    width = values.shape[1]
    return (values * cos + pltpu.roll(values * lower, 16, 1) + pltpu.roll(values * upper, width - 16, 1))

def normed_rows(values, gain, shift):
    average = jnp.mean(values, axis=-1, keepdims=True)
    centered = values - average
    variance = jnp.mean(centered * centered, axis=-1, keepdims=True)
    return centered * lax.rsqrt(variance + norm_eps) * gain + shift

def over_rows(rows, body, chunk=32):
    @pl.loop(0, rows // chunk, unroll=min(4, rows // chunk))
    def _(i):
        body(pl.ds(pl.multiple_of(i * chunk, chunk), chunk))

def attend(q, k, v, mask, lse_ref):
    q_turned = (q * jnp.bfloat16(0.125)).T
    v_turned = v.T
    heads = [slice(h * HEAD, (h + 1) * HEAD) for h in range(q.shape[1] // HEAD)]
    scores = [product_plain(k[:, c], q_turned[c, :]) for c in heads]
    weights, scales = [], []
    for h, s in enumerate(scores):
        s = s + mask
        m = jnp.max(s, axis=0, keepdims=True)
        e = jnp.exp(s - m)
        total = jnp.sum(e, axis=0, keepdims=True)
        weights.append(e.astype(low))
        scales.append(1.0 / total)
        lse_ref[h : h + 1, :] = m + jnp.log(total)
    outs = [product_plain(v_turned[c, :], e) * x for c, e, x in zip(heads, weights, scales)]
    return jnp.concatenate(outs, axis=0).T.astype(low)


def attend_back(q, k, v, g, att, mask, lse):
    scaled = q * jnp.bfloat16(0.125)
    q_turned = scaled.T
    g_turned = g.T
    k_turned = k.T
    weighted = g_turned.astype(f32) * att.T.astype(f32)
    dq, dk, dv = [], [], []
    for h in range(q.shape[1] // HEAD):
        c = slice(h * HEAD, (h + 1) * HEAD)
        p = jnp.exp(product_plain(k[:, c], q_turned[c, :]) + (mask - lse[h : h + 1, :]))
        dp = product_plain(v[:, c], g_turned[c, :])
        inner = jnp.sum(weighted[c, :], axis=0, keepdims=True)
        ds = (p * (dp - inner)).astype(low)
        dq.append(product_plain(k_turned[c, :], ds))
        dk.append(product_plain(ds, scaled[:, c]))
        dv.append(product_plain(p.astype(low), g[:, c]))
    return (
        jnp.concatenate(dq, axis=0).T * 0.125,
        jnp.concatenate(dk, axis=1),
        jnp.concatenate(dv, axis=1),
    )


def self_mask(split, T):
    r=lax.broadcasted_iota(jnp.int32,(T,T),0)>=split
    c=lax.broadcasted_iota(jnp.int32,(T,T),1)>=split
    return jnp.where(r==c,0.0,masked_score).astype(f32)

def key_half(info, index, frames, keys):
    second = info[0] < frames
    start = jnp.where(second, keys // 2, 0) if index == 1 else 0
    live = jnp.where(second, info[2], info[1]) if index == 1 else info[1]
    return start, live


def half_mask(live, keys, frames):
    return jnp.where(
        lax.broadcasted_iota(jnp.int32, (keys, frames), 0) < live, 0.0, masked_score
    ).astype(f32)


def key_blocks(info, k_ref, v_ref, frames):
    keys = k_ref.shape[0]
    k, v, masks = [], [], []
    for index in range(2):
        start, live = key_half(info, index, frames, keys)
        here = pl.ds(start if index == 0 else pl.multiple_of(start, keys // 2), keys // 2)
        k.append(k_ref[here, :])
        v.append(v_ref[here, :])
        masks.append(half_mask(live, keys // 2, frames // 2))
    return k, v, jnp.concatenate(masks, axis=1)


def cross_attend(info, q, k_ref, v_ref, lse_ref):
    half = q.shape[0] // 2
    q_turned = (q * jnp.bfloat16(0.125)).T
    k, v, mask = key_blocks(info, k_ref, v_ref, 2 * half)
    v_turned = [values.T for values in v]
    outs = []
    for h in range(q.shape[1] // HEAD):
        c = slice(h * HEAD, (h + 1) * HEAD)
        s = [product_plain(k[i][:, c], q_turned[c, i * half : (i + 1) * half]) for i in range(2)]
        s = jnp.concatenate(s, axis=1) + mask
        m = jnp.max(s, axis=0, keepdims=True)
        e = jnp.exp(s - m)
        total = jnp.sum(e, axis=0, keepdims=True)
        lse_ref[h : h + 1, :] = m + jnp.log(total)
        e = e.astype(low)
        o = [product_plain(v_turned[i][c, :], e[:, i * half : (i + 1) * half]) for i in range(2)]
        outs.append(jnp.concatenate(o, axis=1) * (1.0 / total))
    return jnp.concatenate(outs, axis=0).T.astype(low)


def cross_attend_back(info, q, k_ref, v_ref, g, att, lse):
    half = q.shape[0] // 2
    scaled = q * jnp.bfloat16(0.125)
    q_turned = scaled.T
    g_turned = g.T
    weighted = g_turned.astype(f32) * att.T.astype(f32)
    k, v, mask = key_blocks(info, k_ref, v_ref, 2 * half)
    k_turned = [values.T for values in k]
    parts = [slice(0, half), slice(half, 2 * half)]
    dq, dk, dv = [], [[], []], [[], []]
    for h in range(q.shape[1] // HEAD):
        c = slice(h * HEAD, (h + 1) * HEAD)
        s = [product_plain(k[i][:, c], q_turned[c, parts[i]]) for i in range(2)]
        dp = [product_plain(v[i][:, c], g_turned[c, parts[i]]) for i in range(2)]
        p = jnp.exp(jnp.concatenate(s, axis=1) + (mask - lse[h : h + 1, :]))
        inner = jnp.sum(weighted[c, :], axis=0, keepdims=True)
        ds = (p * (jnp.concatenate(dp, axis=1) - inner)).astype(low)
        p = p.astype(low)
        dq.append(
            jnp.concatenate(
                [product_plain(k_turned[i][c, :], ds[:, parts[i]]) for i in range(2)], axis=1
            )
        )
        for i in range(2):
            dk[i].append(product_plain(ds[:, parts[i]], scaled[parts[i], c]))
            dv[i].append(product_plain(p[:, parts[i]], g[parts[i], c]))
    second = (info[0] < 2 * half).astype(f32)

    def by_row(halves):
        first, last = (jnp.concatenate(half, axis=1) for half in halves)
        return jnp.concatenate([first + last * (1.0 - second), last * second], axis=0)

    return jnp.concatenate(dq, axis=0).T * 0.125, by_row(dk), by_row(dv)


def norm_back_rows(x,e,gain,above,gain_acc,shift_acc):
    average=jnp.mean(x,axis=-1,keepdims=True)
    centered=x-average
    variance=jnp.mean(centered*centered,axis=-1,keepdims=True)
    inverse=lax.rsqrt(variance+norm_eps)
    n=centered*inverse
    en=e*n
    w=e*gain
    mean_w=jnp.mean(w,axis=-1,keepdims=True)
    mean_wn=jnp.mean(en*gain,axis=-1,keepdims=True)
    fold=lambda t: jnp.sum(t.reshape(t.shape[0]//8,8,t.shape[1]),axis=0)
    gain_acc[...]+=fold(en)
    shift_acc[...]+=fold(e)
    return above+inverse*(w-mean_w-n*mean_wn)

def norm_back_step(x, mine, other, above, gain, total, total_low, kept, vectors, gain_acc, shift_acc):
    step, block = pl.program_id(0), x.shape[0]

    @pl.when(step == 0)
    def _():
        gain_acc[...] = jnp.zeros_like(gain_acc)
        shift_acc[...] = jnp.zeros_like(shift_acc)

    @pl.when(step < BLOCKS)
    def _():
        def rows(r):
            e = mine[r, :].astype(f32) + other[r, :].astype(f32)
            t = norm_back_rows(x[r, :], e, gain[...], above[r, :], gain_acc, shift_acc)
            total[r, :] = t
            total_low[r, :] = t.astype(low)
            kept[within(step, block, r), :] = t.astype(low)

        over_rows(block, rows)

    @pl.when(step == BLOCKS - 1)
    def _():
        vectors[0:1, :] = jnp.sum(gain_acc[...], axis=0, keepdims=True)
        vectors[1:2, :] = jnp.sum(shift_acc[...], axis=0, keepdims=True)


def ordered(kernel, token, args, in_specs, out_specs, out_shape, grid, flops, scratch=(), info=None, brief=False):
    if info is None:
        info = jnp.zeros((1,), jnp.int32)
    inputs, outputs = len(args), len(out_shape)

    def body(info_ref, *refs):
        token_ref = refs[inputs + 1 + outputs]

        @pl.when(functools.reduce(jnp.logical_and, [pl.program_id(i) == 0 for i in range(len(grid))]))
        def _():
            token_ref[...] = jnp.zeros_like(token_ref)

        kernel(
            info_ref,
            *refs[:inputs],
            *refs[inputs + 1 : inputs + 1 + outputs],
            *refs[inputs + 2 + outputs :],
        )

    moved = sum(math.prod(a.shape) * a.dtype.itemsize for a in (*args, *out_shape))
    *results, token = pl.pallas_call(
        body,
        grid_spec=pltpu.PrefetchScalarGridSpec(
            num_scalar_prefetch=1,
            grid=grid,
            in_specs=[*in_specs, pl.BlockSpec(memory_space=pl.ANY)],
            out_specs=[*out_specs, pl.BlockSpec((8, 128), lambda *_: (0, 0))],
            scratch_shapes=list(scratch),
        ),
        out_shape=[*out_shape, sds((8, 128), f32)],
        compiler_params=pltpu.CompilerParams(vmem_limit_bytes=VMEM_LIMIT),
        cost_estimate=pl.CostEstimate(flops=0 if brief else max(FLOOR, int(flops * COST)), bytes_accessed=0 if brief else int(moved * COST), transcendentals=0),
    )(info, *args, token)
    return (*results, token)


def hold(token, values, brief=False):
    def nothing(values_ref, token_ref, out_ref, token_out):
        token_out[...] = jnp.zeros_like(token_out)

    return pl.pallas_call(
        nothing,
        in_specs=[pl.BlockSpec(memory_space=pl.ANY)] * 2,
        out_specs=[pl.BlockSpec(memory_space=pl.ANY), pl.BlockSpec(memory_space=pltpu.VMEM)],
        out_shape=[sds(values.shape, values.dtype), sds((8, 128), f32)],
        input_output_aliases={0: 0},
        compiler_params=pltpu.CompilerParams(vmem_limit_bytes=VMEM_LIMIT),
        cost_estimate=pl.CostEstimate(flops=0 if brief else FLOOR, bytes_accessed=0, transcendentals=0),
    )(values, token)


def specs(frames, width, tile, blocks=0):
    def tile_of(j):
        return jnp.maximum(j - blocks, 0) if blocks else j

    whole = pl.BlockSpec((frames, width), lambda j, *_: (0, 0))
    vector = pl.BlockSpec((6, width), lambda j, *_: (0, 0))
    column = pl.BlockSpec((width, tile), lambda j, *_: (0, tile_of(j)))
    row = pl.BlockSpec((tile, width), lambda j, *_: (tile_of(j), 0))
    act = pl.BlockSpec((frames, tile), lambda j, *_: (0, tile_of(j)))
    table = pl.BlockSpec((frames, 2 * HEAD), lambda j, *_: (0, 0))
    logsum = pl.BlockSpec((8, frames), lambda j, *_: (tile_of(j), 0))
    return whole, vector, column, row, act, table, logsum


BLOCKS = 4


def widened(*tables):
    return tuple(jnp.concatenate([table[...], table[...]], axis=1) for table in tables)


def row_block(frames, width):
    return pl.BlockSpec((frames // BLOCKS, width), lambda j, *_: (jnp.minimum(j, BLOCKS - 1), 0))


def copies_block(frames, width, place):
    return pl.BlockSpec(
        (PLANE, frames // BLOCKS, width),
        lambda j, info: (0, jnp.clip(j - BLOCKS // 2 * info[place], 0, BLOCKS // 2 - 1), 0),
    )


def within(step, rows, r):
    return pl.ds(pl.multiple_of(step * rows + r.start, r.size), r.size)


def added(acc, term, result, first=0):
    step = pl.program_id(0)

    @pl.when(step == first)
    def _():
        acc[...] = term

    @pl.when(step != first)
    def _():
        acc[...] += term

    @pl.when(step == pl.num_programs(0) - 1)
    def _():
        result[...] = acc[...].astype(result.dtype)


def self_kernel(info, hid, norms, wq, wk, wv, wo, cos, lower, upper, grad, copies, grad_copies, q, k, v, att, logsum, part, acc, mask, normed):
    step, frames, block = pl.program_id(0), normed.shape[0], hid.shape[0]
    gain, shift = norms.at[0:1], norms.at[1:2]

    @pl.when(step == 0)
    def _():
        mask[...] = self_mask(info[0], frames)

    @pl.when(step < BLOCKS)
    def _():
        def rows(r):
            normed[within(step, block, r), :] = normed_rows(hid[r, :], gain[...], shift[...]).astype(low)

        over_rows(block, rows)

    @pl.when((step < BLOCKS) & (step * 2 // BLOCKS == info[3]))
    def _():
        mine = normed[pl.ds(pl.multiple_of(step * block, block), block), :]
        for chip in range(PLANE):
            copies[chip] = mine

    @pl.when(step < BLOCKS // 2)
    def _():
        grad_low = grad[...].astype(low)
        for chip in range(PLANE):
            grad_copies[chip] = grad_low

    @pl.when(step >= BLOCKS)
    def _():
        n = normed[...]
        tables = widened(cos, lower, upper)
        q[...] = turn(product_plain(n, wq[...]), *tables).astype(low)
        k[...] = turn(product_plain(n, wk[...]), *tables).astype(low)
        v[...] = product_plain(n, wv[...]).astype(low)
        attended = attend(q[...], k[...], v[...], mask[...], logsum)
        att[...] = attended
        added(acc, product_plain(attended, wo[...]), part, BLOCKS)


def self_forward(token, info, hid, norms, wq, wk, wv, wo, tables, grad, tile=4 * HEAD):
    frames, width = hid.shape
    columns = wq.shape[1]
    whole, vector, column, row, act, table, logsum = specs(frames, width, tile, BLOCKS)
    blocks = row_block(frames, width)
    here = frames // BLOCKS
    return ordered(
        self_kernel,
        token,
        (hid, norms, wq, wk, wv, wo, *tables, grad),
        [blocks, vector, column, column, column, row, table, table, table]
        + [
            pl.BlockSpec(
                (here, width),
                lambda j, info: (BLOCKS // 2 * info[3] + jnp.minimum(j, BLOCKS // 2 - 1), 0),
            )
        ],
        [
            copies_block(frames, width, 3),
            pl.BlockSpec((PLANE, here, width), lambda j, info: (0, jnp.minimum(j, BLOCKS // 2 - 1), 0)),
        ]
        + [act, act, act, act, logsum, whole],
        [sds((PLANE, frames // 2, width), low)] * 2
        + [sds((frames, columns), low)] * 4
        + [sds((columns // tile * 8, frames), f32), sds((frames, width), low)],
        (BLOCKS + columns // tile,),
        2 * frames * columns * (4 * width + 8 * frames),
        [
            pltpu.VMEM((frames, width), f32),
            pltpu.VMEM((frames, frames), f32),
            pltpu.VMEM((frames, width), low),
        ],
        info,
    )


def cross_kernel(info, hid, mine, other, norms, cq, ck, cv, co, total, normed, q, att, logsum, part, acc, kept):
    step, block = pl.program_id(0), hid.shape[0]
    gain, shift = norms.at[2:3], norms.at[3:4]

    @pl.when(step < BLOCKS)
    def _():
        def rows(r):
            x = hid[r, :] + (mine[r, :].astype(f32) + other[r, :].astype(f32))
            total[r, :] = x
            n = normed_rows(x, gain[...], shift[...]).astype(low)
            normed[r, :] = n
            kept[within(step, block, r), :] = n

        over_rows(block, rows)

    @pl.when(step >= BLOCKS)
    def _():
        q[...] = product_plain(kept[...], cq[...]).astype(low)
        attended = cross_attend(info, q[...], ck, cv, logsum)
        att[...] = attended
        added(acc, product_plain(attended, co[...]), part, BLOCKS)


def cross_forward(token, info, hid, mine, other, norms, cq, ck, cv, co, tile=4 * HEAD):
    frames, width = hid.shape
    columns, keys = cq.shape[1], ck.shape[0]
    whole, vector, column, row, act, table, logsum = specs(frames, width, tile, BLOCKS)
    key = pl.BlockSpec((keys, tile), lambda j, *_: (0, jnp.maximum(j - BLOCKS, 0)))
    blocks = row_block(frames, width)
    return ordered(
        cross_kernel,
        token,
        (hid, mine, other, norms, cq, ck, cv, co),
        [blocks, blocks, blocks, vector, column, key, key, row],
        [blocks, blocks, act, act, logsum, whole],
        [
            sds((frames, width), f32),
            sds((frames, width), low),
            sds((frames, columns), low),
            sds((frames, columns), low),
            sds((columns // tile * 8, frames), f32),
            sds((frames, width), low),
        ],
        (BLOCKS + columns // tile,),
        2 * frames * columns * (2 * width + 8 * keys),
        [pltpu.VMEM((frames, width), f32), pltpu.VMEM((frames, width), low)],
        info,
        brief=True,
    )


def norm_kernel(info, hid, mine, other, norms, total, normed, copies):
    gain, shift = norms.at[4:5], norms.at[5:6]

    def rows(r):
        x = hid[r, :] + (mine[r, :].astype(f32) + other[r, :].astype(f32))
        total[r, :] = x
        normed[r, :] = normed_rows(x, gain[...], shift[...]).astype(low)

    over_rows(hid.shape[0], rows)

    @pl.when(pl.program_id(0) * 2 // pl.num_programs(0) == info[3])
    def _():
        values = normed[...]
        for chip in range(PLANE):
            copies[chip] = values


def norm_forward(token, info, hid, mine, other, norms, block=128):
    frames, width = hid.shape
    blocks = frames // (2 * block)
    rows = pl.BlockSpec((block, width), lambda j, *_: (j, 0))
    vector = pl.BlockSpec((6, width), lambda j, *_: (0, 0))
    return ordered(
        norm_kernel,
        token,
        (hid, mine, other, norms),
        [rows, rows, rows, vector],
        [
            rows,
            rows,
            pl.BlockSpec(
                (PLANE, block, width),
                lambda j, info: (0, jnp.clip(j - blocks * info[3], 0, blocks - 1), 0),
            ),
        ],
        [sds((frames, width), f32), sds((frames, width), low), sds((PLANE, frames // 2, width), low)],
        (frames // block,),
        10 * frames * width,
        info=info,
        brief=True,
    )


def cross_back_kernel(info, x, mine, other, above, norms, co, q, ck, cv, att, logsum, cq, total, total_low, vectors, dq, dk, dv, part, acc, gain_acc, shift_acc, kept):
    norm_back_step(x, mine, other, above, norms.at[4:5], total, total_low, kept, vectors, gain_acc, shift_acc)

    @pl.when(pl.program_id(0) >= BLOCKS)
    def _():
        g = product_with_rows(kept[...], co[...]).astype(low)
        a, b, c = cross_attend_back(info, q[...], ck, cv, g, att[...], logsum[...])
        a = a.astype(low)
        dq[...] = a
        dk[...] = b.astype(low)
        dv[...] = c.astype(low)
        added(acc, product_with_rows(a, cq[...]), part, BLOCKS)


def cross_backward(token, info, x, mine, other, above, gain, co, q, ck, cv, att, logsums, cq, tile=4 * HEAD):
    frames, width = x.shape
    columns, keys = cq.shape[1], ck.shape[0]
    whole, vector, column, row, act, table, logsum = specs(frames, width, tile, BLOCKS)
    key = pl.BlockSpec((keys, tile), lambda j, *_: (0, jnp.maximum(j - BLOCKS, 0)))
    blocks = row_block(frames, width)
    two = pl.BlockSpec((2, width), lambda j, *_: (0, 0))
    return ordered(
        cross_back_kernel,
        token,
        (x, mine, other, above, gain, co, q, ck, cv, att, logsums, cq),
        [blocks, blocks, blocks, blocks, vector, row, act, key, key, act, logsum, column],
        [blocks, blocks, two, act, key, key, whole],
        [
            sds((frames, width), f32),
            sds((frames, width), low),
            sds((2, width), f32),
            sds((frames, columns), low),
            sds((keys, columns), low),
            sds((keys, columns), low),
            sds((frames, width), low),
        ],
        (BLOCKS + columns // tile,),
        2 * frames * columns * (2 * width + 20 * keys),
        [
            pltpu.VMEM((frames, width), f32),
            pltpu.VMEM((8, width), f32),
            pltpu.VMEM((8, width), f32),
            pltpu.VMEM((frames, width), low),
        ],
        info,
    )


def self_back_kernel(info, x, mine, other, above, norms, wo, q, k, v, att, logsum, wq, wk, wv, cos, lower, upper, total, total_low, vectors, grads, part, acc, mask, gain_acc, shift_acc, kept):
    step = pl.program_id(0)

    @pl.when(step == 0)
    def _():
        mask[...] = self_mask(info[0], kept.shape[0])

    norm_back_step(x, mine, other, above, norms.at[2:3], total, total_low, kept, vectors, gain_acc, shift_acc)

    @pl.when(step >= BLOCKS)
    def _():
        g = product_with_rows(kept[...], wo[...]).astype(low)
        a, b, c = attend_back(q[...], k[...], v[...], g, att[...], mask[...], logsum[...])
        tables = widened(cos, lower, upper)
        a = turn_back(a, *tables).astype(low)
        b = turn_back(b, *tables).astype(low)
        c = c.astype(low)
        for index, values in enumerate((a, b, c)):
            turned = values.T
            for quarter in range(PLANE):
                grads[quarter, index] = turned[quarter * HEAD : (quarter + 1) * HEAD]
        back = product_with_rows(a, wq[...]) + product_with_rows(b, wk[...])
        added(acc, back + product_with_rows(c, wv[...]), part, BLOCKS)


def self_backward(token, info, x, mine, other, above, gain, wo, q, k, v, att, logsums, wq, wk, wv, tables, tile=4 * HEAD):
    frames, width = x.shape
    columns = wq.shape[1]
    whole, vector, column, row, act, table, logsum = specs(frames, width, tile, BLOCKS)
    blocks = row_block(frames, width)
    two = pl.BlockSpec((2, width), lambda j, *_: (0, 0))
    heads = pl.BlockSpec(
        (PLANE, 3, HEAD, frames), lambda j, *_: (0, 0, jnp.maximum(j - BLOCKS, 0), 0)
    )
    return ordered(
        self_back_kernel,
        token,
        (x, mine, other, above, gain, wo, q, k, v, att, logsums, wq, wk, wv, *tables),
        [blocks] * 4
        + [vector, row, act, act, act, act, logsum, column, column, column, table, table, table],
        [blocks, blocks, two, heads, whole],
        [
            sds((frames, width), f32),
            sds((frames, width), low),
            sds((2, width), f32),
            sds((PLANE, 3, columns // PLANE, frames), low),
            sds((frames, width), low),
        ],
        (BLOCKS + columns // tile,),
        2 * frames * columns * (4 * width + 20 * frames),
        [
            pltpu.VMEM((frames, width), f32),
            pltpu.VMEM((frames, frames), f32),
            pltpu.VMEM((8, width), f32),
            pltpu.VMEM((8, width), f32),
            pltpu.VMEM((frames, width), low),
        ],
        info,
    )


def last_kernel(_, x, mine, other, above, norms, resid, sum_mine, sum_other, total, vectors, result, gain_acc, shift_acc):
    step = pl.program_id(0)
    gain = norms.at[0:1]

    @pl.when(step == 0)
    def _():
        gain_acc[...] = jnp.zeros_like(gain_acc)
        shift_acc[...] = jnp.zeros_like(shift_acc)

    def rows(r):
        e = mine[r, :].astype(f32) + other[r, :].astype(f32)
        total[r, :] = norm_back_rows(x[r, :], e, gain[...], above[r, :], gain_acc, shift_acc)
        result[r, :] = resid[r, :] + (sum_mine[r, :].astype(f32) + sum_other[r, :].astype(f32))

    over_rows(x.shape[0], rows)

    @pl.when(step == pl.num_programs(0) - 1)
    def _():
        vectors[0:1, :] = jnp.sum(gain_acc[...], axis=0, keepdims=True)
        vectors[1:2, :] = jnp.sum(shift_acc[...], axis=0, keepdims=True)


def last_backward(token, x, mine, other, above, gain, resid, sum_mine, sum_other, block=128):
    frames, width = x.shape
    rows = pl.BlockSpec((block, width), lambda j, *_: (j, 0))
    vector = pl.BlockSpec((6, width), lambda j, *_: (0, 0))
    two = pl.BlockSpec((2, width), lambda j, *_: (0, 0))
    return ordered(
        last_kernel,
        token,
        (x, mine, other, above, gain, resid, sum_mine, sum_other),
        [rows, rows, rows, rows, vector, rows, rows, rows],
        [rows, two, rows],
        [sds((frames, width), f32), sds((2, width), f32), sds((frames, width), f32)],
        (frames // block,),
        20 * frames * width,
        [pltpu.VMEM((8, width), f32), pltpu.VMEM((8, width), f32)],
        brief=True,
    )


def ff_kernel(_, in_ref, out_ref, gate_ref, up_ref, down_ref, sum_ref, back_ref, sum_acc, back_acc, out_low):
    @pl.when(pl.program_id(0) == 0)
    def _():
        out_low[...] = out_ref[...].astype(low)

    normed = in_ref[...]
    mixed, grad_gate, grad_up = ff_parts(
        product_plain(normed, gate_ref[...]),
        product_plain(normed, up_ref[...]),
        product_with_rows(out_low[...], down_ref[...]),
    )
    added(sum_acc, product_plain(mixed, down_ref[...]), sum_ref)
    added(
        back_acc,
        product_with_rows(grad_gate, gate_ref[...]) + product_with_rows(grad_up, up_ref[...]),
        back_ref,
    )


def ff_both(token, normed, grad_out, w_gate, w_up, w_down, tile=768):
    frames, width = normed.shape
    units = w_gate.shape[1]
    whole, _, column, row, *_ = specs(frames, width, tile)
    return ordered(
        ff_kernel,
        token,
        (normed, grad_out, w_gate, w_up, w_down),
        [whole, whole, column, column, row],
        [whole, whole],
        [sds((frames, width), low)] * 2,
        (units // tile,),
        12 * frames * width * units,
        [pltpu.VMEM((frames, width), f32)] * 2 + [pltpu.VMEM((frames, width), low)],
    )


def share_kernel(info, in_mine, in_other, out_mine, out_other, gate_ref, up_ref, down_ref, send_ref, keep_ref, acc):
    step = pl.program_id(1)
    normed = jnp.concatenate([in_mine[...], in_other[...]], axis=0)
    grad_out = jnp.concatenate([out_mine[...], out_other[...]], axis=0)
    mixed, grad_gate, grad_up = ff_parts(
        product_plain(normed, gate_ref[...]),
        product_plain(normed, up_ref[...]),
        product_with_rows(grad_out, down_ref[...]),
    )
    fresh = (
        product_over_rows(grad_out, mixed),
        product_over_rows(normed, grad_gate),
        product_over_rows(normed, grad_up),
    )
    for index, term in enumerate(fresh):

        @pl.when(step == 0)
        def _():
            acc[index] = term

        @pl.when(step != 0)
        def _():
            acc[index] += term

    @pl.when(step == pl.num_programs(1) - 1)
    def _():
        rows = send_ref.shape[2] // 3
        for pair in range(2):
            for index in range(3):
                for ref, parity in ((send_ref, 1 - info[5]), (keep_ref, info[5])):
                    start = pl.multiple_of((2 * pair + parity) * rows, rows)
                    ref[0, pair, index * rows : (index + 1) * rows] = acc[
                        index, pl.ds(start, rows), :
                    ].astype(ref.dtype)


def ff_share(token, info, normed, grad_out, w_gate, w_up, w_down, tile, first, count):
    frames, width = normed[0].shape
    chunk = frames // PLANE
    rows = pl.BlockSpec((chunk, width), lambda i, j, info: (j, 0))
    column = pl.BlockSpec((width, tile), lambda i, j, info: (0, info[4] + first + i))
    half = (LEVELS // 2, 3 * width // LEVELS, tile)
    return ordered(
        share_kernel,
        token,
        (*normed, *grad_out, w_gate, w_up, w_down),
        [rows] * 4
        + [column, column, pl.BlockSpec((tile, width), lambda i, j, info: (info[4] + first + i, 0))],
        [pl.BlockSpec((1, *half), lambda i, j, info: (i, 0, 0, 0))] * 2,
        [sds((count, *half), low)] * 2,
        (count, PLANE),
        24 * frames * width * tile * count,
        [pltpu.VMEM((3, width, tile), f32)],
        info,
    )


def weight_kernel(plan, sides_count, _, *refs):
    sides, columns = refs[:sides_count], refs[sides_count : sides_count + len(plan)]
    out = refs[sides_count + len(plan)]
    turned = refs[sides_count + len(plan) + 1 :]

    @pl.when(pl.program_id(0) == 0)
    def _():
        for side, ref in zip(sides, turned):
            ref[...] = side[...].T

    for (which, first), column in zip(plan, columns):
        product = product_plain(turned[which][...], column[...]).astype(low)
        rows = product.shape[0] // (PLANE * LEVELS)
        product = product.reshape(LEVELS, PLANE, rows, product.shape[1])
        for owner in range(PLANE):
            out[owner, :, first : first + rows, :] = product[:, owner]


def weight_products(token, sides, plan, columns, tile=256):
    width = columns[0].shape[1]
    rows = sum(sides[which].shape[1] for which, _ in plan) // (PLANE * LEVELS)
    return ordered(
        functools.partial(weight_kernel, plan, len(sides)),
        token,
        (*sides, *columns),
        [pl.BlockSpec(side.shape, lambda j, *_: (0, 0)) for side in sides]
        + [pl.BlockSpec((column.shape[0], tile), lambda j, *_: (0, j)) for column in columns],
        [pl.BlockSpec((PLANE, LEVELS, rows, tile), lambda j, *_: (0, 0, 0, j))],
        [sds((PLANE, LEVELS, rows, width), low)],
        (width // tile,),
        sum(2 * sides[w].shape[0] * sides[w].shape[1] * width for w, _ in plan),
        [pltpu.VMEM((side.shape[1], side.shape[0]), low) for side in sides],
        brief=len(sides) == 1,
    )


def plane_sum_kernel(info, got, send, keep):
    for ref, parity in ((send, 1 - info[5]), (keep, info[5])):
        total = got[0, 0, parity].astype(f32)
        for source in range(1, PLANE):
            total = total + got[source, 0, parity].astype(f32)
        ref[0] = total.astype(low)


def plane_sum(token, got, info):
    rows, width = got.shape[2:]
    out = pl.BlockSpec((1, rows, width), lambda j, *_: (j, 0, 0))
    return ordered(
        plane_sum_kernel,
        token,
        (got.reshape(PLANE, 2, 2, rows, width),),
        [pl.BlockSpec((PLANE, 1, 2, rows, width), lambda j, *_: (0, j, 0, 0, 0))],
        [out, out],
        [sds((2, rows, width), low)] * 2,
        (2,),
        0,
        info=info,
    )


def level_sum_kernel(_, keep_pass, got_pass, keep_own, got_own, passed, own):
    passed[...] = (keep_pass[0, 0].astype(f32) + got_pass[0, 0].astype(f32)).astype(low)
    own[...] = keep_own[0, 0].astype(f32) + got_own[0, 0].astype(f32)


def level_sum(token, keep, got, info):
    count, _, rows, width = keep.shape
    block = rows // 2 if rows % 32 == 0 else rows
    steps = rows // block
    off = pl.BlockSpec((1, 1, block, width), lambda i, j, info: (i, 1 - info[6], j, 0))
    own = pl.BlockSpec((1, 1, block, width), lambda i, j, info: (i, info[6], j, 0))
    out = pl.BlockSpec((block, width), lambda i, j, info: (i * steps + j, 0))
    return ordered(
        level_sum_kernel,
        token,
        (keep, got, keep, got),
        [off, off, own, own],
        [out, out],
        [sds((count * rows, width), low), sds((count * rows, width), f32)],
        (count, steps),
        0,
        info=info,
    )


def unit_pack_kernel(counts, _, *refs):
    owns, lasts, out = refs[:-1:2], refs[1:-1:2], refs[-1]
    step = pl.program_id(0)
    for own, last, (first, count) in zip(owns, lasts, counts):

        @pl.when((step >= first) & (step < first + count))
        def _():
            total = (own[...] + last[...].astype(f32)).astype(low)
            total = total.reshape(3, PLANE, out.shape[2], out.shape[3])
            for chip in range(PLANE):
                out[chip] = total[:, chip]


def unit_pack(token, sums, rows):
    tile = sums[0][0].shape[1]
    r = rows // (3 * PLANE)
    specs_in, counts, first = [], [], 0
    for own, _ in sums:
        count = own.shape[0] // rows

        def place(j, info, first=first, count=count):
            return (jnp.clip(j - first, 0, count - 1), 0)

        specs_in += [pl.BlockSpec((rows, tile), place)] * 2
        counts.append((first, count))
        first += count
    return ordered(
        functools.partial(unit_pack_kernel, counts),
        token,
        tuple(array for pair in sums for array in pair),
        specs_in,
        [pl.BlockSpec((PLANE, 3, r, tile), lambda j, *_: (0, 0, 0, j))],
        [sds((PLANE, 3, r, tile * first), low)],
        (first,),
        0,
    )


def unit_unpack_kernel(_, got, down, gate, up):
    down[...] = got[0, 0].astype(f32).T
    gate[...] = got[0, 1].astype(f32)
    up[...] = got[0, 2].astype(f32)


def unit_unpack(token, got):
    _, _, r, units = got.shape
    across = pl.BlockSpec((r, units), lambda j, *_: (0, j))
    return ordered(
        unit_unpack_kernel,
        token,
        (got,),
        [pl.BlockSpec((1, 3, r, units), lambda j, *_: (j, 0, 0, 0))],
        [pl.BlockSpec((units, r), lambda j, *_: (j, 0)), across, across],
        [sds((PLANE * units, r), f32)] + [sds((r, PLANE * units), f32)] * 2,
        (PLANE,),
        0,
    )


def head_pack_kernel(_, own, last, out):
    total = (own[...] + last[...].astype(f32)).T.astype(low)
    out[...] = total.reshape(out.shape)


def head_pack(token, own, last):
    features, columns = own.shape
    shape = (PLANE, columns // PLANE, features)
    return ordered(
        head_pack_kernel,
        token,
        (own, last),
        [pl.BlockSpec(own.shape, lambda j, *_: (0, 0))] * 2,
        [pl.BlockSpec(shape, lambda j, *_: (0, 0, 0))],
        [sds(shape, low)],
        (1,),
        0,
    )


def head_unpack_kernel(_, got, *outs):
    groups = got.shape[2] // (3 * HEAD)
    for index, out in enumerate(outs):
        pieces = []
        for group in range(groups):
            first = (index * groups + group) * HEAD
            pieces += [got[chip, :, first : first + HEAD] for chip in range(PLANE)]
        out[...] = jnp.concatenate(pieces, axis=1).astype(f32)


def head_unpack(token, got):
    chips, r, features = got.shape
    shape = (r, chips * features // 3)
    return ordered(
        head_unpack_kernel,
        token,
        (got,),
        [pl.BlockSpec(got.shape, lambda j, *_: (0, 0, 0))],
        [pl.BlockSpec(shape, lambda j, *_: (0, 0))] * 3,
        [sds(shape, f32)] * 3,
        (1,),
        0,
    )


def head_kernel(info, grads_mine, grads_other, in_mine, in_other, send, keep, acc):
    step = pl.program_id(0)
    rows = acc.shape[0]
    term = product_plain(grads_mine[0].reshape(rows, -1), in_mine[...]) + product_plain(
        grads_other[0].reshape(rows, -1), in_other[...]
    )

    @pl.when(step == 0)
    def _():
        acc[...] = term

    @pl.when(step != 0)
    def _():
        acc[...] += term

    @pl.when(step == pl.num_programs(0) - 1)
    def _():
        width = send.shape[2]
        for level in range(LEVELS):
            for ref, parity in ((send, 1 - info[5]), (keep, info[5])):

                @pl.when(parity == level % 2)
                def _():
                    ref[level // 2] = acc[:, level * width : (level + 1) * width].astype(low)


def head_products(token, info, grads, normed):
    _, three, features, frames = grads.shape
    width = normed[0].shape[1]
    chunk = normed[0].shape[0] // PLANE
    rows = pl.BlockSpec((chunk, width), lambda j, info: (j, 0))
    half = (LEVELS // 2, three * features, width // LEVELS)
    return ordered(
        head_kernel,
        token,
        (grads, grads, *normed),
        [
            pl.BlockSpec((1, three, features, chunk), lambda j, info: (j, 0, 0, info[3])),
            pl.BlockSpec((1, three, features, chunk), lambda j, info: (j, 0, 0, 1 - info[3])),
            rows,
            rows,
        ],
        [pl.BlockSpec(half, lambda j, info: (0, 0, 0))] * 2,
        [sds(half, low)] * 2,
        (PLANE,),
        2 * three * features * PLANE * frames * width,
        [pltpu.VMEM((three * features, width), f32)],
        info,
    )


def on_plane(
    hidden_in,
    out_grad,
    prompt_states,
    row_split,
    prompt_len,
    gain_attn,
    bias_attn,
    gain_cross,
    bias_cross,
    gain_ff,
    bias_ff,
    w_query,
    w_key,
    w_value,
    w_out,
    c_query,
    c_key,
    c_value,
    c_out,
    w_gate,
    w_up,
    w_down,
):
    frames, width = hidden_in.shape
    plane, level = lax.axis_index("dp") % PLANE, lax.axis_index("dp") // PLANE
    positions = jnp.arange(frames, dtype=jnp.int32)
    row_ids = (positions >= row_split[0]).astype(jnp.int32)
    tables = rotary_tables((positions - row_ids * row_split[0]).astype(f32), 2 * HEAD)

    tile = 256
    tiles = w_gate.shape[1] // (PLANE * tile)
    places = jnp.stack([lax.axis_index("tensor"), plane * tiles, level % 2, level // 2])
    info = jnp.concatenate([row_split, prompt_len, places])
    norms = jnp.stack([gain_attn, bias_attn, gain_cross, bias_cross, gain_ff, bias_ff])
    chips = [[PLANE * z + p for p in range(PLANE)] for z in range(LEVELS)]

    def swapped(part):
        return lax.ppermute(part, "tensor", [(0, 1), (1, 0)])

    def in_plane(values):
        shape = values.shape
        return lax.all_to_all(
            values, "dp", 0, 0, axis_index_groups=chips, tiled=True
        ).reshape(shape)

    def gathered(copies):
        return in_plane(copies.reshape(-1, width))

    def level_swap(values, mask):
        return lax.ppermute(values, "dp", pairs(mask))

    token = jnp.zeros((8, 128), f32)
    context = prompt_states.reshape(2 * PROMPT, prompt_states.shape[2])
    cross_key = product_plain(context, c_key).astype(low)
    cross_value = product_plain(context, c_value).astype(low)
    copies_one, copies, query, key, value, attended_one, logsum_one, part, token = self_forward(
        token,
        info,
        hidden_in,
        norms,
        w_query,
        w_key,
        w_value,
        w_out,
        tables,
        out_grad,
    )
    part_swapped = swapped(part)
    frames_out = gathered(copies)
    resid_one, input_two, cross_query, attended_two, logsum_two, part, token = cross_forward(
        token,
        info,
        hidden_in,
        part,
        part_swapped,
        norms,
        c_query,
        cross_key,
        cross_value,
        c_out,
    )
    part_swapped = swapped(part)
    resid_two, input_three, copies, token = norm_forward(
        token, info, resid_one, part, part_swapped, norms
    )
    frames_out, token = hold(token, frames_out)
    frames_in = gathered(copies)
    frames_out = (frames_out, swapped(frames_out))
    sum_part, back_part, token = ff_both(token, input_three, out_grad, w_gate, w_up, w_down)
    frames_in, token = hold(token, frames_in)
    frames_in = (frames_in, swapped(frames_in))
    back_swapped = swapped(back_part)
    copies_one, token = hold(token, copies_one)
    frames_one = gathered(copies_one)

    def share(token, index, count):
        return ff_share(token, info, frames_in, frames_out, w_gate, w_up, w_down, tile, index, count)

    send_a, keep_a, token = share(token, 0, 1)
    got_a = level_swap(send_a, PLANE)
    grad_two, grad_cross_out, vectors_ff, query_grad, key_grad, value_grad, part, token = cross_backward(
        token,
        info,
        resid_two,
        back_part,
        back_swapped,
        out_grad,
        norms,
        c_out,
        cross_query,
        cross_key,
        cross_value,
        attended_two,
        logsum_two,
        c_query,
    )
    part_swapped = swapped(part)
    r, c = width // 16, context.shape[1] // 16
    products, token = weight_products(
        token,
        [grad_cross_out, input_two, context],
        [(0, 0), (1, r), (2, 2 * r), (2, 2 * r + c)],
        [attended_two, query_grad, key_grad, value_grad],
    )
    frames_one, token = hold(token, frames_one)
    got_cross = in_plane(products)
    frames_one_other = swapped(frames_one)
    pass_a, own_a, token = level_sum(token, keep_a, got_a, info)
    last_a = level_swap(pass_a, 2 * PLANE)
    send_b, keep_b, token = share(token, 1, 1)
    got_b = level_swap(send_b, PLANE)
    frames_one_other, token = hold(token, frames_one_other, True)
    frames_one = (frames_one, frames_one_other)
    grad_one, grad_self_out, vectors_cross, grads, part, token = self_backward(
        token,
        info,
        resid_one,
        part,
        part_swapped,
        grad_two,
        norms,
        w_out,
        query,
        key,
        value,
        attended_one,
        logsum_one,
        w_query,
        w_key,
        w_value,
        tables,
    )
    last_a, token = hold(token, last_a, True)
    sum_part, token = hold(token, sum_part, True)
    sum_swapped, part_swapped = swapped(sum_part), swapped(part)
    pass_b, own_b, token = level_sum(token, keep_b, got_b, info)
    last_b = level_swap(pass_b, 2 * PLANE)
    send_c, keep_c, token = share(token, 2, tiles - 2)
    got_c = level_swap(send_c, PLANE)
    got_cross, token = hold(token, got_cross)
    grads, token = hold(token, grads)
    got_heads = in_plane(grads)
    products, token = weight_products(token, [grad_self_out], [(0, 0)], [attended_one])
    grad_hidden, vectors_attn, result, token = last_backward(
        token, hidden_in, part, part_swapped, grad_one, norms, resid_two, sum_part, sum_swapped
    )
    vectors = jnp.concatenate([vectors_attn, vectors_cross, vectors_ff])
    vectors_got = level_swap(vectors, 1)
    send_x, keep_x, token = plane_sum(token, got_cross, info)
    got_x = level_swap(send_x, PLANE)
    last_b, token = hold(token, last_b, True)
    pass_c, own_c, token = level_sum(token, keep_c, got_c, info)
    last_c = level_swap(pass_c, 2 * PLANE)
    vectors_got, token = hold(token, vectors_got, True)
    vectors = vectors + vectors_got
    vectors_got = level_swap(vectors, 2)
    got_heads, token = hold(token, got_heads)
    send_h, keep_h, token = head_products(token, info, got_heads, frames_one)
    got_h = level_swap(send_h, PLANE)
    products, token = hold(token, products)
    got_out = in_plane(products)
    last_c, token = hold(token, last_c, True)
    units, token = unit_pack(
        token, [(own_a, last_a), (own_b, last_b), (own_c, last_c)], 3 * width // LEVELS
    )
    vectors_got, token = hold(token, vectors_got, True)
    vectors = vectors + vectors_got
    vectors_got = level_swap(vectors, PLANE)
    pass_h, own_h, token = level_sum(token, keep_h[None], got_h[None], info)
    last_h = level_swap(pass_h, 2 * PLANE)
    got_out, token = hold(token, got_out)
    units, token = hold(token, units, True)
    units = in_plane(units)
    send_o, keep_o, token = plane_sum(token, got_out, info)
    got_o = level_swap(send_o, PLANE)
    pass_x, own_x, token = level_sum(token, keep_x[None], got_x[None], info)
    last_x = level_swap(pass_x, 2 * PLANE)
    vectors_got, token = hold(token, vectors_got, True)
    vectors = vectors + vectors_got
    vectors_got = level_swap(vectors, 2 * PLANE)
    pass_o, own_o, token = level_sum(token, keep_o[None], got_o[None], info)
    last_o = level_swap(pass_o, 2 * PLANE)
    heads, token = head_pack(token, own_h, last_h)
    units, token = hold(token, units)
    heads, token = hold(token, heads, True)
    heads = in_plane(heads)
    grad_w_down, grad_w_gate, grad_w_up, token = unit_unpack(token, units)
    last_x, token = hold(token, last_x)
    cross = add_low(own_x, last_x)
    vectors_got, token = hold(token, vectors_got)
    vectors = own_share(vectors + vectors_got)
    heads, token = hold(token, heads)
    grad_w_query, grad_w_key, grad_w_value, token = head_unpack(token, heads)
    return (
        result,
        grad_hidden,
        *(vectors[index] for index in range(6)),
        grad_w_query,
        grad_w_key,
        grad_w_value,
        add_low(own_o, last_o).T,
        cross[r : 2 * r],
        cross[2 * r : 2 * r + c],
        cross[2 * r + c :],
        cross[:r].T,
        grad_w_gate,
        grad_w_up,
        grad_w_down,
    )


def on_any(
    hidden_in,
    out_grad,
    prompt_states,
    row_split,
    prompt_len,
    gain_attn,
    bias_attn,
    gain_cross,
    bias_cross,
    gain_ff,
    bias_ff,
    w_query,
    w_key,
    w_value,
    w_out,
    c_query,
    c_key,
    c_value,
    c_out,
    w_gate,
    w_up,
    w_down,
):
    frame_count = hidden_in.shape[0]
    positions = jnp.arange(frame_count, dtype=jnp.int32)
    split_here = row_split[0]
    row_ids = (positions >= split_here).astype(jnp.int32)
    tables = rotary_tables((positions - row_ids * split_here).astype(jnp.float32), w_query.shape[1])
    key_index = jnp.arange(2 * PROMPT, dtype=jnp.int32)
    key_rows = key_index // PROMPT
    key_live = key_index % PROMPT < jnp.where(key_rows == 0, prompt_len[0], prompt_len[1])
    self_ok = row_ids[:, None] == row_ids[None, :]
    cross_ok = (row_ids[:, None] == key_rows[None, :]) & key_live[None, :]

    normed, scaled_one, inverse_one = normalize(hidden_in, gain_attn, bias_attn)
    input_one = normed.astype(low)
    query_one = rotate(product_plain(input_one, w_query), tables).astype(low)
    key_one = rotate(product_plain(input_one, w_key), tables).astype(low)
    value_one = product_plain(input_one, w_value).astype(low)
    attended_one, logsum_one = attend_forward(query_one, heads_of(key_one), heads_of(value_one), self_ok)
    resid_one = hidden_in + swap_sum(product_plain(attended_one, w_out))

    normed, scaled_two, inverse_two = normalize(resid_one, gain_cross, bias_cross)
    input_two = normed.astype(low)
    cross_query = product_plain(input_two, c_query).astype(low)
    context_flat = prompt_states.reshape(2 * PROMPT, prompt_states.shape[2])
    cross_key = product_plain(context_flat, c_key).astype(low)
    cross_value = product_plain(context_flat, c_value).astype(low)
    attended_two, logsum_two = attend_forward(
        cross_query, heads_of(cross_key), heads_of(cross_value), cross_ok
    )
    resid_two = resid_one + swap_sum(product_plain(attended_two, c_out))

    normed, scaled_three, inverse_three = normalize(resid_two, gain_ff, bias_ff)
    input_three = normed.astype(low)
    gate_pre = product_plain(input_three, w_gate)
    up_pre = product_plain(input_three, w_up)
    sigmoid_gate = jax.nn.sigmoid(gate_pre)
    mixed_low = (gate_pre * sigmoid_gate * up_pre).astype(low)
    result = resid_two + swap_sum(product_plain(mixed_low, w_down))

    grad_ff_out = out_grad.astype(low)
    grad_w_down = generic_sum(grad_ff_out, mixed_low).T
    grad_mixed = product_with_rows(grad_ff_out, w_down)
    grad_gate = (
        grad_mixed * up_pre * sigmoid_gate * (1.0 + gate_pre * (1.0 - sigmoid_gate))
    ).astype(low)
    grad_up = (grad_mixed * gate_pre * sigmoid_gate).astype(low)
    grad_w_gate = generic_sum(input_three, grad_gate)
    grad_w_up = generic_sum(input_three, grad_up)
    normed_grad_three = swap_sum(
        product_with_rows(grad_gate, w_gate) + product_with_rows(grad_up, w_up)
    )
    back_three, grad_gain_ff, grad_bias_ff = normalize_back(
        normed_grad_three, scaled_three, inverse_three, gain_ff
    )
    grad_two = out_grad + back_three
    grad_cross_out = grad_two.astype(low)
    grad_c_out = generic_sum(grad_cross_out, attended_two).T
    grad_attended_two = product_with_rows(grad_cross_out, c_out).astype(low)
    cross_query_grad, cross_key_grad, cross_value_grad = attend_backward(
        cross_query,
        heads_of(cross_key),
        heads_of(cross_value),
        cross_ok,
        grad_attended_two,
        logsum_two,
    )
    cross_query_grad = cross_query_grad.astype(low)
    cross_key_grad = cross_key_grad.astype(low)
    cross_value_grad = cross_value_grad.astype(low)
    grad_c_query = generic_sum(input_two, cross_query_grad)
    grad_c_key = generic_sum(context_flat, cross_key_grad)
    grad_c_value = generic_sum(context_flat, cross_value_grad)
    normed_grad_two = swap_sum(product_with_rows(cross_query_grad, c_query))
    back_two, grad_gain_cross, grad_bias_cross = normalize_back(
        normed_grad_two, scaled_two, inverse_two, gain_cross
    )
    grad_one = grad_two + back_two
    grad_self_out = grad_one.astype(low)
    grad_w_out = generic_sum(grad_self_out, attended_one).T
    grad_attended_one = product_with_rows(grad_self_out, w_out).astype(low)
    query_grad, key_grad, value_grad = attend_backward(
        query_one, heads_of(key_one), heads_of(value_one), self_ok, grad_attended_one, logsum_one
    )
    query_grad = rotate_back(query_grad, tables).astype(low)
    key_grad = rotate_back(key_grad, tables).astype(low)
    value_grad = value_grad.astype(low)
    grad_w_query = generic_sum(input_one, query_grad)
    grad_w_key = generic_sum(input_one, key_grad)
    grad_w_value = generic_sum(input_one, value_grad)
    normed_grad_one = swap_sum(
        product_with_rows(query_grad, w_query)
        + product_with_rows(key_grad, w_key)
        + product_with_rows(value_grad, w_value)
    )
    back_one, grad_gain_attn, grad_bias_attn = normalize_back(
        normed_grad_one, scaled_one, inverse_one, gain_attn
    )
    grad_hidden = grad_one + back_one
    vectors = lax.psum(
        jnp.stack(
            [
                grad_gain_attn,
                grad_bias_attn,
                grad_gain_cross,
                grad_bias_cross,
                grad_gain_ff,
                grad_bias_ff,
            ]
        ),
        "dp",
    )
    vectors = own_share(vectors)
    return (
        result,
        grad_hidden,
        vectors[0],
        vectors[1],
        vectors[2],
        vectors[3],
        vectors[4],
        vectors[5],
        grad_w_query,
        grad_w_key,
        grad_w_value,
        grad_w_out,
        grad_c_query,
        grad_c_key,
        grad_c_value,
        grad_c_out,
        grad_w_gate,
        grad_w_up,
        grad_w_down,
    )


def solution(mesh):
    in_specs = (
        P("dp", None),
        P("dp", None),
        P("dp", None, None),
        P("dp"),
        P("dp"),
        P(),
        P(),
        P(),
        P(),
        P(),
        P(),
        P(None, "tensor"),
        P(None, "tensor"),
        P(None, "tensor"),
        P("tensor", None),
        P(None, "tensor"),
        P(None, "tensor"),
        P(None, "tensor"),
        P("tensor", None),
        P(None, "tensor"),
        P(None, "tensor"),
        P("tensor", None),
    )
    out_specs = (
        P("dp", None),
        P("dp", None),
        P(("dp", "tensor")),
        P(("dp", "tensor")),
        P(("dp", "tensor")),
        P(("dp", "tensor")),
        P(("dp", "tensor")),
        P(("dp", "tensor")),
        P("dp", "tensor"),
        P("dp", "tensor"),
        P("dp", "tensor"),
        P("tensor", "dp"),
        P("dp", "tensor"),
        P("dp", "tensor"),
        P("dp", "tensor"),
        P("tensor", "dp"),
        P("dp", "tensor"),
        P("dp", "tensor"),
        P("tensor", "dp"),
    )
    known = mesh.shape["dp"] == PLANE * LEVELS and mesh.shape["tensor"] == 2
    return jax.shard_map(
        on_plane if known else on_any, mesh=mesh, in_specs=in_specs, out_specs=out_specs, check_vma=False
    )
```

```python
import functools
import math

import jax
import jax.numpy as jnp
from jax import lax
from jax.experimental import pallas as pl
from jax.experimental.pallas import tpu as pltpu
from jax.sharding import PartitionSpec as P

PROMPT = 128
HEAD = 64
PLANE = 4
LEVELS = 4
VMEM_LIMIT = 62 * 2**20
COST = 3
FLOOR = 15 * 10**9

low = jnp.bfloat16
f32 = jnp.float32
sds = jax.ShapeDtypeStruct


norm_eps = 1e-05
score_scale = 0.125
masked_score = -1e30


def product_plain(left_side, right_side):
    return jnp.dot(left_side, right_side, preferred_element_type=jnp.float32)


def product_over_rows(left_side, right_side):
    return lax.dot_general(
        left_side, right_side, (((0,), (0,)), ((), ())), preferred_element_type=jnp.float32
    )


def product_with_rows(left_side, right_side):
    return lax.dot_general(
        left_side, right_side, (((1,), (1,)), ((), ())), preferred_element_type=jnp.float32
    )


def rotary_tables(positions, width):
    dim_index = jnp.arange(width) % HEAD
    freq_index = (dim_index % 16).astype(jnp.float32)
    inverse_freq = jnp.exp(freq_index * (-math.log(10000.0) / 16.0))
    angles = positions[:, None] * inverse_freq[None, :]
    cosine = jnp.cos(angles)
    sine_part = jnp.sin(angles)
    cos_table = jnp.where(dim_index < 32, cosine, 1.0)
    sin_lower = jnp.where(dim_index < 16, -sine_part, 0.0)
    sin_upper = jnp.where((dim_index >= 16) & (dim_index < 32), sine_part, 0.0)
    return (cos_table, sin_lower, sin_upper)


def rotate(values, tables):
    cos_table, sin_lower, sin_upper = tables
    return (
        values * cos_table
        + jnp.roll(values, -16, axis=1) * sin_lower
        + jnp.roll(values, 16, axis=1) * sin_upper
    )


def rotate_back(incoming, tables):
    cos_table, sin_lower, sin_upper = tables
    return (
        incoming * cos_table
        + jnp.roll(incoming * sin_lower, 16, axis=1)
        + jnp.roll(incoming * sin_upper, -16, axis=1)
    )


def normalize(values, norm_gain, norm_shift):
    average = jnp.mean(values, axis=-1, keepdims=True)
    centered = values - average
    variance = jnp.mean(centered * centered, axis=-1, keepdims=True)
    inverse = lax.rsqrt(variance + norm_eps)
    scaled = centered * inverse
    return (scaled * norm_gain + norm_shift, scaled, inverse)


def normalize_back(incoming, scaled, inverse, norm_gain):
    grad_gain = jnp.sum(incoming * scaled, axis=0)
    grad_shift = jnp.sum(incoming, axis=0)
    weighted = incoming * norm_gain
    grad_input = inverse * (
        weighted
        - jnp.mean(weighted, axis=-1, keepdims=True)
        - scaled * jnp.mean(weighted * scaled, axis=-1, keepdims=True)
    )
    return (grad_input, grad_gain, grad_shift)


def heads_of(values):
    return values.reshape(values.shape[0], values.shape[1] // HEAD, HEAD)


def attend_forward(query_block, key_heads, value_heads, allowed):
    query_heads = heads_of(query_block)
    scores = (
        jnp.einsum("qhd,khd->hqk", query_heads, key_heads, preferred_element_type=jnp.float32)
        * score_scale
    )
    scores = jnp.where(allowed[None], scores, masked_score)
    largest = jnp.max(scores, axis=-1, keepdims=True)
    exp_scores = jnp.exp(scores - largest)
    totals = jnp.sum(exp_scores, axis=-1, keepdims=True)
    soft_weights = (exp_scores / totals).astype(jnp.bfloat16)
    mixed_heads = jnp.einsum(
        "hqk,khd->qhd", soft_weights, value_heads, preferred_element_type=jnp.float32
    )
    mixed_flat = mixed_heads.reshape(query_block.shape[0], query_block.shape[1]).astype(
        jnp.bfloat16
    )
    return (mixed_flat, largest[..., 0] + jnp.log(totals[..., 0]))


def attend_backward(query_block, key_heads, value_heads, allowed, grad_block, logsum_block):
    query_heads = heads_of(query_block)
    grad_heads = heads_of(grad_block)
    scores = (
        jnp.einsum("qhd,khd->hqk", query_heads, key_heads, preferred_element_type=jnp.float32)
        * score_scale
    )
    scores = jnp.where(allowed[None], scores, masked_score)
    soft_weights = jnp.exp(scores - logsum_block[..., None])
    grad_weights = jnp.einsum(
        "qhd,khd->hqk", grad_heads, value_heads, preferred_element_type=jnp.float32
    )
    inner_sum = jnp.sum(soft_weights * grad_weights, axis=-1, keepdims=True)
    grad_scores = (soft_weights * (grad_weights - inner_sum)).astype(jnp.bfloat16)
    grad_query = (
        jnp.einsum("hqk,khd->qhd", grad_scores, key_heads, preferred_element_type=jnp.float32)
        * score_scale
    )
    grad_key = (
        jnp.einsum("hqk,qhd->khd", grad_scores, query_heads, preferred_element_type=jnp.float32)
        * score_scale
    )
    grad_value = jnp.einsum(
        "hqk,qhd->khd",
        soft_weights.astype(jnp.bfloat16),
        grad_heads,
        preferred_element_type=jnp.float32,
    )
    return (
        grad_query.reshape(query_block.shape),
        grad_key.reshape(grad_key.shape[0], -1),
        grad_value.reshape(grad_value.shape[0], -1),
    )


def swap_sum(partial):
    low = partial.astype(jnp.bfloat16)
    if lax.axis_size("tensor") == 2:
        other = lax.ppermute(low, "tensor", [(0, 1), (1, 0)])
        return low.astype(jnp.float32) + other.astype(jnp.float32)
    return lax.psum(low, "tensor").astype(jnp.float32)


def pairs(mask):
    return [(i, i ^ mask) for i in range(16)]


def own_share(vectors):
    share = vectors.shape[1] // (lax.axis_size("dp") * lax.axis_size("tensor"))
    index = lax.axis_index("dp") * lax.axis_size("tensor") + lax.axis_index("tensor")
    return lax.dynamic_slice_in_dim(vectors, index * share, share, 1)


def generic_sum(rows_side, column_side):
    return lax.psum_scatter(
        product_over_rows(rows_side, column_side).astype(jnp.bfloat16),
        "dp",
        scatter_dimension=0,
        tiled=True,
    ).astype(jnp.float32)


def add_low(*terms):
    total = terms[0].astype(jnp.float32)
    for term in terms[1:]:
        total = total + term.astype(jnp.float32)
    return total


def ff_parts(gate, up, grad_mixed):
    sig = 0.5 * jnp.tanh(0.5 * gate) + 0.5
    act = gate * sig
    return (
        (act * up).astype(low),
        (grad_mixed * up * sig * (1.0 + gate * (1.0 - sig))).astype(low),
        (grad_mixed * act).astype(low),
    )


def turn(values, cos, lower, upper):
    width = values.shape[1]
    return (values * cos + pltpu.roll(values, width - 16, 1) * lower + pltpu.roll(values, 16, 1) * upper)

def turn_back(values, cos, lower, upper):
    width = values.shape[1]
    return (values * cos + pltpu.roll(values * lower, 16, 1) + pltpu.roll(values * upper, width - 16, 1))

def normed_rows(values, gain, shift):
    average = jnp.mean(values, axis=-1, keepdims=True)
    centered = values - average
    variance = jnp.mean(centered * centered, axis=-1, keepdims=True)
    return centered * lax.rsqrt(variance + norm_eps) * gain + shift

def over_rows(rows, body, chunk=32):
    @pl.loop(0, rows // chunk, unroll=min(4, rows // chunk))
    def _(i):
        body(pl.ds(pl.multiple_of(i * chunk, chunk), chunk))

def attend(q, k, v, mask, lse_ref):
    q_turned = (q * jnp.bfloat16(0.125)).T
    v_turned = v.T
    heads = [slice(h * HEAD, (h + 1) * HEAD) for h in range(q.shape[1] // HEAD)]
    scores = [product_plain(k[:, c], q_turned[c, :]) for c in heads]
    weights, scales = [], []
    for h, s in enumerate(scores):
        s = s + mask
        m = jnp.max(s, axis=0, keepdims=True)
        e = jnp.exp(s - m)
        total = jnp.sum(e, axis=0, keepdims=True)
        weights.append(e.astype(low))
        scales.append(1.0 / total)
        lse_ref[h : h + 1, :] = m + jnp.log(total)
    outs = [product_plain(v_turned[c, :], e) * x for c, e, x in zip(heads, weights, scales)]
    return jnp.concatenate(outs, axis=0).T.astype(low)


def attend_back(q, k, v, g, att, mask, lse):
    scaled = q * jnp.bfloat16(0.125)
    q_turned = scaled.T
    g_turned = g.T
    k_turned = k.T
    weighted = g_turned.astype(f32) * att.T.astype(f32)
    dq, dk, dv = [], [], []
    for h in range(q.shape[1] // HEAD):
        c = slice(h * HEAD, (h + 1) * HEAD)
        p = jnp.exp(product_plain(k[:, c], q_turned[c, :]) + (mask - lse[h : h + 1, :]))
        dp = product_plain(v[:, c], g_turned[c, :])
        inner = jnp.sum(weighted[c, :], axis=0, keepdims=True)
        ds = (p * (dp - inner)).astype(low)
        dq.append(product_plain(k_turned[c, :], ds))
        dk.append(product_plain(ds, scaled[:, c]))
        dv.append(product_plain(p.astype(low), g[:, c]))
    return (
        jnp.concatenate(dq, axis=0).T * 0.125,
        jnp.concatenate(dk, axis=1),
        jnp.concatenate(dv, axis=1),
    )


def self_mask(split, T):
    r=lax.broadcasted_iota(jnp.int32,(T,T),0)>=split
    c=lax.broadcasted_iota(jnp.int32,(T,T),1)>=split
    return jnp.where(r==c,0.0,masked_score).astype(f32)

def key_half(info, index, frames, keys):
    second = info[0] < frames
    start = jnp.where(second, keys // 2, 0) if index == 1 else 0
    live = jnp.where(second, info[2], info[1]) if index == 1 else info[1]
    return start, live


def half_mask(live, keys, frames):
    return jnp.where(
        lax.broadcasted_iota(jnp.int32, (keys, frames), 0) < live, 0.0, masked_score
    ).astype(f32)


def key_blocks(info, k_ref, v_ref, frames):
    keys = k_ref.shape[0]
    k, v, masks = [], [], []
    for index in range(2):
        start, live = key_half(info, index, frames, keys)
        here = pl.ds(start if index == 0 else pl.multiple_of(start, keys // 2), keys // 2)
        k.append(k_ref[here, :])
        v.append(v_ref[here, :])
        masks.append(half_mask(live, keys // 2, frames // 2))
    return k, v, jnp.concatenate(masks, axis=1)


def cross_attend(info, q, k_ref, v_ref, lse_ref):
    half = q.shape[0] // 2
    q_turned = (q * jnp.bfloat16(0.125)).T
    k, v, mask = key_blocks(info, k_ref, v_ref, 2 * half)
    v_turned = [values.T for values in v]
    outs = []
    for h in range(q.shape[1] // HEAD):
        c = slice(h * HEAD, (h + 1) * HEAD)
        s = [product_plain(k[i][:, c], q_turned[c, i * half : (i + 1) * half]) for i in range(2)]
        s = jnp.concatenate(s, axis=1) + mask
        m = jnp.max(s, axis=0, keepdims=True)
        e = jnp.exp(s - m)
        total = jnp.sum(e, axis=0, keepdims=True)
        lse_ref[h : h + 1, :] = m + jnp.log(total)
        e = e.astype(low)
        o = [product_plain(v_turned[i][c, :], e[:, i * half : (i + 1) * half]) for i in range(2)]
        outs.append(jnp.concatenate(o, axis=1) * (1.0 / total))
    return jnp.concatenate(outs, axis=0).T.astype(low)


def cross_attend_back(info, q, k_ref, v_ref, g, att, lse):
    half = q.shape[0] // 2
    scaled = q * jnp.bfloat16(0.125)
    q_turned = scaled.T
    g_turned = g.T
    weighted = g_turned.astype(f32) * att.T.astype(f32)
    k, v, mask = key_blocks(info, k_ref, v_ref, 2 * half)
    k_turned = [values.T for values in k]
    parts = [slice(0, half), slice(half, 2 * half)]
    dq, dk, dv = [], [[], []], [[], []]
    for h in range(q.shape[1] // HEAD):
        c = slice(h * HEAD, (h + 1) * HEAD)
        s = [product_plain(k[i][:, c], q_turned[c, parts[i]]) for i in range(2)]
        dp = [product_plain(v[i][:, c], g_turned[c, parts[i]]) for i in range(2)]
        p = jnp.exp(jnp.concatenate(s, axis=1) + (mask - lse[h : h + 1, :]))
        inner = jnp.sum(weighted[c, :], axis=0, keepdims=True)
        ds = (p * (jnp.concatenate(dp, axis=1) - inner)).astype(low)
        p = p.astype(low)
        dq.append(
            jnp.concatenate(
                [product_plain(k_turned[i][c, :], ds[:, parts[i]]) for i in range(2)], axis=1
            )
        )
        for i in range(2):
            dk[i].append(product_plain(ds[:, parts[i]], scaled[parts[i], c]))
            dv[i].append(product_plain(p[:, parts[i]], g[parts[i], c]))
    second = (info[0] < 2 * half).astype(f32)

    def by_row(halves):
        first, last = (jnp.concatenate(half, axis=1) for half in halves)
        return jnp.concatenate([first + last * (1.0 - second), last * second], axis=0)

    return jnp.concatenate(dq, axis=0).T * 0.125, by_row(dk), by_row(dv)


def norm_back_rows(x,e,gain,above,gain_acc,shift_acc):
    average=jnp.mean(x,axis=-1,keepdims=True)
    centered=x-average
    variance=jnp.mean(centered*centered,axis=-1,keepdims=True)
    inverse=lax.rsqrt(variance+norm_eps)
    n=centered*inverse
    en=e*n
    w=e*gain
    mean_w=jnp.mean(w,axis=-1,keepdims=True)
    mean_wn=jnp.mean(en*gain,axis=-1,keepdims=True)
    fold=lambda t: jnp.sum(t.reshape(t.shape[0]//8,8,t.shape[1]),axis=0)
    gain_acc[...]+=fold(en)
    shift_acc[...]+=fold(e)
    return above+inverse*(w-mean_w-n*mean_wn)

def norm_back_step(x, mine, other, above, gain, total, total_low, kept, vectors, gain_acc, shift_acc):
    step, block = pl.program_id(0), x.shape[0]

    @pl.when(step == 0)
    def _():
        gain_acc[...] = jnp.zeros_like(gain_acc)
        shift_acc[...] = jnp.zeros_like(shift_acc)

    @pl.when(step < BLOCKS)
    def _():
        def rows(r):
            e = mine[r, :].astype(f32) + other[r, :].astype(f32)
            t = norm_back_rows(x[r, :], e, gain[...], above[r, :], gain_acc, shift_acc)
            total[r, :] = t
            total_low[r, :] = t.astype(low)
            kept[within(step, block, r), :] = t.astype(low)

        over_rows(block, rows)

    @pl.when(step == BLOCKS - 1)
    def _():
        vectors[0:1, :] = jnp.sum(gain_acc[...], axis=0, keepdims=True)
        vectors[1:2, :] = jnp.sum(shift_acc[...], axis=0, keepdims=True)


def ordered(kernel, token, args, in_specs, out_specs, out_shape, grid, flops, scratch=(), info=None, brief=False):
    if info is None:
        info = jnp.zeros((1,), jnp.int32)
    inputs, outputs = len(args), len(out_shape)

    def body(info_ref, *refs):
        token_ref = refs[inputs + 1 + outputs]

        @pl.when(functools.reduce(jnp.logical_and, [pl.program_id(i) == 0 for i in range(len(grid))]))
        def _():
            token_ref[...] = jnp.zeros_like(token_ref)

        kernel(
            info_ref,
            *refs[:inputs],
            *refs[inputs + 1 : inputs + 1 + outputs],
            *refs[inputs + 2 + outputs :],
        )

    moved = sum(math.prod(a.shape) * a.dtype.itemsize for a in (*args, *out_shape))
    *results, token = pl.pallas_call(
        body,
        grid_spec=pltpu.PrefetchScalarGridSpec(
            num_scalar_prefetch=1,
            grid=grid,
            in_specs=[*in_specs, pl.BlockSpec(memory_space=pl.ANY)],
            out_specs=[*out_specs, pl.BlockSpec((8, 128), lambda *_: (0, 0))],
            scratch_shapes=list(scratch),
        ),
        out_shape=[*out_shape, sds((8, 128), f32)],
        compiler_params=pltpu.CompilerParams(vmem_limit_bytes=VMEM_LIMIT),
        cost_estimate=pl.CostEstimate(flops=0 if brief else max(FLOOR, int(flops * COST)), bytes_accessed=0 if brief else int(moved * COST), transcendentals=0),
    )(info, *args, token)
    return (*results, token)


def hold(token, values, brief=False):
    def nothing(values_ref, token_ref, out_ref, token_out):
        token_out[...] = jnp.zeros_like(token_out)

    return pl.pallas_call(
        nothing,
        in_specs=[pl.BlockSpec(memory_space=pl.ANY)] * 2,
        out_specs=[pl.BlockSpec(memory_space=pl.ANY), pl.BlockSpec(memory_space=pltpu.VMEM)],
        out_shape=[sds(values.shape, values.dtype), sds((8, 128), f32)],
        input_output_aliases={0: 0},
        compiler_params=pltpu.CompilerParams(vmem_limit_bytes=VMEM_LIMIT),
        cost_estimate=pl.CostEstimate(flops=0 if brief else FLOOR, bytes_accessed=0, transcendentals=0),
    )(values, token)


def norm_row(norms, index):
    width = norms.shape[1] // 6
    return norms.at[:, index * width : (index + 1) * width]


def specs(frames, width, tile, blocks=0):
    def tile_of(j):
        return jnp.maximum(j - blocks, 0) if blocks else j

    whole = pl.BlockSpec((frames, width), lambda j, *_: (0, 0))
    vector = pl.BlockSpec((1, 6 * width), lambda j, *_: (0, 0))
    column = pl.BlockSpec((width, tile), lambda j, *_: (0, tile_of(j)))
    row = pl.BlockSpec((tile, width), lambda j, *_: (tile_of(j), 0))
    act = pl.BlockSpec((frames, tile), lambda j, *_: (0, tile_of(j)))
    table = pl.BlockSpec((frames, 2 * HEAD), lambda j, *_: (0, 0))
    logsum = pl.BlockSpec((8, frames), lambda j, *_: (tile_of(j), 0))
    return whole, vector, column, row, act, table, logsum


BLOCKS = 4


def widened(*tables):
    return tuple(jnp.concatenate([table[...], table[...]], axis=1) for table in tables)


def row_block(frames, width):
    return pl.BlockSpec((frames // BLOCKS, width), lambda j, *_: (jnp.minimum(j, BLOCKS - 1), 0))


def copies_block(frames, width, place):
    return pl.BlockSpec(
        (PLANE, frames // BLOCKS, width),
        lambda j, info: (0, jnp.clip(j - BLOCKS // 2 * info[place], 0, BLOCKS // 2 - 1), 0),
    )


def within(step, rows, r):
    return pl.ds(pl.multiple_of(step * rows + r.start, r.size), r.size)


def added(acc, term, result, first=0):
    step = pl.program_id(0)

    @pl.when(step == first)
    def _():
        acc[...] = term

    @pl.when(step != first)
    def _():
        acc[...] += term

    @pl.when(step == pl.num_programs(0) - 1)
    def _():
        result[...] = acc[...].astype(result.dtype)


def self_kernel(info, hid, norms, wq, wk, wv, wo, cos, lower, upper, grad, copies, grad_copies, q, k, v, att, logsum, part, acc, mask, normed):
    step, frames, block = pl.program_id(0), normed.shape[0], hid.shape[0]
    gain, shift = norm_row(norms, 0), norm_row(norms, 1)

    @pl.when(step == 0)
    def _():
        mask[...] = self_mask(info[0], frames)

    @pl.when(step < BLOCKS)
    def _():
        def rows(r):
            normed[within(step, block, r), :] = normed_rows(hid[r, :], gain[...], shift[...]).astype(low)

        over_rows(block, rows)

    @pl.when((step < BLOCKS) & (step * 2 // BLOCKS == info[3]))
    def _():
        mine = normed[pl.ds(pl.multiple_of(step * block, block), block), :]
        for chip in range(PLANE):
            copies[chip] = mine

    @pl.when(step < BLOCKS // 2)
    def _():
        grad_low = grad[...].astype(low)
        for chip in range(PLANE):
            grad_copies[chip] = grad_low

    @pl.when(step >= BLOCKS)
    def _():
        n = normed[...]
        tables = widened(cos, lower, upper)
        q[...] = turn(product_plain(n, wq[...]), *tables).astype(low)
        k[...] = turn(product_plain(n, wk[...]), *tables).astype(low)
        v[...] = product_plain(n, wv[...]).astype(low)
        attended = attend(q[...], k[...], v[...], mask[...], logsum)
        att[...] = attended
        added(acc, product_plain(attended, wo[...]), part, BLOCKS)


def self_forward(token, info, hid, norms, wq, wk, wv, wo, tables, grad, tile=4 * HEAD):
    frames, width = hid.shape
    columns = wq.shape[1]
    whole, vector, column, row, act, table, logsum = specs(frames, width, tile, BLOCKS)
    blocks = row_block(frames, width)
    here = frames // BLOCKS
    return ordered(
        self_kernel,
        token,
        (hid, norms, wq, wk, wv, wo, *tables, grad),
        [blocks, vector, column, column, column, row, table, table, table]
        + [
            pl.BlockSpec(
                (here, width),
                lambda j, info: (BLOCKS // 2 * info[3] + jnp.minimum(j, BLOCKS // 2 - 1), 0),
            )
        ],
        [
            copies_block(frames, width, 3),
            pl.BlockSpec((PLANE, here, width), lambda j, info: (0, jnp.minimum(j, BLOCKS // 2 - 1), 0)),
        ]
        + [act, act, act, act, logsum, whole],
        [sds((PLANE, frames // 2, width), low)] * 2
        + [sds((frames, columns), low)] * 4
        + [sds((columns // tile * 8, frames), f32), sds((frames, width), low)],
        (BLOCKS + columns // tile,),
        2 * frames * columns * (4 * width + 8 * frames),
        [
            pltpu.VMEM((frames, width), f32),
            pltpu.VMEM((frames, frames), f32),
            pltpu.VMEM((frames, width), low),
        ],
        info,
    )


def cross_kernel(info, hid, mine, other, norms, cq, ck, cv, co, total, normed, q, att, logsum, part, acc, kept):
    step, block = pl.program_id(0), hid.shape[0]
    gain, shift = norm_row(norms, 2), norm_row(norms, 3)

    @pl.when(step < BLOCKS)
    def _():
        def rows(r):
            x = hid[r, :] + (mine[r, :].astype(f32) + other[r, :].astype(f32))
            total[r, :] = x
            n = normed_rows(x, gain[...], shift[...]).astype(low)
            normed[r, :] = n
            kept[within(step, block, r), :] = n

        over_rows(block, rows)

    @pl.when(step >= BLOCKS)
    def _():
        q[...] = product_plain(kept[...], cq[...]).astype(low)
        attended = cross_attend(info, q[...], ck, cv, logsum)
        att[...] = attended
        added(acc, product_plain(attended, co[...]), part, BLOCKS)


def cross_forward(token, info, hid, mine, other, norms, cq, ck, cv, co, tile=4 * HEAD):
    frames, width = hid.shape
    columns, keys = cq.shape[1], ck.shape[0]
    whole, vector, column, row, act, table, logsum = specs(frames, width, tile, BLOCKS)
    key = pl.BlockSpec((keys, tile), lambda j, *_: (0, jnp.maximum(j - BLOCKS, 0)))
    blocks = row_block(frames, width)
    return ordered(
        cross_kernel,
        token,
        (hid, mine, other, norms, cq, ck, cv, co),
        [blocks, blocks, blocks, vector, column, key, key, row],
        [blocks, blocks, act, act, logsum, whole],
        [
            sds((frames, width), f32),
            sds((frames, width), low),
            sds((frames, columns), low),
            sds((frames, columns), low),
            sds((columns // tile * 8, frames), f32),
            sds((frames, width), low),
        ],
        (BLOCKS + columns // tile,),
        2 * frames * columns * (2 * width + 8 * keys),
        [pltpu.VMEM((frames, width), f32), pltpu.VMEM((frames, width), low)],
        info,
        brief=True,
    )


def norm_kernel(info, hid, mine, other, norms, total, normed, copies):
    gain, shift = norm_row(norms, 4), norm_row(norms, 5)

    def rows(r):
        x = hid[r, :] + (mine[r, :].astype(f32) + other[r, :].astype(f32))
        total[r, :] = x
        normed[r, :] = normed_rows(x, gain[...], shift[...]).astype(low)

    over_rows(hid.shape[0], rows)

    @pl.when(pl.program_id(0) * 2 // pl.num_programs(0) == info[3])
    def _():
        values = normed[...]
        for chip in range(PLANE):
            copies[chip] = values


def norm_forward(token, info, hid, mine, other, norms, block=128):
    frames, width = hid.shape
    blocks = frames // (2 * block)
    rows = pl.BlockSpec((block, width), lambda j, *_: (j, 0))
    vector = pl.BlockSpec((1, 6 * width), lambda j, *_: (0, 0))
    return ordered(
        norm_kernel,
        token,
        (hid, mine, other, norms),
        [rows, rows, rows, vector],
        [
            rows,
            rows,
            pl.BlockSpec(
                (PLANE, block, width),
                lambda j, info: (0, jnp.clip(j - blocks * info[3], 0, blocks - 1), 0),
            ),
        ],
        [sds((frames, width), f32), sds((frames, width), low), sds((PLANE, frames // 2, width), low)],
        (frames // block,),
        10 * frames * width,
        info=info,
        brief=True,
    )


def cross_back_kernel(info, x, mine, other, above, norms, co, q, ck, cv, att, logsum, cq, total, total_low, vectors, dq, dk, dv, part, acc, gain_acc, shift_acc, kept):
    norm_back_step(x, mine, other, above, norm_row(norms, 4), total, total_low, kept, vectors, gain_acc, shift_acc)

    @pl.when(pl.program_id(0) >= BLOCKS)
    def _():
        g = product_with_rows(kept[...], co[...]).astype(low)
        a, b, c = cross_attend_back(info, q[...], ck, cv, g, att[...], logsum[...])
        a = a.astype(low)
        dq[...] = a
        dk[...] = b.astype(low)
        dv[...] = c.astype(low)
        added(acc, product_with_rows(a, cq[...]), part, BLOCKS)


def cross_backward(token, info, x, mine, other, above, gain, co, q, ck, cv, att, logsums, cq, tile=4 * HEAD):
    frames, width = x.shape
    columns, keys = cq.shape[1], ck.shape[0]
    whole, vector, column, row, act, table, logsum = specs(frames, width, tile, BLOCKS)
    key = pl.BlockSpec((keys, tile), lambda j, *_: (0, jnp.maximum(j - BLOCKS, 0)))
    blocks = row_block(frames, width)
    two = pl.BlockSpec((2, width), lambda j, *_: (0, 0))
    return ordered(
        cross_back_kernel,
        token,
        (x, mine, other, above, gain, co, q, ck, cv, att, logsums, cq),
        [blocks, blocks, blocks, blocks, vector, row, act, key, key, act, logsum, column],
        [blocks, blocks, two, act, key, key, whole],
        [
            sds((frames, width), f32),
            sds((frames, width), low),
            sds((2, width), f32),
            sds((frames, columns), low),
            sds((keys, columns), low),
            sds((keys, columns), low),
            sds((frames, width), low),
        ],
        (BLOCKS + columns // tile,),
        2 * frames * columns * (2 * width + 20 * keys),
        [
            pltpu.VMEM((frames, width), f32),
            pltpu.VMEM((8, width), f32),
            pltpu.VMEM((8, width), f32),
            pltpu.VMEM((frames, width), low),
        ],
        info,
    )


def self_back_kernel(info, x, mine, other, above, norms, wo, q, k, v, att, logsum, wq, wk, wv, cos, lower, upper, total, total_low, vectors, grads, part, acc, mask, gain_acc, shift_acc, kept):
    step = pl.program_id(0)

    @pl.when(step == 0)
    def _():
        mask[...] = self_mask(info[0], kept.shape[0])

    norm_back_step(x, mine, other, above, norm_row(norms, 2), total, total_low, kept, vectors, gain_acc, shift_acc)

    @pl.when(step >= BLOCKS)
    def _():
        g = product_with_rows(kept[...], wo[...]).astype(low)
        a, b, c = attend_back(q[...], k[...], v[...], g, att[...], mask[...], logsum[...])
        tables = widened(cos, lower, upper)
        a = turn_back(a, *tables).astype(low)
        b = turn_back(b, *tables).astype(low)
        c = c.astype(low)
        for index, values in enumerate((a, b, c)):
            turned = values.T
            for quarter in range(PLANE):
                grads[quarter, index] = turned[quarter * HEAD : (quarter + 1) * HEAD]
        back = product_with_rows(a, wq[...]) + product_with_rows(b, wk[...])
        added(acc, back + product_with_rows(c, wv[...]), part, BLOCKS)


def self_backward(token, info, x, mine, other, above, gain, wo, q, k, v, att, logsums, wq, wk, wv, tables, tile=4 * HEAD):
    frames, width = x.shape
    columns = wq.shape[1]
    whole, vector, column, row, act, table, logsum = specs(frames, width, tile, BLOCKS)
    blocks = row_block(frames, width)
    two = pl.BlockSpec((2, width), lambda j, *_: (0, 0))
    heads = pl.BlockSpec(
        (PLANE, 3, HEAD, frames), lambda j, *_: (0, 0, jnp.maximum(j - BLOCKS, 0), 0)
    )
    return ordered(
        self_back_kernel,
        token,
        (x, mine, other, above, gain, wo, q, k, v, att, logsums, wq, wk, wv, *tables),
        [blocks] * 4
        + [vector, row, act, act, act, act, logsum, column, column, column, table, table, table],
        [blocks, blocks, two, heads, whole],
        [
            sds((frames, width), f32),
            sds((frames, width), low),
            sds((2, width), f32),
            sds((PLANE, 3, columns // PLANE, frames), low),
            sds((frames, width), low),
        ],
        (BLOCKS + columns // tile,),
        2 * frames * columns * (4 * width + 20 * frames),
        [
            pltpu.VMEM((frames, width), f32),
            pltpu.VMEM((frames, frames), f32),
            pltpu.VMEM((8, width), f32),
            pltpu.VMEM((8, width), f32),
            pltpu.VMEM((frames, width), low),
        ],
        info,
    )


def last_kernel(_, x, mine, other, above, norms, resid, sum_mine, sum_other, total, vectors, result, gain_acc, shift_acc):
    step = pl.program_id(0)
    gain = norm_row(norms, 0)

    @pl.when(step == 0)
    def _():
        gain_acc[...] = jnp.zeros_like(gain_acc)
        shift_acc[...] = jnp.zeros_like(shift_acc)

    def rows(r):
        e = mine[r, :].astype(f32) + other[r, :].astype(f32)
        total[r, :] = norm_back_rows(x[r, :], e, gain[...], above[r, :], gain_acc, shift_acc)
        result[r, :] = resid[r, :] + (sum_mine[r, :].astype(f32) + sum_other[r, :].astype(f32))

    over_rows(x.shape[0], rows)

    @pl.when(step == pl.num_programs(0) - 1)
    def _():
        vectors[0:1, :] = jnp.sum(gain_acc[...], axis=0, keepdims=True)
        vectors[1:2, :] = jnp.sum(shift_acc[...], axis=0, keepdims=True)


def last_backward(token, x, mine, other, above, gain, resid, sum_mine, sum_other, block=128):
    frames, width = x.shape
    rows = pl.BlockSpec((block, width), lambda j, *_: (j, 0))
    vector = pl.BlockSpec((1, 6 * width), lambda j, *_: (0, 0))
    two = pl.BlockSpec((2, width), lambda j, *_: (0, 0))
    return ordered(
        last_kernel,
        token,
        (x, mine, other, above, gain, resid, sum_mine, sum_other),
        [rows, rows, rows, rows, vector, rows, rows, rows],
        [rows, two, rows],
        [sds((frames, width), f32), sds((2, width), f32), sds((frames, width), f32)],
        (frames // block,),
        20 * frames * width,
        [pltpu.VMEM((8, width), f32), pltpu.VMEM((8, width), f32)],
        brief=True,
    )


def ff_kernel(_, in_ref, out_ref, gate_ref, up_ref, down_ref, sum_ref, back_ref, sum_acc, back_acc, out_low):
    @pl.when(pl.program_id(0) == 0)
    def _():
        out_low[...] = out_ref[...].astype(low)

    normed = in_ref[...]
    mixed, grad_gate, grad_up = ff_parts(
        product_plain(normed, gate_ref[...]),
        product_plain(normed, up_ref[...]),
        product_with_rows(out_low[...], down_ref[...]),
    )
    added(sum_acc, product_plain(mixed, down_ref[...]), sum_ref)
    added(
        back_acc,
        product_with_rows(grad_gate, gate_ref[...]) + product_with_rows(grad_up, up_ref[...]),
        back_ref,
    )


def ff_both(token, normed, grad_out, w_gate, w_up, w_down, tile=768):
    frames, width = normed.shape
    units = w_gate.shape[1]
    whole, _, column, row, *_ = specs(frames, width, tile)
    return ordered(
        ff_kernel,
        token,
        (normed, grad_out, w_gate, w_up, w_down),
        [whole, whole, column, column, row],
        [whole, whole],
        [sds((frames, width), low)] * 2,
        (units // tile,),
        12 * frames * width * units,
        [pltpu.VMEM((frames, width), f32)] * 2 + [pltpu.VMEM((frames, width), low)],
    )


def share_kernel(info, in_mine, in_other, out_mine, out_other, gate_ref, up_ref, down_ref, send_ref, keep_ref, acc):
    step = pl.program_id(1)
    normed = jnp.concatenate([in_mine[...], in_other[...]], axis=0)
    grad_out = jnp.concatenate([out_mine[...], out_other[...]], axis=0)
    mixed, grad_gate, grad_up = ff_parts(
        product_plain(normed, gate_ref[...]),
        product_plain(normed, up_ref[...]),
        product_with_rows(grad_out, down_ref[...]),
    )
    fresh = (
        product_over_rows(grad_out, mixed),
        product_over_rows(normed, grad_gate),
        product_over_rows(normed, grad_up),
    )
    for index, term in enumerate(fresh):

        @pl.when(step == 0)
        def _():
            acc[index] = term

        @pl.when(step != 0)
        def _():
            acc[index] += term

    @pl.when(step == pl.num_programs(1) - 1)
    def _():
        rows = send_ref.shape[2] // 3
        for pair in range(2):
            for index in range(3):
                for ref, parity in ((send_ref, 1 - info[5]), (keep_ref, info[5])):
                    start = pl.multiple_of((2 * pair + parity) * rows, rows)
                    ref[0, pair, index * rows : (index + 1) * rows] = acc[
                        index, pl.ds(start, rows), :
                    ].astype(ref.dtype)


def ff_share(token, info, normed, grad_out, w_gate, w_up, w_down, tile, first, count):
    frames, width = normed[0].shape
    chunk = frames // PLANE
    rows = pl.BlockSpec((chunk, width), lambda i, j, info: (j, 0))
    column = pl.BlockSpec((width, tile), lambda i, j, info: (0, info[4] + first + i))
    half = (LEVELS // 2, 3 * width // LEVELS, tile)
    return ordered(
        share_kernel,
        token,
        (*normed, *grad_out, w_gate, w_up, w_down),
        [rows] * 4
        + [column, column, pl.BlockSpec((tile, width), lambda i, j, info: (info[4] + first + i, 0))],
        [pl.BlockSpec((1, *half), lambda i, j, info: (i, 0, 0, 0))] * 2,
        [sds((count, *half), low)] * 2,
        (count, PLANE),
        24 * frames * width * tile * count,
        [pltpu.VMEM((3, width, tile), f32)],
        info,
    )


def weight_kernel(plan, sides_count, _, *refs):
    sides, columns = refs[:sides_count], refs[sides_count : sides_count + len(plan)]
    out = refs[sides_count + len(plan)]
    turned = refs[sides_count + len(plan) + 1 :]

    @pl.when(pl.program_id(0) == 0)
    def _():
        for side, ref in zip(sides, turned):
            ref[...] = side[...].T

    for (which, first), column in zip(plan, columns):
        product = product_plain(turned[which][...], column[...]).astype(low)
        rows = product.shape[0] // (PLANE * LEVELS)
        product = product.reshape(LEVELS, PLANE, rows, product.shape[1])
        for owner in range(PLANE):
            out[owner, :, first : first + rows, :] = product[:, owner]


def weight_products(token, sides, plan, columns, tile=256):
    width = columns[0].shape[1]
    rows = sum(sides[which].shape[1] for which, _ in plan) // (PLANE * LEVELS)
    return ordered(
        functools.partial(weight_kernel, plan, len(sides)),
        token,
        (*sides, *columns),
        [pl.BlockSpec(side.shape, lambda j, *_: (0, 0)) for side in sides]
        + [pl.BlockSpec((column.shape[0], tile), lambda j, *_: (0, j)) for column in columns],
        [pl.BlockSpec((PLANE, LEVELS, rows, tile), lambda j, *_: (0, 0, 0, j))],
        [sds((PLANE, LEVELS, rows, width), low)],
        (width // tile,),
        sum(2 * sides[w].shape[0] * sides[w].shape[1] * width for w, _ in plan),
        [pltpu.VMEM((side.shape[1], side.shape[0]), low) for side in sides],
        brief=len(sides) == 1,
    )


def plane_sum_kernel(info, got, send, keep):
    for ref, parity in ((send, 1 - info[5]), (keep, info[5])):
        total = got[0, 0, parity].astype(f32)
        for source in range(1, PLANE):
            total = total + got[source, 0, parity].astype(f32)
        ref[0] = total.astype(low)


def plane_sum(token, got, info):
    rows, width = got.shape[2:]
    out = pl.BlockSpec((1, rows, width), lambda j, *_: (j, 0, 0))
    return ordered(
        plane_sum_kernel,
        token,
        (got.reshape(PLANE, 2, 2, rows, width),),
        [pl.BlockSpec((PLANE, 1, 2, rows, width), lambda j, *_: (0, j, 0, 0, 0))],
        [out, out],
        [sds((2, rows, width), low)] * 2,
        (2,),
        0,
        info=info,
    )


def level_sum_kernel(_, keep_pass, got_pass, keep_own, got_own, passed, own):
    passed[...] = (keep_pass[0, 0].astype(f32) + got_pass[0, 0].astype(f32)).astype(low)
    own[...] = keep_own[0, 0].astype(f32) + got_own[0, 0].astype(f32)


def level_sum(token, keep, got, info):
    count, _, rows, width = keep.shape
    block = rows // 2 if rows % 32 == 0 else rows
    steps = rows // block
    off = pl.BlockSpec((1, 1, block, width), lambda i, j, info: (i, 1 - info[6], j, 0))
    own = pl.BlockSpec((1, 1, block, width), lambda i, j, info: (i, info[6], j, 0))
    out = pl.BlockSpec((block, width), lambda i, j, info: (i * steps + j, 0))
    return ordered(
        level_sum_kernel,
        token,
        (keep, got, keep, got),
        [off, off, own, own],
        [out, out],
        [sds((count * rows, width), low), sds((count * rows, width), f32)],
        (count, steps),
        0,
        info=info,
        brief=True,
    )


def unit_pack_kernel(counts, _, *refs):
    owns, lasts, out = refs[:-1:2], refs[1:-1:2], refs[-1]
    step = pl.program_id(0)
    for own, last, (first, count) in zip(owns, lasts, counts):

        @pl.when((step >= first) & (step < first + count))
        def _():
            total = (own[...] + last[...].astype(f32)).astype(low)
            total = total.reshape(3, PLANE, out.shape[2], out.shape[3])
            for chip in range(PLANE):
                out[chip] = total[:, chip]


def unit_pack(token, sums, rows):
    tile = sums[0][0].shape[1]
    r = rows // (3 * PLANE)
    specs_in, counts, first = [], [], 0
    for own, _ in sums:
        count = own.shape[0] // rows

        def place(j, info, first=first, count=count):
            return (jnp.clip(j - first, 0, count - 1), 0)

        specs_in += [pl.BlockSpec((rows, tile), place)] * 2
        counts.append((first, count))
        first += count
    return ordered(
        functools.partial(unit_pack_kernel, counts),
        token,
        tuple(array for pair in sums for array in pair),
        specs_in,
        [pl.BlockSpec((PLANE, 3, r, tile), lambda j, *_: (0, 0, 0, j))],
        [sds((PLANE, 3, r, tile * first), low)],
        (first,),
        0,
    )


def unit_unpack_kernel(_, got, down, gate, up):
    down[...] = got[0, 0].astype(f32).T
    gate[...] = got[0, 1].astype(f32)
    up[...] = got[0, 2].astype(f32)


def unit_unpack(token, got):
    _, _, r, units = got.shape
    across = pl.BlockSpec((r, units), lambda j, *_: (0, j))
    return ordered(
        unit_unpack_kernel,
        token,
        (got,),
        [pl.BlockSpec((1, 3, r, units), lambda j, *_: (j, 0, 0, 0))],
        [pl.BlockSpec((units, r), lambda j, *_: (j, 0)), across, across],
        [sds((PLANE * units, r), f32)] + [sds((r, PLANE * units), f32)] * 2,
        (PLANE,),
        0,
    )


def head_pack_kernel(_, own, last, out):
    total = (own[...] + last[...].astype(f32)).T.astype(low)
    out[...] = total.reshape(out.shape)


def head_pack(token, own, last):
    features, columns = own.shape
    shape = (PLANE, columns // PLANE, features)
    return ordered(
        head_pack_kernel,
        token,
        (own, last),
        [pl.BlockSpec(own.shape, lambda j, *_: (0, 0))] * 2,
        [pl.BlockSpec(shape, lambda j, *_: (0, 0, 0))],
        [sds(shape, low)],
        (1,),
        0,
        brief=True,
    )


def head_unpack_kernel(_, got, *outs):
    groups = got.shape[2] // (3 * HEAD)
    for index, out in enumerate(outs):
        pieces = []
        for group in range(groups):
            first = (index * groups + group) * HEAD
            pieces += [got[chip, :, first : first + HEAD] for chip in range(PLANE)]
        out[...] = jnp.concatenate(pieces, axis=1).astype(f32)


def head_unpack(token, got):
    chips, r, features = got.shape
    shape = (r, chips * features // 3)
    return ordered(
        head_unpack_kernel,
        token,
        (got,),
        [pl.BlockSpec(got.shape, lambda j, *_: (0, 0, 0))],
        [pl.BlockSpec(shape, lambda j, *_: (0, 0))] * 3,
        [sds(shape, f32)] * 3,
        (1,),
        0,
    )


def head_kernel(info, grads_mine, grads_other, in_mine, in_other, send, keep, acc):
    step = pl.program_id(0)
    rows = acc.shape[0]
    term = product_plain(grads_mine[0].reshape(rows, -1), in_mine[...]) + product_plain(
        grads_other[0].reshape(rows, -1), in_other[...]
    )

    @pl.when(step == 0)
    def _():
        acc[...] = term

    @pl.when(step != 0)
    def _():
        acc[...] += term

    @pl.when(step == pl.num_programs(0) - 1)
    def _():
        width = send.shape[2]
        for level in range(LEVELS):
            for ref, parity in ((send, 1 - info[5]), (keep, info[5])):

                @pl.when(parity == level % 2)
                def _():
                    ref[level // 2] = acc[:, level * width : (level + 1) * width].astype(low)


def head_products(token, info, grads, normed):
    _, three, features, frames = grads.shape
    width = normed[0].shape[1]
    chunk = normed[0].shape[0] // PLANE
    rows = pl.BlockSpec((chunk, width), lambda j, info: (j, 0))
    half = (LEVELS // 2, three * features, width // LEVELS)
    return ordered(
        head_kernel,
        token,
        (grads, grads, *normed),
        [
            pl.BlockSpec((1, three, features, chunk), lambda j, info: (j, 0, 0, info[3])),
            pl.BlockSpec((1, three, features, chunk), lambda j, info: (j, 0, 0, 1 - info[3])),
            rows,
            rows,
        ],
        [pl.BlockSpec(half, lambda j, info: (0, 0, 0))] * 2,
        [sds(half, low)] * 2,
        (PLANE,),
        2 * three * features * PLANE * frames * width,
        [pltpu.VMEM((three * features, width), f32)],
        info,
        brief=True,
    )


def on_plane(
    hidden_in,
    out_grad,
    prompt_states,
    row_split,
    prompt_len,
    gain_attn,
    bias_attn,
    gain_cross,
    bias_cross,
    gain_ff,
    bias_ff,
    w_query,
    w_key,
    w_value,
    w_out,
    c_query,
    c_key,
    c_value,
    c_out,
    w_gate,
    w_up,
    w_down,
):
    frames, width = hidden_in.shape
    plane, level = lax.axis_index("dp") % PLANE, lax.axis_index("dp") // PLANE
    positions = jnp.arange(frames, dtype=jnp.int32)
    row_ids = (positions >= row_split[0]).astype(jnp.int32)
    tables = rotary_tables((positions - row_ids * row_split[0]).astype(f32), 2 * HEAD)

    tile = 256
    tiles = w_gate.shape[1] // (PLANE * tile)
    places = jnp.stack([lax.axis_index("tensor"), plane * tiles, level % 2, level // 2])
    info = jnp.concatenate([row_split, prompt_len, places])
    norms = jnp.concatenate([gain_attn, bias_attn, gain_cross, bias_cross, gain_ff, bias_ff])[None]
    chips = [[PLANE * z + p for p in range(PLANE)] for z in range(LEVELS)]

    def swapped(part):
        return lax.ppermute(part, "tensor", [(0, 1), (1, 0)])

    def in_plane(values):
        shape = values.shape
        return lax.all_to_all(
            values, "dp", 0, 0, axis_index_groups=chips, tiled=True
        ).reshape(shape)

    def gathered(copies):
        return in_plane(copies.reshape(-1, width))

    def level_swap(values, mask):
        return lax.ppermute(values, "dp", pairs(mask))

    token = jnp.zeros((8, 128), f32)
    context = prompt_states.reshape(2 * PROMPT, prompt_states.shape[2])
    cross_key = product_plain(context, c_key).astype(low)
    cross_value = product_plain(context, c_value).astype(low)
    copies_one, copies, query, key, value, attended_one, logsum_one, part, token = self_forward(
        token,
        info,
        hidden_in,
        norms,
        w_query,
        w_key,
        w_value,
        w_out,
        tables,
        out_grad,
    )
    part_swapped = swapped(part)
    frames_out = gathered(copies)
    resid_one, input_two, cross_query, attended_two, logsum_two, part, token = cross_forward(
        token,
        info,
        hidden_in,
        part,
        part_swapped,
        norms,
        c_query,
        cross_key,
        cross_value,
        c_out,
    )
    part_swapped = swapped(part)
    resid_two, input_three, copies, token = norm_forward(
        token, info, resid_one, part, part_swapped, norms
    )
    frames_out, token = hold(token, frames_out)
    frames_in = gathered(copies)
    frames_out = (frames_out, swapped(frames_out))
    sum_part, back_part, token = ff_both(token, input_three, out_grad, w_gate, w_up, w_down)
    frames_in, token = hold(token, frames_in)
    frames_in = (frames_in, swapped(frames_in))
    back_swapped = swapped(back_part)
    copies_one, token = hold(token, copies_one)
    frames_one = gathered(copies_one)

    def share(token, index, count):
        return ff_share(token, info, frames_in, frames_out, w_gate, w_up, w_down, tile, index, count)

    send_a, keep_a, token = share(token, 0, 1)
    got_a = level_swap(send_a, PLANE)
    grad_two, grad_cross_out, vectors_ff, query_grad, key_grad, value_grad, part, token = cross_backward(
        token,
        info,
        resid_two,
        back_part,
        back_swapped,
        out_grad,
        norms,
        c_out,
        cross_query,
        cross_key,
        cross_value,
        attended_two,
        logsum_two,
        c_query,
    )
    part_swapped = swapped(part)
    r, c = width // 16, context.shape[1] // 16
    products, token = weight_products(
        token,
        [grad_cross_out, input_two, context],
        [(0, 0), (1, r), (2, 2 * r), (2, 2 * r + c)],
        [attended_two, query_grad, key_grad, value_grad],
    )
    frames_one, token = hold(token, frames_one)
    got_cross = in_plane(products)
    frames_one_other = swapped(frames_one)
    pass_a, own_a, token = level_sum(token, keep_a, got_a, info)
    last_a = level_swap(pass_a, 2 * PLANE)
    send_b, keep_b, token = share(token, 1, 1)
    got_b = level_swap(send_b, PLANE)
    send_c, keep_c, token = share(token, 2, tiles - 2)
    got_c = level_swap(send_c, PLANE)
    frames_one_other, token = hold(token, frames_one_other, True)
    frames_one = (frames_one, frames_one_other)
    grad_one, grad_self_out, vectors_cross, grads, part, token = self_backward(
        token,
        info,
        resid_one,
        part,
        part_swapped,
        grad_two,
        norms,
        w_out,
        query,
        key,
        value,
        attended_one,
        logsum_one,
        w_query,
        w_key,
        w_value,
        tables,
    )
    last_a, token = hold(token, last_a, True)
    sum_part, token = hold(token, sum_part, True)
    sum_swapped, part_swapped = swapped(sum_part), swapped(part)
    pass_b, own_b, token = level_sum(token, keep_b, got_b, info)
    last_b = level_swap(pass_b, 2 * PLANE)
    got_cross, token = hold(token, got_cross)
    grads, token = hold(token, grads)
    got_heads = in_plane(grads)
    pass_c, own_c, token = level_sum(token, keep_c, got_c, info)
    last_c = level_swap(pass_c, 2 * PLANE)
    send_x, keep_x, token = plane_sum(token, got_cross, info)
    got_x = level_swap(send_x, PLANE)
    products, token = weight_products(token, [grad_self_out], [(0, 0)], [attended_one])
    last_b, token = hold(token, last_b, True)
    grad_hidden, vectors_attn, result, token = last_backward(
        token, hidden_in, part, part_swapped, grad_one, norms, resid_two, sum_part, sum_swapped
    )
    vectors = jnp.concatenate([vectors_attn, vectors_cross, vectors_ff])
    vectors_got = level_swap(vectors, 1)
    got_heads, token = hold(token, got_heads, True)
    send_h, keep_h, token = head_products(token, info, got_heads, frames_one)
    got_h = level_swap(send_h, PLANE)
    products, token = hold(token, products, True)
    got_out = in_plane(products)
    vectors_got, token = hold(token, vectors_got, True)
    vectors = vectors + vectors_got
    vectors_got = level_swap(vectors, 2)
    pass_x, own_x, token = level_sum(token, keep_x[None], got_x[None], info)
    last_x = level_swap(pass_x, 2 * PLANE)
    last_c, token = hold(token, last_c, True)
    units, token = unit_pack(
        token, [(own_a, last_a), (own_b, last_b), (own_c, last_c)], 3 * width // LEVELS
    )
    vectors_got, token = hold(token, vectors_got, True)
    vectors = vectors + vectors_got
    vectors_got = level_swap(vectors, PLANE)
    pass_h, own_h, token = level_sum(token, keep_h[None], got_h[None], info)
    last_h = level_swap(pass_h, 2 * PLANE)
    got_out, token = hold(token, got_out)
    units, token = hold(token, units, True)
    units = in_plane(units)
    send_o, keep_o, token = plane_sum(token, got_out, info)
    got_o = level_swap(send_o, PLANE)
    vectors_got, token = hold(token, vectors_got, True)
    vectors = vectors + vectors_got
    vectors_got = level_swap(vectors, 2 * PLANE)
    last_x, token = hold(token, last_x, True)
    cross = add_low(own_x, last_x)
    pass_o, own_o, token = level_sum(token, keep_o[None], got_o[None], info)
    last_o = level_swap(pass_o, 2 * PLANE)
    vectors_got, token = hold(token, vectors_got, True)
    vectors = own_share(vectors + vectors_got)
    heads, token = head_pack(token, own_h, last_h)
    units, token = hold(token, units)
    heads, token = hold(token, heads, True)
    heads = in_plane(heads)
    grad_w_down, grad_w_gate, grad_w_up, token = unit_unpack(token, units)
    last_o, token = hold(token, last_o)
    heads, token = hold(token, heads)
    grad_w_query, grad_w_key, grad_w_value, token = head_unpack(token, heads)
    return (
        result,
        grad_hidden,
        *(vectors[index] for index in range(6)),
        grad_w_query,
        grad_w_key,
        grad_w_value,
        add_low(own_o, last_o).T,
        cross[r : 2 * r],
        cross[2 * r : 2 * r + c],
        cross[2 * r + c :],
        cross[:r].T,
        grad_w_gate,
        grad_w_up,
        grad_w_down,
    )


def on_any(
    hidden_in,
    out_grad,
    prompt_states,
    row_split,
    prompt_len,
    gain_attn,
    bias_attn,
    gain_cross,
    bias_cross,
    gain_ff,
    bias_ff,
    w_query,
    w_key,
    w_value,
    w_out,
    c_query,
    c_key,
    c_value,
    c_out,
    w_gate,
    w_up,
    w_down,
):
    frame_count = hidden_in.shape[0]
    positions = jnp.arange(frame_count, dtype=jnp.int32)
    split_here = row_split[0]
    row_ids = (positions >= split_here).astype(jnp.int32)
    tables = rotary_tables((positions - row_ids * split_here).astype(jnp.float32), w_query.shape[1])
    key_index = jnp.arange(2 * PROMPT, dtype=jnp.int32)
    key_rows = key_index // PROMPT
    key_live = key_index % PROMPT < jnp.where(key_rows == 0, prompt_len[0], prompt_len[1])
    self_ok = row_ids[:, None] == row_ids[None, :]
    cross_ok = (row_ids[:, None] == key_rows[None, :]) & key_live[None, :]

    normed, scaled_one, inverse_one = normalize(hidden_in, gain_attn, bias_attn)
    input_one = normed.astype(low)
    query_one = rotate(product_plain(input_one, w_query), tables).astype(low)
    key_one = rotate(product_plain(input_one, w_key), tables).astype(low)
    value_one = product_plain(input_one, w_value).astype(low)
    attended_one, logsum_one = attend_forward(query_one, heads_of(key_one), heads_of(value_one), self_ok)
    resid_one = hidden_in + swap_sum(product_plain(attended_one, w_out))

    normed, scaled_two, inverse_two = normalize(resid_one, gain_cross, bias_cross)
    input_two = normed.astype(low)
    cross_query = product_plain(input_two, c_query).astype(low)
    context_flat = prompt_states.reshape(2 * PROMPT, prompt_states.shape[2])
    cross_key = product_plain(context_flat, c_key).astype(low)
    cross_value = product_plain(context_flat, c_value).astype(low)
    attended_two, logsum_two = attend_forward(
        cross_query, heads_of(cross_key), heads_of(cross_value), cross_ok
    )
    resid_two = resid_one + swap_sum(product_plain(attended_two, c_out))

    normed, scaled_three, inverse_three = normalize(resid_two, gain_ff, bias_ff)
    input_three = normed.astype(low)
    gate_pre = product_plain(input_three, w_gate)
    up_pre = product_plain(input_three, w_up)
    sigmoid_gate = jax.nn.sigmoid(gate_pre)
    mixed_low = (gate_pre * sigmoid_gate * up_pre).astype(low)
    result = resid_two + swap_sum(product_plain(mixed_low, w_down))

    grad_ff_out = out_grad.astype(low)
    grad_w_down = generic_sum(grad_ff_out, mixed_low).T
    grad_mixed = product_with_rows(grad_ff_out, w_down)
    grad_gate = (
        grad_mixed * up_pre * sigmoid_gate * (1.0 + gate_pre * (1.0 - sigmoid_gate))
    ).astype(low)
    grad_up = (grad_mixed * gate_pre * sigmoid_gate).astype(low)
    grad_w_gate = generic_sum(input_three, grad_gate)
    grad_w_up = generic_sum(input_three, grad_up)
    normed_grad_three = swap_sum(
        product_with_rows(grad_gate, w_gate) + product_with_rows(grad_up, w_up)
    )
    back_three, grad_gain_ff, grad_bias_ff = normalize_back(
        normed_grad_three, scaled_three, inverse_three, gain_ff
    )
    grad_two = out_grad + back_three
    grad_cross_out = grad_two.astype(low)
    grad_c_out = generic_sum(grad_cross_out, attended_two).T
    grad_attended_two = product_with_rows(grad_cross_out, c_out).astype(low)
    cross_query_grad, cross_key_grad, cross_value_grad = attend_backward(
        cross_query,
        heads_of(cross_key),
        heads_of(cross_value),
        cross_ok,
        grad_attended_two,
        logsum_two,
    )
    cross_query_grad = cross_query_grad.astype(low)
    cross_key_grad = cross_key_grad.astype(low)
    cross_value_grad = cross_value_grad.astype(low)
    grad_c_query = generic_sum(input_two, cross_query_grad)
    grad_c_key = generic_sum(context_flat, cross_key_grad)
    grad_c_value = generic_sum(context_flat, cross_value_grad)
    normed_grad_two = swap_sum(product_with_rows(cross_query_grad, c_query))
    back_two, grad_gain_cross, grad_bias_cross = normalize_back(
        normed_grad_two, scaled_two, inverse_two, gain_cross
    )
    grad_one = grad_two + back_two
    grad_self_out = grad_one.astype(low)
    grad_w_out = generic_sum(grad_self_out, attended_one).T
    grad_attended_one = product_with_rows(grad_self_out, w_out).astype(low)
    query_grad, key_grad, value_grad = attend_backward(
        query_one, heads_of(key_one), heads_of(value_one), self_ok, grad_attended_one, logsum_one
    )
    query_grad = rotate_back(query_grad, tables).astype(low)
    key_grad = rotate_back(key_grad, tables).astype(low)
    value_grad = value_grad.astype(low)
    grad_w_query = generic_sum(input_one, query_grad)
    grad_w_key = generic_sum(input_one, key_grad)
    grad_w_value = generic_sum(input_one, value_grad)
    normed_grad_one = swap_sum(
        product_with_rows(query_grad, w_query)
        + product_with_rows(key_grad, w_key)
        + product_with_rows(value_grad, w_value)
    )
    back_one, grad_gain_attn, grad_bias_attn = normalize_back(
        normed_grad_one, scaled_one, inverse_one, gain_attn
    )
    grad_hidden = grad_one + back_one
    vectors = lax.psum(
        jnp.stack(
            [
                grad_gain_attn,
                grad_bias_attn,
                grad_gain_cross,
                grad_bias_cross,
                grad_gain_ff,
                grad_bias_ff,
            ]
        ),
        "dp",
    )
    vectors = own_share(vectors)
    return (
        result,
        grad_hidden,
        vectors[0],
        vectors[1],
        vectors[2],
        vectors[3],
        vectors[4],
        vectors[5],
        grad_w_query,
        grad_w_key,
        grad_w_value,
        grad_w_out,
        grad_c_query,
        grad_c_key,
        grad_c_value,
        grad_c_out,
        grad_w_gate,
        grad_w_up,
        grad_w_down,
    )


def solution(mesh):
    in_specs = (
        P("dp", None),
        P("dp", None),
        P("dp", None, None),
        P("dp"),
        P("dp"),
        P(),
        P(),
        P(),
        P(),
        P(),
        P(),
        P(None, "tensor"),
        P(None, "tensor"),
        P(None, "tensor"),
        P("tensor", None),
        P(None, "tensor"),
        P(None, "tensor"),
        P(None, "tensor"),
        P("tensor", None),
        P(None, "tensor"),
        P(None, "tensor"),
        P("tensor", None),
    )
    out_specs = (
        P("dp", None),
        P("dp", None),
        P(("dp", "tensor")),
        P(("dp", "tensor")),
        P(("dp", "tensor")),
        P(("dp", "tensor")),
        P(("dp", "tensor")),
        P(("dp", "tensor")),
        P("dp", "tensor"),
        P("dp", "tensor"),
        P("dp", "tensor"),
        P("tensor", "dp"),
        P("dp", "tensor"),
        P("dp", "tensor"),
        P("dp", "tensor"),
        P("tensor", "dp"),
        P("dp", "tensor"),
        P("dp", "tensor"),
        P("tensor", "dp"),
    )
    known = mesh.shape["dp"] == PLANE * LEVELS and mesh.shape["tensor"] == 2
    return jax.shard_map(
        on_plane if known else on_any, mesh=mesh, in_specs=in_specs, out_specs=out_specs, check_vma=False
    )
```

```python
import functools
import math

import jax
import jax.numpy as jnp
from jax import lax
from jax.experimental import pallas as pl
from jax.experimental.pallas import tpu as pltpu
from jax.sharding import PartitionSpec as P

PROMPT = 128
HEAD = 64
PLANE = 4
LEVELS = 4
VMEM_LIMIT = 62 * 2**20
COST = 3
FLOOR = 15 * 10**9

low = jnp.bfloat16
f32 = jnp.float32
sds = jax.ShapeDtypeStruct


norm_eps = 1e-05
score_scale = 0.125
masked_score = -1e30


def product_plain(left_side, right_side):
    return jnp.dot(left_side, right_side, preferred_element_type=jnp.float32)


def product_over_rows(left_side, right_side):
    return lax.dot_general(
        left_side, right_side, (((0,), (0,)), ((), ())), preferred_element_type=jnp.float32
    )


def product_with_rows(left_side, right_side):
    return lax.dot_general(
        left_side, right_side, (((1,), (1,)), ((), ())), preferred_element_type=jnp.float32
    )


def rotary_tables(positions, width):
    dim_index = jnp.arange(width) % HEAD
    freq_index = (dim_index % 16).astype(jnp.float32)
    inverse_freq = jnp.exp(freq_index * (-math.log(10000.0) / 16.0))
    angles = positions[:, None] * inverse_freq[None, :]
    cosine = jnp.cos(angles)
    sine_part = jnp.sin(angles)
    cos_table = jnp.where(dim_index < 32, cosine, 1.0)
    sin_lower = jnp.where(dim_index < 16, -sine_part, 0.0)
    sin_upper = jnp.where((dim_index >= 16) & (dim_index < 32), sine_part, 0.0)
    return (cos_table, sin_lower, sin_upper)


def rotate(values, tables):
    cos_table, sin_lower, sin_upper = tables
    return (
        values * cos_table
        + jnp.roll(values, -16, axis=1) * sin_lower
        + jnp.roll(values, 16, axis=1) * sin_upper
    )


def rotate_back(incoming, tables):
    cos_table, sin_lower, sin_upper = tables
    return (
        incoming * cos_table
        + jnp.roll(incoming * sin_lower, 16, axis=1)
        + jnp.roll(incoming * sin_upper, -16, axis=1)
    )


def normalize(values, norm_gain, norm_shift):
    average = jnp.mean(values, axis=-1, keepdims=True)
    centered = values - average
    variance = jnp.mean(centered * centered, axis=-1, keepdims=True)
    inverse = lax.rsqrt(variance + norm_eps)
    scaled = centered * inverse
    return (scaled * norm_gain + norm_shift, scaled, inverse)


def normalize_back(incoming, scaled, inverse, norm_gain):
    grad_gain = jnp.sum(incoming * scaled, axis=0)
    grad_shift = jnp.sum(incoming, axis=0)
    weighted = incoming * norm_gain
    grad_input = inverse * (
        weighted
        - jnp.mean(weighted, axis=-1, keepdims=True)
        - scaled * jnp.mean(weighted * scaled, axis=-1, keepdims=True)
    )
    return (grad_input, grad_gain, grad_shift)


def heads_of(values):
    return values.reshape(values.shape[0], values.shape[1] // HEAD, HEAD)


def attend_forward(query_block, key_heads, value_heads, allowed):
    query_heads = heads_of(query_block)
    scores = (
        jnp.einsum("qhd,khd->hqk", query_heads, key_heads, preferred_element_type=jnp.float32)
        * score_scale
    )
    scores = jnp.where(allowed[None], scores, masked_score)
    largest = jnp.max(scores, axis=-1, keepdims=True)
    exp_scores = jnp.exp(scores - largest)
    totals = jnp.sum(exp_scores, axis=-1, keepdims=True)
    soft_weights = (exp_scores / totals).astype(jnp.bfloat16)
    mixed_heads = jnp.einsum(
        "hqk,khd->qhd", soft_weights, value_heads, preferred_element_type=jnp.float32
    )
    mixed_flat = mixed_heads.reshape(query_block.shape[0], query_block.shape[1]).astype(
        jnp.bfloat16
    )
    return (mixed_flat, largest[..., 0] + jnp.log(totals[..., 0]))


def attend_backward(query_block, key_heads, value_heads, allowed, grad_block, logsum_block):
    query_heads = heads_of(query_block)
    grad_heads = heads_of(grad_block)
    scores = (
        jnp.einsum("qhd,khd->hqk", query_heads, key_heads, preferred_element_type=jnp.float32)
        * score_scale
    )
    scores = jnp.where(allowed[None], scores, masked_score)
    soft_weights = jnp.exp(scores - logsum_block[..., None])
    grad_weights = jnp.einsum(
        "qhd,khd->hqk", grad_heads, value_heads, preferred_element_type=jnp.float32
    )
    inner_sum = jnp.sum(soft_weights * grad_weights, axis=-1, keepdims=True)
    grad_scores = (soft_weights * (grad_weights - inner_sum)).astype(jnp.bfloat16)
    grad_query = (
        jnp.einsum("hqk,khd->qhd", grad_scores, key_heads, preferred_element_type=jnp.float32)
        * score_scale
    )
    grad_key = (
        jnp.einsum("hqk,qhd->khd", grad_scores, query_heads, preferred_element_type=jnp.float32)
        * score_scale
    )
    grad_value = jnp.einsum(
        "hqk,qhd->khd",
        soft_weights.astype(jnp.bfloat16),
        grad_heads,
        preferred_element_type=jnp.float32,
    )
    return (
        grad_query.reshape(query_block.shape),
        grad_key.reshape(grad_key.shape[0], -1),
        grad_value.reshape(grad_value.shape[0], -1),
    )


def swap_sum(partial):
    low = partial.astype(jnp.bfloat16)
    if lax.axis_size("tensor") == 2:
        other = lax.ppermute(low, "tensor", [(0, 1), (1, 0)])
        return low.astype(jnp.float32) + other.astype(jnp.float32)
    return lax.psum(low, "tensor").astype(jnp.float32)


def pairs(mask):
    return [(i, i ^ mask) for i in range(16)]


def own_share(vectors):
    share = vectors.shape[1] // (lax.axis_size("dp") * lax.axis_size("tensor"))
    index = lax.axis_index("dp") * lax.axis_size("tensor") + lax.axis_index("tensor")
    return lax.dynamic_slice_in_dim(vectors, index * share, share, 1)


def generic_sum(rows_side, column_side):
    return lax.psum_scatter(
        product_over_rows(rows_side, column_side).astype(jnp.bfloat16),
        "dp",
        scatter_dimension=0,
        tiled=True,
    ).astype(jnp.float32)


def add_low(*terms):
    total = terms[0].astype(jnp.float32)
    for term in terms[1:]:
        total = total + term.astype(jnp.float32)
    return total


def ff_parts(gate, up, grad_mixed):
    sig = 0.5 * jnp.tanh(0.5 * gate) + 0.5
    act = gate * sig
    return (
        (act * up).astype(low),
        (grad_mixed * up * sig * (1.0 + gate * (1.0 - sig))).astype(low),
        (grad_mixed * act).astype(low),
    )


def turn(values, cos, lower, upper):
    width = values.shape[1]
    return (values * cos + pltpu.roll(values, width - 16, 1) * lower + pltpu.roll(values, 16, 1) * upper)

def turn_back(values, cos, lower, upper):
    width = values.shape[1]
    return (values * cos + pltpu.roll(values * lower, 16, 1) + pltpu.roll(values * upper, width - 16, 1))

def normed_rows(values, gain, shift):
    average = jnp.mean(values, axis=-1, keepdims=True)
    centered = values - average
    variance = jnp.mean(centered * centered, axis=-1, keepdims=True)
    return centered * lax.rsqrt(variance + norm_eps) * gain + shift

def over_rows(rows, body, chunk=32):
    @pl.loop(0, rows // chunk, unroll=min(4, rows // chunk))
    def _(i):
        body(pl.ds(pl.multiple_of(i * chunk, chunk), chunk))

def attend(q, k, v, mask, lse_ref):
    q_turned = (q * jnp.bfloat16(0.125)).T
    v_turned = v.T
    heads = [slice(h * HEAD, (h + 1) * HEAD) for h in range(q.shape[1] // HEAD)]
    scores = [product_plain(k[:, c], q_turned[c, :]) for c in heads]
    weights, scales = [], []
    for h, s in enumerate(scores):
        s = s + mask
        m = jnp.max(s, axis=0, keepdims=True)
        e = jnp.exp(s - m)
        total = jnp.sum(e, axis=0, keepdims=True)
        weights.append(e.astype(low))
        scales.append(1.0 / total)
        lse_ref[h : h + 1, :] = m + jnp.log(total)
    outs = [product_plain(v_turned[c, :], e) * x for c, e, x in zip(heads, weights, scales)]
    return jnp.concatenate(outs, axis=0).T.astype(low)


def attend_back(q, k, v, g, att, mask, lse):
    scaled = q * jnp.bfloat16(0.125)
    q_turned = scaled.T
    g_turned = g.T
    k_turned = k.T
    weighted = g_turned.astype(f32) * att.T.astype(f32)
    dq, dk, dv = [], [], []
    for h in range(q.shape[1] // HEAD):
        c = slice(h * HEAD, (h + 1) * HEAD)
        p = jnp.exp(product_plain(k[:, c], q_turned[c, :]) + (mask - lse[h : h + 1, :]))
        dp = product_plain(v[:, c], g_turned[c, :])
        inner = jnp.sum(weighted[c, :], axis=0, keepdims=True)
        ds = (p * (dp - inner)).astype(low)
        dq.append(product_plain(k_turned[c, :], ds))
        dk.append(product_plain(ds, scaled[:, c]))
        dv.append(product_plain(p.astype(low), g[:, c]))
    return (
        jnp.concatenate(dq, axis=0).T * 0.125,
        jnp.concatenate(dk, axis=1),
        jnp.concatenate(dv, axis=1),
    )


def self_mask(split, T):
    r=lax.broadcasted_iota(jnp.int32,(T,T),0)>=split
    c=lax.broadcasted_iota(jnp.int32,(T,T),1)>=split
    return jnp.where(r==c,0.0,masked_score).astype(f32)

def key_half(info, index, frames, keys):
    second = info[0] < frames
    start = jnp.where(second, keys // 2, 0) if index == 1 else 0
    live = jnp.where(second, info[2], info[1]) if index == 1 else info[1]
    return start, live


def half_mask(live, keys, frames):
    return jnp.where(
        lax.broadcasted_iota(jnp.int32, (keys, frames), 0) < live, 0.0, masked_score
    ).astype(f32)


def key_blocks(info, k_ref, v_ref, frames):
    keys = k_ref.shape[0]
    k, v, masks = [], [], []
    for index in range(2):
        start, live = key_half(info, index, frames, keys)
        here = pl.ds(start if index == 0 else pl.multiple_of(start, keys // 2), keys // 2)
        k.append(k_ref[here, :])
        v.append(v_ref[here, :])
        masks.append(half_mask(live, keys // 2, frames // 2))
    return k, v, jnp.concatenate(masks, axis=1)


def cross_attend(info, q, k_ref, v_ref, lse_ref):
    half = q.shape[0] // 2
    q_turned = (q * jnp.bfloat16(0.125)).T
    k, v, mask = key_blocks(info, k_ref, v_ref, 2 * half)
    v_turned = [values.T for values in v]
    outs = []
    for h in range(q.shape[1] // HEAD):
        c = slice(h * HEAD, (h + 1) * HEAD)
        s = [product_plain(k[i][:, c], q_turned[c, i * half : (i + 1) * half]) for i in range(2)]
        s = jnp.concatenate(s, axis=1) + mask
        m = jnp.max(s, axis=0, keepdims=True)
        e = jnp.exp(s - m)
        total = jnp.sum(e, axis=0, keepdims=True)
        lse_ref[h : h + 1, :] = m + jnp.log(total)
        e = e.astype(low)
        o = [product_plain(v_turned[i][c, :], e[:, i * half : (i + 1) * half]) for i in range(2)]
        outs.append(jnp.concatenate(o, axis=1) * (1.0 / total))
    return jnp.concatenate(outs, axis=0).T.astype(low)


def cross_attend_back(info, q, k_ref, v_ref, g, att, lse):
    half = q.shape[0] // 2
    scaled = q * jnp.bfloat16(0.125)
    q_turned = scaled.T
    g_turned = g.T
    weighted = g_turned.astype(f32) * att.T.astype(f32)
    k, v, mask = key_blocks(info, k_ref, v_ref, 2 * half)
    k_turned = [values.T for values in k]
    parts = [slice(0, half), slice(half, 2 * half)]
    dq, dk, dv = [], [[], []], [[], []]
    for h in range(q.shape[1] // HEAD):
        c = slice(h * HEAD, (h + 1) * HEAD)
        s = [product_plain(k[i][:, c], q_turned[c, parts[i]]) for i in range(2)]
        dp = [product_plain(v[i][:, c], g_turned[c, parts[i]]) for i in range(2)]
        p = jnp.exp(jnp.concatenate(s, axis=1) + (mask - lse[h : h + 1, :]))
        inner = jnp.sum(weighted[c, :], axis=0, keepdims=True)
        ds = (p * (jnp.concatenate(dp, axis=1) - inner)).astype(low)
        p = p.astype(low)
        dq.append(
            jnp.concatenate(
                [product_plain(k_turned[i][c, :], ds[:, parts[i]]) for i in range(2)], axis=1
            )
        )
        for i in range(2):
            dk[i].append(product_plain(ds[:, parts[i]], scaled[parts[i], c]))
            dv[i].append(product_plain(p[:, parts[i]], g[parts[i], c]))
    second = (info[0] < 2 * half).astype(f32)

    def by_row(halves):
        first, last = (jnp.concatenate(half, axis=1) for half in halves)
        return jnp.concatenate([first + last * (1.0 - second), last * second], axis=0)

    return jnp.concatenate(dq, axis=0).T * 0.125, by_row(dk), by_row(dv)


def norm_back_rows(x,e,gain,above,gain_acc,shift_acc):
    average=jnp.mean(x,axis=-1,keepdims=True)
    centered=x-average
    variance=jnp.mean(centered*centered,axis=-1,keepdims=True)
    inverse=lax.rsqrt(variance+norm_eps)
    n=centered*inverse
    en=e*n
    w=e*gain
    mean_w=jnp.mean(w,axis=-1,keepdims=True)
    mean_wn=jnp.mean(en*gain,axis=-1,keepdims=True)
    fold=lambda t: jnp.sum(t.reshape(t.shape[0]//8,8,t.shape[1]),axis=0)
    gain_acc[...]+=fold(en)
    shift_acc[...]+=fold(e)
    return above+inverse*(w-mean_w-n*mean_wn)

def norm_back_step(x, mine, other, above, gain, total, total_low, kept, vectors, gain_acc, shift_acc):
    step, block = pl.program_id(0), x.shape[0]

    @pl.when(step == 0)
    def _():
        gain_acc[...] = jnp.zeros_like(gain_acc)
        shift_acc[...] = jnp.zeros_like(shift_acc)

    @pl.when(step < BLOCKS)
    def _():
        def rows(r):
            e = mine[r, :].astype(f32) + other[r, :].astype(f32)
            t = norm_back_rows(x[r, :], e, gain[...][None], above[r, :], gain_acc, shift_acc)
            total[r, :] = t
            total_low[r, :] = t.astype(low)
            kept[within(step, block, r), :] = t.astype(low)

        over_rows(block, rows)

    @pl.when(step == BLOCKS - 1)
    def _():
        vectors[0:1, :] = jnp.sum(gain_acc[...], axis=0, keepdims=True)
        vectors[1:2, :] = jnp.sum(shift_acc[...], axis=0, keepdims=True)


def ordered(kernel, token, args, in_specs, out_specs, out_shape, grid, flops, scratch=(), info=None, brief=False):
    if info is None:
        info = jnp.zeros((1,), jnp.int32)
    inputs, outputs = len(args), len(out_shape)

    def body(info_ref, *refs):
        token_ref = refs[inputs + 1 + outputs]

        @pl.when(functools.reduce(jnp.logical_and, [pl.program_id(i) == 0 for i in range(len(grid))]))
        def _():
            token_ref[...] = jnp.zeros_like(token_ref)

        kernel(
            info_ref,
            *refs[:inputs],
            *refs[inputs + 1 : inputs + 1 + outputs],
            *refs[inputs + 2 + outputs :],
        )

    moved = sum(math.prod(a.shape) * a.dtype.itemsize for a in (*args, *out_shape))
    *results, token = pl.pallas_call(
        body,
        grid_spec=pltpu.PrefetchScalarGridSpec(
            num_scalar_prefetch=1,
            grid=grid,
            in_specs=[*in_specs, pl.BlockSpec(memory_space=pl.ANY)],
            out_specs=[*out_specs, pl.BlockSpec((8, 128), lambda *_: (0, 0))],
            scratch_shapes=list(scratch),
        ),
        out_shape=[*out_shape, sds((8, 128), f32)],
        compiler_params=pltpu.CompilerParams(vmem_limit_bytes=VMEM_LIMIT),
        cost_estimate=pl.CostEstimate(flops=0 if brief else max(FLOOR, int(flops * COST)), bytes_accessed=0 if brief else int(moved * COST), transcendentals=0),
    )(info, *args, token)
    return (*results, token)


def hold(token, values, brief=False):
    def nothing(values_ref, token_ref, out_ref, token_out):
        token_out[...] = jnp.zeros_like(token_out)

    return pl.pallas_call(
        nothing,
        in_specs=[pl.BlockSpec(memory_space=pl.ANY)] * 2,
        out_specs=[pl.BlockSpec(memory_space=pl.ANY), pl.BlockSpec(memory_space=pltpu.VMEM)],
        out_shape=[sds(values.shape, values.dtype), sds((8, 128), f32)],
        input_output_aliases={0: 0},
        compiler_params=pltpu.CompilerParams(vmem_limit_bytes=VMEM_LIMIT),
        cost_estimate=pl.CostEstimate(flops=0 if brief else FLOOR, bytes_accessed=0, transcendentals=0),
    )(values, token)


def specs(frames, width, tile, blocks=0):
    def tile_of(j):
        return jnp.maximum(j - blocks, 0) if blocks else j

    whole = pl.BlockSpec((frames, width), lambda j, *_: (0, 0))
    vector = pl.BlockSpec((width,), lambda j, *_: (0,))
    column = pl.BlockSpec((width, tile), lambda j, *_: (0, tile_of(j)))
    row = pl.BlockSpec((tile, width), lambda j, *_: (tile_of(j), 0))
    act = pl.BlockSpec((frames, tile), lambda j, *_: (0, tile_of(j)))
    table = pl.BlockSpec((frames, 2 * HEAD), lambda j, *_: (0, 0))
    logsum = pl.BlockSpec((8, frames), lambda j, *_: (tile_of(j), 0))
    return whole, vector, column, row, act, table, logsum


BLOCKS = 4


def widened(*tables):
    return tuple(jnp.concatenate([table[...], table[...]], axis=1) for table in tables)


def row_block(frames, width):
    return pl.BlockSpec((frames // BLOCKS, width), lambda j, *_: (jnp.minimum(j, BLOCKS - 1), 0))


def copies_block(frames, width, place):
    return pl.BlockSpec(
        (PLANE, frames // BLOCKS, width),
        lambda j, info: (0, jnp.clip(j - BLOCKS // 2 * info[place], 0, BLOCKS // 2 - 1), 0),
    )


def within(step, rows, r):
    return pl.ds(pl.multiple_of(step * rows + r.start, r.size), r.size)


def added(acc, term, result, first=0):
    step = pl.program_id(0)

    @pl.when(step == first)
    def _():
        acc[...] = term

    @pl.when(step != first)
    def _():
        acc[...] += term

    @pl.when(step == pl.num_programs(0) - 1)
    def _():
        result[...] = acc[...].astype(result.dtype)


def self_kernel(info, hid, gain, shift, wq, wk, wv, wo, cos, lower, upper, grad, copies, grad_copies, q, k, v, att, logsum, part, acc, mask, normed):
    step, frames, block = pl.program_id(0), normed.shape[0], hid.shape[0]

    @pl.when(step == 0)
    def _():
        mask[...] = self_mask(info[0], frames)

    @pl.when(step < BLOCKS)
    def _():
        def rows(r):
            normed[within(step, block, r), :] = normed_rows(hid[r, :], gain[...][None], shift[...][None]).astype(low)

        over_rows(block, rows)

    @pl.when((step < BLOCKS) & (step * 2 // BLOCKS == info[3]))
    def _():
        mine = normed[pl.ds(pl.multiple_of(step * block, block), block), :]
        for chip in range(PLANE):
            copies[chip] = mine

    @pl.when(step < BLOCKS // 2)
    def _():
        grad_low = grad[...].astype(low)
        for chip in range(PLANE):
            grad_copies[chip] = grad_low

    @pl.when(step >= BLOCKS)
    def _():
        n = normed[...]
        tables = widened(cos, lower, upper)
        q[...] = turn(product_plain(n, wq[...]), *tables).astype(low)
        k[...] = turn(product_plain(n, wk[...]), *tables).astype(low)
        v[...] = product_plain(n, wv[...]).astype(low)
        attended = attend(q[...], k[...], v[...], mask[...], logsum)
        att[...] = attended
        added(acc, product_plain(attended, wo[...]), part, BLOCKS)


def self_forward(token, info, hid, gain, shift, wq, wk, wv, wo, tables, grad, tile=4 * HEAD):
    frames, width = hid.shape
    columns = wq.shape[1]
    whole, vector, column, row, act, table, logsum = specs(frames, width, tile, BLOCKS)
    blocks = row_block(frames, width)
    here = frames // BLOCKS
    return ordered(
        self_kernel,
        token,
        (hid, gain, shift, wq, wk, wv, wo, *tables, grad),
        [blocks, vector, vector, column, column, column, row, table, table, table]
        + [
            pl.BlockSpec(
                (here, width),
                lambda j, info: (BLOCKS // 2 * info[3] + jnp.minimum(j, BLOCKS // 2 - 1), 0),
            )
        ],
        [
            copies_block(frames, width, 3),
            pl.BlockSpec((PLANE, here, width), lambda j, info: (0, jnp.minimum(j, BLOCKS // 2 - 1), 0)),
        ]
        + [act, act, act, act, logsum, whole],
        [sds((PLANE, frames // 2, width), low)] * 2
        + [sds((frames, columns), low)] * 4
        + [sds((columns // tile * 8, frames), f32), sds((frames, width), low)],
        (BLOCKS + columns // tile,),
        2 * frames * columns * (4 * width + 8 * frames),
        [
            pltpu.VMEM((frames, width), f32),
            pltpu.VMEM((frames, frames), f32),
            pltpu.VMEM((frames, width), low),
        ],
        info,
    )


def cross_kernel(info, hid, mine, other, gain, shift, cq, ck, cv, co, total, normed, q, att, logsum, part, acc, kept):
    step, block = pl.program_id(0), hid.shape[0]

    @pl.when(step < BLOCKS)
    def _():
        def rows(r):
            x = hid[r, :] + (mine[r, :].astype(f32) + other[r, :].astype(f32))
            total[r, :] = x
            n = normed_rows(x, gain[...][None], shift[...][None]).astype(low)
            normed[r, :] = n
            kept[within(step, block, r), :] = n

        over_rows(block, rows)

    @pl.when(step >= BLOCKS)
    def _():
        q[...] = product_plain(kept[...], cq[...]).astype(low)
        attended = cross_attend(info, q[...], ck, cv, logsum)
        att[...] = attended
        added(acc, product_plain(attended, co[...]), part, BLOCKS)


def cross_forward(token, info, hid, mine, other, gain, shift, cq, ck, cv, co, tile=4 * HEAD):
    frames, width = hid.shape
    columns, keys = cq.shape[1], ck.shape[0]
    whole, vector, column, row, act, table, logsum = specs(frames, width, tile, BLOCKS)
    key = pl.BlockSpec((keys, tile), lambda j, *_: (0, jnp.maximum(j - BLOCKS, 0)))
    blocks = row_block(frames, width)
    return ordered(
        cross_kernel,
        token,
        (hid, mine, other, gain, shift, cq, ck, cv, co),
        [blocks, blocks, blocks, vector, vector, column, key, key, row],
        [blocks, blocks, act, act, logsum, whole],
        [
            sds((frames, width), f32),
            sds((frames, width), low),
            sds((frames, columns), low),
            sds((frames, columns), low),
            sds((columns // tile * 8, frames), f32),
            sds((frames, width), low),
        ],
        (BLOCKS + columns // tile,),
        2 * frames * columns * (2 * width + 8 * keys),
        [pltpu.VMEM((frames, width), f32), pltpu.VMEM((frames, width), low)],
        info,
        brief=True,
    )


def norm_kernel(info, hid, mine, other, gain, shift, total, normed, copies):
    def rows(r):
        x = hid[r, :] + (mine[r, :].astype(f32) + other[r, :].astype(f32))
        total[r, :] = x
        normed[r, :] = normed_rows(x, gain[...][None], shift[...][None]).astype(low)

    over_rows(hid.shape[0], rows)

    @pl.when(pl.program_id(0) * 2 // pl.num_programs(0) == info[0])
    def _():
        values = normed[...]
        for chip in range(PLANE):
            copies[chip] = values


def norm_forward(token, info, hid, mine, other, gain, shift, block=128):
    frames, width = hid.shape
    blocks = frames // (2 * block)
    rows = pl.BlockSpec((block, width), lambda j, *_: (j, 0))
    vector = pl.BlockSpec((width,), lambda j, *_: (0,))
    return ordered(
        norm_kernel,
        token,
        (hid, mine, other, gain, shift),
        [rows, rows, rows, vector, vector],
        [
            rows,
            rows,
            pl.BlockSpec(
                (PLANE, block, width),
                lambda j, info: (0, jnp.clip(j - blocks * info[0], 0, blocks - 1), 0),
            ),
        ],
        [sds((frames, width), f32), sds((frames, width), low), sds((PLANE, frames // 2, width), low)],
        (frames // block,),
        10 * frames * width,
        info=info,
        brief=True,
    )


def cross_back_kernel(info, x, mine, other, above, gain, co, q, ck, cv, att, logsum, cq, total, total_low, vectors, dq, dk, dv, part, acc, gain_acc, shift_acc, kept):
    norm_back_step(x, mine, other, above, gain, total, total_low, kept, vectors, gain_acc, shift_acc)

    @pl.when(pl.program_id(0) >= BLOCKS)
    def _():
        g = product_with_rows(kept[...], co[...]).astype(low)
        a, b, c = cross_attend_back(info, q[...], ck, cv, g, att[...], logsum[...])
        a = a.astype(low)
        dq[...] = a
        dk[...] = b.astype(low)
        dv[...] = c.astype(low)
        added(acc, product_with_rows(a, cq[...]), part, BLOCKS)


def cross_backward(token, info, x, mine, other, above, gain, co, q, ck, cv, att, logsums, cq, tile=4 * HEAD):
    frames, width = x.shape
    columns, keys = cq.shape[1], ck.shape[0]
    whole, vector, column, row, act, table, logsum = specs(frames, width, tile, BLOCKS)
    key = pl.BlockSpec((keys, tile), lambda j, *_: (0, jnp.maximum(j - BLOCKS, 0)))
    blocks = row_block(frames, width)
    two = pl.BlockSpec((2, width), lambda j, *_: (0, 0))
    return ordered(
        cross_back_kernel,
        token,
        (x, mine, other, above, gain, co, q, ck, cv, att, logsums, cq),
        [blocks, blocks, blocks, blocks, vector, row, act, key, key, act, logsum, column],
        [blocks, blocks, two, act, key, key, whole],
        [
            sds((frames, width), f32),
            sds((frames, width), low),
            sds((2, width), f32),
            sds((frames, columns), low),
            sds((keys, columns), low),
            sds((keys, columns), low),
            sds((frames, width), low),
        ],
        (BLOCKS + columns // tile,),
        2 * frames * columns * (2 * width + 20 * keys),
        [
            pltpu.VMEM((frames, width), f32),
            pltpu.VMEM((8, width), f32),
            pltpu.VMEM((8, width), f32),
            pltpu.VMEM((frames, width), low),
        ],
        info,
    )


def self_back_kernel(info, x, mine, other, above, gain, wo, q, k, v, att, logsum, wq, wk, wv, cos, lower, upper, total, total_low, vectors, grads, part, acc, mask, gain_acc, shift_acc, kept):
    step = pl.program_id(0)

    @pl.when(step == 0)
    def _():
        mask[...] = self_mask(info[0], kept.shape[0])

    norm_back_step(x, mine, other, above, gain, total, total_low, kept, vectors, gain_acc, shift_acc)

    @pl.when(step >= BLOCKS)
    def _():
        g = product_with_rows(kept[...], wo[...]).astype(low)
        a, b, c = attend_back(q[...], k[...], v[...], g, att[...], mask[...], logsum[...])
        tables = widened(cos, lower, upper)
        a = turn_back(a, *tables).astype(low)
        b = turn_back(b, *tables).astype(low)
        c = c.astype(low)
        for index, values in enumerate((a, b, c)):
            turned = values.T
            for quarter in range(PLANE):
                grads[quarter, index] = turned[quarter * HEAD : (quarter + 1) * HEAD]
        back = product_with_rows(a, wq[...]) + product_with_rows(b, wk[...])
        added(acc, back + product_with_rows(c, wv[...]), part, BLOCKS)


def self_backward(token, info, x, mine, other, above, gain, wo, q, k, v, att, logsums, wq, wk, wv, tables, tile=4 * HEAD):
    frames, width = x.shape
    columns = wq.shape[1]
    whole, vector, column, row, act, table, logsum = specs(frames, width, tile, BLOCKS)
    blocks = row_block(frames, width)
    two = pl.BlockSpec((2, width), lambda j, *_: (0, 0))
    heads = pl.BlockSpec(
        (PLANE, 3, HEAD, frames), lambda j, *_: (0, 0, jnp.maximum(j - BLOCKS, 0), 0)
    )
    return ordered(
        self_back_kernel,
        token,
        (x, mine, other, above, gain, wo, q, k, v, att, logsums, wq, wk, wv, *tables),
        [blocks] * 4
        + [vector, row, act, act, act, act, logsum, column, column, column, table, table, table],
        [blocks, blocks, two, heads, whole],
        [
            sds((frames, width), f32),
            sds((frames, width), low),
            sds((2, width), f32),
            sds((PLANE, 3, columns // PLANE, frames), low),
            sds((frames, width), low),
        ],
        (BLOCKS + columns // tile,),
        2 * frames * columns * (4 * width + 20 * frames),
        [
            pltpu.VMEM((frames, width), f32),
            pltpu.VMEM((frames, frames), f32),
            pltpu.VMEM((8, width), f32),
            pltpu.VMEM((8, width), f32),
            pltpu.VMEM((frames, width), low),
        ],
        info,
    )


def last_kernel(_, x, mine, other, above, gain, resid, sum_mine, sum_other, total, vectors, result, gain_acc, shift_acc):
    step = pl.program_id(0)

    @pl.when(step == 0)
    def _():
        gain_acc[...] = jnp.zeros_like(gain_acc)
        shift_acc[...] = jnp.zeros_like(shift_acc)

    def rows(r):
        e = mine[r, :].astype(f32) + other[r, :].astype(f32)
        total[r, :] = norm_back_rows(x[r, :], e, gain[...][None], above[r, :], gain_acc, shift_acc)
        result[r, :] = resid[r, :] + (sum_mine[r, :].astype(f32) + sum_other[r, :].astype(f32))

    over_rows(x.shape[0], rows)

    @pl.when(step == pl.num_programs(0) - 1)
    def _():
        vectors[0:1, :] = jnp.sum(gain_acc[...], axis=0, keepdims=True)
        vectors[1:2, :] = jnp.sum(shift_acc[...], axis=0, keepdims=True)


def last_backward(token, x, mine, other, above, gain, resid, sum_mine, sum_other, block=128):
    frames, width = x.shape
    rows = pl.BlockSpec((block, width), lambda j, *_: (j, 0))
    vector = pl.BlockSpec((width,), lambda j, *_: (0,))
    two = pl.BlockSpec((2, width), lambda j, *_: (0, 0))
    return ordered(
        last_kernel,
        token,
        (x, mine, other, above, gain, resid, sum_mine, sum_other),
        [rows, rows, rows, rows, vector, rows, rows, rows],
        [rows, two, rows],
        [sds((frames, width), f32), sds((2, width), f32), sds((frames, width), f32)],
        (frames // block,),
        20 * frames * width,
        [pltpu.VMEM((8, width), f32), pltpu.VMEM((8, width), f32)],
        brief=True,
    )


def ff_kernel(_, in_ref, out_ref, gate_ref, up_ref, down_ref, sum_ref, back_ref, sum_acc, back_acc, out_low):
    @pl.when(pl.program_id(0) == 0)
    def _():
        out_low[...] = out_ref[...].astype(low)

    normed = in_ref[...]
    mixed, grad_gate, grad_up = ff_parts(
        product_plain(normed, gate_ref[...]),
        product_plain(normed, up_ref[...]),
        product_with_rows(out_low[...], down_ref[...]),
    )
    added(sum_acc, product_plain(mixed, down_ref[...]), sum_ref)
    added(
        back_acc,
        product_with_rows(grad_gate, gate_ref[...]) + product_with_rows(grad_up, up_ref[...]),
        back_ref,
    )


def ff_both(token, normed, grad_out, w_gate, w_up, w_down, tile=768):
    frames, width = normed.shape
    units = w_gate.shape[1]
    whole, _, column, row, *_ = specs(frames, width, tile)
    return ordered(
        ff_kernel,
        token,
        (normed, grad_out, w_gate, w_up, w_down),
        [whole, whole, column, column, row],
        [whole, whole],
        [sds((frames, width), low)] * 2,
        (units // tile,),
        12 * frames * width * units,
        [pltpu.VMEM((frames, width), f32)] * 2 + [pltpu.VMEM((frames, width), low)],
    )


def share_kernel(info, in_mine, in_other, out_mine, out_other, gate_ref, up_ref, down_ref, send_ref, keep_ref, acc):
    step = pl.program_id(1)
    normed = jnp.concatenate([in_mine[...], in_other[...]], axis=0)
    grad_out = jnp.concatenate([out_mine[...], out_other[...]], axis=0)
    mixed, grad_gate, grad_up = ff_parts(
        product_plain(normed, gate_ref[...]),
        product_plain(normed, up_ref[...]),
        product_with_rows(grad_out, down_ref[...]),
    )
    fresh = (
        product_over_rows(grad_out, mixed),
        product_over_rows(normed, grad_gate),
        product_over_rows(normed, grad_up),
    )
    for index, term in enumerate(fresh):

        @pl.when(step == 0)
        def _():
            acc[index] = term

        @pl.when(step != 0)
        def _():
            acc[index] += term

    @pl.when(step == pl.num_programs(1) - 1)
    def _():
        rows = send_ref.shape[2] // 3
        for pair in range(2):
            for index in range(3):
                for ref, parity in ((send_ref, 1 - info[1]), (keep_ref, info[1])):
                    start = pl.multiple_of((2 * pair + parity) * rows, rows)
                    ref[0, pair, index * rows : (index + 1) * rows] = acc[
                        index, pl.ds(start, rows), :
                    ].astype(ref.dtype)


def ff_share(token, info, normed, grad_out, w_gate, w_up, w_down, tile, first, count):
    frames, width = normed[0].shape
    chunk = frames // PLANE
    rows = pl.BlockSpec((chunk, width), lambda i, j, info: (j, 0))
    column = pl.BlockSpec((width, tile), lambda i, j, info: (0, info[0] + first + i))
    half = (LEVELS // 2, 3 * width // LEVELS, tile)
    return ordered(
        share_kernel,
        token,
        (*normed, *grad_out, w_gate, w_up, w_down),
        [rows] * 4
        + [column, column, pl.BlockSpec((tile, width), lambda i, j, info: (info[0] + first + i, 0))],
        [pl.BlockSpec((1, *half), lambda i, j, info: (i, 0, 0, 0))] * 2,
        [sds((count, *half), low)] * 2,
        (count, PLANE),
        24 * frames * width * tile * count,
        [pltpu.VMEM((3, width, tile), f32)],
        info,
    )


def weight_kernel(plan, sides_count, _, *refs):
    sides, columns = refs[:sides_count], refs[sides_count : sides_count + len(plan)]
    out = refs[sides_count + len(plan)]
    turned = refs[sides_count + len(plan) + 1 :]

    @pl.when(pl.program_id(0) == 0)
    def _():
        for side, ref in zip(sides, turned):
            ref[...] = side[...].T

    for (which, first), column in zip(plan, columns):
        product = product_plain(turned[which][...], column[...]).astype(low)
        rows = product.shape[0] // (PLANE * LEVELS)
        product = product.reshape(LEVELS, PLANE, rows, product.shape[1])
        for owner in range(PLANE):
            out[owner, :, first : first + rows, :] = product[:, owner]


def weight_products(token, sides, plan, columns, tile=256):
    width = columns[0].shape[1]
    rows = sum(sides[which].shape[1] for which, _ in plan) // (PLANE * LEVELS)
    return ordered(
        functools.partial(weight_kernel, plan, len(sides)),
        token,
        (*sides, *columns),
        [pl.BlockSpec(side.shape, lambda j, *_: (0, 0)) for side in sides]
        + [pl.BlockSpec((column.shape[0], tile), lambda j, *_: (0, j)) for column in columns],
        [pl.BlockSpec((PLANE, LEVELS, rows, tile), lambda j, *_: (0, 0, 0, j))],
        [sds((PLANE, LEVELS, rows, width), low)],
        (width // tile,),
        sum(2 * sides[w].shape[0] * sides[w].shape[1] * width for w, _ in plan),
        [pltpu.VMEM((side.shape[1], side.shape[0]), low) for side in sides],
        brief=len(sides) == 1,
    )


def out_kernel(_, side, column, first, second, third, out, turned):
    step = pl.program_id(0)

    @pl.when(step == 0)
    def _():
        turned[...] = side[...].T

    def store(values):
        values = values.astype(low).reshape(LEVELS, PLANE, out.shape[2], out.shape[3])
        for owner in range(PLANE):
            out[owner] = values[:, owner]

    @pl.when(step < pl.num_programs(0) - 1)
    def _():
        store(product_plain(turned[...], column[...]))

    @pl.when(step == pl.num_programs(0) - 1)
    def _():
        empty = jnp.zeros((out.shape[3] - 6, side.shape[1]), f32)
        store(jnp.concatenate([first[...], second[...], third[...], empty], axis=0).T)


def out_products(token, side, column, vectors, tile=128):
    frames, width = side.shape
    columns = column.shape[1]
    tiles = columns // tile
    rows = width // (PLANE * LEVELS)
    return ordered(
        out_kernel,
        token,
        (side, column, *vectors),
        [
            pl.BlockSpec((frames, width), lambda j, *_: (0, 0)),
            pl.BlockSpec((frames, tile), lambda j, *_: (0, jnp.minimum(j, tiles - 1))),
        ]
        + [pl.BlockSpec((2, width), lambda j, *_: (0, 0))] * 3,
        [pl.BlockSpec((PLANE, LEVELS, rows, tile), lambda j, *_: (0, 0, 0, j))],
        [sds((PLANE, LEVELS, rows, columns + tile), low)],
        (tiles + 1,),
        0,
        [pltpu.VMEM((width, frames), low)],
        brief=True,
    )


def plane_sum_kernel(info, got, send, keep):
    for ref, parity in ((send, 1 - info[0]), (keep, info[0])):
        total = got[0, 0, parity].astype(f32)
        for source in range(1, PLANE):
            total = total + got[source, 0, parity].astype(f32)
        ref[0] = total.astype(low)


def plane_sum(token, got, info):
    rows, width = got.shape[2:]
    out = pl.BlockSpec((1, rows, width), lambda j, *_: (j, 0, 0))
    return ordered(
        plane_sum_kernel,
        token,
        (got.reshape(PLANE, 2, 2, rows, width),),
        [pl.BlockSpec((PLANE, 1, 2, rows, width), lambda j, *_: (0, j, 0, 0, 0))],
        [out, out],
        [sds((2, rows, width), low)] * 2,
        (2,),
        0,
        info=info,
    )


def level_sum_kernel(_, keep_pass, got_pass, keep_own, got_own, passed, own):
    passed[...] = (keep_pass[0, 0].astype(f32) + got_pass[0, 0].astype(f32)).astype(low)
    own[...] = keep_own[0, 0].astype(f32) + got_own[0, 0].astype(f32)


def level_sum(token, keep, got, info, brief=True):
    count, _, rows, width = keep.shape
    block = rows // 2 if rows % 32 == 0 else rows
    steps = rows // block
    off = pl.BlockSpec((1, 1, block, width), lambda i, j, info: (i, 1 - info[0], j, 0))
    own = pl.BlockSpec((1, 1, block, width), lambda i, j, info: (i, info[0], j, 0))
    out = pl.BlockSpec((block, width), lambda i, j, info: (i * steps + j, 0))
    return ordered(
        level_sum_kernel,
        token,
        (keep, got, keep, got),
        [off, off, own, own],
        [out, out],
        [sds((count * rows, width), low), sds((count * rows, width), f32)],
        (count, steps),
        0,
        info=info,
        brief=brief,
    )


def unit_pack_kernel(counts, _, *refs):
    owns, lasts, out = refs[:-1:2], refs[1:-1:2], refs[-1]
    step = pl.program_id(0)
    for own, last, (first, count) in zip(owns, lasts, counts):

        @pl.when((step >= first) & (step < first + count))
        def _():
            total = (own[...] + last[...].astype(f32)).astype(low)
            total = total.reshape(3, PLANE, out.shape[2], out.shape[3])
            for chip in range(PLANE):
                out[chip] = total[:, chip]


def unit_pack(token, sums, rows):
    tile = sums[0][0].shape[1]
    r = rows // (3 * PLANE)
    specs_in, counts, first = [], [], 0
    for own, _ in sums:
        count = own.shape[0] // rows

        def place(j, info, first=first, count=count):
            return (jnp.clip(j - first, 0, count - 1), 0)

        specs_in += [pl.BlockSpec((rows, tile), place)] * 2
        counts.append((first, count))
        first += count
    return ordered(
        functools.partial(unit_pack_kernel, counts),
        token,
        tuple(array for pair in sums for array in pair),
        specs_in,
        [pl.BlockSpec((PLANE, 3, r, tile), lambda j, *_: (0, 0, 0, j))],
        [sds((PLANE, 3, r, tile * first), low)],
        (first,),
        0,
    )


def unit_unpack_kernel(_, got, down, gate, up):
    down[...] = got[0, 0].astype(f32).T
    gate[...] = got[0, 1].astype(f32)
    up[...] = got[0, 2].astype(f32)


def unit_unpack(token, got):
    _, _, r, units = got.shape
    across = pl.BlockSpec((r, units), lambda j, *_: (0, j))
    return ordered(
        unit_unpack_kernel,
        token,
        (got,),
        [pl.BlockSpec((1, 3, r, units), lambda j, *_: (j, 0, 0, 0))],
        [pl.BlockSpec((units, r), lambda j, *_: (j, 0)), across, across],
        [sds((PLANE * units, r), f32)] + [sds((r, PLANE * units), f32)] * 2,
        (PLANE,),
        0,
    )


def head_pack_kernel(_, own, last, out):
    total = (own[...] + last[...].astype(f32)).T.astype(low)
    out[...] = total.reshape(out.shape)


def head_pack(token, own, last):
    features, columns = own.shape
    shape = (PLANE, columns // PLANE, features)
    return ordered(
        head_pack_kernel,
        token,
        (own, last),
        [pl.BlockSpec(own.shape, lambda j, *_: (0, 0))] * 2,
        [pl.BlockSpec(shape, lambda j, *_: (0, 0, 0))],
        [sds(shape, low)],
        (1,),
        0,
        brief=True,
    )


def head_unpack_kernel(_, got, *outs):
    groups = got.shape[2] // (3 * HEAD)
    for index, out in enumerate(outs):
        pieces = []
        for group in range(groups):
            first = (index * groups + group) * HEAD
            pieces += [got[chip, :, first : first + HEAD] for chip in range(PLANE)]
        out[...] = jnp.concatenate(pieces, axis=1).astype(f32)


def head_unpack(token, got):
    chips, r, features = got.shape
    shape = (r, chips * features // 3)
    return ordered(
        head_unpack_kernel,
        token,
        (got,),
        [pl.BlockSpec(got.shape, lambda j, *_: (0, 0, 0))],
        [pl.BlockSpec(shape, lambda j, *_: (0, 0))] * 3,
        [sds(shape, f32)] * 3,
        (1,),
        0,
    )


def head_kernel(info, grads_mine, grads_other, in_mine, in_other, send, keep, acc):
    step = pl.program_id(0)
    rows = acc.shape[0]
    term = product_plain(grads_mine[0].reshape(rows, -1), in_mine[...]) + product_plain(
        grads_other[0].reshape(rows, -1), in_other[...]
    )

    @pl.when(step == 0)
    def _():
        acc[...] = term

    @pl.when(step != 0)
    def _():
        acc[...] += term

    @pl.when(step == pl.num_programs(0) - 1)
    def _():
        width = send.shape[2]
        for level in range(LEVELS):
            for ref, parity in ((send, 1 - info[1]), (keep, info[1])):

                @pl.when(parity == level % 2)
                def _():
                    ref[level // 2] = acc[:, level * width : (level + 1) * width].astype(low)


def head_products(token, info, grads, normed):
    _, three, features, frames = grads.shape
    width = normed[0].shape[1]
    chunk = normed[0].shape[0] // PLANE
    rows = pl.BlockSpec((chunk, width), lambda j, info: (j, 0))
    half = (LEVELS // 2, three * features, width // LEVELS)
    return ordered(
        head_kernel,
        token,
        (grads, grads, *normed),
        [
            pl.BlockSpec((1, three, features, chunk), lambda j, info: (j, 0, 0, info[0])),
            pl.BlockSpec((1, three, features, chunk), lambda j, info: (j, 0, 0, 1 - info[0])),
            rows,
            rows,
        ],
        [pl.BlockSpec(half, lambda j, info: (0, 0, 0))] * 2,
        [sds(half, low)] * 2,
        (PLANE,),
        2 * three * features * PLANE * frames * width,
        [pltpu.VMEM((three * features, width), f32)],
        info,
        brief=True,
    )


def on_plane(
    hidden_in,
    out_grad,
    prompt_states,
    row_split,
    prompt_len,
    gain_attn,
    bias_attn,
    gain_cross,
    bias_cross,
    gain_ff,
    bias_ff,
    w_query,
    w_key,
    w_value,
    w_out,
    c_query,
    c_key,
    c_value,
    c_out,
    w_gate,
    w_up,
    w_down,
):
    frames, width = hidden_in.shape
    plane, level = lax.axis_index("dp") % PLANE, lax.axis_index("dp") // PLANE
    positions = jnp.arange(frames, dtype=jnp.int32)
    row_ids = (positions >= row_split[0]).astype(jnp.int32)
    tables = rotary_tables((positions - row_ids * row_split[0]).astype(f32), 2 * HEAD)

    tile = 256
    tiles = w_gate.shape[1] // (PLANE * tile)
    zero = jnp.zeros((1,), jnp.int32)
    half = zero + lax.axis_index("tensor")
    parity, upper = zero + level % 2, zero + level // 2
    info = jnp.concatenate([row_split, prompt_len, half])
    unit_info = jnp.concatenate([zero + plane * tiles, parity])
    head_info = jnp.concatenate([half, parity])
    chips = [[PLANE * z + p for p in range(PLANE)] for z in range(LEVELS)]

    def swapped(part):
        return lax.ppermute(part, "tensor", [(0, 1), (1, 0)])

    def in_plane(values):
        shape = values.shape
        return lax.all_to_all(
            values, "dp", 0, 0, axis_index_groups=chips, tiled=True
        ).reshape(shape)

    def gathered(copies):
        return in_plane(copies.reshape(-1, width))

    def level_swap(values, mask):
        return lax.ppermute(values, "dp", pairs(mask))

    token = jnp.zeros((8, 128), f32)
    context = prompt_states.reshape(2 * PROMPT, prompt_states.shape[2])
    cross_key = product_plain(context, c_key).astype(low)
    cross_value = product_plain(context, c_value).astype(low)
    copies_one, copies, query, key, value, attended_one, logsum_one, part, token = self_forward(
        token,
        info,
        hidden_in,
        gain_attn,
        bias_attn,
        w_query,
        w_key,
        w_value,
        w_out,
        tables,
        out_grad,
    )
    part_swapped = swapped(part)
    frames_out = gathered(copies)
    resid_one, input_two, cross_query, attended_two, logsum_two, part, token = cross_forward(
        token,
        info,
        hidden_in,
        part,
        part_swapped,
        gain_cross,
        bias_cross,
        c_query,
        cross_key,
        cross_value,
        c_out,
    )
    part_swapped = swapped(part)
    resid_two, input_three, copies, token = norm_forward(
        token, half, resid_one, part, part_swapped, gain_ff, bias_ff
    )
    frames_out, token = hold(token, frames_out)
    frames_in = gathered(copies)
    frames_out = (frames_out, swapped(frames_out))
    sum_part, back_part, token = ff_both(token, input_three, out_grad, w_gate, w_up, w_down)
    frames_in, token = hold(token, frames_in)
    frames_in = (frames_in, swapped(frames_in))
    back_swapped = swapped(back_part)
    copies_one, token = hold(token, copies_one)
    frames_one = gathered(copies_one)

    def share(token, index, count):
        return ff_share(token, unit_info, frames_in, frames_out, w_gate, w_up, w_down, tile, index, count)

    send_a, keep_a, token = share(token, 0, 1)
    got_a = level_swap(send_a, PLANE)
    grad_two, grad_cross_out, vectors_ff, query_grad, key_grad, value_grad, part, token = cross_backward(
        token,
        info,
        resid_two,
        back_part,
        back_swapped,
        out_grad,
        gain_ff,
        c_out,
        cross_query,
        cross_key,
        cross_value,
        attended_two,
        logsum_two,
        c_query,
    )
    part_swapped = swapped(part)
    r, c = width // 16, context.shape[1] // 16
    products, token = weight_products(
        token,
        [grad_cross_out, input_two, context],
        [(0, 0), (1, r), (2, 2 * r), (2, 2 * r + c)],
        [attended_two, query_grad, key_grad, value_grad],
    )
    frames_one, token = hold(token, frames_one)
    got_cross = in_plane(products)
    frames_one_other = swapped(frames_one)
    pass_a, own_a, token = level_sum(token, keep_a, got_a, upper)
    last_a = level_swap(pass_a, 2 * PLANE)
    send_b, keep_b, token = share(token, 1, 1)
    got_b = level_swap(send_b, PLANE)
    send_c, keep_c, token = share(token, 2, tiles - 2)
    got_c = level_swap(send_c, PLANE)
    frames_one_other, token = hold(token, frames_one_other, True)
    frames_one = (frames_one, frames_one_other)
    grad_one, grad_self_out, vectors_cross, grads, part, token = self_backward(
        token,
        info,
        resid_one,
        part,
        part_swapped,
        grad_two,
        gain_cross,
        w_out,
        query,
        key,
        value,
        attended_one,
        logsum_one,
        w_query,
        w_key,
        w_value,
        tables,
    )
    last_a, token = hold(token, last_a, True)
    sum_part, token = hold(token, sum_part, True)
    sum_swapped, part_swapped = swapped(sum_part), swapped(part)
    pass_b, own_b, token = level_sum(token, keep_b, got_b, upper)
    last_b = level_swap(pass_b, 2 * PLANE)
    got_cross, token = hold(token, got_cross)
    grads, token = hold(token, grads)
    got_heads = in_plane(grads)
    pass_c, own_c, token = level_sum(token, keep_c, got_c, upper)
    last_c = level_swap(pass_c, 2 * PLANE)
    send_x, keep_x, token = plane_sum(token, got_cross, parity)
    got_x = level_swap(send_x, PLANE)
    grad_hidden, vectors_attn, result, token = last_backward(
        token, hidden_in, part, part_swapped, grad_one, gain_attn, resid_two, sum_part, sum_swapped
    )
    products, token = out_products(
        token, grad_self_out, attended_one, (vectors_attn, vectors_cross, vectors_ff)
    )
    got_heads, token = hold(token, got_heads, True)
    products, token = hold(token, products, True)
    got_out = in_plane(products)
    send_h, keep_h, token = head_products(token, head_info, got_heads, frames_one)
    got_h = level_swap(send_h, PLANE)
    pass_x, own_x, token = level_sum(token, keep_x[None], got_x[None], upper)
    last_x = level_swap(pass_x, 2 * PLANE)
    last_b, token = hold(token, last_b, True)
    last_c, token = hold(token, last_c, True)
    units, token = unit_pack(
        token, [(own_a, last_a), (own_b, last_b), (own_c, last_c)], 3 * width // LEVELS
    )
    pass_h, own_h, token = level_sum(token, keep_h[None], got_h[None], upper, False)
    last_h = level_swap(pass_h, 2 * PLANE)
    got_out, token = hold(token, got_out)
    units, token = hold(token, units, True)
    units = in_plane(units)
    send_o, keep_o, token = plane_sum(token, got_out, parity)
    got_o = level_swap(send_o, PLANE)
    last_x, token = hold(token, last_x, True)
    cross = add_low(own_x, last_x)
    pass_o, own_o, token = level_sum(token, keep_o[None], got_o[None], upper)
    last_o = level_swap(pass_o, 2 * PLANE)
    heads, token = head_pack(token, own_h, last_h)
    units, token = hold(token, units)
    heads, token = hold(token, heads, True)
    heads = in_plane(heads)
    grad_w_down, grad_w_gate, grad_w_up, token = unit_unpack(token, units)
    last_o, token = hold(token, last_o)
    outs = add_low(own_o, last_o)
    share_of = r // 2
    vectors = lax.dynamic_slice_in_dim(
        outs, lax.axis_index("tensor") * share_of, share_of, 0
    )[:, w_query.shape[1] : w_query.shape[1] + 6].T
    heads, token = hold(token, heads)
    grad_w_query, grad_w_key, grad_w_value, token = head_unpack(token, heads)
    return (
        result,
        grad_hidden,
        *(vectors[index] for index in range(6)),
        grad_w_query,
        grad_w_key,
        grad_w_value,
        outs[:, : w_query.shape[1]].T,
        cross[r : 2 * r],
        cross[2 * r : 2 * r + c],
        cross[2 * r + c :],
        cross[:r].T,
        grad_w_gate,
        grad_w_up,
        grad_w_down,
    )


def on_any(
    hidden_in,
    out_grad,
    prompt_states,
    row_split,
    prompt_len,
    gain_attn,
    bias_attn,
    gain_cross,
    bias_cross,
    gain_ff,
    bias_ff,
    w_query,
    w_key,
    w_value,
    w_out,
    c_query,
    c_key,
    c_value,
    c_out,
    w_gate,
    w_up,
    w_down,
):
    frame_count = hidden_in.shape[0]
    positions = jnp.arange(frame_count, dtype=jnp.int32)
    split_here = row_split[0]
    row_ids = (positions >= split_here).astype(jnp.int32)
    tables = rotary_tables((positions - row_ids * split_here).astype(jnp.float32), w_query.shape[1])
    key_index = jnp.arange(2 * PROMPT, dtype=jnp.int32)
    key_rows = key_index // PROMPT
    key_live = key_index % PROMPT < jnp.where(key_rows == 0, prompt_len[0], prompt_len[1])
    self_ok = row_ids[:, None] == row_ids[None, :]
    cross_ok = (row_ids[:, None] == key_rows[None, :]) & key_live[None, :]

    normed, scaled_one, inverse_one = normalize(hidden_in, gain_attn, bias_attn)
    input_one = normed.astype(low)
    query_one = rotate(product_plain(input_one, w_query), tables).astype(low)
    key_one = rotate(product_plain(input_one, w_key), tables).astype(low)
    value_one = product_plain(input_one, w_value).astype(low)
    attended_one, logsum_one = attend_forward(query_one, heads_of(key_one), heads_of(value_one), self_ok)
    resid_one = hidden_in + swap_sum(product_plain(attended_one, w_out))

    normed, scaled_two, inverse_two = normalize(resid_one, gain_cross, bias_cross)
    input_two = normed.astype(low)
    cross_query = product_plain(input_two, c_query).astype(low)
    context_flat = prompt_states.reshape(2 * PROMPT, prompt_states.shape[2])
    cross_key = product_plain(context_flat, c_key).astype(low)
    cross_value = product_plain(context_flat, c_value).astype(low)
    attended_two, logsum_two = attend_forward(
        cross_query, heads_of(cross_key), heads_of(cross_value), cross_ok
    )
    resid_two = resid_one + swap_sum(product_plain(attended_two, c_out))

    normed, scaled_three, inverse_three = normalize(resid_two, gain_ff, bias_ff)
    input_three = normed.astype(low)
    gate_pre = product_plain(input_three, w_gate)
    up_pre = product_plain(input_three, w_up)
    sigmoid_gate = jax.nn.sigmoid(gate_pre)
    mixed_low = (gate_pre * sigmoid_gate * up_pre).astype(low)
    result = resid_two + swap_sum(product_plain(mixed_low, w_down))

    grad_ff_out = out_grad.astype(low)
    grad_w_down = generic_sum(grad_ff_out, mixed_low).T
    grad_mixed = product_with_rows(grad_ff_out, w_down)
    grad_gate = (
        grad_mixed * up_pre * sigmoid_gate * (1.0 + gate_pre * (1.0 - sigmoid_gate))
    ).astype(low)
    grad_up = (grad_mixed * gate_pre * sigmoid_gate).astype(low)
    grad_w_gate = generic_sum(input_three, grad_gate)
    grad_w_up = generic_sum(input_three, grad_up)
    normed_grad_three = swap_sum(
        product_with_rows(grad_gate, w_gate) + product_with_rows(grad_up, w_up)
    )
    back_three, grad_gain_ff, grad_bias_ff = normalize_back(
        normed_grad_three, scaled_three, inverse_three, gain_ff
    )
    grad_two = out_grad + back_three
    grad_cross_out = grad_two.astype(low)
    grad_c_out = generic_sum(grad_cross_out, attended_two).T
    grad_attended_two = product_with_rows(grad_cross_out, c_out).astype(low)
    cross_query_grad, cross_key_grad, cross_value_grad = attend_backward(
        cross_query,
        heads_of(cross_key),
        heads_of(cross_value),
        cross_ok,
        grad_attended_two,
        logsum_two,
    )
    cross_query_grad = cross_query_grad.astype(low)
    cross_key_grad = cross_key_grad.astype(low)
    cross_value_grad = cross_value_grad.astype(low)
    grad_c_query = generic_sum(input_two, cross_query_grad)
    grad_c_key = generic_sum(context_flat, cross_key_grad)
    grad_c_value = generic_sum(context_flat, cross_value_grad)
    normed_grad_two = swap_sum(product_with_rows(cross_query_grad, c_query))
    back_two, grad_gain_cross, grad_bias_cross = normalize_back(
        normed_grad_two, scaled_two, inverse_two, gain_cross
    )
    grad_one = grad_two + back_two
    grad_self_out = grad_one.astype(low)
    grad_w_out = generic_sum(grad_self_out, attended_one).T
    grad_attended_one = product_with_rows(grad_self_out, w_out).astype(low)
    query_grad, key_grad, value_grad = attend_backward(
        query_one, heads_of(key_one), heads_of(value_one), self_ok, grad_attended_one, logsum_one
    )
    query_grad = rotate_back(query_grad, tables).astype(low)
    key_grad = rotate_back(key_grad, tables).astype(low)
    value_grad = value_grad.astype(low)
    grad_w_query = generic_sum(input_one, query_grad)
    grad_w_key = generic_sum(input_one, key_grad)
    grad_w_value = generic_sum(input_one, value_grad)
    normed_grad_one = swap_sum(
        product_with_rows(query_grad, w_query)
        + product_with_rows(key_grad, w_key)
        + product_with_rows(value_grad, w_value)
    )
    back_one, grad_gain_attn, grad_bias_attn = normalize_back(
        normed_grad_one, scaled_one, inverse_one, gain_attn
    )
    grad_hidden = grad_one + back_one
    vectors = lax.psum(
        jnp.stack(
            [
                grad_gain_attn,
                grad_bias_attn,
                grad_gain_cross,
                grad_bias_cross,
                grad_gain_ff,
                grad_bias_ff,
            ]
        ),
        "dp",
    )
    vectors = own_share(vectors)
    return (
        result,
        grad_hidden,
        vectors[0],
        vectors[1],
        vectors[2],
        vectors[3],
        vectors[4],
        vectors[5],
        grad_w_query,
        grad_w_key,
        grad_w_value,
        grad_w_out,
        grad_c_query,
        grad_c_key,
        grad_c_value,
        grad_c_out,
        grad_w_gate,
        grad_w_up,
        grad_w_down,
    )


def solution(mesh):
    in_specs = (
        P("dp", None),
        P("dp", None),
        P("dp", None, None),
        P("dp"),
        P("dp"),
        P(),
        P(),
        P(),
        P(),
        P(),
        P(),
        P(None, "tensor"),
        P(None, "tensor"),
        P(None, "tensor"),
        P("tensor", None),
        P(None, "tensor"),
        P(None, "tensor"),
        P(None, "tensor"),
        P("tensor", None),
        P(None, "tensor"),
        P(None, "tensor"),
        P("tensor", None),
    )
    out_specs = (
        P("dp", None),
        P("dp", None),
        P(("dp", "tensor")),
        P(("dp", "tensor")),
        P(("dp", "tensor")),
        P(("dp", "tensor")),
        P(("dp", "tensor")),
        P(("dp", "tensor")),
        P("dp", "tensor"),
        P("dp", "tensor"),
        P("dp", "tensor"),
        P("tensor", "dp"),
        P("dp", "tensor"),
        P("dp", "tensor"),
        P("dp", "tensor"),
        P("tensor", "dp"),
        P("dp", "tensor"),
        P("dp", "tensor"),
        P("tensor", "dp"),
    )
    known = mesh.shape["dp"] == PLANE * LEVELS and mesh.shape["tensor"] == 2
    return jax.shard_map(
        on_plane if known else on_any, mesh=mesh, in_specs=in_specs, out_specs=out_specs, check_vma=False
    )
```

```python
import functools
import math

import jax
import jax.numpy as jnp
from jax import lax
from jax.experimental import pallas as pl
from jax.experimental.pallas import tpu as pltpu
from jax.sharding import PartitionSpec as P

PROMPT = 128
HEAD = 64
PLANE = 4
LEVELS = 4
VMEM_LIMIT = 62 * 2**20
COST = 3
FLOOR = 15 * 10**9

low = jnp.bfloat16
f32 = jnp.float32
sds = jax.ShapeDtypeStruct


norm_eps = 1e-05
score_scale = 0.125
masked_score = -1e30


def product_plain(left_side, right_side):
    return jnp.dot(left_side, right_side, preferred_element_type=jnp.float32)


def product_over_rows(left_side, right_side):
    return lax.dot_general(
        left_side, right_side, (((0,), (0,)), ((), ())), preferred_element_type=jnp.float32
    )


def product_with_rows(left_side, right_side):
    return lax.dot_general(
        left_side, right_side, (((1,), (1,)), ((), ())), preferred_element_type=jnp.float32
    )


def rotary_tables(positions, width):
    dim_index = jnp.arange(width) % HEAD
    freq_index = (dim_index % 16).astype(jnp.float32)
    inverse_freq = jnp.exp(freq_index * (-math.log(10000.0) / 16.0))
    angles = positions[:, None] * inverse_freq[None, :]
    cosine = jnp.cos(angles)
    sine_part = jnp.sin(angles)
    cos_table = jnp.where(dim_index < 32, cosine, 1.0)
    sin_lower = jnp.where(dim_index < 16, -sine_part, 0.0)
    sin_upper = jnp.where((dim_index >= 16) & (dim_index < 32), sine_part, 0.0)
    return (cos_table, sin_lower, sin_upper)


def rotate(values, tables):
    cos_table, sin_lower, sin_upper = tables
    return (
        values * cos_table
        + jnp.roll(values, -16, axis=1) * sin_lower
        + jnp.roll(values, 16, axis=1) * sin_upper
    )


def rotate_back(incoming, tables):
    cos_table, sin_lower, sin_upper = tables
    return (
        incoming * cos_table
        + jnp.roll(incoming * sin_lower, 16, axis=1)
        + jnp.roll(incoming * sin_upper, -16, axis=1)
    )


def normalize(values, norm_gain, norm_shift):
    average = jnp.mean(values, axis=-1, keepdims=True)
    centered = values - average
    variance = jnp.mean(centered * centered, axis=-1, keepdims=True)
    inverse = lax.rsqrt(variance + norm_eps)
    scaled = centered * inverse
    return (scaled * norm_gain + norm_shift, scaled, inverse)


def normalize_back(incoming, scaled, inverse, norm_gain):
    grad_gain = jnp.sum(incoming * scaled, axis=0)
    grad_shift = jnp.sum(incoming, axis=0)
    weighted = incoming * norm_gain
    grad_input = inverse * (
        weighted
        - jnp.mean(weighted, axis=-1, keepdims=True)
        - scaled * jnp.mean(weighted * scaled, axis=-1, keepdims=True)
    )
    return (grad_input, grad_gain, grad_shift)


def heads_of(values):
    return values.reshape(values.shape[0], values.shape[1] // HEAD, HEAD)


def attend_forward(query_block, key_heads, value_heads, allowed):
    query_heads = heads_of(query_block)
    scores = (
        jnp.einsum("qhd,khd->hqk", query_heads, key_heads, preferred_element_type=jnp.float32)
        * score_scale
    )
    scores = jnp.where(allowed[None], scores, masked_score)
    largest = jnp.max(scores, axis=-1, keepdims=True)
    exp_scores = jnp.exp(scores - largest)
    totals = jnp.sum(exp_scores, axis=-1, keepdims=True)
    soft_weights = (exp_scores / totals).astype(jnp.bfloat16)
    mixed_heads = jnp.einsum(
        "hqk,khd->qhd", soft_weights, value_heads, preferred_element_type=jnp.float32
    )
    mixed_flat = mixed_heads.reshape(query_block.shape[0], query_block.shape[1]).astype(
        jnp.bfloat16
    )
    return (mixed_flat, largest[..., 0] + jnp.log(totals[..., 0]))


def attend_backward(query_block, key_heads, value_heads, allowed, grad_block, logsum_block):
    query_heads = heads_of(query_block)
    grad_heads = heads_of(grad_block)
    scores = (
        jnp.einsum("qhd,khd->hqk", query_heads, key_heads, preferred_element_type=jnp.float32)
        * score_scale
    )
    scores = jnp.where(allowed[None], scores, masked_score)
    soft_weights = jnp.exp(scores - logsum_block[..., None])
    grad_weights = jnp.einsum(
        "qhd,khd->hqk", grad_heads, value_heads, preferred_element_type=jnp.float32
    )
    inner_sum = jnp.sum(soft_weights * grad_weights, axis=-1, keepdims=True)
    grad_scores = (soft_weights * (grad_weights - inner_sum)).astype(jnp.bfloat16)
    grad_query = (
        jnp.einsum("hqk,khd->qhd", grad_scores, key_heads, preferred_element_type=jnp.float32)
        * score_scale
    )
    grad_key = (
        jnp.einsum("hqk,qhd->khd", grad_scores, query_heads, preferred_element_type=jnp.float32)
        * score_scale
    )
    grad_value = jnp.einsum(
        "hqk,qhd->khd",
        soft_weights.astype(jnp.bfloat16),
        grad_heads,
        preferred_element_type=jnp.float32,
    )
    return (
        grad_query.reshape(query_block.shape),
        grad_key.reshape(grad_key.shape[0], -1),
        grad_value.reshape(grad_value.shape[0], -1),
    )


def swap_sum(partial):
    low = partial.astype(jnp.bfloat16)
    if lax.axis_size("tensor") == 2:
        other = lax.ppermute(low, "tensor", [(0, 1), (1, 0)])
        return low.astype(jnp.float32) + other.astype(jnp.float32)
    return lax.psum(low, "tensor").astype(jnp.float32)


def pairs(mask):
    return [(i, i ^ mask) for i in range(16)]


def own_share(vectors):
    share = vectors.shape[1] // (lax.axis_size("dp") * lax.axis_size("tensor"))
    index = lax.axis_index("dp") * lax.axis_size("tensor") + lax.axis_index("tensor")
    return lax.dynamic_slice_in_dim(vectors, index * share, share, 1)


def generic_sum(rows_side, column_side):
    return lax.psum_scatter(
        product_over_rows(rows_side, column_side).astype(jnp.bfloat16),
        "dp",
        scatter_dimension=0,
        tiled=True,
    ).astype(jnp.float32)


def add_low(*terms):
    total = terms[0].astype(jnp.float32)
    for term in terms[1:]:
        total = total + term.astype(jnp.float32)
    return total


def ff_parts(gate, up, grad_mixed):
    sig = 0.5 * jnp.tanh(0.5 * gate) + 0.5
    act = gate * sig
    return (
        (act * up).astype(low),
        (grad_mixed * up * sig * (1.0 + gate * (1.0 - sig))).astype(low),
        (grad_mixed * act).astype(low),
    )


def turn(values, cos, lower, upper):
    width = values.shape[1]
    return (values * cos + pltpu.roll(values, width - 16, 1) * lower + pltpu.roll(values, 16, 1) * upper)

def turn_back(values, cos, lower, upper):
    width = values.shape[1]
    return (values * cos + pltpu.roll(values * lower, 16, 1) + pltpu.roll(values * upper, width - 16, 1))

def normed_rows(values, gain, shift):
    average = jnp.mean(values, axis=-1, keepdims=True)
    centered = values - average
    variance = jnp.mean(centered * centered, axis=-1, keepdims=True)
    return centered * lax.rsqrt(variance + norm_eps) * gain + shift

def over_rows(rows, body, chunk=32):
    @pl.loop(0, rows // chunk, unroll=min(4, rows // chunk))
    def _(i):
        body(pl.ds(pl.multiple_of(i * chunk, chunk), chunk))

def attend(q, k, v, mask, lse_ref):
    q_turned = (q * jnp.bfloat16(0.125)).T
    v_turned = v.T
    heads = [slice(h * HEAD, (h + 1) * HEAD) for h in range(q.shape[1] // HEAD)]
    scores = [product_plain(k[:, c], q_turned[c, :]) for c in heads]
    weights, scales = [], []
    for h, s in enumerate(scores):
        s = s + mask
        m = jnp.max(s, axis=0, keepdims=True)
        e = jnp.exp(s - m)
        total = jnp.sum(e, axis=0, keepdims=True)
        weights.append(e.astype(low))
        scales.append(1.0 / total)
        lse_ref[h : h + 1, :] = m + jnp.log(total)
    outs = [product_plain(v_turned[c, :], e) * x for c, e, x in zip(heads, weights, scales)]
    return jnp.concatenate(outs, axis=0).T.astype(low)


def attend_back(q, k, v, g, att, mask, lse):
    scaled = q * jnp.bfloat16(0.125)
    q_turned = scaled.T
    g_turned = g.T
    k_turned = k.T
    weighted = g_turned.astype(f32) * att.T.astype(f32)
    dq, dk, dv = [], [], []
    for h in range(q.shape[1] // HEAD):
        c = slice(h * HEAD, (h + 1) * HEAD)
        p = jnp.exp(product_plain(k[:, c], q_turned[c, :]) + (mask - lse[h : h + 1, :]))
        dp = product_plain(v[:, c], g_turned[c, :])
        inner = jnp.sum(weighted[c, :], axis=0, keepdims=True)
        ds = (p * (dp - inner)).astype(low)
        dq.append(product_plain(k_turned[c, :], ds))
        dk.append(product_plain(ds, scaled[:, c]))
        dv.append(product_plain(p.astype(low), g[:, c]))
    return (
        jnp.concatenate(dq, axis=0).T * 0.125,
        jnp.concatenate(dk, axis=1),
        jnp.concatenate(dv, axis=1),
    )


def self_mask(split, T):
    r=lax.broadcasted_iota(jnp.int32,(T,T),0)>=split
    c=lax.broadcasted_iota(jnp.int32,(T,T),1)>=split
    return jnp.where(r==c,0.0,masked_score).astype(f32)

def key_half(info, index, frames, keys):
    second = info[0] < frames
    start = jnp.where(second, keys // 2, 0) if index == 1 else 0
    live = jnp.where(second, info[2], info[1]) if index == 1 else info[1]
    return start, live


def half_mask(live, keys, frames):
    return jnp.where(
        lax.broadcasted_iota(jnp.int32, (keys, frames), 0) < live, 0.0, masked_score
    ).astype(f32)


def key_blocks(info, k_ref, v_ref, frames):
    keys = k_ref.shape[0]
    k, v, masks = [], [], []
    for index in range(2):
        start, live = key_half(info, index, frames, keys)
        here = pl.ds(start if index == 0 else pl.multiple_of(start, keys // 2), keys // 2)
        k.append(k_ref[here, :])
        v.append(v_ref[here, :])
        masks.append(half_mask(live, keys // 2, frames // 2))
    return k, v, jnp.concatenate(masks, axis=1)


def cross_attend(info, q, k_ref, v_ref, lse_ref):
    half = q.shape[0] // 2
    q_turned = (q * jnp.bfloat16(0.125)).T
    k, v, mask = key_blocks(info, k_ref, v_ref, 2 * half)
    v_turned = [values.T for values in v]
    outs = []
    for h in range(q.shape[1] // HEAD):
        c = slice(h * HEAD, (h + 1) * HEAD)
        s = [product_plain(k[i][:, c], q_turned[c, i * half : (i + 1) * half]) for i in range(2)]
        s = jnp.concatenate(s, axis=1) + mask
        m = jnp.max(s, axis=0, keepdims=True)
        e = jnp.exp(s - m)
        total = jnp.sum(e, axis=0, keepdims=True)
        lse_ref[h : h + 1, :] = m + jnp.log(total)
        e = e.astype(low)
        o = [product_plain(v_turned[i][c, :], e[:, i * half : (i + 1) * half]) for i in range(2)]
        outs.append(jnp.concatenate(o, axis=1) * (1.0 / total))
    return jnp.concatenate(outs, axis=0).T.astype(low)


def cross_attend_back(info, q, k_ref, v_ref, g, att, lse):
    half = q.shape[0] // 2
    scaled = q * jnp.bfloat16(0.125)
    q_turned = scaled.T
    g_turned = g.T
    weighted = g_turned.astype(f32) * att.T.astype(f32)
    k, v, mask = key_blocks(info, k_ref, v_ref, 2 * half)
    k_turned = [values.T for values in k]
    parts = [slice(0, half), slice(half, 2 * half)]
    dq, dk, dv = [], [[], []], [[], []]
    for h in range(q.shape[1] // HEAD):
        c = slice(h * HEAD, (h + 1) * HEAD)
        s = [product_plain(k[i][:, c], q_turned[c, parts[i]]) for i in range(2)]
        dp = [product_plain(v[i][:, c], g_turned[c, parts[i]]) for i in range(2)]
        p = jnp.exp(jnp.concatenate(s, axis=1) + (mask - lse[h : h + 1, :]))
        inner = jnp.sum(weighted[c, :], axis=0, keepdims=True)
        ds = (p * (jnp.concatenate(dp, axis=1) - inner)).astype(low)
        p = p.astype(low)
        dq.append(
            jnp.concatenate(
                [product_plain(k_turned[i][c, :], ds[:, parts[i]]) for i in range(2)], axis=1
            )
        )
        for i in range(2):
            dk[i].append(product_plain(ds[:, parts[i]], scaled[parts[i], c]))
            dv[i].append(product_plain(p[:, parts[i]], g[parts[i], c]))
    second = (info[0] < 2 * half).astype(f32)

    def by_row(halves):
        first, last = (jnp.concatenate(half, axis=1) for half in halves)
        return jnp.concatenate([first + last * (1.0 - second), last * second], axis=0)

    return jnp.concatenate(dq, axis=0).T * 0.125, by_row(dk), by_row(dv)


def norm_back_rows(x,e,gain,above,gain_acc,shift_acc):
    average=jnp.mean(x,axis=-1,keepdims=True)
    centered=x-average
    variance=jnp.mean(centered*centered,axis=-1,keepdims=True)
    inverse=lax.rsqrt(variance+norm_eps)
    n=centered*inverse
    en=e*n
    w=e*gain
    mean_w=jnp.mean(w,axis=-1,keepdims=True)
    mean_wn=jnp.mean(en*gain,axis=-1,keepdims=True)
    fold=lambda t: jnp.sum(t.reshape(t.shape[0]//8,8,t.shape[1]),axis=0)
    gain_acc[...]+=fold(en)
    shift_acc[...]+=fold(e)
    return above+inverse*(w-mean_w-n*mean_wn)

def norm_back_step(x, mine, other, above, gain, total, total_low, kept, vectors, gain_acc, shift_acc):
    step, block = pl.program_id(0), x.shape[0]

    @pl.when(step == 0)
    def _():
        gain_acc[...] = jnp.zeros_like(gain_acc)
        shift_acc[...] = jnp.zeros_like(shift_acc)

    @pl.when(step < BLOCKS)
    def _():
        def rows(r):
            e = mine[r, :].astype(f32) + other[r, :].astype(f32)
            t = norm_back_rows(x[r, :], e, gain[...][None], above[r, :], gain_acc, shift_acc)
            total[r, :] = t
            total_low[r, :] = t.astype(low)
            kept[within(step, block, r), :] = t.astype(low)

        over_rows(block, rows)

    @pl.when(step == BLOCKS - 1)
    def _():
        vectors[0:1, :] = jnp.sum(gain_acc[...], axis=0, keepdims=True)
        vectors[1:2, :] = jnp.sum(shift_acc[...], axis=0, keepdims=True)


def ordered(kernel, token, args, in_specs, out_specs, out_shape, grid, flops, scratch=(), info=None, brief=False):
    if info is None:
        info = jnp.zeros((1,), jnp.int32)
    inputs, outputs = len(args), len(out_shape)

    def body(info_ref, *refs):
        token_ref = refs[inputs + 1 + outputs]

        @pl.when(functools.reduce(jnp.logical_and, [pl.program_id(i) == 0 for i in range(len(grid))]))
        def _():
            token_ref[...] = jnp.zeros_like(token_ref)

        kernel(
            info_ref,
            *refs[:inputs],
            *refs[inputs + 1 : inputs + 1 + outputs],
            *refs[inputs + 2 + outputs :],
        )

    moved = sum(math.prod(a.shape) * a.dtype.itemsize for a in (*args, *out_shape))
    *results, token = pl.pallas_call(
        body,
        grid_spec=pltpu.PrefetchScalarGridSpec(
            num_scalar_prefetch=1,
            grid=grid,
            in_specs=[*in_specs, pl.BlockSpec(memory_space=pl.ANY)],
            out_specs=[*out_specs, pl.BlockSpec((8, 128), lambda *_: (0, 0))],
            scratch_shapes=list(scratch),
        ),
        out_shape=[*out_shape, sds((8, 128), f32)],
        compiler_params=pltpu.CompilerParams(vmem_limit_bytes=VMEM_LIMIT),
        cost_estimate=pl.CostEstimate(flops=0 if brief else max(FLOOR, int(flops * COST)), bytes_accessed=0 if brief else int(moved * COST), transcendentals=0),
    )(info, *args, token)
    return (*results, token)


def hold(token, values, brief=False):
    def nothing(values_ref, token_ref, out_ref, token_out):
        token_out[...] = jnp.zeros_like(token_out)

    return pl.pallas_call(
        nothing,
        in_specs=[pl.BlockSpec(memory_space=pl.ANY)] * 2,
        out_specs=[pl.BlockSpec(memory_space=pl.ANY), pl.BlockSpec(memory_space=pltpu.VMEM)],
        out_shape=[sds(values.shape, values.dtype), sds((8, 128), f32)],
        input_output_aliases={0: 0},
        compiler_params=pltpu.CompilerParams(vmem_limit_bytes=VMEM_LIMIT),
        cost_estimate=pl.CostEstimate(flops=0 if brief else FLOOR, bytes_accessed=0, transcendentals=0),
    )(values, token)


def specs(frames, width, tile, blocks=0):
    def tile_of(j):
        return jnp.maximum(j - blocks, 0) if blocks else j

    whole = pl.BlockSpec((frames, width), lambda j, *_: (0, 0))
    vector = pl.BlockSpec((width,), lambda j, *_: (0,))
    column = pl.BlockSpec((width, tile), lambda j, *_: (0, tile_of(j)))
    row = pl.BlockSpec((tile, width), lambda j, *_: (tile_of(j), 0))
    act = pl.BlockSpec((frames, tile), lambda j, *_: (0, tile_of(j)))
    table = pl.BlockSpec((frames, 2 * HEAD), lambda j, *_: (0, 0))
    logsum = pl.BlockSpec((8, frames), lambda j, *_: (tile_of(j), 0))
    return whole, vector, column, row, act, table, logsum


BLOCKS = 4


def widened(*tables):
    return tuple(jnp.concatenate([table[...], table[...]], axis=1) for table in tables)


def row_block(frames, width):
    return pl.BlockSpec((frames // BLOCKS, width), lambda j, *_: (jnp.minimum(j, BLOCKS - 1), 0))


def copies_block(frames, width, place):
    return pl.BlockSpec(
        (PLANE, frames // BLOCKS, width),
        lambda j, info: (0, jnp.clip(j - BLOCKS // 2 * info[place], 0, BLOCKS // 2 - 1), 0),
    )


def within(step, rows, r):
    return pl.ds(pl.multiple_of(step * rows + r.start, r.size), r.size)


def added(acc, term, result, first=0):
    step = pl.program_id(0)

    @pl.when(step == first)
    def _():
        acc[...] = term

    @pl.when(step != first)
    def _():
        acc[...] += term

    @pl.when(step == pl.num_programs(0) - 1)
    def _():
        result[...] = acc[...].astype(result.dtype)


def self_kernel(info, hid, gain, shift, wq, wk, wv, wo, cos, lower, upper, grad, copies, grad_copies, q, k, v, att, logsum, part, acc, mask, normed):
    step, frames, block = pl.program_id(0), normed.shape[0], hid.shape[0]

    @pl.when(step == 0)
    def _():
        mask[...] = self_mask(info[0], frames)

    @pl.when(step < BLOCKS)
    def _():
        def rows(r):
            normed[within(step, block, r), :] = normed_rows(hid[r, :], gain[...][None], shift[...][None]).astype(low)

        over_rows(block, rows)

    @pl.when((step < BLOCKS) & (step * 2 // BLOCKS == info[3]))
    def _():
        mine = normed[pl.ds(pl.multiple_of(step * block, block), block), :]
        for chip in range(PLANE):
            copies[chip] = mine

    @pl.when(step < BLOCKS // 2)
    def _():
        grad_low = grad[...].astype(low)
        for chip in range(PLANE):
            grad_copies[chip] = grad_low

    @pl.when(step >= BLOCKS)
    def _():
        n = normed[...]
        tables = widened(cos, lower, upper)
        q[...] = turn(product_plain(n, wq[...]), *tables).astype(low)
        k[...] = turn(product_plain(n, wk[...]), *tables).astype(low)
        v[...] = product_plain(n, wv[...]).astype(low)
        attended = attend(q[...], k[...], v[...], mask[...], logsum)
        att[...] = attended
        added(acc, product_plain(attended, wo[...]), part, BLOCKS)


def self_forward(token, info, hid, gain, shift, wq, wk, wv, wo, tables, grad, tile=4 * HEAD):
    frames, width = hid.shape
    columns = wq.shape[1]
    whole, vector, column, row, act, table, logsum = specs(frames, width, tile, BLOCKS)
    blocks = row_block(frames, width)
    here = frames // BLOCKS
    return ordered(
        self_kernel,
        token,
        (hid, gain, shift, wq, wk, wv, wo, *tables, grad),
        [blocks, vector, vector, column, column, column, row, table, table, table]
        + [
            pl.BlockSpec(
                (here, width),
                lambda j, info: (BLOCKS // 2 * info[3] + jnp.minimum(j, BLOCKS // 2 - 1), 0),
            )
        ],
        [
            copies_block(frames, width, 3),
            pl.BlockSpec((PLANE, here, width), lambda j, info: (0, jnp.minimum(j, BLOCKS // 2 - 1), 0)),
        ]
        + [act, act, act, act, logsum, whole],
        [sds((PLANE, frames // 2, width), low)] * 2
        + [sds((frames, columns), low)] * 4
        + [sds((columns // tile * 8, frames), f32), sds((frames, width), low)],
        (BLOCKS + columns // tile,),
        2 * frames * columns * (4 * width + 8 * frames),
        [
            pltpu.VMEM((frames, width), f32),
            pltpu.VMEM((frames, frames), f32),
            pltpu.VMEM((frames, width), low),
        ],
        info,
    )


def cross_kernel(info, hid, mine, other, gain, shift, cq, ck, cv, co, total, normed, q, att, logsum, part, acc, kept):
    step, block = pl.program_id(0), hid.shape[0]

    @pl.when(step < BLOCKS)
    def _():
        def rows(r):
            x = hid[r, :] + (mine[r, :].astype(f32) + other[r, :].astype(f32))
            total[r, :] = x
            n = normed_rows(x, gain[...][None], shift[...][None]).astype(low)
            normed[r, :] = n
            kept[within(step, block, r), :] = n

        over_rows(block, rows)

    @pl.when(step >= BLOCKS)
    def _():
        q[...] = product_plain(kept[...], cq[...]).astype(low)
        attended = cross_attend(info, q[...], ck, cv, logsum)
        att[...] = attended
        added(acc, product_plain(attended, co[...]), part, BLOCKS)


def cross_forward(token, info, hid, mine, other, gain, shift, cq, ck, cv, co, tile=4 * HEAD):
    frames, width = hid.shape
    columns, keys = cq.shape[1], ck.shape[0]
    whole, vector, column, row, act, table, logsum = specs(frames, width, tile, BLOCKS)
    key = pl.BlockSpec((keys, tile), lambda j, *_: (0, jnp.maximum(j - BLOCKS, 0)))
    blocks = row_block(frames, width)
    return ordered(
        cross_kernel,
        token,
        (hid, mine, other, gain, shift, cq, ck, cv, co),
        [blocks, blocks, blocks, vector, vector, column, key, key, row],
        [blocks, blocks, act, act, logsum, whole],
        [
            sds((frames, width), f32),
            sds((frames, width), low),
            sds((frames, columns), low),
            sds((frames, columns), low),
            sds((columns // tile * 8, frames), f32),
            sds((frames, width), low),
        ],
        (BLOCKS + columns // tile,),
        2 * frames * columns * (2 * width + 8 * keys),
        [pltpu.VMEM((frames, width), f32), pltpu.VMEM((frames, width), low)],
        info,
        brief=True,
    )


def norm_kernel(info, hid, mine, other, gain, shift, total, normed, copies):
    def rows(r):
        x = hid[r, :] + (mine[r, :].astype(f32) + other[r, :].astype(f32))
        total[r, :] = x
        normed[r, :] = normed_rows(x, gain[...][None], shift[...][None]).astype(low)

    over_rows(hid.shape[0], rows)

    @pl.when(pl.program_id(0) * 2 // pl.num_programs(0) == info[0])
    def _():
        values = normed[...]
        for chip in range(PLANE):
            copies[chip] = values


def norm_forward(token, info, hid, mine, other, gain, shift, block=128):
    frames, width = hid.shape
    blocks = frames // (2 * block)
    rows = pl.BlockSpec((block, width), lambda j, *_: (j, 0))
    vector = pl.BlockSpec((width,), lambda j, *_: (0,))
    return ordered(
        norm_kernel,
        token,
        (hid, mine, other, gain, shift),
        [rows, rows, rows, vector, vector],
        [
            rows,
            rows,
            pl.BlockSpec(
                (PLANE, block, width),
                lambda j, info: (0, jnp.clip(j - blocks * info[0], 0, blocks - 1), 0),
            ),
        ],
        [sds((frames, width), f32), sds((frames, width), low), sds((PLANE, frames // 2, width), low)],
        (frames // block,),
        10 * frames * width,
        info=info,
        brief=True,
    )


def cross_back_kernel(info, x, mine, other, above, gain, co, q, ck, cv, att, logsum, cq, total, total_low, vectors, dq, dk, dv, part, acc, gain_acc, shift_acc, kept):
    norm_back_step(x, mine, other, above, gain, total, total_low, kept, vectors, gain_acc, shift_acc)

    @pl.when(pl.program_id(0) >= BLOCKS)
    def _():
        g = product_with_rows(kept[...], co[...]).astype(low)
        a, b, c = cross_attend_back(info, q[...], ck, cv, g, att[...], logsum[...])
        a = a.astype(low)
        dq[...] = a
        dk[...] = b.astype(low)
        dv[...] = c.astype(low)
        added(acc, product_with_rows(a, cq[...]), part, BLOCKS)


def cross_backward(token, info, x, mine, other, above, gain, co, q, ck, cv, att, logsums, cq, tile=4 * HEAD):
    frames, width = x.shape
    columns, keys = cq.shape[1], ck.shape[0]
    whole, vector, column, row, act, table, logsum = specs(frames, width, tile, BLOCKS)
    key = pl.BlockSpec((keys, tile), lambda j, *_: (0, jnp.maximum(j - BLOCKS, 0)))
    blocks = row_block(frames, width)
    two = pl.BlockSpec((2, width), lambda j, *_: (0, 0))
    return ordered(
        cross_back_kernel,
        token,
        (x, mine, other, above, gain, co, q, ck, cv, att, logsums, cq),
        [blocks, blocks, blocks, blocks, vector, row, act, key, key, act, logsum, column],
        [blocks, blocks, two, act, key, key, whole],
        [
            sds((frames, width), f32),
            sds((frames, width), low),
            sds((2, width), f32),
            sds((frames, columns), low),
            sds((keys, columns), low),
            sds((keys, columns), low),
            sds((frames, width), low),
        ],
        (BLOCKS + columns // tile,),
        2 * frames * columns * (2 * width + 20 * keys),
        [
            pltpu.VMEM((frames, width), f32),
            pltpu.VMEM((8, width), f32),
            pltpu.VMEM((8, width), f32),
            pltpu.VMEM((frames, width), low),
        ],
        info,
    )


def self_back_kernel(info, x, mine, other, above, gain, wo, q, k, v, att, logsum, wq, wk, wv, cos, lower, upper, total, total_low, vectors, grads, part, acc, mask, gain_acc, shift_acc, kept):
    step = pl.program_id(0)

    @pl.when(step == 0)
    def _():
        mask[...] = self_mask(info[0], kept.shape[0])

    norm_back_step(x, mine, other, above, gain, total, total_low, kept, vectors, gain_acc, shift_acc)

    @pl.when(step >= BLOCKS)
    def _():
        g = product_with_rows(kept[...], wo[...]).astype(low)
        a, b, c = attend_back(q[...], k[...], v[...], g, att[...], mask[...], logsum[...])
        tables = widened(cos, lower, upper)
        a = turn_back(a, *tables).astype(low)
        b = turn_back(b, *tables).astype(low)
        c = c.astype(low)
        for index, values in enumerate((a, b, c)):
            turned = values.T
            for quarter in range(PLANE):
                grads[quarter, index] = turned[quarter * HEAD : (quarter + 1) * HEAD]
        back = product_with_rows(a, wq[...]) + product_with_rows(b, wk[...])
        added(acc, back + product_with_rows(c, wv[...]), part, BLOCKS)


def self_backward(token, info, x, mine, other, above, gain, wo, q, k, v, att, logsums, wq, wk, wv, tables, tile=4 * HEAD):
    frames, width = x.shape
    columns = wq.shape[1]
    whole, vector, column, row, act, table, logsum = specs(frames, width, tile, BLOCKS)
    blocks = row_block(frames, width)
    two = pl.BlockSpec((2, width), lambda j, *_: (0, 0))
    heads = pl.BlockSpec(
        (PLANE, 3, HEAD, frames), lambda j, *_: (0, 0, jnp.maximum(j - BLOCKS, 0), 0)
    )
    return ordered(
        self_back_kernel,
        token,
        (x, mine, other, above, gain, wo, q, k, v, att, logsums, wq, wk, wv, *tables),
        [blocks] * 4
        + [vector, row, act, act, act, act, logsum, column, column, column, table, table, table],
        [blocks, blocks, two, heads, whole],
        [
            sds((frames, width), f32),
            sds((frames, width), low),
            sds((2, width), f32),
            sds((PLANE, 3, columns // PLANE, frames), low),
            sds((frames, width), low),
        ],
        (BLOCKS + columns // tile,),
        2 * frames * columns * (4 * width + 20 * frames),
        [
            pltpu.VMEM((frames, width), f32),
            pltpu.VMEM((frames, frames), f32),
            pltpu.VMEM((8, width), f32),
            pltpu.VMEM((8, width), f32),
            pltpu.VMEM((frames, width), low),
        ],
        info,
    )


def last_kernel(_, x, mine, other, above, gain, resid, sum_mine, sum_other, total, vectors, result, gain_acc, shift_acc):
    step = pl.program_id(0)

    @pl.when(step == 0)
    def _():
        gain_acc[...] = jnp.zeros_like(gain_acc)
        shift_acc[...] = jnp.zeros_like(shift_acc)

    def rows(r):
        e = mine[r, :].astype(f32) + other[r, :].astype(f32)
        total[r, :] = norm_back_rows(x[r, :], e, gain[...][None], above[r, :], gain_acc, shift_acc)
        result[r, :] = resid[r, :] + (sum_mine[r, :].astype(f32) + sum_other[r, :].astype(f32))

    over_rows(x.shape[0], rows)

    @pl.when(step == pl.num_programs(0) - 1)
    def _():
        vectors[0:1, :] = jnp.sum(gain_acc[...], axis=0, keepdims=True)
        vectors[1:2, :] = jnp.sum(shift_acc[...], axis=0, keepdims=True)


def last_backward(token, x, mine, other, above, gain, resid, sum_mine, sum_other, block=128):
    frames, width = x.shape
    rows = pl.BlockSpec((block, width), lambda j, *_: (j, 0))
    vector = pl.BlockSpec((width,), lambda j, *_: (0,))
    two = pl.BlockSpec((2, width), lambda j, *_: (0, 0))
    return ordered(
        last_kernel,
        token,
        (x, mine, other, above, gain, resid, sum_mine, sum_other),
        [rows, rows, rows, rows, vector, rows, rows, rows],
        [rows, two, rows],
        [sds((frames, width), f32), sds((2, width), f32), sds((frames, width), f32)],
        (frames // block,),
        20 * frames * width,
        [pltpu.VMEM((8, width), f32), pltpu.VMEM((8, width), f32)],
        brief=True,
    )


def ff_kernel(_, in_ref, out_ref, gate_ref, up_ref, down_ref, sum_ref, back_ref, sum_acc, back_acc, out_low):
    @pl.when(pl.program_id(0) == 0)
    def _():
        out_low[...] = out_ref[...].astype(low)

    normed = in_ref[...]
    mixed, grad_gate, grad_up = ff_parts(
        product_plain(normed, gate_ref[...]),
        product_plain(normed, up_ref[...]),
        product_with_rows(out_low[...], down_ref[...]),
    )
    added(sum_acc, product_plain(mixed, down_ref[...]), sum_ref)
    added(
        back_acc,
        product_with_rows(grad_gate, gate_ref[...]) + product_with_rows(grad_up, up_ref[...]),
        back_ref,
    )


def ff_both(token, normed, grad_out, w_gate, w_up, w_down, tile=768):
    frames, width = normed.shape
    units = w_gate.shape[1]
    whole, _, column, row, *_ = specs(frames, width, tile)
    return ordered(
        ff_kernel,
        token,
        (normed, grad_out, w_gate, w_up, w_down),
        [whole, whole, column, column, row],
        [whole, whole],
        [sds((frames, width), low)] * 2,
        (units // tile,),
        12 * frames * width * units,
        [pltpu.VMEM((frames, width), f32)] * 2 + [pltpu.VMEM((frames, width), low)],
    )


def share_kernel(info, in_mine, in_other, out_mine, out_other, gate_ref, up_ref, down_ref, send_ref, keep_ref, acc):
    step = pl.program_id(1)
    normed = jnp.concatenate([in_mine[...], in_other[...]], axis=0)
    grad_out = jnp.concatenate([out_mine[...], out_other[...]], axis=0)
    mixed, grad_gate, grad_up = ff_parts(
        product_plain(normed, gate_ref[...]),
        product_plain(normed, up_ref[...]),
        product_with_rows(grad_out, down_ref[...]),
    )
    fresh = (
        product_over_rows(grad_out, mixed),
        product_over_rows(normed, grad_gate),
        product_over_rows(normed, grad_up),
    )
    for index, term in enumerate(fresh):

        @pl.when(step == 0)
        def _():
            acc[index] = term

        @pl.when(step != 0)
        def _():
            acc[index] += term

    @pl.when(step == pl.num_programs(1) - 1)
    def _():
        rows = send_ref.shape[2] // 3
        for pair in range(2):
            for index in range(3):
                for ref, parity in ((send_ref, 1 - info[1]), (keep_ref, info[1])):
                    start = pl.multiple_of((2 * pair + parity) * rows, rows)
                    ref[0, pair, index * rows : (index + 1) * rows] = acc[
                        index, pl.ds(start, rows), :
                    ].astype(ref.dtype)


def ff_share(token, info, normed, grad_out, w_gate, w_up, w_down, tile, first, count):
    frames, width = normed[0].shape
    chunk = frames // PLANE
    rows = pl.BlockSpec((chunk, width), lambda i, j, info: (j, 0))
    column = pl.BlockSpec((width, tile), lambda i, j, info: (0, info[0] + first + i))
    half = (LEVELS // 2, 3 * width // LEVELS, tile)
    return ordered(
        share_kernel,
        token,
        (*normed, *grad_out, w_gate, w_up, w_down),
        [rows] * 4
        + [column, column, pl.BlockSpec((tile, width), lambda i, j, info: (info[0] + first + i, 0))],
        [pl.BlockSpec((1, *half), lambda i, j, info: (i, 0, 0, 0))] * 2,
        [sds((count, *half), low)] * 2,
        (count, PLANE),
        24 * frames * width * tile * count,
        [pltpu.VMEM((3, width, tile), f32)],
        info,
    )


def weight_kernel(plan, sides_count, _, *refs):
    sides, columns = refs[:sides_count], refs[sides_count : sides_count + len(plan)]
    out = refs[sides_count + len(plan)]
    turned = refs[sides_count + len(plan) + 1 :]

    @pl.when(pl.program_id(0) == 0)
    def _():
        for side, ref in zip(sides, turned):
            ref[...] = side[...].T

    for (which, first), column in zip(plan, columns):
        product = product_plain(turned[which][...], column[...]).astype(low)
        rows = product.shape[0] // (PLANE * LEVELS)
        product = product.reshape(LEVELS, PLANE, rows, product.shape[1])
        for owner in range(PLANE):
            out[owner, :, first : first + rows, :] = product[:, owner]


def weight_products(token, sides, plan, columns, tile=256):
    width = columns[0].shape[1]
    rows = sum(sides[which].shape[1] for which, _ in plan) // (PLANE * LEVELS)
    return ordered(
        functools.partial(weight_kernel, plan, len(sides)),
        token,
        (*sides, *columns),
        [pl.BlockSpec(side.shape, lambda j, *_: (0, 0)) for side in sides]
        + [pl.BlockSpec((column.shape[0], tile), lambda j, *_: (0, j)) for column in columns],
        [pl.BlockSpec((PLANE, LEVELS, rows, tile), lambda j, *_: (0, 0, 0, j))],
        [sds((PLANE, LEVELS, rows, width), low)],
        (width // tile,),
        sum(2 * sides[w].shape[0] * sides[w].shape[1] * width for w, _ in plan),
        [pltpu.VMEM((side.shape[1], side.shape[0]), low) for side in sides],
        brief=len(sides) == 1,
    )


def out_kernel(_, side, column, first, second, third, out, turned):
    step = pl.program_id(0)

    @pl.when(step == 0)
    def _():
        turned[...] = side[...].T

    def store(values):
        values = values.astype(low).reshape(LEVELS, PLANE, out.shape[2], out.shape[3])
        for owner in range(PLANE):
            out[owner] = values[:, owner]

    @pl.when(step < pl.num_programs(0) - 1)
    def _():
        store(product_plain(turned[...], column[...]))

    @pl.when(step == pl.num_programs(0) - 1)
    def _():
        empty = jnp.zeros((out.shape[3] - 6, side.shape[1]), f32)
        store(jnp.concatenate([first[...], second[...], third[...], empty], axis=0).T)


def out_products(token, side, column, vectors, tile=128):
    frames, width = side.shape
    columns = column.shape[1]
    tiles = columns // tile
    rows = width // (PLANE * LEVELS)
    return ordered(
        out_kernel,
        token,
        (side, column, *vectors),
        [
            pl.BlockSpec((frames, width), lambda j, *_: (0, 0)),
            pl.BlockSpec((frames, tile), lambda j, *_: (0, jnp.minimum(j, tiles - 1))),
        ]
        + [pl.BlockSpec((2, width), lambda j, *_: (0, 0))] * 3,
        [pl.BlockSpec((PLANE, LEVELS, rows, tile), lambda j, *_: (0, 0, 0, j))],
        [sds((PLANE, LEVELS, rows, columns + tile), low)],
        (tiles + 1,),
        0,
        [pltpu.VMEM((width, frames), low)],
        brief=True,
    )


def plane_sum_kernel(info, got, send, keep):
    for ref, parity in ((send, 1 - info[0]), (keep, info[0])):
        total = got[0, 0, parity].astype(f32)
        for source in range(1, PLANE):
            total = total + got[source, 0, parity].astype(f32)
        ref[0] = total.astype(low)


def plane_sum(token, got, info):
    rows, width = got.shape[2:]
    out = pl.BlockSpec((1, rows, width), lambda j, *_: (j, 0, 0))
    return ordered(
        plane_sum_kernel,
        token,
        (got.reshape(PLANE, 2, 2, rows, width),),
        [pl.BlockSpec((PLANE, 1, 2, rows, width), lambda j, *_: (0, j, 0, 0, 0))],
        [out, out],
        [sds((2, rows, width), low)] * 2,
        (2,),
        0,
        info=info,
    )


def level_sum_kernel(_, keep_pass, got_pass, keep_own, got_own, passed, own):
    passed[...] = (keep_pass[0, 0].astype(f32) + got_pass[0, 0].astype(f32)).astype(low)
    own[...] = keep_own[0, 0].astype(f32) + got_own[0, 0].astype(f32)


def level_sum(token, keep, got, info, brief=True):
    count, _, rows, width = keep.shape
    block = rows // 2 if rows % 32 == 0 else rows
    steps = rows // block
    off = pl.BlockSpec((1, 1, block, width), lambda i, j, info: (i, 1 - info[0], j, 0))
    own = pl.BlockSpec((1, 1, block, width), lambda i, j, info: (i, info[0], j, 0))
    out = pl.BlockSpec((block, width), lambda i, j, info: (i * steps + j, 0))
    return ordered(
        level_sum_kernel,
        token,
        (keep, got, keep, got),
        [off, off, own, own],
        [out, out],
        [sds((count * rows, width), low), sds((count * rows, width), f32)],
        (count, steps),
        0,
        info=info,
        brief=brief,
    )


def unit_pack_kernel(counts, _, *refs):
    owns, lasts, out = refs[:-1:2], refs[1:-1:2], refs[-1]
    step = pl.program_id(0)
    for own, last, (first, count) in zip(owns, lasts, counts):

        @pl.when((step >= first) & (step < first + count))
        def _():
            total = (own[...] + last[...].astype(f32)).astype(low)
            total = total.reshape(3, PLANE, out.shape[2], out.shape[3])
            for chip in range(PLANE):
                out[chip] = total[:, chip]


def unit_pack(token, sums, rows):
    tile = sums[0][0].shape[1]
    r = rows // (3 * PLANE)
    specs_in, counts, first = [], [], 0
    for own, _ in sums:
        count = own.shape[0] // rows

        def place(j, info, first=first, count=count):
            return (jnp.clip(j - first, 0, count - 1), 0)

        specs_in += [pl.BlockSpec((rows, tile), place)] * 2
        counts.append((first, count))
        first += count
    return ordered(
        functools.partial(unit_pack_kernel, counts),
        token,
        tuple(array for pair in sums for array in pair),
        specs_in,
        [pl.BlockSpec((PLANE, 3, r, tile), lambda j, *_: (0, 0, 0, j))],
        [sds((PLANE, 3, r, tile * first), low)],
        (first,),
        0,
    )


def unit_unpack_kernel(_, got, down, gate, up):
    down[...] = got[0, 0].astype(f32).T
    gate[...] = got[0, 1].astype(f32)
    up[...] = got[0, 2].astype(f32)


def unit_unpack(token, got):
    _, _, r, units = got.shape
    across = pl.BlockSpec((r, units), lambda j, *_: (0, j))
    return ordered(
        unit_unpack_kernel,
        token,
        (got,),
        [pl.BlockSpec((1, 3, r, units), lambda j, *_: (j, 0, 0, 0))],
        [pl.BlockSpec((units, r), lambda j, *_: (j, 0)), across, across],
        [sds((PLANE * units, r), f32)] + [sds((r, PLANE * units), f32)] * 2,
        (PLANE,),
        0,
        brief=True,
    )


def head_pack_kernel(_, own, last, out):
    total = (own[...] + last[...].astype(f32)).T.astype(low)
    out[...] = total.reshape(out.shape)


def head_pack(token, own, last):
    features, columns = own.shape
    shape = (PLANE, columns // PLANE, features)
    return ordered(
        head_pack_kernel,
        token,
        (own, last),
        [pl.BlockSpec(own.shape, lambda j, *_: (0, 0))] * 2,
        [pl.BlockSpec(shape, lambda j, *_: (0, 0, 0))],
        [sds(shape, low)],
        (1,),
        0,
        brief=True,
    )


def head_unpack_kernel(_, got, *outs):
    groups = got.shape[2] // (3 * HEAD)
    for index, out in enumerate(outs):
        pieces = []
        for group in range(groups):
            first = (index * groups + group) * HEAD
            pieces += [got[chip, :, first : first + HEAD] for chip in range(PLANE)]
        out[...] = jnp.concatenate(pieces, axis=1).astype(f32)


def head_unpack(token, got):
    chips, r, features = got.shape
    shape = (r, chips * features // 3)
    return ordered(
        head_unpack_kernel,
        token,
        (got,),
        [pl.BlockSpec(got.shape, lambda j, *_: (0, 0, 0))],
        [pl.BlockSpec(shape, lambda j, *_: (0, 0))] * 3,
        [sds(shape, f32)] * 3,
        (1,),
        0,
    )


def head_kernel(info, grads_mine, grads_other, in_mine, in_other, send, keep, acc):
    step = pl.program_id(0)
    rows = acc.shape[0]
    term = product_plain(grads_mine[0].reshape(rows, -1), in_mine[...]) + product_plain(
        grads_other[0].reshape(rows, -1), in_other[...]
    )

    @pl.when(step == 0)
    def _():
        acc[...] = term

    @pl.when(step != 0)
    def _():
        acc[...] += term

    @pl.when(step == pl.num_programs(0) - 1)
    def _():
        width = send.shape[2]
        for level in range(LEVELS):
            for ref, parity in ((send, 1 - info[1]), (keep, info[1])):

                @pl.when(parity == level % 2)
                def _():
                    ref[level // 2] = acc[:, level * width : (level + 1) * width].astype(low)


def head_products(token, info, grads, normed):
    _, three, features, frames = grads.shape
    width = normed[0].shape[1]
    chunk = normed[0].shape[0] // PLANE
    rows = pl.BlockSpec((chunk, width), lambda j, info: (j, 0))
    half = (LEVELS // 2, three * features, width // LEVELS)
    return ordered(
        head_kernel,
        token,
        (grads, grads, *normed),
        [
            pl.BlockSpec((1, three, features, chunk), lambda j, info: (j, 0, 0, info[0])),
            pl.BlockSpec((1, three, features, chunk), lambda j, info: (j, 0, 0, 1 - info[0])),
            rows,
            rows,
        ],
        [pl.BlockSpec(half, lambda j, info: (0, 0, 0))] * 2,
        [sds(half, low)] * 2,
        (PLANE,),
        2 * three * features * PLANE * frames * width,
        [pltpu.VMEM((three * features, width), f32)],
        info,
        brief=True,
    )


def on_plane(
    hidden_in,
    out_grad,
    prompt_states,
    row_split,
    prompt_len,
    gain_attn,
    bias_attn,
    gain_cross,
    bias_cross,
    gain_ff,
    bias_ff,
    w_query,
    w_key,
    w_value,
    w_out,
    c_query,
    c_key,
    c_value,
    c_out,
    w_gate,
    w_up,
    w_down,
):
    frames, width = hidden_in.shape
    plane, level = lax.axis_index("dp") % PLANE, lax.axis_index("dp") // PLANE
    positions = jnp.arange(frames, dtype=jnp.int32)
    row_ids = (positions >= row_split[0]).astype(jnp.int32)
    tables = rotary_tables((positions - row_ids * row_split[0]).astype(f32), 2 * HEAD)

    tile = 256
    tiles = w_gate.shape[1] // (PLANE * tile)
    zero = jnp.zeros((1,), jnp.int32)
    half = zero + lax.axis_index("tensor")
    parity, upper = zero + level % 2, zero + level // 2
    info = jnp.concatenate([row_split, prompt_len, half])
    unit_info = jnp.concatenate([zero + plane * tiles, parity])
    head_info = jnp.concatenate([half, parity])
    chips = [[PLANE * z + p for p in range(PLANE)] for z in range(LEVELS)]

    def swapped(part):
        return lax.ppermute(part, "tensor", [(0, 1), (1, 0)])

    def in_plane(values):
        shape = values.shape
        return lax.all_to_all(
            values, "dp", 0, 0, axis_index_groups=chips, tiled=True
        ).reshape(shape)

    def gathered(copies):
        return in_plane(copies.reshape(-1, width))

    def level_swap(values, mask):
        return lax.ppermute(values, "dp", pairs(mask))

    token = jnp.zeros((8, 128), f32)
    context = prompt_states.reshape(2 * PROMPT, prompt_states.shape[2])
    cross_key = product_plain(context, c_key).astype(low)
    cross_value = product_plain(context, c_value).astype(low)
    copies_one, copies, query, key, value, attended_one, logsum_one, part, token = self_forward(
        token,
        info,
        hidden_in,
        gain_attn,
        bias_attn,
        w_query,
        w_key,
        w_value,
        w_out,
        tables,
        out_grad,
    )
    part_swapped = swapped(part)
    frames_out = gathered(copies)
    resid_one, input_two, cross_query, attended_two, logsum_two, part, token = cross_forward(
        token,
        info,
        hidden_in,
        part,
        part_swapped,
        gain_cross,
        bias_cross,
        c_query,
        cross_key,
        cross_value,
        c_out,
    )
    part_swapped = swapped(part)
    resid_two, input_three, copies, token = norm_forward(
        token, half, resid_one, part, part_swapped, gain_ff, bias_ff
    )
    frames_out, token = hold(token, frames_out)
    frames_in = gathered(copies)
    frames_out = (frames_out, swapped(frames_out))
    sum_part, back_part, token = ff_both(token, input_three, out_grad, w_gate, w_up, w_down)
    frames_in, token = hold(token, frames_in)
    frames_in = (frames_in, swapped(frames_in))
    back_swapped = swapped(back_part)
    copies_one, token = hold(token, copies_one)
    frames_one = gathered(copies_one)

    def share(token, index, count):
        return ff_share(token, unit_info, frames_in, frames_out, w_gate, w_up, w_down, tile, index, count)

    send_a, keep_a, token = share(token, 0, 1)
    got_a = level_swap(send_a, PLANE)
    grad_two, grad_cross_out, vectors_ff, query_grad, key_grad, value_grad, part, token = cross_backward(
        token,
        info,
        resid_two,
        back_part,
        back_swapped,
        out_grad,
        gain_ff,
        c_out,
        cross_query,
        cross_key,
        cross_value,
        attended_two,
        logsum_two,
        c_query,
    )
    part_swapped = swapped(part)
    r, c = width // 16, context.shape[1] // 16
    products, token = weight_products(
        token,
        [grad_cross_out, input_two, context],
        [(0, 0), (1, r), (2, 2 * r), (2, 2 * r + c)],
        [attended_two, query_grad, key_grad, value_grad],
    )
    frames_one, token = hold(token, frames_one)
    got_cross = in_plane(products)
    frames_one_other = swapped(frames_one)
    pass_a, own_a, token = level_sum(token, keep_a, got_a, upper)
    last_a = level_swap(pass_a, 2 * PLANE)
    send_b, keep_b, token = share(token, 1, 1)
    got_b = level_swap(send_b, PLANE)
    send_c, keep_c, token = share(token, 2, tiles - 2)
    got_c = level_swap(send_c, PLANE)
    frames_one_other, token = hold(token, frames_one_other, True)
    last_a, token = hold(token, last_a, True)
    pass_b, own_b, token = level_sum(token, keep_b, got_b, upper)
    last_b = level_swap(pass_b, 2 * PLANE)
    frames_one = (frames_one, frames_one_other)
    grad_one, grad_self_out, vectors_cross, grads, part, token = self_backward(
        token,
        info,
        resid_one,
        part,
        part_swapped,
        grad_two,
        gain_cross,
        w_out,
        query,
        key,
        value,
        attended_one,
        logsum_one,
        w_query,
        w_key,
        w_value,
        tables,
    )
    last_b, token = hold(token, last_b, True)
    sum_part, token = hold(token, sum_part, True)
    sum_swapped, part_swapped = swapped(sum_part), swapped(part)
    got_cross, token = hold(token, got_cross)
    grads, token = hold(token, grads)
    got_heads = in_plane(grads)
    pass_c, own_c, token = level_sum(token, keep_c, got_c, upper)
    last_c = level_swap(pass_c, 2 * PLANE)
    send_x, keep_x, token = plane_sum(token, got_cross, parity)
    got_x = level_swap(send_x, PLANE)
    grad_hidden, vectors_attn, result, token = last_backward(
        token, hidden_in, part, part_swapped, grad_one, gain_attn, resid_two, sum_part, sum_swapped
    )
    products, token = out_products(
        token, grad_self_out, attended_one, (vectors_attn, vectors_cross, vectors_ff)
    )
    got_heads, token = hold(token, got_heads, True)
    products, token = hold(token, products, True)
    got_out = in_plane(products)
    send_h, keep_h, token = head_products(token, head_info, got_heads, frames_one)
    got_h = level_swap(send_h, PLANE)
    pass_x, own_x, token = level_sum(token, keep_x[None], got_x[None], upper)
    last_x = level_swap(pass_x, 2 * PLANE)
    last_c, token = hold(token, last_c, True)
    units, token = unit_pack(
        token, [(own_a, last_a), (own_b, last_b), (own_c, last_c)], 3 * width // LEVELS
    )
    pass_h, own_h, token = level_sum(token, keep_h[None], got_h[None], upper, False)
    last_h = level_swap(pass_h, 2 * PLANE)
    got_out, token = hold(token, got_out)
    units, token = hold(token, units, True)
    units = in_plane(units)
    send_o, keep_o, token = plane_sum(token, got_out, parity)
    got_o = level_swap(send_o, PLANE)
    last_x, token = hold(token, last_x, True)
    cross = add_low(own_x, last_x)
    heads, token = head_pack(token, own_h, last_h)
    pass_o, own_o, token = level_sum(token, keep_o[None], got_o[None], upper)
    last_o = level_swap(pass_o, 2 * PLANE)
    units, token = hold(token, units)
    heads, token = hold(token, heads, True)
    heads = in_plane(heads)
    grad_w_down, grad_w_gate, grad_w_up, token = unit_unpack(token, units)
    last_o, token = hold(token, last_o, True)
    outs = add_low(own_o, last_o)
    share_of = r // 2
    vectors = lax.dynamic_slice_in_dim(
        outs, lax.axis_index("tensor") * share_of, share_of, 0
    )[:, w_query.shape[1] : w_query.shape[1] + 6].T
    heads, token = hold(token, heads)
    grad_w_query, grad_w_key, grad_w_value, token = head_unpack(token, heads)
    return (
        result,
        grad_hidden,
        *(vectors[index] for index in range(6)),
        grad_w_query,
        grad_w_key,
        grad_w_value,
        outs[:, : w_query.shape[1]].T,
        cross[r : 2 * r],
        cross[2 * r : 2 * r + c],
        cross[2 * r + c :],
        cross[:r].T,
        grad_w_gate,
        grad_w_up,
        grad_w_down,
    )


def on_any(
    hidden_in,
    out_grad,
    prompt_states,
    row_split,
    prompt_len,
    gain_attn,
    bias_attn,
    gain_cross,
    bias_cross,
    gain_ff,
    bias_ff,
    w_query,
    w_key,
    w_value,
    w_out,
    c_query,
    c_key,
    c_value,
    c_out,
    w_gate,
    w_up,
    w_down,
):
    frame_count = hidden_in.shape[0]
    positions = jnp.arange(frame_count, dtype=jnp.int32)
    split_here = row_split[0]
    row_ids = (positions >= split_here).astype(jnp.int32)
    tables = rotary_tables((positions - row_ids * split_here).astype(jnp.float32), w_query.shape[1])
    key_index = jnp.arange(2 * PROMPT, dtype=jnp.int32)
    key_rows = key_index // PROMPT
    key_live = key_index % PROMPT < jnp.where(key_rows == 0, prompt_len[0], prompt_len[1])
    self_ok = row_ids[:, None] == row_ids[None, :]
    cross_ok = (row_ids[:, None] == key_rows[None, :]) & key_live[None, :]

    normed, scaled_one, inverse_one = normalize(hidden_in, gain_attn, bias_attn)
    input_one = normed.astype(low)
    query_one = rotate(product_plain(input_one, w_query), tables).astype(low)
    key_one = rotate(product_plain(input_one, w_key), tables).astype(low)
    value_one = product_plain(input_one, w_value).astype(low)
    attended_one, logsum_one = attend_forward(query_one, heads_of(key_one), heads_of(value_one), self_ok)
    resid_one = hidden_in + swap_sum(product_plain(attended_one, w_out))

    normed, scaled_two, inverse_two = normalize(resid_one, gain_cross, bias_cross)
    input_two = normed.astype(low)
    cross_query = product_plain(input_two, c_query).astype(low)
    context_flat = prompt_states.reshape(2 * PROMPT, prompt_states.shape[2])
    cross_key = product_plain(context_flat, c_key).astype(low)
    cross_value = product_plain(context_flat, c_value).astype(low)
    attended_two, logsum_two = attend_forward(
        cross_query, heads_of(cross_key), heads_of(cross_value), cross_ok
    )
    resid_two = resid_one + swap_sum(product_plain(attended_two, c_out))

    normed, scaled_three, inverse_three = normalize(resid_two, gain_ff, bias_ff)
    input_three = normed.astype(low)
    gate_pre = product_plain(input_three, w_gate)
    up_pre = product_plain(input_three, w_up)
    sigmoid_gate = jax.nn.sigmoid(gate_pre)
    mixed_low = (gate_pre * sigmoid_gate * up_pre).astype(low)
    result = resid_two + swap_sum(product_plain(mixed_low, w_down))

    grad_ff_out = out_grad.astype(low)
    grad_w_down = generic_sum(grad_ff_out, mixed_low).T
    grad_mixed = product_with_rows(grad_ff_out, w_down)
    grad_gate = (
        grad_mixed * up_pre * sigmoid_gate * (1.0 + gate_pre * (1.0 - sigmoid_gate))
    ).astype(low)
    grad_up = (grad_mixed * gate_pre * sigmoid_gate).astype(low)
    grad_w_gate = generic_sum(input_three, grad_gate)
    grad_w_up = generic_sum(input_three, grad_up)
    normed_grad_three = swap_sum(
        product_with_rows(grad_gate, w_gate) + product_with_rows(grad_up, w_up)
    )
    back_three, grad_gain_ff, grad_bias_ff = normalize_back(
        normed_grad_three, scaled_three, inverse_three, gain_ff
    )
    grad_two = out_grad + back_three
    grad_cross_out = grad_two.astype(low)
    grad_c_out = generic_sum(grad_cross_out, attended_two).T
    grad_attended_two = product_with_rows(grad_cross_out, c_out).astype(low)
    cross_query_grad, cross_key_grad, cross_value_grad = attend_backward(
        cross_query,
        heads_of(cross_key),
        heads_of(cross_value),
        cross_ok,
        grad_attended_two,
        logsum_two,
    )
    cross_query_grad = cross_query_grad.astype(low)
    cross_key_grad = cross_key_grad.astype(low)
    cross_value_grad = cross_value_grad.astype(low)
    grad_c_query = generic_sum(input_two, cross_query_grad)
    grad_c_key = generic_sum(context_flat, cross_key_grad)
    grad_c_value = generic_sum(context_flat, cross_value_grad)
    normed_grad_two = swap_sum(product_with_rows(cross_query_grad, c_query))
    back_two, grad_gain_cross, grad_bias_cross = normalize_back(
        normed_grad_two, scaled_two, inverse_two, gain_cross
    )
    grad_one = grad_two + back_two
    grad_self_out = grad_one.astype(low)
    grad_w_out = generic_sum(grad_self_out, attended_one).T
    grad_attended_one = product_with_rows(grad_self_out, w_out).astype(low)
    query_grad, key_grad, value_grad = attend_backward(
        query_one, heads_of(key_one), heads_of(value_one), self_ok, grad_attended_one, logsum_one
    )
    query_grad = rotate_back(query_grad, tables).astype(low)
    key_grad = rotate_back(key_grad, tables).astype(low)
    value_grad = value_grad.astype(low)
    grad_w_query = generic_sum(input_one, query_grad)
    grad_w_key = generic_sum(input_one, key_grad)
    grad_w_value = generic_sum(input_one, value_grad)
    normed_grad_one = swap_sum(
        product_with_rows(query_grad, w_query)
        + product_with_rows(key_grad, w_key)
        + product_with_rows(value_grad, w_value)
    )
    back_one, grad_gain_attn, grad_bias_attn = normalize_back(
        normed_grad_one, scaled_one, inverse_one, gain_attn
    )
    grad_hidden = grad_one + back_one
    vectors = lax.psum(
        jnp.stack(
            [
                grad_gain_attn,
                grad_bias_attn,
                grad_gain_cross,
                grad_bias_cross,
                grad_gain_ff,
                grad_bias_ff,
            ]
        ),
        "dp",
    )
    vectors = own_share(vectors)
    return (
        result,
        grad_hidden,
        vectors[0],
        vectors[1],
        vectors[2],
        vectors[3],
        vectors[4],
        vectors[5],
        grad_w_query,
        grad_w_key,
        grad_w_value,
        grad_w_out,
        grad_c_query,
        grad_c_key,
        grad_c_value,
        grad_c_out,
        grad_w_gate,
        grad_w_up,
        grad_w_down,
    )


def solution(mesh):
    in_specs = (
        P("dp", None),
        P("dp", None),
        P("dp", None, None),
        P("dp"),
        P("dp"),
        P(),
        P(),
        P(),
        P(),
        P(),
        P(),
        P(None, "tensor"),
        P(None, "tensor"),
        P(None, "tensor"),
        P("tensor", None),
        P(None, "tensor"),
        P(None, "tensor"),
        P(None, "tensor"),
        P("tensor", None),
        P(None, "tensor"),
        P(None, "tensor"),
        P("tensor", None),
    )
    out_specs = (
        P("dp", None),
        P("dp", None),
        P(("dp", "tensor")),
        P(("dp", "tensor")),
        P(("dp", "tensor")),
        P(("dp", "tensor")),
        P(("dp", "tensor")),
        P(("dp", "tensor")),
        P("dp", "tensor"),
        P("dp", "tensor"),
        P("dp", "tensor"),
        P("tensor", "dp"),
        P("dp", "tensor"),
        P("dp", "tensor"),
        P("dp", "tensor"),
        P("tensor", "dp"),
        P("dp", "tensor"),
        P("dp", "tensor"),
        P("tensor", "dp"),
    )
    known = mesh.shape["dp"] == PLANE * LEVELS and mesh.shape["tensor"] == 2
    return jax.shard_map(
        on_plane if known else on_any, mesh=mesh, in_specs=in_specs, out_specs=out_specs, check_vma=False
    )
```

```python
import functools
import math

import jax
import jax.numpy as jnp
from jax import lax
from jax.experimental import pallas as pl
from jax.experimental.pallas import tpu as pltpu
from jax.sharding import PartitionSpec as P

PROMPT = 128
HEAD = 64
PLANE = 4
LEVELS = 4
VMEM_LIMIT = 62 * 2**20
COST = 3
FLOOR = 15 * 10**9

low = jnp.bfloat16
f32 = jnp.float32
sds = jax.ShapeDtypeStruct


norm_eps = 1e-05
score_scale = 0.125
masked_score = -1e30


def product_plain(left_side, right_side):
    return jnp.dot(left_side, right_side, preferred_element_type=jnp.float32)


def product_over_rows(left_side, right_side):
    return lax.dot_general(
        left_side, right_side, (((0,), (0,)), ((), ())), preferred_element_type=jnp.float32
    )


def product_with_rows(left_side, right_side):
    return lax.dot_general(
        left_side, right_side, (((1,), (1,)), ((), ())), preferred_element_type=jnp.float32
    )


def rotary_tables(positions, width):
    dim_index = jnp.arange(width) % HEAD
    freq_index = (dim_index % 16).astype(jnp.float32)
    inverse_freq = jnp.exp(freq_index * (-math.log(10000.0) / 16.0))
    angles = positions[:, None] * inverse_freq[None, :]
    cosine = jnp.cos(angles)
    sine_part = jnp.sin(angles)
    cos_table = jnp.where(dim_index < 32, cosine, 1.0)
    sin_lower = jnp.where(dim_index < 16, -sine_part, 0.0)
    sin_upper = jnp.where((dim_index >= 16) & (dim_index < 32), sine_part, 0.0)
    return (cos_table, sin_lower, sin_upper)


def rotate(values, tables):
    cos_table, sin_lower, sin_upper = tables
    return (
        values * cos_table
        + jnp.roll(values, -16, axis=1) * sin_lower
        + jnp.roll(values, 16, axis=1) * sin_upper
    )


def rotate_back(incoming, tables):
    cos_table, sin_lower, sin_upper = tables
    return (
        incoming * cos_table
        + jnp.roll(incoming * sin_lower, 16, axis=1)
        + jnp.roll(incoming * sin_upper, -16, axis=1)
    )


def normalize(values, norm_gain, norm_shift):
    average = jnp.mean(values, axis=-1, keepdims=True)
    centered = values - average
    variance = jnp.mean(centered * centered, axis=-1, keepdims=True)
    inverse = lax.rsqrt(variance + norm_eps)
    scaled = centered * inverse
    return (scaled * norm_gain + norm_shift, scaled, inverse)


def normalize_back(incoming, scaled, inverse, norm_gain):
    grad_gain = jnp.sum(incoming * scaled, axis=0)
    grad_shift = jnp.sum(incoming, axis=0)
    weighted = incoming * norm_gain
    grad_input = inverse * (
        weighted
        - jnp.mean(weighted, axis=-1, keepdims=True)
        - scaled * jnp.mean(weighted * scaled, axis=-1, keepdims=True)
    )
    return (grad_input, grad_gain, grad_shift)


def heads_of(values):
    return values.reshape(values.shape[0], values.shape[1] // HEAD, HEAD)


def attend_forward(query_block, key_heads, value_heads, allowed):
    query_heads = heads_of(query_block)
    scores = (
        jnp.einsum("qhd,khd->hqk", query_heads, key_heads, preferred_element_type=jnp.float32)
        * score_scale
    )
    scores = jnp.where(allowed[None], scores, masked_score)
    largest = jnp.max(scores, axis=-1, keepdims=True)
    exp_scores = jnp.exp(scores - largest)
    totals = jnp.sum(exp_scores, axis=-1, keepdims=True)
    soft_weights = (exp_scores / totals).astype(jnp.bfloat16)
    mixed_heads = jnp.einsum(
        "hqk,khd->qhd", soft_weights, value_heads, preferred_element_type=jnp.float32
    )
    mixed_flat = mixed_heads.reshape(query_block.shape[0], query_block.shape[1]).astype(
        jnp.bfloat16
    )
    return (mixed_flat, largest[..., 0] + jnp.log(totals[..., 0]))


def attend_backward(query_block, key_heads, value_heads, allowed, grad_block, logsum_block):
    query_heads = heads_of(query_block)
    grad_heads = heads_of(grad_block)
    scores = (
        jnp.einsum("qhd,khd->hqk", query_heads, key_heads, preferred_element_type=jnp.float32)
        * score_scale
    )
    scores = jnp.where(allowed[None], scores, masked_score)
    soft_weights = jnp.exp(scores - logsum_block[..., None])
    grad_weights = jnp.einsum(
        "qhd,khd->hqk", grad_heads, value_heads, preferred_element_type=jnp.float32
    )
    inner_sum = jnp.sum(soft_weights * grad_weights, axis=-1, keepdims=True)
    grad_scores = (soft_weights * (grad_weights - inner_sum)).astype(jnp.bfloat16)
    grad_query = (
        jnp.einsum("hqk,khd->qhd", grad_scores, key_heads, preferred_element_type=jnp.float32)
        * score_scale
    )
    grad_key = (
        jnp.einsum("hqk,qhd->khd", grad_scores, query_heads, preferred_element_type=jnp.float32)
        * score_scale
    )
    grad_value = jnp.einsum(
        "hqk,qhd->khd",
        soft_weights.astype(jnp.bfloat16),
        grad_heads,
        preferred_element_type=jnp.float32,
    )
    return (
        grad_query.reshape(query_block.shape),
        grad_key.reshape(grad_key.shape[0], -1),
        grad_value.reshape(grad_value.shape[0], -1),
    )


def swap_sum(partial):
    low = partial.astype(jnp.bfloat16)
    if lax.axis_size("tensor") == 2:
        other = lax.ppermute(low, "tensor", [(0, 1), (1, 0)])
        return low.astype(jnp.float32) + other.astype(jnp.float32)
    return lax.psum(low, "tensor").astype(jnp.float32)


def pairs(mask):
    return [(i, i ^ mask) for i in range(16)]


def own_share(vectors):
    share = vectors.shape[1] // (lax.axis_size("dp") * lax.axis_size("tensor"))
    index = lax.axis_index("dp") * lax.axis_size("tensor") + lax.axis_index("tensor")
    return lax.dynamic_slice_in_dim(vectors, index * share, share, 1)


def generic_sum(rows_side, column_side):
    return lax.psum_scatter(
        product_over_rows(rows_side, column_side).astype(jnp.bfloat16),
        "dp",
        scatter_dimension=0,
        tiled=True,
    ).astype(jnp.float32)


def add_low(*terms):
    total = terms[0].astype(jnp.float32)
    for term in terms[1:]:
        total = total + term.astype(jnp.float32)
    return total


def ff_parts(gate, up, grad_mixed):
    sig = 0.5 * jnp.tanh(0.5 * gate) + 0.5
    act = gate * sig
    return (
        (act * up).astype(low),
        (grad_mixed * up * sig * (1.0 + gate * (1.0 - sig))).astype(low),
        (grad_mixed * act).astype(low),
    )


def turn(values, cos, lower, upper):
    width = values.shape[1]
    return (values * cos + pltpu.roll(values, width - 16, 1) * lower + pltpu.roll(values, 16, 1) * upper)

def turn_back(values, cos, lower, upper):
    width = values.shape[1]
    return (values * cos + pltpu.roll(values * lower, 16, 1) + pltpu.roll(values * upper, width - 16, 1))

def normed_rows(values, gain, shift):
    average = jnp.mean(values, axis=-1, keepdims=True)
    centered = values - average
    variance = jnp.mean(centered * centered, axis=-1, keepdims=True)
    return centered * lax.rsqrt(variance + norm_eps) * gain + shift

def over_rows(rows, body, chunk=32):
    @pl.loop(0, rows // chunk, unroll=min(4, rows // chunk))
    def _(i):
        body(pl.ds(pl.multiple_of(i * chunk, chunk), chunk))

def attend(q, k, v, mask, lse_ref):
    q_turned = (q * jnp.bfloat16(0.125)).T
    v_turned = v.T
    heads = [slice(h * HEAD, (h + 1) * HEAD) for h in range(q.shape[1] // HEAD)]
    scores = [product_plain(k[:, c], q_turned[c, :]) for c in heads]
    weights, scales = [], []
    for h, s in enumerate(scores):
        s = s + mask
        m = jnp.max(s, axis=0, keepdims=True)
        e = jnp.exp(s - m)
        total = jnp.sum(e, axis=0, keepdims=True)
        weights.append(e.astype(low))
        scales.append(1.0 / total)
        lse_ref[h : h + 1, :] = m + jnp.log(total)
    outs = [product_plain(v_turned[c, :], e) * x for c, e, x in zip(heads, weights, scales)]
    return jnp.concatenate(outs, axis=0).T.astype(low)


def attend_back(q, k, v, g, att, mask, lse):
    scaled = q * jnp.bfloat16(0.125)
    q_turned = scaled.T
    g_turned = g.T
    k_turned = k.T
    weighted = g_turned.astype(f32) * att.T.astype(f32)
    dq, dk, dv = [], [], []
    for h in range(q.shape[1] // HEAD):
        c = slice(h * HEAD, (h + 1) * HEAD)
        p = jnp.exp(product_plain(k[:, c], q_turned[c, :]) + (mask - lse[h : h + 1, :]))
        dp = product_plain(v[:, c], g_turned[c, :])
        inner = jnp.sum(weighted[c, :], axis=0, keepdims=True)
        ds = (p * (dp - inner)).astype(low)
        dq.append(product_plain(k_turned[c, :], ds))
        dk.append(product_plain(ds, scaled[:, c]))
        dv.append(product_plain(p.astype(low), g[:, c]))
    return (
        jnp.concatenate(dq, axis=0).T * 0.125,
        jnp.concatenate(dk, axis=1),
        jnp.concatenate(dv, axis=1),
    )


def self_mask(split, T):
    r=lax.broadcasted_iota(jnp.int32,(T,T),0)>=split
    c=lax.broadcasted_iota(jnp.int32,(T,T),1)>=split
    return jnp.where(r==c,0.0,masked_score).astype(f32)

def key_half(info, index, frames, keys):
    second = info[0] < frames
    start = jnp.where(second, keys // 2, 0) if index == 1 else 0
    live = jnp.where(second, info[2], info[1]) if index == 1 else info[1]
    return start, live


def half_mask(live, keys, frames):
    return jnp.where(
        lax.broadcasted_iota(jnp.int32, (keys, frames), 0) < live, 0.0, masked_score
    ).astype(f32)


def key_blocks(info, k_ref, v_ref, frames):
    keys = k_ref.shape[0]
    k, v, masks = [], [], []
    for index in range(2):
        start, live = key_half(info, index, frames, keys)
        here = pl.ds(start if index == 0 else pl.multiple_of(start, keys // 2), keys // 2)
        k.append(k_ref[here, :])
        v.append(v_ref[here, :])
        masks.append(half_mask(live, keys // 2, frames // 2))
    return k, v, jnp.concatenate(masks, axis=1)


def cross_attend(info, q, k_ref, v_ref, lse_ref):
    half = q.shape[0] // 2
    q_turned = (q * jnp.bfloat16(0.125)).T
    k, v, mask = key_blocks(info, k_ref, v_ref, 2 * half)
    v_turned = [values.T for values in v]
    outs = []
    for h in range(q.shape[1] // HEAD):
        c = slice(h * HEAD, (h + 1) * HEAD)
        s = [product_plain(k[i][:, c], q_turned[c, i * half : (i + 1) * half]) for i in range(2)]
        s = jnp.concatenate(s, axis=1) + mask
        m = jnp.max(s, axis=0, keepdims=True)
        e = jnp.exp(s - m)
        total = jnp.sum(e, axis=0, keepdims=True)
        lse_ref[h : h + 1, :] = m + jnp.log(total)
        e = e.astype(low)
        o = [product_plain(v_turned[i][c, :], e[:, i * half : (i + 1) * half]) for i in range(2)]
        outs.append(jnp.concatenate(o, axis=1) * (1.0 / total))
    return jnp.concatenate(outs, axis=0).T.astype(low)


def cross_attend_back(info, q, k_ref, v_ref, g, att, lse):
    half = q.shape[0] // 2
    scaled = q * jnp.bfloat16(0.125)
    q_turned = scaled.T
    g_turned = g.T
    weighted = g_turned.astype(f32) * att.T.astype(f32)
    k, v, mask = key_blocks(info, k_ref, v_ref, 2 * half)
    k_turned = [values.T for values in k]
    parts = [slice(0, half), slice(half, 2 * half)]
    dq, dk, dv = [], [[], []], [[], []]
    for h in range(q.shape[1] // HEAD):
        c = slice(h * HEAD, (h + 1) * HEAD)
        s = [product_plain(k[i][:, c], q_turned[c, parts[i]]) for i in range(2)]
        dp = [product_plain(v[i][:, c], g_turned[c, parts[i]]) for i in range(2)]
        p = jnp.exp(jnp.concatenate(s, axis=1) + (mask - lse[h : h + 1, :]))
        inner = jnp.sum(weighted[c, :], axis=0, keepdims=True)
        ds = (p * (jnp.concatenate(dp, axis=1) - inner)).astype(low)
        p = p.astype(low)
        dq.append(
            jnp.concatenate(
                [product_plain(k_turned[i][c, :], ds[:, parts[i]]) for i in range(2)], axis=1
            )
        )
        for i in range(2):
            dk[i].append(product_plain(ds[:, parts[i]], scaled[parts[i], c]))
            dv[i].append(product_plain(p[:, parts[i]], g[parts[i], c]))
    second = (info[0] < 2 * half).astype(f32)

    def by_row(halves):
        first, last = (jnp.concatenate(half, axis=1) for half in halves)
        return jnp.concatenate([first + last * (1.0 - second), last * second], axis=0)

    return jnp.concatenate(dq, axis=0).T * 0.125, by_row(dk), by_row(dv)


def norm_back_rows(x,e,gain,above,gain_acc,shift_acc):
    average=jnp.mean(x,axis=-1,keepdims=True)
    centered=x-average
    variance=jnp.mean(centered*centered,axis=-1,keepdims=True)
    inverse=lax.rsqrt(variance+norm_eps)
    n=centered*inverse
    en=e*n
    w=e*gain
    mean_w=jnp.mean(w,axis=-1,keepdims=True)
    mean_wn=jnp.mean(en*gain,axis=-1,keepdims=True)
    fold=lambda t: jnp.sum(t.reshape(t.shape[0]//8,8,t.shape[1]),axis=0)
    gain_acc[...]+=fold(en)
    shift_acc[...]+=fold(e)
    return above+inverse*(w-mean_w-n*mean_wn)

def norm_back_step(x, mine, other, above, gain, total, total_low, kept, vectors, gain_acc, shift_acc):
    step, block = pl.program_id(0), x.shape[0]

    @pl.when(step == 0)
    def _():
        gain_acc[...] = jnp.zeros_like(gain_acc)
        shift_acc[...] = jnp.zeros_like(shift_acc)

    @pl.when(step < BLOCKS)
    def _():
        def rows(r):
            e = mine[r, :].astype(f32) + other[r, :].astype(f32)
            t = norm_back_rows(x[r, :], e, gain[...][None], above[r, :], gain_acc, shift_acc)
            total[r, :] = t
            total_low[r, :] = t.astype(low)
            kept[within(step, block, r), :] = t.astype(low)

        over_rows(block, rows)

    @pl.when(step == BLOCKS - 1)
    def _():
        vectors[0:1, :] = jnp.sum(gain_acc[...], axis=0, keepdims=True)
        vectors[1:2, :] = jnp.sum(shift_acc[...], axis=0, keepdims=True)


def ordered(kernel, token, args, in_specs, out_specs, out_shape, grid, flops, scratch=(), info=None, brief=False):
    if info is None:
        info = jnp.zeros((1,), jnp.int32)
    inputs, outputs = len(args), len(out_shape)

    def body(info_ref, *refs):
        token_ref = refs[inputs + 1 + outputs]

        @pl.when(functools.reduce(jnp.logical_and, [pl.program_id(i) == 0 for i in range(len(grid))]))
        def _():
            token_ref[...] = jnp.zeros_like(token_ref)

        kernel(
            info_ref,
            *refs[:inputs],
            *refs[inputs + 1 : inputs + 1 + outputs],
            *refs[inputs + 2 + outputs :],
        )

    moved = sum(math.prod(a.shape) * a.dtype.itemsize for a in (*args, *out_shape))
    *results, token = pl.pallas_call(
        body,
        grid_spec=pltpu.PrefetchScalarGridSpec(
            num_scalar_prefetch=1,
            grid=grid,
            in_specs=[*in_specs, pl.BlockSpec(memory_space=pl.ANY)],
            out_specs=[*out_specs, pl.BlockSpec((8, 128), lambda *_: (0, 0))],
            scratch_shapes=list(scratch),
        ),
        out_shape=[*out_shape, sds((8, 128), f32)],
        compiler_params=pltpu.CompilerParams(vmem_limit_bytes=VMEM_LIMIT),
        cost_estimate=pl.CostEstimate(flops=0 if brief else max(FLOOR, int(flops * COST)), bytes_accessed=0 if brief else int(moved * COST), transcendentals=0),
    )(info, *args, token)
    return (*results, token)


def hold(token, values, brief=False):
    def nothing(values_ref, token_ref, out_ref, token_out):
        token_out[...] = jnp.zeros_like(token_out)

    return pl.pallas_call(
        nothing,
        in_specs=[pl.BlockSpec(memory_space=pl.ANY)] * 2,
        out_specs=[pl.BlockSpec(memory_space=pl.ANY), pl.BlockSpec(memory_space=pltpu.VMEM)],
        out_shape=[sds(values.shape, values.dtype), sds((8, 128), f32)],
        input_output_aliases={0: 0},
        compiler_params=pltpu.CompilerParams(vmem_limit_bytes=VMEM_LIMIT),
        cost_estimate=pl.CostEstimate(flops=0 if brief else FLOOR, bytes_accessed=0, transcendentals=0),
    )(values, token)


def specs(frames, width, tile, blocks=0):
    def tile_of(j):
        return jnp.maximum(j - blocks, 0) if blocks else j

    whole = pl.BlockSpec((frames, width), lambda j, *_: (0, 0))
    vector = pl.BlockSpec((width,), lambda j, *_: (0,))
    column = pl.BlockSpec((width, tile), lambda j, *_: (0, tile_of(j)))
    row = pl.BlockSpec((tile, width), lambda j, *_: (tile_of(j), 0))
    act = pl.BlockSpec((frames, tile), lambda j, *_: (0, tile_of(j)))
    table = pl.BlockSpec((frames, 2 * HEAD), lambda j, *_: (0, 0))
    logsum = pl.BlockSpec((8, frames), lambda j, *_: (tile_of(j), 0))
    return whole, vector, column, row, act, table, logsum


BLOCKS = 4


def widened(*tables):
    return tuple(jnp.concatenate([table[...], table[...]], axis=1) for table in tables)


def row_block(frames, width):
    return pl.BlockSpec((frames // BLOCKS, width), lambda j, *_: (jnp.minimum(j, BLOCKS - 1), 0))


def copies_block(frames, width, place):
    return pl.BlockSpec(
        (PLANE, frames // BLOCKS, width),
        lambda j, info: (0, jnp.clip(j - BLOCKS // 2 * info[place], 0, BLOCKS // 2 - 1), 0),
    )


def within(step, rows, r):
    return pl.ds(pl.multiple_of(step * rows + r.start, r.size), r.size)


def added(acc, term, result, first=0):
    step = pl.program_id(0)

    @pl.when(step == first)
    def _():
        acc[...] = term

    @pl.when(step != first)
    def _():
        acc[...] += term

    @pl.when(step == pl.num_programs(0) - 1)
    def _():
        result[...] = acc[...].astype(result.dtype)


def self_kernel(info, hid, gain, shift, wq, wk, wv, wo, cos, lower, upper, grad, copies, grad_copies, q, k, v, att, logsum, part, acc, mask, normed):
    step, frames, block = pl.program_id(0), normed.shape[0], hid.shape[0]

    @pl.when(step == 0)
    def _():
        mask[...] = self_mask(info[0], frames)

    @pl.when(step < BLOCKS)
    def _():
        def rows(r):
            normed[within(step, block, r), :] = normed_rows(hid[r, :], gain[...][None], shift[...][None]).astype(low)

        over_rows(block, rows)

    @pl.when((step < BLOCKS) & (step * 2 // BLOCKS == info[3]))
    def _():
        mine = normed[pl.ds(pl.multiple_of(step * block, block), block), :]
        for chip in range(PLANE):
            copies[chip] = mine

    @pl.when(step < BLOCKS // 2)
    def _():
        grad_low = grad[...].astype(low)
        for chip in range(PLANE):
            grad_copies[chip] = grad_low

    @pl.when(step >= BLOCKS)
    def _():
        n = normed[...]
        tables = widened(cos, lower, upper)
        q[...] = turn(product_plain(n, wq[...]), *tables).astype(low)
        k[...] = turn(product_plain(n, wk[...]), *tables).astype(low)
        v[...] = product_plain(n, wv[...]).astype(low)
        attended = attend(q[...], k[...], v[...], mask[...], logsum)
        att[...] = attended
        added(acc, product_plain(attended, wo[...]), part, BLOCKS)


def self_forward(token, info, hid, gain, shift, wq, wk, wv, wo, tables, grad, tile=4 * HEAD):
    frames, width = hid.shape
    columns = wq.shape[1]
    whole, vector, column, row, act, table, logsum = specs(frames, width, tile, BLOCKS)
    blocks = row_block(frames, width)
    here = frames // BLOCKS
    return ordered(
        self_kernel,
        token,
        (hid, gain, shift, wq, wk, wv, wo, *tables, grad),
        [blocks, vector, vector, column, column, column, row, table, table, table]
        + [
            pl.BlockSpec(
                (here, width),
                lambda j, info: (BLOCKS // 2 * info[3] + jnp.minimum(j, BLOCKS // 2 - 1), 0),
            )
        ],
        [
            copies_block(frames, width, 3),
            pl.BlockSpec((PLANE, here, width), lambda j, info: (0, jnp.minimum(j, BLOCKS // 2 - 1), 0)),
        ]
        + [act, act, act, act, logsum, whole],
        [sds((PLANE, frames // 2, width), low)] * 2
        + [sds((frames, columns), low)] * 4
        + [sds((columns // tile * 8, frames), f32), sds((frames, width), low)],
        (BLOCKS + columns // tile,),
        2 * frames * columns * (4 * width + 8 * frames),
        [
            pltpu.VMEM((frames, width), f32),
            pltpu.VMEM((frames, frames), f32),
            pltpu.VMEM((frames, width), low),
        ],
        info,
    )


def cross_kernel(info, hid, mine, other, gain, shift, cq, ck, cv, co, total, normed, q, att, logsum, part, acc, kept):
    step, block = pl.program_id(0), hid.shape[0]

    @pl.when(step < BLOCKS)
    def _():
        def rows(r):
            x = hid[r, :] + (mine[r, :].astype(f32) + other[r, :].astype(f32))
            total[r, :] = x
            n = normed_rows(x, gain[...][None], shift[...][None]).astype(low)
            normed[r, :] = n
            kept[within(step, block, r), :] = n

        over_rows(block, rows)

    @pl.when(step >= BLOCKS)
    def _():
        q[...] = product_plain(kept[...], cq[...]).astype(low)
        attended = cross_attend(info, q[...], ck, cv, logsum)
        att[...] = attended
        added(acc, product_plain(attended, co[...]), part, BLOCKS)


def cross_forward(token, info, hid, mine, other, gain, shift, cq, ck, cv, co, tile=4 * HEAD):
    frames, width = hid.shape
    columns, keys = cq.shape[1], ck.shape[0]
    whole, vector, column, row, act, table, logsum = specs(frames, width, tile, BLOCKS)
    key = pl.BlockSpec((keys, tile), lambda j, *_: (0, jnp.maximum(j - BLOCKS, 0)))
    blocks = row_block(frames, width)
    return ordered(
        cross_kernel,
        token,
        (hid, mine, other, gain, shift, cq, ck, cv, co),
        [blocks, blocks, blocks, vector, vector, column, key, key, row],
        [blocks, blocks, act, act, logsum, whole],
        [
            sds((frames, width), f32),
            sds((frames, width), low),
            sds((frames, columns), low),
            sds((frames, columns), low),
            sds((columns // tile * 8, frames), f32),
            sds((frames, width), low),
        ],
        (BLOCKS + columns // tile,),
        2 * frames * columns * (2 * width + 8 * keys),
        [pltpu.VMEM((frames, width), f32), pltpu.VMEM((frames, width), low)],
        info,
        brief=True,
    )


def norm_kernel(info, hid, mine, other, gain, shift, total, normed, copies):
    def rows(r):
        x = hid[r, :] + (mine[r, :].astype(f32) + other[r, :].astype(f32))
        total[r, :] = x
        normed[r, :] = normed_rows(x, gain[...][None], shift[...][None]).astype(low)

    over_rows(hid.shape[0], rows)

    @pl.when(pl.program_id(0) * 2 // pl.num_programs(0) == info[0])
    def _():
        values = normed[...]
        for chip in range(PLANE):
            copies[chip] = values


def norm_forward(token, info, hid, mine, other, gain, shift, block=128):
    frames, width = hid.shape
    blocks = frames // (2 * block)
    rows = pl.BlockSpec((block, width), lambda j, *_: (j, 0))
    vector = pl.BlockSpec((width,), lambda j, *_: (0,))
    return ordered(
        norm_kernel,
        token,
        (hid, mine, other, gain, shift),
        [rows, rows, rows, vector, vector],
        [
            rows,
            rows,
            pl.BlockSpec(
                (PLANE, block, width),
                lambda j, info: (0, jnp.clip(j - blocks * info[0], 0, blocks - 1), 0),
            ),
        ],
        [sds((frames, width), f32), sds((frames, width), low), sds((PLANE, frames // 2, width), low)],
        (frames // block,),
        10 * frames * width,
        info=info,
        brief=True,
    )


def cross_back_kernel(info, x, mine, other, above, gain, co, q, ck, cv, att, logsum, cq, total, total_low, vectors, dq, dk, dv, part, acc, gain_acc, shift_acc, kept):
    norm_back_step(x, mine, other, above, gain, total, total_low, kept, vectors, gain_acc, shift_acc)

    @pl.when(pl.program_id(0) >= BLOCKS)
    def _():
        g = product_with_rows(kept[...], co[...]).astype(low)
        a, b, c = cross_attend_back(info, q[...], ck, cv, g, att[...], logsum[...])
        a = a.astype(low)
        dq[...] = a
        dk[...] = b.astype(low)
        dv[...] = c.astype(low)
        added(acc, product_with_rows(a, cq[...]), part, BLOCKS)


def cross_backward(token, info, x, mine, other, above, gain, co, q, ck, cv, att, logsums, cq, tile=4 * HEAD):
    frames, width = x.shape
    columns, keys = cq.shape[1], ck.shape[0]
    whole, vector, column, row, act, table, logsum = specs(frames, width, tile, BLOCKS)
    key = pl.BlockSpec((keys, tile), lambda j, *_: (0, jnp.maximum(j - BLOCKS, 0)))
    blocks = row_block(frames, width)
    two = pl.BlockSpec((2, width), lambda j, *_: (0, 0))
    return ordered(
        cross_back_kernel,
        token,
        (x, mine, other, above, gain, co, q, ck, cv, att, logsums, cq),
        [blocks, blocks, blocks, blocks, vector, row, act, key, key, act, logsum, column],
        [blocks, blocks, two, act, key, key, whole],
        [
            sds((frames, width), f32),
            sds((frames, width), low),
            sds((2, width), f32),
            sds((frames, columns), low),
            sds((keys, columns), low),
            sds((keys, columns), low),
            sds((frames, width), low),
        ],
        (BLOCKS + columns // tile,),
        2 * frames * columns * (2 * width + 20 * keys),
        [
            pltpu.VMEM((frames, width), f32),
            pltpu.VMEM((8, width), f32),
            pltpu.VMEM((8, width), f32),
            pltpu.VMEM((frames, width), low),
        ],
        info,
    )


def self_back_kernel(info, x, mine, other, above, gain, wo, q, k, v, att, logsum, wq, wk, wv, cos, lower, upper, total, total_low, vectors, grads, part, acc, mask, gain_acc, shift_acc, kept):
    step = pl.program_id(0)

    @pl.when(step == 0)
    def _():
        mask[...] = self_mask(info[0], kept.shape[0])

    norm_back_step(x, mine, other, above, gain, total, total_low, kept, vectors, gain_acc, shift_acc)

    @pl.when(step >= BLOCKS)
    def _():
        g = product_with_rows(kept[...], wo[...]).astype(low)
        a, b, c = attend_back(q[...], k[...], v[...], g, att[...], mask[...], logsum[...])
        tables = widened(cos, lower, upper)
        a = turn_back(a, *tables).astype(low)
        b = turn_back(b, *tables).astype(low)
        c = c.astype(low)
        for index, values in enumerate((a, b, c)):
            turned = values.T
            for quarter in range(PLANE):
                grads[quarter, index] = turned[quarter * HEAD : (quarter + 1) * HEAD]
        back = product_with_rows(a, wq[...]) + product_with_rows(b, wk[...])
        added(acc, back + product_with_rows(c, wv[...]), part, BLOCKS)


def self_backward(token, info, x, mine, other, above, gain, wo, q, k, v, att, logsums, wq, wk, wv, tables, tile=4 * HEAD):
    frames, width = x.shape
    columns = wq.shape[1]
    whole, vector, column, row, act, table, logsum = specs(frames, width, tile, BLOCKS)
    blocks = row_block(frames, width)
    two = pl.BlockSpec((2, width), lambda j, *_: (0, 0))
    heads = pl.BlockSpec(
        (PLANE, 3, HEAD, frames), lambda j, *_: (0, 0, jnp.maximum(j - BLOCKS, 0), 0)
    )
    return ordered(
        self_back_kernel,
        token,
        (x, mine, other, above, gain, wo, q, k, v, att, logsums, wq, wk, wv, *tables),
        [blocks] * 4
        + [vector, row, act, act, act, act, logsum, column, column, column, table, table, table],
        [blocks, blocks, two, heads, whole],
        [
            sds((frames, width), f32),
            sds((frames, width), low),
            sds((2, width), f32),
            sds((PLANE, 3, columns // PLANE, frames), low),
            sds((frames, width), low),
        ],
        (BLOCKS + columns // tile,),
        2 * frames * columns * (4 * width + 20 * frames),
        [
            pltpu.VMEM((frames, width), f32),
            pltpu.VMEM((frames, frames), f32),
            pltpu.VMEM((8, width), f32),
            pltpu.VMEM((8, width), f32),
            pltpu.VMEM((frames, width), low),
        ],
        info,
    )


def last_kernel(_, x, mine, other, above, gain, resid, sum_mine, sum_other, total, vectors, result, gain_acc, shift_acc):
    step = pl.program_id(0)

    @pl.when(step == 0)
    def _():
        gain_acc[...] = jnp.zeros_like(gain_acc)
        shift_acc[...] = jnp.zeros_like(shift_acc)

    def rows(r):
        e = mine[r, :].astype(f32) + other[r, :].astype(f32)
        total[r, :] = norm_back_rows(x[r, :], e, gain[...][None], above[r, :], gain_acc, shift_acc)
        result[r, :] = resid[r, :] + (sum_mine[r, :].astype(f32) + sum_other[r, :].astype(f32))

    over_rows(x.shape[0], rows)

    @pl.when(step == pl.num_programs(0) - 1)
    def _():
        vectors[0:1, :] = jnp.sum(gain_acc[...], axis=0, keepdims=True)
        vectors[1:2, :] = jnp.sum(shift_acc[...], axis=0, keepdims=True)


def last_backward(token, x, mine, other, above, gain, resid, sum_mine, sum_other, block=128):
    frames, width = x.shape
    rows = pl.BlockSpec((block, width), lambda j, *_: (j, 0))
    vector = pl.BlockSpec((width,), lambda j, *_: (0,))
    two = pl.BlockSpec((2, width), lambda j, *_: (0, 0))
    return ordered(
        last_kernel,
        token,
        (x, mine, other, above, gain, resid, sum_mine, sum_other),
        [rows, rows, rows, rows, vector, rows, rows, rows],
        [rows, two, rows],
        [sds((frames, width), f32), sds((2, width), f32), sds((frames, width), f32)],
        (frames // block,),
        20 * frames * width,
        [pltpu.VMEM((8, width), f32), pltpu.VMEM((8, width), f32)],
        brief=True,
    )


def ff_kernel(_, in_ref, out_ref, gate_ref, up_ref, down_ref, sum_ref, back_ref, sum_acc, back_acc, out_low):
    @pl.when(pl.program_id(0) == 0)
    def _():
        out_low[...] = out_ref[...].astype(low)

    normed = in_ref[...]
    mixed, grad_gate, grad_up = ff_parts(
        product_plain(normed, gate_ref[...]),
        product_plain(normed, up_ref[...]),
        product_with_rows(out_low[...], down_ref[...]),
    )
    added(sum_acc, product_plain(mixed, down_ref[...]), sum_ref)
    added(
        back_acc,
        product_with_rows(grad_gate, gate_ref[...]) + product_with_rows(grad_up, up_ref[...]),
        back_ref,
    )


def ff_both(token, normed, grad_out, w_gate, w_up, w_down, tile=768):
    frames, width = normed.shape
    units = w_gate.shape[1]
    whole, _, column, row, *_ = specs(frames, width, tile)
    return ordered(
        ff_kernel,
        token,
        (normed, grad_out, w_gate, w_up, w_down),
        [whole, whole, column, column, row],
        [whole, whole],
        [sds((frames, width), low)] * 2,
        (units // tile,),
        12 * frames * width * units,
        [pltpu.VMEM((frames, width), f32)] * 2 + [pltpu.VMEM((frames, width), low)],
    )


def share_kernel(info, in_mine, in_other, out_mine, out_other, gate_ref, up_ref, down_ref, send_ref, keep_ref, acc):
    step = pl.program_id(1)
    normed = jnp.concatenate([in_mine[...], in_other[...]], axis=0)
    grad_out = jnp.concatenate([out_mine[...], out_other[...]], axis=0)
    mixed, grad_gate, grad_up = ff_parts(
        product_plain(normed, gate_ref[...]),
        product_plain(normed, up_ref[...]),
        product_with_rows(grad_out, down_ref[...]),
    )
    fresh = (
        product_over_rows(grad_out, mixed),
        product_over_rows(normed, grad_gate),
        product_over_rows(normed, grad_up),
    )
    for index, term in enumerate(fresh):

        @pl.when(step == 0)
        def _():
            acc[index] = term

        @pl.when(step != 0)
        def _():
            acc[index] += term

    @pl.when(step == pl.num_programs(1) - 1)
    def _():
        rows = send_ref.shape[2] // 3
        for pair in range(2):
            for index in range(3):
                for ref, parity in ((send_ref, 1 - info[1]), (keep_ref, info[1])):
                    start = pl.multiple_of((2 * pair + parity) * rows, rows)
                    ref[0, pair, index * rows : (index + 1) * rows] = acc[
                        index, pl.ds(start, rows), :
                    ].astype(ref.dtype)


def ff_share(token, info, normed, grad_out, w_gate, w_up, w_down, tile, first, count):
    frames, width = normed[0].shape
    chunk = frames // PLANE
    rows = pl.BlockSpec((chunk, width), lambda i, j, info: (j, 0))
    column = pl.BlockSpec((width, tile), lambda i, j, info: (0, info[0] + first + i))
    half = (LEVELS // 2, 3 * width // LEVELS, tile)
    return ordered(
        share_kernel,
        token,
        (*normed, *grad_out, w_gate, w_up, w_down),
        [rows] * 4
        + [column, column, pl.BlockSpec((tile, width), lambda i, j, info: (info[0] + first + i, 0))],
        [pl.BlockSpec((1, *half), lambda i, j, info: (i, 0, 0, 0))] * 2,
        [sds((count, *half), low)] * 2,
        (count, PLANE),
        24 * frames * width * tile * count,
        [pltpu.VMEM((3, width, tile), f32)],
        info,
    )


def weight_kernel(plan, sides_count, _, *refs):
    sides, columns = refs[:sides_count], refs[sides_count : sides_count + len(plan)]
    out = refs[sides_count + len(plan)]
    turned = refs[sides_count + len(plan) + 1 :]

    @pl.when(pl.program_id(0) == 0)
    def _():
        for side, ref in zip(sides, turned):
            ref[...] = side[...].T

    for (which, first), column in zip(plan, columns):
        product = product_plain(turned[which][...], column[...]).astype(low)
        rows = product.shape[0] // (PLANE * LEVELS)
        product = product.reshape(LEVELS, PLANE, rows, product.shape[1])
        for owner in range(PLANE):
            out[owner, :, first : first + rows, :] = product[:, owner]


def weight_products(token, sides, plan, columns, tile=256):
    width = columns[0].shape[1]
    rows = sum(sides[which].shape[1] for which, _ in plan) // (PLANE * LEVELS)
    return ordered(
        functools.partial(weight_kernel, plan, len(sides)),
        token,
        (*sides, *columns),
        [pl.BlockSpec(side.shape, lambda j, *_: (0, 0)) for side in sides]
        + [pl.BlockSpec((column.shape[0], tile), lambda j, *_: (0, j)) for column in columns],
        [pl.BlockSpec((PLANE, LEVELS, rows, tile), lambda j, *_: (0, 0, 0, j))],
        [sds((PLANE, LEVELS, rows, width), low)],
        (width // tile,),
        sum(2 * sides[w].shape[0] * sides[w].shape[1] * width for w, _ in plan),
        [pltpu.VMEM((side.shape[1], side.shape[0]), low) for side in sides],
        brief=len(sides) == 1,
    )


def out_kernel(_, side, column, first, second, third, out, turned):
    step = pl.program_id(0)

    @pl.when(step == 0)
    def _():
        turned[...] = side[...].T

    def store(values):
        values = values.astype(low).reshape(LEVELS, PLANE, out.shape[2], out.shape[3])
        for owner in range(PLANE):
            out[owner] = values[:, owner]

    @pl.when(step < pl.num_programs(0) - 1)
    def _():
        store(product_plain(turned[...], column[...]))

    @pl.when(step == pl.num_programs(0) - 1)
    def _():
        empty = jnp.zeros((out.shape[3] - 6, side.shape[1]), f32)
        store(jnp.concatenate([first[...], second[...], third[...], empty], axis=0).T)


def out_products(token, side, column, vectors, tile=128):
    frames, width = side.shape
    columns = column.shape[1]
    tiles = columns // tile
    rows = width // (PLANE * LEVELS)
    return ordered(
        out_kernel,
        token,
        (side, column, *vectors),
        [
            pl.BlockSpec((frames, width), lambda j, *_: (0, 0)),
            pl.BlockSpec((frames, tile), lambda j, *_: (0, jnp.minimum(j, tiles - 1))),
        ]
        + [pl.BlockSpec((2, width), lambda j, *_: (0, 0))] * 3,
        [pl.BlockSpec((PLANE, LEVELS, rows, tile), lambda j, *_: (0, 0, 0, j))],
        [sds((PLANE, LEVELS, rows, columns + tile), low)],
        (tiles + 1,),
        0,
        [pltpu.VMEM((width, frames), low)],
        brief=True,
    )


def plane_sum_kernel(info, got, send, keep):
    for ref, parity in ((send, 1 - info[0]), (keep, info[0])):
        total = got[0, 0, parity].astype(f32)
        for source in range(1, PLANE):
            total = total + got[source, 0, parity].astype(f32)
        ref[0] = total.astype(low)


def plane_sum(token, got, info):
    rows, width = got.shape[2:]
    out = pl.BlockSpec((1, rows, width), lambda j, *_: (j, 0, 0))
    return ordered(
        plane_sum_kernel,
        token,
        (got.reshape(PLANE, 2, 2, rows, width),),
        [pl.BlockSpec((PLANE, 1, 2, rows, width), lambda j, *_: (0, j, 0, 0, 0))],
        [out, out],
        [sds((2, rows, width), low)] * 2,
        (2,),
        0,
        info=info,
    )


def level_sum_kernel(_, keep_pass, got_pass, keep_own, got_own, passed, own):
    passed[...] = (keep_pass[0, 0].astype(f32) + got_pass[0, 0].astype(f32)).astype(low)
    own[...] = keep_own[0, 0].astype(f32) + got_own[0, 0].astype(f32)


def level_sum(token, keep, got, info, brief=True):
    count, _, rows, width = keep.shape
    block = rows // 2 if rows % 32 == 0 else rows
    steps = rows // block
    off = pl.BlockSpec((1, 1, block, width), lambda i, j, info: (i, 1 - info[0], j, 0))
    own = pl.BlockSpec((1, 1, block, width), lambda i, j, info: (i, info[0], j, 0))
    out = pl.BlockSpec((block, width), lambda i, j, info: (i * steps + j, 0))
    return ordered(
        level_sum_kernel,
        token,
        (keep, got, keep, got),
        [off, off, own, own],
        [out, out],
        [sds((count * rows, width), low), sds((count * rows, width), f32)],
        (count, steps),
        0,
        info=info,
        brief=brief,
    )


def unit_pack_kernel(counts, _, *refs):
    owns, lasts, out = refs[:-1:2], refs[1:-1:2], refs[-1]
    step = pl.program_id(0)
    for own, last, (first, count) in zip(owns, lasts, counts):

        @pl.when((step >= first) & (step < first + count))
        def _():
            total = (own[...] + last[...].astype(f32)).astype(low)
            total = total.reshape(3, PLANE, out.shape[2], out.shape[3])
            for chip in range(PLANE):
                out[chip] = total[:, chip]


def unit_pack(token, sums, rows):
    tile = sums[0][0].shape[1]
    r = rows // (3 * PLANE)
    specs_in, counts, first = [], [], 0
    for own, _ in sums:
        count = own.shape[0] // rows

        def place(j, info, first=first, count=count):
            return (jnp.clip(j - first, 0, count - 1), 0)

        specs_in += [pl.BlockSpec((rows, tile), place)] * 2
        counts.append((first, count))
        first += count
    return ordered(
        functools.partial(unit_pack_kernel, counts),
        token,
        tuple(array for pair in sums for array in pair),
        specs_in,
        [pl.BlockSpec((PLANE, 3, r, tile), lambda j, *_: (0, 0, 0, j))],
        [sds((PLANE, 3, r, tile * first), low)],
        (first,),
        0,
    )


def unit_unpack_kernel(_, got, down, gate, up):
    down[...] = got[0, 0].astype(f32).T
    gate[...] = got[0, 1].astype(f32)
    up[...] = got[0, 2].astype(f32)


def unit_unpack(token, got):
    _, _, r, units = got.shape
    across = pl.BlockSpec((r, units), lambda j, *_: (0, j))
    return ordered(
        unit_unpack_kernel,
        token,
        (got,),
        [pl.BlockSpec((1, 3, r, units), lambda j, *_: (j, 0, 0, 0))],
        [pl.BlockSpec((units, r), lambda j, *_: (j, 0)), across, across],
        [sds((PLANE * units, r), f32)] + [sds((r, PLANE * units), f32)] * 2,
        (PLANE,),
        0,
    )


def head_pack_kernel(_, own, last, out):
    total = (own[...] + last[...].astype(f32)).T.astype(low)
    out[...] = total.reshape(out.shape)


def head_pack(token, own, last):
    features, columns = own.shape
    shape = (PLANE, columns // PLANE, features)
    return ordered(
        head_pack_kernel,
        token,
        (own, last),
        [pl.BlockSpec(own.shape, lambda j, *_: (0, 0))] * 2,
        [pl.BlockSpec(shape, lambda j, *_: (0, 0, 0))],
        [sds(shape, low)],
        (1,),
        0,
        brief=True,
    )


def head_unpack_kernel(_, got, *outs):
    groups = got.shape[2] // (3 * HEAD)
    for index, out in enumerate(outs):
        pieces = []
        for group in range(groups):
            first = (index * groups + group) * HEAD
            pieces += [got[chip, :, first : first + HEAD] for chip in range(PLANE)]
        out[...] = jnp.concatenate(pieces, axis=1).astype(f32)


def head_unpack(token, got):
    chips, r, features = got.shape
    shape = (r, chips * features // 3)
    return ordered(
        head_unpack_kernel,
        token,
        (got,),
        [pl.BlockSpec(got.shape, lambda j, *_: (0, 0, 0))],
        [pl.BlockSpec(shape, lambda j, *_: (0, 0))] * 3,
        [sds(shape, f32)] * 3,
        (1,),
        0,
    )


def head_kernel(info, grads_mine, grads_other, in_mine, in_other, send, keep, acc):
    step = pl.program_id(0)
    rows = acc.shape[0]
    term = product_plain(grads_mine[0].reshape(rows, -1), in_mine[...]) + product_plain(
        grads_other[0].reshape(rows, -1), in_other[...]
    )

    @pl.when(step == 0)
    def _():
        acc[...] = term

    @pl.when(step != 0)
    def _():
        acc[...] += term

    @pl.when(step == pl.num_programs(0) - 1)
    def _():
        width = send.shape[2]
        for level in range(LEVELS):
            for ref, parity in ((send, 1 - info[1]), (keep, info[1])):

                @pl.when(parity == level % 2)
                def _():
                    ref[level // 2] = acc[:, level * width : (level + 1) * width].astype(low)


def head_products(token, info, grads, normed):
    _, three, features, frames = grads.shape
    width = normed[0].shape[1]
    chunk = normed[0].shape[0] // PLANE
    rows = pl.BlockSpec((chunk, width), lambda j, info: (j, 0))
    half = (LEVELS // 2, three * features, width // LEVELS)
    return ordered(
        head_kernel,
        token,
        (grads, grads, *normed),
        [
            pl.BlockSpec((1, three, features, chunk), lambda j, info: (j, 0, 0, info[0])),
            pl.BlockSpec((1, three, features, chunk), lambda j, info: (j, 0, 0, 1 - info[0])),
            rows,
            rows,
        ],
        [pl.BlockSpec(half, lambda j, info: (0, 0, 0))] * 2,
        [sds(half, low)] * 2,
        (PLANE,),
        2 * three * features * PLANE * frames * width,
        [pltpu.VMEM((three * features, width), f32)],
        info,
        brief=True,
    )


def on_plane(
    hidden_in,
    out_grad,
    prompt_states,
    row_split,
    prompt_len,
    gain_attn,
    bias_attn,
    gain_cross,
    bias_cross,
    gain_ff,
    bias_ff,
    w_query,
    w_key,
    w_value,
    w_out,
    c_query,
    c_key,
    c_value,
    c_out,
    w_gate,
    w_up,
    w_down,
):
    frames, width = hidden_in.shape
    plane, level = lax.axis_index("dp") % PLANE, lax.axis_index("dp") // PLANE
    positions = jnp.arange(frames, dtype=jnp.int32)
    row_ids = (positions >= row_split[0]).astype(jnp.int32)
    tables = rotary_tables((positions - row_ids * row_split[0]).astype(f32), 2 * HEAD)

    tile = 256
    tiles = w_gate.shape[1] // (PLANE * tile)
    zero = jnp.zeros((1,), jnp.int32)
    half = zero + lax.axis_index("tensor")
    parity, upper = zero + level % 2, zero + level // 2
    info = jnp.concatenate([row_split, prompt_len, half])
    unit_info = jnp.concatenate([zero + plane * tiles, parity])
    head_info = jnp.concatenate([half, parity])
    chips = [[PLANE * z + p for p in range(PLANE)] for z in range(LEVELS)]

    def swapped(part):
        return lax.ppermute(part, "tensor", [(0, 1), (1, 0)])

    def in_plane(values):
        shape = values.shape
        return lax.all_to_all(
            values, "dp", 0, 0, axis_index_groups=chips, tiled=True
        ).reshape(shape)

    def gathered(copies):
        return in_plane(copies.reshape(-1, width))

    def level_swap(values, mask):
        return lax.ppermute(values, "dp", pairs(mask))

    token = jnp.zeros((8, 128), f32)
    context = prompt_states.reshape(2 * PROMPT, prompt_states.shape[2])
    cross_key = product_plain(context, c_key).astype(low)
    cross_value = product_plain(context, c_value).astype(low)
    copies_one, copies, query, key, value, attended_one, logsum_one, part, token = self_forward(
        token,
        info,
        hidden_in,
        gain_attn,
        bias_attn,
        w_query,
        w_key,
        w_value,
        w_out,
        tables,
        out_grad,
    )
    part_swapped = swapped(part)
    frames_out = gathered(copies)
    resid_one, input_two, cross_query, attended_two, logsum_two, part, token = cross_forward(
        token,
        info,
        hidden_in,
        part,
        part_swapped,
        gain_cross,
        bias_cross,
        c_query,
        cross_key,
        cross_value,
        c_out,
    )
    part_swapped = swapped(part)
    resid_two, input_three, copies, token = norm_forward(
        token, half, resid_one, part, part_swapped, gain_ff, bias_ff
    )
    frames_out, token = hold(token, frames_out)
    frames_in = gathered(copies)
    frames_out = (frames_out, swapped(frames_out))
    sum_part, back_part, token = ff_both(token, input_three, out_grad, w_gate, w_up, w_down)
    frames_in, token = hold(token, frames_in)
    frames_in = (frames_in, swapped(frames_in))
    back_swapped = swapped(back_part)
    copies_one, token = hold(token, copies_one)
    frames_one = gathered(copies_one)

    def share(token, index, count):
        return ff_share(token, unit_info, frames_in, frames_out, w_gate, w_up, w_down, tile, index, count)

    send_a, keep_a, token = share(token, 0, 1)
    got_a = level_swap(send_a, PLANE)
    grad_two, grad_cross_out, vectors_ff, query_grad, key_grad, value_grad, part, token = cross_backward(
        token,
        info,
        resid_two,
        back_part,
        back_swapped,
        out_grad,
        gain_ff,
        c_out,
        cross_query,
        cross_key,
        cross_value,
        attended_two,
        logsum_two,
        c_query,
    )
    part_swapped = swapped(part)
    r, c = width // 16, context.shape[1] // 16
    products, token = weight_products(
        token,
        [grad_cross_out, input_two, context],
        [(0, 0), (1, r), (2, 2 * r), (2, 2 * r + c)],
        [attended_two, query_grad, key_grad, value_grad],
    )
    frames_one, token = hold(token, frames_one)
    got_cross = in_plane(products)
    frames_one_other = swapped(frames_one)
    pass_a, own_a, token = level_sum(token, keep_a, got_a, upper)
    last_a = level_swap(pass_a, 2 * PLANE)
    send_b, keep_b, token = share(token, 1, 1)
    got_b = level_swap(send_b, PLANE)
    send_c, keep_c, token = share(token, 2, tiles - 2)
    got_c = level_swap(send_c, PLANE)
    frames_one_other, token = hold(token, frames_one_other, True)
    frames_one = (frames_one, frames_one_other)
    grad_one, grad_self_out, vectors_cross, grads, part, token = self_backward(
        token,
        info,
        resid_one,
        part,
        part_swapped,
        grad_two,
        gain_cross,
        w_out,
        query,
        key,
        value,
        attended_one,
        logsum_one,
        w_query,
        w_key,
        w_value,
        tables,
    )
    last_a, token = hold(token, last_a, True)
    sum_part, token = hold(token, sum_part, True)
    sum_swapped, part_swapped = swapped(sum_part), swapped(part)
    pass_b, own_b, token = level_sum(token, keep_b, got_b, upper)
    last_b = level_swap(pass_b, 2 * PLANE)
    got_cross, token = hold(token, got_cross)
    grads, token = hold(token, grads)
    got_heads = in_plane(grads)
    pass_c, own_c, token = level_sum(token, keep_c, got_c, upper)
    last_c = level_swap(pass_c, 2 * PLANE)
    send_x, keep_x, token = plane_sum(token, got_cross, parity)
    got_x = level_swap(send_x, PLANE)
    grad_hidden, vectors_attn, result, token = last_backward(
        token, hidden_in, part, part_swapped, grad_one, gain_attn, resid_two, sum_part, sum_swapped
    )
    products, token = out_products(
        token, grad_self_out, attended_one, (vectors_attn, vectors_cross, vectors_ff)
    )
    last_b, token = hold(token, last_b, True)
    got_heads, token = hold(token, got_heads, True)
    products, token = hold(token, products, True)
    got_out = in_plane(products)
    send_h, keep_h, token = head_products(token, head_info, got_heads, frames_one)
    got_h = level_swap(send_h, PLANE)
    pass_x, own_x, token = level_sum(token, keep_x[None], got_x[None], upper)
    last_x = level_swap(pass_x, 2 * PLANE)
    last_c, token = hold(token, last_c, True)
    units, token = unit_pack(
        token, [(own_a, last_a), (own_b, last_b), (own_c, last_c)], 3 * width // LEVELS
    )
    pass_h, own_h, token = level_sum(token, keep_h[None], got_h[None], upper, False)
    last_h = level_swap(pass_h, 2 * PLANE)
    got_out, token = hold(token, got_out)
    units, token = hold(token, units, True)
    units = in_plane(units)
    send_o, keep_o, token = plane_sum(token, got_out, parity)
    got_o = level_swap(send_o, PLANE)
    last_x, token = hold(token, last_x, True)
    cross = add_low(own_x, last_x)
    heads, token = head_pack(token, own_h, last_h)
    pass_o, own_o, token = level_sum(token, keep_o[None], got_o[None], upper)
    last_o = level_swap(pass_o, 2 * PLANE)
    units, token = hold(token, units)
    heads, token = hold(token, heads, True)
    heads = in_plane(heads)
    grad_w_down, grad_w_gate, grad_w_up, token = unit_unpack(token, units)
    last_o, token = hold(token, last_o, True)
    outs = add_low(own_o, last_o)
    share_of = r // 2
    vectors = lax.dynamic_slice_in_dim(
        outs, lax.axis_index("tensor") * share_of, share_of, 0
    )[:, w_query.shape[1] : w_query.shape[1] + 6].T
    heads, token = hold(token, heads)
    grad_w_query, grad_w_key, grad_w_value, token = head_unpack(token, heads)
    return (
        result,
        grad_hidden,
        *(vectors[index] for index in range(6)),
        grad_w_query,
        grad_w_key,
        grad_w_value,
        outs[:, : w_query.shape[1]].T,
        cross[r : 2 * r],
        cross[2 * r : 2 * r + c],
        cross[2 * r + c :],
        cross[:r].T,
        grad_w_gate,
        grad_w_up,
        grad_w_down,
    )


def on_any(
    hidden_in,
    out_grad,
    prompt_states,
    row_split,
    prompt_len,
    gain_attn,
    bias_attn,
    gain_cross,
    bias_cross,
    gain_ff,
    bias_ff,
    w_query,
    w_key,
    w_value,
    w_out,
    c_query,
    c_key,
    c_value,
    c_out,
    w_gate,
    w_up,
    w_down,
):
    frame_count = hidden_in.shape[0]
    positions = jnp.arange(frame_count, dtype=jnp.int32)
    split_here = row_split[0]
    row_ids = (positions >= split_here).astype(jnp.int32)
    tables = rotary_tables((positions - row_ids * split_here).astype(jnp.float32), w_query.shape[1])
    key_index = jnp.arange(2 * PROMPT, dtype=jnp.int32)
    key_rows = key_index // PROMPT
    key_live = key_index % PROMPT < jnp.where(key_rows == 0, prompt_len[0], prompt_len[1])
    self_ok = row_ids[:, None] == row_ids[None, :]
    cross_ok = (row_ids[:, None] == key_rows[None, :]) & key_live[None, :]

    normed, scaled_one, inverse_one = normalize(hidden_in, gain_attn, bias_attn)
    input_one = normed.astype(low)
    query_one = rotate(product_plain(input_one, w_query), tables).astype(low)
    key_one = rotate(product_plain(input_one, w_key), tables).astype(low)
    value_one = product_plain(input_one, w_value).astype(low)
    attended_one, logsum_one = attend_forward(query_one, heads_of(key_one), heads_of(value_one), self_ok)
    resid_one = hidden_in + swap_sum(product_plain(attended_one, w_out))

    normed, scaled_two, inverse_two = normalize(resid_one, gain_cross, bias_cross)
    input_two = normed.astype(low)
    cross_query = product_plain(input_two, c_query).astype(low)
    context_flat = prompt_states.reshape(2 * PROMPT, prompt_states.shape[2])
    cross_key = product_plain(context_flat, c_key).astype(low)
    cross_value = product_plain(context_flat, c_value).astype(low)
    attended_two, logsum_two = attend_forward(
        cross_query, heads_of(cross_key), heads_of(cross_value), cross_ok
    )
    resid_two = resid_one + swap_sum(product_plain(attended_two, c_out))

    normed, scaled_three, inverse_three = normalize(resid_two, gain_ff, bias_ff)
    input_three = normed.astype(low)
    gate_pre = product_plain(input_three, w_gate)
    up_pre = product_plain(input_three, w_up)
    sigmoid_gate = jax.nn.sigmoid(gate_pre)
    mixed_low = (gate_pre * sigmoid_gate * up_pre).astype(low)
    result = resid_two + swap_sum(product_plain(mixed_low, w_down))

    grad_ff_out = out_grad.astype(low)
    grad_w_down = generic_sum(grad_ff_out, mixed_low).T
    grad_mixed = product_with_rows(grad_ff_out, w_down)
    grad_gate = (
        grad_mixed * up_pre * sigmoid_gate * (1.0 + gate_pre * (1.0 - sigmoid_gate))
    ).astype(low)
    grad_up = (grad_mixed * gate_pre * sigmoid_gate).astype(low)
    grad_w_gate = generic_sum(input_three, grad_gate)
    grad_w_up = generic_sum(input_three, grad_up)
    normed_grad_three = swap_sum(
        product_with_rows(grad_gate, w_gate) + product_with_rows(grad_up, w_up)
    )
    back_three, grad_gain_ff, grad_bias_ff = normalize_back(
        normed_grad_three, scaled_three, inverse_three, gain_ff
    )
    grad_two = out_grad + back_three
    grad_cross_out = grad_two.astype(low)
    grad_c_out = generic_sum(grad_cross_out, attended_two).T
    grad_attended_two = product_with_rows(grad_cross_out, c_out).astype(low)
    cross_query_grad, cross_key_grad, cross_value_grad = attend_backward(
        cross_query,
        heads_of(cross_key),
        heads_of(cross_value),
        cross_ok,
        grad_attended_two,
        logsum_two,
    )
    cross_query_grad = cross_query_grad.astype(low)
    cross_key_grad = cross_key_grad.astype(low)
    cross_value_grad = cross_value_grad.astype(low)
    grad_c_query = generic_sum(input_two, cross_query_grad)
    grad_c_key = generic_sum(context_flat, cross_key_grad)
    grad_c_value = generic_sum(context_flat, cross_value_grad)
    normed_grad_two = swap_sum(product_with_rows(cross_query_grad, c_query))
    back_two, grad_gain_cross, grad_bias_cross = normalize_back(
        normed_grad_two, scaled_two, inverse_two, gain_cross
    )
    grad_one = grad_two + back_two
    grad_self_out = grad_one.astype(low)
    grad_w_out = generic_sum(grad_self_out, attended_one).T
    grad_attended_one = product_with_rows(grad_self_out, w_out).astype(low)
    query_grad, key_grad, value_grad = attend_backward(
        query_one, heads_of(key_one), heads_of(value_one), self_ok, grad_attended_one, logsum_one
    )
    query_grad = rotate_back(query_grad, tables).astype(low)
    key_grad = rotate_back(key_grad, tables).astype(low)
    value_grad = value_grad.astype(low)
    grad_w_query = generic_sum(input_one, query_grad)
    grad_w_key = generic_sum(input_one, key_grad)
    grad_w_value = generic_sum(input_one, value_grad)
    normed_grad_one = swap_sum(
        product_with_rows(query_grad, w_query)
        + product_with_rows(key_grad, w_key)
        + product_with_rows(value_grad, w_value)
    )
    back_one, grad_gain_attn, grad_bias_attn = normalize_back(
        normed_grad_one, scaled_one, inverse_one, gain_attn
    )
    grad_hidden = grad_one + back_one
    vectors = lax.psum(
        jnp.stack(
            [
                grad_gain_attn,
                grad_bias_attn,
                grad_gain_cross,
                grad_bias_cross,
                grad_gain_ff,
                grad_bias_ff,
            ]
        ),
        "dp",
    )
    vectors = own_share(vectors)
    return (
        result,
        grad_hidden,
        vectors[0],
        vectors[1],
        vectors[2],
        vectors[3],
        vectors[4],
        vectors[5],
        grad_w_query,
        grad_w_key,
        grad_w_value,
        grad_w_out,
        grad_c_query,
        grad_c_key,
        grad_c_value,
        grad_c_out,
        grad_w_gate,
        grad_w_up,
        grad_w_down,
    )


def solution(mesh):
    in_specs = (
        P("dp", None),
        P("dp", None),
        P("dp", None, None),
        P("dp"),
        P("dp"),
        P(),
        P(),
        P(),
        P(),
        P(),
        P(),
        P(None, "tensor"),
        P(None, "tensor"),
        P(None, "tensor"),
        P("tensor", None),
        P(None, "tensor"),
        P(None, "tensor"),
        P(None, "tensor"),
        P("tensor", None),
        P(None, "tensor"),
        P(None, "tensor"),
        P("tensor", None),
    )
    out_specs = (
        P("dp", None),
        P("dp", None),
        P(("dp", "tensor")),
        P(("dp", "tensor")),
        P(("dp", "tensor")),
        P(("dp", "tensor")),
        P(("dp", "tensor")),
        P(("dp", "tensor")),
        P("dp", "tensor"),
        P("dp", "tensor"),
        P("dp", "tensor"),
        P("tensor", "dp"),
        P("dp", "tensor"),
        P("dp", "tensor"),
        P("dp", "tensor"),
        P("tensor", "dp"),
        P("dp", "tensor"),
        P("dp", "tensor"),
        P("tensor", "dp"),
    )
    known = mesh.shape["dp"] == PLANE * LEVELS and mesh.shape["tensor"] == 2
    return jax.shard_map(
        on_plane if known else on_any, mesh=mesh, in_specs=in_specs, out_specs=out_specs, check_vma=False
    )
```

```python
import functools
import math

import jax
import jax.numpy as jnp
from jax import lax
from jax.experimental import pallas as pl
from jax.experimental.pallas import tpu as pltpu
from jax.sharding import PartitionSpec as P

PROMPT = 128
HEAD = 64
PLANE = 4
LEVELS = 4
VMEM_LIMIT = 62 * 2**20
COST = 3
FLOOR = 15 * 10**9

low = jnp.bfloat16
f32 = jnp.float32
sds = jax.ShapeDtypeStruct


norm_eps = 1e-05
score_scale = 0.125
masked_score = -1e30


def product_plain(left_side, right_side):
    return jnp.dot(left_side, right_side, preferred_element_type=jnp.float32)


def product_over_rows(left_side, right_side):
    return lax.dot_general(
        left_side, right_side, (((0,), (0,)), ((), ())), preferred_element_type=jnp.float32
    )


def product_with_rows(left_side, right_side):
    return lax.dot_general(
        left_side, right_side, (((1,), (1,)), ((), ())), preferred_element_type=jnp.float32
    )


def rotary_tables(positions, width):
    dim_index = jnp.arange(width) % HEAD
    freq_index = (dim_index % 16).astype(jnp.float32)
    inverse_freq = jnp.exp(freq_index * (-math.log(10000.0) / 16.0))
    angles = positions[:, None] * inverse_freq[None, :]
    cosine = jnp.cos(angles)
    sine_part = jnp.sin(angles)
    cos_table = jnp.where(dim_index < 32, cosine, 1.0)
    sin_lower = jnp.where(dim_index < 16, -sine_part, 0.0)
    sin_upper = jnp.where((dim_index >= 16) & (dim_index < 32), sine_part, 0.0)
    return (cos_table, sin_lower, sin_upper)


def rotate(values, tables):
    cos_table, sin_lower, sin_upper = tables
    return (
        values * cos_table
        + jnp.roll(values, -16, axis=1) * sin_lower
        + jnp.roll(values, 16, axis=1) * sin_upper
    )


def rotate_back(incoming, tables):
    cos_table, sin_lower, sin_upper = tables
    return (
        incoming * cos_table
        + jnp.roll(incoming * sin_lower, 16, axis=1)
        + jnp.roll(incoming * sin_upper, -16, axis=1)
    )


def normalize(values, norm_gain, norm_shift):
    average = jnp.mean(values, axis=-1, keepdims=True)
    centered = values - average
    variance = jnp.mean(centered * centered, axis=-1, keepdims=True)
    inverse = lax.rsqrt(variance + norm_eps)
    scaled = centered * inverse
    return (scaled * norm_gain + norm_shift, scaled, inverse)


def normalize_back(incoming, scaled, inverse, norm_gain):
    grad_gain = jnp.sum(incoming * scaled, axis=0)
    grad_shift = jnp.sum(incoming, axis=0)
    weighted = incoming * norm_gain
    grad_input = inverse * (
        weighted
        - jnp.mean(weighted, axis=-1, keepdims=True)
        - scaled * jnp.mean(weighted * scaled, axis=-1, keepdims=True)
    )
    return (grad_input, grad_gain, grad_shift)


def heads_of(values):
    return values.reshape(values.shape[0], values.shape[1] // HEAD, HEAD)


def attend_forward(query_block, key_heads, value_heads, allowed):
    query_heads = heads_of(query_block)
    scores = (
        jnp.einsum("qhd,khd->hqk", query_heads, key_heads, preferred_element_type=jnp.float32)
        * score_scale
    )
    scores = jnp.where(allowed[None], scores, masked_score)
    largest = jnp.max(scores, axis=-1, keepdims=True)
    exp_scores = jnp.exp(scores - largest)
    totals = jnp.sum(exp_scores, axis=-1, keepdims=True)
    soft_weights = (exp_scores / totals).astype(jnp.bfloat16)
    mixed_heads = jnp.einsum(
        "hqk,khd->qhd", soft_weights, value_heads, preferred_element_type=jnp.float32
    )
    mixed_flat = mixed_heads.reshape(query_block.shape[0], query_block.shape[1]).astype(
        jnp.bfloat16
    )
    return (mixed_flat, largest[..., 0] + jnp.log(totals[..., 0]))


def attend_backward(query_block, key_heads, value_heads, allowed, grad_block, logsum_block):
    query_heads = heads_of(query_block)
    grad_heads = heads_of(grad_block)
    scores = (
        jnp.einsum("qhd,khd->hqk", query_heads, key_heads, preferred_element_type=jnp.float32)
        * score_scale
    )
    scores = jnp.where(allowed[None], scores, masked_score)
    soft_weights = jnp.exp(scores - logsum_block[..., None])
    grad_weights = jnp.einsum(
        "qhd,khd->hqk", grad_heads, value_heads, preferred_element_type=jnp.float32
    )
    inner_sum = jnp.sum(soft_weights * grad_weights, axis=-1, keepdims=True)
    grad_scores = (soft_weights * (grad_weights - inner_sum)).astype(jnp.bfloat16)
    grad_query = (
        jnp.einsum("hqk,khd->qhd", grad_scores, key_heads, preferred_element_type=jnp.float32)
        * score_scale
    )
    grad_key = (
        jnp.einsum("hqk,qhd->khd", grad_scores, query_heads, preferred_element_type=jnp.float32)
        * score_scale
    )
    grad_value = jnp.einsum(
        "hqk,qhd->khd",
        soft_weights.astype(jnp.bfloat16),
        grad_heads,
        preferred_element_type=jnp.float32,
    )
    return (
        grad_query.reshape(query_block.shape),
        grad_key.reshape(grad_key.shape[0], -1),
        grad_value.reshape(grad_value.shape[0], -1),
    )


def swap_sum(partial):
    low = partial.astype(jnp.bfloat16)
    if lax.axis_size("tensor") == 2:
        other = lax.ppermute(low, "tensor", [(0, 1), (1, 0)])
        return low.astype(jnp.float32) + other.astype(jnp.float32)
    return lax.psum(low, "tensor").astype(jnp.float32)


def pairs(mask):
    return [(i, i ^ mask) for i in range(16)]


def own_share(vectors):
    share = vectors.shape[1] // (lax.axis_size("dp") * lax.axis_size("tensor"))
    index = lax.axis_index("dp") * lax.axis_size("tensor") + lax.axis_index("tensor")
    return lax.dynamic_slice_in_dim(vectors, index * share, share, 1)


def generic_sum(rows_side, column_side):
    return lax.psum_scatter(
        product_over_rows(rows_side, column_side).astype(jnp.bfloat16),
        "dp",
        scatter_dimension=0,
        tiled=True,
    ).astype(jnp.float32)


def add_low(*terms):
    total = terms[0].astype(jnp.float32)
    for term in terms[1:]:
        total = total + term.astype(jnp.float32)
    return total


def ff_parts(gate, up, grad_mixed):
    sig = 0.5 * jnp.tanh(0.5 * gate) + 0.5
    act = gate * sig
    return (
        (act * up).astype(low),
        (grad_mixed * up * sig * (1.0 + gate * (1.0 - sig))).astype(low),
        (grad_mixed * act).astype(low),
    )


def turn(values, cos, lower, upper):
    width = values.shape[1]
    return (values * cos + pltpu.roll(values, width - 16, 1) * lower + pltpu.roll(values, 16, 1) * upper)

def turn_back(values, cos, lower, upper):
    width = values.shape[1]
    return (values * cos + pltpu.roll(values * lower, 16, 1) + pltpu.roll(values * upper, width - 16, 1))

def normed_rows(values, gain, shift):
    average = jnp.mean(values, axis=-1, keepdims=True)
    centered = values - average
    variance = jnp.mean(centered * centered, axis=-1, keepdims=True)
    return centered * lax.rsqrt(variance + norm_eps) * gain + shift

def over_rows(rows, body, chunk=32):
    @pl.loop(0, rows // chunk, unroll=min(4, rows // chunk))
    def _(i):
        body(pl.ds(pl.multiple_of(i * chunk, chunk), chunk))

def attend(q, k, v, mask, lse_ref):
    q_turned = (q * jnp.bfloat16(0.125)).T
    v_turned = v.T
    heads = [slice(h * HEAD, (h + 1) * HEAD) for h in range(q.shape[1] // HEAD)]
    scores = [product_plain(k[:, c], q_turned[c, :]) for c in heads]
    weights, scales = [], []
    for h, s in enumerate(scores):
        s = s + mask
        m = jnp.max(s, axis=0, keepdims=True)
        e = jnp.exp(s - m)
        total = jnp.sum(e, axis=0, keepdims=True)
        weights.append(e.astype(low))
        scales.append(1.0 / total)
        lse_ref[h : h + 1, :] = m + jnp.log(total)
    outs = [product_plain(v_turned[c, :], e) * x for c, e, x in zip(heads, weights, scales)]
    return jnp.concatenate(outs, axis=0).T.astype(low)


def attend_back(q, k, v, g, att, mask, lse):
    scaled = q * jnp.bfloat16(0.125)
    q_turned = scaled.T
    g_turned = g.T
    k_turned = k.T
    weighted = g_turned.astype(f32) * att.T.astype(f32)
    dq, dk, dv = [], [], []
    for h in range(q.shape[1] // HEAD):
        c = slice(h * HEAD, (h + 1) * HEAD)
        p = jnp.exp(product_plain(k[:, c], q_turned[c, :]) + (mask - lse[h : h + 1, :]))
        dp = product_plain(v[:, c], g_turned[c, :])
        inner = jnp.sum(weighted[c, :], axis=0, keepdims=True)
        ds = (p * (dp - inner)).astype(low)
        dq.append(product_plain(k_turned[c, :], ds))
        dk.append(product_plain(ds, scaled[:, c]))
        dv.append(product_plain(p.astype(low), g[:, c]))
    return (
        jnp.concatenate(dq, axis=0).T * 0.125,
        jnp.concatenate(dk, axis=1),
        jnp.concatenate(dv, axis=1),
    )


def self_mask(split, T):
    r=lax.broadcasted_iota(jnp.int32,(T,T),0)>=split
    c=lax.broadcasted_iota(jnp.int32,(T,T),1)>=split
    return jnp.where(r==c,0.0,masked_score).astype(f32)

def key_half(info, index, frames, keys):
    second = info[0] < frames
    start = jnp.where(second, keys // 2, 0) if index == 1 else 0
    live = jnp.where(second, info[2], info[1]) if index == 1 else info[1]
    return start, live


def half_mask(live, keys, frames):
    return jnp.where(
        lax.broadcasted_iota(jnp.int32, (keys, frames), 0) < live, 0.0, masked_score
    ).astype(f32)


def key_blocks(info, k_ref, v_ref, frames):
    keys = k_ref.shape[0]
    k, v, masks = [], [], []
    for index in range(2):
        start, live = key_half(info, index, frames, keys)
        here = pl.ds(start if index == 0 else pl.multiple_of(start, keys // 2), keys // 2)
        k.append(k_ref[here, :])
        v.append(v_ref[here, :])
        masks.append(half_mask(live, keys // 2, frames // 2))
    return k, v, jnp.concatenate(masks, axis=1)


def cross_attend(info, q, k_ref, v_ref, lse_ref):
    half = q.shape[0] // 2
    q_turned = (q * jnp.bfloat16(0.125)).T
    k, v, mask = key_blocks(info, k_ref, v_ref, 2 * half)
    v_turned = [values.T for values in v]
    outs = []
    for h in range(q.shape[1] // HEAD):
        c = slice(h * HEAD, (h + 1) * HEAD)
        s = [product_plain(k[i][:, c], q_turned[c, i * half : (i + 1) * half]) for i in range(2)]
        s = jnp.concatenate(s, axis=1) + mask
        m = jnp.max(s, axis=0, keepdims=True)
        e = jnp.exp(s - m)
        total = jnp.sum(e, axis=0, keepdims=True)
        lse_ref[h : h + 1, :] = m + jnp.log(total)
        e = e.astype(low)
        o = [product_plain(v_turned[i][c, :], e[:, i * half : (i + 1) * half]) for i in range(2)]
        outs.append(jnp.concatenate(o, axis=1) * (1.0 / total))
    return jnp.concatenate(outs, axis=0).T.astype(low)


def cross_attend_back(info, q, k_ref, v_ref, g, att, lse):
    half = q.shape[0] // 2
    scaled = q * jnp.bfloat16(0.125)
    q_turned = scaled.T
    g_turned = g.T
    weighted = g_turned.astype(f32) * att.T.astype(f32)
    k, v, mask = key_blocks(info, k_ref, v_ref, 2 * half)
    k_turned = [values.T for values in k]
    parts = [slice(0, half), slice(half, 2 * half)]
    dq, dk, dv = [], [[], []], [[], []]
    for h in range(q.shape[1] // HEAD):
        c = slice(h * HEAD, (h + 1) * HEAD)
        s = [product_plain(k[i][:, c], q_turned[c, parts[i]]) for i in range(2)]
        dp = [product_plain(v[i][:, c], g_turned[c, parts[i]]) for i in range(2)]
        p = jnp.exp(jnp.concatenate(s, axis=1) + (mask - lse[h : h + 1, :]))
        inner = jnp.sum(weighted[c, :], axis=0, keepdims=True)
        ds = (p * (jnp.concatenate(dp, axis=1) - inner)).astype(low)
        p = p.astype(low)
        dq.append(
            jnp.concatenate(
                [product_plain(k_turned[i][c, :], ds[:, parts[i]]) for i in range(2)], axis=1
            )
        )
        for i in range(2):
            dk[i].append(product_plain(ds[:, parts[i]], scaled[parts[i], c]))
            dv[i].append(product_plain(p[:, parts[i]], g[parts[i], c]))
    second = (info[0] < 2 * half).astype(f32)

    def by_row(halves):
        first, last = (jnp.concatenate(half, axis=1) for half in halves)
        return jnp.concatenate([first + last * (1.0 - second), last * second], axis=0)

    return jnp.concatenate(dq, axis=0).T * 0.125, by_row(dk), by_row(dv)


def norm_back_rows(x,e,gain,above,gain_acc,shift_acc):
    average=jnp.mean(x,axis=-1,keepdims=True)
    centered=x-average
    variance=jnp.mean(centered*centered,axis=-1,keepdims=True)
    inverse=lax.rsqrt(variance+norm_eps)
    n=centered*inverse
    en=e*n
    w=e*gain
    mean_w=jnp.mean(w,axis=-1,keepdims=True)
    mean_wn=jnp.mean(en*gain,axis=-1,keepdims=True)
    fold=lambda t: jnp.sum(t.reshape(t.shape[0]//8,8,t.shape[1]),axis=0)
    gain_acc[...]+=fold(en)
    shift_acc[...]+=fold(e)
    return above+inverse*(w-mean_w-n*mean_wn)

def norm_back_step(x, mine, other, above, gain, total, total_low, kept, vectors, gain_acc, shift_acc):
    step, block = pl.program_id(0), x.shape[0]

    @pl.when(step == 0)
    def _():
        gain_acc[...] = jnp.zeros_like(gain_acc)
        shift_acc[...] = jnp.zeros_like(shift_acc)

    @pl.when(step < BLOCKS)
    def _():
        def rows(r):
            e = mine[r, :].astype(f32) + other[r, :].astype(f32)
            t = norm_back_rows(x[r, :], e, gain[...][None], above[r, :], gain_acc, shift_acc)
            total[r, :] = t
            total_low[r, :] = t.astype(low)
            kept[within(step, block, r), :] = t.astype(low)

        over_rows(block, rows)

    @pl.when(step == BLOCKS - 1)
    def _():
        vectors[0:1, :] = jnp.sum(gain_acc[...], axis=0, keepdims=True)
        vectors[1:2, :] = jnp.sum(shift_acc[...], axis=0, keepdims=True)


def ordered(kernel, token, args, in_specs, out_specs, out_shape, grid, flops, scratch=(), info=None, brief=False):
    if info is None:
        info = jnp.zeros((1,), jnp.int32)
    inputs, outputs = len(args), len(out_shape)

    def body(info_ref, *refs):
        token_ref = refs[inputs + 1 + outputs]

        @pl.when(functools.reduce(jnp.logical_and, [pl.program_id(i) == 0 for i in range(len(grid))]))
        def _():
            token_ref[...] = jnp.zeros_like(token_ref)

        kernel(
            info_ref,
            *refs[:inputs],
            *refs[inputs + 1 : inputs + 1 + outputs],
            *refs[inputs + 2 + outputs :],
        )

    moved = sum(math.prod(a.shape) * a.dtype.itemsize for a in (*args, *out_shape))
    *results, token = pl.pallas_call(
        body,
        grid_spec=pltpu.PrefetchScalarGridSpec(
            num_scalar_prefetch=1,
            grid=grid,
            in_specs=[*in_specs, pl.BlockSpec(memory_space=pl.ANY)],
            out_specs=[*out_specs, pl.BlockSpec((8, 128), lambda *_: (0, 0))],
            scratch_shapes=list(scratch),
        ),
        out_shape=[*out_shape, sds((8, 128), f32)],
        compiler_params=pltpu.CompilerParams(vmem_limit_bytes=VMEM_LIMIT),
        cost_estimate=pl.CostEstimate(flops=0 if brief else max(FLOOR, int(flops * COST)), bytes_accessed=0 if brief else int(moved * COST), transcendentals=0),
    )(info, *args, token)
    return (*results, token)


def hold(token, values, brief=False):
    def nothing(values_ref, token_ref, out_ref, token_out):
        token_out[...] = jnp.zeros_like(token_out)

    return pl.pallas_call(
        nothing,
        in_specs=[pl.BlockSpec(memory_space=pl.ANY)] * 2,
        out_specs=[pl.BlockSpec(memory_space=pl.ANY), pl.BlockSpec(memory_space=pltpu.VMEM)],
        out_shape=[sds(values.shape, values.dtype), sds((8, 128), f32)],
        input_output_aliases={0: 0},
        compiler_params=pltpu.CompilerParams(vmem_limit_bytes=VMEM_LIMIT),
        cost_estimate=pl.CostEstimate(flops=0 if brief else FLOOR, bytes_accessed=0, transcendentals=0),
    )(values, token)


def specs(frames, width, tile, blocks=0):
    def tile_of(j):
        return jnp.maximum(j - blocks, 0) if blocks else j

    whole = pl.BlockSpec((frames, width), lambda j, *_: (0, 0))
    vector = pl.BlockSpec((width,), lambda j, *_: (0,))
    column = pl.BlockSpec((width, tile), lambda j, *_: (0, tile_of(j)))
    row = pl.BlockSpec((tile, width), lambda j, *_: (tile_of(j), 0))
    act = pl.BlockSpec((frames, tile), lambda j, *_: (0, tile_of(j)))
    table = pl.BlockSpec((frames, 2 * HEAD), lambda j, *_: (0, 0))
    logsum = pl.BlockSpec((8, frames), lambda j, *_: (tile_of(j), 0))
    return whole, vector, column, row, act, table, logsum


BLOCKS = 4


def widened(*tables):
    return tuple(jnp.concatenate([table[...], table[...]], axis=1) for table in tables)


def row_block(frames, width):
    return pl.BlockSpec((frames // BLOCKS, width), lambda j, *_: (jnp.minimum(j, BLOCKS - 1), 0))


def copies_block(frames, width, place):
    return pl.BlockSpec(
        (PLANE, frames // BLOCKS, width),
        lambda j, info: (0, jnp.clip(j - BLOCKS // 2 * info[place], 0, BLOCKS // 2 - 1), 0),
    )


def within(step, rows, r):
    return pl.ds(pl.multiple_of(step * rows + r.start, r.size), r.size)


def added(acc, term, result, first=0):
    step = pl.program_id(0)

    @pl.when(step == first)
    def _():
        acc[...] = term

    @pl.when(step != first)
    def _():
        acc[...] += term

    @pl.when(step == pl.num_programs(0) - 1)
    def _():
        result[...] = acc[...].astype(result.dtype)


def self_kernel(info, hid, gain, shift, wq, wk, wv, wo, cos, lower, upper, grad, copies, grad_copies, q, k, v, att, logsum, part, acc, mask, normed):
    step, frames, block = pl.program_id(0), normed.shape[0], hid.shape[0]

    @pl.when(step == 0)
    def _():
        mask[...] = self_mask(info[0], frames)

    @pl.when(step < BLOCKS)
    def _():
        def rows(r):
            normed[within(step, block, r), :] = normed_rows(hid[r, :], gain[...][None], shift[...][None]).astype(low)

        over_rows(block, rows)

    @pl.when((step < BLOCKS) & (step * 2 // BLOCKS == info[3]))
    def _():
        mine = normed[pl.ds(pl.multiple_of(step * block, block), block), :]
        for chip in range(PLANE):
            copies[chip] = mine

    @pl.when(step < BLOCKS // 2)
    def _():
        grad_low = grad[...].astype(low)
        for chip in range(PLANE):
            grad_copies[chip] = grad_low

    @pl.when(step >= BLOCKS)
    def _():
        n = normed[...]
        tables = widened(cos, lower, upper)
        q[...] = turn(product_plain(n, wq[...]), *tables).astype(low)
        k[...] = turn(product_plain(n, wk[...]), *tables).astype(low)
        v[...] = product_plain(n, wv[...]).astype(low)
        attended = attend(q[...], k[...], v[...], mask[...], logsum)
        att[...] = attended
        added(acc, product_plain(attended, wo[...]), part, BLOCKS)


def self_forward(token, info, hid, gain, shift, wq, wk, wv, wo, tables, grad, tile=4 * HEAD):
    frames, width = hid.shape
    columns = wq.shape[1]
    whole, vector, column, row, act, table, logsum = specs(frames, width, tile, BLOCKS)
    blocks = row_block(frames, width)
    here = frames // BLOCKS
    return ordered(
        self_kernel,
        token,
        (hid, gain, shift, wq, wk, wv, wo, *tables, grad),
        [blocks, vector, vector, column, column, column, row, table, table, table]
        + [
            pl.BlockSpec(
                (here, width),
                lambda j, info: (BLOCKS // 2 * info[3] + jnp.minimum(j, BLOCKS // 2 - 1), 0),
            )
        ],
        [
            copies_block(frames, width, 3),
            pl.BlockSpec((PLANE, here, width), lambda j, info: (0, jnp.minimum(j, BLOCKS // 2 - 1), 0)),
        ]
        + [act, act, act, act, logsum, whole],
        [sds((PLANE, frames // 2, width), low)] * 2
        + [sds((frames, columns), low)] * 4
        + [sds((columns // tile * 8, frames), f32), sds((frames, width), low)],
        (BLOCKS + columns // tile,),
        2 * frames * columns * (4 * width + 8 * frames),
        [
            pltpu.VMEM((frames, width), f32),
            pltpu.VMEM((frames, frames), f32),
            pltpu.VMEM((frames, width), low),
        ],
        info,
    )


def cross_kernel(info, hid, mine, other, gain, shift, cq, ck, cv, co, total, normed, q, att, logsum, part, acc, kept):
    step, block = pl.program_id(0), hid.shape[0]

    @pl.when(step < BLOCKS)
    def _():
        def rows(r):
            x = hid[r, :] + (mine[r, :].astype(f32) + other[r, :].astype(f32))
            total[r, :] = x
            n = normed_rows(x, gain[...][None], shift[...][None]).astype(low)
            normed[r, :] = n
            kept[within(step, block, r), :] = n

        over_rows(block, rows)

    @pl.when(step >= BLOCKS)
    def _():
        q[...] = product_plain(kept[...], cq[...]).astype(low)
        attended = cross_attend(info, q[...], ck, cv, logsum)
        att[...] = attended
        added(acc, product_plain(attended, co[...]), part, BLOCKS)


def cross_forward(token, info, hid, mine, other, gain, shift, cq, ck, cv, co, tile=4 * HEAD):
    frames, width = hid.shape
    columns, keys = cq.shape[1], ck.shape[0]
    whole, vector, column, row, act, table, logsum = specs(frames, width, tile, BLOCKS)
    key = pl.BlockSpec((keys, tile), lambda j, *_: (0, jnp.maximum(j - BLOCKS, 0)))
    blocks = row_block(frames, width)
    return ordered(
        cross_kernel,
        token,
        (hid, mine, other, gain, shift, cq, ck, cv, co),
        [blocks, blocks, blocks, vector, vector, column, key, key, row],
        [blocks, blocks, act, act, logsum, whole],
        [
            sds((frames, width), f32),
            sds((frames, width), low),
            sds((frames, columns), low),
            sds((frames, columns), low),
            sds((columns // tile * 8, frames), f32),
            sds((frames, width), low),
        ],
        (BLOCKS + columns // tile,),
        2 * frames * columns * (2 * width + 8 * keys),
        [pltpu.VMEM((frames, width), f32), pltpu.VMEM((frames, width), low)],
        info,
        brief=True,
    )


def norm_kernel(info, hid, mine, other, gain, shift, total, normed, copies):
    def rows(r):
        x = hid[r, :] + (mine[r, :].astype(f32) + other[r, :].astype(f32))
        total[r, :] = x
        normed[r, :] = normed_rows(x, gain[...][None], shift[...][None]).astype(low)

    over_rows(hid.shape[0], rows)

    @pl.when(pl.program_id(0) * 2 // pl.num_programs(0) == info[0])
    def _():
        values = normed[...]
        for chip in range(PLANE):
            copies[chip] = values


def norm_forward(token, info, hid, mine, other, gain, shift, block=128):
    frames, width = hid.shape
    blocks = frames // (2 * block)
    rows = pl.BlockSpec((block, width), lambda j, *_: (j, 0))
    vector = pl.BlockSpec((width,), lambda j, *_: (0,))
    return ordered(
        norm_kernel,
        token,
        (hid, mine, other, gain, shift),
        [rows, rows, rows, vector, vector],
        [
            rows,
            rows,
            pl.BlockSpec(
                (PLANE, block, width),
                lambda j, info: (0, jnp.clip(j - blocks * info[0], 0, blocks - 1), 0),
            ),
        ],
        [sds((frames, width), f32), sds((frames, width), low), sds((PLANE, frames // 2, width), low)],
        (frames // block,),
        10 * frames * width,
        info=info,
        brief=True,
    )


def cross_back_kernel(info, x, mine, other, above, gain, co, q, ck, cv, att, logsum, cq, total, total_low, vectors, dq, dk, dv, part, acc, gain_acc, shift_acc, kept):
    norm_back_step(x, mine, other, above, gain, total, total_low, kept, vectors, gain_acc, shift_acc)

    @pl.when(pl.program_id(0) >= BLOCKS)
    def _():
        g = product_with_rows(kept[...], co[...]).astype(low)
        a, b, c = cross_attend_back(info, q[...], ck, cv, g, att[...], logsum[...])
        a = a.astype(low)
        dq[...] = a
        dk[...] = b.astype(low)
        dv[...] = c.astype(low)
        added(acc, product_with_rows(a, cq[...]), part, BLOCKS)


def cross_backward(token, info, x, mine, other, above, gain, co, q, ck, cv, att, logsums, cq, tile=4 * HEAD):
    frames, width = x.shape
    columns, keys = cq.shape[1], ck.shape[0]
    whole, vector, column, row, act, table, logsum = specs(frames, width, tile, BLOCKS)
    key = pl.BlockSpec((keys, tile), lambda j, *_: (0, jnp.maximum(j - BLOCKS, 0)))
    blocks = row_block(frames, width)
    two = pl.BlockSpec((2, width), lambda j, *_: (0, 0))
    return ordered(
        cross_back_kernel,
        token,
        (x, mine, other, above, gain, co, q, ck, cv, att, logsums, cq),
        [blocks, blocks, blocks, blocks, vector, row, act, key, key, act, logsum, column],
        [blocks, blocks, two, act, key, key, whole],
        [
            sds((frames, width), f32),
            sds((frames, width), low),
            sds((2, width), f32),
            sds((frames, columns), low),
            sds((keys, columns), low),
            sds((keys, columns), low),
            sds((frames, width), low),
        ],
        (BLOCKS + columns // tile,),
        2 * frames * columns * (2 * width + 20 * keys),
        [
            pltpu.VMEM((frames, width), f32),
            pltpu.VMEM((8, width), f32),
            pltpu.VMEM((8, width), f32),
            pltpu.VMEM((frames, width), low),
        ],
        info,
    )


def self_back_kernel(info, x, mine, other, above, gain, wo, q, k, v, att, logsum, wq, wk, wv, cos, lower, upper, total, total_low, vectors, grads, part, acc, mask, gain_acc, shift_acc, kept):
    step = pl.program_id(0)

    @pl.when(step == 0)
    def _():
        mask[...] = self_mask(info[0], kept.shape[0])

    norm_back_step(x, mine, other, above, gain, total, total_low, kept, vectors, gain_acc, shift_acc)

    @pl.when(step >= BLOCKS)
    def _():
        g = product_with_rows(kept[...], wo[...]).astype(low)
        a, b, c = attend_back(q[...], k[...], v[...], g, att[...], mask[...], logsum[...])
        tables = widened(cos, lower, upper)
        a = turn_back(a, *tables).astype(low)
        b = turn_back(b, *tables).astype(low)
        c = c.astype(low)
        for index, values in enumerate((a, b, c)):
            turned = values.T
            for quarter in range(PLANE):
                grads[quarter, index] = turned[quarter * HEAD : (quarter + 1) * HEAD]
        back = product_with_rows(a, wq[...]) + product_with_rows(b, wk[...])
        added(acc, back + product_with_rows(c, wv[...]), part, BLOCKS)


def self_backward(token, info, x, mine, other, above, gain, wo, q, k, v, att, logsums, wq, wk, wv, tables, tile=4 * HEAD):
    frames, width = x.shape
    columns = wq.shape[1]
    whole, vector, column, row, act, table, logsum = specs(frames, width, tile, BLOCKS)
    blocks = row_block(frames, width)
    two = pl.BlockSpec((2, width), lambda j, *_: (0, 0))
    heads = pl.BlockSpec(
        (PLANE, 3, HEAD, frames), lambda j, *_: (0, 0, jnp.maximum(j - BLOCKS, 0), 0)
    )
    return ordered(
        self_back_kernel,
        token,
        (x, mine, other, above, gain, wo, q, k, v, att, logsums, wq, wk, wv, *tables),
        [blocks] * 4
        + [vector, row, act, act, act, act, logsum, column, column, column, table, table, table],
        [blocks, blocks, two, heads, whole],
        [
            sds((frames, width), f32),
            sds((frames, width), low),
            sds((2, width), f32),
            sds((PLANE, 3, columns // PLANE, frames), low),
            sds((frames, width), low),
        ],
        (BLOCKS + columns // tile,),
        2 * frames * columns * (4 * width + 20 * frames),
        [
            pltpu.VMEM((frames, width), f32),
            pltpu.VMEM((frames, frames), f32),
            pltpu.VMEM((8, width), f32),
            pltpu.VMEM((8, width), f32),
            pltpu.VMEM((frames, width), low),
        ],
        info,
    )


def last_kernel(_, x, mine, other, above, gain, resid, sum_mine, sum_other, total, vectors, result, gain_acc, shift_acc):
    step = pl.program_id(0)

    @pl.when(step == 0)
    def _():
        gain_acc[...] = jnp.zeros_like(gain_acc)
        shift_acc[...] = jnp.zeros_like(shift_acc)

    def rows(r):
        e = mine[r, :].astype(f32) + other[r, :].astype(f32)
        total[r, :] = norm_back_rows(x[r, :], e, gain[...][None], above[r, :], gain_acc, shift_acc)
        result[r, :] = resid[r, :] + (sum_mine[r, :].astype(f32) + sum_other[r, :].astype(f32))

    over_rows(x.shape[0], rows)

    @pl.when(step == pl.num_programs(0) - 1)
    def _():
        vectors[0:1, :] = jnp.sum(gain_acc[...], axis=0, keepdims=True)
        vectors[1:2, :] = jnp.sum(shift_acc[...], axis=0, keepdims=True)


def last_backward(token, x, mine, other, above, gain, resid, sum_mine, sum_other, block=128):
    frames, width = x.shape
    rows = pl.BlockSpec((block, width), lambda j, *_: (j, 0))
    vector = pl.BlockSpec((width,), lambda j, *_: (0,))
    two = pl.BlockSpec((2, width), lambda j, *_: (0, 0))
    return ordered(
        last_kernel,
        token,
        (x, mine, other, above, gain, resid, sum_mine, sum_other),
        [rows, rows, rows, rows, vector, rows, rows, rows],
        [rows, two, rows],
        [sds((frames, width), f32), sds((2, width), f32), sds((frames, width), f32)],
        (frames // block,),
        20 * frames * width,
        [pltpu.VMEM((8, width), f32), pltpu.VMEM((8, width), f32)],
        brief=True,
    )


def ff_kernel(_, in_ref, out_ref, gate_ref, up_ref, down_ref, sum_ref, back_ref, sum_acc, back_acc, out_low):
    @pl.when(pl.program_id(0) == 0)
    def _():
        out_low[...] = out_ref[...].astype(low)

    normed = in_ref[...]
    mixed, grad_gate, grad_up = ff_parts(
        product_plain(normed, gate_ref[...]),
        product_plain(normed, up_ref[...]),
        product_with_rows(out_low[...], down_ref[...]),
    )
    added(sum_acc, product_plain(mixed, down_ref[...]), sum_ref)
    added(
        back_acc,
        product_with_rows(grad_gate, gate_ref[...]) + product_with_rows(grad_up, up_ref[...]),
        back_ref,
    )


def ff_both(token, normed, grad_out, w_gate, w_up, w_down, tile=768):
    frames, width = normed.shape
    units = w_gate.shape[1]
    whole, _, column, row, *_ = specs(frames, width, tile)
    return ordered(
        ff_kernel,
        token,
        (normed, grad_out, w_gate, w_up, w_down),
        [whole, whole, column, column, row],
        [whole, whole],
        [sds((frames, width), low)] * 2,
        (units // tile,),
        12 * frames * width * units,
        [pltpu.VMEM((frames, width), f32)] * 2 + [pltpu.VMEM((frames, width), low)],
    )


def share_kernel(info, in_mine, in_other, out_mine, out_other, gate_ref, up_ref, down_ref, send_ref, keep_ref, acc):
    step = pl.program_id(1)
    normed = jnp.concatenate([in_mine[...], in_other[...]], axis=0)
    grad_out = jnp.concatenate([out_mine[...], out_other[...]], axis=0)
    mixed, grad_gate, grad_up = ff_parts(
        product_plain(normed, gate_ref[...]),
        product_plain(normed, up_ref[...]),
        product_with_rows(grad_out, down_ref[...]),
    )
    fresh = (
        product_over_rows(grad_out, mixed),
        product_over_rows(normed, grad_gate),
        product_over_rows(normed, grad_up),
    )
    for index, term in enumerate(fresh):

        @pl.when(step == 0)
        def _():
            acc[index] = term

        @pl.when(step != 0)
        def _():
            acc[index] += term

    @pl.when(step == pl.num_programs(1) - 1)
    def _():
        rows = send_ref.shape[2] // 3
        for pair in range(2):
            for index in range(3):
                for ref, parity in ((send_ref, 1 - info[1]), (keep_ref, info[1])):
                    start = pl.multiple_of((2 * pair + parity) * rows, rows)
                    ref[0, pair, index * rows : (index + 1) * rows] = acc[
                        index, pl.ds(start, rows), :
                    ].astype(ref.dtype)


def ff_share(token, info, normed, grad_out, w_gate, w_up, w_down, tile, first, count):
    frames, width = normed[0].shape
    chunk = frames // PLANE
    rows = pl.BlockSpec((chunk, width), lambda i, j, info: (j, 0))
    column = pl.BlockSpec((width, tile), lambda i, j, info: (0, info[0] + first + i))
    half = (LEVELS // 2, 3 * width // LEVELS, tile)
    return ordered(
        share_kernel,
        token,
        (*normed, *grad_out, w_gate, w_up, w_down),
        [rows] * 4
        + [column, column, pl.BlockSpec((tile, width), lambda i, j, info: (info[0] + first + i, 0))],
        [pl.BlockSpec((1, *half), lambda i, j, info: (i, 0, 0, 0))] * 2,
        [sds((count, *half), low)] * 2,
        (count, PLANE),
        24 * frames * width * tile * count,
        [pltpu.VMEM((3, width, tile), f32)],
        info,
    )


def weight_kernel(plan, sides_count, _, *refs):
    sides, columns = refs[:sides_count], refs[sides_count : sides_count + len(plan)]
    out = refs[sides_count + len(plan)]
    turned = refs[sides_count + len(plan) + 1 :]

    @pl.when(pl.program_id(0) == 0)
    def _():
        for side, ref in zip(sides, turned):
            ref[...] = side[...].T

    for (which, first), column in zip(plan, columns):
        product = product_plain(turned[which][...], column[...]).astype(low)
        rows = product.shape[0] // (PLANE * LEVELS)
        product = product.reshape(LEVELS, PLANE, rows, product.shape[1])
        for owner in range(PLANE):
            out[owner, :, first : first + rows, :] = product[:, owner]


def weight_products(token, sides, plan, columns, tile=256):
    width = columns[0].shape[1]
    rows = sum(sides[which].shape[1] for which, _ in plan) // (PLANE * LEVELS)
    return ordered(
        functools.partial(weight_kernel, plan, len(sides)),
        token,
        (*sides, *columns),
        [pl.BlockSpec(side.shape, lambda j, *_: (0, 0)) for side in sides]
        + [pl.BlockSpec((column.shape[0], tile), lambda j, *_: (0, j)) for column in columns],
        [pl.BlockSpec((PLANE, LEVELS, rows, tile), lambda j, *_: (0, 0, 0, j))],
        [sds((PLANE, LEVELS, rows, width), low)],
        (width // tile,),
        sum(2 * sides[w].shape[0] * sides[w].shape[1] * width for w, _ in plan),
        [pltpu.VMEM((side.shape[1], side.shape[0]), low) for side in sides],
        brief=len(sides) == 1,
    )


def out_kernel(_, side, column, first, second, third, out, turned):
    step = pl.program_id(0)

    @pl.when(step == 0)
    def _():
        turned[...] = side[...].T

    def store(values):
        values = values.astype(low).reshape(LEVELS, PLANE, out.shape[2], out.shape[3])
        for owner in range(PLANE):
            out[owner] = values[:, owner]

    @pl.when(step < pl.num_programs(0) - 1)
    def _():
        store(product_plain(turned[...], column[...]))

    @pl.when(step == pl.num_programs(0) - 1)
    def _():
        empty = jnp.zeros((out.shape[3] - 6, side.shape[1]), f32)
        store(jnp.concatenate([first[...], second[...], third[...], empty], axis=0).T)


def out_products(token, side, column, vectors, tile=128):
    frames, width = side.shape
    columns = column.shape[1]
    tiles = columns // tile
    rows = width // (PLANE * LEVELS)
    return ordered(
        out_kernel,
        token,
        (side, column, *vectors),
        [
            pl.BlockSpec((frames, width), lambda j, *_: (0, 0)),
            pl.BlockSpec((frames, tile), lambda j, *_: (0, jnp.minimum(j, tiles - 1))),
        ]
        + [pl.BlockSpec((2, width), lambda j, *_: (0, 0))] * 3,
        [pl.BlockSpec((PLANE, LEVELS, rows, tile), lambda j, *_: (0, 0, 0, j))],
        [sds((PLANE, LEVELS, rows, columns + tile), low)],
        (tiles + 1,),
        0,
        [pltpu.VMEM((width, frames), low)],
        brief=True,
    )


def plane_sum_kernel(info, got, send, keep):
    for ref, parity in ((send, 1 - info[0]), (keep, info[0])):
        total = got[0, 0, parity].astype(f32)
        for source in range(1, PLANE):
            total = total + got[source, 0, parity].astype(f32)
        ref[0] = total.astype(low)


def plane_sum(token, got, info):
    rows, width = got.shape[2:]
    out = pl.BlockSpec((1, rows, width), lambda j, *_: (j, 0, 0))
    return ordered(
        plane_sum_kernel,
        token,
        (got.reshape(PLANE, 2, 2, rows, width),),
        [pl.BlockSpec((PLANE, 1, 2, rows, width), lambda j, *_: (0, j, 0, 0, 0))],
        [out, out],
        [sds((2, rows, width), low)] * 2,
        (2,),
        0,
        info=info,
    )


def level_sum_kernel(_, keep_pass, got_pass, keep_own, got_own, passed, own):
    passed[...] = (keep_pass[0, 0].astype(f32) + got_pass[0, 0].astype(f32)).astype(low)
    own[...] = keep_own[0, 0].astype(f32) + got_own[0, 0].astype(f32)


def level_sum(token, keep, got, info, brief=True):
    count, _, rows, width = keep.shape
    block = rows // 2 if rows % 32 == 0 else rows
    steps = rows // block
    off = pl.BlockSpec((1, 1, block, width), lambda i, j, info: (i, 1 - info[0], j, 0))
    own = pl.BlockSpec((1, 1, block, width), lambda i, j, info: (i, info[0], j, 0))
    out = pl.BlockSpec((block, width), lambda i, j, info: (i * steps + j, 0))
    return ordered(
        level_sum_kernel,
        token,
        (keep, got, keep, got),
        [off, off, own, own],
        [out, out],
        [sds((count * rows, width), low), sds((count * rows, width), f32)],
        (count, steps),
        0,
        info=info,
        brief=brief,
    )


def unit_pack_kernel(counts, _, *refs):
    owns, lasts, out = refs[:-1:2], refs[1:-1:2], refs[-1]
    step = pl.program_id(0)
    for own, last, (first, count) in zip(owns, lasts, counts):

        @pl.when((step >= first) & (step < first + count))
        def _():
            total = (own[...] + last[...].astype(f32)).astype(low)
            total = total.reshape(3, PLANE, out.shape[2], out.shape[3])
            for chip in range(PLANE):
                out[chip] = total[:, chip]


def unit_pack(token, sums, rows):
    tile = sums[0][0].shape[1]
    r = rows // (3 * PLANE)
    specs_in, counts, first = [], [], 0
    for own, _ in sums:
        count = own.shape[0] // rows

        def place(j, info, first=first, count=count):
            return (jnp.clip(j - first, 0, count - 1), 0)

        specs_in += [pl.BlockSpec((rows, tile), place)] * 2
        counts.append((first, count))
        first += count
    return ordered(
        functools.partial(unit_pack_kernel, counts),
        token,
        tuple(array for pair in sums for array in pair),
        specs_in,
        [pl.BlockSpec((PLANE, 3, r, tile), lambda j, *_: (0, 0, 0, j))],
        [sds((PLANE, 3, r, tile * first), low)],
        (first,),
        0,
    )


def unit_unpack_kernel(_, got, down, gate, up):
    down[...] = got[0, 0].astype(f32).T
    gate[...] = got[0, 1].astype(f32)
    up[...] = got[0, 2].astype(f32)


def unit_unpack(token, got):
    _, _, r, units = got.shape
    across = pl.BlockSpec((r, units), lambda j, *_: (0, j))
    return ordered(
        unit_unpack_kernel,
        token,
        (got,),
        [pl.BlockSpec((1, 3, r, units), lambda j, *_: (j, 0, 0, 0))],
        [pl.BlockSpec((units, r), lambda j, *_: (j, 0)), across, across],
        [sds((PLANE * units, r), f32)] + [sds((r, PLANE * units), f32)] * 2,
        (PLANE,),
        0,
    )


def head_pack_kernel(_, own, last, out):
    total = (own[...] + last[...].astype(f32)).T.astype(low)
    out[...] = total.reshape(out.shape)


def head_pack(token, own, last):
    features, columns = own.shape
    shape = (PLANE, columns // PLANE, features)
    return ordered(
        head_pack_kernel,
        token,
        (own, last),
        [pl.BlockSpec(own.shape, lambda j, *_: (0, 0))] * 2,
        [pl.BlockSpec(shape, lambda j, *_: (0, 0, 0))],
        [sds(shape, low)],
        (1,),
        0,
        brief=True,
    )


def head_unpack_kernel(_, got, *outs):
    groups = got.shape[2] // (3 * HEAD)
    for index, out in enumerate(outs):
        pieces = []
        for group in range(groups):
            first = (index * groups + group) * HEAD
            pieces += [got[chip, :, first : first + HEAD] for chip in range(PLANE)]
        out[...] = jnp.concatenate(pieces, axis=1).astype(f32)


def head_unpack(token, got):
    chips, r, features = got.shape
    shape = (r, chips * features // 3)
    return ordered(
        head_unpack_kernel,
        token,
        (got,),
        [pl.BlockSpec(got.shape, lambda j, *_: (0, 0, 0))],
        [pl.BlockSpec(shape, lambda j, *_: (0, 0))] * 3,
        [sds(shape, f32)] * 3,
        (1,),
        0,
    )


def head_kernel(info, grads_mine, grads_other, in_mine, in_other, send, keep, acc):
    step = pl.program_id(0)
    rows = acc.shape[0]
    term = product_plain(grads_mine[0].reshape(rows, -1), in_mine[...]) + product_plain(
        grads_other[0].reshape(rows, -1), in_other[...]
    )

    @pl.when(step == 0)
    def _():
        acc[...] = term

    @pl.when(step != 0)
    def _():
        acc[...] += term

    @pl.when(step == pl.num_programs(0) - 1)
    def _():
        width = send.shape[2]
        for level in range(LEVELS):
            for ref, parity in ((send, 1 - info[1]), (keep, info[1])):

                @pl.when(parity == level % 2)
                def _():
                    ref[level // 2] = acc[:, level * width : (level + 1) * width].astype(low)


def head_products(token, info, grads, normed):
    _, three, features, frames = grads.shape
    width = normed[0].shape[1]
    chunk = normed[0].shape[0] // PLANE
    rows = pl.BlockSpec((chunk, width), lambda j, info: (j, 0))
    half = (LEVELS // 2, three * features, width // LEVELS)
    return ordered(
        head_kernel,
        token,
        (grads, grads, *normed),
        [
            pl.BlockSpec((1, three, features, chunk), lambda j, info: (j, 0, 0, info[0])),
            pl.BlockSpec((1, three, features, chunk), lambda j, info: (j, 0, 0, 1 - info[0])),
            rows,
            rows,
        ],
        [pl.BlockSpec(half, lambda j, info: (0, 0, 0))] * 2,
        [sds(half, low)] * 2,
        (PLANE,),
        2 * three * features * PLANE * frames * width,
        [pltpu.VMEM((three * features, width), f32)],
        info,
        brief=True,
    )


def on_plane(
    hidden_in,
    out_grad,
    prompt_states,
    row_split,
    prompt_len,
    gain_attn,
    bias_attn,
    gain_cross,
    bias_cross,
    gain_ff,
    bias_ff,
    w_query,
    w_key,
    w_value,
    w_out,
    c_query,
    c_key,
    c_value,
    c_out,
    w_gate,
    w_up,
    w_down,
):
    frames, width = hidden_in.shape
    plane, level = lax.axis_index("dp") % PLANE, lax.axis_index("dp") // PLANE
    positions = jnp.arange(frames, dtype=jnp.int32)
    row_ids = (positions >= row_split[0]).astype(jnp.int32)
    tables = rotary_tables((positions - row_ids * row_split[0]).astype(f32), 2 * HEAD)

    tile = 256
    tiles = w_gate.shape[1] // (PLANE * tile)
    zero = jnp.zeros((1,), jnp.int32)
    half = zero + lax.axis_index("tensor")
    parity, upper = zero + level % 2, zero + level // 2
    info = jnp.concatenate([row_split, prompt_len, half])
    unit_info = jnp.concatenate([zero + plane * tiles, parity])
    head_info = jnp.concatenate([half, parity])
    chips = [[PLANE * z + p for p in range(PLANE)] for z in range(LEVELS)]

    def swapped(part):
        return lax.ppermute(part, "tensor", [(0, 1), (1, 0)])

    def in_plane(values):
        shape = values.shape
        return lax.all_to_all(
            values, "dp", 0, 0, axis_index_groups=chips, tiled=True
        ).reshape(shape)

    def gathered(copies):
        return in_plane(copies.reshape(-1, width))

    def level_swap(values, mask):
        return lax.ppermute(values, "dp", pairs(mask))

    token = jnp.zeros((8, 128), f32)
    context = prompt_states.reshape(2 * PROMPT, prompt_states.shape[2])
    cross_key = product_plain(context, c_key).astype(low)
    cross_value = product_plain(context, c_value).astype(low)
    copies_one, copies, query, key, value, attended_one, logsum_one, part, token = self_forward(
        token,
        info,
        hidden_in,
        gain_attn,
        bias_attn,
        w_query,
        w_key,
        w_value,
        w_out,
        tables,
        out_grad,
    )
    part_swapped = swapped(part)
    frames_out = gathered(copies)
    resid_one, input_two, cross_query, attended_two, logsum_two, part, token = cross_forward(
        token,
        info,
        hidden_in,
        part,
        part_swapped,
        gain_cross,
        bias_cross,
        c_query,
        cross_key,
        cross_value,
        c_out,
    )
    part_swapped = swapped(part)
    resid_two, input_three, copies, token = norm_forward(
        token, half, resid_one, part, part_swapped, gain_ff, bias_ff
    )
    frames_out, token = hold(token, frames_out)
    frames_in = gathered(copies)
    frames_out = (frames_out, swapped(frames_out))
    sum_part, back_part, token = ff_both(token, input_three, out_grad, w_gate, w_up, w_down)
    frames_in, token = hold(token, frames_in)
    frames_in = (frames_in, swapped(frames_in))
    back_swapped = swapped(back_part)
    copies_one, token = hold(token, copies_one)
    frames_one = gathered(copies_one)

    def share(token, index, count):
        return ff_share(token, unit_info, frames_in, frames_out, w_gate, w_up, w_down, tile, index, count)

    send_a, keep_a, token = share(token, 0, 1)
    got_a = level_swap(send_a, PLANE)
    grad_two, grad_cross_out, vectors_ff, query_grad, key_grad, value_grad, part, token = cross_backward(
        token,
        info,
        resid_two,
        back_part,
        back_swapped,
        out_grad,
        gain_ff,
        c_out,
        cross_query,
        cross_key,
        cross_value,
        attended_two,
        logsum_two,
        c_query,
    )
    part_swapped = swapped(part)
    r, c = width // 16, context.shape[1] // 16
    products, token = weight_products(
        token,
        [grad_cross_out, input_two, context],
        [(0, 0), (1, r), (2, 2 * r), (2, 2 * r + c)],
        [attended_two, query_grad, key_grad, value_grad],
    )
    frames_one, token = hold(token, frames_one)
    got_cross = in_plane(products)
    frames_one_other = swapped(frames_one)
    pass_a, own_a, token = level_sum(token, keep_a, got_a, upper)
    last_a = level_swap(pass_a, 2 * PLANE)
    send_b, keep_b, token = share(token, 1, 1)
    got_b = level_swap(send_b, PLANE)
    send_c, keep_c, token = share(token, 2, tiles - 2)
    got_c = level_swap(send_c, PLANE)
    frames_one_other, token = hold(token, frames_one_other, True)
    frames_one = (frames_one, frames_one_other)
    grad_one, grad_self_out, vectors_cross, grads, part, token = self_backward(
        token,
        info,
        resid_one,
        part,
        part_swapped,
        grad_two,
        gain_cross,
        w_out,
        query,
        key,
        value,
        attended_one,
        logsum_one,
        w_query,
        w_key,
        w_value,
        tables,
    )
    last_a, token = hold(token, last_a, True)
    sum_part, token = hold(token, sum_part, True)
    sum_swapped, part_swapped = swapped(sum_part), swapped(part)
    pass_b, own_b, token = level_sum(token, keep_b, got_b, upper)
    last_b = level_swap(pass_b, 2 * PLANE)
    got_cross, token = hold(token, got_cross)
    grads, token = hold(token, grads)
    got_heads = in_plane(grads)
    pass_c, own_c, token = level_sum(token, keep_c, got_c, upper)
    last_c = level_swap(pass_c, 2 * PLANE)
    send_x, keep_x, token = plane_sum(token, got_cross, parity)
    got_x = level_swap(send_x, PLANE)
    grad_hidden, vectors_attn, result, token = last_backward(
        token, hidden_in, part, part_swapped, grad_one, gain_attn, resid_two, sum_part, sum_swapped
    )
    products, token = out_products(
        token, grad_self_out, attended_one, (vectors_attn, vectors_cross, vectors_ff)
    )
    got_heads, token = hold(token, got_heads, True)
    products, token = hold(token, products, True)
    got_out = in_plane(products)
    send_h, keep_h, token = head_products(token, head_info, got_heads, frames_one)
    got_h = level_swap(send_h, PLANE)
    pass_x, own_x, token = level_sum(token, keep_x[None], got_x[None], upper)
    last_x = level_swap(pass_x, 2 * PLANE)
    last_b, token = hold(token, last_b, True)
    last_c, token = hold(token, last_c, True)
    units, token = unit_pack(
        token, [(own_a, last_a), (own_b, last_b), (own_c, last_c)], 3 * width // LEVELS
    )
    pass_h, own_h, token = level_sum(token, keep_h[None], got_h[None], upper, False)
    last_h = level_swap(pass_h, 2 * PLANE)
    got_out, token = hold(token, got_out)
    units, token = hold(token, units, True)
    units = in_plane(units)
    send_o, keep_o, token = plane_sum(token, got_out, parity)
    got_o = level_swap(send_o, PLANE)
    last_x, token = hold(token, last_x, True)
    cross = add_low(own_x, last_x)
    heads, token = head_pack(token, own_h, last_h)
    pass_o, own_o, token = level_sum(token, keep_o[None], got_o[None], upper)
    last_o = level_swap(pass_o, 2 * PLANE)
    units, token = hold(token, units)
    heads, token = hold(token, heads, True)
    heads = in_plane(heads)
    grad_w_down, grad_w_gate, grad_w_up, token = unit_unpack(token, units)
    last_o, token = hold(token, last_o, True)
    outs = add_low(own_o, last_o)
    share_of = r // 2
    vectors = lax.dynamic_slice_in_dim(
        outs, lax.axis_index("tensor") * share_of, share_of, 0
    )[:, w_query.shape[1] : w_query.shape[1] + 6].T
    heads, token = hold(token, heads)
    grad_w_query, grad_w_key, grad_w_value, token = head_unpack(token, heads)
    return (
        result,
        grad_hidden,
        *(vectors[index] for index in range(6)),
        grad_w_query,
        grad_w_key,
        grad_w_value,
        outs[:, : w_query.shape[1]].T,
        cross[r : 2 * r],
        cross[2 * r : 2 * r + c],
        cross[2 * r + c :],
        cross[:r].T,
        grad_w_gate,
        grad_w_up,
        grad_w_down,
    )


def on_any(
    hidden_in,
    out_grad,
    prompt_states,
    row_split,
    prompt_len,
    gain_attn,
    bias_attn,
    gain_cross,
    bias_cross,
    gain_ff,
    bias_ff,
    w_query,
    w_key,
    w_value,
    w_out,
    c_query,
    c_key,
    c_value,
    c_out,
    w_gate,
    w_up,
    w_down,
):
    frame_count = hidden_in.shape[0]
    positions = jnp.arange(frame_count, dtype=jnp.int32)
    split_here = row_split[0]
    row_ids = (positions >= split_here).astype(jnp.int32)
    tables = rotary_tables((positions - row_ids * split_here).astype(jnp.float32), w_query.shape[1])
    key_index = jnp.arange(2 * PROMPT, dtype=jnp.int32)
    key_rows = key_index // PROMPT
    key_live = key_index % PROMPT < jnp.where(key_rows == 0, prompt_len[0], prompt_len[1])
    self_ok = row_ids[:, None] == row_ids[None, :]
    cross_ok = (row_ids[:, None] == key_rows[None, :]) & key_live[None, :]

    normed, scaled_one, inverse_one = normalize(hidden_in, gain_attn, bias_attn)
    input_one = normed.astype(low)
    query_one = rotate(product_plain(input_one, w_query), tables).astype(low)
    key_one = rotate(product_plain(input_one, w_key), tables).astype(low)
    value_one = product_plain(input_one, w_value).astype(low)
    attended_one, logsum_one = attend_forward(query_one, heads_of(key_one), heads_of(value_one), self_ok)
    resid_one = hidden_in + swap_sum(product_plain(attended_one, w_out))

    normed, scaled_two, inverse_two = normalize(resid_one, gain_cross, bias_cross)
    input_two = normed.astype(low)
    cross_query = product_plain(input_two, c_query).astype(low)
    context_flat = prompt_states.reshape(2 * PROMPT, prompt_states.shape[2])
    cross_key = product_plain(context_flat, c_key).astype(low)
    cross_value = product_plain(context_flat, c_value).astype(low)
    attended_two, logsum_two = attend_forward(
        cross_query, heads_of(cross_key), heads_of(cross_value), cross_ok
    )
    resid_two = resid_one + swap_sum(product_plain(attended_two, c_out))

    normed, scaled_three, inverse_three = normalize(resid_two, gain_ff, bias_ff)
    input_three = normed.astype(low)
    gate_pre = product_plain(input_three, w_gate)
    up_pre = product_plain(input_three, w_up)
    sigmoid_gate = jax.nn.sigmoid(gate_pre)
    mixed_low = (gate_pre * sigmoid_gate * up_pre).astype(low)
    result = resid_two + swap_sum(product_plain(mixed_low, w_down))

    grad_ff_out = out_grad.astype(low)
    grad_w_down = generic_sum(grad_ff_out, mixed_low).T
    grad_mixed = product_with_rows(grad_ff_out, w_down)
    grad_gate = (
        grad_mixed * up_pre * sigmoid_gate * (1.0 + gate_pre * (1.0 - sigmoid_gate))
    ).astype(low)
    grad_up = (grad_mixed * gate_pre * sigmoid_gate).astype(low)
    grad_w_gate = generic_sum(input_three, grad_gate)
    grad_w_up = generic_sum(input_three, grad_up)
    normed_grad_three = swap_sum(
        product_with_rows(grad_gate, w_gate) + product_with_rows(grad_up, w_up)
    )
    back_three, grad_gain_ff, grad_bias_ff = normalize_back(
        normed_grad_three, scaled_three, inverse_three, gain_ff
    )
    grad_two = out_grad + back_three
    grad_cross_out = grad_two.astype(low)
    grad_c_out = generic_sum(grad_cross_out, attended_two).T
    grad_attended_two = product_with_rows(grad_cross_out, c_out).astype(low)
    cross_query_grad, cross_key_grad, cross_value_grad = attend_backward(
        cross_query,
        heads_of(cross_key),
        heads_of(cross_value),
        cross_ok,
        grad_attended_two,
        logsum_two,
    )
    cross_query_grad = cross_query_grad.astype(low)
    cross_key_grad = cross_key_grad.astype(low)
    cross_value_grad = cross_value_grad.astype(low)
    grad_c_query = generic_sum(input_two, cross_query_grad)
    grad_c_key = generic_sum(context_flat, cross_key_grad)
    grad_c_value = generic_sum(context_flat, cross_value_grad)
    normed_grad_two = swap_sum(product_with_rows(cross_query_grad, c_query))
    back_two, grad_gain_cross, grad_bias_cross = normalize_back(
        normed_grad_two, scaled_two, inverse_two, gain_cross
    )
    grad_one = grad_two + back_two
    grad_self_out = grad_one.astype(low)
    grad_w_out = generic_sum(grad_self_out, attended_one).T
    grad_attended_one = product_with_rows(grad_self_out, w_out).astype(low)
    query_grad, key_grad, value_grad = attend_backward(
        query_one, heads_of(key_one), heads_of(value_one), self_ok, grad_attended_one, logsum_one
    )
    query_grad = rotate_back(query_grad, tables).astype(low)
    key_grad = rotate_back(key_grad, tables).astype(low)
    value_grad = value_grad.astype(low)
    grad_w_query = generic_sum(input_one, query_grad)
    grad_w_key = generic_sum(input_one, key_grad)
    grad_w_value = generic_sum(input_one, value_grad)
    normed_grad_one = swap_sum(
        product_with_rows(query_grad, w_query)
        + product_with_rows(key_grad, w_key)
        + product_with_rows(value_grad, w_value)
    )
    back_one, grad_gain_attn, grad_bias_attn = normalize_back(
        normed_grad_one, scaled_one, inverse_one, gain_attn
    )
    grad_hidden = grad_one + back_one
    vectors = lax.psum(
        jnp.stack(
            [
                grad_gain_attn,
                grad_bias_attn,
                grad_gain_cross,
                grad_bias_cross,
                grad_gain_ff,
                grad_bias_ff,
            ]
        ),
        "dp",
    )
    vectors = own_share(vectors)
    return (
        result,
        grad_hidden,
        vectors[0],
        vectors[1],
        vectors[2],
        vectors[3],
        vectors[4],
        vectors[5],
        grad_w_query,
        grad_w_key,
        grad_w_value,
        grad_w_out,
        grad_c_query,
        grad_c_key,
        grad_c_value,
        grad_c_out,
        grad_w_gate,
        grad_w_up,
        grad_w_down,
    )


def solution(mesh):
    in_specs = (
        P("dp", None),
        P("dp", None),
        P("dp", None, None),
        P("dp"),
        P("dp"),
        P(),
        P(),
        P(),
        P(),
        P(),
        P(),
        P(None, "tensor"),
        P(None, "tensor"),
        P(None, "tensor"),
        P("tensor", None),
        P(None, "tensor"),
        P(None, "tensor"),
        P(None, "tensor"),
        P("tensor", None),
        P(None, "tensor"),
        P(None, "tensor"),
        P("tensor", None),
    )
    out_specs = (
        P("dp", None),
        P("dp", None),
        P(("dp", "tensor")),
        P(("dp", "tensor")),
        P(("dp", "tensor")),
        P(("dp", "tensor")),
        P(("dp", "tensor")),
        P(("dp", "tensor")),
        P("dp", "tensor"),
        P("dp", "tensor"),
        P("dp", "tensor"),
        P("tensor", "dp"),
        P("dp", "tensor"),
        P("dp", "tensor"),
        P("dp", "tensor"),
        P("tensor", "dp"),
        P("dp", "tensor"),
        P("dp", "tensor"),
        P("tensor", "dp"),
    )
    known = mesh.shape["dp"] == PLANE * LEVELS and mesh.shape["tensor"] == 2
    return jax.shard_map(
        on_plane if known else on_any, mesh=mesh, in_specs=in_specs, out_specs=out_specs, check_vma=False
    )
```

```python
import functools
import math

import jax
import jax.numpy as jnp
from jax import lax
from jax.experimental import pallas as pl
from jax.experimental.pallas import tpu as pltpu
from jax.sharding import PartitionSpec as P

PROMPT = 128
HEAD = 64
PLANE = 4
LEVELS = 4
VMEM_LIMIT = 62 * 2**20
COST = 3
FLOOR = 15 * 10**9

low = jnp.bfloat16
f32 = jnp.float32
sds = jax.ShapeDtypeStruct


norm_eps = 1e-05
score_scale = 0.125
masked_score = -1e30


def product_plain(left_side, right_side):
    return jnp.dot(left_side, right_side, preferred_element_type=jnp.float32)


def product_over_rows(left_side, right_side):
    return lax.dot_general(
        left_side, right_side, (((0,), (0,)), ((), ())), preferred_element_type=jnp.float32
    )


def product_with_rows(left_side, right_side):
    return lax.dot_general(
        left_side, right_side, (((1,), (1,)), ((), ())), preferred_element_type=jnp.float32
    )


def rotary_tables(positions, width):
    dim_index = jnp.arange(width) % HEAD
    freq_index = (dim_index % 16).astype(jnp.float32)
    inverse_freq = jnp.exp(freq_index * (-math.log(10000.0) / 16.0))
    angles = positions[:, None] * inverse_freq[None, :]
    cosine = jnp.cos(angles)
    sine_part = jnp.sin(angles)
    cos_table = jnp.where(dim_index < 32, cosine, 1.0)
    sin_lower = jnp.where(dim_index < 16, -sine_part, 0.0)
    sin_upper = jnp.where((dim_index >= 16) & (dim_index < 32), sine_part, 0.0)
    return (cos_table, sin_lower, sin_upper)


def rotate(values, tables):
    cos_table, sin_lower, sin_upper = tables
    return (
        values * cos_table
        + jnp.roll(values, -16, axis=1) * sin_lower
        + jnp.roll(values, 16, axis=1) * sin_upper
    )


def rotate_back(incoming, tables):
    cos_table, sin_lower, sin_upper = tables
    return (
        incoming * cos_table
        + jnp.roll(incoming * sin_lower, 16, axis=1)
        + jnp.roll(incoming * sin_upper, -16, axis=1)
    )


def normalize(values, norm_gain, norm_shift):
    average = jnp.mean(values, axis=-1, keepdims=True)
    centered = values - average
    variance = jnp.mean(centered * centered, axis=-1, keepdims=True)
    inverse = lax.rsqrt(variance + norm_eps)
    scaled = centered * inverse
    return (scaled * norm_gain + norm_shift, scaled, inverse)


def normalize_back(incoming, scaled, inverse, norm_gain):
    grad_gain = jnp.sum(incoming * scaled, axis=0)
    grad_shift = jnp.sum(incoming, axis=0)
    weighted = incoming * norm_gain
    grad_input = inverse * (
        weighted
        - jnp.mean(weighted, axis=-1, keepdims=True)
        - scaled * jnp.mean(weighted * scaled, axis=-1, keepdims=True)
    )
    return (grad_input, grad_gain, grad_shift)


def heads_of(values):
    return values.reshape(values.shape[0], values.shape[1] // HEAD, HEAD)


def attend_forward(query_block, key_heads, value_heads, allowed):
    query_heads = heads_of(query_block)
    scores = (
        jnp.einsum("qhd,khd->hqk", query_heads, key_heads, preferred_element_type=jnp.float32)
        * score_scale
    )
    scores = jnp.where(allowed[None], scores, masked_score)
    largest = jnp.max(scores, axis=-1, keepdims=True)
    exp_scores = jnp.exp(scores - largest)
    totals = jnp.sum(exp_scores, axis=-1, keepdims=True)
    soft_weights = (exp_scores / totals).astype(jnp.bfloat16)
    mixed_heads = jnp.einsum(
        "hqk,khd->qhd", soft_weights, value_heads, preferred_element_type=jnp.float32
    )
    mixed_flat = mixed_heads.reshape(query_block.shape[0], query_block.shape[1]).astype(
        jnp.bfloat16
    )
    return (mixed_flat, largest[..., 0] + jnp.log(totals[..., 0]))


def attend_backward(query_block, key_heads, value_heads, allowed, grad_block, logsum_block):
    query_heads = heads_of(query_block)
    grad_heads = heads_of(grad_block)
    scores = (
        jnp.einsum("qhd,khd->hqk", query_heads, key_heads, preferred_element_type=jnp.float32)
        * score_scale
    )
    scores = jnp.where(allowed[None], scores, masked_score)
    soft_weights = jnp.exp(scores - logsum_block[..., None])
    grad_weights = jnp.einsum(
        "qhd,khd->hqk", grad_heads, value_heads, preferred_element_type=jnp.float32
    )
    inner_sum = jnp.sum(soft_weights * grad_weights, axis=-1, keepdims=True)
    grad_scores = (soft_weights * (grad_weights - inner_sum)).astype(jnp.bfloat16)
    grad_query = (
        jnp.einsum("hqk,khd->qhd", grad_scores, key_heads, preferred_element_type=jnp.float32)
        * score_scale
    )
    grad_key = (
        jnp.einsum("hqk,qhd->khd", grad_scores, query_heads, preferred_element_type=jnp.float32)
        * score_scale
    )
    grad_value = jnp.einsum(
        "hqk,qhd->khd",
        soft_weights.astype(jnp.bfloat16),
        grad_heads,
        preferred_element_type=jnp.float32,
    )
    return (
        grad_query.reshape(query_block.shape),
        grad_key.reshape(grad_key.shape[0], -1),
        grad_value.reshape(grad_value.shape[0], -1),
    )


def swap_sum(partial):
    low = partial.astype(jnp.bfloat16)
    if lax.axis_size("tensor") == 2:
        other = lax.ppermute(low, "tensor", [(0, 1), (1, 0)])
        return low.astype(jnp.float32) + other.astype(jnp.float32)
    return lax.psum(low, "tensor").astype(jnp.float32)


def pairs(mask):
    return [(i, i ^ mask) for i in range(16)]


def own_share(vectors):
    share = vectors.shape[1] // (lax.axis_size("dp") * lax.axis_size("tensor"))
    index = lax.axis_index("dp") * lax.axis_size("tensor") + lax.axis_index("tensor")
    return lax.dynamic_slice_in_dim(vectors, index * share, share, 1)


def generic_sum(rows_side, column_side):
    return lax.psum_scatter(
        product_over_rows(rows_side, column_side).astype(jnp.bfloat16),
        "dp",
        scatter_dimension=0,
        tiled=True,
    ).astype(jnp.float32)


def add_low(*terms):
    total = terms[0].astype(jnp.float32)
    for term in terms[1:]:
        total = total + term.astype(jnp.float32)
    return total


def ff_parts(gate, up, grad_mixed):
    sig = 0.5 * jnp.tanh(0.5 * gate) + 0.5
    act = gate * sig
    return (
        (act * up).astype(low),
        (grad_mixed * up * sig * (1.0 + gate * (1.0 - sig))).astype(low),
        (grad_mixed * act).astype(low),
    )


def turn(values, cos, lower, upper):
    width = values.shape[1]
    return (values * cos + pltpu.roll(values, width - 16, 1) * lower + pltpu.roll(values, 16, 1) * upper)

def turn_back(values, cos, lower, upper):
    width = values.shape[1]
    return (values * cos + pltpu.roll(values * lower, 16, 1) + pltpu.roll(values * upper, width - 16, 1))

def normed_rows(values, gain, shift):
    average = jnp.mean(values, axis=-1, keepdims=True)
    centered = values - average
    variance = jnp.mean(centered * centered, axis=-1, keepdims=True)
    return centered * lax.rsqrt(variance + norm_eps) * gain + shift

def over_rows(rows, body, chunk=32):
    @pl.loop(0, rows // chunk, unroll=min(4, rows // chunk))
    def _(i):
        body(pl.ds(pl.multiple_of(i * chunk, chunk), chunk))

def attend(q, k, v, mask, lse_ref):
    q_turned = (q * jnp.bfloat16(0.125)).T
    v_turned = v.T
    heads = [slice(h * HEAD, (h + 1) * HEAD) for h in range(q.shape[1] // HEAD)]
    scores = [product_plain(k[:, c], q_turned[c, :]) for c in heads]
    weights, scales = [], []
    for h, s in enumerate(scores):
        s = s + mask
        m = jnp.max(s, axis=0, keepdims=True)
        e = jnp.exp(s - m)
        total = jnp.sum(e, axis=0, keepdims=True)
        weights.append(e.astype(low))
        scales.append(1.0 / total)
        lse_ref[h : h + 1, :] = m + jnp.log(total)
    outs = [product_plain(v_turned[c, :], e) * x for c, e, x in zip(heads, weights, scales)]
    return jnp.concatenate(outs, axis=0).T.astype(low)


def attend_back(q, k, v, g, att, mask, lse):
    scaled = q * jnp.bfloat16(0.125)
    q_turned = scaled.T
    g_turned = g.T
    k_turned = k.T
    weighted = g_turned.astype(f32) * att.T.astype(f32)
    dq, dk, dv = [], [], []
    for h in range(q.shape[1] // HEAD):
        c = slice(h * HEAD, (h + 1) * HEAD)
        p = jnp.exp(product_plain(k[:, c], q_turned[c, :]) + (mask - lse[h : h + 1, :]))
        dp = product_plain(v[:, c], g_turned[c, :])
        inner = jnp.sum(weighted[c, :], axis=0, keepdims=True)
        ds = (p * (dp - inner)).astype(low)
        dq.append(product_plain(k_turned[c, :], ds))
        dk.append(product_plain(ds, scaled[:, c]))
        dv.append(product_plain(p.astype(low), g[:, c]))
    return (
        jnp.concatenate(dq, axis=0).T * 0.125,
        jnp.concatenate(dk, axis=1),
        jnp.concatenate(dv, axis=1),
    )


def self_mask(split, T):
    r=lax.broadcasted_iota(jnp.int32,(T,T),0)>=split
    c=lax.broadcasted_iota(jnp.int32,(T,T),1)>=split
    return jnp.where(r==c,0.0,masked_score).astype(f32)

def key_half(info, index, frames, keys):
    second = info[0] < frames
    start = jnp.where(second, keys // 2, 0) if index == 1 else 0
    live = jnp.where(second, info[2], info[1]) if index == 1 else info[1]
    return start, live


def half_mask(live, keys, frames):
    return jnp.where(
        lax.broadcasted_iota(jnp.int32, (keys, frames), 0) < live, 0.0, masked_score
    ).astype(f32)


def key_blocks(info, k_ref, v_ref, frames):
    keys = k_ref.shape[0]
    k, v, masks = [], [], []
    for index in range(2):
        start, live = key_half(info, index, frames, keys)
        here = pl.ds(start if index == 0 else pl.multiple_of(start, keys // 2), keys // 2)
        k.append(k_ref[here, :])
        v.append(v_ref[here, :])
        masks.append(half_mask(live, keys // 2, frames // 2))
    return k, v, jnp.concatenate(masks, axis=1)


def cross_attend(info, q, k_ref, v_ref, lse_ref):
    half = q.shape[0] // 2
    q_turned = (q * jnp.bfloat16(0.125)).T
    k, v, mask = key_blocks(info, k_ref, v_ref, 2 * half)
    v_turned = [values.T for values in v]
    outs = []
    for h in range(q.shape[1] // HEAD):
        c = slice(h * HEAD, (h + 1) * HEAD)
        s = [product_plain(k[i][:, c], q_turned[c, i * half : (i + 1) * half]) for i in range(2)]
        s = jnp.concatenate(s, axis=1) + mask
        m = jnp.max(s, axis=0, keepdims=True)
        e = jnp.exp(s - m)
        total = jnp.sum(e, axis=0, keepdims=True)
        lse_ref[h : h + 1, :] = m + jnp.log(total)
        e = e.astype(low)
        o = [product_plain(v_turned[i][c, :], e[:, i * half : (i + 1) * half]) for i in range(2)]
        outs.append(jnp.concatenate(o, axis=1) * (1.0 / total))
    return jnp.concatenate(outs, axis=0).T.astype(low)


def cross_attend_back(info, q, k_ref, v_ref, g, att, lse):
    half = q.shape[0] // 2
    scaled = q * jnp.bfloat16(0.125)
    q_turned = scaled.T
    g_turned = g.T
    weighted = g_turned.astype(f32) * att.T.astype(f32)
    k, v, mask = key_blocks(info, k_ref, v_ref, 2 * half)
    k_turned = [values.T for values in k]
    parts = [slice(0, half), slice(half, 2 * half)]
    dq, dk, dv = [], [[], []], [[], []]
    for h in range(q.shape[1] // HEAD):
        c = slice(h * HEAD, (h + 1) * HEAD)
        s = [product_plain(k[i][:, c], q_turned[c, parts[i]]) for i in range(2)]
        dp = [product_plain(v[i][:, c], g_turned[c, parts[i]]) for i in range(2)]
        p = jnp.exp(jnp.concatenate(s, axis=1) + (mask - lse[h : h + 1, :]))
        inner = jnp.sum(weighted[c, :], axis=0, keepdims=True)
        ds = (p * (jnp.concatenate(dp, axis=1) - inner)).astype(low)
        p = p.astype(low)
        dq.append(
            jnp.concatenate(
                [product_plain(k_turned[i][c, :], ds[:, parts[i]]) for i in range(2)], axis=1
            )
        )
        for i in range(2):
            dk[i].append(product_plain(ds[:, parts[i]], scaled[parts[i], c]))
            dv[i].append(product_plain(p[:, parts[i]], g[parts[i], c]))
    second = (info[0] < 2 * half).astype(f32)

    def by_row(halves):
        first, last = (jnp.concatenate(half, axis=1) for half in halves)
        return jnp.concatenate([first + last * (1.0 - second), last * second], axis=0)

    return jnp.concatenate(dq, axis=0).T * 0.125, by_row(dk), by_row(dv)


def norm_back_rows(x,e,gain,above,gain_acc,shift_acc):
    average=jnp.mean(x,axis=-1,keepdims=True)
    centered=x-average
    variance=jnp.mean(centered*centered,axis=-1,keepdims=True)
    inverse=lax.rsqrt(variance+norm_eps)
    n=centered*inverse
    en=e*n
    w=e*gain
    mean_w=jnp.mean(w,axis=-1,keepdims=True)
    mean_wn=jnp.mean(en*gain,axis=-1,keepdims=True)
    fold=lambda t: jnp.sum(t.reshape(t.shape[0]//8,8,t.shape[1]),axis=0)
    gain_acc[...]+=fold(en)
    shift_acc[...]+=fold(e)
    return above+inverse*(w-mean_w-n*mean_wn)

def norm_back_step(x, mine, other, above, gain, total, total_low, kept, vectors, gain_acc, shift_acc):
    step, block = pl.program_id(0), x.shape[0]

    @pl.when(step == 0)
    def _():
        gain_acc[...] = jnp.zeros_like(gain_acc)
        shift_acc[...] = jnp.zeros_like(shift_acc)

    @pl.when(step < BLOCKS)
    def _():
        def rows(r):
            e = mine[r, :].astype(f32) + other[r, :].astype(f32)
            t = norm_back_rows(x[r, :], e, gain[...][None], above[r, :], gain_acc, shift_acc)
            total[r, :] = t
            total_low[r, :] = t.astype(low)
            kept[within(step, block, r), :] = t.astype(low)

        over_rows(block, rows)

    @pl.when(step == BLOCKS - 1)
    def _():
        vectors[0:1, :] = jnp.sum(gain_acc[...], axis=0, keepdims=True)
        vectors[1:2, :] = jnp.sum(shift_acc[...], axis=0, keepdims=True)


def ordered(kernel, token, args, in_specs, out_specs, out_shape, grid, flops, scratch=(), info=None, brief=False):
    if info is None:
        info = jnp.zeros((1,), jnp.int32)
    inputs, outputs = len(args), len(out_shape)

    def body(info_ref, *refs):
        token_ref = refs[inputs + 1 + outputs]

        @pl.when(functools.reduce(jnp.logical_and, [pl.program_id(i) == 0 for i in range(len(grid))]))
        def _():
            token_ref[...] = jnp.zeros_like(token_ref)

        kernel(
            info_ref,
            *refs[:inputs],
            *refs[inputs + 1 : inputs + 1 + outputs],
            *refs[inputs + 2 + outputs :],
        )

    moved = sum(math.prod(a.shape) * a.dtype.itemsize for a in (*args, *out_shape))
    *results, token = pl.pallas_call(
        body,
        grid_spec=pltpu.PrefetchScalarGridSpec(
            num_scalar_prefetch=1,
            grid=grid,
            in_specs=[*in_specs, pl.BlockSpec(memory_space=pl.ANY)],
            out_specs=[*out_specs, pl.BlockSpec((8, 128), lambda *_: (0, 0))],
            scratch_shapes=list(scratch),
        ),
        out_shape=[*out_shape, sds((8, 128), f32)],
        compiler_params=pltpu.CompilerParams(vmem_limit_bytes=VMEM_LIMIT),
        cost_estimate=pl.CostEstimate(flops=0 if brief else max(FLOOR, int(flops * COST)), bytes_accessed=0 if brief else int(moved * COST), transcendentals=0),
    )(info, *args, token)
    return (*results, token)


def hold(token, values, brief=False):
    def nothing(values_ref, token_ref, out_ref, token_out):
        token_out[...] = jnp.zeros_like(token_out)

    return pl.pallas_call(
        nothing,
        in_specs=[pl.BlockSpec(memory_space=pl.ANY)] * 2,
        out_specs=[pl.BlockSpec(memory_space=pl.ANY), pl.BlockSpec(memory_space=pltpu.VMEM)],
        out_shape=[sds(values.shape, values.dtype), sds((8, 128), f32)],
        input_output_aliases={0: 0},
        compiler_params=pltpu.CompilerParams(vmem_limit_bytes=VMEM_LIMIT),
        cost_estimate=pl.CostEstimate(flops=0 if brief else FLOOR, bytes_accessed=0, transcendentals=0),
    )(values, token)


def specs(frames, width, tile, blocks=0):
    def tile_of(j):
        return jnp.maximum(j - blocks, 0) if blocks else j

    whole = pl.BlockSpec((frames, width), lambda j, *_: (0, 0))
    vector = pl.BlockSpec((width,), lambda j, *_: (0,))
    column = pl.BlockSpec((width, tile), lambda j, *_: (0, tile_of(j)))
    row = pl.BlockSpec((tile, width), lambda j, *_: (tile_of(j), 0))
    act = pl.BlockSpec((frames, tile), lambda j, *_: (0, tile_of(j)))
    table = pl.BlockSpec((frames, 2 * HEAD), lambda j, *_: (0, 0))
    logsum = pl.BlockSpec((8, frames), lambda j, *_: (tile_of(j), 0))
    return whole, vector, column, row, act, table, logsum


BLOCKS = 4


def widened(*tables):
    return tuple(jnp.concatenate([table[...], table[...]], axis=1) for table in tables)


def row_block(frames, width):
    return pl.BlockSpec((frames // BLOCKS, width), lambda j, *_: (jnp.minimum(j, BLOCKS - 1), 0))


def copies_block(frames, width, place):
    return pl.BlockSpec(
        (PLANE, frames // BLOCKS, width),
        lambda j, info: (0, jnp.clip(j - BLOCKS // 2 * info[place], 0, BLOCKS // 2 - 1), 0),
    )


def within(step, rows, r):
    return pl.ds(pl.multiple_of(step * rows + r.start, r.size), r.size)


def added(acc, term, result, first=0):
    step = pl.program_id(0)

    @pl.when(step == first)
    def _():
        acc[...] = term

    @pl.when(step != first)
    def _():
        acc[...] += term

    @pl.when(step == pl.num_programs(0) - 1)
    def _():
        result[...] = acc[...].astype(result.dtype)


def self_kernel(info, hid, gain, shift, wq, wk, wv, wo, cos, lower, upper, grad, copies, grad_copies, q, k, v, att, logsum, part, acc, mask, normed):
    step, frames, block = pl.program_id(0), normed.shape[0], hid.shape[0]

    @pl.when(step == 0)
    def _():
        mask[...] = self_mask(info[0], frames)

    @pl.when(step < BLOCKS)
    def _():
        def rows(r):
            normed[within(step, block, r), :] = normed_rows(hid[r, :], gain[...][None], shift[...][None]).astype(low)

        over_rows(block, rows)

    @pl.when((step < BLOCKS) & (step * 2 // BLOCKS == info[3]))
    def _():
        mine = normed[pl.ds(pl.multiple_of(step * block, block), block), :]
        for chip in range(PLANE):
            copies[chip] = mine

    @pl.when(step < BLOCKS // 2)
    def _():
        grad_low = grad[...].astype(low)
        for chip in range(PLANE):
            grad_copies[chip] = grad_low

    @pl.when(step >= BLOCKS)
    def _():
        n = normed[...]
        tables = widened(cos, lower, upper)
        q[...] = turn(product_plain(n, wq[...]), *tables).astype(low)
        k[...] = turn(product_plain(n, wk[...]), *tables).astype(low)
        v[...] = product_plain(n, wv[...]).astype(low)
        attended = attend(q[...], k[...], v[...], mask[...], logsum)
        att[...] = attended
        added(acc, product_plain(attended, wo[...]), part, BLOCKS)


def self_forward(token, info, hid, gain, shift, wq, wk, wv, wo, tables, grad, tile=4 * HEAD):
    frames, width = hid.shape
    columns = wq.shape[1]
    whole, vector, column, row, act, table, logsum = specs(frames, width, tile, BLOCKS)
    blocks = row_block(frames, width)
    here = frames // BLOCKS
    return ordered(
        self_kernel,
        token,
        (hid, gain, shift, wq, wk, wv, wo, *tables, grad),
        [blocks, vector, vector, column, column, column, row, table, table, table]
        + [
            pl.BlockSpec(
                (here, width),
                lambda j, info: (BLOCKS // 2 * info[3] + jnp.minimum(j, BLOCKS // 2 - 1), 0),
            )
        ],
        [
            copies_block(frames, width, 3),
            pl.BlockSpec((PLANE, here, width), lambda j, info: (0, jnp.minimum(j, BLOCKS // 2 - 1), 0)),
        ]
        + [act, act, act, act, logsum, whole],
        [sds((PLANE, frames // 2, width), low)] * 2
        + [sds((frames, columns), low)] * 4
        + [sds((columns // tile * 8, frames), f32), sds((frames, width), low)],
        (BLOCKS + columns // tile,),
        2 * frames * columns * (4 * width + 8 * frames),
        [
            pltpu.VMEM((frames, width), f32),
            pltpu.VMEM((frames, frames), f32),
            pltpu.VMEM((frames, width), low),
        ],
        info,
    )


def cross_kernel(info, hid, mine, other, gain, shift, cq, ck, cv, co, total, normed, q, att, logsum, part, acc, kept):
    step, block = pl.program_id(0), hid.shape[0]

    @pl.when(step < BLOCKS)
    def _():
        def rows(r):
            x = hid[r, :] + (mine[r, :].astype(f32) + other[r, :].astype(f32))
            total[r, :] = x
            n = normed_rows(x, gain[...][None], shift[...][None]).astype(low)
            normed[r, :] = n
            kept[within(step, block, r), :] = n

        over_rows(block, rows)

    @pl.when(step >= BLOCKS)
    def _():
        q[...] = product_plain(kept[...], cq[...]).astype(low)
        attended = cross_attend(info, q[...], ck, cv, logsum)
        att[...] = attended
        added(acc, product_plain(attended, co[...]), part, BLOCKS)


def cross_forward(token, info, hid, mine, other, gain, shift, cq, ck, cv, co, tile=4 * HEAD):
    frames, width = hid.shape
    columns, keys = cq.shape[1], ck.shape[0]
    whole, vector, column, row, act, table, logsum = specs(frames, width, tile, BLOCKS)
    key = pl.BlockSpec((keys, tile), lambda j, *_: (0, jnp.maximum(j - BLOCKS, 0)))
    blocks = row_block(frames, width)
    return ordered(
        cross_kernel,
        token,
        (hid, mine, other, gain, shift, cq, ck, cv, co),
        [blocks, blocks, blocks, vector, vector, column, key, key, row],
        [blocks, blocks, act, act, logsum, whole],
        [
            sds((frames, width), f32),
            sds((frames, width), low),
            sds((frames, columns), low),
            sds((frames, columns), low),
            sds((columns // tile * 8, frames), f32),
            sds((frames, width), low),
        ],
        (BLOCKS + columns // tile,),
        2 * frames * columns * (2 * width + 8 * keys),
        [pltpu.VMEM((frames, width), f32), pltpu.VMEM((frames, width), low)],
        info,
        brief=True,
    )


def norm_kernel(info, hid, mine, other, gain, shift, total, normed, copies):
    def rows(r):
        x = hid[r, :] + (mine[r, :].astype(f32) + other[r, :].astype(f32))
        total[r, :] = x
        normed[r, :] = normed_rows(x, gain[...][None], shift[...][None]).astype(low)

    over_rows(hid.shape[0], rows)

    @pl.when(pl.program_id(0) * 2 // pl.num_programs(0) == info[0])
    def _():
        values = normed[...]
        for chip in range(PLANE):
            copies[chip] = values


def norm_forward(token, info, hid, mine, other, gain, shift, block=128):
    frames, width = hid.shape
    blocks = frames // (2 * block)
    rows = pl.BlockSpec((block, width), lambda j, *_: (j, 0))
    vector = pl.BlockSpec((width,), lambda j, *_: (0,))
    return ordered(
        norm_kernel,
        token,
        (hid, mine, other, gain, shift),
        [rows, rows, rows, vector, vector],
        [
            rows,
            rows,
            pl.BlockSpec(
                (PLANE, block, width),
                lambda j, info: (0, jnp.clip(j - blocks * info[0], 0, blocks - 1), 0),
            ),
        ],
        [sds((frames, width), f32), sds((frames, width), low), sds((PLANE, frames // 2, width), low)],
        (frames // block,),
        10 * frames * width,
        info=info,
        brief=True,
    )


def cross_back_kernel(info, x, mine, other, above, gain, co, q, ck, cv, att, logsum, cq, total, total_low, vectors, dq, dk, dv, part, acc, gain_acc, shift_acc, kept):
    norm_back_step(x, mine, other, above, gain, total, total_low, kept, vectors, gain_acc, shift_acc)

    @pl.when(pl.program_id(0) >= BLOCKS)
    def _():
        g = product_with_rows(kept[...], co[...]).astype(low)
        a, b, c = cross_attend_back(info, q[...], ck, cv, g, att[...], logsum[...])
        a = a.astype(low)
        dq[...] = a
        dk[...] = b.astype(low)
        dv[...] = c.astype(low)
        added(acc, product_with_rows(a, cq[...]), part, BLOCKS)


def cross_backward(token, info, x, mine, other, above, gain, co, q, ck, cv, att, logsums, cq, tile=4 * HEAD):
    frames, width = x.shape
    columns, keys = cq.shape[1], ck.shape[0]
    whole, vector, column, row, act, table, logsum = specs(frames, width, tile, BLOCKS)
    key = pl.BlockSpec((keys, tile), lambda j, *_: (0, jnp.maximum(j - BLOCKS, 0)))
    blocks = row_block(frames, width)
    two = pl.BlockSpec((2, width), lambda j, *_: (0, 0))
    return ordered(
        cross_back_kernel,
        token,
        (x, mine, other, above, gain, co, q, ck, cv, att, logsums, cq),
        [blocks, blocks, blocks, blocks, vector, row, act, key, key, act, logsum, column],
        [blocks, blocks, two, act, key, key, whole],
        [
            sds((frames, width), f32),
            sds((frames, width), low),
            sds((2, width), f32),
            sds((frames, columns), low),
            sds((keys, columns), low),
            sds((keys, columns), low),
            sds((frames, width), low),
        ],
        (BLOCKS + columns // tile,),
        2 * frames * columns * (2 * width + 20 * keys),
        [
            pltpu.VMEM((frames, width), f32),
            pltpu.VMEM((8, width), f32),
            pltpu.VMEM((8, width), f32),
            pltpu.VMEM((frames, width), low),
        ],
        info,
    )


def self_back_kernel(info, x, mine, other, above, gain, wo, q, k, v, att, logsum, wq, wk, wv, cos, lower, upper, total, total_low, vectors, grads, part, acc, mask, gain_acc, shift_acc, kept):
    step = pl.program_id(0)

    @pl.when(step == 0)
    def _():
        mask[...] = self_mask(info[0], kept.shape[0])

    norm_back_step(x, mine, other, above, gain, total, total_low, kept, vectors, gain_acc, shift_acc)

    @pl.when(step >= BLOCKS)
    def _():
        g = product_with_rows(kept[...], wo[...]).astype(low)
        a, b, c = attend_back(q[...], k[...], v[...], g, att[...], mask[...], logsum[...])
        tables = widened(cos, lower, upper)
        a = turn_back(a, *tables).astype(low)
        b = turn_back(b, *tables).astype(low)
        c = c.astype(low)
        for index, values in enumerate((a, b, c)):
            turned = values.T
            for quarter in range(PLANE):
                grads[quarter, index] = turned[quarter * HEAD : (quarter + 1) * HEAD]
        back = product_with_rows(a, wq[...]) + product_with_rows(b, wk[...])
        added(acc, back + product_with_rows(c, wv[...]), part, BLOCKS)


def self_backward(token, info, x, mine, other, above, gain, wo, q, k, v, att, logsums, wq, wk, wv, tables, tile=4 * HEAD):
    frames, width = x.shape
    columns = wq.shape[1]
    whole, vector, column, row, act, table, logsum = specs(frames, width, tile, BLOCKS)
    blocks = row_block(frames, width)
    two = pl.BlockSpec((2, width), lambda j, *_: (0, 0))
    heads = pl.BlockSpec(
        (PLANE, 3, HEAD, frames), lambda j, *_: (0, 0, jnp.maximum(j - BLOCKS, 0), 0)
    )
    return ordered(
        self_back_kernel,
        token,
        (x, mine, other, above, gain, wo, q, k, v, att, logsums, wq, wk, wv, *tables),
        [blocks] * 4
        + [vector, row, act, act, act, act, logsum, column, column, column, table, table, table],
        [blocks, blocks, two, heads, whole],
        [
            sds((frames, width), f32),
            sds((frames, width), low),
            sds((2, width), f32),
            sds((PLANE, 3, columns // PLANE, frames), low),
            sds((frames, width), low),
        ],
        (BLOCKS + columns // tile,),
        2 * frames * columns * (4 * width + 20 * frames),
        [
            pltpu.VMEM((frames, width), f32),
            pltpu.VMEM((frames, frames), f32),
            pltpu.VMEM((8, width), f32),
            pltpu.VMEM((8, width), f32),
            pltpu.VMEM((frames, width), low),
        ],
        info,
    )


def last_kernel(_, x, mine, other, above, gain, resid, sum_mine, sum_other, total, vectors, result, gain_acc, shift_acc):
    step = pl.program_id(0)

    @pl.when(step == 0)
    def _():
        gain_acc[...] = jnp.zeros_like(gain_acc)
        shift_acc[...] = jnp.zeros_like(shift_acc)

    def rows(r):
        e = mine[r, :].astype(f32) + other[r, :].astype(f32)
        total[r, :] = norm_back_rows(x[r, :], e, gain[...][None], above[r, :], gain_acc, shift_acc)
        result[r, :] = resid[r, :] + (sum_mine[r, :].astype(f32) + sum_other[r, :].astype(f32))

    over_rows(x.shape[0], rows)

    @pl.when(step == pl.num_programs(0) - 1)
    def _():
        vectors[0:1, :] = jnp.sum(gain_acc[...], axis=0, keepdims=True)
        vectors[1:2, :] = jnp.sum(shift_acc[...], axis=0, keepdims=True)


def last_backward(token, x, mine, other, above, gain, resid, sum_mine, sum_other, block=128):
    frames, width = x.shape
    rows = pl.BlockSpec((block, width), lambda j, *_: (j, 0))
    vector = pl.BlockSpec((width,), lambda j, *_: (0,))
    two = pl.BlockSpec((2, width), lambda j, *_: (0, 0))
    return ordered(
        last_kernel,
        token,
        (x, mine, other, above, gain, resid, sum_mine, sum_other),
        [rows, rows, rows, rows, vector, rows, rows, rows],
        [rows, two, rows],
        [sds((frames, width), f32), sds((2, width), f32), sds((frames, width), f32)],
        (frames // block,),
        20 * frames * width,
        [pltpu.VMEM((8, width), f32), pltpu.VMEM((8, width), f32)],
        brief=True,
    )


def ff_kernel(_, in_ref, out_ref, gate_ref, up_ref, down_ref, sum_ref, back_ref, sum_acc, back_acc, out_low):
    @pl.when(pl.program_id(0) == 0)
    def _():
        out_low[...] = out_ref[...].astype(low)

    normed = in_ref[...]
    mixed, grad_gate, grad_up = ff_parts(
        product_plain(normed, gate_ref[...]),
        product_plain(normed, up_ref[...]),
        product_with_rows(out_low[...], down_ref[...]),
    )
    added(sum_acc, product_plain(mixed, down_ref[...]), sum_ref)
    added(
        back_acc,
        product_with_rows(grad_gate, gate_ref[...]) + product_with_rows(grad_up, up_ref[...]),
        back_ref,
    )


def ff_both(token, normed, grad_out, w_gate, w_up, w_down, tile=768):
    frames, width = normed.shape
    units = w_gate.shape[1]
    whole, _, column, row, *_ = specs(frames, width, tile)
    return ordered(
        ff_kernel,
        token,
        (normed, grad_out, w_gate, w_up, w_down),
        [whole, whole, column, column, row],
        [whole, whole],
        [sds((frames, width), low)] * 2,
        (units // tile,),
        12 * frames * width * units,
        [pltpu.VMEM((frames, width), f32)] * 2 + [pltpu.VMEM((frames, width), low)],
    )


def share_kernel(info, in_mine, in_other, out_mine, out_other, gate_ref, up_ref, down_ref, send_ref, keep_ref, acc):
    step = pl.program_id(1)
    normed = jnp.concatenate([in_mine[...], in_other[...]], axis=0)
    grad_out = jnp.concatenate([out_mine[...], out_other[...]], axis=0)
    mixed, grad_gate, grad_up = ff_parts(
        product_plain(normed, gate_ref[...]),
        product_plain(normed, up_ref[...]),
        product_with_rows(grad_out, down_ref[...]),
    )
    fresh = (
        product_over_rows(grad_out, mixed),
        product_over_rows(normed, grad_gate),
        product_over_rows(normed, grad_up),
    )
    for index, term in enumerate(fresh):

        @pl.when(step == 0)
        def _():
            acc[index] = term

        @pl.when(step != 0)
        def _():
            acc[index] += term

    @pl.when(step == pl.num_programs(1) - 1)
    def _():
        rows = send_ref.shape[2] // 3
        for pair in range(2):
            for index in range(3):
                for ref, parity in ((send_ref, 1 - info[1]), (keep_ref, info[1])):
                    start = pl.multiple_of((2 * pair + parity) * rows, rows)
                    ref[0, pair, index * rows : (index + 1) * rows] = acc[
                        index, pl.ds(start, rows), :
                    ].astype(ref.dtype)


def ff_share(token, info, normed, grad_out, w_gate, w_up, w_down, tile, first, count):
    frames, width = normed[0].shape
    chunk = frames // PLANE
    rows = pl.BlockSpec((chunk, width), lambda i, j, info: (j, 0))
    column = pl.BlockSpec((width, tile), lambda i, j, info: (0, info[0] + first + i))
    half = (LEVELS // 2, 3 * width // LEVELS, tile)
    return ordered(
        share_kernel,
        token,
        (*normed, *grad_out, w_gate, w_up, w_down),
        [rows] * 4
        + [column, column, pl.BlockSpec((tile, width), lambda i, j, info: (info[0] + first + i, 0))],
        [pl.BlockSpec((1, *half), lambda i, j, info: (i, 0, 0, 0))] * 2,
        [sds((count, *half), low)] * 2,
        (count, PLANE),
        24 * frames * width * tile * count,
        [pltpu.VMEM((3, width, tile), f32)],
        info,
    )


def weight_kernel(plan, sides_count, _, *refs):
    sides, columns = refs[:sides_count], refs[sides_count : sides_count + len(plan)]
    out = refs[sides_count + len(plan)]
    turned = refs[sides_count + len(plan) + 1 :]

    @pl.when(pl.program_id(0) == 0)
    def _():
        for side, ref in zip(sides, turned):
            ref[...] = side[...].T

    for (which, first), column in zip(plan, columns):
        product = product_plain(turned[which][...], column[...]).astype(low)
        rows = product.shape[0] // (PLANE * LEVELS)
        product = product.reshape(LEVELS, PLANE, rows, product.shape[1])
        for owner in range(PLANE):
            out[owner, :, first : first + rows, :] = product[:, owner]


def weight_products(token, sides, plan, columns, tile=256):
    width = columns[0].shape[1]
    rows = sum(sides[which].shape[1] for which, _ in plan) // (PLANE * LEVELS)
    return ordered(
        functools.partial(weight_kernel, plan, len(sides)),
        token,
        (*sides, *columns),
        [pl.BlockSpec(side.shape, lambda j, *_: (0, 0)) for side in sides]
        + [pl.BlockSpec((column.shape[0], tile), lambda j, *_: (0, j)) for column in columns],
        [pl.BlockSpec((PLANE, LEVELS, rows, tile), lambda j, *_: (0, 0, 0, j))],
        [sds((PLANE, LEVELS, rows, width), low)],
        (width // tile,),
        sum(2 * sides[w].shape[0] * sides[w].shape[1] * width for w, _ in plan),
        [pltpu.VMEM((side.shape[1], side.shape[0]), low) for side in sides],
        brief=len(sides) == 1,
    )


def out_kernel(_, side, column, first, second, third, out, turned):
    step = pl.program_id(0)

    @pl.when(step == 0)
    def _():
        turned[...] = side[...].T

    def store(values):
        values = values.astype(low).reshape(LEVELS, PLANE, out.shape[2], out.shape[3])
        for owner in range(PLANE):
            out[owner] = values[:, owner]

    @pl.when(step < pl.num_programs(0) - 1)
    def _():
        store(product_plain(turned[...], column[...]))

    @pl.when(step == pl.num_programs(0) - 1)
    def _():
        empty = jnp.zeros((out.shape[3] - 6, side.shape[1]), f32)
        store(jnp.concatenate([first[...], second[...], third[...], empty], axis=0).T)


def out_products(token, side, column, vectors, tile=128):
    frames, width = side.shape
    columns = column.shape[1]
    tiles = columns // tile
    rows = width // (PLANE * LEVELS)
    return ordered(
        out_kernel,
        token,
        (side, column, *vectors),
        [
            pl.BlockSpec((frames, width), lambda j, *_: (0, 0)),
            pl.BlockSpec((frames, tile), lambda j, *_: (0, jnp.minimum(j, tiles - 1))),
        ]
        + [pl.BlockSpec((2, width), lambda j, *_: (0, 0))] * 3,
        [pl.BlockSpec((PLANE, LEVELS, rows, tile), lambda j, *_: (0, 0, 0, j))],
        [sds((PLANE, LEVELS, rows, columns + tile), low)],
        (tiles + 1,),
        0,
        [pltpu.VMEM((width, frames), low)],
        brief=True,
    )


def plane_sum_kernel(info, got, send, keep):
    for ref, parity in ((send, 1 - info[0]), (keep, info[0])):
        total = got[0, 0, parity].astype(f32)
        for source in range(1, PLANE):
            total = total + got[source, 0, parity].astype(f32)
        ref[0] = total.astype(low)


def plane_sum(token, got, info):
    rows, width = got.shape[2:]
    out = pl.BlockSpec((1, rows, width), lambda j, *_: (j, 0, 0))
    return ordered(
        plane_sum_kernel,
        token,
        (got.reshape(PLANE, 2, 2, rows, width),),
        [pl.BlockSpec((PLANE, 1, 2, rows, width), lambda j, *_: (0, j, 0, 0, 0))],
        [out, out],
        [sds((2, rows, width), low)] * 2,
        (2,),
        0,
        info=info,
    )


def level_sum_kernel(_, keep_pass, got_pass, keep_own, got_own, passed, own):
    passed[...] = (keep_pass[0, 0].astype(f32) + got_pass[0, 0].astype(f32)).astype(low)
    own[...] = keep_own[0, 0].astype(f32) + got_own[0, 0].astype(f32)


def level_sum(token, keep, got, info, brief=True):
    count, _, rows, width = keep.shape
    block = rows // 2 if rows % 32 == 0 else rows
    steps = rows // block
    off = pl.BlockSpec((1, 1, block, width), lambda i, j, info: (i, 1 - info[0], j, 0))
    own = pl.BlockSpec((1, 1, block, width), lambda i, j, info: (i, info[0], j, 0))
    out = pl.BlockSpec((block, width), lambda i, j, info: (i * steps + j, 0))
    return ordered(
        level_sum_kernel,
        token,
        (keep, got, keep, got),
        [off, off, own, own],
        [out, out],
        [sds((count * rows, width), low), sds((count * rows, width), f32)],
        (count, steps),
        0,
        info=info,
        brief=brief,
    )


def unit_pack_kernel(counts, _, *refs):
    owns, lasts, out = refs[:-1:2], refs[1:-1:2], refs[-1]
    step = pl.program_id(0)
    for own, last, (first, count) in zip(owns, lasts, counts):

        @pl.when((step >= first) & (step < first + count))
        def _():
            total = (own[...] + last[...].astype(f32)).astype(low)
            total = total.reshape(3, PLANE, out.shape[2], out.shape[3])
            for chip in range(PLANE):
                out[chip] = total[:, chip]


def unit_pack(token, sums, rows):
    tile = sums[0][0].shape[1]
    r = rows // (3 * PLANE)
    specs_in, counts, first = [], [], 0
    for own, _ in sums:
        count = own.shape[0] // rows

        def place(j, info, first=first, count=count):
            return (jnp.clip(j - first, 0, count - 1), 0)

        specs_in += [pl.BlockSpec((rows, tile), place)] * 2
        counts.append((first, count))
        first += count
    return ordered(
        functools.partial(unit_pack_kernel, counts),
        token,
        tuple(array for pair in sums for array in pair),
        specs_in,
        [pl.BlockSpec((PLANE, 3, r, tile), lambda j, *_: (0, 0, 0, j))],
        [sds((PLANE, 3, r, tile * first), low)],
        (first,),
        0,
    )


def unit_unpack_kernel(_, got, down, gate, up):
    down[...] = got[0, 0].astype(f32).T
    gate[...] = got[0, 1].astype(f32)
    up[...] = got[0, 2].astype(f32)


def unit_unpack(token, got):
    _, _, r, units = got.shape
    across = pl.BlockSpec((r, units), lambda j, *_: (0, j))
    return ordered(
        unit_unpack_kernel,
        token,
        (got,),
        [pl.BlockSpec((1, 3, r, units), lambda j, *_: (j, 0, 0, 0))],
        [pl.BlockSpec((units, r), lambda j, *_: (j, 0)), across, across],
        [sds((PLANE * units, r), f32)] + [sds((r, PLANE * units), f32)] * 2,
        (PLANE,),
        0,
    )


def head_pack_kernel(_, own, last, out):
    total = (own[...] + last[...].astype(f32)).T.astype(low)
    out[...] = total.reshape(out.shape)


def head_pack(token, own, last):
    features, columns = own.shape
    shape = (PLANE, columns // PLANE, features)
    return ordered(
        head_pack_kernel,
        token,
        (own, last),
        [pl.BlockSpec(own.shape, lambda j, *_: (0, 0))] * 2,
        [pl.BlockSpec(shape, lambda j, *_: (0, 0, 0))],
        [sds(shape, low)],
        (1,),
        0,
        brief=True,
    )


def head_unpack_kernel(_, got, *outs):
    groups = got.shape[2] // (3 * HEAD)
    for index, out in enumerate(outs):
        pieces = []
        for group in range(groups):
            first = (index * groups + group) * HEAD
            pieces += [got[chip, :, first : first + HEAD] for chip in range(PLANE)]
        out[...] = jnp.concatenate(pieces, axis=1).astype(f32)


def head_unpack(token, got):
    chips, r, features = got.shape
    shape = (r, chips * features // 3)
    return ordered(
        head_unpack_kernel,
        token,
        (got,),
        [pl.BlockSpec(got.shape, lambda j, *_: (0, 0, 0))],
        [pl.BlockSpec(shape, lambda j, *_: (0, 0))] * 3,
        [sds(shape, f32)] * 3,
        (1,),
        0,
    )


def head_kernel(info, grads_mine, grads_other, in_mine, in_other, send, keep, acc):
    step = pl.program_id(0)
    rows = acc.shape[0]
    term = product_plain(grads_mine[0].reshape(rows, -1), in_mine[...]) + product_plain(
        grads_other[0].reshape(rows, -1), in_other[...]
    )

    @pl.when(step == 0)
    def _():
        acc[...] = term

    @pl.when(step != 0)
    def _():
        acc[...] += term

    @pl.when(step == pl.num_programs(0) - 1)
    def _():
        width = send.shape[2]
        for level in range(LEVELS):
            for ref, parity in ((send, 1 - info[1]), (keep, info[1])):

                @pl.when(parity == level % 2)
                def _():
                    ref[level // 2] = acc[:, level * width : (level + 1) * width].astype(low)


def head_products(token, info, grads, normed):
    _, three, features, frames = grads.shape
    width = normed[0].shape[1]
    chunk = normed[0].shape[0] // PLANE
    rows = pl.BlockSpec((chunk, width), lambda j, info: (j, 0))
    half = (LEVELS // 2, three * features, width // LEVELS)
    return ordered(
        head_kernel,
        token,
        (grads, grads, *normed),
        [
            pl.BlockSpec((1, three, features, chunk), lambda j, info: (j, 0, 0, info[0])),
            pl.BlockSpec((1, three, features, chunk), lambda j, info: (j, 0, 0, 1 - info[0])),
            rows,
            rows,
        ],
        [pl.BlockSpec(half, lambda j, info: (0, 0, 0))] * 2,
        [sds(half, low)] * 2,
        (PLANE,),
        2 * three * features * PLANE * frames * width,
        [pltpu.VMEM((three * features, width), f32)],
        info,
        brief=True,
    )


def on_plane(
    hidden_in,
    out_grad,
    prompt_states,
    row_split,
    prompt_len,
    gain_attn,
    bias_attn,
    gain_cross,
    bias_cross,
    gain_ff,
    bias_ff,
    w_query,
    w_key,
    w_value,
    w_out,
    c_query,
    c_key,
    c_value,
    c_out,
    w_gate,
    w_up,
    w_down,
):
    frames, width = hidden_in.shape
    plane, level = lax.axis_index("dp") % PLANE, lax.axis_index("dp") // PLANE
    positions = jnp.arange(frames, dtype=jnp.int32)
    row_ids = (positions >= row_split[0]).astype(jnp.int32)
    tables = rotary_tables((positions - row_ids * row_split[0]).astype(f32), 2 * HEAD)

    tile = 256
    tiles = w_gate.shape[1] // (PLANE * tile)
    zero = jnp.zeros((1,), jnp.int32)
    half = zero + lax.axis_index("tensor")
    parity, upper = zero + level % 2, zero + level // 2
    info = jnp.concatenate([row_split, prompt_len, half])
    unit_info = jnp.concatenate([zero + plane * tiles, parity])
    head_info = jnp.concatenate([half, parity])
    chips = [[PLANE * z + p for p in range(PLANE)] for z in range(LEVELS)]

    def swapped(part):
        return lax.ppermute(part, "tensor", [(0, 1), (1, 0)])

    def in_plane(values):
        shape = values.shape
        return lax.all_to_all(
            values, "dp", 0, 0, axis_index_groups=chips, tiled=True
        ).reshape(shape)

    def gathered(copies):
        return in_plane(copies.reshape(-1, width))

    def level_swap(values, mask):
        return lax.ppermute(values, "dp", pairs(mask))

    token = jnp.zeros((8, 128), f32)
    context = prompt_states.reshape(2 * PROMPT, prompt_states.shape[2])
    cross_key = product_plain(context, c_key).astype(low)
    cross_value = product_plain(context, c_value).astype(low)
    copies_one, copies, query, key, value, attended_one, logsum_one, part, token = self_forward(
        token,
        info,
        hidden_in,
        gain_attn,
        bias_attn,
        w_query,
        w_key,
        w_value,
        w_out,
        tables,
        out_grad,
    )
    part_swapped = swapped(part)
    frames_out = gathered(copies)
    resid_one, input_two, cross_query, attended_two, logsum_two, part, token = cross_forward(
        token,
        info,
        hidden_in,
        part,
        part_swapped,
        gain_cross,
        bias_cross,
        c_query,
        cross_key,
        cross_value,
        c_out,
    )
    part_swapped = swapped(part)
    resid_two, input_three, copies, token = norm_forward(
        token, half, resid_one, part, part_swapped, gain_ff, bias_ff
    )
    frames_out, token = hold(token, frames_out)
    frames_in = gathered(copies)
    frames_out = (frames_out, swapped(frames_out))
    sum_part, back_part, token = ff_both(token, input_three, out_grad, w_gate, w_up, w_down)
    frames_in, token = hold(token, frames_in)
    frames_in = (frames_in, swapped(frames_in))
    back_swapped = swapped(back_part)
    copies_one, token = hold(token, copies_one)
    frames_one = gathered(copies_one)

    def share(token, index, count):
        return ff_share(token, unit_info, frames_in, frames_out, w_gate, w_up, w_down, tile, index, count)

    send_a, keep_a, token = share(token, 0, 1)
    got_a = level_swap(send_a, PLANE)
    grad_two, grad_cross_out, vectors_ff, query_grad, key_grad, value_grad, part, token = cross_backward(
        token,
        info,
        resid_two,
        back_part,
        back_swapped,
        out_grad,
        gain_ff,
        c_out,
        cross_query,
        cross_key,
        cross_value,
        attended_two,
        logsum_two,
        c_query,
    )
    part_swapped = swapped(part)
    r, c = width // 16, context.shape[1] // 16
    products, token = weight_products(
        token,
        [grad_cross_out, input_two, context],
        [(0, 0), (1, r), (2, 2 * r), (2, 2 * r + c)],
        [attended_two, query_grad, key_grad, value_grad],
    )
    frames_one, token = hold(token, frames_one)
    got_cross = in_plane(products)
    frames_one_other = swapped(frames_one)
    pass_a, own_a, token = level_sum(token, keep_a, got_a, upper)
    last_a = level_swap(pass_a, 2 * PLANE)
    send_b, keep_b, token = share(token, 1, 1)
    got_b = level_swap(send_b, PLANE)
    send_c, keep_c, token = share(token, 2, tiles - 2)
    got_c = level_swap(send_c, PLANE)
    frames_one_other, token = hold(token, frames_one_other, True)
    frames_one = (frames_one, frames_one_other)
    grad_one, grad_self_out, vectors_cross, grads, part, token = self_backward(
        token,
        info,
        resid_one,
        part,
        part_swapped,
        grad_two,
        gain_cross,
        w_out,
        query,
        key,
        value,
        attended_one,
        logsum_one,
        w_query,
        w_key,
        w_value,
        tables,
    )
    last_a, token = hold(token, last_a, True)
    sum_part, token = hold(token, sum_part, True)
    sum_swapped, part_swapped = swapped(sum_part), swapped(part)
    pass_b, own_b, token = level_sum(token, keep_b, got_b, upper)
    last_b = level_swap(pass_b, 2 * PLANE)
    got_cross, token = hold(token, got_cross)
    grads, token = hold(token, grads)
    got_heads = in_plane(grads)
    pass_c, own_c, token = level_sum(token, keep_c, got_c, upper)
    last_c = level_swap(pass_c, 2 * PLANE)
    send_x, keep_x, token = plane_sum(token, got_cross, parity)
    got_x = level_swap(send_x, PLANE)
    grad_hidden, vectors_attn, result, token = last_backward(
        token, hidden_in, part, part_swapped, grad_one, gain_attn, resid_two, sum_part, sum_swapped
    )
    products, token = out_products(
        token, grad_self_out, attended_one, (vectors_attn, vectors_cross, vectors_ff)
    )
    got_heads, token = hold(token, got_heads, True)
    products, token = hold(token, products, True)
    got_out = in_plane(products)
    send_h, keep_h, token = head_products(token, head_info, got_heads, frames_one)
    got_h = level_swap(send_h, PLANE)
    pass_x, own_x, token = level_sum(token, keep_x[None], got_x[None], upper)
    last_x = level_swap(pass_x, 2 * PLANE)
    last_b, token = hold(token, last_b, True)
    last_c, token = hold(token, last_c, True)
    units, token = unit_pack(
        token, [(own_a, last_a), (own_b, last_b), (own_c, last_c)], 3 * width // LEVELS
    )
    pass_h, own_h, token = level_sum(token, keep_h[None], got_h[None], upper, False)
    last_h = level_swap(pass_h, 2 * PLANE)
    got_out, token = hold(token, got_out)
    units, token = hold(token, units, True)
    units = in_plane(units)
    send_o, keep_o, token = plane_sum(token, got_out, parity)
    got_o = level_swap(send_o, PLANE)
    heads, token = head_pack(token, own_h, last_h)
    pass_o, own_o, token = level_sum(token, keep_o[None], got_o[None], upper)
    last_o = level_swap(pass_o, 2 * PLANE)
    last_x, token = hold(token, last_x, True)
    cross = add_low(own_x, last_x)
    units, token = hold(token, units)
    heads, token = hold(token, heads, True)
    heads = in_plane(heads)
    grad_w_down, grad_w_gate, grad_w_up, token = unit_unpack(token, units)
    last_o, token = hold(token, last_o, True)
    outs = add_low(own_o, last_o)
    share_of = r // 2
    vectors = lax.dynamic_slice_in_dim(
        outs, lax.axis_index("tensor") * share_of, share_of, 0
    )[:, w_query.shape[1] : w_query.shape[1] + 6].T
    heads, token = hold(token, heads)
    grad_w_query, grad_w_key, grad_w_value, token = head_unpack(token, heads)
    return (
        result,
        grad_hidden,
        *(vectors[index] for index in range(6)),
        grad_w_query,
        grad_w_key,
        grad_w_value,
        outs[:, : w_query.shape[1]].T,
        cross[r : 2 * r],
        cross[2 * r : 2 * r + c],
        cross[2 * r + c :],
        cross[:r].T,
        grad_w_gate,
        grad_w_up,
        grad_w_down,
    )


def on_any(
    hidden_in,
    out_grad,
    prompt_states,
    row_split,
    prompt_len,
    gain_attn,
    bias_attn,
    gain_cross,
    bias_cross,
    gain_ff,
    bias_ff,
    w_query,
    w_key,
    w_value,
    w_out,
    c_query,
    c_key,
    c_value,
    c_out,
    w_gate,
    w_up,
    w_down,
):
    frame_count = hidden_in.shape[0]
    positions = jnp.arange(frame_count, dtype=jnp.int32)
    split_here = row_split[0]
    row_ids = (positions >= split_here).astype(jnp.int32)
    tables = rotary_tables((positions - row_ids * split_here).astype(jnp.float32), w_query.shape[1])
    key_index = jnp.arange(2 * PROMPT, dtype=jnp.int32)
    key_rows = key_index // PROMPT
    key_live = key_index % PROMPT < jnp.where(key_rows == 0, prompt_len[0], prompt_len[1])
    self_ok = row_ids[:, None] == row_ids[None, :]
    cross_ok = (row_ids[:, None] == key_rows[None, :]) & key_live[None, :]

    normed, scaled_one, inverse_one = normalize(hidden_in, gain_attn, bias_attn)
    input_one = normed.astype(low)
    query_one = rotate(product_plain(input_one, w_query), tables).astype(low)
    key_one = rotate(product_plain(input_one, w_key), tables).astype(low)
    value_one = product_plain(input_one, w_value).astype(low)
    attended_one, logsum_one = attend_forward(query_one, heads_of(key_one), heads_of(value_one), self_ok)
    resid_one = hidden_in + swap_sum(product_plain(attended_one, w_out))

    normed, scaled_two, inverse_two = normalize(resid_one, gain_cross, bias_cross)
    input_two = normed.astype(low)
    cross_query = product_plain(input_two, c_query).astype(low)
    context_flat = prompt_states.reshape(2 * PROMPT, prompt_states.shape[2])
    cross_key = product_plain(context_flat, c_key).astype(low)
    cross_value = product_plain(context_flat, c_value).astype(low)
    attended_two, logsum_two = attend_forward(
        cross_query, heads_of(cross_key), heads_of(cross_value), cross_ok
    )
    resid_two = resid_one + swap_sum(product_plain(attended_two, c_out))

    normed, scaled_three, inverse_three = normalize(resid_two, gain_ff, bias_ff)
    input_three = normed.astype(low)
    gate_pre = product_plain(input_three, w_gate)
    up_pre = product_plain(input_three, w_up)
    sigmoid_gate = jax.nn.sigmoid(gate_pre)
    mixed_low = (gate_pre * sigmoid_gate * up_pre).astype(low)
    result = resid_two + swap_sum(product_plain(mixed_low, w_down))

    grad_ff_out = out_grad.astype(low)
    grad_w_down = generic_sum(grad_ff_out, mixed_low).T
    grad_mixed = product_with_rows(grad_ff_out, w_down)
    grad_gate = (
        grad_mixed * up_pre * sigmoid_gate * (1.0 + gate_pre * (1.0 - sigmoid_gate))
    ).astype(low)
    grad_up = (grad_mixed * gate_pre * sigmoid_gate).astype(low)
    grad_w_gate = generic_sum(input_three, grad_gate)
    grad_w_up = generic_sum(input_three, grad_up)
    normed_grad_three = swap_sum(
        product_with_rows(grad_gate, w_gate) + product_with_rows(grad_up, w_up)
    )
    back_three, grad_gain_ff, grad_bias_ff = normalize_back(
        normed_grad_three, scaled_three, inverse_three, gain_ff
    )
    grad_two = out_grad + back_three
    grad_cross_out = grad_two.astype(low)
    grad_c_out = generic_sum(grad_cross_out, attended_two).T
    grad_attended_two = product_with_rows(grad_cross_out, c_out).astype(low)
    cross_query_grad, cross_key_grad, cross_value_grad = attend_backward(
        cross_query,
        heads_of(cross_key),
        heads_of(cross_value),
        cross_ok,
        grad_attended_two,
        logsum_two,
    )
    cross_query_grad = cross_query_grad.astype(low)
    cross_key_grad = cross_key_grad.astype(low)
    cross_value_grad = cross_value_grad.astype(low)
    grad_c_query = generic_sum(input_two, cross_query_grad)
    grad_c_key = generic_sum(context_flat, cross_key_grad)
    grad_c_value = generic_sum(context_flat, cross_value_grad)
    normed_grad_two = swap_sum(product_with_rows(cross_query_grad, c_query))
    back_two, grad_gain_cross, grad_bias_cross = normalize_back(
        normed_grad_two, scaled_two, inverse_two, gain_cross
    )
    grad_one = grad_two + back_two
    grad_self_out = grad_one.astype(low)
    grad_w_out = generic_sum(grad_self_out, attended_one).T
    grad_attended_one = product_with_rows(grad_self_out, w_out).astype(low)
    query_grad, key_grad, value_grad = attend_backward(
        query_one, heads_of(key_one), heads_of(value_one), self_ok, grad_attended_one, logsum_one
    )
    query_grad = rotate_back(query_grad, tables).astype(low)
    key_grad = rotate_back(key_grad, tables).astype(low)
    value_grad = value_grad.astype(low)
    grad_w_query = generic_sum(input_one, query_grad)
    grad_w_key = generic_sum(input_one, key_grad)
    grad_w_value = generic_sum(input_one, value_grad)
    normed_grad_one = swap_sum(
        product_with_rows(query_grad, w_query)
        + product_with_rows(key_grad, w_key)
        + product_with_rows(value_grad, w_value)
    )
    back_one, grad_gain_attn, grad_bias_attn = normalize_back(
        normed_grad_one, scaled_one, inverse_one, gain_attn
    )
    grad_hidden = grad_one + back_one
    vectors = lax.psum(
        jnp.stack(
            [
                grad_gain_attn,
                grad_bias_attn,
                grad_gain_cross,
                grad_bias_cross,
                grad_gain_ff,
                grad_bias_ff,
            ]
        ),
        "dp",
    )
    vectors = own_share(vectors)
    return (
        result,
        grad_hidden,
        vectors[0],
        vectors[1],
        vectors[2],
        vectors[3],
        vectors[4],
        vectors[5],
        grad_w_query,
        grad_w_key,
        grad_w_value,
        grad_w_out,
        grad_c_query,
        grad_c_key,
        grad_c_value,
        grad_c_out,
        grad_w_gate,
        grad_w_up,
        grad_w_down,
    )


def solution(mesh):
    in_specs = (
        P("dp", None),
        P("dp", None),
        P("dp", None, None),
        P("dp"),
        P("dp"),
        P(),
        P(),
        P(),
        P(),
        P(),
        P(),
        P(None, "tensor"),
        P(None, "tensor"),
        P(None, "tensor"),
        P("tensor", None),
        P(None, "tensor"),
        P(None, "tensor"),
        P(None, "tensor"),
        P("tensor", None),
        P(None, "tensor"),
        P(None, "tensor"),
        P("tensor", None),
    )
    out_specs = (
        P("dp", None),
        P("dp", None),
        P(("dp", "tensor")),
        P(("dp", "tensor")),
        P(("dp", "tensor")),
        P(("dp", "tensor")),
        P(("dp", "tensor")),
        P(("dp", "tensor")),
        P("dp", "tensor"),
        P("dp", "tensor"),
        P("dp", "tensor"),
        P("tensor", "dp"),
        P("dp", "tensor"),
        P("dp", "tensor"),
        P("dp", "tensor"),
        P("tensor", "dp"),
        P("dp", "tensor"),
        P("dp", "tensor"),
        P("tensor", "dp"),
    )
    known = mesh.shape["dp"] == PLANE * LEVELS and mesh.shape["tensor"] == 2
    return jax.shard_map(
        on_plane if known else on_any, mesh=mesh, in_specs=in_specs, out_specs=out_specs, check_vma=False
    )
```
